32 devices in a mesh: gz: 16 (over z, y, core), gy: 2 (over x).
Axes of the slice: x: 2, y: 2, z: 4, core: 2. Of those that a mesh axis runs over, the one named last changes fastest.
Arguments:
- field: float32 [32, 16, 128, 256], P(None, 'gz', 'gy'), may hold values from -6 to 6
- spectral_filter: float32 [2, 16, 16, 1024], P(None, None, 'gy', 'gz'), may hold values from -6 to 6
- depth_weight: float32 [32, 27], replicated, may hold values from -1.25 to 1.25
- point_weight: float32 [32, 32], replicated, may hold values from -1 to 1
- bias_vector: float32 [32], replicated, may hold values from -3 to 3
Outputs:
- layer_out: float32 [32, 16, 128, 256], P(None, 'gz', 'gy')
The draws below stay inside these ranges and needn't reach their ends.
All inputs are finite; a program needn't handle non-finite values.
Results may differ from the reference program's by a relative error of at most 0.000057.
Values sent between devices are 32-bit elements; how exact they have to be, the bound alone decides.
No kernel may reach another device: no remote copies, remote signals or barrier semaphores. Data moves between devices by JAX's collectives and lax.ppermute only.
A program may use at most 64 MiB of HBM per device.

```python
import math
import jax
import jax.numpy as jnp
from jax import lax

CHANNELS = 32
NX = 256
NY = 128
MX = 32
MY = 16
MZ = 16
NZ = 16


def levels(rng, dims, pieces, smallest, top_value):
    level, own = 1.0, jax.random.fold_in(rng, 6)
    for dim, shards_of in pieces:
        heights = jnp.exp(jax.random.uniform(jax.random.fold_in(own, dim), (shards_of,), jnp.float32, smallest / len(pieces), top_value / len(pieces)))
        level = level * jnp.repeat(heights, dims[dim] // shards_of).reshape([-1 if axis == dim else 1 for axis in range(len(dims))])
    return level


def normal_values(stream_key, shape, width, reach, cuts=(), kind=jnp.bfloat16):
    array = jax.random.normal(stream_key, shape, jnp.float32) * width
    if len(cuts) > 0:
        array = levels(stream_key, shape, cuts, -0.22, 0.18) * array
    return jnp.clip(array, min=-reach, max=reach).astype(kind)


def setup_inputs(seed: int = 0) -> dict:
    splits = jax.random.split(jax.random.key(seed), 6)
    field = normal_values(splits[0], (CHANNELS, NZ, NY, NX), 1.0, 6.0, ((1, 16), (2, 2)), jnp.float32)
    spectral_filter = normal_values(splits[1], (2, MZ, MY, CHANNELS * MX), 1.0, 6.0, ((2, 2), (3, 16)), jnp.float32)
    depth_weight = normal_values(splits[2], (CHANNELS, 27), 27 ** -0.5, 1.25, (), jnp.float32)
    point_weight = normal_values(splits[3], (CHANNELS, CHANNELS), CHANNELS ** -0.5, 1.0, (), jnp.float32)
    bias_vector = normal_values(splits[4], (CHANNELS,), 0.5, 3.0, (), jnp.float32)
    return {"field": field, "spectral_filter": spectral_filter, "depth_weight": depth_weight, "point_weight": point_weight, "bias_vector": bias_vector}


def kept_freqs(count, total):
    series = jnp.arange(count, dtype=jnp.int32)
    return jnp.where(series < count // 2, series, total - count + series).astype(jnp.int32)

def reference(field, spectral_filter, depth_weight, point_weight, bias_vector):
    layout = spectral_filter.reshape(2, MZ, MY, CHANNELS, MX)
    gains = jnp.transpose(lax.complex(layout[0], layout[1]), (2, 0, 1, 3))
    z_keep = kept_freqs(MZ, NZ)
    y_keep = kept_freqs(MY, NY)
    factor = NX * NY * NZ / math.sqrt(2.0 * MX * MY * MZ)

    def one_channel(pack):
        plane, gain_set, taps = pack
        spectrum = jnp.fft.rfftn(plane, norm='ortho')
        kept = spectrum[z_keep][:, y_keep][:, :, :MX]
        product = kept * gain_set
        placed = jnp.zeros(spectrum.shape, spectrum.dtype).at[z_keep[:, None], y_keep[None, :], :MX].set(product)
        back = jnp.fft.irfftn(placed, s=plane.shape) * factor
        depth = jnp.zeros_like(plane)
        for off_z in (-1, 0, 1):
            for off_y in (-1, 0, 1):
                for off_x in (-1, 0, 1):
                    tap_index = (off_z + 1) * 9 + (off_y + 1) * 3 + (off_x + 1)
                    moved = jnp.roll(plane, (-off_z, -off_y, -off_x), axis=(0, 1, 2))
                    depth = depth + taps[tap_index] * moved
        return (back, depth)
    spectral, depth = lax.map(one_channel, (field, gains, depth_weight))
    point = jnp.einsum('dc,czyx->dzyx', point_weight, depth, precision=lax.Precision.HIGHEST)
    return jax.nn.gelu(spectral + point + bias_vector[:, None, None, None], approximate=False)
```

```python
import functools
import math

import jax
import jax.numpy as jnp
import ml_dtypes
import numpy as np
from jax import lax
from jax.experimental import pallas as pl
from jax.experimental.pallas import tpu as pltpu
from jax.sharding import PartitionSpec as P

NX = 256
MX = 32
MY = 16
MZ = 16
CH = 32
VMEM_BYTES = 40 * 1024 * 1024
BF = jnp.bfloat16
F32 = jnp.float32


def kept(count, total):
    series = np.arange(count)
    return np.where(series < count // 2, series, total - count + series)


def trig(freqs, places, total):
    angle = 2.0 * np.pi * ((freqs[:, None] * places[None, :]) % total) / total
    return np.cos(angle), np.sin(angle)


def halves(table):
    table = np.asarray(table, np.float64)
    top = table.astype(np.float32).astype(ml_dtypes.bfloat16)
    rest = (table - top.astype(np.float64)).astype(np.float32).astype(ml_dtypes.bfloat16)
    return top, rest


def y_forward_table(y_local, gy, group):
    out = np.zeros((gy, 2, group, MY, group, y_local))
    for g in range(gy):
        c, s = trig(kept(MY, y_local * gy), g * y_local + np.arange(y_local), y_local * gy)
        for i in range(group):
            out[g, 0, i, :, i] = c
            out[g, 1, i, :, i] = s
    return out.reshape(gy, 2 * group * MY, group * y_local)


def x_forward_table():
    c, s = trig(np.arange(MX), np.arange(NX), NX)
    out = np.zeros((2, 2, NX, 2, 2, MX))
    for p in range(2):
        out[p, 0, :, p, 0] = c.T
        out[p, 0, :, p, 1] = -s.T
        out[p, 1, :, p, 0] = -s.T
        out[p, 1, :, p, 1] = -c.T
    return out.reshape(4, NX, 4 * MX)


def x_inverse_table(scale):
    c, s = trig(np.arange(MX), np.arange(NX), NX)
    w = np.where(np.arange(MX) == 0, 1.0, 2.0)[:, None] * scale
    out = np.zeros((2, 2, 2, MX, 2, NX))
    for p in range(2):
        out[p, p, 0, :, 0] = w * c
        out[p, p, 1, :, 0] = -w * s
        out[p, p, 0, :, 1] = w * s
        out[p, p, 1, :, 1] = w * c
    return out.reshape(2, 4 * MX, 2 * NX)


def y_inverse_table(y_local, gy, group):
    out = np.zeros((gy, group, y_local, 2, group, MY))
    for g in range(gy):
        c, s = trig(kept(MY, y_local * gy), g * y_local + np.arange(y_local), y_local * gy)
        for i in range(group):
            out[g, i, :, 0, i] = c.T
            out[g, i, :, 1, i] = -s.T
    return out.reshape(gy, group * y_local, 2 * group * MY)


def z_tables(gz, gy, rows, scale):
    c, s = trig(kept(MZ, gz), np.arange(gz), gz)
    eye = np.eye(rows)
    one = np.ones(gy)
    both = np.stack([c, s])
    fwd = np.einsum("tqz,g,jk->tqjzgk", both, one, eye) * scale
    inv = np.einsum("tqz,g,jk->tzgjqk", both, one, eye)
    return fwd.reshape(2 * MZ * rows, gz * gy * rows), inv.reshape(2 * gz * gy * rows, MZ * rows)


def parts(value):
    top = value.astype(BF)
    return top, (value - top.astype(F32)).astype(BF)


def dot(a, b):
    return jnp.dot(a, b, preferred_element_type=F32)


def dot3(a, b):
    return dot(a[0], b[0]) + (dot(a[0], b[1]) + dot(a[1], b[0]))


def forward_kernel(group, _, field, y_top, y_rest, x_top, x_rest, out):
    y_table = (y_top[0], y_rest[0])
    half = group * MY
    total = jnp.zeros((half, 4 * MX), F32)
    for p in range(2):
        rows = jnp.concatenate([field[2 * i + p] for i in range(group)], axis=0)
        turned = dot3(y_table, parts(rows))
        for t in range(2):
            piece = parts(turned[t * half : (t + 1) * half])
            total = total + dot3(piece, (x_top[2 * p + t], x_rest[2 * p + t]))
    out[...] = total.reshape(group, MY, 4 * MX)


def swap_parts(value):
    lane = lax.broadcasted_iota(jnp.int32, value.shape, 1)
    is_real = (lane // MX) % 2 == 0
    return jnp.where(is_real, pltpu.roll(value, 4 * MX - MX, 1), pltpu.roll(value, MX, 1)), is_real


def filter_kernel(arrived, gain_same, gain_cross, f_top, f_rest, i_top, i_rest, out):
    half = f_top.shape[0] // 2
    turned = dot3((f_top[...], f_rest[...]), parts(arrived[...]))
    crossed, is_real = swap_parts(turned[half:])
    modes = turned[:half] + jnp.where(is_real, crossed, -crossed)
    crossed, _ = swap_parts(modes)
    filtered = modes * gain_same[...] + crossed * gain_cross[...]
    half = i_top.shape[0] // 2
    back = dot3((i_top[...], i_rest[...]), parts(filtered))
    crossed, is_real = swap_parts(back[half:])
    out[...] = back[:half] + jnp.where(is_real, -crossed, crossed)


def inverse_kernel(group, _, modes, base, bias, x_top, x_rest, y_top, y_rest, out):
    step = pl.program_id(0)
    y_table = (y_top[0], y_rest[0])
    rows = parts(modes[...].reshape(group * MY, 4 * MX))
    y_local = out.shape[1]
    for p in range(2):
        wide = dot3(rows, (x_top[p], x_rest[p]))
        tall = jnp.concatenate([wide[:, :NX], wide[:, NX:]], axis=0)
        planes = dot3(y_table, parts(tall)).reshape(group, y_local, NX)
        for i in range(group):
            c = 2 * i + p
            out[c] = planes[i] + (base[c] + bias[step * 2 * group + c])


def conv_kernel(top_tile, bottom_tile, weight, point, main, above, below, down, mid, up, shifted, depth):
    rows = main.shape[1]

    def load(c, _):
        if top_tile:
            first = above[c, 7:8, :]
        else:
            first = above[pl.ds(c, 1), :]
        if bottom_tile:
            last = below[c, 0:1, :]
        else:
            last = below[pl.ds(c, 1), :]
        centre = main[c]
        for e, turn in ((0, 1), (1, 0), (2, NX - 1)):
            for place, value in ((pl.ds(7, 1), first), (pl.ds(8, rows), centre), (pl.ds(8 + rows, 1), last)):
                shifted[e, c, place, :] = pltpu.roll(value, turn, 1) if turn else value
        return 0

    lax.fori_loop(0, CH, load, 0)

    def taps(c, _):
        sums = [None, None, None]
        for e in range(3):
            for b in range(3):
                value = shifted[e, c, pl.ds(7 + b, rows), :]
                for a in range(3):
                    term = weight[c * 27 + a * 9 + b * 3 + e] * value
                    sums[a] = term if sums[a] is None else sums[a] + term
        for a in range(3):
            depth[a, c] = sums[a]
        return 0

    lax.fori_loop(0, CH, taps, 0)

    spread = (
        lax.broadcasted_iota(jnp.int32, (8 * CH, CH), 0) // 8
        == lax.broadcasted_iota(jnp.int32, (8 * CH, CH), 1)
    ).astype(BF)
    gather = (
        lax.broadcasted_iota(jnp.int32, (CH, 8 * CH), 1) // 8
        == lax.broadcasted_iota(jnp.int32, (CH, 8 * CH), 0)
    ).astype(BF)
    same = (
        lax.broadcasted_iota(jnp.int32, (8 * CH, 8 * CH), 0) % 8
        == lax.broadcasted_iota(jnp.int32, (8 * CH, 8 * CH), 1) % 8
    )
    mix = tuple(
        jnp.where(same, dot(dot(spread, part).astype(BF), gather), 0.0).astype(BF)
        for part in parts(point[...])
    )
    for a, out in ((0, down), (1, mid), (2, up)):
        for t in range(rows // 8):
            tile = depth[a, :, pl.ds(8 * t, 8), :].reshape(8 * CH, NX)
            out[:, pl.ds(8 * t, 8), :] = dot3(mix, parts(tile)).reshape(CH, 8, NX)


def finish_kernel(aliased, base, low, high, *rest):
    out = rest[-1]
    total = base[...] + (low[...] + high[...])
    out[...] = 0.5 * total * (1.0 + lax.erf(total * (1.0 / math.sqrt(2.0))))


def params():
    return pltpu.CompilerParams(vmem_limit_bytes=VMEM_BYTES)


def cost(flops, moved):
    return pl.CostEstimate(flops=flops, bytes_accessed=moved, transcendentals=0)


def forward_call(field, place, gy):
    y_local = field.shape[1]
    group = max(1, min(CH // 2, 256 // y_local))
    y_tab = halves(y_forward_table(y_local, gy, group))
    x_tab = halves(x_forward_table())
    tall, wide = y_tab[0].shape[1:]
    y_spec = pl.BlockSpec((1, tall, wide), lambda i, s: (s[0], 0, 0))
    x_spec = pl.BlockSpec((4, NX, 4 * MX), lambda i, s: (0, 0, 0))
    return pl.pallas_call(
        functools.partial(forward_kernel, group),
        out_shape=jax.ShapeDtypeStruct((CH // 2, MY, 4 * MX), F32),
        grid_spec=pltpu.PrefetchScalarGridSpec(
            num_scalar_prefetch=1,
            grid=(CH // 2 // group,),
            in_specs=[
                pl.BlockSpec((2 * group, y_local, NX), lambda i, s: (i, 0, 0)),
                y_spec, y_spec, x_spec, x_spec,
            ],
            out_specs=pl.BlockSpec((group, MY, 4 * MX), lambda i, s: (i, 0, 0)),
        ),
        compiler_params=params(),
        cost_estimate=cost(2 * 10**9, 4 * 2**20),
        name="forward_modes",
    )(place, field, *y_tab, *x_tab)


def filter_call(arrived, gains, gz, gy, scale):
    rows = gains.shape[2]
    fwd, inv = z_tables(gz, gy, rows, scale)
    fwd, inv = halves(fwd), halves(inv)
    split = gains.reshape(2, MZ * rows, 2, 1, MX)
    same = jnp.concatenate([split[0], split[0]], axis=2).reshape(MZ * rows, 4 * MX)
    cross = jnp.concatenate([-split[1], split[1]], axis=2).reshape(MZ * rows, 4 * MX)
    return pl.pallas_call(
        filter_kernel,
        out_shape=jax.ShapeDtypeStruct(arrived.shape, F32),
        compiler_params=params(),
        cost_estimate=cost(2 * 10**8, 2**20),
        name="filter_modes",
    )(arrived, same, cross, *fwd, *inv)


def inverse_call(modes, base, bias, place, gy, scale):
    y_local = base.shape[1]
    group = 8
    x_tab = halves(x_inverse_table(scale))
    y_tab = halves(y_inverse_table(y_local, gy, group))
    tall, wide = y_tab[0].shape[1:]
    y_spec = pl.BlockSpec((1, tall, wide), lambda i, s: (s[0], 0, 0))
    x_spec = pl.BlockSpec((2, 4 * MX, 2 * NX), lambda i, s: (0, 0, 0))
    plane = pl.BlockSpec((2 * group, y_local, NX), lambda i, s: (i, 0, 0))
    return pl.pallas_call(
        functools.partial(inverse_kernel, group),
        out_shape=jax.ShapeDtypeStruct(base.shape, F32),
        grid_spec=pltpu.PrefetchScalarGridSpec(
            num_scalar_prefetch=1,
            grid=(CH // 2 // group,),
            in_specs=[
                pl.BlockSpec((group, MY, 4 * MX), lambda i, s: (i, 0, 0)),
                plane,
                pl.BlockSpec(memory_space=pltpu.SMEM),
                x_spec, x_spec, y_spec, y_spec,
            ],
            out_specs=plane,
        ),
        compiler_params=params(),
        cost_estimate=cost(2 * 10**9, 6 * 2**20),
        name="inverse_modes",
    )(place, modes, base, bias, *x_tab, *y_tab)


def conv_call(field, above, below, weight, point, start, rows):
    y_local = field.shape[1]
    top_tile, bottom_tile = start > 0, start + rows < y_local
    whole = pl.BlockSpec((CH, rows, NX), lambda i: (0, 0, 0))
    edge = pl.BlockSpec((CH, NX), lambda i: (0, 0))
    tile = lambda at: pl.BlockSpec((CH, 8, NX), lambda i: (0, at, 0))
    return pl.pallas_call(
        functools.partial(conv_kernel, top_tile, bottom_tile),
        out_shape=[jax.ShapeDtypeStruct((CH, rows, NX), F32)] * 3,
        grid=(1,),
        in_specs=[
            pl.BlockSpec(memory_space=pltpu.SMEM),
            pl.BlockSpec((CH, CH), lambda i: (0, 0)),
            pl.BlockSpec((CH, rows, NX), lambda i: (0, start // rows, 0)),
            tile(start // 8 - 1) if top_tile else edge,
            tile((start + rows) // 8) if bottom_tile else edge,
        ],
        out_specs=[whole] * 3,
        scratch_shapes=[
            pltpu.VMEM((3, CH, rows + 16, NX), F32),
            pltpu.VMEM((3, CH, rows, NX), F32),
        ],
        compiler_params=params(),
        cost_estimate=cost(2 * 10**9, 4 * 2**20),
        name="mixed_planes",
    )(weight, point, field, field if top_tile else above, field if bottom_tile else below)


def finish_call(base, low, high, so_far, start, rows):
    block = pl.BlockSpec((CH, 8, NX), lambda i: (0, start // 8 + i, 0))
    piece = pl.BlockSpec((CH, 8, NX), lambda i: (0, i, 0))
    operands, specs, alias = [base, low, high], [block, piece, piece], {}
    if so_far is not None:
        operands.append(so_far)
        specs.append(pl.BlockSpec(memory_space=pl.ANY))
        alias = {3: 0}
    return pl.pallas_call(
        functools.partial(finish_kernel, bool(alias)),
        out_shape=jax.ShapeDtypeStruct(base.shape, F32),
        grid=(rows // 8,),
        in_specs=specs,
        out_specs=block,
        input_output_aliases=alias,
        compiler_params=params(),
        cost_estimate=cost(10**9, 4 * rows * CH * NX * 4),
        name="finished_rows",
    )(*operands)


def general_filter(coarse, gains, gz, gy, scale):
    j_own, n_own = gains.shape[2], gains.shape[3]
    both = ("gz", "gy")
    flat = coarse.reshape(CH // 2, MY, 2, 2, MX).transpose(3, 1, 0, 2, 4).reshape(2, MY, CH * MX)
    sent = flat.reshape(2, gy, j_own, gz, n_own).transpose(3, 1, 0, 2, 4).reshape(gz * gy, -1)
    got = lax.all_to_all(sent, both, split_axis=0, concat_axis=0, tiled=True)
    got = got.reshape(gz, gy, 2, j_own, n_own)
    c, s = (jnp.asarray(t, F32) for t in trig(kept(MZ, gz), np.arange(gz), gz))
    mul = functools.partial(jnp.einsum, precision=lax.Precision.HIGHEST)
    whole = got.sum(axis=1) * scale
    real = mul("zjn,qz->qjn", whole[:, 0], c) + mul("zjn,qz->qjn", whole[:, 1], s)
    imag = mul("zjn,qz->qjn", whole[:, 1], c) - mul("zjn,qz->qjn", whole[:, 0], s)
    real, imag = real * gains[0] - imag * gains[1], real * gains[1] + imag * gains[0]
    out = jnp.stack(
        [
            mul("qjn,qz->zjn", real, c) - mul("qjn,qz->zjn", imag, s),
            mul("qjn,qz->zjn", real, s) + mul("qjn,qz->zjn", imag, c),
        ],
        axis=1,
    )
    out = jnp.broadcast_to(out[:, None], (gz, gy, 2, j_own, n_own)).reshape(gz * gy, -1)
    back = lax.all_to_all(out, both, split_axis=0, concat_axis=0, tiled=True)
    back = back.reshape(gz, gy, 2, j_own, n_own).transpose(2, 1, 3, 0, 4)
    back = back.reshape(2, MY, CH // 2, 2, MX)
    return back.transpose(2, 1, 3, 0, 4).reshape(CH // 2, MY, 4 * MX)


def body(field, spectral_filter, depth_weight, point_weight, bias_vector):
    gz, gy = lax.axis_size("gz"), lax.axis_size("gy")
    y_local = field.shape[2]
    place = lax.axis_index("gy").astype(jnp.int32).reshape(1)
    field = field.reshape(CH, y_local, NX)
    weight = depth_weight.reshape(-1)
    y_total = gy * y_local
    forward_scale = 1.0 / math.sqrt(float(NX) * y_total * gz)
    inverse_scale = 1.0 / math.sqrt(2.0 * MX * MY * MZ)

    def ring(axis, count, by):
        return [(i, (i + by) % count) for i in range(count)]

    above = lax.ppermute(field[:, y_local - 1, :], "gy", ring("gy", gy, 1))
    below = lax.ppermute(field[:, 0, :], "gy", ring("gy", gy, -1))

    rows = max(8, y_local // 4)
    starts = list(range(0, y_local, rows))
    order = sorted(starts, key=lambda s: (s == 0 or s + rows == y_local, s))
    pieces = {}
    mids = {}
    for start in order:
        down, mid, up = conv_call(field, above, below, weight, point_weight, start, rows)
        mids[start] = mid
        pieces[start] = (
            lax.ppermute(down, "gz", ring("gz", gz, 1)),
            lax.ppermute(up, "gz", ring("gz", gz, -1)),
        )

    coarse = forward_call(field, place, gy)
    j_own, n_own = spectral_filter.shape[2], spectral_filter.shape[3]
    if j_own == 8 and n_own == 2 * MX:
        both = ("gz", "gy")
        sent = coarse.reshape(gz * gy * 8, 4 * MX)
        got = lax.all_to_all(sent, both, split_axis=0, concat_axis=0, tiled=True)
        out = filter_call(got, spectral_filter, gz, gy, forward_scale)
        back = lax.all_to_all(out, both, split_axis=0, concat_axis=0, tiled=True)
        back = back.reshape(CH // 2, MY, 4 * MX)
    else:
        back = general_filter(coarse, spectral_filter, gz, gy, forward_scale)

    base = jnp.concatenate([mids[s] for s in starts], axis=1)
    base = inverse_call(back, base, bias_vector, place, gy, inverse_scale)
    result = None
    for start in order:
        result = finish_call(base, *pieces[start], result, start, rows)
    return result.reshape(CH, 1, y_local, NX)


def solution(mesh):
    in_specs = (P(None, "gz", "gy", None), P(None, None, "gy", "gz"), P(), P(), P())
    out_specs = P(None, "gz", "gy", None)
    return jax.shard_map(body, mesh=mesh, in_specs=in_specs, out_specs=out_specs, check_vma=False)
```

```python
import functools
import math

import jax
import jax.numpy as jnp
import ml_dtypes
import numpy as np
from jax import lax
from jax.experimental import pallas as pl
from jax.experimental.pallas import tpu as pltpu
from jax.sharding import PartitionSpec as P

NX = 256
MX = 32
MY = 16
MZ = 16
CH = 32
VMEM_BYTES = 58 * 1024 * 1024
BF = jnp.bfloat16
F32 = jnp.float32


def kept(count, total):
    series = np.arange(count)
    return np.where(series < count // 2, series, total - count + series)


def trig(freqs, places, total):
    angle = 2.0 * np.pi * ((freqs[:, None] * places[None, :]) % total) / total
    return np.cos(angle), np.sin(angle)


def halves(table):
    table = np.asarray(table, np.float64)
    top = table.astype(np.float32).astype(ml_dtypes.bfloat16)
    rest = (table - top.astype(np.float64)).astype(np.float32).astype(ml_dtypes.bfloat16)
    return top, rest


def y_forward_table(y_local, gy, group):
    out = np.zeros((gy, 2, group, MY, group, y_local))
    for g in range(gy):
        c, s = trig(kept(MY, y_local * gy), g * y_local + np.arange(y_local), y_local * gy)
        for i in range(group):
            out[g, 0, i, :, i] = c
            out[g, 1, i, :, i] = s
    return out.reshape(gy, 2 * group * MY, group * y_local)


def x_forward_table():
    c, s = trig(np.arange(MX), np.arange(NX), NX)
    out = np.zeros((2, 2, NX, 2, 2, MX))
    for p in range(2):
        out[p, 0, :, p, 0] = c.T
        out[p, 0, :, p, 1] = -s.T
        out[p, 1, :, p, 0] = -s.T
        out[p, 1, :, p, 1] = -c.T
    return out.reshape(4, NX, 4 * MX)


def x_inverse_table(scale):
    c, s = trig(np.arange(MX), np.arange(NX), NX)
    w = np.where(np.arange(MX) == 0, 1.0, 2.0)[:, None] * scale
    out = np.zeros((2, 2, 2, MX, 2, NX))
    for p in range(2):
        out[p, p, 0, :, 0] = w * c
        out[p, p, 1, :, 0] = -w * s
        out[p, p, 0, :, 1] = w * s
        out[p, p, 1, :, 1] = w * c
    return out.reshape(2, 4 * MX, 2 * NX)


def y_inverse_table(y_local, gy, group):
    out = np.zeros((gy, group, y_local, 2, group, MY))
    for g in range(gy):
        c, s = trig(kept(MY, y_local * gy), g * y_local + np.arange(y_local), y_local * gy)
        for i in range(group):
            out[g, i, :, 0, i] = c.T
            out[g, i, :, 1, i] = -s.T
    return out.reshape(gy, group * y_local, 2 * group * MY)


def z_tables(gz, gy, rows, scale):
    c, s = trig(kept(MZ, gz), np.arange(gz), gz)
    eye = np.eye(rows)
    one = np.ones(gy)
    both = np.stack([c, s])
    fwd = np.einsum("tqz,g,jk->tqjzgk", both, one, eye) * scale
    inv = np.einsum("tqz,g,jk->tzgjqk", both, one, eye)
    return fwd.reshape(2 * MZ * rows, gz * gy * rows), inv.reshape(2 * gz * gy * rows, MZ * rows)


def parts(value):
    top = value.astype(BF)
    return top, (value - top.astype(F32)).astype(BF)


def dot(a, b):
    return jnp.dot(a, b, preferred_element_type=F32)


def dot3(a, b):
    rows = a[0].shape[0]
    both = dot(jnp.concatenate([a[0], a[1]], axis=0), b[0])
    return both[:rows] + (both[rows:] + dot(a[0], b[1]))


def forward_kernel(group, _, field, y_top, y_rest, x_top, x_rest, out, edges):
    y_table = (y_top[0], y_rest[0])
    half = group * MY
    total = jnp.zeros((half, 4 * MX), F32)
    for p in range(2):
        rows = jnp.concatenate([field[2 * i + p] for i in range(group)], axis=0)
        turned = dot3(y_table, parts(rows))
        for t in range(2):
            piece = parts(turned[t * half : (t + 1) * half])
            total = total + dot3(piece, (x_top[2 * p + t], x_rest[2 * p + t]))
    out[...] = total.reshape(group, MY, 4 * MX)
    last = field.shape[1] - 1
    for i in range(2 * group):
        edges[0, i : i + 1, :] = field[i, last : last + 1, :]
        edges[1, i : i + 1, :] = field[i, 0:1, :]


def swap_parts(value):
    lane = lax.broadcasted_iota(jnp.int32, value.shape, 1)
    is_real = (lane // MX) % 2 == 0
    return jnp.where(is_real, pltpu.roll(value, 4 * MX - MX, 1), pltpu.roll(value, MX, 1)), is_real


def filter_kernel(arrived, gains, f_top, f_rest, i_top, i_rest, out):
    real, imag = (gains[r].reshape(-1, 2 * MX) for r in range(2))
    first, second = slice(0, MX), slice(MX, 2 * MX)
    same = jnp.concatenate([real[:, first], real[:, first], real[:, second], real[:, second]], axis=1)
    cross = jnp.concatenate([-imag[:, first], imag[:, first], -imag[:, second], imag[:, second]], axis=1)
    half = f_top.shape[0] // 2
    turned = dot3((f_top[...], f_rest[...]), parts(arrived[...]))
    crossed, is_real = swap_parts(turned[half:])
    modes = turned[:half] + jnp.where(is_real, crossed, -crossed)
    crossed, _ = swap_parts(modes)
    filtered = modes * same + crossed * cross
    half = i_top.shape[0] // 2
    back = dot3((i_top[...], i_rest[...]), parts(filtered))
    crossed, is_real = swap_parts(back[half:])
    out[...] = back[:half] + jnp.where(is_real, -crossed, crossed)


def conv_kernel(inner, rows, weight, point, *refs):
    if inner:
        above, first, second, below = refs[:4]
        segments = ((8, 2 * rows, 0),)
        blocks = ((above, 0, 8), (first, 8, rows), (second, 8 + rows, rows), (below, 8 + 2 * rows, 8))
        refs = refs[4:]
    else:
        halo, first, below, above, second = refs[:5]
        start = rows + 24
        segments = ((8, rows, 0), (start, rows, rows))
        blocks = ((first, 8, rows), (below, 8 + rows, 8), (above, start - 8, 8), (second, start, rows))
        refs = refs[5:]
    outs, (shifted, depth) = refs[:3], refs[3:]
    turns = (1, 0, NX - 1)
    step = 8

    def load(i, _):
        c = pl.multiple_of(i * step, step)
        for ref, at, count in blocks:
            value = ref[pl.ds(c, step)].reshape(step * count, NX)
            for e, turn in enumerate(turns):
                moved = pltpu.roll(value, turn, 1) if turn else value
                for h in range(2):
                    shifted[e, h, pl.ds(c, step), pl.ds(at, count), :] = moved[
                        :, 128 * h : 128 * h + 128
                    ].reshape(step, count, 128)
        return 0

    lax.fori_loop(0, CH // step, load, 0)
    if not inner:
        for side, at in ((0, 7), (1, start + rows)):
            value = halo[side]
            for e, turn in enumerate(turns):
                moved = pltpu.roll(value, turn, 1) if turn else value
                for h in range(2):
                    shifted[e, h, :, pl.ds(at, 1), :] = moved[:, 128 * h : 128 * h + 128].reshape(CH, 1, 128)

    def taps(c, _):
        gain = [weight[c, k] for k in range(27)]
        for at, count, to in segments:
            for h in range(2):
                for part in range(0, count, 16):
                    size = min(16, count - part)
                    sums = [None, None, None]
                    for e in range(3):
                        for b in range(3):
                            value = shifted[e, h, c, pl.ds(at + part + b - 1, size), :]
                            for a in range(3):
                                term = gain[a * 9 + b * 3 + e] * value
                                sums[a] = term if sums[a] is None else sums[a] + term
                    for a in range(3):
                        depth[a, c, pl.ds(to + part, size), pl.ds(128 * h, 128)] = sums[a]
        return 0

    lax.fori_loop(0, CH, taps, 0, unroll=2)

    spread = (
        lax.broadcasted_iota(jnp.int32, (8 * CH, CH), 0) // 8
        == lax.broadcasted_iota(jnp.int32, (8 * CH, CH), 1)
    ).astype(BF)
    gather = (
        lax.broadcasted_iota(jnp.int32, (CH, 8 * CH), 1) // 8
        == lax.broadcasted_iota(jnp.int32, (CH, 8 * CH), 0)
    ).astype(BF)
    same = (
        lax.broadcasted_iota(jnp.int32, (8 * CH, 8 * CH), 0) % 8
        == lax.broadcasted_iota(jnp.int32, (8 * CH, 8 * CH), 1) % 8
    )
    mix = tuple(
        jnp.where(same, dot(dot(spread, part).astype(BF), gather), 0.0).astype(BF)
        for part in parts(point[...])
    )
    for t in range(2 * rows // 8):
        for a, out in enumerate(outs):
            tile = depth[a, :, pl.ds(8 * t, 8), :].reshape(8 * CH, NX)
            out[:, pl.ds(8 * t, 8), :] = dot3(mix, parts(tile)).reshape(CH, 8, NX)


def gelu(value):
    return 0.5 * value * (1.0 + lax.erf(value * (1.0 / math.sqrt(2.0))))


def inverse_kernel(group, _, modes, inner, outer, low, high, bias, x_top, x_rest, y_top, y_rest, out):
    step = pl.program_id(0)
    y_table = (y_top[0], y_rest[0])
    mode_rows = parts(modes[...].reshape(group * MY, 4 * MX))
    y_local = out.shape[1]
    rows = y_local // 4
    for p in range(2):
        wide = dot3(mode_rows, (x_top[p], x_rest[p]))
        tall = jnp.concatenate([wide[:, :NX], wide[:, NX:]], axis=0)
        planes = dot3(y_table, parts(tall)).reshape(group, y_local, NX)
        for i in range(group):
            c = 2 * i + p
            plane = planes[i] + bias[step * 2 * group + c]
            out[c, :rows] = plane[:rows] + outer[c, :rows]
            out[c, 3 * rows :] = plane[3 * rows :] + outer[c, rows:]
            out[c, rows : 3 * rows] = gelu(plane[rows : 3 * rows] + (inner[c] + (low[c] + high[c])))


def finish_kernel(base, low, high, out):
    out[...] = gelu(base[...] + (low[...] + high[...]))


def params():
    return pltpu.CompilerParams(vmem_limit_bytes=VMEM_BYTES)


def cost(flops, moved):
    return pl.CostEstimate(flops=flops, bytes_accessed=moved, transcendentals=0)


def forward_call(field, place, gy):
    y_local = field.shape[1]
    group = max(1, min(CH // 2, 256 // y_local))
    y_tab = halves(y_forward_table(y_local, gy, group))
    x_tab = halves(x_forward_table())
    tall, wide = y_tab[0].shape[1:]
    y_spec = pl.BlockSpec((1, tall, wide), lambda i, s: (s[0], 0, 0))
    x_spec = pl.BlockSpec((4, NX, 4 * MX), lambda i, s: (0, 0, 0))
    return pl.pallas_call(
        functools.partial(forward_kernel, group),
        out_shape=[
            jax.ShapeDtypeStruct((CH // 2, MY, 4 * MX), F32),
            jax.ShapeDtypeStruct((2, CH, NX), F32),
        ],
        grid_spec=pltpu.PrefetchScalarGridSpec(
            num_scalar_prefetch=1,
            grid=(CH // 2 // group,),
            in_specs=[
                pl.BlockSpec((2 * group, y_local, NX), lambda i, s: (i, 0, 0)),
                y_spec, y_spec, x_spec, x_spec,
            ],
            out_specs=[
                pl.BlockSpec((group, MY, 4 * MX), lambda i, s: (i, 0, 0)),
                pl.BlockSpec((2, 2 * group, NX), lambda i, s: (0, i, 0)),
            ],
        ),
        compiler_params=params(),
        cost_estimate=cost(2 * 10**9, 4 * 2**20),
        name="forward_modes",
    )(place, field, *y_tab, *x_tab)


def filter_call(arrived, gains, gz, gy, scale):
    fwd, inv = z_tables(gz, gy, gains.shape[2], scale)
    fwd, inv = halves(fwd), halves(inv)
    return pl.pallas_call(
        filter_kernel,
        out_shape=jax.ShapeDtypeStruct(arrived.shape, F32),
        compiler_params=params(),
        cost_estimate=cost(2 * 10**8, 2**20),
        name="filter_modes",
    )(arrived, gains, *fwd, *inv)


def inverse_call(modes, inner, outer, low, high, bias, place, gy, scale):
    y_local = 2 * inner.shape[1]
    group = 8
    x_tab = halves(x_inverse_table(scale))
    y_tab = halves(y_inverse_table(y_local, gy, group))
    tall, wide = y_tab[0].shape[1:]
    y_spec = pl.BlockSpec((1, tall, wide), lambda i, s: (s[0], 0, 0))
    x_spec = pl.BlockSpec((2, 4 * MX, 2 * NX), lambda i, s: (0, 0, 0))
    half = pl.BlockSpec((2 * group, y_local // 2, NX), lambda i, s: (i, 0, 0))
    return pl.pallas_call(
        functools.partial(inverse_kernel, group),
        out_shape=jax.ShapeDtypeStruct((CH, y_local, NX), F32),
        grid_spec=pltpu.PrefetchScalarGridSpec(
            num_scalar_prefetch=1,
            grid=(CH // 2 // group,),
            in_specs=[
                pl.BlockSpec((group, MY, 4 * MX), lambda i, s: (i, 0, 0)),
                half, half, half, half,
                pl.BlockSpec(memory_space=pltpu.SMEM),
                x_spec, x_spec, y_spec, y_spec,
            ],
            out_specs=pl.BlockSpec((2 * group, y_local, NX), lambda i, s: (i, 0, 0)),
        ),
        compiler_params=params(),
        cost_estimate=cost(4 * 10**9, 6 * 2**20),
        name="inverse_modes",
    )(place, modes, inner, outer, low, high, bias, *x_tab, *y_tab)


def conv_call(field, halo, weight, point, inner):
    rows = field.shape[1] // 4
    tile = lambda at: pl.BlockSpec((CH, 8, NX), lambda i: (0, at, 0))
    quarter = lambda at: pl.BlockSpec((CH, rows, NX), lambda i: (0, at, 0))
    first, last = rows // 8, 3 * rows // 8
    if inner:
        specs = [tile(first - 1), quarter(1), quarter(2), tile(last)]
        operands = [field] * 4
    else:
        specs = [pl.BlockSpec((2, CH, NX), lambda i: (0, 0, 0)), quarter(0), tile(first), tile(last - 1), quarter(3)]
        operands = [halo] + [field] * 4
    return pl.pallas_call(
        functools.partial(conv_kernel, inner, rows),
        out_shape=[jax.ShapeDtypeStruct((CH, 2 * rows, NX), F32)] * 3,
        grid=(1,),
        in_specs=[
            pl.BlockSpec(memory_space=pltpu.SMEM),
            pl.BlockSpec((CH, CH), lambda i: (0, 0)),
            *specs,
        ],
        out_specs=[pl.BlockSpec((CH, 2 * rows, NX), lambda i: (0, 0, 0))] * 3,
        scratch_shapes=[
            pltpu.VMEM((3, 2, CH, 2 * rows + 32, 128), F32),
            pltpu.VMEM((3, CH, 2 * rows, NX), F32),
        ],
        compiler_params=params(),
        cost_estimate=cost(2 * 10**9, 4 * 2**20),
        name="mixed_planes",
    )(weight, point, *operands)


def finish_call(result, low, high):
    rows = result.shape[1] // 4
    tiles = rows // 8
    block = pl.BlockSpec((CH, 8, NX), lambda i: (0, i + (i // tiles) * 2 * tiles, 0))
    piece = pl.BlockSpec((CH, 8, NX), lambda i: (0, i, 0))
    return pl.pallas_call(
        finish_kernel,
        out_shape=jax.ShapeDtypeStruct(result.shape, F32),
        grid=(2 * tiles,),
        in_specs=[block, piece, piece],
        out_specs=block,
        input_output_aliases={0: 0},
        compiler_params=params(),
        cost_estimate=cost(10**9, 4 * 2 * rows * CH * NX * 4),
        name="finished_rows",
    )(result, low, high)


def general_filter(coarse, gains, gz, gy, scale):
    j_own, n_own = gains.shape[2], gains.shape[3]
    both = ("gz", "gy")
    flat = coarse.reshape(CH // 2, MY, 2, 2, MX).transpose(3, 1, 0, 2, 4).reshape(2, MY, CH * MX)
    sent = flat.reshape(2, gy, j_own, gz, n_own).transpose(3, 1, 0, 2, 4).reshape(gz * gy, -1)
    got = lax.all_to_all(sent, both, split_axis=0, concat_axis=0, tiled=True)
    got = got.reshape(gz, gy, 2, j_own, n_own)
    c, s = (jnp.asarray(t, F32) for t in trig(kept(MZ, gz), np.arange(gz), gz))
    mul = functools.partial(jnp.einsum, precision=lax.Precision.HIGHEST)
    whole = got.sum(axis=1) * scale
    real = mul("zjn,qz->qjn", whole[:, 0], c) + mul("zjn,qz->qjn", whole[:, 1], s)
    imag = mul("zjn,qz->qjn", whole[:, 1], c) - mul("zjn,qz->qjn", whole[:, 0], s)
    real, imag = real * gains[0] - imag * gains[1], real * gains[1] + imag * gains[0]
    out = jnp.stack(
        [
            mul("qjn,qz->zjn", real, c) - mul("qjn,qz->zjn", imag, s),
            mul("qjn,qz->zjn", real, s) + mul("qjn,qz->zjn", imag, c),
        ],
        axis=1,
    )
    out = jnp.broadcast_to(out[:, None], (gz, gy, 2, j_own, n_own)).reshape(gz * gy, -1)
    back = lax.all_to_all(out, both, split_axis=0, concat_axis=0, tiled=True)
    back = back.reshape(gz, gy, 2, j_own, n_own).transpose(2, 1, 3, 0, 4)
    back = back.reshape(2, MY, CH // 2, 2, MX)
    return back.transpose(2, 1, 3, 0, 4).reshape(CH // 2, MY, 4 * MX)


def body(field, spectral_filter, depth_weight, point_weight, bias_vector):
    gz, gy = lax.axis_size("gz"), lax.axis_size("gy")
    y_local = field.shape[2]
    place = lax.axis_index("gy").astype(jnp.int32).reshape(1)
    field = field.reshape(CH, y_local, NX)
    y_total = gy * y_local
    forward_scale = 1.0 / math.sqrt(float(NX) * y_total * gz)
    inverse_scale = 1.0 / math.sqrt(2.0 * MX * MY * MZ)

    def ring(axis, count, by):
        return [(i, (i + by) % count) for i in range(count)]

    def to_neighbours(down, up):
        return (
            lax.ppermute(down, "gz", ring("gz", gz, 1)),
            lax.ppermute(up, "gz", ring("gz", gz, -1)),
        )

    down, inner, up = conv_call(field, None, depth_weight, point_weight, True)
    inner_low, inner_high = to_neighbours(down, up)
    field, _ = lax.optimization_barrier((field, down))
    coarse, edges = forward_call(field, place, gy)
    if gy == 2:
        halo = lax.ppermute(edges, "gy", ring("gy", gy, 1))
    else:
        halo = jnp.stack(
            [
                lax.ppermute(edges[0], "gy", ring("gy", gy, 1)),
                lax.ppermute(edges[1], "gy", ring("gy", gy, -1)),
            ]
        )
    down, outer, up = conv_call(field, halo, depth_weight, point_weight, False)
    outer_low, outer_high = to_neighbours(down, up)

    j_own, n_own = spectral_filter.shape[2], spectral_filter.shape[3]
    if j_own == 8 and n_own == 2 * MX:
        both = ("gz", "gy")
        sent = coarse.reshape(gz * gy * 8, 4 * MX)
        got = lax.all_to_all(sent, both, split_axis=0, concat_axis=0, tiled=True)
        out = filter_call(got, spectral_filter, gz, gy, forward_scale)
        back = lax.all_to_all(out, both, split_axis=0, concat_axis=0, tiled=True)
        back = back.reshape(CH // 2, MY, 4 * MX)
    else:
        back = general_filter(coarse, spectral_filter, gz, gy, forward_scale)

    result = inverse_call(
        back, inner, outer, inner_low, inner_high, bias_vector, place, gy, inverse_scale
    )
    result = finish_call(result, outer_low, outer_high)
    return result.reshape(CH, 1, y_local, NX)


def solution(mesh):
    in_specs = (P(None, "gz", "gy", None), P(None, None, "gy", "gz"), P(), P(), P())
    out_specs = P(None, "gz", "gy", None)
    return jax.shard_map(body, mesh=mesh, in_specs=in_specs, out_specs=out_specs, check_vma=False)
```

```python
import functools
import math

import jax
import jax.numpy as jnp
import ml_dtypes
import numpy as np
from jax import lax
from jax.experimental import pallas as pl
from jax.experimental.pallas import tpu as pltpu
from jax.sharding import PartitionSpec as P

NX = 256
MX = 32
MY = 16
MZ = 16
CH = 32
VMEM_BYTES = 24 * 1024 * 1024
BF = jnp.bfloat16
F32 = jnp.float32


def kept(count, total):
    series = np.arange(count)
    return np.where(series < count // 2, series, total - count + series)


def trig(freqs, places, total):
    angle = 2.0 * np.pi * ((freqs[:, None] * places[None, :]) % total) / total
    return np.cos(angle), np.sin(angle)


def halves(table):
    table = np.asarray(table, np.float64)
    top = table.astype(np.float32).astype(ml_dtypes.bfloat16)
    rest = (table - top.astype(np.float64)).astype(np.float32).astype(ml_dtypes.bfloat16)
    return jnp.asarray(top), jnp.asarray(rest)


def y_forward_table(y_local, gy, group):
    out = np.zeros((gy, 2, group, MY, group, y_local))
    for g in range(gy):
        c, s = trig(kept(MY, y_local * gy), g * y_local + np.arange(y_local), y_local * gy)
        for i in range(group):
            out[g, 0, i, :, i] = c
            out[g, 1, i, :, i] = s
    return out.reshape(gy, 2 * group * MY, group * y_local)


def x_forward_table():
    c, s = trig(np.arange(MX), np.arange(NX), NX)
    out = np.zeros((2, 2, NX, 2, 2, MX))
    for p in range(2):
        out[p, 0, :, p, 0] = c.T
        out[p, 0, :, p, 1] = -s.T
        out[p, 1, :, p, 0] = -s.T
        out[p, 1, :, p, 1] = -c.T
    return out.reshape(4, NX, 4 * MX)


def x_inverse_table(scale):
    c, s = trig(np.arange(MX), np.arange(NX), NX)
    w = np.where(np.arange(MX) == 0, 1.0, 2.0)[:, None] * scale
    out = np.zeros((2, 2, 2, MX, 2, NX))
    for p in range(2):
        out[p, p, 0, :, 0] = w * c
        out[p, p, 1, :, 0] = -w * s
        out[p, p, 0, :, 1] = w * s
        out[p, p, 1, :, 1] = w * c
    return out.reshape(2, 4 * MX, 2 * NX)


def y_inverse_table(y_local, gy, group):
    out = np.zeros((gy, group, y_local, 2, group, MY))
    for g in range(gy):
        c, s = trig(kept(MY, y_local * gy), g * y_local + np.arange(y_local), y_local * gy)
        for i in range(group):
            out[g, i, :, 0, i] = c.T
            out[g, i, :, 1, i] = -s.T
    return out.reshape(gy, group * y_local, 2 * group * MY)


def z_tables(gz, gy, rows, scale):
    c, s = trig(kept(MZ, gz), np.arange(gz), gz)
    eye = np.eye(rows)
    one = np.ones(gy)
    both = np.stack([c, s])
    fwd = np.einsum("tqz,g,jk->tqjzgk", both, one, eye) * scale
    inv = np.einsum("tqz,g,jk->tzgjqk", both, one, eye)
    return fwd.reshape(2 * MZ * rows, gz * gy * rows), inv.reshape(2 * gz * gy * rows, MZ * rows)


def parts(value):
    top = value.astype(BF)
    return top, (value - top.astype(F32)).astype(BF)


def dot(a, b):
    return jnp.dot(a, b, preferred_element_type=F32)


def dot3(a, b):
    rows = a[0].shape[0]
    both = dot(jnp.concatenate([a[0], a[1]], axis=0), b[0])
    return both[:rows] + (both[rows:] + dot(a[0], b[1]))


def forward_kernel(group, _, field, y_top, y_rest, x_top, x_rest, out, edges, turned):
    y_table = (y_top[0], y_rest[0])
    half = group * MY
    step = pl.program_id(0)
    for p in range(2):
        rows = jnp.concatenate([field[2 * i + p] for i in range(group)], axis=0)
        both = dot3(y_table, parts(rows))
        for t in range(2):
            at = pl.multiple_of(step * half, half)
            turned[2 * p + t, pl.ds(at, half), :] = both[t * half : (t + 1) * half]
    last = field.shape[1] - 1
    for i in range(2 * group):
        edges[0, i : i + 1, :] = field[i, last : last + 1, :]
        edges[1, i : i + 1, :] = field[i, 0:1, :]

    @pl.when(step == pl.num_programs(0) - 1)
    def _():
        total = dot3(parts(turned[0]), (x_top[0], x_rest[0]))
        for k in range(1, 4):
            total = total + dot3(parts(turned[k]), (x_top[k], x_rest[k]))
        out[...] = total.reshape(CH // 2, MY, 4 * MX)


def swap_parts(value):
    lane = lax.broadcasted_iota(jnp.int32, value.shape, 1)
    is_real = (lane // MX) % 2 == 0
    return jnp.where(is_real, pltpu.roll(value, 4 * MX - MX, 1), pltpu.roll(value, MX, 1)), is_real


def filter_kernel(arrived, gains, f_top, f_rest, i_top, i_rest, out):
    real, imag = (gains[r].reshape(-1, 2 * MX) for r in range(2))
    first, second = slice(0, MX), slice(MX, 2 * MX)
    same = jnp.concatenate([real[:, first], real[:, first], real[:, second], real[:, second]], axis=1)
    cross = jnp.concatenate([-imag[:, first], imag[:, first], -imag[:, second], imag[:, second]], axis=1)
    half = f_top.shape[0] // 2
    turned = dot3((f_top[...], f_rest[...]), parts(arrived[...]))
    crossed, is_real = swap_parts(turned[half:])
    modes = turned[:half] + jnp.where(is_real, crossed, -crossed)
    crossed, _ = swap_parts(modes)
    filtered = modes * same + crossed * cross
    half = i_top.shape[0] // 2
    back = dot3((i_top[...], i_rest[...]), parts(filtered))
    crossed, is_real = swap_parts(back[half:])
    out[...] = back[:half] + jnp.where(is_real, -crossed, crossed)


def conv_kernel(count, weight, point, *refs):
    tiles, refs = refs[: 2 * (count + 2)], refs[2 * (count + 2) :]
    halo = None
    if len(refs) == 7:
        halo, refs = refs[0], refs[1:]
    outs, (turned, depth, gains) = refs[:3], refs[3:]
    tiles = [[t.reshape(CH * 8, 128) for t in tiles[2 * i : 2 * i + 2]] for i in range(count + 2)]

    def row(tile, r):
        return jnp.concatenate([half[pl.ds(r, CH, stride=8), :] for half in tile], axis=1)

    if halo is None:
        segments = [([lambda: row(tiles[0], 7)], tiles[1:-1], [lambda: row(tiles[-1], 0)])]
    else:
        top, under, over, bottom = tiles
        segments = [
            ([lambda: halo[0]], [top], [lambda: row(under, 0)]),
            ([lambda: row(over, 7)], [bottom], [lambda: halo[1]]),
        ]
    runs, at, done = [], 0, 0
    for before, whole, after in segments:
        makers = before + [functools.partial(row, t, r) for t in whole for r in range(8)] + after
        for i, make in enumerate(makers):
            value = make()
            turned[0, at + i] = pltpu.roll(value, 1, 1)
            turned[1, at + i] = value
            turned[2, at + i] = pltpu.roll(value, NX - 1, 1)
        runs.append((at, done, 8 * len(whole)))
        at, done = at + len(makers), done + 8 * len(whole)
    for k in range(27):
        gains[k] = jnp.broadcast_to(weight[:, k : k + 1], (CH, 128))

    def taps(i, _):
        chans = pl.ds(pl.multiple_of(i * 8, 8), 8)
        gain = [gains[k, chans, :] for k in range(27)]
        for h in range(2):
            lanes = pl.ds(128 * h, 128)
            for first, to, rows in runs:
                sums = {}
                for r in range(rows + 2):
                    values = [turned[e, first + r, chans, lanes] for e in range(3)]
                    for b in range(3):
                        o = r - b
                        if o < 0 or o >= rows:
                            continue
                        for a in range(3):
                            for e in range(3):
                                term = gain[a * 9 + b * 3 + e] * values[e]
                                sums[o, a] = sums[o, a] + term if (o, a) in sums else term
                    if r >= 2:
                        for a in range(3):
                            depth[a, to + r - 2, chans, lanes] = sums.pop((r - 2, a))
        return 0

    lax.fori_loop(0, CH // 8, taps, 0)

    down = (
        lax.broadcasted_iota(jnp.int32, (8 * CH, CH), 0) // 8
        == lax.broadcasted_iota(jnp.int32, (8 * CH, CH), 1)
    ).astype(BF)
    across = (
        lax.broadcasted_iota(jnp.int32, (CH, 8 * CH), 1) % CH
        == lax.broadcasted_iota(jnp.int32, (CH, 8 * CH), 0)
    ).astype(BF)
    same = (
        lax.broadcasted_iota(jnp.int32, (8 * CH, 8 * CH), 0) % 8
        == lax.broadcasted_iota(jnp.int32, (8 * CH, 8 * CH), 1) // CH
    )
    mix = tuple(
        jnp.where(same, dot(dot(down, part).astype(BF), across), 0.0).astype(BF)
        for part in parts(point[...])
    )
    for t in range(done // 8):
        for a, out in enumerate(outs):
            tile = depth[a, pl.ds(8 * t, 8)].reshape(8 * CH, NX)
            out[:, pl.ds(8 * t, 8), :] = dot3(mix, parts(tile)).reshape(CH, 8, NX)


def gelu(value):
    return 0.5 * value * (1.0 + lax.erf(value * (1.0 / math.sqrt(2.0))))


def inverse_kernel(group, chunks, _, modes, bias, x_top, x_rest, y_top, y_rest, outer, *refs):
    out = refs[-1]
    step = pl.program_id(0)
    y_table = (y_top[0], y_rest[0])
    mode_rows = parts(modes[...].reshape(group * MY, 4 * MX))
    y_local = out.shape[1]
    for p in range(2):
        wide = dot3(mode_rows, (x_top[p], x_rest[p]))
        tall = jnp.concatenate([wide[:, :NX], wide[:, NX:]], axis=0)
        planes = dot3(y_table, parts(tall)).reshape(group, y_local, NX)
        for i in range(group):
            c = 2 * i + p
            plane = planes[i] + bias[step * 2 * group + c]
            out[c, :8] = plane[:8] + outer[c, :8]
            out[c, y_local - 8 :] = plane[y_local - 8 :] + outer[c, 8:]
            for k, (first, count) in enumerate(chunks):
                rows = slice(8 * first, 8 * (first + count))
                own, low, high = refs[3 * k : 3 * k + 3]
                out[c, rows] = gelu(plane[rows] + (own[c] + (low[c] + high[c])))


def finish_kernel(base, low, high, out):
    out[...] = gelu(base[...] + (low[...] + high[...]))


def in_hbm(*arrays):
    return [pltpu.with_memory_space_constraint(a, pltpu.HBM) for a in arrays]


def params():
    return pltpu.CompilerParams(vmem_limit_bytes=VMEM_BYTES)


def cost(flops, moved):
    return pl.CostEstimate(flops=flops, bytes_accessed=moved, transcendentals=0)


def forward_call(field, place, gy):
    y_local = field.shape[1]
    group = max(1, min(CH // 2, 256 // y_local))
    y_tab = halves(y_forward_table(y_local, gy, group))
    x_tab = halves(x_forward_table())
    tall, wide = y_tab[0].shape[1:]
    y_spec = pl.BlockSpec((1, tall, wide), lambda i, s: (s[0], 0, 0))
    x_spec = pl.BlockSpec((4, NX, 4 * MX), lambda i, s: (0, 0, 0))
    return pl.pallas_call(
        functools.partial(forward_kernel, group),
        out_shape=[
            jax.ShapeDtypeStruct((CH // 2, MY, 4 * MX), F32),
            jax.ShapeDtypeStruct((2, CH, NX), F32),
        ],
        grid_spec=pltpu.PrefetchScalarGridSpec(
            num_scalar_prefetch=1,
            grid=(CH // 2 // group,),
            in_specs=[
                pl.BlockSpec((2 * group, y_local, NX), lambda i, s: (i, 0, 0)),
                y_spec, y_spec, x_spec, x_spec,
            ],
            out_specs=[
                pl.BlockSpec((CH // 2, MY, 4 * MX), lambda i, s: (0, 0, 0)),
                pl.BlockSpec((2, 2 * group, NX), lambda i, s: (0, i, 0)),
            ],
            scratch_shapes=[pltpu.VMEM((4, CH // 2 * MY, NX), F32)],
        ),
        compiler_params=params(),
        cost_estimate=cost(2 * 10**9, 4 * 2**20),
        name="forward_modes",
    )(place, *in_hbm(field, *y_tab, *x_tab))


def filter_call(arrived, gains, gz, gy, scale):
    fwd, inv = z_tables(gz, gy, gains.shape[2], scale)
    fwd, inv = halves(fwd), halves(inv)
    return pl.pallas_call(
        filter_kernel,
        out_shape=jax.ShapeDtypeStruct(arrived.shape, F32),
        compiler_params=params(),
        cost_estimate=cost(2 * 10**8, 2**20),
        name="filter_modes",
    )(arrived, gains, *in_hbm(*fwd, *inv))


def inverse_call(modes, bias, outer, inner, chunks, y_local, place, gy, scale):
    group = 8
    x_tab = halves(x_inverse_table(scale))
    y_tab = halves(y_inverse_table(y_local, gy, group))
    tall, wide = y_tab[0].shape[1:]
    y_spec = pl.BlockSpec((1, tall, wide), lambda i, s: (s[0], 0, 0))
    x_spec = pl.BlockSpec((2, 4 * MX, 2 * NX), lambda i, s: (0, 0, 0))
    some = lambda rows: pl.BlockSpec((2 * group, rows, NX), lambda i, s: (i, 0, 0))
    return pl.pallas_call(
        functools.partial(inverse_kernel, group, chunks),
        out_shape=jax.ShapeDtypeStruct((CH, y_local, NX), F32),
        grid_spec=pltpu.PrefetchScalarGridSpec(
            num_scalar_prefetch=1,
            grid=(CH // 2 // group,),
            in_specs=[
                pl.BlockSpec((group, MY, 4 * MX), lambda i, s: (i, 0, 0)),
                pl.BlockSpec(memory_space=pltpu.SMEM),
                x_spec, x_spec, y_spec, y_spec,
                some(16),
                *[some(8 * count) for _, count in chunks for _ in range(3)],
            ],
            out_specs=some(y_local),
        ),
        compiler_params=params(),
        cost_estimate=cost(4 * 10**9, 6 * 2**20),
        name="inverse_modes",
    )(place, modes, bias, *in_hbm(*x_tab, *y_tab), outer, *inner)


def conv_call(field, halo, weight, point, first, count):
    last = field.shape[1] // 8 - 1
    if halo is None:
        chosen = range(first - 1, first + count + 1)
    else:
        chosen = (0, 1, last - 1, last)
    tile = lambda t, h: pl.BlockSpec((CH, 8, 128), lambda i: (0, t, h))
    specs = [tile(t, h) for t in chosen for h in range(2)]
    weight, point, field = in_hbm(weight, point, field)
    operands = [field] * len(specs)
    if halo is not None:
        specs.append(pl.BlockSpec((2, CH, NX), lambda i: (0, 0, 0)))
        operands.append(halo)
    rows = 8 * count
    return pl.pallas_call(
        functools.partial(conv_kernel, count),
        out_shape=[
            pltpu.HBM((CH, rows, NX), F32),
            jax.ShapeDtypeStruct((CH, rows, NX), F32),
            pltpu.HBM((CH, rows, NX), F32),
        ],
        grid=(1,),
        in_specs=[
            pl.BlockSpec((CH, 27), lambda i: (0, 0)),
            pl.BlockSpec((CH, CH), lambda i: (0, 0)),
            *specs,
        ],
        out_specs=[pl.BlockSpec((CH, rows, NX), lambda i: (0, 0, 0))] * 3,
        scratch_shapes=[
            pltpu.VMEM((3, rows + 4, CH, NX), F32),
            pltpu.VMEM((3, rows, CH, NX), F32),
            pltpu.VMEM((27, CH, 128), F32),
        ],
        compiler_params=params(),
        cost_estimate=cost(10**8 * count, count * 2**19),
        name="mixed_planes",
    )(weight, point, *operands)


def finish_call(result, low, high):
    last = result.shape[1] // 8 - 1
    block = pl.BlockSpec((CH // 2, 8, NX), lambda i, j: (j, i * last, 0))
    piece = pl.BlockSpec((CH // 2, 8, NX), lambda i, j: (j, i, 0))
    return pl.pallas_call(
        finish_kernel,
        out_shape=jax.ShapeDtypeStruct(result.shape, F32),
        grid=(2, 2),
        in_specs=[block, piece, piece],
        out_specs=block,
        input_output_aliases={0: 0},
        compiler_params=params(),
        cost_estimate=cost(10**8, 4 * 16 * CH * NX * 4),
        name="finished_rows",
    )(result, low, high)


def general_filter(coarse, gains, gz, gy, scale):
    j_own, n_own = gains.shape[2], gains.shape[3]
    both = ("gz", "gy")
    flat = coarse.reshape(CH // 2, MY, 2, 2, MX).transpose(3, 1, 0, 2, 4).reshape(2, MY, CH * MX)
    sent = flat.reshape(2, gy, j_own, gz, n_own).transpose(3, 1, 0, 2, 4).reshape(gz * gy, -1)
    got = lax.all_to_all(sent, both, split_axis=0, concat_axis=0, tiled=True)
    got = got.reshape(gz, gy, 2, j_own, n_own)
    c, s = (jnp.asarray(t, F32) for t in trig(kept(MZ, gz), np.arange(gz), gz))
    mul = functools.partial(jnp.einsum, precision=lax.Precision.HIGHEST)
    whole = got.sum(axis=1) * scale
    real = mul("zjn,qz->qjn", whole[:, 0], c) + mul("zjn,qz->qjn", whole[:, 1], s)
    imag = mul("zjn,qz->qjn", whole[:, 1], c) - mul("zjn,qz->qjn", whole[:, 0], s)
    real, imag = real * gains[0] - imag * gains[1], real * gains[1] + imag * gains[0]
    out = jnp.stack(
        [
            mul("qjn,qz->zjn", real, c) - mul("qjn,qz->zjn", imag, s),
            mul("qjn,qz->zjn", real, s) + mul("qjn,qz->zjn", imag, c),
        ],
        axis=1,
    )
    out = jnp.broadcast_to(out[:, None], (gz, gy, 2, j_own, n_own)).reshape(gz * gy, -1)
    back = lax.all_to_all(out, both, split_axis=0, concat_axis=0, tiled=True)
    back = back.reshape(gz, gy, 2, j_own, n_own).transpose(2, 1, 3, 0, 4)
    back = back.reshape(2, MY, CH // 2, 2, MX)
    return back.transpose(2, 1, 3, 0, 4).reshape(CH // 2, MY, 4 * MX)


def body(field, spectral_filter, depth_weight, point_weight, bias_vector):
    gz, gy = lax.axis_size("gz"), lax.axis_size("gy")
    y_local = field.shape[2]
    place = lax.axis_index("gy").astype(jnp.int32).reshape(1)
    field = field.reshape(CH, y_local, NX)
    y_total = gy * y_local
    forward_scale = 1.0 / math.sqrt(float(NX) * y_total * gz)
    inverse_scale = 1.0 / math.sqrt(2.0 * MX * MY * MZ)

    def ring(axis, count, by):
        return [(i, (i + by) % count) for i in range(count)]

    def to_neighbours(down, up):
        return (
            lax.ppermute(down, "gz", ring("gz", gz, 1)),
            lax.ppermute(up, "gz", ring("gz", gz, -1)),
        )

    tiles = y_local // 8
    chunks, at = [], 1
    for count in (1, 2, tiles):
        count = min(count, tiles - 1 - at)
        if count > 0:
            chunks.append((at, count))
            at += count

    def sums_for(k, source):
        down, own, up = conv_call(source, None, depth_weight, point_weight, *chunks[k])
        return [own, *to_neighbours(down, up)], down

    inner = []
    for k in range(min(2, len(chunks))):
        got, mark = sums_for(k, field)
        inner += got
        field, _ = lax.optimization_barrier((field, mark))
    coarse, edges = forward_call(field, place, gy)
    if gy == 2:
        halo = lax.ppermute(edges, "gy", ring("gy", gy, 1))
    else:
        halo = jnp.stack(
            [
                lax.ppermute(edges[0], "gy", ring("gy", gy, 1)),
                lax.ppermute(edges[1], "gy", ring("gy", gy, -1)),
            ]
        )
    for k in range(2, len(chunks)):
        inner += sums_for(k, field)[0]
    down, outer, up = conv_call(field, halo, depth_weight, point_weight, 0, 2)
    outer_low, outer_high = to_neighbours(down, up)

    j_own, n_own = spectral_filter.shape[2], spectral_filter.shape[3]
    if j_own == 8 and n_own == 2 * MX:
        both = ("gz", "gy")
        sent = coarse.reshape(gz * gy * 8, 4 * MX)
        got = lax.all_to_all(sent, both, split_axis=0, concat_axis=0, tiled=True)
        out = filter_call(got, spectral_filter, gz, gy, forward_scale)
        back = lax.all_to_all(out, both, split_axis=0, concat_axis=0, tiled=True)
        back = back.reshape(CH // 2, MY, 4 * MX)
    else:
        back = general_filter(coarse, spectral_filter, gz, gy, forward_scale)

    result = inverse_call(
        back, bias_vector, outer, inner, chunks, y_local, place, gy, inverse_scale
    )
    result = finish_call(result, outer_low, outer_high)
    return result.reshape(CH, 1, y_local, NX)


def solution(mesh):
    in_specs = (P(None, "gz", "gy", None), P(None, None, "gy", "gz"), P(), P(), P())
    out_specs = P(None, "gz", "gy", None)
    return jax.shard_map(body, mesh=mesh, in_specs=in_specs, out_specs=out_specs, check_vma=False)
```

```python
import functools
import math

import jax
import jax.numpy as jnp
import ml_dtypes
import numpy as np
from jax import lax
from jax.experimental import pallas as pl
from jax.experimental.pallas import tpu as pltpu
from jax.sharding import PartitionSpec as P

NX = 256
MX = 32
MY = 16
MZ = 16
CH = 32
VMEM_BYTES = 24 * 1024 * 1024
BF = jnp.bfloat16
F32 = jnp.float32


def kept(count, total):
    series = np.arange(count)
    return np.where(series < count // 2, series, total - count + series)


def trig(freqs, places, total):
    angle = 2.0 * np.pi * ((freqs[:, None] * places[None, :]) % total) / total
    return np.cos(angle), np.sin(angle)


def halves(table):
    table = np.asarray(table, np.float64)
    top = table.astype(np.float32).astype(ml_dtypes.bfloat16)
    rest = (table - top.astype(np.float64)).astype(np.float32).astype(ml_dtypes.bfloat16)
    return jnp.asarray(top), jnp.asarray(rest)


def y_forward_table(y_local, gy, group):
    out = np.zeros((gy, 2, group, MY, group, y_local))
    for g in range(gy):
        c, s = trig(kept(MY, y_local * gy), g * y_local + np.arange(y_local), y_local * gy)
        for i in range(group):
            out[g, 0, i, :, i] = c
            out[g, 1, i, :, i] = s
    return out.reshape(gy, 2 * group * MY, group * y_local)


def x_forward_table():
    c, s = trig(np.arange(MX), np.arange(NX), NX)
    out = np.zeros((2, 2, NX, 2, 2, MX))
    for p in range(2):
        out[p, 0, :, p, 0] = c.T
        out[p, 0, :, p, 1] = -s.T
        out[p, 1, :, p, 0] = -s.T
        out[p, 1, :, p, 1] = -c.T
    return out.reshape(4, NX, 4 * MX)


def x_inverse_table(scale):
    c, s = trig(np.arange(MX), np.arange(NX), NX)
    w = np.where(np.arange(MX) == 0, 1.0, 2.0)[:, None] * scale
    out = np.zeros((2, 2, 2, MX, 2, NX))
    for p in range(2):
        out[p, p, 0, :, 0] = w * c
        out[p, p, 1, :, 0] = -w * s
        out[p, p, 0, :, 1] = w * s
        out[p, p, 1, :, 1] = w * c
    return out.reshape(2, 4 * MX, 2 * NX)


def y_inverse_table(y_local, gy, group):
    out = np.zeros((gy, group, y_local, 2, group, MY))
    for g in range(gy):
        c, s = trig(kept(MY, y_local * gy), g * y_local + np.arange(y_local), y_local * gy)
        for i in range(group):
            out[g, i, :, 0, i] = c.T
            out[g, i, :, 1, i] = -s.T
    return out.reshape(gy, group * y_local, 2 * group * MY)


def z_tables(gz, gy, rows, scale):
    c, s = trig(kept(MZ, gz), np.arange(gz), gz)
    eye = np.eye(rows)
    one = np.ones(gy)
    both = np.stack([c, s])
    fwd = np.einsum("tqz,g,jk->tqjzgk", both, one, eye) * scale
    inv = np.einsum("tqz,g,jk->tzgjqk", both, one, eye)
    return fwd.reshape(2 * MZ * rows, gz * gy * rows), inv.reshape(2 * gz * gy * rows, MZ * rows)


def parts(value):
    top = value.astype(BF)
    return top, (value - top.astype(F32)).astype(BF)


def dot(a, b):
    return jnp.dot(a, b, preferred_element_type=F32)


def dot3(a, b):
    rows = a[0].shape[0]
    both = dot(jnp.concatenate([a[0], a[1]], axis=0), b[0])
    return both[:rows] + (both[rows:] + dot(a[0], b[1]))


def forward_kernel(group, field, y_top, y_rest, x_top, x_rest, out, turned):
    gy = lax.axis_index("gy")
    y_table = (y_top[gy], y_rest[gy])
    half = group * MY
    step = pl.program_id(0)
    for p in range(2):
        rows = jnp.concatenate([field[2 * i + p] for i in range(group)], axis=0)
        both = dot3(y_table, parts(rows))
        for t in range(2):
            at = pl.multiple_of(step * half, half)
            turned[2 * p + t, pl.ds(at, half), :] = both[t * half : (t + 1) * half]
    @pl.when(step == pl.num_programs(0) - 1)
    def _():
        total = dot3(parts(turned[0]), (x_top[0], x_rest[0]))
        for k in range(1, 4):
            total = total + dot3(parts(turned[k]), (x_top[k], x_rest[k]))
        out[...] = total.reshape(CH // 2, MY, 4 * MX)


def swap_parts(value):
    lane = lax.broadcasted_iota(jnp.int32, value.shape, 1)
    is_real = (lane // MX) % 2 == 0
    return jnp.where(is_real, pltpu.roll(value, 4 * MX - MX, 1), pltpu.roll(value, MX, 1)), is_real


def filter_kernel(arrived, gains, f_top, f_rest, i_top, i_rest, out):
    real, imag = (gains[r].reshape(-1, 2 * MX) for r in range(2))
    first, second = slice(0, MX), slice(MX, 2 * MX)
    same = jnp.concatenate([real[:, first], real[:, first], real[:, second], real[:, second]], axis=1)
    cross = jnp.concatenate([-imag[:, first], imag[:, first], -imag[:, second], imag[:, second]], axis=1)
    half = f_top.shape[0] // 2
    turned = dot3((f_top[...], f_rest[...]), parts(arrived[...]))
    crossed, is_real = swap_parts(turned[half:])
    modes = turned[:half] + jnp.where(is_real, crossed, -crossed)
    crossed, _ = swap_parts(modes)
    filtered = modes * same + crossed * cross
    half = i_top.shape[0] // 2
    back = dot3((i_top[...], i_rest[...]), parts(filtered))
    crossed, is_real = swap_parts(back[half:])
    out[...] = back[:half] + jnp.where(is_real, -crossed, crossed)


def conv_kernel(plan, weight, point, field, *refs):
    offsets, tiles, outer, with_edges = plan
    last = field.shape[1] // 8 - 1
    if outer:
        halo, refs = refs[0], refs[1:]
    count = len(offsets)
    outs, refs = refs[:count], refs[count:]
    if with_edges:
        edges_out, refs = refs[0], refs[1:]
    taken, halo_rows, weights, points, edges, sent, turned, depth, gains, sem_in, sem_out, sem_few = refs
    wanted = [0, 1, last - 1, last] if outer else list(range(tiles[0] - 1, tiles[-1] + 2))
    if with_edges:
        wanted += [t for t in (0, last) if t not in wanted]
    few = [
        pltpu.make_async_copy(weight, weights, sem_few.at[0]),
        pltpu.make_async_copy(point, points, sem_few.at[1]),
    ]
    if outer:
        few.append(pltpu.make_async_copy(halo, halo_rows, sem_few.at[2]))
    for copy in few:
        copy.start()
    pending = {}
    for k, t in enumerate(wanted):
        pending[t] = [
            pltpu.make_async_copy(
                field.at[:, pl.ds(8 * t, 8), pl.ds(128 * h, 128)], taken.at[k, h], sem_in.at[k, h]
            )
            for h in range(2)
        ]
        for copy in pending[t]:
            copy.start()
    for copy in few:
        copy.wait()
    for k in offsets:
        for j in range(9):
            gains[9 * k + j] = jnp.broadcast_to(weights[:, 9 * k + j : 9 * k + j + 1], (CH, 128))

    down = (
        lax.broadcasted_iota(jnp.int32, (8 * CH, CH), 0) // 8
        == lax.broadcasted_iota(jnp.int32, (8 * CH, CH), 1)
    ).astype(BF)
    across = (
        lax.broadcasted_iota(jnp.int32, (CH, 8 * CH), 1) % CH
        == lax.broadcasted_iota(jnp.int32, (CH, 8 * CH), 0)
    ).astype(BF)
    same = (
        lax.broadcasted_iota(jnp.int32, (8 * CH, 8 * CH), 0) % 8
        == lax.broadcasted_iota(jnp.int32, (8 * CH, 8 * CH), 1) // CH
    )
    mix = tuple(
        jnp.where(same, dot(dot(down, part).astype(BF), across), 0.0).astype(BF)
        for part in parts(points[...])
    )

    def row(t, r):
        for copy in pending.pop(t, ()):
            copy.wait()
        k = wanted.index(t)
        return jnp.concatenate(
            [taken.at[k, h].reshape(CH * 8, 128)[pl.ds(r, CH, stride=8), :] for h in range(2)], axis=1
        )

    if outer:
        segments = [
            [None, *[(0, r) for r in range(8)], (1, 0)],
            [(last - 1, 7), *[(last, r) for r in range(8)], None],
        ]
    else:
        segments = [
            [(tiles[0] - 1, 7), *[(t, r) for t in tiles for r in range(8)], (tiles[-1] + 1, 0)]
        ]
    runs, at, done = [], 0, 0
    for side, places in enumerate(segments):
        for i, place in enumerate(places):
            value = halo_rows[side] if place is None else row(*place)
            turned[0, at + i] = pltpu.roll(value, 1, 1)
            turned[1, at + i] = value
            turned[2, at + i] = pltpu.roll(value, NX - 1, 1)
        runs.append((at, done, len(places) - 2))
        at, done = at + len(places), done + len(places) - 2
    copies = []
    if with_edges:
        edges[0] = row(last, 7)
        edges[1] = row(0, 0)
        copies.append(pltpu.make_async_copy(edges, edges_out, sem_few.at[3]))
        copies[-1].start()

    def taps(i, _):
        chans = pl.ds(pl.multiple_of(i * 8, 8), 8)
        gain = {k: gains[k, chans, :] for a in offsets for k in range(9 * a, 9 * a + 9)}
        for h in range(2):
            lanes = pl.ds(128 * h, 128)
            for first, to, rows in runs:
                sums = {}
                for r in range(rows + 2):
                    values = [turned[e, first + r, chans, lanes] for e in range(3)]
                    for b in range(3):
                        o = r - b
                        if o < 0 or o >= rows:
                            continue
                        for a in offsets:
                            for e in range(3):
                                term = gain[a * 9 + b * 3 + e] * values[e]
                                sums[o, a] = sums[o, a] + term if (o, a) in sums else term
                    if r >= 2:
                        for k, a in enumerate(offsets):
                            depth[k, to + r - 2, chans, lanes] = sums.pop((r - 2, a))
        return 0

    lax.fori_loop(0, CH // 8, taps, 0)

    for t in range(done // 8):
        rows = pl.ds(8 * t, 8)
        for k, out in enumerate(outs):
            tile = depth[k, rows].reshape(8 * CH, NX)
            sent[k, t] = dot3(mix, parts(tile)).reshape(CH, 8, NX)
            copies.append(pltpu.make_async_copy(sent.at[k, t], out.at[:, rows, :], sem_out.at[k, t]))
            copies[-1].start()
    for copies_of in (copies, *pending.values()):
        for copy in copies_of:
            copy.wait()


def gelu(value):
    return 0.5 * value * (1.0 + lax.erf(value * (1.0 / math.sqrt(2.0))))


def inverse_kernel(group, chunks, modes, bias, x_top, x_rest, y_top, y_rest, outer, *refs):
    out, base = refs[-2:]
    step = pl.program_id(0)
    gy = lax.axis_index("gy")
    y_table = (y_top[gy], y_rest[gy])
    mode_rows = parts(modes[...].reshape(group * MY, 4 * MX))
    y_local = out.shape[1]
    for p in range(2):
        wide = dot3(mode_rows, (x_top[p], x_rest[p]))
        tall = jnp.concatenate([wide[:, :NX], wide[:, NX:]], axis=0)
        planes = dot3(y_table, parts(tall)).reshape(group, y_local, NX)
        for i in range(group):
            c = 2 * i + p
            plane = planes[i] + bias[step * 2 * group + c]
            base[c, :8] = plane[:8] + outer[c, :8]
            base[c, 8:] = plane[y_local - 8 :] + outer[c, 8:]
            for k, (first, count) in enumerate(chunks):
                rows = slice(8 * first, 8 * (first + count))
                own, low, high = refs[3 * k : 3 * k + 3]
                out[c, rows] = gelu(plane[rows] + (own[c] + (low[c] + high[c])))


def finish_kernel(_, base, low, high, out):
    out[...] = gelu(base[...] + (low[...] + high[...]))


def in_hbm(*arrays):
    return [pltpu.with_memory_space_constraint(a, pltpu.HBM) for a in arrays]


def params():
    return pltpu.CompilerParams(vmem_limit_bytes=VMEM_BYTES)


def cost(flops, moved):
    return pl.CostEstimate(flops=flops, bytes_accessed=moved, transcendentals=0)


def whole_block(table):
    return pl.BlockSpec(table.shape, lambda i: (0,) * table.ndim)


def forward_call(field, gy):
    y_local = field.shape[1]
    group = max(1, min(CH // 2, 256 // y_local))
    tables = [*halves(y_forward_table(y_local, gy, group)), *halves(x_forward_table())]
    return pl.pallas_call(
        functools.partial(forward_kernel, group),
        out_shape=jax.ShapeDtypeStruct((CH // 2, MY, 4 * MX), F32),
        grid=(CH // 2 // group,),
        in_specs=[
            pl.BlockSpec((2 * group, y_local, NX), lambda i: (i, 0, 0)),
            *[whole_block(t) for t in tables],
        ],
        out_specs=pl.BlockSpec((CH // 2, MY, 4 * MX), lambda i: (0, 0, 0)),
        scratch_shapes=[pltpu.VMEM((4, CH // 2 * MY, NX), F32)],
        compiler_params=params(),
        cost_estimate=cost(10**8, 2**18),
        name="forward_modes",
    )(*in_hbm(field, *tables))


def filter_call(arrived, gains, gz, gy, scale):
    fwd, inv = z_tables(gz, gy, gains.shape[2], scale)
    fwd, inv = halves(fwd), halves(inv)
    return pl.pallas_call(
        filter_kernel,
        out_shape=jax.ShapeDtypeStruct(arrived.shape, F32),
        compiler_params=params(),
        cost_estimate=cost(10**8, 2**18),
        name="filter_modes",
    )(arrived, gains, *in_hbm(*fwd, *inv))


def inverse_call(modes, bias, outer, inner, chunks, y_local, gy, scale):
    group = 4
    tables = [*halves(x_inverse_table(scale)), *halves(y_inverse_table(y_local, gy, group))]
    some = lambda rows: pl.BlockSpec((2 * group, rows, NX), lambda i: (i, 0, 0))
    return pl.pallas_call(
        functools.partial(inverse_kernel, group, chunks),
        out_shape=[
            jax.ShapeDtypeStruct((CH, y_local, NX), F32),
            jax.ShapeDtypeStruct((CH, 16, NX), F32),
        ],
        grid=(CH // 2 // group,),
        in_specs=[
            pl.BlockSpec((group, MY, 4 * MX), lambda i: (i, 0, 0)),
            pl.BlockSpec(memory_space=pltpu.SMEM),
            *[whole_block(t) for t in tables],
            some(16),
            *[some(8 * count) for _, count in chunks for _ in range(3)],
        ],
        out_specs=[some(y_local), some(16)],
        compiler_params=params(),
        cost_estimate=cost(10**8, 2**18),
        name="inverse_modes",
    )(modes, bias, *in_hbm(*tables), outer, *inner)


def conv_call(field, weight, point, offsets, tiles, halo=None, with_edges=False):
    outer = halo is not None
    rows, count = 8 * len(tiles), len(offsets)
    hbm = pl.BlockSpec(memory_space=pltpu.HBM)
    operands = in_hbm(weight, point, field)
    shapes = [pltpu.HBM((CH, rows, NX), F32)] * count
    if outer:
        operands += in_hbm(halo)
    if with_edges:
        shapes.append(pltpu.HBM((2, CH, NX), F32))
    fetched = len(tiles) + 4
    return pl.pallas_call(
        functools.partial(conv_kernel, (offsets, tiles, outer, with_edges)),
        out_shape=shapes,
        in_specs=[hbm] * len(operands),
        out_specs=[hbm] * len(shapes),
        scratch_shapes=[
            pltpu.VMEM((fetched, 2, CH, 8, 128), F32),
            pltpu.VMEM((2, CH, NX), F32),
            pltpu.VMEM((CH, 27), F32),
            pltpu.VMEM((CH, CH), F32),
            pltpu.VMEM((2, CH, NX), F32),
            pltpu.VMEM((count, len(tiles), CH, 8, NX), F32),
            pltpu.VMEM((3, rows + 4, CH, NX), F32),
            pltpu.VMEM((count, rows, CH, NX), F32),
            pltpu.VMEM((27, CH, 128), F32),
            pltpu.SemaphoreType.DMA((fetched, 2)),
            pltpu.SemaphoreType.DMA((count, len(tiles))),
            pltpu.SemaphoreType.DMA((4,)),
        ],
        compiler_params=params(),
        cost_estimate=cost(10**8, 2**18),
        name="mixed_planes",
    )(*operands)


def finish_call(result, base, low, high):
    last = result.shape[1] // 8 - 1
    piece = pl.BlockSpec((CH, 8, NX), lambda i: (0, i, 0))
    return pl.pallas_call(
        finish_kernel,
        out_shape=jax.ShapeDtypeStruct(result.shape, F32),
        grid=(2,),
        in_specs=[pl.BlockSpec(memory_space=pl.ANY), piece, piece, piece],
        out_specs=pl.BlockSpec((CH, 8, NX), lambda i: (0, i * last, 0)),
        input_output_aliases={0: 0},
        compiler_params=params(),
        cost_estimate=cost(10**8, 2**18),
        name="finished_rows",
    )(result, base, low, high)


def general_filter(coarse, gains, gz, gy, scale):
    j_own, n_own = gains.shape[2], gains.shape[3]
    both = ("gz", "gy")
    flat = coarse.reshape(CH // 2, MY, 2, 2, MX).transpose(3, 1, 0, 2, 4).reshape(2, MY, CH * MX)
    sent = flat.reshape(2, gy, j_own, gz, n_own).transpose(3, 1, 0, 2, 4).reshape(gz * gy, -1)
    got = lax.all_to_all(sent, both, split_axis=0, concat_axis=0, tiled=True)
    got = got.reshape(gz, gy, 2, j_own, n_own)
    c, s = (jnp.asarray(t, F32) for t in trig(kept(MZ, gz), np.arange(gz), gz))
    mul = functools.partial(jnp.einsum, precision=lax.Precision.HIGHEST)
    whole = got.sum(axis=1) * scale
    real = mul("zjn,qz->qjn", whole[:, 0], c) + mul("zjn,qz->qjn", whole[:, 1], s)
    imag = mul("zjn,qz->qjn", whole[:, 1], c) - mul("zjn,qz->qjn", whole[:, 0], s)
    real, imag = real * gains[0] - imag * gains[1], real * gains[1] + imag * gains[0]
    out = jnp.stack(
        [
            mul("qjn,qz->zjn", real, c) - mul("qjn,qz->zjn", imag, s),
            mul("qjn,qz->zjn", real, s) + mul("qjn,qz->zjn", imag, c),
        ],
        axis=1,
    )
    out = jnp.broadcast_to(out[:, None], (gz, gy, 2, j_own, n_own)).reshape(gz * gy, -1)
    back = lax.all_to_all(out, both, split_axis=0, concat_axis=0, tiled=True)
    back = back.reshape(gz, gy, 2, j_own, n_own).transpose(2, 1, 3, 0, 4)
    back = back.reshape(2, MY, CH // 2, 2, MX)
    return back.transpose(2, 1, 3, 0, 4).reshape(CH // 2, MY, 4 * MX)


def body(field, spectral_filter, depth_weight, point_weight, bias_vector):
    gz, gy = lax.axis_size("gz"), lax.axis_size("gy")
    y_local = field.shape[2]
    field = field.reshape(CH, y_local, NX)
    y_total = gy * y_local
    forward_scale = 1.0 / math.sqrt(float(NX) * y_total * gz)
    inverse_scale = 1.0 / math.sqrt(2.0 * MX * MY * MZ)

    def ring(axis, count, by):
        return [(i, (i + by) % count) for i in range(count)]

    def to_neighbours(down, up):
        return (
            lax.ppermute(down, "gz", ring("gz", gz, 1)),
            lax.ppermute(up, "gz", ring("gz", gz, -1)),
        )

    def after(value, *others):
        return lax.optimization_barrier((value, *others))[0]

    tiles = y_local // 8
    middle = 1 + (tiles - 1) // 2
    spans = [tuple(range(1, middle)), tuple(range(middle, tiles - 1))]
    chunks = [(span[0], len(span)) for span in spans if span]
    conv = functools.partial(conv_call, weight=depth_weight, point=point_weight)

    down, up, edges = conv(field, offsets=(0, 2), tiles=spans[0], with_edges=True)
    first_pair = to_neighbours(down, up)
    if gy == 2:
        halo = lax.ppermute(edges, "gy", ring("gy", gy, 1))
    else:
        halo = jnp.stack(
            [
                lax.ppermute(edges[0], "gy", ring("gy", gy, 1)),
                lax.ppermute(edges[1], "gy", ring("gy", gy, -1)),
            ]
        )
    coarse = forward_call(after(field, down), gy)
    second = []
    mark = coarse
    if spans[1]:
        down, own, up = conv(after(field, coarse), offsets=(0, 1, 2), tiles=spans[1])
        second = [own, *to_neighbours(down, up)]
        mark = down

    j_own, n_own = spectral_filter.shape[2], spectral_filter.shape[3]
    if j_own == 8 and n_own == 2 * MX:
        both = ("gz", "gy")
        sent = coarse.reshape(gz * gy * 8, 4 * MX)
        got = lax.all_to_all(sent, both, split_axis=0, concat_axis=0, tiled=True)
        out = filter_call(got, after(spectral_filter, mark), gz, gy, forward_scale)
        back = lax.all_to_all(out, both, split_axis=0, concat_axis=0, tiled=True)
        back = back.reshape(CH // 2, MY, 4 * MX)
        mark = out
    else:
        back = general_filter(coarse, spectral_filter, gz, gy, forward_scale)

    down, outer, up = conv(after(field, mark), offsets=(0, 1, 2), tiles=(0, tiles - 1), halo=halo)
    outer_pair = to_neighbours(down, up)
    (own,) = conv(after(field, down), offsets=(1,), tiles=spans[0])
    inner = [own, *first_pair, *second]
    result, base = inverse_call(
        back, bias_vector, outer, inner, chunks, y_local, gy, inverse_scale
    )
    result = finish_call(result, base, *outer_pair)
    return result.reshape(CH, 1, y_local, NX)


def solution(mesh):
    in_specs = (P(None, "gz", "gy", None), P(None, None, "gy", "gz"), P(), P(), P())
    out_specs = P(None, "gz", "gy", None)
    return jax.shard_map(body, mesh=mesh, in_specs=in_specs, out_specs=out_specs, check_vma=False)
```

```python
import functools
import math

import jax
import jax.numpy as jnp
import ml_dtypes
import numpy as np
from jax import lax
from jax.experimental import pallas as pl
from jax.experimental.pallas import tpu as pltpu
from jax.sharding import PartitionSpec as P

NX = 256
MX = 32
MY = 16
MZ = 16
CH = 32
VMEM_BYTES = 24 * 1024 * 1024
BF = jnp.bfloat16
F32 = jnp.float32


def kept(count, total):
    series = np.arange(count)
    return np.where(series < count // 2, series, total - count + series)


def trig(freqs, places, total):
    angle = 2.0 * np.pi * ((freqs[:, None] * places[None, :]) % total) / total
    return np.cos(angle), np.sin(angle)


def halves(table):
    table = np.asarray(table, np.float64)
    top = table.astype(np.float32).astype(ml_dtypes.bfloat16)
    rest = (table - top.astype(np.float64)).astype(np.float32).astype(ml_dtypes.bfloat16)
    return jnp.asarray(top), jnp.asarray(rest)


def y_forward_table(y_local, gy, group):
    out = np.zeros((gy, 2, group, MY, group, y_local))
    for g in range(gy):
        c, s = trig(kept(MY, y_local * gy), g * y_local + np.arange(y_local), y_local * gy)
        for i in range(group):
            out[g, 0, i, :, i] = c
            out[g, 1, i, :, i] = s
    return out.reshape(gy, 2 * group * MY, group * y_local)


def x_forward_table():
    c, s = trig(np.arange(MX), np.arange(NX), NX)
    out = np.zeros((2, 2, NX, 2, 2, MX))
    for p in range(2):
        out[p, 0, :, p, 0] = c.T
        out[p, 0, :, p, 1] = -s.T
        out[p, 1, :, p, 0] = -s.T
        out[p, 1, :, p, 1] = -c.T
    return out.reshape(4, NX, 4 * MX)


def x_inverse_table(scale):
    c, s = trig(np.arange(MX), np.arange(NX), NX)
    w = np.where(np.arange(MX) == 0, 1.0, 2.0)[:, None] * scale
    out = np.zeros((2, 2, 2, MX, 2, NX))
    for p in range(2):
        out[p, p, 0, :, 0] = w * c
        out[p, p, 1, :, 0] = -w * s
        out[p, p, 0, :, 1] = w * s
        out[p, p, 1, :, 1] = w * c
    return out.reshape(2, 4 * MX, 2 * NX)


def y_inverse_table(y_local, gy, group):
    out = np.zeros((gy, group, y_local, 2, group, MY))
    for g in range(gy):
        c, s = trig(kept(MY, y_local * gy), g * y_local + np.arange(y_local), y_local * gy)
        for i in range(group):
            out[g, i, :, 0, i] = c.T
            out[g, i, :, 1, i] = -s.T
    return out.reshape(gy, group * y_local, 2 * group * MY)


def z_tables(gz, gy, rows, scale):
    c, s = trig(kept(MZ, gz), np.arange(gz), gz)
    eye = np.eye(rows)
    one = np.ones(gy)
    both = np.stack([c, s])
    fwd = np.einsum("tqz,g,jk->tqjzgk", both, one, eye) * scale
    inv = np.einsum("tqz,g,jk->tzgjqk", both, one, eye)
    return fwd.reshape(2 * MZ * rows, gz * gy * rows), inv.reshape(2 * gz * gy * rows, MZ * rows)


def parts(value):
    top = value.astype(BF)
    return top, (value - top.astype(F32)).astype(BF)


def dot(a, b):
    return jnp.dot(a, b, preferred_element_type=F32)


def dot3(a, b):
    rows = a[0].shape[0]
    both = dot(jnp.concatenate([a[0], a[1]], axis=0), b[0])
    return both[:rows] + (both[rows:] + dot(a[0], b[1]))


def forward_kernel(group, field, y_top, y_rest, x_top, x_rest, out, turned):
    gy = lax.axis_index("gy")
    y_table = (y_top[gy], y_rest[gy])
    half = group * MY
    step = pl.program_id(0)
    for p in range(2):
        rows = jnp.concatenate([field[2 * i + p] for i in range(group)], axis=0)
        both = dot3(y_table, parts(rows))
        for t in range(2):
            at = pl.multiple_of(step * half, half)
            turned[2 * p + t, pl.ds(at, half), :] = both[t * half : (t + 1) * half]
    @pl.when(step == pl.num_programs(0) - 1)
    def _():
        total = dot3(parts(turned[0]), (x_top[0], x_rest[0]))
        for k in range(1, 4):
            total = total + dot3(parts(turned[k]), (x_top[k], x_rest[k]))
        out[...] = total.reshape(CH // 2, MY, 4 * MX)


def swap_parts(value):
    lane = lax.broadcasted_iota(jnp.int32, value.shape, 1)
    is_real = (lane // MX) % 2 == 0
    return jnp.where(is_real, pltpu.roll(value, 4 * MX - MX, 1), pltpu.roll(value, MX, 1)), is_real


def filter_kernel(arrived, gains, f_top, f_rest, i_top, i_rest, out):
    real, imag = (gains[r].reshape(-1, 2 * MX) for r in range(2))
    first, second = slice(0, MX), slice(MX, 2 * MX)
    same = jnp.concatenate([real[:, first], real[:, first], real[:, second], real[:, second]], axis=1)
    cross = jnp.concatenate([-imag[:, first], imag[:, first], -imag[:, second], imag[:, second]], axis=1)
    half = f_top.shape[0] // 2
    turned = dot3((f_top[...], f_rest[...]), parts(arrived[...]))
    crossed, is_real = swap_parts(turned[half:])
    modes = turned[:half] + jnp.where(is_real, crossed, -crossed)
    crossed, _ = swap_parts(modes)
    filtered = modes * same + crossed * cross
    half = i_top.shape[0] // 2
    back = dot3((i_top[...], i_rest[...]), parts(filtered))
    crossed, is_real = swap_parts(back[half:])
    out[...] = back[:half] + jnp.where(is_real, -crossed, crossed)


def fetch_tiles(field, taken, sems, wanted):
    pending = {}
    for k, t in enumerate(wanted):
        pending[t] = [
            pltpu.make_async_copy(
                field.at[:, pl.ds(8 * t, 8), pl.ds(128 * h, 128)], taken.at[k, h], sems.at[k, h]
            )
            for h in range(2)
        ]
        for copy in pending[t]:
            copy.start()

    def row(t, r):
        for copy in pending.pop(t, ()):
            copy.wait()
        k = wanted.index(t)
        return jnp.concatenate(
            [taken.at[k, h].reshape(CH * 8, 128)[pl.ds(r, CH, stride=8), :] for h in range(2)], axis=1
        )

    return row


def spread_gains(weights, gains, offsets):
    for k in [9 * a + j for a in offsets for j in range(9)]:
        gains[k] = jnp.broadcast_to(weights[:, k : k + 1], (CH, 128))


def mixing(points):
    down = (
        lax.broadcasted_iota(jnp.int32, (8 * CH, CH), 0) // 8
        == lax.broadcasted_iota(jnp.int32, (8 * CH, CH), 1)
    ).astype(BF)
    across = (
        lax.broadcasted_iota(jnp.int32, (CH, 8 * CH), 1) % CH
        == lax.broadcasted_iota(jnp.int32, (CH, 8 * CH), 0)
    ).astype(BF)
    same = (
        lax.broadcasted_iota(jnp.int32, (8 * CH, 8 * CH), 0) % 8
        == lax.broadcasted_iota(jnp.int32, (8 * CH, 8 * CH), 1) // CH
    )
    return tuple(
        jnp.where(same, dot(dot(down, part).astype(BF), across), 0.0).astype(BF)
        for part in parts(points)
    )


def turn(turned, at, value):
    turned[0, at] = pltpu.roll(value, 1, 1)
    turned[1, at] = value
    turned[2, at] = pltpu.roll(value, NX - 1, 1)


def tap_sums(turned, depth, gains, runs, offsets, fresh):
    def some(i, _):
        chans = pl.ds(pl.multiple_of(i * 8, 8), 8)
        gain = {k: gains[k, chans, :] for a in offsets for k in range(9 * a, 9 * a + 9)}
        for h in range(2):
            lanes = pl.ds(128 * h, 128)
            for first, to, rows in runs:
                sums = {}
                for r in range(rows + 2):
                    values = [turned[e, first + r, chans, lanes] for e in range(3)]
                    for b in range(3):
                        o = r - b
                        if o < 0 or o >= rows:
                            continue
                        for k, a in enumerate(offsets):
                            for e in range(3):
                                term = gain[a * 9 + b * 3 + e] * values[e]
                                if (o, k) in sums:
                                    sums[o, k] = sums[o, k] + term
                                elif fresh:
                                    sums[o, k] = term
                                else:
                                    sums[o, k] = depth[k, to + o, chans, lanes] + term
                    if r >= 2:
                        for k in range(len(offsets)):
                            depth[k, to + r - 2, chans, lanes] = sums.pop((r - 2, k))
        return 0

    lax.fori_loop(0, CH // 8, some, 0)


def mix_tile(mix, depth, k, t):
    tile = depth[k, pl.ds(8 * t, 8)].reshape(8 * CH, NX)
    return dot3(mix, parts(tile)).reshape(CH, 8, NX)


def pack_kernel(middle, field, packed, edges, taken, rows, ends, sem_in, sem_out):
    last = field.shape[1] // 8 - 1
    before, after = middle[0] - 1, middle[-1] + 1
    wanted = [before, *middle, after] + [t for t in (0, last) if t not in (before, after)]
    row = fetch_tiles(field, taken, sem_in, wanted)
    places = [(before, 7), *[(t, r) for t in middle for r in range(8)], (after, 0)]
    copies, sent = [], 0
    for i, place in enumerate(places):
        rows[i] = row(*place)
        if i + 1 - sent >= 17 or i + 1 == len(places):
            some = pl.ds(sent, i + 1 - sent)
            copies.append(pltpu.make_async_copy(rows.at[some], packed.at[some], sem_out.at[len(copies)]))
            copies[-1].start()
            sent = i + 1
    ends[0] = row(last, 7)
    ends[1] = row(0, 0)
    copies.append(pltpu.make_async_copy(ends, edges, sem_out.at[len(copies)]))
    copies[-1].start()
    for copy in copies:
        copy.wait()


def own_kernel(plan, weight, point, field, halo, *refs):
    upper, lower, count = plan
    outs, refs = refs[:count], refs[count:]
    taken, halo_rows, weights, points, sent, turned, depth, gains, sem_in, sem_out, sem_few = refs
    few = [
        pltpu.make_async_copy(a, b, sem_few.at[i])
        for i, (a, b) in enumerate(((weight, weights), (point, points), (halo, halo_rows)))
    ]
    for copy in few:
        copy.start()
    wanted = [*upper, upper[-1] + 1, lower[0] - 1, *lower]
    row = fetch_tiles(field, taken, sem_in, wanted)
    for copy in few:
        copy.wait()
    spread_gains(weights, gains, range(3))
    mix = mixing(points[...])
    rows = 8 * len(upper)
    for i, place in enumerate([None, *[(t, r) for t in upper for r in range(8)], (upper[-1] + 1, 0)]):
        turn(turned, i, halo_rows[0] if place is None else row(*place))
    for i, place in enumerate([(lower[0] - 1, 7), *[(t, r) for t in lower for r in range(8)], None]):
        turn(turned, rows + 2 + i, halo_rows[1] if place is None else row(*place))
    tap_sums(turned, depth, gains, [(0, 0, rows), (rows + 2, rows, rows)], range(3), True)
    copies = []
    own, pairs = outs[0], outs[1:]
    tiles = [*upper, *lower]
    order = sorted(range(len(tiles)), key=lambda t: tiles[t] in (upper[0], lower[-1]))
    for t in order:
        outer = tiles[t] in (upper[0], lower[-1])
        group = pairs[2:] if count == 5 and not outer else pairs[:2]
        slot = 0 if t < len(upper) else 1
        for k, out, at in ((0, group[0], slot), (2, group[1], slot), (1, own, t)):
            sent[k, t] = mix_tile(mix, depth, k, t)
            copies.append(
                pltpu.make_async_copy(sent.at[k, t], out.at[:, pl.ds(8 * at, 8), :], sem_out.at[k, t])
            )
            copies[-1].start()
    for copy in copies:
        copy.wait()


def middle_kernel(weight, point, *refs):
    planes, out = refs[:3], refs[3]
    taken, weights, points, sent, turned, depth, gains, sem_in, sem_out, sem_few = refs[4:]
    few = [
        pltpu.make_async_copy(a, b, sem_few.at[i])
        for i, (a, b) in enumerate(((weight, weights), (point, points)))
    ]
    arrivals = [pltpu.make_async_copy(planes[a], taken.at[a], sem_in.at[a]) for a in range(3)]
    for copy in few + arrivals:
        copy.start()
    for copy in few:
        copy.wait()
    spread_gains(weights, gains, range(3))
    mix = mixing(points[...])
    rows = out.shape[1]
    for a in (1, 0, 2):
        arrivals[a].wait()

        def one(r, _):
            turn(turned, r, taken[a, r])
            return 0

        lax.fori_loop(0, rows + 2, one, 0, unroll=2)
        tap_sums(turned, depth, gains, [(0, 0, rows)], [a], a == 1)
    copies = []
    for t in range(rows // 8):
        sent[t] = mix_tile(mix, depth, 0, t)
        copies.append(pltpu.make_async_copy(sent.at[t], out.at[:, pl.ds(8 * t, 8), :], sem_out.at[t]))
        copies[-1].start()
    for copy in copies:
        copy.wait()


def gelu(value):
    return 0.5 * value * (1.0 + lax.erf(value * (1.0 / math.sqrt(2.0))))


def inverse_kernel(group, plan, modes, bias, x_top, x_rest, y_top, y_rest, middle, own, *refs):
    upper, lower = plan
    out, base = refs[-2:]
    step = pl.program_id(0)
    gy = lax.axis_index("gy")
    y_table = (y_top[gy], y_rest[gy])
    mode_rows = parts(modes[...].reshape(group * MY, 4 * MX))
    y_local = out.shape[1]
    start, stop = 8 * upper[-1] + 8, 8 * lower[0]
    for p in range(2):
        wide = dot3(mode_rows, (x_top[p], x_rest[p]))
        tall = jnp.concatenate([wide[:, :NX], wide[:, NX:]], axis=0)
        planes = dot3(y_table, parts(tall)).reshape(group, y_local, NX)
        for i in range(group):
            c = 2 * i + p
            plane = planes[i] + bias[step * 2 * group + c]
            out[c, start:stop] = gelu(plane[start:stop] + middle[c])
            first = plane[:start] + own[c, :start]
            second = plane[stop:] + own[c, start:]
            base[c, :8] = first[:8]
            base[c, 8:] = second[-8:]
            if start > 8:
                low, high = refs[:2]
                out[c, 8:start] = gelu(first[8:] + (low[c, : start - 8] + high[c, : start - 8]))
                out[c, stop : y_local - 8] = gelu(
                    second[:-8] + (low[c, start - 8 :] + high[c, start - 8 :])
                )


def finish_kernel(_, base, low, high, out):
    out[...] = gelu(base[...] + (low[...] + high[...]))


def in_hbm(*arrays):
    return [pltpu.with_memory_space_constraint(a, pltpu.HBM) for a in arrays]


def params():
    return pltpu.CompilerParams(vmem_limit_bytes=VMEM_BYTES)


def cost(flops, moved):
    return pl.CostEstimate(flops=flops, bytes_accessed=moved, transcendentals=0)


def whole_block(table):
    return pl.BlockSpec(table.shape, lambda i: (0,) * table.ndim)


def forward_call(field, gy):
    y_local = field.shape[1]
    group = max(1, min(CH // 2, 256 // y_local))
    tables = [*halves(y_forward_table(y_local, gy, group)), *halves(x_forward_table())]
    return pl.pallas_call(
        functools.partial(forward_kernel, group),
        out_shape=jax.ShapeDtypeStruct((CH // 2, MY, 4 * MX), F32),
        grid=(CH // 2 // group,),
        in_specs=[
            pl.BlockSpec((2 * group, y_local, NX), lambda i: (i, 0, 0)),
            *[whole_block(t) for t in tables],
        ],
        out_specs=pl.BlockSpec((CH // 2, MY, 4 * MX), lambda i: (0, 0, 0)),
        scratch_shapes=[pltpu.VMEM((4, CH // 2 * MY, NX), F32)],
        compiler_params=params(),
        cost_estimate=cost(10**8, 2**18),
        name="forward_modes",
    )(*in_hbm(field, *tables))


def filter_call(arrived, gains, gz, gy, scale):
    fwd, inv = z_tables(gz, gy, gains.shape[2], scale)
    fwd, inv = halves(fwd), halves(inv)
    return pl.pallas_call(
        filter_kernel,
        out_shape=jax.ShapeDtypeStruct(arrived.shape, F32),
        compiler_params=params(),
        cost_estimate=cost(10**8, 2**18),
        name="filter_modes",
    )(arrived, gains, *in_hbm(*fwd, *inv))


def inverse_call(modes, bias, middle, own, pair, plan, y_local, gy, scale):
    group = 4
    tables = [*halves(x_inverse_table(scale)), *halves(y_inverse_table(y_local, gy, group))]
    some = lambda rows: pl.BlockSpec((2 * group, rows, NX), lambda i: (i, 0, 0))
    planes = [*in_hbm(middle, own), *pair]
    return pl.pallas_call(
        functools.partial(inverse_kernel, group, plan),
        out_shape=[
            jax.ShapeDtypeStruct((CH, y_local, NX), F32),
            jax.ShapeDtypeStruct((CH, 16, NX), F32),
        ],
        grid=(CH // 2 // group,),
        in_specs=[
            pl.BlockSpec((group, MY, 4 * MX), lambda i: (i, 0, 0)),
            pl.BlockSpec(memory_space=pltpu.SMEM),
            *[whole_block(t) for t in tables],
            *[some(p.shape[1]) for p in planes],
        ],
        out_specs=[some(y_local), some(16)],
        compiler_params=params(),
        cost_estimate=cost(10**8, 2**18),
        name="inverse_modes",
    )(modes, bias, *in_hbm(*tables), *planes)


def pack_call(field, middle):
    count = 8 * len(middle) + 2
    fetched = len(middle) + 4
    hbm = pl.BlockSpec(memory_space=pltpu.HBM)
    return pl.pallas_call(
        functools.partial(pack_kernel, middle),
        out_shape=[pltpu.HBM((count, CH, NX), F32), pltpu.HBM((2, CH, NX), F32)],
        in_specs=[hbm],
        out_specs=[hbm] * 2,
        scratch_shapes=[
            pltpu.VMEM((fetched, 2, CH, 8, 128), F32),
            pltpu.VMEM((count, CH, NX), F32),
            pltpu.VMEM((2, CH, NX), F32),
            pltpu.SemaphoreType.DMA((fetched, 2)),
            pltpu.SemaphoreType.DMA((count // 17 + 2,)),
        ],
        compiler_params=params(),
        cost_estimate=cost(10**8, 2**18),
        name="packed_rows",
    )(*in_hbm(field))


def own_call(field, halo, weight, point, upper, lower):
    tiles = len(upper) + len(lower)
    rows = 8 * tiles
    hbm = pl.BlockSpec(memory_space=pltpu.HBM)
    shapes = [pltpu.HBM((CH, rows, NX), F32)] + [pltpu.HBM((CH, 16, NX), F32)] * 2
    if tiles > 2:
        shapes += [pltpu.HBM((CH, rows - 16, NX), F32)] * 2
    return pl.pallas_call(
        functools.partial(own_kernel, (upper, lower, len(shapes))),
        out_shape=shapes,
        in_specs=[hbm] * 3 + [pl.BlockSpec(memory_space=pl.ANY)],
        out_specs=[hbm] * len(shapes),
        scratch_shapes=[
            pltpu.VMEM((tiles + 2, 2, CH, 8, 128), F32),
            pltpu.VMEM((2, CH, NX), F32),
            pltpu.VMEM((CH, 27), F32),
            pltpu.VMEM((CH, CH), F32),
            pltpu.VMEM((3, tiles, CH, 8, NX), F32),
            pltpu.VMEM((3, rows + 4, CH, NX), F32),
            pltpu.VMEM((3, rows, CH, NX), F32),
            pltpu.VMEM((27, CH, 128), F32),
            pltpu.SemaphoreType.DMA((tiles + 2, 2)),
            pltpu.SemaphoreType.DMA((3, tiles)),
            pltpu.SemaphoreType.DMA((3,)),
        ],
        compiler_params=params(),
        cost_estimate=cost(10**8, 2**18),
        name="own_sums",
    )(*in_hbm(weight, point, field), halo)


def middle_call(weight, point, low, own, high):
    rows = own.shape[0] - 2
    hbm = pl.BlockSpec(memory_space=pltpu.HBM)
    return pl.pallas_call(
        middle_kernel,
        out_shape=pltpu.HBM((CH, rows, NX), F32),
        in_specs=[hbm] * 2 + [pl.BlockSpec(memory_space=pl.ANY)] * 3,
        out_specs=hbm,
        scratch_shapes=[
            pltpu.VMEM((3, rows + 2, CH, NX), F32),
            pltpu.VMEM((CH, 27), F32),
            pltpu.VMEM((CH, CH), F32),
            pltpu.VMEM((rows // 8, CH, 8, NX), F32),
            pltpu.VMEM((3, rows + 2, CH, NX), F32),
            pltpu.VMEM((1, rows, CH, NX), F32),
            pltpu.VMEM((27, CH, 128), F32),
            pltpu.SemaphoreType.DMA((3,)),
            pltpu.SemaphoreType.DMA((rows // 8,)),
            pltpu.SemaphoreType.DMA((2,)),
        ],
        compiler_params=params(),
        cost_estimate=cost(10**8, 2**18),
        name="middle_sums",
    )(*in_hbm(weight, point), low, own, high)


def finish_call(result, base, low, high):
    last = result.shape[1] // 8 - 1
    piece = pl.BlockSpec((CH, 8, NX), lambda i: (0, i, 0))
    return pl.pallas_call(
        finish_kernel,
        out_shape=jax.ShapeDtypeStruct(result.shape, F32),
        grid=(2,),
        in_specs=[pl.BlockSpec(memory_space=pl.ANY), piece, piece, piece],
        out_specs=pl.BlockSpec((CH, 8, NX), lambda i: (0, i * last, 0)),
        input_output_aliases={0: 0},
        compiler_params=params(),
        cost_estimate=cost(10**8, 2**18),
        name="finished_rows",
    )(result, base, low, high)


def general_filter(coarse, gains, gz, gy, scale):
    j_own, n_own = gains.shape[2], gains.shape[3]
    both = ("gz", "gy")
    flat = coarse.reshape(CH // 2, MY, 2, 2, MX).transpose(3, 1, 0, 2, 4).reshape(2, MY, CH * MX)
    sent = flat.reshape(2, gy, j_own, gz, n_own).transpose(3, 1, 0, 2, 4).reshape(gz * gy, -1)
    got = lax.all_to_all(sent, both, split_axis=0, concat_axis=0, tiled=True)
    got = got.reshape(gz, gy, 2, j_own, n_own)
    c, s = (jnp.asarray(t, F32) for t in trig(kept(MZ, gz), np.arange(gz), gz))
    mul = functools.partial(jnp.einsum, precision=lax.Precision.HIGHEST)
    whole = got.sum(axis=1) * scale
    real = mul("zjn,qz->qjn", whole[:, 0], c) + mul("zjn,qz->qjn", whole[:, 1], s)
    imag = mul("zjn,qz->qjn", whole[:, 1], c) - mul("zjn,qz->qjn", whole[:, 0], s)
    real, imag = real * gains[0] - imag * gains[1], real * gains[1] + imag * gains[0]
    out = jnp.stack(
        [
            mul("qjn,qz->zjn", real, c) - mul("qjn,qz->zjn", imag, s),
            mul("qjn,qz->zjn", real, s) + mul("qjn,qz->zjn", imag, c),
        ],
        axis=1,
    )
    out = jnp.broadcast_to(out[:, None], (gz, gy, 2, j_own, n_own)).reshape(gz * gy, -1)
    back = lax.all_to_all(out, both, split_axis=0, concat_axis=0, tiled=True)
    back = back.reshape(gz, gy, 2, j_own, n_own).transpose(2, 1, 3, 0, 4)
    back = back.reshape(2, MY, CH // 2, 2, MX)
    return back.transpose(2, 1, 3, 0, 4).reshape(CH // 2, MY, 4 * MX)


def body(field, spectral_filter, depth_weight, point_weight, bias_vector):
    gz, gy = lax.axis_size("gz"), lax.axis_size("gy")
    y_local = field.shape[2]
    field = field.reshape(CH, y_local, NX)
    y_total = gy * y_local
    forward_scale = 1.0 / math.sqrt(float(NX) * y_total * gz)
    inverse_scale = 1.0 / math.sqrt(2.0 * MX * MY * MZ)

    def ring(axis, count, by):
        return [(i, (i + by) % count) for i in range(count)]

    def to_neighbours(down, up):
        return (
            lax.ppermute(down, "gz", ring("gz", gz, 1)),
            lax.ppermute(up, "gz", ring("gz", gz, -1)),
        )

    def after(value, *others):
        return lax.optimization_barrier((value, *others))[0]

    tiles = y_local // 8
    side = 2 if tiles >= 6 else 1
    upper, lower = tuple(range(side)), tuple(range(tiles - side, tiles))
    middle = tuple(range(side, tiles - side))

    packed, edges = pack_call(field, middle)
    packed_low, packed_high = to_neighbours(packed, packed)
    if gy == 2:
        halo = lax.ppermute(edges, "gy", ring("gy", gy, 1))
    else:
        halo = jnp.stack(
            [
                lax.ppermute(edges[0], "gy", ring("gy", gy, 1)),
                lax.ppermute(edges[1], "gy", ring("gy", gy, -1)),
            ]
        )
    coarse = forward_call(after(field, packed), gy)
    sums = own_call(after(field, coarse), halo, depth_weight, point_weight, upper, lower)
    own, down, up = sums[:3]
    inner_pair = to_neighbours(*sums[3:]) if len(sums) > 3 else ()

    j_own, n_own = spectral_filter.shape[2], spectral_filter.shape[3]
    if j_own == 8 and n_own == 2 * MX:
        both = ("gz", "gy")
        sent = coarse.reshape(gz * gy * 8, 4 * MX)
        got = lax.all_to_all(sent, both, split_axis=0, concat_axis=0, tiled=True)
        out = filter_call(got, after(spectral_filter, own), gz, gy, forward_scale)
        back = lax.all_to_all(out, both, split_axis=0, concat_axis=0, tiled=True)
        back = back.reshape(CH // 2, MY, 4 * MX)
    else:
        back = general_filter(coarse, spectral_filter, gz, gy, forward_scale)

    down, up = (after(value, back) for value in (down, up))
    outer_pair = to_neighbours(down, up)
    mixed = middle_call(depth_weight, point_weight, packed_low, after(packed, back), packed_high)
    result, base = inverse_call(
        back, bias_vector, mixed, own, inner_pair, (upper, lower), y_local, gy, inverse_scale
    )
    result = finish_call(result, base, *outer_pair)
    return result.reshape(CH, 1, y_local, NX)


def solution(mesh):
    in_specs = (P(None, "gz", "gy", None), P(None, None, "gy", "gz"), P(), P(), P())
    out_specs = P(None, "gz", "gy", None)
    return jax.shard_map(body, mesh=mesh, in_specs=in_specs, out_specs=out_specs, check_vma=False)
```

```python
import functools
import math

import jax
import jax.numpy as jnp
import ml_dtypes
import numpy as np
from jax import lax
from jax.experimental import pallas as pl
from jax.experimental.pallas import tpu as pltpu
from jax.sharding import PartitionSpec as P

NX = 256
MX = 32
MY = 16
MZ = 16
CH = 32
VMEM_BYTES = 24 * 1024 * 1024
BF = jnp.bfloat16
F32 = jnp.float32


def kept(count, total):
    series = np.arange(count)
    return np.where(series < count // 2, series, total - count + series)


def trig(freqs, places, total):
    angle = 2.0 * np.pi * ((freqs[:, None] * places[None, :]) % total) / total
    return np.cos(angle), np.sin(angle)


def halves(table):
    table = np.asarray(table, np.float64)
    top = table.astype(np.float32).astype(ml_dtypes.bfloat16)
    rest = (table - top.astype(np.float64)).astype(np.float32).astype(ml_dtypes.bfloat16)
    return jnp.asarray(top), jnp.asarray(rest)


def y_table(y_local, gy, inverse):
    out = []
    for g in range(gy):
        places = g * y_local + np.arange(y_local)
        out.append(np.concatenate(trig(kept(MY, y_local * gy), places, y_local * gy), axis=0))
    return np.stack([t.T for t in out] if inverse else out)


def x_table(inverse, scale=1.0):
    c, s = trig(np.arange(MX), np.arange(NX), NX)
    w = np.where(np.arange(MX) == 0, 1.0, 2.0)[:, None] if inverse else 1.0
    out = np.zeros((2, 2, 2, MX, NX))
    for p in range(2):
        out[p, p, 0] = w * c * scale
        out[p, p, 1] = -w * s * scale
    out = out.reshape(2, 4 * MX, NX)
    return out if inverse else out.transpose(0, 2, 1)


def z_tables(gz, gy, rows, scale):
    c, s = trig(kept(MZ, gz), np.arange(gz), gz)
    eye = np.eye(rows)
    one = np.ones(gy)
    both = np.stack([c, s])
    fwd = np.einsum("tqz,g,jk->tqjzgk", both, one, eye) * scale
    inv = np.einsum("tqz,g,jk->tzgjqk", both, one, eye)
    return fwd.reshape(2 * MZ * rows, gz * gy * rows), inv.reshape(2 * gz * gy * rows, MZ * rows)


def parts(value):
    top = value.astype(BF)
    return top, (value - top.astype(F32)).astype(BF)


def dot(a, b):
    return jnp.dot(a, b, preferred_element_type=F32)


def dot3(a, b):
    rows = a[0].shape[0]
    both = dot(jnp.concatenate([a[0], a[1]], axis=0), b[0])
    return both[:rows] + (both[rows:] + dot(a[0], b[1]))


def swap_parts(value):
    lane = lax.broadcasted_iota(jnp.int32, value.shape, 1)
    is_real = (lane // MX) % 2 == 0
    width = value.shape[1]
    return jnp.where(is_real, pltpu.roll(value, width - MX, 1), pltpu.roll(value, MX, 1)), is_real


def forward_kernel(field, x_top, x_rest, y_top, y_rest, out, taken, x_both, y_both, sem):
    gy = lax.axis_index("gy")
    few = [
        pltpu.make_async_copy(src, dst, sem.at[4 + i])
        for i, (src, dst) in enumerate(
            ((x_top, x_both.at[0]), (x_rest, x_both.at[1]), (y_top.at[gy], y_both.at[0]), (y_rest.at[gy], y_both.at[1]))
        )
    ]
    copies = [pltpu.make_async_copy(field.at[:, q], taken.at[q], sem.at[q]) for q in range(4)]
    for copy in few + copies:
        copy.start()
    for copy in few:
        copy.wait()
    groups, rows = taken.shape[1:3]
    halves_of = []
    for q in range(4):
        copies[q].wait()
        part = dot3(parts(taken[q].reshape(groups * rows, NX)), (x_both[0, q % 2], x_both[1, q % 2]))
        if q % 2:
            halves_of[-1] = halves_of[-1] + part
        else:
            halves_of.append(part)
    total = jnp.concatenate(halves_of, axis=1)
    for g in range(groups):
        both = dot3((y_both[0], y_both[1]), parts(total[g * rows : (g + 1) * rows]))
        crossed, is_real = swap_parts(both[MY:])
        modes = both[:MY] + jnp.where(is_real, crossed, -crossed)
        out[pl.ds(2 * g * MY, MY), :] = modes[:, : 4 * MX]
        out[pl.ds((2 * g + 1) * MY, MY), :] = modes[:, 4 * MX :]


def filter_kernel(arrived, gains, f_top, f_rest, i_top, i_rest, out):
    real, imag = (gains[r].reshape(-1, 2 * MX) for r in range(2))
    first, second = slice(0, MX), slice(MX, 2 * MX)
    same = jnp.concatenate([real[:, first], real[:, first], real[:, second], real[:, second]], axis=1)
    cross = jnp.concatenate([-imag[:, first], imag[:, first], -imag[:, second], imag[:, second]], axis=1)
    half = f_top.shape[0] // 2
    turned = dot3((f_top[...], f_rest[...]), parts(arrived[...]))
    crossed, is_real = swap_parts(turned[half:])
    modes = turned[:half] + jnp.where(is_real, crossed, -crossed)
    crossed, _ = swap_parts(modes)
    filtered = modes * same + crossed * cross
    half = i_top.shape[0] // 2
    back = dot3((i_top[...], i_rest[...]), parts(filtered))
    crossed, is_real = swap_parts(back[half:])
    out[...] = back[:half] + jnp.where(is_real, -crossed, crossed)


def fetch_tiles(field, taken, sems, wanted):
    pending = {}
    for k, t in enumerate(wanted):
        pending[t] = [
            pltpu.make_async_copy(
                field.at[:, pl.ds(8 * t, 8), pl.ds(128 * h, 128)], taken.at[k, h], sems.at[k, h]
            )
            for h in range(2)
        ]
        for copy in pending[t]:
            copy.start()

    def row(t, r):
        for copy in pending.pop(t, ()):
            copy.wait()
        k = wanted.index(t)
        return jnp.concatenate(
            [taken.at[k, h].reshape(CH * 8, 128)[pl.ds(r, CH, stride=8), :] for h in range(2)], axis=1
        )

    return row


def spread_gains(weights, gains, offsets):
    for k in [9 * a + j for a in offsets for j in range(9)]:
        gains[k] = jnp.broadcast_to(weights[:, k : k + 1], (CH, 128))


def mixing(points):
    down = (
        lax.broadcasted_iota(jnp.int32, (8 * CH, CH), 0) // 8
        == lax.broadcasted_iota(jnp.int32, (8 * CH, CH), 1)
    ).astype(BF)
    across = (
        lax.broadcasted_iota(jnp.int32, (CH, 8 * CH), 1) % CH
        == lax.broadcasted_iota(jnp.int32, (CH, 8 * CH), 0)
    ).astype(BF)
    same = (
        lax.broadcasted_iota(jnp.int32, (8 * CH, 8 * CH), 0) % 8
        == lax.broadcasted_iota(jnp.int32, (8 * CH, 8 * CH), 1) // CH
    )
    return tuple(
        jnp.where(same, dot(dot(down, part).astype(BF), across), 0.0).astype(BF)
        for part in parts(points)
    )


def turn(turned, at, value):
    turned[0, at] = pltpu.roll(value, 1, 1)
    turned[1, at] = value
    turned[2, at] = pltpu.roll(value, NX - 1, 1)


def tap_sums(turned, depth, gains, runs, offsets, fresh):
    def some(i, _):
        chans = pl.ds(pl.multiple_of(i * 8, 8), 8)
        gain = {k: gains[k, chans, :] for a in offsets for k in range(9 * a, 9 * a + 9)}
        for h in range(2):
            lanes = pl.ds(128 * h, 128)
            for first, to, rows in runs:
                sums = {}
                for r in range(rows + 2):
                    values = [turned[e, first + r, chans, lanes] for e in range(3)]
                    for b in range(3):
                        o = r - b
                        if o < 0 or o >= rows:
                            continue
                        for k, a in enumerate(offsets):
                            for e in range(3):
                                term = gain[a * 9 + b * 3 + e] * values[e]
                                if (o, k) in sums:
                                    sums[o, k] = sums[o, k] + term
                                elif fresh:
                                    sums[o, k] = term
                                else:
                                    sums[o, k] = depth[k, to + o, chans, lanes] + term
                    if r >= 2:
                        for k in range(len(offsets)):
                            depth[k, to + r - 2, chans, lanes] = sums.pop((r - 2, k))
        return 0

    lax.fori_loop(0, CH // 8, some, 0)


def mix_tile(mix, depth, k, t):
    tile = depth[k, pl.ds(8 * t, 8)].reshape(8 * CH, NX)
    return dot3(mix, parts(tile)).reshape(CH, 8, NX)


def pack_kernel(middle, field, packed, edges, taken, rows, ends, sem_in, sem_out):
    last = field.shape[1] // 8 - 1
    before, after = middle[0] - 1, middle[-1] + 1
    wanted = [before, *middle, after] + [t for t in (0, last) if t not in (before, after)]
    row = fetch_tiles(field, taken, sem_in, wanted)
    places = [(before, 7), *[(t, r) for t in middle for r in range(8)], (after, 0)]
    copies, sent = [], 0
    for i, place in enumerate(places):
        rows[i] = row(*place)
        if i + 1 - sent >= 17 or i + 1 == len(places):
            some = pl.ds(sent, i + 1 - sent)
            copies.append(pltpu.make_async_copy(rows.at[some], packed.at[some], sem_out.at[len(copies)]))
            copies[-1].start()
            sent = i + 1
    ends[0] = row(last, 7)
    ends[1] = row(0, 0)
    copies.append(pltpu.make_async_copy(ends, edges, sem_out.at[len(copies)]))
    copies[-1].start()
    for copy in copies:
        copy.wait()


def own_kernel(plan, weight, point, field, halo, *refs):
    upper, lower, count = plan
    outs, refs = refs[:count], refs[count:]
    taken, halo_rows, weights, points, sent, turned, depth, gains, sem_in, sem_out, sem_few = refs
    few = [
        pltpu.make_async_copy(a, b, sem_few.at[i])
        for i, (a, b) in enumerate(((weight, weights), (point, points), (halo, halo_rows)))
    ]
    for copy in few:
        copy.start()
    wanted = [*upper, upper[-1] + 1, lower[0] - 1, *lower]
    row = fetch_tiles(field, taken, sem_in, wanted)
    for copy in few:
        copy.wait()
    spread_gains(weights, gains, range(3))
    mix = mixing(points[...])
    rows = 8 * len(upper)
    for i, place in enumerate([None, *[(t, r) for t in upper for r in range(8)], (upper[-1] + 1, 0)]):
        turn(turned, i, halo_rows[0] if place is None else row(*place))
    for i, place in enumerate([(lower[0] - 1, 7), *[(t, r) for t in lower for r in range(8)], None]):
        turn(turned, rows + 2 + i, halo_rows[1] if place is None else row(*place))
    tap_sums(turned, depth, gains, [(0, 0, rows), (rows + 2, rows, rows)], range(3), True)
    copies = []
    own, pairs = outs[0], outs[1:]
    tiles = [*upper, *lower]
    order = sorted(range(len(tiles)), key=lambda t: tiles[t] in (upper[0], lower[-1]))
    for t in order:
        outer = tiles[t] in (upper[0], lower[-1])
        group = pairs[2:] if count == 5 and not outer else pairs[:2]
        slot = 0 if t < len(upper) else 1
        for k, out, at in ((0, group[0], slot), (2, group[1], slot), (1, own, t)):
            sent[k, t] = mix_tile(mix, depth, k, t)
            copies.append(
                pltpu.make_async_copy(sent.at[k, t], out.at[:, pl.ds(8 * at, 8), :], sem_out.at[k, t])
            )
            copies[-1].start()
    for copy in copies:
        copy.wait()


def middle_kernel(weight, point, *refs):
    planes, out = refs[:3], refs[3]
    taken, weights, points, sent, turned, depth, gains, sem_in, sem_out, sem_few = refs[4:]
    few = [
        pltpu.make_async_copy(a, b, sem_few.at[i])
        for i, (a, b) in enumerate(((weight, weights), (point, points)))
    ]
    arrivals = [pltpu.make_async_copy(planes[a], taken.at[a], sem_in.at[a]) for a in range(3)]
    for copy in few + arrivals:
        copy.start()
    for copy in few:
        copy.wait()
    spread_gains(weights, gains, range(3))
    mix = mixing(points[...])
    rows = out.shape[1]
    for a in (1, 0, 2):
        arrivals[a].wait()
        for r in range(rows + 2):
            turn(turned, r, taken[a, r])
        tap_sums(turned, depth, gains, [(0, 0, rows)], [a], a == 1)
    copies = []
    for t in range(rows // 8):
        sent[t] = mix_tile(mix, depth, 0, t)
        copies.append(pltpu.make_async_copy(sent.at[t], out.at[:, pl.ds(8 * t, 8), :], sem_out.at[t]))
        copies[-1].start()
    for copy in copies:
        copy.wait()


def gelu(value):
    return 0.5 * value * (1.0 + lax.erf(value * (1.0 / math.sqrt(2.0))))


def inverse_kernel(plan, modes, bias, x_top, x_rest, y_top, y_rest, middle, own, *refs):
    upper, lower = plan
    out, base, columns = refs[-3:]
    q = pl.program_id(0)
    groups, _, y_local, _ = out.shape

    @pl.when(q == 0)
    def _():
        gy = lax.axis_index("gy")
        for g in range(groups):
            own_modes = jnp.concatenate([modes[2 * g], modes[2 * g + 1]], axis=1)
            crossed, is_real = swap_parts(own_modes)
            stack = jnp.concatenate([own_modes, jnp.where(is_real, -crossed, crossed)], axis=0)
            pair = parts(dot3((y_top[gy], y_rest[gy]), parts(stack)))
            for h in range(2):
                for k in range(2):
                    columns[h, k, pl.ds(g * y_local, y_local), :] = pair[k][:, 128 * h : 128 * h + 128]

    h, p = q // 2, q % 2
    rows = dot3((columns[h, 0], columns[h, 1]), (x_top[p], x_rest[p]))
    start, stop = 8 * upper[-1] + 8, 8 * lower[0]
    for g in range(groups):
        plane = rows[g * y_local : (g + 1) * y_local] + bias[4 * g + q]
        out[g, 0, start:stop] = gelu(plane[start:stop] + middle[g, 0])
        first = plane[:start] + own[g, 0, :start]
        second = plane[stop:] + own[g, 0, start:]
        base[g, 0, :8] = first[:8]
        base[g, 0, 8:] = second[-8:]
        if start > 8:
            low, high = refs[:2]
            out[g, 0, 8:start] = gelu(first[8:] + (low[g, 0, : start - 8] + high[g, 0, : start - 8]))
            out[g, 0, stop : y_local - 8] = gelu(
                second[:-8] + (low[g, 0, start - 8 :] + high[g, 0, start - 8 :])
            )


def finish_kernel(_, base, low, high, out):
    out[...] = gelu(base[...] + (low[...] + high[...]))


def in_hbm(*arrays):
    return [pltpu.with_memory_space_constraint(a, pltpu.HBM) for a in arrays]


def params():
    return pltpu.CompilerParams(vmem_limit_bytes=VMEM_BYTES)


def cost(flops, moved):
    return pl.CostEstimate(flops=flops, bytes_accessed=moved, transcendentals=0)


def whole_block(table):
    return pl.BlockSpec(table.shape, lambda i: (0,) * table.ndim)


def by_four(array):
    return array.reshape(CH // 4, 4, *array.shape[1:])


def forward_call(field, gy, pinned):
    y_local = field.shape[1]
    tables = [*halves(x_table(False)), *halves(y_table(y_local, gy, False))]
    hbm = pl.BlockSpec(memory_space=pltpu.HBM)
    return pl.pallas_call(
        forward_kernel,
        out_shape=(pltpu.HBM if pinned else jax.ShapeDtypeStruct)((CH // 2 * MY, 4 * MX), F32),
        in_specs=[hbm] * 5,
        scratch_shapes=[
            pltpu.VMEM((4, CH // 4, y_local, NX), F32),
            pltpu.VMEM((2, 2, NX, 4 * MX), BF),
            pltpu.VMEM((2, 2 * MY, y_local), BF),
            pltpu.SemaphoreType.DMA((8,)),
        ],
        compiler_params=params(),
        cost_estimate=cost(10**8, 2**18),
        name="forward_modes",
    )(*in_hbm(by_four(field), *tables))


def filter_call(arrived, gains, gz, gy, scale):
    fwd, inv = z_tables(gz, gy, gains.shape[2], scale)
    fwd, inv = halves(fwd), halves(inv)
    return pl.pallas_call(
        filter_kernel,
        out_shape=pltpu.HBM(arrived.shape, F32),
        compiler_params=params(),
        cost_estimate=cost(10**8, 2**18),
        name="filter_modes",
    )(arrived, *in_hbm(gains, *fwd, *inv))


def inverse_call(modes, bias, middle, own, pair, plan, y_local, gy, scale):
    tables = [*halves(x_table(True, scale)), *halves(y_table(y_local, gy, True))]
    some = lambda rows: pl.BlockSpec((CH // 4, 1, rows, NX), lambda i: (0, i, 0, 0))
    planes = [*in_hbm(by_four(middle), by_four(own)), *map(by_four, pair)]
    result, base = pl.pallas_call(
        functools.partial(inverse_kernel, plan),
        out_shape=[
            jax.ShapeDtypeStruct((CH // 4, 4, y_local, NX), F32),
            jax.ShapeDtypeStruct((CH // 4, 4, 16, NX), F32),
        ],
        grid=(4,),
        in_specs=[
            whole_block(modes),
            pl.BlockSpec(memory_space=pltpu.SMEM),
            *[whole_block(t) for t in tables],
            *[some(p.shape[2]) for p in planes],
        ],
        out_specs=[some(y_local), some(16)],
        scratch_shapes=[pltpu.VMEM((2, 2, CH // 4 * y_local, 128), BF)],
        compiler_params=params(),
        cost_estimate=cost(10**8, 2**18),
        name="inverse_modes",
    )(modes, *in_hbm(bias, *tables), *planes)
    return result.reshape(CH, y_local, NX), base.reshape(CH, 16, NX)


def pack_call(field, middle):
    count = 8 * len(middle) + 2
    fetched = len(middle) + 4
    hbm = pl.BlockSpec(memory_space=pltpu.HBM)
    return pl.pallas_call(
        functools.partial(pack_kernel, middle),
        out_shape=[pltpu.HBM((count, CH, NX), F32), pltpu.HBM((2, CH, NX), F32)],
        in_specs=[hbm],
        out_specs=[hbm] * 2,
        scratch_shapes=[
            pltpu.VMEM((fetched, 2, CH, 8, 128), F32),
            pltpu.VMEM((count, CH, NX), F32),
            pltpu.VMEM((2, CH, NX), F32),
            pltpu.SemaphoreType.DMA((fetched, 2)),
            pltpu.SemaphoreType.DMA((count // 17 + 2,)),
        ],
        compiler_params=params(),
        cost_estimate=cost(10**8, 2**18),
        name="packed_rows",
    )(*in_hbm(field))


def own_call(field, halo, weight, point, upper, lower):
    tiles = len(upper) + len(lower)
    rows = 8 * tiles
    hbm = pl.BlockSpec(memory_space=pltpu.HBM)
    shapes = [pltpu.HBM((CH, rows, NX), F32)] + [pltpu.HBM((CH, 16, NX), F32)] * 2
    if tiles > 2:
        shapes += [pltpu.HBM((CH, rows - 16, NX), F32)] * 2
    return pl.pallas_call(
        functools.partial(own_kernel, (upper, lower, len(shapes))),
        out_shape=shapes,
        in_specs=[hbm] * 3 + [pl.BlockSpec(memory_space=pl.ANY)],
        out_specs=[hbm] * len(shapes),
        scratch_shapes=[
            pltpu.VMEM((tiles + 2, 2, CH, 8, 128), F32),
            pltpu.VMEM((2, CH, NX), F32),
            pltpu.VMEM((CH, 27), F32),
            pltpu.VMEM((CH, CH), F32),
            pltpu.VMEM((3, tiles, CH, 8, NX), F32),
            pltpu.VMEM((3, rows + 4, CH, NX), F32),
            pltpu.VMEM((3, rows, CH, NX), F32),
            pltpu.VMEM((27, CH, 128), F32),
            pltpu.SemaphoreType.DMA((tiles + 2, 2)),
            pltpu.SemaphoreType.DMA((3, tiles)),
            pltpu.SemaphoreType.DMA((3,)),
        ],
        compiler_params=params(),
        cost_estimate=cost(10**8, 2**18),
        name="own_sums",
    )(*in_hbm(weight, point, field), halo)


def middle_call(weight, point, low, own, high):
    rows = own.shape[0] - 2
    hbm = pl.BlockSpec(memory_space=pltpu.HBM)
    return pl.pallas_call(
        middle_kernel,
        out_shape=pltpu.HBM((CH, rows, NX), F32),
        in_specs=[hbm] * 2 + [pl.BlockSpec(memory_space=pl.ANY)] * 3,
        out_specs=hbm,
        scratch_shapes=[
            pltpu.VMEM((3, rows + 2, CH, NX), F32),
            pltpu.VMEM((CH, 27), F32),
            pltpu.VMEM((CH, CH), F32),
            pltpu.VMEM((rows // 8, CH, 8, NX), F32),
            pltpu.VMEM((3, rows + 2, CH, NX), F32),
            pltpu.VMEM((1, rows, CH, NX), F32),
            pltpu.VMEM((27, CH, 128), F32),
            pltpu.SemaphoreType.DMA((3,)),
            pltpu.SemaphoreType.DMA((rows // 8,)),
            pltpu.SemaphoreType.DMA((2,)),
        ],
        compiler_params=params(),
        cost_estimate=cost(10**8, 2**18),
        name="middle_sums",
    )(*in_hbm(weight, point), low, *in_hbm(own), high)


def finish_call(result, base, low, high):
    last = result.shape[1] // 8 - 1
    piece = pl.BlockSpec((CH, 8, NX), lambda i: (0, i, 0))
    return pl.pallas_call(
        finish_kernel,
        out_shape=jax.ShapeDtypeStruct(result.shape, F32),
        grid=(2,),
        in_specs=[pl.BlockSpec(memory_space=pl.ANY), piece, piece, piece],
        out_specs=pl.BlockSpec((CH, 8, NX), lambda i: (0, i * last, 0)),
        input_output_aliases={0: 0},
        compiler_params=params(),
        cost_estimate=cost(10**8, 2**18),
        name="finished_rows",
    )(result, base, low, high)


def general_filter(coarse, gains, gz, gy, scale):
    j_own, n_own = gains.shape[2], gains.shape[3]
    both = ("gz", "gy")
    flat = coarse.reshape(CH // 2, MY, 2, 2, MX).transpose(3, 1, 0, 2, 4).reshape(2, MY, CH * MX)
    sent = flat.reshape(2, gy, j_own, gz, n_own).transpose(3, 1, 0, 2, 4).reshape(gz * gy, -1)
    got = lax.all_to_all(sent, both, split_axis=0, concat_axis=0, tiled=True)
    got = got.reshape(gz, gy, 2, j_own, n_own)
    c, s = (jnp.asarray(t, F32) for t in trig(kept(MZ, gz), np.arange(gz), gz))
    mul = functools.partial(jnp.einsum, precision=lax.Precision.HIGHEST)
    whole = got.sum(axis=1) * scale
    real = mul("zjn,qz->qjn", whole[:, 0], c) + mul("zjn,qz->qjn", whole[:, 1], s)
    imag = mul("zjn,qz->qjn", whole[:, 1], c) - mul("zjn,qz->qjn", whole[:, 0], s)
    real, imag = real * gains[0] - imag * gains[1], real * gains[1] + imag * gains[0]
    out = jnp.stack(
        [
            mul("qjn,qz->zjn", real, c) - mul("qjn,qz->zjn", imag, s),
            mul("qjn,qz->zjn", real, s) + mul("qjn,qz->zjn", imag, c),
        ],
        axis=1,
    )
    out = jnp.broadcast_to(out[:, None], (gz, gy, 2, j_own, n_own)).reshape(gz * gy, -1)
    back = lax.all_to_all(out, both, split_axis=0, concat_axis=0, tiled=True)
    back = back.reshape(gz, gy, 2, j_own, n_own).transpose(2, 1, 3, 0, 4)
    back = back.reshape(2, MY, CH // 2, 2, MX)
    return back.transpose(2, 1, 3, 0, 4).reshape(CH // 2, MY, 4 * MX)


def body(field, spectral_filter, depth_weight, point_weight, bias_vector):
    gz, gy = lax.axis_size("gz"), lax.axis_size("gy")
    y_local = field.shape[2]
    field = field.reshape(CH, y_local, NX)
    y_total = gy * y_local
    forward_scale = 1.0 / math.sqrt(float(NX) * y_total * gz)
    inverse_scale = 1.0 / math.sqrt(2.0 * MX * MY * MZ)

    def ring(axis, count, by):
        return [(i, (i + by) % count) for i in range(count)]

    def to_neighbours(down, up):
        return (
            lax.ppermute(down, "gz", ring("gz", gz, 1)),
            lax.ppermute(up, "gz", ring("gz", gz, -1)),
        )

    def after(value, *others):
        return lax.optimization_barrier((value, *others))[0]

    tiles = y_local // 8
    side = 2 if tiles >= 6 else 1
    upper, lower = tuple(range(side)), tuple(range(tiles - side, tiles))
    middle = tuple(range(side, tiles - side))

    packed, edges = pack_call(field, middle)
    packed_low, packed_high = to_neighbours(packed, packed)
    if gy == 2:
        halo = lax.ppermute(edges, "gy", ring("gy", gy, 1))
    else:
        halo = jnp.stack(
            [
                lax.ppermute(edges[0], "gy", ring("gy", gy, 1)),
                lax.ppermute(edges[1], "gy", ring("gy", gy, -1)),
            ]
        )
    j_own, n_own = spectral_filter.shape[2], spectral_filter.shape[3]
    whole_tiles = j_own == 8 and n_own == 2 * MX
    coarse = forward_call(after(field, packed), gy, whole_tiles)
    coarse = after(coarse, halo)
    sums = own_call(after(field, coarse), halo, depth_weight, point_weight, upper, lower)
    own, down, up = sums[:3]
    inner_pair = to_neighbours(*sums[3:]) if len(sums) > 3 else ()

    if whole_tiles:
        both = ("gz", "gy")
        got = lax.all_to_all(coarse, both, split_axis=0, concat_axis=0, tiled=True)
        out = filter_call(got, after(spectral_filter, own), gz, gy, forward_scale)
        back = lax.all_to_all(out, both, split_axis=0, concat_axis=0, tiled=True)
        back = back.reshape(CH // 2, MY, 4 * MX)
    else:
        back = general_filter(coarse, spectral_filter, gz, gy, forward_scale)

    down, up, packed, *inner_pair = lax.optimization_barrier((down, up, packed, *inner_pair, back))[:-1]
    outer_pair = to_neighbours(down, up)
    mixed = middle_call(depth_weight, point_weight, packed_low, packed, packed_high)
    result, base = inverse_call(
        back, bias_vector, mixed, own, inner_pair, (upper, lower), y_local, gy, inverse_scale
    )
    result = finish_call(result, base, *outer_pair)
    return result.reshape(CH, 1, y_local, NX)


def solution(mesh):
    in_specs = (P(None, "gz", "gy", None), P(None, None, "gy", "gz"), P(), P(), P())
    out_specs = P(None, "gz", "gy", None)
    return jax.shard_map(body, mesh=mesh, in_specs=in_specs, out_specs=out_specs, check_vma=False)
```

```python
import functools
import math

import jax
import jax.numpy as jnp
import ml_dtypes
import numpy as np
from jax import lax
from jax.experimental import pallas as pl
from jax.experimental.pallas import tpu as pltpu
from jax.sharding import PartitionSpec as P

NX = 256
MX = 32
MY = 16
MZ = 16
CH = 32
VMEM_BYTES = 24 * 1024 * 1024
BF = jnp.bfloat16
F32 = jnp.float32


def kept(count, total):
    series = np.arange(count)
    return np.where(series < count // 2, series, total - count + series)


def trig(freqs, places, total):
    angle = 2.0 * np.pi * ((freqs[:, None] * places[None, :]) % total) / total
    return np.cos(angle), np.sin(angle)


def halves(table):
    table = np.asarray(table, np.float64)
    top = table.astype(np.float32).astype(ml_dtypes.bfloat16)
    rest = (table - top.astype(np.float64)).astype(np.float32).astype(ml_dtypes.bfloat16)
    return jnp.asarray(top), jnp.asarray(rest)


def y_table(y_local, gy, inverse):
    out = []
    for g in range(gy):
        places = g * y_local + np.arange(y_local)
        out.append(np.concatenate(trig(kept(MY, y_local * gy), places, y_local * gy), axis=0))
    return np.stack([t.T for t in out] if inverse else out)


def x_table(inverse, scale=1.0):
    c, s = trig(np.arange(MX), np.arange(NX), NX)
    w = np.where(np.arange(MX) == 0, 1.0, 2.0)[:, None] if inverse else 1.0
    out = np.zeros((2, 2, 2, MX, NX))
    for p in range(2):
        out[p, p, 0] = w * c * scale
        out[p, p, 1] = -w * s * scale
    out = out.reshape(2, 4 * MX, NX)
    return out if inverse else out.transpose(0, 2, 1)


def z_tables(gz, gy, rows, scale):
    c, s = trig(kept(MZ, gz), np.arange(gz), gz)
    eye = np.eye(rows)
    one = np.ones(gy)
    both = np.stack([c, s])
    fwd = np.einsum("tqz,g,jk->tqjzgk", both, one, eye) * scale
    inv = np.einsum("tqz,g,jk->tzgjqk", both, one, eye)
    return fwd.reshape(2 * MZ * rows, gz * gy * rows), inv.reshape(2 * gz * gy * rows, MZ * rows)


def parts(value):
    top = value.astype(BF)
    return top, (value - top.astype(F32)).astype(BF)


def dot(a, b):
    return jnp.dot(a, b, preferred_element_type=F32)


def dot3(a, b):
    rows = a[0].shape[0]
    both = dot(jnp.concatenate([a[0], a[1]], axis=0), b[0])
    return both[:rows] + (both[rows:] + dot(a[0], b[1]))


def swap_parts(value):
    lane = lax.broadcasted_iota(jnp.int32, value.shape, 1)
    is_real = (lane // MX) % 2 == 0
    width = value.shape[1]
    return jnp.where(is_real, pltpu.roll(value, width - MX, 1), pltpu.roll(value, MX, 1)), is_real


def forward_kernel(field, x_top, x_rest, y_top, y_rest, out, taken, x_both, y_both, sem):
    gy = lax.axis_index("gy")
    few = [
        pltpu.make_async_copy(src, dst, sem.at[4 + i])
        for i, (src, dst) in enumerate(
            ((x_top, x_both.at[0]), (x_rest, x_both.at[1]), (y_top.at[gy], y_both.at[0]), (y_rest.at[gy], y_both.at[1]))
        )
    ]
    copies = [pltpu.make_async_copy(field.at[:, q], taken.at[q], sem.at[q]) for q in range(4)]
    for copy in few + copies:
        copy.start()
    for copy in few:
        copy.wait()
    groups, rows = taken.shape[1:3]
    halves_of = []
    for q in range(4):
        copies[q].wait()
        part = dot3(parts(taken[q].reshape(groups * rows, NX)), (x_both[0, q % 2], x_both[1, q % 2]))
        if q % 2:
            halves_of[-1] = halves_of[-1] + part
        else:
            halves_of.append(part)
    total = jnp.concatenate(halves_of, axis=1)
    for g in range(groups):
        both = dot3((y_both[0], y_both[1]), parts(total[g * rows : (g + 1) * rows]))
        crossed, is_real = swap_parts(both[MY:])
        modes = both[:MY] + jnp.where(is_real, crossed, -crossed)
        out[pl.ds(2 * g * MY, MY), :] = modes[:, : 4 * MX]
        out[pl.ds((2 * g + 1) * MY, MY), :] = modes[:, 4 * MX :]


def filter_kernel(arrived, gains, f_top, f_rest, i_top, i_rest, out):
    real, imag = (gains[r].reshape(-1, 2 * MX) for r in range(2))
    first, second = slice(0, MX), slice(MX, 2 * MX)
    same = jnp.concatenate([real[:, first], real[:, first], real[:, second], real[:, second]], axis=1)
    cross = jnp.concatenate([-imag[:, first], imag[:, first], -imag[:, second], imag[:, second]], axis=1)
    half = f_top.shape[0] // 2
    turned = dot3((f_top[...], f_rest[...]), parts(arrived[...]))
    crossed, is_real = swap_parts(turned[half:])
    modes = turned[:half] + jnp.where(is_real, crossed, -crossed)
    crossed, _ = swap_parts(modes)
    filtered = modes * same + crossed * cross
    half = i_top.shape[0] // 2
    back = dot3((i_top[...], i_rest[...]), parts(filtered))
    crossed, is_real = swap_parts(back[half:])
    out[...] = back[:half] + jnp.where(is_real, -crossed, crossed)


def fetch_tiles(field, taken, sems, wanted):
    pending = {}
    for k, t in enumerate(wanted):
        pending[t] = [
            pltpu.make_async_copy(
                field.at[:, pl.ds(8 * t, 8), pl.ds(128 * h, 128)], taken.at[k, h], sems.at[k, h]
            )
            for h in range(2)
        ]
        for copy in pending[t]:
            copy.start()

    def row(t, r):
        for copy in pending.pop(t, ()):
            copy.wait()
        k = wanted.index(t)
        return jnp.concatenate(
            [taken.at[k, h].reshape(CH * 8, 128)[pl.ds(r, CH, stride=8), :] for h in range(2)], axis=1
        )

    return row


def spread_gains(weights, gains, offsets):
    for k in [9 * a + j for a in offsets for j in range(9)]:
        gains[k] = jnp.broadcast_to(weights[:, k : k + 1], (CH, 128))


def mixing(points):
    down = (
        lax.broadcasted_iota(jnp.int32, (8 * CH, CH), 0) // 8
        == lax.broadcasted_iota(jnp.int32, (8 * CH, CH), 1)
    ).astype(BF)
    across = (
        lax.broadcasted_iota(jnp.int32, (CH, 8 * CH), 1) % CH
        == lax.broadcasted_iota(jnp.int32, (CH, 8 * CH), 0)
    ).astype(BF)
    same = (
        lax.broadcasted_iota(jnp.int32, (8 * CH, 8 * CH), 0) % 8
        == lax.broadcasted_iota(jnp.int32, (8 * CH, 8 * CH), 1) // CH
    )
    return tuple(
        jnp.where(same, dot(dot(down, part).astype(BF), across), 0.0).astype(BF)
        for part in parts(points)
    )


def turn(turned, at, value):
    turned[0, at] = pltpu.roll(value, 1, 1)
    turned[1, at] = value
    turned[2, at] = pltpu.roll(value, NX - 1, 1)


def tap_sums(turned, depth, gains, runs, offsets, fresh):
    def some(i, _):
        chans = pl.ds(pl.multiple_of(i * 8, 8), 8)
        gain = {k: gains[k, chans, :] for a in offsets for k in range(9 * a, 9 * a + 9)}
        for h in range(2):
            lanes = pl.ds(128 * h, 128)
            for first, to, rows in runs:
                sums = {}
                for r in range(rows + 2):
                    values = [turned[e, first + r, chans, lanes] for e in range(3)]
                    for b in range(3):
                        o = r - b
                        if o < 0 or o >= rows:
                            continue
                        for k, a in enumerate(offsets):
                            for e in range(3):
                                term = gain[a * 9 + b * 3 + e] * values[e]
                                if (o, k) in sums:
                                    sums[o, k] = sums[o, k] + term
                                elif fresh:
                                    sums[o, k] = term
                                else:
                                    sums[o, k] = depth[k, to + o, chans, lanes] + term
                    if r >= 2:
                        for k in range(len(offsets)):
                            depth[k, to + r - 2, chans, lanes] = sums.pop((r - 2, k))
        return 0

    lax.fori_loop(0, CH // 8, some, 0)


def mix_tile(mix, depth, k, t):
    tile = depth[k, pl.ds(8 * t, 8)].reshape(8 * CH, NX)
    return dot3(mix, parts(tile)).reshape(CH, 8, NX)


def pack_kernel(middle, field, packed, edges, taken, rows, ends, sem_in, sem_out):
    last = field.shape[1] // 8 - 1
    before, after = middle[0] - 1, middle[-1] + 1
    wanted = [before, *middle, after] + [t for t in (0, last) if t not in (before, after)]
    row = fetch_tiles(field, taken, sem_in, wanted)
    places = [(before, 7), *[(t, r) for t in middle for r in range(8)], (after, 0)]
    copies, sent = [], 0
    for i, place in enumerate(places):
        rows[i] = row(*place)
        if i + 1 - sent >= 17 or i + 1 == len(places):
            some = pl.ds(sent, i + 1 - sent)
            copies.append(pltpu.make_async_copy(rows.at[some], packed.at[some], sem_out.at[len(copies)]))
            copies[-1].start()
            sent = i + 1
    ends[0] = row(last, 7)
    ends[1] = row(0, 0)
    copies.append(pltpu.make_async_copy(ends, edges, sem_out.at[len(copies)]))
    copies[-1].start()
    for copy in copies:
        copy.wait()


def own_kernel(plan, weight, point, field, halo, *refs):
    upper, lower = plan
    outs, refs = refs[:3], refs[3:]
    taken, halo_rows, weights, points, sent, turned, depth, gains, sem_in, sem_out, sem_few = refs
    few = [
        pltpu.make_async_copy(a, b, sem_few.at[i])
        for i, (a, b) in enumerate(((weight, weights), (point, points), (halo, halo_rows)))
    ]
    for copy in few:
        copy.start()
    wanted = [*upper, upper[-1] + 1, lower[0] - 1, *lower]
    row = fetch_tiles(field, taken, sem_in, wanted)
    for copy in few:
        copy.wait()
    spread_gains(weights, gains, range(3))
    mix = mixing(points[...])
    rows = 8 * len(upper)
    for i, place in enumerate([None, *[(t, r) for t in upper for r in range(8)], (upper[-1] + 1, 0)]):
        turn(turned, i, halo_rows[0] if place is None else row(*place))
    for i, place in enumerate([(lower[0] - 1, 7), *[(t, r) for t in lower for r in range(8)], None]):
        turn(turned, rows + 2 + i, halo_rows[1] if place is None else row(*place))
    tap_sums(turned, depth, gains, [(0, 0, rows), (rows + 2, rows, rows)], range(3), True)
    copies = []
    for t in range(2 * len(upper)):
        for k, out in enumerate(outs):
            sent[k, t] = mix_tile(mix, depth, k, t)
            copies.append(
                pltpu.make_async_copy(sent.at[k, t], out.at[:, pl.ds(8 * t, 8), :], sem_out.at[k, t])
            )
            copies[-1].start()
    for copy in copies:
        copy.wait()


def middle_kernel(weight, point, *refs):
    planes, out = refs[:3], refs[3]
    taken, weights, points, sent, turned, depth, gains, sem_in, sem_out, sem_few = refs[4:]
    few = [
        pltpu.make_async_copy(a, b, sem_few.at[i])
        for i, (a, b) in enumerate(((weight, weights), (point, points)))
    ]
    arrivals = [pltpu.make_async_copy(planes[a], taken.at[a], sem_in.at[a]) for a in range(3)]
    for copy in few + arrivals:
        copy.start()
    for copy in few:
        copy.wait()
    spread_gains(weights, gains, range(3))
    mix = mixing(points[...])
    rows = out.shape[1]
    for a in (1, 0, 2):
        arrivals[a].wait()
        for r in range(rows + 2):
            turn(turned, r, taken[a, r])
        tap_sums(turned, depth, gains, [(0, 0, rows)], [a], a == 1)
    copies = []
    for t in range(rows // 8):
        sent[t] = mix_tile(mix, depth, 0, t)
        copies.append(pltpu.make_async_copy(sent.at[t], out.at[:, pl.ds(8 * t, 8), :], sem_out.at[t]))
        copies[-1].start()
    for copy in copies:
        copy.wait()


def gelu(value):
    size = jnp.abs(value) * math.sqrt(0.5)
    below = 1.0 + 0.3275911 * size
    t = pl.reciprocal(below, approx=True)
    t = t * (2.0 - below * t)
    series = 1.061405429 * t - 1.453152027
    for factor in (1.421413741, -0.284496736, 0.254829592):
        series = series * t + factor
    tail = 0.5 * (series * t) * jnp.exp(-(size * size))
    return value * jnp.where(value < 0.0, tail, 1.0 - tail)


def inverse_kernel(modes, bias, x_top, x_rest, y_top, y_rest, middle, own, low, high, out, columns):
    q = pl.program_id(0)
    groups, _, y_local, _ = out.shape

    @pl.when(q == 0)
    def _():
        gy = lax.axis_index("gy")
        for g in range(groups):
            own_modes = jnp.concatenate([modes[2 * g], modes[2 * g + 1]], axis=1)
            crossed, is_real = swap_parts(own_modes)
            stack = jnp.concatenate([own_modes, jnp.where(is_real, -crossed, crossed)], axis=0)
            pair = parts(dot3((y_top[gy], y_rest[gy]), parts(stack)))
            for h in range(2):
                for k in range(2):
                    columns[h, k, pl.ds(g * y_local, y_local), :] = pair[k][:, 128 * h : 128 * h + 128]

    h, p = q // 2, q % 2
    rows = dot3((columns[h, 0], columns[h, 1]), (x_top[p], x_rest[p]))
    side = own.shape[2] // 2
    for g in range(groups):
        plane = rows[g * y_local : (g + 1) * y_local] + bias[4 * g + q]
        rim = own[g, 0] + (low[g, 0] + high[g, 0])
        out[g, 0, :side] = gelu(plane[:side] + rim[:side])
        out[g, 0, side : y_local - side] = gelu(plane[side : y_local - side] + middle[g, 0])
        out[g, 0, y_local - side :] = gelu(plane[y_local - side :] + rim[side:])


def in_hbm(*arrays):
    return [pltpu.with_memory_space_constraint(a, pltpu.HBM) for a in arrays]


def params():
    return pltpu.CompilerParams(vmem_limit_bytes=VMEM_BYTES)


def cost(flops, moved):
    return pl.CostEstimate(flops=flops, bytes_accessed=moved, transcendentals=0)


def whole_block(table):
    return pl.BlockSpec(table.shape, lambda i: (0,) * table.ndim)


def by_four(array):
    return array.reshape(CH // 4, 4, *array.shape[1:])


def forward_call(field, gy, pinned):
    y_local = field.shape[1]
    tables = [*halves(x_table(False)), *halves(y_table(y_local, gy, False))]
    hbm = pl.BlockSpec(memory_space=pltpu.HBM)
    return pl.pallas_call(
        forward_kernel,
        out_shape=(pltpu.HBM if pinned else jax.ShapeDtypeStruct)((CH // 2 * MY, 4 * MX), F32),
        in_specs=[hbm] * 5,
        scratch_shapes=[
            pltpu.VMEM((4, CH // 4, y_local, NX), F32),
            pltpu.VMEM((2, 2, NX, 4 * MX), BF),
            pltpu.VMEM((2, 2 * MY, y_local), BF),
            pltpu.SemaphoreType.DMA((8,)),
        ],
        compiler_params=params(),
        cost_estimate=cost(10**8, 2**18),
        name="forward_modes",
    )(*in_hbm(by_four(field), *tables))


def filter_call(arrived, gains, gz, gy, scale):
    fwd, inv = z_tables(gz, gy, gains.shape[2], scale)
    fwd, inv = halves(fwd), halves(inv)
    return pl.pallas_call(
        filter_kernel,
        out_shape=pltpu.HBM(arrived.shape, F32),
        compiler_params=params(),
        cost_estimate=cost(2 * 10**11, 2**18),
        name="filter_modes",
    )(arrived, *in_hbm(gains, *fwd, *inv))


def inverse_call(modes, bias, middle, own, pair, y_local, gy, scale):
    tables = [*halves(x_table(True, scale)), *halves(y_table(y_local, gy, True))]
    some = lambda rows: pl.BlockSpec((CH // 4, 1, rows, NX), lambda i: (0, i, 0, 0))
    planes = [*in_hbm(by_four(middle), by_four(own)), *map(by_four, pair)]
    result = pl.pallas_call(
        inverse_kernel,
        out_shape=jax.ShapeDtypeStruct((CH // 4, 4, y_local, NX), F32),
        grid=(4,),
        in_specs=[
            whole_block(modes),
            pl.BlockSpec(memory_space=pltpu.SMEM),
            *[whole_block(t) for t in tables],
            *[some(p.shape[2]) for p in planes],
        ],
        out_specs=some(y_local),
        scratch_shapes=[pltpu.VMEM((2, 2, CH // 4 * y_local, 128), BF)],
        compiler_params=params(),
        cost_estimate=cost(10**8, 2**18),
        name="inverse_modes",
    )(modes, *in_hbm(bias, *tables), *planes)
    return result.reshape(CH, y_local, NX)


def pack_call(field, middle):
    count = 8 * len(middle) + 2
    fetched = len(middle) + 4
    hbm = pl.BlockSpec(memory_space=pltpu.HBM)
    return pl.pallas_call(
        functools.partial(pack_kernel, middle),
        out_shape=[pltpu.HBM((count, CH, NX), F32), pltpu.HBM((2, CH, NX), F32)],
        in_specs=[hbm],
        out_specs=[hbm] * 2,
        scratch_shapes=[
            pltpu.VMEM((fetched, 2, CH, 8, 128), F32),
            pltpu.VMEM((count, CH, NX), F32),
            pltpu.VMEM((2, CH, NX), F32),
            pltpu.SemaphoreType.DMA((fetched, 2)),
            pltpu.SemaphoreType.DMA((count // 17 + 2,)),
        ],
        compiler_params=params(),
        cost_estimate=cost(10**8, 2**18),
        name="packed_rows",
    )(*in_hbm(field))


def own_call(field, halo, weight, point, upper, lower):
    tiles = len(upper) + len(lower)
    rows = 8 * tiles
    hbm = pl.BlockSpec(memory_space=pltpu.HBM)
    shapes = [pltpu.HBM((CH, rows, NX), F32)] * 3
    return pl.pallas_call(
        functools.partial(own_kernel, (upper, lower)),
        out_shape=shapes,
        in_specs=[hbm] * 3 + [pl.BlockSpec(memory_space=pl.ANY)],
        out_specs=[hbm] * len(shapes),
        scratch_shapes=[
            pltpu.VMEM((tiles + 2, 2, CH, 8, 128), F32),
            pltpu.VMEM((2, CH, NX), F32),
            pltpu.VMEM((CH, 27), F32),
            pltpu.VMEM((CH, CH), F32),
            pltpu.VMEM((3, tiles, CH, 8, NX), F32),
            pltpu.VMEM((3, rows + 4, CH, NX), F32),
            pltpu.VMEM((3, rows, CH, NX), F32),
            pltpu.VMEM((27, CH, 128), F32),
            pltpu.SemaphoreType.DMA((tiles + 2, 2)),
            pltpu.SemaphoreType.DMA((3, tiles)),
            pltpu.SemaphoreType.DMA((3,)),
        ],
        compiler_params=params(),
        cost_estimate=cost(10**8, 2**18),
        name="own_sums",
    )(*in_hbm(weight, point, field), halo)


def middle_call(weight, point, low, own, high):
    rows = own.shape[0] - 2
    hbm = pl.BlockSpec(memory_space=pltpu.HBM)
    return pl.pallas_call(
        middle_kernel,
        out_shape=pltpu.HBM((CH, rows, NX), F32),
        in_specs=[hbm] * 2 + [pl.BlockSpec(memory_space=pl.ANY)] * 3,
        out_specs=hbm,
        scratch_shapes=[
            pltpu.VMEM((3, rows + 2, CH, NX), F32),
            pltpu.VMEM((CH, 27), F32),
            pltpu.VMEM((CH, CH), F32),
            pltpu.VMEM((rows // 8, CH, 8, NX), F32),
            pltpu.VMEM((3, rows + 2, CH, NX), F32),
            pltpu.VMEM((1, rows, CH, NX), F32),
            pltpu.VMEM((27, CH, 128), F32),
            pltpu.SemaphoreType.DMA((3,)),
            pltpu.SemaphoreType.DMA((rows // 8,)),
            pltpu.SemaphoreType.DMA((2,)),
        ],
        compiler_params=params(),
        cost_estimate=cost(10**8, 2**18),
        name="middle_sums",
    )(*in_hbm(weight, point), low, *in_hbm(own), high)


def general_filter(coarse, gains, gz, gy, scale):
    j_own, n_own = gains.shape[2], gains.shape[3]
    both = ("gz", "gy")
    flat = coarse.reshape(CH // 2, MY, 2, 2, MX).transpose(3, 1, 0, 2, 4).reshape(2, MY, CH * MX)
    sent = flat.reshape(2, gy, j_own, gz, n_own).transpose(3, 1, 0, 2, 4).reshape(gz * gy, -1)
    got = lax.all_to_all(sent, both, split_axis=0, concat_axis=0, tiled=True)
    got = got.reshape(gz, gy, 2, j_own, n_own)
    c, s = (jnp.asarray(t, F32) for t in trig(kept(MZ, gz), np.arange(gz), gz))
    mul = functools.partial(jnp.einsum, precision=lax.Precision.HIGHEST)
    whole = got.sum(axis=1) * scale
    real = mul("zjn,qz->qjn", whole[:, 0], c) + mul("zjn,qz->qjn", whole[:, 1], s)
    imag = mul("zjn,qz->qjn", whole[:, 1], c) - mul("zjn,qz->qjn", whole[:, 0], s)
    real, imag = real * gains[0] - imag * gains[1], real * gains[1] + imag * gains[0]
    out = jnp.stack(
        [
            mul("qjn,qz->zjn", real, c) - mul("qjn,qz->zjn", imag, s),
            mul("qjn,qz->zjn", real, s) + mul("qjn,qz->zjn", imag, c),
        ],
        axis=1,
    )
    out = jnp.broadcast_to(out[:, None], (gz, gy, 2, j_own, n_own)).reshape(gz * gy, -1)
    back = lax.all_to_all(out, both, split_axis=0, concat_axis=0, tiled=True)
    back = back.reshape(gz, gy, 2, j_own, n_own).transpose(2, 1, 3, 0, 4)
    back = back.reshape(2, MY, CH // 2, 2, MX)
    return back.transpose(2, 1, 3, 0, 4).reshape(CH // 2, MY, 4 * MX)


def body(field, spectral_filter, depth_weight, point_weight, bias_vector):
    gz, gy = lax.axis_size("gz"), lax.axis_size("gy")
    y_local = field.shape[2]
    field = field.reshape(CH, y_local, NX)
    y_total = gy * y_local
    forward_scale = 1.0 / math.sqrt(float(NX) * y_total * gz)
    inverse_scale = 1.0 / math.sqrt(2.0 * MX * MY * MZ)

    def ring(axis, count, by):
        return [(i, (i + by) % count) for i in range(count)]

    def to_neighbours(down, up):
        return (
            lax.ppermute(down, "gz", ring("gz", gz, 1)),
            lax.ppermute(up, "gz", ring("gz", gz, -1)),
        )

    def after(value, *others):
        return lax.optimization_barrier((value, *others))[0]

    tiles = y_local // 8
    side = 2 if tiles >= 6 else 1
    upper, lower = tuple(range(side)), tuple(range(tiles - side, tiles))
    middle = tuple(range(side, tiles - side))

    packed, edges = pack_call(field, middle)
    packed_low, packed_high = to_neighbours(packed, packed)
    if gy == 2:
        halo = lax.ppermute(edges, "gy", ring("gy", gy, 1))
    else:
        halo = jnp.stack(
            [
                lax.ppermute(edges[0], "gy", ring("gy", gy, 1)),
                lax.ppermute(edges[1], "gy", ring("gy", gy, -1)),
            ]
        )
    j_own, n_own = spectral_filter.shape[2], spectral_filter.shape[3]
    whole_tiles = j_own == 8 and n_own == 2 * MX
    coarse = forward_call(after(field, packed), gy, whole_tiles)
    coarse = after(coarse, halo)
    sums = own_call(after(field, coarse), halo, depth_weight, point_weight, upper, lower)
    down, own, up = sums
    pair = to_neighbours(down, up)

    if whole_tiles:
        both = ("gz", "gy")
        got = lax.all_to_all(coarse, both, split_axis=0, concat_axis=0, tiled=True)
        out = filter_call(got, after(spectral_filter, own, packed_low, packed_high), gz, gy, forward_scale)
        back = lax.all_to_all(out, both, split_axis=0, concat_axis=0, tiled=True)
        back = back.reshape(CH // 2, MY, 4 * MX)
        mark = out
    else:
        mark = back = general_filter(coarse, spectral_filter, gz, gy, forward_scale)

    mixed = middle_call(depth_weight, point_weight, packed_low, after(packed, mark), packed_high)
    result = inverse_call(back, bias_vector, mixed, own, pair, y_local, gy, inverse_scale)
    return result.reshape(CH, 1, y_local, NX)


def solution(mesh):
    in_specs = (P(None, "gz", "gy", None), P(None, None, "gy", "gz"), P(), P(), P())
    out_specs = P(None, "gz", "gy", None)
    return jax.shard_map(body, mesh=mesh, in_specs=in_specs, out_specs=out_specs, check_vma=False)
```

```python
import functools
import math

import jax
import jax.numpy as jnp
import ml_dtypes
import numpy as np
from jax import lax
from jax.experimental import pallas as pl
from jax.experimental.pallas import tpu as pltpu
from jax.sharding import PartitionSpec as P

NX = 256
MX = 32
MY = 16
MZ = 16
CH = 32
VMEM_BYTES = 24 * 1024 * 1024
BF = jnp.bfloat16
F32 = jnp.float32


def kept(count, total):
    series = np.arange(count)
    return np.where(series < count // 2, series, total - count + series)


def trig(freqs, places, total):
    angle = 2.0 * np.pi * ((freqs[:, None] * places[None, :]) % total) / total
    return np.cos(angle), np.sin(angle)


def halves(table):
    table = np.asarray(table, np.float64)
    top = table.astype(np.float32).astype(ml_dtypes.bfloat16)
    rest = (table - top.astype(np.float64)).astype(np.float32).astype(ml_dtypes.bfloat16)
    return jnp.asarray(top), jnp.asarray(rest)


def y_table(y_local, gy, inverse):
    out = []
    for g in range(gy):
        places = g * y_local + np.arange(y_local)
        out.append(np.concatenate(trig(kept(MY, y_local * gy), places, y_local * gy), axis=0))
    return np.stack([t.T for t in out] if inverse else out)


def x_table(inverse, scale=1.0):
    c, s = trig(np.arange(MX), np.arange(NX), NX)
    w = np.where(np.arange(MX) == 0, 1.0, 2.0)[:, None] if inverse else 1.0
    out = np.zeros((2, 2, 2, MX, NX))
    for p in range(2):
        out[p, p, 0] = w * c * scale
        out[p, p, 1] = -w * s * scale
    out = out.reshape(2, 4 * MX, NX)
    return out if inverse else out.transpose(0, 2, 1)


def z_tables(gz, gy, rows, scale):
    c, s = trig(kept(MZ, gz), np.arange(gz), gz)
    eye = np.eye(rows)
    one = np.ones(gy)
    both = np.stack([c, s])
    fwd = np.einsum("tqz,g,jk->tqjzgk", both, one, eye) * scale
    inv = np.einsum("tqz,g,jk->tzgjqk", both, one, eye)
    return fwd.reshape(2 * MZ * rows, gz * gy * rows), inv.reshape(2 * gz * gy * rows, MZ * rows)


def parts(value):
    top = value.astype(BF)
    return top, (value - top.astype(F32)).astype(BF)


def dot(a, b):
    return jnp.dot(a, b, preferred_element_type=F32)


def dot3(a, b):
    rows = a[0].shape[0]
    both = dot(jnp.concatenate([a[0], a[1]], axis=0), b[0])
    return both[:rows] + (both[rows:] + dot(a[0], b[1]))


def swap_parts(value):
    lane = lax.broadcasted_iota(jnp.int32, value.shape, 1)
    is_real = (lane // MX) % 2 == 0
    width = value.shape[1]
    return jnp.where(is_real, pltpu.roll(value, width - MX, 1), pltpu.roll(value, MX, 1)), is_real


def forward_kernel(field, x_top, x_rest, y_top, y_rest, out, taken, x_both, y_both, sem):
    gy = lax.axis_index("gy")
    few = [
        pltpu.make_async_copy(src, dst, sem.at[4 + i])
        for i, (src, dst) in enumerate(
            ((x_top, x_both.at[0]), (x_rest, x_both.at[1]), (y_top.at[gy], y_both.at[0]), (y_rest.at[gy], y_both.at[1]))
        )
    ]
    copies = [pltpu.make_async_copy(field.at[:, q], taken.at[q], sem.at[q]) for q in range(4)]
    for copy in few + copies:
        copy.start()
    for copy in few:
        copy.wait()
    groups, rows = taken.shape[1:3]
    halves_of = []
    for q in range(4):
        copies[q].wait()
        part = dot3(parts(taken[q].reshape(groups * rows, NX)), (x_both[0, q % 2], x_both[1, q % 2]))
        if q % 2:
            halves_of[-1] = halves_of[-1] + part
        else:
            halves_of.append(part)
    total = jnp.concatenate(halves_of, axis=1)
    for g in range(groups):
        both = dot3((y_both[0], y_both[1]), parts(total[g * rows : (g + 1) * rows]))
        crossed, is_real = swap_parts(both[MY:])
        modes = both[:MY] + jnp.where(is_real, crossed, -crossed)
        out[pl.ds(2 * g * MY, MY), :] = modes[:, : 4 * MX]
        out[pl.ds((2 * g + 1) * MY, MY), :] = modes[:, 4 * MX :]


def filter_kernel(arrived, gains, f_top, f_rest, i_top, i_rest, out):
    real, imag = (gains[r].reshape(-1, 2 * MX) for r in range(2))
    first, second = slice(0, MX), slice(MX, 2 * MX)
    same = jnp.concatenate([real[:, first], real[:, first], real[:, second], real[:, second]], axis=1)
    cross = jnp.concatenate([-imag[:, first], imag[:, first], -imag[:, second], imag[:, second]], axis=1)
    half = f_top.shape[0] // 2
    turned = dot3((f_top[...], f_rest[...]), parts(arrived[...]))
    crossed, is_real = swap_parts(turned[half:])
    modes = turned[:half] + jnp.where(is_real, crossed, -crossed)
    crossed, _ = swap_parts(modes)
    filtered = modes * same + crossed * cross
    half = i_top.shape[0] // 2
    back = dot3((i_top[...], i_rest[...]), parts(filtered))
    crossed, is_real = swap_parts(back[half:])
    out[...] = back[:half] + jnp.where(is_real, -crossed, crossed)


def fetch_tiles(field, taken, sems, wanted):
    pending = {}
    for k, t in enumerate(wanted):
        pending[t] = [
            pltpu.make_async_copy(
                field.at[:, pl.ds(8 * t, 8), pl.ds(128 * h, 128)], taken.at[k, h], sems.at[k, h]
            )
            for h in range(2)
        ]
        for copy in pending[t]:
            copy.start()

    def row(t, r):
        for copy in pending.pop(t, ()):
            copy.wait()
        k = wanted.index(t)
        return jnp.concatenate(
            [taken.at[k, h].reshape(CH * 8, 128)[pl.ds(r, CH, stride=8), :] for h in range(2)], axis=1
        )

    return row


def spread_gains(weights, gains, offsets):
    for k in [9 * a + j for a in offsets for j in range(9)]:
        gains[k] = jnp.broadcast_to(weights[:, k : k + 1], (CH, 128))


def mixing(points):
    down = (
        lax.broadcasted_iota(jnp.int32, (8 * CH, CH), 0) // 8
        == lax.broadcasted_iota(jnp.int32, (8 * CH, CH), 1)
    ).astype(BF)
    across = (
        lax.broadcasted_iota(jnp.int32, (CH, 8 * CH), 1) % CH
        == lax.broadcasted_iota(jnp.int32, (CH, 8 * CH), 0)
    ).astype(BF)
    same = (
        lax.broadcasted_iota(jnp.int32, (8 * CH, 8 * CH), 0) % 8
        == lax.broadcasted_iota(jnp.int32, (8 * CH, 8 * CH), 1) // CH
    )
    return tuple(
        jnp.where(same, dot(dot(down, part).astype(BF), across), 0.0).astype(BF)
        for part in parts(points)
    )


def turn(turned, at, value):
    turned[0, at] = pltpu.roll(value, 1, 1)
    turned[1, at] = value
    turned[2, at] = pltpu.roll(value, NX - 1, 1)


def tap_sums(turned, depth, gains, runs, offsets, fresh):
    def some(i, _):
        chans = pl.ds(pl.multiple_of(i * 8, 8), 8)
        gain = {k: gains[k, chans, :] for a in offsets for k in range(9 * a, 9 * a + 9)}
        for h in range(2):
            lanes = pl.ds(128 * h, 128)
            for first, to, rows in runs:
                sums = {}
                for r in range(rows + 2):
                    values = [turned[e, first + r, chans, lanes] for e in range(3)]
                    for b in range(3):
                        o = r - b
                        if o < 0 or o >= rows:
                            continue
                        for k, a in enumerate(offsets):
                            for e in range(3):
                                term = gain[a * 9 + b * 3 + e] * values[e]
                                if (o, k) in sums:
                                    sums[o, k] = sums[o, k] + term
                                elif fresh:
                                    sums[o, k] = term
                                else:
                                    sums[o, k] = depth[k, to + o, chans, lanes] + term
                    if r >= 2:
                        for k in range(len(offsets)):
                            depth[k, to + r - 2, chans, lanes] = sums.pop((r - 2, k))
        return 0

    lax.fori_loop(0, CH // 8, some, 0)


def mix_tile(mix, depth, k, t):
    tile = depth[k, pl.ds(8 * t, 8)].reshape(8 * CH, NX)
    return dot3(mix, parts(tile)).reshape(CH, 8, NX)


def pack_kernel(plan, field, packed, later, edges, taken, rows, ends, sem_in, sem_out):
    middle, split = plan
    last = field.shape[1] // 8 - 1
    before, after = middle[0] - 1, middle[-1] + 1
    wanted = [before, *middle, after] + [t for t in (0, last) if t not in (before, after)]
    row = fetch_tiles(field, taken, sem_in, wanted)
    places = [(before, 7), *[(t, r) for t in middle for r in range(8)], (after, 0)]
    copies = []
    for i, place in enumerate(places):
        rows[i] = row(*place)
        if i + 1 == split:
            copies.append(pltpu.make_async_copy(rows.at[pl.ds(0, split)], packed, sem_out.at[0]))
            copies[-1].start()
    copies.append(pltpu.make_async_copy(rows.at[pl.ds(split, len(places) - split)], later, sem_out.at[1]))
    copies[-1].start()
    ends[0] = row(last, 7)
    ends[1] = row(0, 0)
    copies.append(pltpu.make_async_copy(ends, edges, sem_out.at[2]))
    copies[-1].start()
    for copy in copies:
        copy.wait()


def own_kernel(plan, weight, point, field, halo, *refs):
    upper, lower = plan
    outs, refs = refs[:3], refs[3:]
    taken, halo_rows, weights, points, sent, turned, depth, gains, sem_in, sem_out, sem_few = refs
    few = [
        pltpu.make_async_copy(a, b, sem_few.at[i])
        for i, (a, b) in enumerate(((weight, weights), (point, points), (halo, halo_rows)))
    ]
    for copy in few:
        copy.start()
    wanted = [*upper, upper[-1] + 1, lower[0] - 1, *lower]
    row = fetch_tiles(field, taken, sem_in, wanted)
    for copy in few:
        copy.wait()
    spread_gains(weights, gains, range(3))
    mix = mixing(points[...])
    rows, others = 8 * len(upper), 8 * len(lower)
    for i, place in enumerate([None, *[(t, r) for t in upper for r in range(8)], (upper[-1] + 1, 0)]):
        turn(turned, i, halo_rows[0] if place is None else row(*place))
    for i, place in enumerate([(lower[0] - 1, 7), *[(t, r) for t in lower for r in range(8)], None]):
        turn(turned, rows + 2 + i, halo_rows[1] if place is None else row(*place))
    tap_sums(turned, depth, gains, [(0, 0, rows), (rows + 2, rows, others)], range(3), True)
    copies = []
    for t in range((rows + others) // 8):
        for k, out in enumerate(outs):
            sent[k, t] = mix_tile(mix, depth, k, t)
            copies.append(
                pltpu.make_async_copy(sent.at[k, t], out.at[:, pl.ds(8 * t, 8), :], sem_out.at[k, t])
            )
            copies[-1].start()
    for copy in copies:
        copy.wait()


def middle_kernel(weight, point, *refs):
    planes, out = refs[:6], refs[6]
    taken, weights, points, sent, turned, depth, gains, sem_in, sem_out, sem_few = refs[7:]
    split = planes[0].shape[0]
    few = [
        pltpu.make_async_copy(a, b, sem_few.at[i])
        for i, (a, b) in enumerate(((weight, weights), (point, points)))
    ]
    arrivals = [
        [
            pltpu.make_async_copy(planes[2 * a], taken.at[a, pl.ds(0, split)], sem_in.at[a, 0]),
            pltpu.make_async_copy(
                planes[2 * a + 1], taken.at[a, pl.ds(split, taken.shape[1] - split)], sem_in.at[a, 1]
            ),
        ]
        for a in range(3)
    ]
    for a in (1, 0, 2):
        for copy in arrivals[a]:
            copy.start()
    for copy in few:
        copy.start()
    for copy in few:
        copy.wait()
    spread_gains(weights, gains, range(3))
    mix = mixing(points[...])
    rows = out.shape[1]
    for a in (1, 0, 2):
        for copy in arrivals[a]:
            copy.wait()
        for r in range(rows + 2):
            turn(turned, r, taken[a, r])
        tap_sums(turned, depth, gains, [(0, 0, rows)], [a], a == 1)
    copies = []
    for t in range(rows // 8):
        sent[t] = mix_tile(mix, depth, 0, t)
        copies.append(pltpu.make_async_copy(sent.at[t], out.at[:, pl.ds(8 * t, 8), :], sem_out.at[t]))
        copies[-1].start()
    for copy in copies:
        copy.wait()


def gelu(value):
    size = jnp.abs(value) * math.sqrt(0.5)
    below = 1.0 + 0.3275911 * size
    t = pl.reciprocal(below, approx=True)
    t = t * (2.0 - below * t)
    series = 1.061405429 * t - 1.453152027
    for factor in (1.421413741, -0.284496736, 0.254829592):
        series = series * t + factor
    tail = 0.5 * (series * t) * jnp.exp(-(size * size))
    return value * jnp.where(value < 0.0, tail, 1.0 - tail)


def inverse_kernel(upper, modes, bias, x_top, x_rest, y_top, y_rest, middle, own, out, base, columns):
    q = pl.program_id(0)
    groups, _, y_local, _ = out.shape

    @pl.when(q == 0)
    def _():
        gy = lax.axis_index("gy")
        for g in range(groups):
            own_modes = jnp.concatenate([modes[2 * g], modes[2 * g + 1]], axis=1)
            crossed, is_real = swap_parts(own_modes)
            stack = jnp.concatenate([own_modes, jnp.where(is_real, -crossed, crossed)], axis=0)
            pair = parts(dot3((y_top[gy], y_rest[gy]), parts(stack)))
            for h in range(2):
                for k in range(2):
                    columns[h, k, pl.ds(g * y_local, y_local), :] = pair[k][:, 128 * h : 128 * h + 128]

    h, p = q // 2, q % 2
    rows = dot3((columns[h, 0], columns[h, 1]), (x_top[p], x_rest[p]))
    start, stop = upper, upper + middle.shape[2]
    for g in range(groups):
        plane = rows[g * y_local : (g + 1) * y_local] + bias[4 * g + q]
        out[g, 0, start:stop] = gelu(plane[start:stop] + middle[g, 0])
        base[g, 0, :start] = plane[:start] + own[g, 0, :start]
        base[g, 0, start:] = plane[stop:] + own[g, 0, start:]


def finish_kernel(_, base, low, high, out):
    out[...] = gelu(base[...] + (low[...] + high[...]))


def in_hbm(*arrays):
    return [pltpu.with_memory_space_constraint(a, pltpu.HBM) for a in arrays]


def params():
    return pltpu.CompilerParams(vmem_limit_bytes=VMEM_BYTES)


def cost(flops, moved):
    return pl.CostEstimate(flops=flops, bytes_accessed=moved, transcendentals=0)


def whole_block(table):
    return pl.BlockSpec(table.shape, lambda i: (0,) * table.ndim)


def by_four(array):
    return array.reshape(CH // 4, 4, *array.shape[1:])


def forward_call(field, gy, pinned):
    y_local = field.shape[1]
    tables = [*halves(x_table(False)), *halves(y_table(y_local, gy, False))]
    hbm = pl.BlockSpec(memory_space=pltpu.HBM)
    return pl.pallas_call(
        forward_kernel,
        out_shape=(pltpu.HBM if pinned else jax.ShapeDtypeStruct)((CH // 2 * MY, 4 * MX), F32),
        in_specs=[hbm] * 5,
        scratch_shapes=[
            pltpu.VMEM((4, CH // 4, y_local, NX), F32),
            pltpu.VMEM((2, 2, NX, 4 * MX), BF),
            pltpu.VMEM((2, 2 * MY, y_local), BF),
            pltpu.SemaphoreType.DMA((8,)),
        ],
        compiler_params=params(),
        cost_estimate=cost(10**8, 2**18),
        name="forward_modes",
    )(*in_hbm(by_four(field), *tables))


def filter_call(arrived, gains, gz, gy, scale):
    fwd, inv = z_tables(gz, gy, gains.shape[2], scale)
    fwd, inv = halves(fwd), halves(inv)
    return pl.pallas_call(
        filter_kernel,
        out_shape=pltpu.HBM(arrived.shape, F32),
        compiler_params=params(),
        cost_estimate=cost(2 * 10**11, 2**18),
        name="filter_modes",
    )(arrived, *in_hbm(gains, *fwd, *inv))


def inverse_call(modes, bias, middle, own, upper, y_local, gy, scale):
    tables = [*halves(x_table(True, scale)), *halves(y_table(y_local, gy, True))]
    some = lambda rows: pl.BlockSpec((CH // 4, 1, rows, NX), lambda i: (0, i, 0, 0))
    planes = in_hbm(by_four(middle), by_four(own))
    rim = own.shape[1]
    result, base = pl.pallas_call(
        functools.partial(inverse_kernel, upper),
        out_shape=[
            jax.ShapeDtypeStruct((CH // 4, 4, y_local, NX), F32),
            jax.ShapeDtypeStruct((CH // 4, 4, rim, NX), F32),
        ],
        grid=(4,),
        in_specs=[
            whole_block(modes),
            pl.BlockSpec(memory_space=pltpu.SMEM),
            *[whole_block(t) for t in tables],
            *[some(p.shape[2]) for p in planes],
        ],
        out_specs=[some(y_local), some(rim)],
        scratch_shapes=[pltpu.VMEM((2, 2, CH // 4 * y_local, 128), BF)],
        compiler_params=params(),
        cost_estimate=cost(10**8, 2**18),
        name="inverse_modes",
    )(modes, *in_hbm(bias, *tables), *planes)
    return result.reshape(CH, y_local, NX), base.reshape(CH, rim, NX)


def finish_call(result, base, low, high, upper):
    tiles = base.shape[1] // 8
    gap = result.shape[1] // 8 - tiles
    piece = pl.BlockSpec((CH, 8, NX), lambda i: (0, i, 0))
    return pl.pallas_call(
        finish_kernel,
        out_shape=jax.ShapeDtypeStruct(result.shape, F32),
        grid=(tiles,),
        in_specs=[pl.BlockSpec(memory_space=pl.ANY), piece, piece, piece],
        out_specs=pl.BlockSpec((CH, 8, NX), lambda i: (0, jnp.where(i < upper, i, i + gap), 0)),
        input_output_aliases={0: 0},
        compiler_params=params(),
        cost_estimate=cost(10**8, 2**18),
        name="finished_rows",
    )(result, base, low, high)


def pack_call(field, middle, first):
    count = 8 * len(middle) + 2
    split = 8 * first + 2
    fetched = len(middle) + 4
    hbm = pl.BlockSpec(memory_space=pltpu.HBM)
    return pl.pallas_call(
        functools.partial(pack_kernel, (middle, split)),
        out_shape=[
            pltpu.HBM((split, CH, NX), F32),
            pltpu.HBM((count - split, CH, NX), F32),
            pltpu.HBM((2, CH, NX), F32),
        ],
        in_specs=[hbm],
        out_specs=[hbm] * 3,
        scratch_shapes=[
            pltpu.VMEM((fetched, 2, CH, 8, 128), F32),
            pltpu.VMEM((count, CH, NX), F32),
            pltpu.VMEM((2, CH, NX), F32),
            pltpu.SemaphoreType.DMA((fetched, 2)),
            pltpu.SemaphoreType.DMA((3,)),
        ],
        compiler_params=params(),
        cost_estimate=cost(10**8, 2**18),
        name="packed_rows",
    )(*in_hbm(field))


def own_call(field, halo, weight, point, upper, lower):
    tiles = len(upper) + len(lower)
    rows = 8 * tiles
    hbm = pl.BlockSpec(memory_space=pltpu.HBM)
    shapes = [pltpu.HBM((CH, rows, NX), F32)] * 3
    return pl.pallas_call(
        functools.partial(own_kernel, (upper, lower)),
        out_shape=shapes,
        in_specs=[hbm] * 3 + [pl.BlockSpec(memory_space=pl.ANY)],
        out_specs=[hbm] * len(shapes),
        scratch_shapes=[
            pltpu.VMEM((tiles + 2, 2, CH, 8, 128), F32),
            pltpu.VMEM((2, CH, NX), F32),
            pltpu.VMEM((CH, 27), F32),
            pltpu.VMEM((CH, CH), F32),
            pltpu.VMEM((3, tiles, CH, 8, NX), F32),
            pltpu.VMEM((3, rows + 4, CH, NX), F32),
            pltpu.VMEM((3, rows, CH, NX), F32),
            pltpu.VMEM((27, CH, 128), F32),
            pltpu.SemaphoreType.DMA((tiles + 2, 2)),
            pltpu.SemaphoreType.DMA((3, tiles)),
            pltpu.SemaphoreType.DMA((3,)),
        ],
        compiler_params=params(),
        cost_estimate=cost(10**8, 2**18),
        name="own_sums",
    )(*in_hbm(weight, point, field), halo)


def middle_call(weight, point, low, own, high):
    rows = own[0].shape[0] + own[1].shape[0] - 2
    hbm = pl.BlockSpec(memory_space=pltpu.HBM)
    return pl.pallas_call(
        middle_kernel,
        out_shape=pltpu.HBM((CH, rows, NX), F32),
        in_specs=[hbm] * 2 + [pl.BlockSpec(memory_space=pl.ANY)] * 6,
        out_specs=hbm,
        scratch_shapes=[
            pltpu.VMEM((3, rows + 2, CH, NX), F32),
            pltpu.VMEM((CH, 27), F32),
            pltpu.VMEM((CH, CH), F32),
            pltpu.VMEM((rows // 8, CH, 8, NX), F32),
            pltpu.VMEM((3, rows + 2, CH, NX), F32),
            pltpu.VMEM((1, rows, CH, NX), F32),
            pltpu.VMEM((27, CH, 128), F32),
            pltpu.SemaphoreType.DMA((3, 2)),
            pltpu.SemaphoreType.DMA((rows // 8,)),
            pltpu.SemaphoreType.DMA((2,)),
        ],
        compiler_params=params(),
        cost_estimate=cost(2 * 10**11, 2**18),
        name="middle_sums",
    )(*in_hbm(weight, point), *low, *in_hbm(*own), *high)


def general_filter(coarse, gains, gz, gy, scale):
    j_own, n_own = gains.shape[2], gains.shape[3]
    both = ("gz", "gy")
    flat = coarse.reshape(CH // 2, MY, 2, 2, MX).transpose(3, 1, 0, 2, 4).reshape(2, MY, CH * MX)
    sent = flat.reshape(2, gy, j_own, gz, n_own).transpose(3, 1, 0, 2, 4).reshape(gz * gy, -1)
    got = lax.all_to_all(sent, both, split_axis=0, concat_axis=0, tiled=True)
    got = got.reshape(gz, gy, 2, j_own, n_own)
    c, s = (jnp.asarray(t, F32) for t in trig(kept(MZ, gz), np.arange(gz), gz))
    mul = functools.partial(jnp.einsum, precision=lax.Precision.HIGHEST)
    whole = got.sum(axis=1) * scale
    real = mul("zjn,qz->qjn", whole[:, 0], c) + mul("zjn,qz->qjn", whole[:, 1], s)
    imag = mul("zjn,qz->qjn", whole[:, 1], c) - mul("zjn,qz->qjn", whole[:, 0], s)
    real, imag = real * gains[0] - imag * gains[1], real * gains[1] + imag * gains[0]
    out = jnp.stack(
        [
            mul("qjn,qz->zjn", real, c) - mul("qjn,qz->zjn", imag, s),
            mul("qjn,qz->zjn", real, s) + mul("qjn,qz->zjn", imag, c),
        ],
        axis=1,
    )
    out = jnp.broadcast_to(out[:, None], (gz, gy, 2, j_own, n_own)).reshape(gz * gy, -1)
    back = lax.all_to_all(out, both, split_axis=0, concat_axis=0, tiled=True)
    back = back.reshape(gz, gy, 2, j_own, n_own).transpose(2, 1, 3, 0, 4)
    back = back.reshape(2, MY, CH // 2, 2, MX)
    return back.transpose(2, 1, 3, 0, 4).reshape(CH // 2, MY, 4 * MX)


def body(field, spectral_filter, depth_weight, point_weight, bias_vector):
    gz, gy = lax.axis_size("gz"), lax.axis_size("gy")
    y_local = field.shape[2]
    field = field.reshape(CH, y_local, NX)
    y_total = gy * y_local
    forward_scale = 1.0 / math.sqrt(float(NX) * y_total * gz)
    inverse_scale = 1.0 / math.sqrt(2.0 * MX * MY * MZ)

    def ring(axis, count, by):
        return [(i, (i + by) % count) for i in range(count)]

    def to_neighbours(down, up):
        return (
            lax.ppermute(down, "gz", ring("gz", gz, 1)),
            lax.ppermute(up, "gz", ring("gz", gz, -1)),
        )

    def after(value, *others):
        return lax.optimization_barrier((value, *others))[0]

    tiles = y_local // 8
    upper = (0,)
    lower = tuple(range(tiles - max(1, tiles // 4), tiles))
    middle = tuple(range(1, lower[0]))
    packed, later, edges = pack_call(field, middle, max(1, 2 * len(middle) // 5))
    first_low, first_high = to_neighbours(packed, packed)
    if gy == 2:
        halo = lax.ppermute(edges, "gy", ring("gy", gy, 1))
    else:
        halo = jnp.stack(
            [
                lax.ppermute(edges[0], "gy", ring("gy", gy, 1)),
                lax.ppermute(edges[1], "gy", ring("gy", gy, -1)),
            ]
        )
    j_own, n_own = spectral_filter.shape[2], spectral_filter.shape[3]
    whole_tiles = j_own == 8 and n_own == 2 * MX
    coarse = after(forward_call(after(field, packed), gy, whole_tiles), halo)
    if whole_tiles:
        both = ("gz", "gy")
        got = lax.all_to_all(coarse, both, split_axis=0, concat_axis=0, tiled=True)
        sent = after(later, got)
        later_low, later_high = to_neighbours(sent, sent)
        gains = after(spectral_filter, first_low, first_high)
        filtered = filter_call(got, gains, gz, gy, forward_scale)
        back = lax.all_to_all(filtered, both, split_axis=0, concat_axis=0, tiled=True)
        back = back.reshape(CH // 2, MY, 4 * MX)
    else:
        later_low, later_high = to_neighbours(later, later)
        filtered = back = general_filter(coarse, spectral_filter, gz, gy, forward_scale)
    down, own, up = own_call(after(field, filtered), halo, depth_weight, point_weight, upper, lower)
    low, high = to_neighbours(down, up)
    mixed = middle_call(
        depth_weight,
        point_weight,
        (first_low, later_low),
        (after(packed, back), later),
        (first_high, later_high),
    )
    result, base = inverse_call(back, bias_vector, mixed, own, 8, y_local, gy, inverse_scale)
    result = finish_call(result, base, low, high, 1)
    return result.reshape(CH, 1, y_local, NX)


def solution(mesh):
    in_specs = (P(None, "gz", "gy", None), P(None, None, "gy", "gz"), P(), P(), P())
    out_specs = P(None, "gz", "gy", None)
    return jax.shard_map(body, mesh=mesh, in_specs=in_specs, out_specs=out_specs, check_vma=False)
```

```python
import functools
import math

import jax
import jax.numpy as jnp
import ml_dtypes
import numpy as np
from jax import lax
from jax.experimental import pallas as pl
from jax.experimental.pallas import tpu as pltpu
from jax.sharding import PartitionSpec as P

NX = 256
MX = 32
MY = 16
MZ = 16
CH = 32
VMEM_BYTES = 16 * 1024 * 1024
BF = jnp.bfloat16
F32 = jnp.float32


def kept(count, total):
    series = np.arange(count)
    return np.where(series < count // 2, series, total - count + series)


def trig(freqs, places, total):
    angle = 2.0 * np.pi * ((freqs[:, None] * places[None, :]) % total) / total
    return np.cos(angle), np.sin(angle)


def halves(table):
    table = np.asarray(table, np.float64)
    top = table.astype(np.float32).astype(ml_dtypes.bfloat16)
    rest = (table - top.astype(np.float64)).astype(np.float32).astype(ml_dtypes.bfloat16)
    return jnp.asarray(top), jnp.asarray(rest)


def y_table(y_local, gy, inverse):
    out = []
    for g in range(gy):
        places = g * y_local + np.arange(y_local)
        out.append(np.concatenate(trig(kept(MY, y_local * gy), places, y_local * gy), axis=0))
    return np.stack([t.T for t in out] if inverse else out)


def x_table(inverse, scale=1.0):
    c, s = trig(np.arange(MX), np.arange(NX), NX)
    w = np.where(np.arange(MX) == 0, 1.0, 2.0)[:, None] if inverse else 1.0
    out = np.zeros((2, 2, 2, MX, NX))
    for p in range(2):
        out[p, p, 0] = w * c * scale
        out[p, p, 1] = -w * s * scale
    out = out.reshape(2, 4 * MX, NX)
    return out if inverse else out.transpose(0, 2, 1)


def z_tables(gz, gy, rows, scale):
    c, s = trig(kept(MZ, gz), np.arange(gz), gz)
    eye = np.eye(rows)
    one = np.ones(gy)
    both = np.stack([c, s])
    fwd = np.einsum("tqz,g,jk->tqjzgk", both, one, eye) * scale
    inv = np.einsum("tqz,g,jk->tzgjqk", both, one, eye)
    return fwd.reshape(2 * MZ * rows, gz * gy * rows), inv.reshape(2 * gz * gy * rows, MZ * rows)


def parts(value):
    top = value.astype(BF)
    return top, (value - top.astype(F32)).astype(BF)


def dot(a, b):
    return jnp.dot(a, b, preferred_element_type=F32)


def dot3(a, b):
    rows = a[0].shape[0]
    both = dot(jnp.concatenate([a[0], a[1]], axis=0), b[0])
    return both[:rows] + (both[rows:] + dot(a[0], b[1]))


def swap_parts(value):
    lane = lax.broadcasted_iota(jnp.int32, value.shape, 1)
    is_real = (lane // MX) % 2 == 0
    width = value.shape[1]
    return jnp.where(is_real, pltpu.roll(value, width - MX, 1), pltpu.roll(value, MX, 1)), is_real


def forward_kernel(field, x_top, x_rest, y_top, y_rest, out, taken, x_both, y_both, sem):
    gy = lax.axis_index("gy")
    few = [
        pltpu.make_async_copy(src, dst, sem.at[4 + i])
        for i, (src, dst) in enumerate(
            ((x_top, x_both.at[0]), (x_rest, x_both.at[1]), (y_top.at[gy], y_both.at[0]), (y_rest.at[gy], y_both.at[1]))
        )
    ]
    copies = [pltpu.make_async_copy(field.at[:, q], taken.at[q], sem.at[q]) for q in range(4)]
    for copy in few + copies:
        copy.start()
    for copy in few:
        copy.wait()
    groups, rows = taken.shape[1:3]
    halves_of = []
    for q in range(4):
        copies[q].wait()
        part = dot3(parts(taken[q].reshape(groups * rows, NX)), (x_both[0, q % 2], x_both[1, q % 2]))
        if q % 2:
            halves_of[-1] = halves_of[-1] + part
        else:
            halves_of.append(part)
    total = jnp.concatenate(halves_of, axis=1)
    for g in range(groups):
        both = dot3((y_both[0], y_both[1]), parts(total[g * rows : (g + 1) * rows]))
        crossed, is_real = swap_parts(both[MY:])
        modes = both[:MY] + jnp.where(is_real, crossed, -crossed)
        out[pl.ds(2 * g * MY, MY), :] = modes[:, : 4 * MX]
        out[pl.ds((2 * g + 1) * MY, MY), :] = modes[:, 4 * MX :]


def filter_kernel(arrived, gains, f_top, f_rest, i_top, i_rest, out):
    real, imag = (gains[r].reshape(-1, 2 * MX) for r in range(2))
    first, second = slice(0, MX), slice(MX, 2 * MX)
    same = jnp.concatenate([real[:, first], real[:, first], real[:, second], real[:, second]], axis=1)
    cross = jnp.concatenate([-imag[:, first], imag[:, first], -imag[:, second], imag[:, second]], axis=1)
    half = f_top.shape[0] // 2
    turned = dot3((f_top[...], f_rest[...]), parts(arrived[...]))
    crossed, is_real = swap_parts(turned[half:])
    modes = turned[:half] + jnp.where(is_real, crossed, -crossed)
    crossed, _ = swap_parts(modes)
    filtered = modes * same + crossed * cross
    half = i_top.shape[0] // 2
    back = dot3((i_top[...], i_rest[...]), parts(filtered))
    crossed, is_real = swap_parts(back[half:])
    out[...] = back[:half] + jnp.where(is_real, -crossed, crossed)


def fetch_tiles(field, taken, sems, wanted):
    pending = {}
    for k, t in enumerate(wanted):
        pending[t] = [
            pltpu.make_async_copy(
                field.at[:, pl.ds(8 * t, 8), pl.ds(128 * h, 128)], taken.at[k, h], sems.at[k, h]
            )
            for h in range(2)
        ]
        for copy in pending[t]:
            copy.start()

    def row(t, r):
        for copy in pending.pop(t, ()):
            copy.wait()
        k = wanted.index(t)
        return jnp.concatenate(
            [taken.at[k, h].reshape(CH * 8, 128)[pl.ds(r, CH, stride=8), :] for h in range(2)], axis=1
        )

    return row


def spread_gains(weights, gains, offsets):
    for k in [9 * a + j for a in offsets for j in range(9)]:
        gains[k] = jnp.broadcast_to(weights[:, k : k + 1], (CH, 128))


def mixing(points):
    down = (
        lax.broadcasted_iota(jnp.int32, (8 * CH, CH), 0) // 8
        == lax.broadcasted_iota(jnp.int32, (8 * CH, CH), 1)
    ).astype(BF)
    across = (
        lax.broadcasted_iota(jnp.int32, (CH, 8 * CH), 1) % CH
        == lax.broadcasted_iota(jnp.int32, (CH, 8 * CH), 0)
    ).astype(BF)
    same = (
        lax.broadcasted_iota(jnp.int32, (8 * CH, 8 * CH), 0) % 8
        == lax.broadcasted_iota(jnp.int32, (8 * CH, 8 * CH), 1) // CH
    )
    return tuple(
        jnp.where(same, dot(dot(down, part).astype(BF), across), 0.0).astype(BF)
        for part in parts(points)
    )


def turn(turned, at, value):
    turned[0, at] = pltpu.roll(value, 1, 1)
    turned[1, at] = value
    turned[2, at] = pltpu.roll(value, NX - 1, 1)


def tap_sums(turned, depth, gains, runs, offsets, fresh):
    def some(i, _):
        chans = pl.ds(pl.multiple_of(i * 8, 8), 8)
        gain = {k: gains[k, chans, :] for a in offsets for k in range(9 * a, 9 * a + 9)}
        for h in range(2):
            lanes = pl.ds(128 * h, 128)
            for first, to, rows in runs:
                sums = {}
                for r in range(rows + 2):
                    values = [turned[e, first + r, chans, lanes] for e in range(3)]
                    for b in range(3):
                        o = r - b
                        if o < 0 or o >= rows:
                            continue
                        for k, a in enumerate(offsets):
                            for e in range(3):
                                term = gain[a * 9 + b * 3 + e] * values[e]
                                if (o, k) in sums:
                                    sums[o, k] = sums[o, k] + term
                                elif fresh:
                                    sums[o, k] = term
                                else:
                                    sums[o, k] = depth[k, to + o, chans, lanes] + term
                    if r >= 2:
                        for k in range(len(offsets)):
                            depth[k, to + r - 2, chans, lanes] = sums.pop((r - 2, k))
        return 0

    lax.fori_loop(0, CH // 8, some, 0)


def mix_tile(mix, depth, k, t):
    tile = depth[k, pl.ds(8 * t, 8)].reshape(8 * CH, NX)
    return dot3(mix, parts(tile)).reshape(CH, 8, NX)


def pack_kernel(plan, field, packed, later, edges, taken, rows, ends, sem_in, sem_out):
    middle, split = plan
    last = field.shape[1] // 8 - 1
    before, after = middle[0] - 1, middle[-1] + 1
    wanted = [before, *middle, after] + [t for t in (0, last) if t not in (before, after)]
    row = fetch_tiles(field, taken, sem_in, wanted)
    places = [(before, 7), *[(t, r) for t in middle for r in range(8)], (after, 0)]
    copies = []
    for i, place in enumerate(places):
        rows[i] = row(*place)
        if i + 1 == split:
            copies.append(pltpu.make_async_copy(rows.at[pl.ds(0, split)], packed, sem_out.at[0]))
            copies[-1].start()
    copies.append(pltpu.make_async_copy(rows.at[pl.ds(split, len(places) - split)], later, sem_out.at[1]))
    copies[-1].start()
    ends[0] = row(last, 7)
    ends[1] = row(0, 0)
    copies.append(pltpu.make_async_copy(ends, edges, sem_out.at[2]))
    copies[-1].start()
    for copy in copies:
        copy.wait()


def own_kernel(plan, weight, point, field, halo, *refs):
    upper, lower = plan
    outs, refs = refs[:3], refs[3:]
    taken, halo_rows, weights, points, sent, turned, depth, gains, sem_in, sem_out, sem_few = refs
    few = [
        pltpu.make_async_copy(a, b, sem_few.at[i])
        for i, (a, b) in enumerate(((weight, weights), (point, points), (halo, halo_rows)))
    ]
    for copy in few:
        copy.start()
    wanted = [*upper, upper[-1] + 1, lower[0] - 1, *lower]
    row = fetch_tiles(field, taken, sem_in, wanted)
    for copy in few:
        copy.wait()
    spread_gains(weights, gains, range(3))
    mix = mixing(points[...])
    rows, others = 8 * len(upper), 8 * len(lower)
    for i, place in enumerate([None, *[(t, r) for t in upper for r in range(8)], (upper[-1] + 1, 0)]):
        turn(turned, i, halo_rows[0] if place is None else row(*place))
    for i, place in enumerate([(lower[0] - 1, 7), *[(t, r) for t in lower for r in range(8)], None]):
        turn(turned, rows + 2 + i, halo_rows[1] if place is None else row(*place))
    tap_sums(turned, depth, gains, [(0, 0, rows), (rows + 2, rows, others)], range(3), True)
    copies = []
    for t in range((rows + others) // 8):
        for k, out in enumerate(outs):
            sent[k, t] = mix_tile(mix, depth, k, t)
            copies.append(
                pltpu.make_async_copy(sent.at[k, t], out.at[:, pl.ds(8 * t, 8), :], sem_out.at[k, t])
            )
            copies[-1].start()
    for copy in copies:
        copy.wait()


def middle_kernel(weight, point, *refs):
    planes, out = refs[:6], refs[6]
    taken, weights, points, sent, turned, depth, gains, sem_in, sem_out, sem_few = refs[7:]
    split = planes[0].shape[0]
    few = [
        pltpu.make_async_copy(a, b, sem_few.at[i])
        for i, (a, b) in enumerate(((weight, weights), (point, points)))
    ]
    arrivals = [
        [
            pltpu.make_async_copy(planes[2 * a], taken.at[a, pl.ds(0, split)], sem_in.at[a, 0]),
            pltpu.make_async_copy(
                planes[2 * a + 1], taken.at[a, pl.ds(split, taken.shape[1] - split)], sem_in.at[a, 1]
            ),
        ]
        for a in range(3)
    ]
    for a in (1, 0, 2):
        for copy in arrivals[a]:
            copy.start()
    for copy in few:
        copy.start()
    for copy in few:
        copy.wait()
    spread_gains(weights, gains, range(3))
    mix = mixing(points[...])
    rows = out.shape[1]
    for a in (1, 0, 2):
        for copy in arrivals[a]:
            copy.wait()
        for r in range(rows + 2):
            turn(turned, r, taken[a, r])
        tap_sums(turned, depth, gains, [(0, 0, rows)], [a], a == 1)
    copies = []
    for t in range(rows // 8):
        sent[t] = mix_tile(mix, depth, 0, t)
        copies.append(pltpu.make_async_copy(sent.at[t], out.at[:, pl.ds(8 * t, 8), :], sem_out.at[t]))
        copies[-1].start()
    for copy in copies:
        copy.wait()


def gelu(value):
    size = jnp.abs(value) * math.sqrt(0.5)
    below = 1.0 + 0.3275911 * size
    t = pl.reciprocal(below, approx=True)
    t = t * (2.0 - below * t)
    series = 1.061405429 * t - 1.453152027
    for factor in (1.421413741, -0.284496736, 0.254829592):
        series = series * t + factor
    tail = 0.5 * (series * t) * jnp.exp(-(size * size))
    return value * jnp.where(value < 0.0, tail, 1.0 - tail)


def inverse_kernel(upper, modes, bias, x_top, x_rest, y_top, y_rest, middle, own, out, base, columns):
    q = pl.program_id(0)
    groups, _, y_local, _ = out.shape

    @pl.when(q == 0)
    def _():
        gy = lax.axis_index("gy")
        for g in range(groups):
            own_modes = jnp.concatenate([modes[2 * g], modes[2 * g + 1]], axis=1)
            crossed, is_real = swap_parts(own_modes)
            stack = jnp.concatenate([own_modes, jnp.where(is_real, -crossed, crossed)], axis=0)
            pair = parts(dot3((y_top[gy], y_rest[gy]), parts(stack)))
            for h in range(2):
                for k in range(2):
                    columns[h, k, pl.ds(g * y_local, y_local), :] = pair[k][:, 128 * h : 128 * h + 128]

    h, p = q // 2, q % 2
    rows = dot3((columns[h, 0], columns[h, 1]), (x_top[p], x_rest[p]))
    start, stop = upper, upper + middle.shape[2]
    for g in range(groups):
        plane = rows[g * y_local : (g + 1) * y_local] + bias[4 * g + q]
        out[g, 0, start:stop] = gelu(plane[start:stop] + middle[g, 0])
        base[g, 0, :start] = plane[:start] + own[g, 0, :start]
        base[g, 0, start:] = plane[stop:] + own[g, 0, start:]


def finish_kernel(upper, _, base, low, high, out, held, sent, sem_in, sem_out):
    tiles = base.shape[1] // 8
    gap = out.shape[1] // 8 - tiles
    arrivals = [
        [
            pltpu.make_async_copy(src.at[:, pl.ds(8 * t, 8), :], held.at[i, t], sem_in.at[i, t])
            for i, src in enumerate((base, low, high))
        ]
        for t in range(tiles)
    ]
    for copies in arrivals:
        for copy in copies:
            copy.start()
    done = []
    for t in range(tiles):
        for copy in arrivals[t]:
            copy.wait()
        sent[t] = gelu(held[0, t] + (held[1, t] + held[2, t]))
        to = t if t < upper else t + gap
        done.append(pltpu.make_async_copy(sent.at[t], out.at[:, pl.ds(8 * to, 8), :], sem_out.at[t]))
        done[-1].start()
    for copy in done:
        copy.wait()


def in_hbm(*arrays):
    return [pltpu.with_memory_space_constraint(a, pltpu.HBM) for a in arrays]


def params():
    return pltpu.CompilerParams(vmem_limit_bytes=VMEM_BYTES)


def cost(flops, moved):
    return pl.CostEstimate(flops=flops, bytes_accessed=moved, transcendentals=0)


def whole_block(table):
    return pl.BlockSpec(table.shape, lambda i: (0,) * table.ndim)


def by_four(array):
    return array.reshape(CH // 4, 4, *array.shape[1:])


def forward_call(field, gy, pinned):
    y_local = field.shape[1]
    tables = [*halves(x_table(False)), *halves(y_table(y_local, gy, False))]
    hbm = pl.BlockSpec(memory_space=pltpu.HBM)
    return pl.pallas_call(
        forward_kernel,
        out_shape=(pltpu.HBM if pinned else jax.ShapeDtypeStruct)((CH // 2 * MY, 4 * MX), F32),
        in_specs=[hbm] * 5,
        scratch_shapes=[
            pltpu.VMEM((4, CH // 4, y_local, NX), F32),
            pltpu.VMEM((2, 2, NX, 4 * MX), BF),
            pltpu.VMEM((2, 2 * MY, y_local), BF),
            pltpu.SemaphoreType.DMA((8,)),
        ],
        compiler_params=params(),
        cost_estimate=cost(10**8, 2**18),
        name="forward_modes",
    )(*in_hbm(by_four(field), *tables))


def filter_call(arrived, gains, gz, gy, scale):
    fwd, inv = z_tables(gz, gy, gains.shape[2], scale)
    fwd, inv = halves(fwd), halves(inv)
    return pl.pallas_call(
        filter_kernel,
        out_shape=pltpu.HBM(arrived.shape, F32),
        compiler_params=params(),
        cost_estimate=cost(2 * 10**11, 2**18),
        name="filter_modes",
    )(arrived, *in_hbm(gains, *fwd, *inv))


def inverse_call(modes, bias, middle, own, upper, y_local, gy, scale):
    tables = [*halves(x_table(True, scale)), *halves(y_table(y_local, gy, True))]
    some = lambda rows: pl.BlockSpec((CH // 4, 1, rows, NX), lambda i: (0, i, 0, 0))
    planes = in_hbm(by_four(middle), by_four(own))
    rim = own.shape[1]
    result, base = pl.pallas_call(
        functools.partial(inverse_kernel, upper),
        out_shape=[
            jax.ShapeDtypeStruct((CH // 4, 4, y_local, NX), F32),
            jax.ShapeDtypeStruct((CH // 4, 4, rim, NX), F32),
        ],
        grid=(4,),
        in_specs=[
            whole_block(modes),
            pl.BlockSpec(memory_space=pltpu.SMEM),
            *[whole_block(t) for t in tables],
            *[some(p.shape[2]) for p in planes],
        ],
        out_specs=[some(y_local), some(rim)],
        scratch_shapes=[pltpu.VMEM((2, 2, CH // 4 * y_local, 128), BF)],
        compiler_params=params(),
        cost_estimate=cost(10**8, 2**18),
        name="inverse_modes",
    )(modes, *in_hbm(bias, *tables), *planes)
    return result.reshape(CH, y_local, NX), base.reshape(CH, rim, NX)


def finish_call(result, base, low, high, upper):
    tiles = base.shape[1] // 8
    anywhere = pl.BlockSpec(memory_space=pl.ANY)
    return pl.pallas_call(
        functools.partial(finish_kernel, upper),
        out_shape=jax.ShapeDtypeStruct(result.shape, F32),
        in_specs=[anywhere] * 4,
        out_specs=anywhere,
        scratch_shapes=[
            pltpu.VMEM((3, tiles, CH, 8, NX), F32),
            pltpu.VMEM((tiles, CH, 8, NX), F32),
            pltpu.SemaphoreType.DMA((3, tiles)),
            pltpu.SemaphoreType.DMA((tiles,)),
        ],
        input_output_aliases={0: 0},
        compiler_params=params(),
        cost_estimate=cost(10**8, 2**18),
        name="finished_rows",
    )(result, base, low, high)


def pack_call(field, middle, first):
    count = 8 * len(middle) + 2
    split = 8 * first + 2
    fetched = len(middle) + 4
    hbm = pl.BlockSpec(memory_space=pltpu.HBM)
    return pl.pallas_call(
        functools.partial(pack_kernel, (middle, split)),
        out_shape=[
            pltpu.HBM((split, CH, NX), F32),
            pltpu.HBM((count - split, CH, NX), F32),
            pltpu.HBM((2, CH, NX), F32),
        ],
        in_specs=[hbm],
        out_specs=[hbm] * 3,
        scratch_shapes=[
            pltpu.VMEM((fetched, 2, CH, 8, 128), F32),
            pltpu.VMEM((count, CH, NX), F32),
            pltpu.VMEM((2, CH, NX), F32),
            pltpu.SemaphoreType.DMA((fetched, 2)),
            pltpu.SemaphoreType.DMA((3,)),
        ],
        compiler_params=params(),
        cost_estimate=cost(10**8, 2**18),
        name="packed_rows",
    )(*in_hbm(field))


def own_call(field, halo, weight, point, upper, lower):
    tiles = len(upper) + len(lower)
    rows = 8 * tiles
    hbm = pl.BlockSpec(memory_space=pltpu.HBM)
    shapes = [pltpu.HBM((CH, rows, NX), F32)] * 3
    return pl.pallas_call(
        functools.partial(own_kernel, (upper, lower)),
        out_shape=shapes,
        in_specs=[hbm] * 3 + [pl.BlockSpec(memory_space=pl.ANY)],
        out_specs=[hbm] * len(shapes),
        scratch_shapes=[
            pltpu.VMEM((tiles + 2, 2, CH, 8, 128), F32),
            pltpu.VMEM((2, CH, NX), F32),
            pltpu.VMEM((CH, 27), F32),
            pltpu.VMEM((CH, CH), F32),
            pltpu.VMEM((3, tiles, CH, 8, NX), F32),
            pltpu.VMEM((3, rows + 4, CH, NX), F32),
            pltpu.VMEM((3, rows, CH, NX), F32),
            pltpu.VMEM((27, CH, 128), F32),
            pltpu.SemaphoreType.DMA((tiles + 2, 2)),
            pltpu.SemaphoreType.DMA((3, tiles)),
            pltpu.SemaphoreType.DMA((3,)),
        ],
        compiler_params=params(),
        cost_estimate=cost(10**8, 2**18),
        name="own_sums",
    )(*in_hbm(weight, point, field), halo)


def middle_call(weight, point, low, own, high):
    rows = own[0].shape[0] + own[1].shape[0] - 2
    hbm = pl.BlockSpec(memory_space=pltpu.HBM)
    return pl.pallas_call(
        middle_kernel,
        out_shape=pltpu.HBM((CH, rows, NX), F32),
        in_specs=[hbm] * 2 + [pl.BlockSpec(memory_space=pl.ANY)] * 6,
        out_specs=hbm,
        scratch_shapes=[
            pltpu.VMEM((3, rows + 2, CH, NX), F32),
            pltpu.VMEM((CH, 27), F32),
            pltpu.VMEM((CH, CH), F32),
            pltpu.VMEM((rows // 8, CH, 8, NX), F32),
            pltpu.VMEM((3, rows + 2, CH, NX), F32),
            pltpu.VMEM((1, rows, CH, NX), F32),
            pltpu.VMEM((27, CH, 128), F32),
            pltpu.SemaphoreType.DMA((3, 2)),
            pltpu.SemaphoreType.DMA((rows // 8,)),
            pltpu.SemaphoreType.DMA((2,)),
        ],
        compiler_params=params(),
        cost_estimate=cost(2 * 10**11, 2**18),
        name="middle_sums",
    )(*in_hbm(weight, point), *low, *in_hbm(*own), *high)


def general_filter(coarse, gains, gz, gy, scale):
    j_own, n_own = gains.shape[2], gains.shape[3]
    both = ("gz", "gy")
    flat = coarse.reshape(CH // 2, MY, 2, 2, MX).transpose(3, 1, 0, 2, 4).reshape(2, MY, CH * MX)
    sent = flat.reshape(2, gy, j_own, gz, n_own).transpose(3, 1, 0, 2, 4).reshape(gz * gy, -1)
    got = lax.all_to_all(sent, both, split_axis=0, concat_axis=0, tiled=True)
    got = got.reshape(gz, gy, 2, j_own, n_own)
    c, s = (jnp.asarray(t, F32) for t in trig(kept(MZ, gz), np.arange(gz), gz))
    mul = functools.partial(jnp.einsum, precision=lax.Precision.HIGHEST)
    whole = got.sum(axis=1) * scale
    real = mul("zjn,qz->qjn", whole[:, 0], c) + mul("zjn,qz->qjn", whole[:, 1], s)
    imag = mul("zjn,qz->qjn", whole[:, 1], c) - mul("zjn,qz->qjn", whole[:, 0], s)
    real, imag = real * gains[0] - imag * gains[1], real * gains[1] + imag * gains[0]
    out = jnp.stack(
        [
            mul("qjn,qz->zjn", real, c) - mul("qjn,qz->zjn", imag, s),
            mul("qjn,qz->zjn", real, s) + mul("qjn,qz->zjn", imag, c),
        ],
        axis=1,
    )
    out = jnp.broadcast_to(out[:, None], (gz, gy, 2, j_own, n_own)).reshape(gz * gy, -1)
    back = lax.all_to_all(out, both, split_axis=0, concat_axis=0, tiled=True)
    back = back.reshape(gz, gy, 2, j_own, n_own).transpose(2, 1, 3, 0, 4)
    back = back.reshape(2, MY, CH // 2, 2, MX)
    return back.transpose(2, 1, 3, 0, 4).reshape(CH // 2, MY, 4 * MX)


def body(field, spectral_filter, depth_weight, point_weight, bias_vector):
    gz, gy = lax.axis_size("gz"), lax.axis_size("gy")
    y_local = field.shape[2]
    field = field.reshape(CH, y_local, NX)
    y_total = gy * y_local
    forward_scale = 1.0 / math.sqrt(float(NX) * y_total * gz)
    inverse_scale = 1.0 / math.sqrt(2.0 * MX * MY * MZ)

    def ring(axis, count, by):
        return [(i, (i + by) % count) for i in range(count)]

    def to_neighbours(down, up):
        return (
            lax.ppermute(down, "gz", ring("gz", gz, 1)),
            lax.ppermute(up, "gz", ring("gz", gz, -1)),
        )

    def after(value, *others):
        return lax.optimization_barrier((value, *others))[0]

    tiles = y_local // 8
    upper = (0,)
    lower = tuple(range(tiles - max(1, tiles // 4), tiles))
    middle = tuple(range(1, lower[0]))
    packed, later, edges = pack_call(field, middle, (len(middle) + 1) // 2)
    first_low, first_high = to_neighbours(packed, packed)
    if gy == 2:
        halo = lax.ppermute(edges, "gy", ring("gy", gy, 1))
    else:
        halo = jnp.stack(
            [
                lax.ppermute(edges[0], "gy", ring("gy", gy, 1)),
                lax.ppermute(edges[1], "gy", ring("gy", gy, -1)),
            ]
        )
    j_own, n_own = spectral_filter.shape[2], spectral_filter.shape[3]
    whole_tiles = j_own == 8 and n_own == 2 * MX
    coarse = forward_call(after(field, packed), gy, whole_tiles)
    down, own, up = own_call(after(field, coarse), halo, depth_weight, point_weight, upper, lower)
    if whole_tiles:
        both = ("gz", "gy")
        got = lax.all_to_all(coarse, both, split_axis=0, concat_axis=0, tiled=True)
        sent = after(later, got)
        later_low, later_high = to_neighbours(sent, sent)
        gains = after(spectral_filter, first_low, first_high, own)
        filtered = filter_call(got, gains, gz, gy, forward_scale)
        back = lax.all_to_all(filtered, both, split_axis=0, concat_axis=0, tiled=True)
        back = back.reshape(CH // 2, MY, 4 * MX)
    else:
        later_low, later_high = to_neighbours(later, later)
        back = general_filter(coarse, spectral_filter, gz, gy, forward_scale)
    low, high = to_neighbours(after(down, back), after(up, back))
    mixed = middle_call(
        depth_weight,
        point_weight,
        (first_low, later_low),
        (after(packed, back), later),
        (first_high, later_high),
    )
    result, base = inverse_call(back, bias_vector, mixed, own, 8, y_local, gy, inverse_scale)
    result = finish_call(result, base, low, high, 1)
    return result.reshape(CH, 1, y_local, NX)


def solution(mesh):
    in_specs = (P(None, "gz", "gy", None), P(None, None, "gy", "gz"), P(), P(), P())
    out_specs = P(None, "gz", "gy", None)
    return jax.shard_map(body, mesh=mesh, in_specs=in_specs, out_specs=out_specs, check_vma=False)
```

```python
import functools
import math

import jax
import jax.numpy as jnp
import ml_dtypes
import numpy as np
from jax import lax
from jax.experimental import pallas as pl
from jax.experimental.pallas import tpu as pltpu
from jax.sharding import PartitionSpec as P

NX = 256
MX = 32
MY = 16
MZ = 16
CH = 32
VMEM_BYTES = 16 * 1024 * 1024
BF = jnp.bfloat16
F32 = jnp.float32


def kept(count, total):
    series = np.arange(count)
    return np.where(series < count // 2, series, total - count + series)


def trig(freqs, places, total):
    angle = 2.0 * np.pi * ((freqs[:, None] * places[None, :]) % total) / total
    return np.cos(angle), np.sin(angle)


def halves(table):
    table = np.asarray(table, np.float64)
    top = table.astype(np.float32).astype(ml_dtypes.bfloat16)
    rest = (table - top.astype(np.float64)).astype(np.float32).astype(ml_dtypes.bfloat16)
    return jnp.asarray(top), jnp.asarray(rest)


def y_table(y_local, gy, inverse):
    out = []
    for g in range(gy):
        places = g * y_local + np.arange(y_local)
        out.append(np.concatenate(trig(kept(MY, y_local * gy), places, y_local * gy), axis=0))
    return np.stack([t.T for t in out] if inverse else out)


def x_table(inverse, scale=1.0):
    c, s = trig(np.arange(MX), np.arange(NX), NX)
    w = np.where(np.arange(MX) == 0, 1.0, 2.0)[:, None] if inverse else 1.0
    out = np.zeros((2, 2, 2, MX, NX))
    for p in range(2):
        out[p, p, 0] = w * c * scale
        out[p, p, 1] = -w * s * scale
    out = out.reshape(2, 4 * MX, NX)
    return out if inverse else out.transpose(0, 2, 1)


def z_tables(gz, gy, rows, scale):
    c, s = trig(kept(MZ, gz), np.arange(gz), gz)
    eye = np.eye(rows)
    one = np.ones(gy)
    both = np.stack([c, s])
    fwd = np.einsum("tqz,g,jk->tqjzgk", both, one, eye) * scale
    inv = np.einsum("tqz,g,jk->tzgjqk", both, one, eye)
    return fwd.reshape(2 * MZ * rows, gz * gy * rows), inv.reshape(2 * gz * gy * rows, MZ * rows)


def parts(value):
    top = value.astype(BF)
    return top, (value - top.astype(F32)).astype(BF)


def dot(a, b):
    return jnp.dot(a, b, preferred_element_type=F32)


def dot3(a, b):
    rows = a[0].shape[0]
    both = dot(jnp.concatenate([a[0], a[1]], axis=0), b[0])
    return both[:rows] + (both[rows:] + dot(a[0], b[1]))


def swap_parts(value):
    lane = lax.broadcasted_iota(jnp.int32, value.shape, 1)
    is_real = (lane // MX) % 2 == 0
    width = value.shape[1]
    return jnp.where(is_real, pltpu.roll(value, width - MX, 1), pltpu.roll(value, MX, 1)), is_real


def forward_kernel(field, x_top, x_rest, y_top, y_rest, out, taken, x_both, y_both, sem):
    gy = lax.axis_index("gy")
    few = [
        pltpu.make_async_copy(src, dst, sem.at[4 + i])
        for i, (src, dst) in enumerate(
            ((x_top, x_both.at[0]), (x_rest, x_both.at[1]), (y_top.at[gy], y_both.at[0]), (y_rest.at[gy], y_both.at[1]))
        )
    ]
    copies = [pltpu.make_async_copy(field.at[:, q], taken.at[q], sem.at[q]) for q in range(4)]
    for copy in few + copies:
        copy.start()
    for copy in few:
        copy.wait()
    groups, rows = taken.shape[1:3]
    halves_of = []
    for q in range(4):
        copies[q].wait()
        part = dot3(parts(taken[q].reshape(groups * rows, NX)), (x_both[0, q % 2], x_both[1, q % 2]))
        if q % 2:
            halves_of[-1] = halves_of[-1] + part
        else:
            halves_of.append(part)
    total = jnp.concatenate(halves_of, axis=1)
    for g in range(groups):
        both = dot3((y_both[0], y_both[1]), parts(total[g * rows : (g + 1) * rows]))
        crossed, is_real = swap_parts(both[MY:])
        modes = both[:MY] + jnp.where(is_real, crossed, -crossed)
        out[pl.ds(2 * g * MY, MY), :] = modes[:, : 4 * MX]
        out[pl.ds((2 * g + 1) * MY, MY), :] = modes[:, 4 * MX :]


def filter_kernel(arrived, gains, f_top, f_rest, i_top, i_rest, out):
    real, imag = (gains[r].reshape(-1, 2 * MX) for r in range(2))
    first, second = slice(0, MX), slice(MX, 2 * MX)
    same = jnp.concatenate([real[:, first], real[:, first], real[:, second], real[:, second]], axis=1)
    cross = jnp.concatenate([-imag[:, first], imag[:, first], -imag[:, second], imag[:, second]], axis=1)
    half = f_top.shape[0] // 2
    turned = dot3((f_top[...], f_rest[...]), parts(arrived[...]))
    crossed, is_real = swap_parts(turned[half:])
    modes = turned[:half] + jnp.where(is_real, crossed, -crossed)
    crossed, _ = swap_parts(modes)
    filtered = modes * same + crossed * cross
    half = i_top.shape[0] // 2
    back = dot3((i_top[...], i_rest[...]), parts(filtered))
    crossed, is_real = swap_parts(back[half:])
    out[...] = back[:half] + jnp.where(is_real, -crossed, crossed)


def fetch_tiles(field, taken, sems, wanted):
    pending = {}
    for k, t in enumerate(wanted):
        pending[t] = [
            pltpu.make_async_copy(
                field.at[:, pl.ds(8 * t, 8), pl.ds(128 * h, 128)], taken.at[k, h], sems.at[k, h]
            )
            for h in range(2)
        ]
        for copy in pending[t]:
            copy.start()

    def row(t, r):
        for copy in pending.pop(t, ()):
            copy.wait()
        k = wanted.index(t)
        return jnp.concatenate(
            [taken.at[k, h].reshape(CH * 8, 128)[pl.ds(r, CH, stride=8), :] for h in range(2)], axis=1
        )

    return row


def spread_gains(weights, gains, offsets):
    for k in [9 * a + j for a in offsets for j in range(9)]:
        gains[k] = jnp.broadcast_to(weights[:, k : k + 1], (CH, 128))


def mixing(points):
    down = (
        lax.broadcasted_iota(jnp.int32, (8 * CH, CH), 0) // 8
        == lax.broadcasted_iota(jnp.int32, (8 * CH, CH), 1)
    ).astype(BF)
    across = (
        lax.broadcasted_iota(jnp.int32, (CH, 8 * CH), 1) % CH
        == lax.broadcasted_iota(jnp.int32, (CH, 8 * CH), 0)
    ).astype(BF)
    same = (
        lax.broadcasted_iota(jnp.int32, (8 * CH, 8 * CH), 0) % 8
        == lax.broadcasted_iota(jnp.int32, (8 * CH, 8 * CH), 1) // CH
    )
    return tuple(
        jnp.where(same, dot(dot(down, part).astype(BF), across), 0.0).astype(BF)
        for part in parts(points)
    )


def turn(turned, at, value):
    turned[0, at] = pltpu.roll(value, 1, 1)
    turned[1, at] = value
    turned[2, at] = pltpu.roll(value, NX - 1, 1)


def tap_sums(turned, depth, gains, runs, offsets, fresh):
    def some(i, _):
        chans = pl.ds(pl.multiple_of(i * 8, 8), 8)
        gain = {k: gains[k, chans, :] for a in offsets for k in range(9 * a, 9 * a + 9)}
        for h in range(2):
            lanes = pl.ds(128 * h, 128)
            for first, to, rows in runs:
                sums = {}
                for r in range(rows + 2):
                    values = [turned[e, first + r, chans, lanes] for e in range(3)]
                    for b in range(3):
                        o = r - b
                        if o < 0 or o >= rows:
                            continue
                        for k, a in enumerate(offsets):
                            for e in range(3):
                                term = gain[a * 9 + b * 3 + e] * values[e]
                                if (o, k) in sums:
                                    sums[o, k] = sums[o, k] + term
                                elif fresh:
                                    sums[o, k] = term
                                else:
                                    sums[o, k] = depth[k, to + o, chans, lanes] + term
                    if r >= 2:
                        for k in range(len(offsets)):
                            depth[k, to + r - 2, chans, lanes] = sums.pop((r - 2, k))
        return 0

    lax.fori_loop(0, CH // 8, some, 0)


def mix_tile(mix, depth, k, t):
    tile = depth[k, pl.ds(8 * t, 8)].reshape(8 * CH, NX)
    return dot3(mix, parts(tile)).reshape(CH, 8, NX)


def pack_kernel(plan, field, packed, later, edges, taken, rows, ends, sem_in, sem_out):
    middle, split = plan
    last = field.shape[1] // 8 - 1
    before, after = middle[0] - 1, middle[-1] + 1
    wanted = [before, *middle, after] + [t for t in (0, last) if t not in (before, after)]
    row = fetch_tiles(field, taken, sem_in, wanted)
    places = [(before, 7), *[(t, r) for t in middle for r in range(8)], (after, 0)]
    copies = []
    for i, place in enumerate(places):
        rows[i] = row(*place)
        if i + 1 == split:
            copies.append(pltpu.make_async_copy(rows.at[pl.ds(0, split)], packed, sem_out.at[0]))
            copies[-1].start()
    copies.append(pltpu.make_async_copy(rows.at[pl.ds(split, len(places) - split)], later, sem_out.at[1]))
    copies[-1].start()
    ends[0] = row(last, 7)
    ends[1] = row(0, 0)
    copies.append(pltpu.make_async_copy(ends, edges, sem_out.at[2]))
    copies[-1].start()
    for copy in copies:
        copy.wait()


def own_kernel(plan, weight, point, field, halo, *refs):
    upper, lower = plan
    outs, refs = refs[:3], refs[3:]
    taken, halo_rows, weights, points, sent, turned, depth, gains, sem_in, sem_out, sem_few = refs
    few = [
        pltpu.make_async_copy(a, b, sem_few.at[i])
        for i, (a, b) in enumerate(((weight, weights), (point, points), (halo, halo_rows)))
    ]
    for copy in few:
        copy.start()
    wanted = [*upper, upper[-1] + 1, lower[0] - 1, *lower]
    row = fetch_tiles(field, taken, sem_in, wanted)
    for copy in few:
        copy.wait()
    spread_gains(weights, gains, range(3))
    mix = mixing(points[...])
    rows, others = 8 * len(upper), 8 * len(lower)
    for i, place in enumerate([None, *[(t, r) for t in upper for r in range(8)], (upper[-1] + 1, 0)]):
        turn(turned, i, halo_rows[0] if place is None else row(*place))
    for i, place in enumerate([(lower[0] - 1, 7), *[(t, r) for t in lower for r in range(8)], None]):
        turn(turned, rows + 2 + i, halo_rows[1] if place is None else row(*place))
    tap_sums(turned, depth, gains, [(0, 0, rows), (rows + 2, rows, others)], range(3), True)
    copies = []
    for t in range((rows + others) // 8):
        for k, out in enumerate(outs):
            sent[k, t] = mix_tile(mix, depth, k, t)
            copies.append(
                pltpu.make_async_copy(sent.at[k, t], out.at[:, pl.ds(8 * t, 8), :], sem_out.at[k, t])
            )
            copies[-1].start()
    for copy in copies:
        copy.wait()


def middle_kernel(pieces, weight, point, *refs):
    count = len(pieces)
    planes, out = refs[: 3 * count], refs[3 * count]
    taken, weights, points, sent, turned, depth, gains, sem_in, sem_out, sem_few = refs[3 * count + 1 :]
    few = [
        pltpu.make_async_copy(a, b, sem_few.at[i])
        for i, (a, b) in enumerate(((weight, weights), (point, points)))
    ]
    arrivals = []
    for a in range(3):
        copies, to = [], 0
        for k, (first, rows) in enumerate(pieces):
            copies.append(
                pltpu.make_async_copy(
                    planes[count * a + k].at[pl.ds(first, rows)], taken.at[a, pl.ds(to, rows)], sem_in.at[a, k]
                )
            )
            to += rows
        arrivals.append(copies)
    for a in (1, 0, 2):
        for copy in arrivals[a]:
            copy.start()
    for copy in few:
        copy.start()
    for copy in few:
        copy.wait()
    spread_gains(weights, gains, range(3))
    mix = mixing(points[...])
    rows = out.shape[1]
    for a in (1, 0, 2):
        for copy in arrivals[a]:
            copy.wait()
        for r in range(rows + 2):
            turn(turned, r, taken[a, r])
        tap_sums(turned, depth, gains, [(0, 0, rows)], [a], a == 1)
    copies = []
    for t in range(rows // 8):
        sent[t] = mix_tile(mix, depth, 0, t)
        copies.append(pltpu.make_async_copy(sent.at[t], out.at[:, pl.ds(8 * t, 8), :], sem_out.at[t]))
        copies[-1].start()
    for copy in copies:
        copy.wait()


def gelu(value):
    size = jnp.abs(value) * math.sqrt(0.5)
    below = 1.0 + 0.3275911 * size
    t = pl.reciprocal(below, approx=True)
    t = t * (2.0 - below * t)
    series = 1.061405429 * t - 1.453152027
    for factor in (1.421413741, -0.284496736, 0.254829592):
        series = series * t + factor
    tail = 0.5 * (series * t) * jnp.exp(-(size * size))
    return value * jnp.where(value < 0.0, tail, 1.0 - tail)


def inverse_kernel(upper, modes, bias, x_top, x_rest, y_top, y_rest, own, *refs):
    middle, (out, base, columns) = refs[:-3], refs[-3:]
    q = pl.program_id(0)
    groups, _, y_local, _ = out.shape

    @pl.when(q == 0)
    def _():
        gy = lax.axis_index("gy")
        for g in range(groups):
            own_modes = jnp.concatenate([modes[2 * g], modes[2 * g + 1]], axis=1)
            crossed, is_real = swap_parts(own_modes)
            stack = jnp.concatenate([own_modes, jnp.where(is_real, -crossed, crossed)], axis=0)
            pair = parts(dot3((y_top[gy], y_rest[gy]), parts(stack)))
            for h in range(2):
                for k in range(2):
                    columns[h, k, pl.ds(g * y_local, y_local), :] = pair[k][:, 128 * h : 128 * h + 128]

    h, p = q // 2, q % 2
    rows = dot3((columns[h, 0], columns[h, 1]), (x_top[p], x_rest[p]))
    for g in range(groups):
        plane = rows[g * y_local : (g + 1) * y_local] + bias[4 * g + q]
        base[g, 0, :upper] = plane[:upper] + own[g, 0, :upper]
        at = upper
        for part in middle:
            to = at + part.shape[2]
            out[g, 0, at:to] = gelu(plane[at:to] + part[g, 0])
            at = to
        base[g, 0, upper:] = plane[at:] + own[g, 0, upper:]


def finish_kernel(upper, _, base, low, high, out, held, sent, sem_in, sem_out):
    tiles = base.shape[1] // 8
    gap = out.shape[1] // 8 - tiles
    arrivals = [
        [
            pltpu.make_async_copy(src.at[:, pl.ds(8 * t, 8), :], held.at[i, t], sem_in.at[i, t])
            for i, src in enumerate((base, low, high))
        ]
        for t in range(tiles)
    ]
    for copies in arrivals:
        for copy in copies:
            copy.start()
    done = []
    for t in range(tiles):
        for copy in arrivals[t]:
            copy.wait()
        sent[t] = gelu(held[0, t] + (held[1, t] + held[2, t]))
        to = t if t < upper else t + gap
        done.append(pltpu.make_async_copy(sent.at[t], out.at[:, pl.ds(8 * to, 8), :], sem_out.at[t]))
        done[-1].start()
    for copy in done:
        copy.wait()


def in_hbm(*arrays):
    return [pltpu.with_memory_space_constraint(a, pltpu.HBM) for a in arrays]


def params():
    return pltpu.CompilerParams(vmem_limit_bytes=VMEM_BYTES)


def cost(flops, moved):
    return pl.CostEstimate(flops=flops, bytes_accessed=moved, transcendentals=0)


def whole_block(table):
    return pl.BlockSpec(table.shape, lambda i: (0,) * table.ndim)


def by_four(array):
    return array.reshape(CH // 4, 4, *array.shape[1:])


def forward_call(field, gy, pinned):
    y_local = field.shape[1]
    tables = [*halves(x_table(False)), *halves(y_table(y_local, gy, False))]
    hbm = pl.BlockSpec(memory_space=pltpu.HBM)
    return pl.pallas_call(
        forward_kernel,
        out_shape=(pltpu.HBM if pinned else jax.ShapeDtypeStruct)((CH // 2 * MY, 4 * MX), F32),
        in_specs=[hbm] * 5,
        scratch_shapes=[
            pltpu.VMEM((4, CH // 4, y_local, NX), F32),
            pltpu.VMEM((2, 2, NX, 4 * MX), BF),
            pltpu.VMEM((2, 2 * MY, y_local), BF),
            pltpu.SemaphoreType.DMA((8,)),
        ],
        compiler_params=params(),
        cost_estimate=cost(10**8, 2**18),
        name="forward_modes",
    )(*in_hbm(by_four(field), *tables))


def filter_call(arrived, gains, gz, gy, scale):
    fwd, inv = z_tables(gz, gy, gains.shape[2], scale)
    fwd, inv = halves(fwd), halves(inv)
    return pl.pallas_call(
        filter_kernel,
        out_shape=pltpu.HBM(arrived.shape, F32),
        compiler_params=params(),
        cost_estimate=cost(2 * 10**11, 2**18),
        name="filter_modes",
    )(arrived, *in_hbm(gains, *fwd, *inv))


def inverse_call(modes, bias, middle, own, upper, y_local, gy, scale):
    tables = [*halves(x_table(True, scale)), *halves(y_table(y_local, gy, True))]
    some = lambda rows: pl.BlockSpec((CH // 4, 1, rows, NX), lambda i: (0, i, 0, 0))
    planes = in_hbm(by_four(own), *map(by_four, middle))
    rim = own.shape[1]
    result, base = pl.pallas_call(
        functools.partial(inverse_kernel, upper),
        out_shape=[
            jax.ShapeDtypeStruct((CH // 4, 4, y_local, NX), F32),
            jax.ShapeDtypeStruct((CH // 4, 4, rim, NX), F32),
        ],
        grid=(4,),
        in_specs=[
            whole_block(modes),
            pl.BlockSpec(memory_space=pltpu.SMEM),
            *[whole_block(t) for t in tables],
            *[some(p.shape[2]) for p in planes],
        ],
        out_specs=[some(y_local), some(rim)],
        scratch_shapes=[pltpu.VMEM((2, 2, CH // 4 * y_local, 128), BF)],
        compiler_params=params(),
        cost_estimate=cost(10**8, 2**18),
        name="inverse_modes",
    )(modes, *in_hbm(bias, *tables), *planes)
    return result.reshape(CH, y_local, NX), base.reshape(CH, rim, NX)


def finish_call(result, base, low, high, upper):
    tiles = base.shape[1] // 8
    anywhere = pl.BlockSpec(memory_space=pl.ANY)
    return pl.pallas_call(
        functools.partial(finish_kernel, upper),
        out_shape=jax.ShapeDtypeStruct(result.shape, F32),
        in_specs=[anywhere] * 4,
        out_specs=anywhere,
        scratch_shapes=[
            pltpu.VMEM((3, tiles, CH, 8, NX), F32),
            pltpu.VMEM((tiles, CH, 8, NX), F32),
            pltpu.SemaphoreType.DMA((3, tiles)),
            pltpu.SemaphoreType.DMA((tiles,)),
        ],
        input_output_aliases={0: 0},
        compiler_params=params(),
        cost_estimate=cost(10**8, 2**18),
        name="finished_rows",
    )(result, base, low, high)


def pack_call(field, middle, first):
    count = 8 * len(middle) + 2
    split = 8 * first + 2
    fetched = len(middle) + 4
    hbm = pl.BlockSpec(memory_space=pltpu.HBM)
    return pl.pallas_call(
        functools.partial(pack_kernel, (middle, split)),
        out_shape=[
            pltpu.HBM((split, CH, NX), F32),
            pltpu.HBM((count - split, CH, NX), F32),
            pltpu.HBM((2, CH, NX), F32),
        ],
        in_specs=[hbm],
        out_specs=[hbm] * 3,
        scratch_shapes=[
            pltpu.VMEM((fetched, 2, CH, 8, 128), F32),
            pltpu.VMEM((count, CH, NX), F32),
            pltpu.VMEM((2, CH, NX), F32),
            pltpu.SemaphoreType.DMA((fetched, 2)),
            pltpu.SemaphoreType.DMA((3,)),
        ],
        compiler_params=params(),
        cost_estimate=cost(10**8, 2**18),
        name="packed_rows",
    )(*in_hbm(field))


def own_call(field, halo, weight, point, upper, lower):
    tiles = len(upper) + len(lower)
    rows = 8 * tiles
    hbm = pl.BlockSpec(memory_space=pltpu.HBM)
    shapes = [pltpu.HBM((CH, rows, NX), F32)] * 3
    return pl.pallas_call(
        functools.partial(own_kernel, (upper, lower)),
        out_shape=shapes,
        in_specs=[hbm] * 3 + [pl.BlockSpec(memory_space=pl.ANY)],
        out_specs=[hbm] * len(shapes),
        scratch_shapes=[
            pltpu.VMEM((tiles + 2, 2, CH, 8, 128), F32),
            pltpu.VMEM((2, CH, NX), F32),
            pltpu.VMEM((CH, 27), F32),
            pltpu.VMEM((CH, CH), F32),
            pltpu.VMEM((3, tiles, CH, 8, NX), F32),
            pltpu.VMEM((3, rows + 4, CH, NX), F32),
            pltpu.VMEM((3, rows, CH, NX), F32),
            pltpu.VMEM((27, CH, 128), F32),
            pltpu.SemaphoreType.DMA((tiles + 2, 2)),
            pltpu.SemaphoreType.DMA((3, tiles)),
            pltpu.SemaphoreType.DMA((3,)),
        ],
        compiler_params=params(),
        cost_estimate=cost(10**8, 2**18),
        name="own_sums",
    )(*in_hbm(weight, point, field), halo)


def middle_call(weight, point, low, own, high, pieces):
    rows = sum(r for _, r in pieces) - 2
    hbm = pl.BlockSpec(memory_space=pltpu.HBM)
    return pl.pallas_call(
        functools.partial(middle_kernel, pieces),
        out_shape=pltpu.HBM((CH, rows, NX), F32),
        in_specs=[hbm] * 2 + [pl.BlockSpec(memory_space=pl.ANY)] * (3 * len(pieces)),
        out_specs=hbm,
        scratch_shapes=[
            pltpu.VMEM((3, rows + 2, CH, NX), F32),
            pltpu.VMEM((CH, 27), F32),
            pltpu.VMEM((CH, CH), F32),
            pltpu.VMEM((rows // 8, CH, 8, NX), F32),
            pltpu.VMEM((3, rows + 2, CH, NX), F32),
            pltpu.VMEM((1, rows, CH, NX), F32),
            pltpu.VMEM((27, CH, 128), F32),
            pltpu.SemaphoreType.DMA((3, len(pieces))),
            pltpu.SemaphoreType.DMA((rows // 8,)),
            pltpu.SemaphoreType.DMA((2,)),
        ],
        compiler_params=params(),
        cost_estimate=cost(2 * 10**11 if len(pieces) > 1 else 10**8, 2**18),
        name="middle_sums",
    )(*in_hbm(weight, point), *low, *in_hbm(*own), *high)


def general_filter(coarse, gains, gz, gy, scale):
    j_own, n_own = gains.shape[2], gains.shape[3]
    both = ("gz", "gy")
    flat = coarse.reshape(CH // 2, MY, 2, 2, MX).transpose(3, 1, 0, 2, 4).reshape(2, MY, CH * MX)
    sent = flat.reshape(2, gy, j_own, gz, n_own).transpose(3, 1, 0, 2, 4).reshape(gz * gy, -1)
    got = lax.all_to_all(sent, both, split_axis=0, concat_axis=0, tiled=True)
    got = got.reshape(gz, gy, 2, j_own, n_own)
    c, s = (jnp.asarray(t, F32) for t in trig(kept(MZ, gz), np.arange(gz), gz))
    mul = functools.partial(jnp.einsum, precision=lax.Precision.HIGHEST)
    whole = got.sum(axis=1) * scale
    real = mul("zjn,qz->qjn", whole[:, 0], c) + mul("zjn,qz->qjn", whole[:, 1], s)
    imag = mul("zjn,qz->qjn", whole[:, 1], c) - mul("zjn,qz->qjn", whole[:, 0], s)
    real, imag = real * gains[0] - imag * gains[1], real * gains[1] + imag * gains[0]
    out = jnp.stack(
        [
            mul("qjn,qz->zjn", real, c) - mul("qjn,qz->zjn", imag, s),
            mul("qjn,qz->zjn", real, s) + mul("qjn,qz->zjn", imag, c),
        ],
        axis=1,
    )
    out = jnp.broadcast_to(out[:, None], (gz, gy, 2, j_own, n_own)).reshape(gz * gy, -1)
    back = lax.all_to_all(out, both, split_axis=0, concat_axis=0, tiled=True)
    back = back.reshape(gz, gy, 2, j_own, n_own).transpose(2, 1, 3, 0, 4)
    back = back.reshape(2, MY, CH // 2, 2, MX)
    return back.transpose(2, 1, 3, 0, 4).reshape(CH // 2, MY, 4 * MX)


def body(field, spectral_filter, depth_weight, point_weight, bias_vector):
    gz, gy = lax.axis_size("gz"), lax.axis_size("gy")
    y_local = field.shape[2]
    field = field.reshape(CH, y_local, NX)
    y_total = gy * y_local
    forward_scale = 1.0 / math.sqrt(float(NX) * y_total * gz)
    inverse_scale = 1.0 / math.sqrt(2.0 * MX * MY * MZ)

    def ring(axis, count, by):
        return [(i, (i + by) % count) for i in range(count)]

    def to_neighbours(down, up):
        return (
            lax.ppermute(down, "gz", ring("gz", gz, 1)),
            lax.ppermute(up, "gz", ring("gz", gz, -1)),
        )

    def after(value, *others):
        return lax.optimization_barrier((value, *others))[0]

    tiles = y_local // 8
    upper = (0,)
    lower = (tiles - 1,)
    middle = tuple(range(1, lower[0]))
    early = 8 * ((len(middle) + 1) // 2)
    late = 8 * len(middle) - early
    packed, later, edges = pack_call(field, middle, early // 8)
    first_low, first_high = to_neighbours(packed, packed)
    if gy == 2:
        halo = lax.ppermute(edges, "gy", ring("gy", gy, 1))
    else:
        halo = jnp.stack(
            [
                lax.ppermute(edges[0], "gy", ring("gy", gy, 1)),
                lax.ppermute(edges[1], "gy", ring("gy", gy, -1)),
            ]
        )
    j_own, n_own = spectral_filter.shape[2], spectral_filter.shape[3]
    whole_tiles = j_own == 8 and n_own == 2 * MX
    coarse = forward_call(after(field, packed), gy, whole_tiles)
    down, own, up = own_call(after(field, coarse), halo, depth_weight, point_weight, upper, lower)
    if whole_tiles:
        both = ("gz", "gy")
        got = lax.all_to_all(coarse, both, split_axis=0, concat_axis=0, tiled=True)
        sent = after(later, got)
        later_low, later_high = to_neighbours(sent, sent)
        gains = after(spectral_filter, first_low, first_high, own)
        filtered = filter_call(got, gains, gz, gy, forward_scale)
        back = lax.all_to_all(filtered, both, split_axis=0, concat_axis=0, tiled=True)
        back = back.reshape(CH // 2, MY, 4 * MX)
        mark = filtered
    else:
        later_low, later_high = to_neighbours(later, later)
        mark = back = general_filter(coarse, spectral_filter, gz, gy, forward_scale)
    mixed = middle_call(
        depth_weight, point_weight, (first_low,), (after(packed, mark),), (first_high,), ((0, early + 2),)
    )
    down, up, later, _, _ = lax.optimization_barrier((down, up, later, back, mixed))
    low, high = to_neighbours(down, up)
    mixed_later = middle_call(
        depth_weight,
        point_weight,
        (first_low, later_low),
        (packed, later),
        (first_high, later_high),
        ((early, 2), (0, late)),
    )
    result, base = inverse_call(
        back, bias_vector, (mixed, mixed_later), own, 8, y_local, gy, inverse_scale
    )
    result = finish_call(result, base, low, high, 1)
    return result.reshape(CH, 1, y_local, NX)


def solution(mesh):
    in_specs = (P(None, "gz", "gy", None), P(None, None, "gy", "gz"), P(), P(), P())
    out_specs = P(None, "gz", "gy", None)
    return jax.shard_map(body, mesh=mesh, in_specs=in_specs, out_specs=out_specs, check_vma=False)
```

```python
import functools
import math

import jax
import jax.numpy as jnp
import ml_dtypes
import numpy as np
from jax import lax
from jax.experimental import pallas as pl
from jax.experimental.pallas import tpu as pltpu
from jax.sharding import PartitionSpec as P

NX = 256
MX = 32
MY = 16
MZ = 16
CH = 32
VMEM_BYTES = 16 * 1024 * 1024
BF = jnp.bfloat16
F32 = jnp.float32


def kept(count, total):
    series = np.arange(count)
    return np.where(series < count // 2, series, total - count + series)


def trig(freqs, places, total):
    angle = 2.0 * np.pi * ((freqs[:, None] * places[None, :]) % total) / total
    return np.cos(angle), np.sin(angle)


def halves(table):
    table = np.asarray(table, np.float64)
    top = table.astype(np.float32).astype(ml_dtypes.bfloat16)
    rest = (table - top.astype(np.float64)).astype(np.float32).astype(ml_dtypes.bfloat16)
    return jnp.asarray(top), jnp.asarray(rest)


def y_table(y_local, gy, inverse):
    out = []
    for g in range(gy):
        places = g * y_local + np.arange(y_local)
        out.append(np.concatenate(trig(kept(MY, y_local * gy), places, y_local * gy), axis=0))
    return np.stack([t.T for t in out] if inverse else out)


def x_table(inverse, scale=1.0):
    c, s = trig(np.arange(MX), np.arange(NX), NX)
    w = np.where(np.arange(MX) == 0, 1.0, 2.0)[:, None] if inverse else 1.0
    out = np.zeros((2, 2, 2, MX, NX))
    for p in range(2):
        out[p, p, 0] = w * c * scale
        out[p, p, 1] = -w * s * scale
    out = out.reshape(2, 4 * MX, NX)
    return out if inverse else out.transpose(0, 2, 1)


def z_tables(gz, gy, rows, scale):
    c, s = trig(kept(MZ, gz), np.arange(gz), gz)
    eye = np.eye(rows)
    one = np.ones(gy)
    both = np.stack([c, s])
    fwd = np.einsum("tqz,g,jk->tqjzgk", both, one, eye) * scale
    inv = np.einsum("tqz,g,jk->tzgjqk", both, one, eye)
    return fwd.reshape(2 * MZ * rows, gz * gy * rows), inv.reshape(2 * gz * gy * rows, MZ * rows)


def parts(value):
    top = value.astype(BF)
    return top, (value - top.astype(F32)).astype(BF)


def dot(a, b):
    return jnp.dot(a, b, preferred_element_type=F32)


def dot3(a, b):
    rows = a[0].shape[0]
    both = dot(jnp.concatenate([a[0], a[1]], axis=0), b[0])
    return both[:rows] + (both[rows:] + dot(a[0], b[1]))


def swap_parts(value):
    lane = lax.broadcasted_iota(jnp.int32, value.shape, 1)
    is_real = (lane // MX) % 2 == 0
    width = value.shape[1]
    return jnp.where(is_real, pltpu.roll(value, width - MX, 1), pltpu.roll(value, MX, 1)), is_real


def forward_kernel(field, x_top, x_rest, y_top, y_rest, out, taken, x_both, y_both, sem):
    gy = lax.axis_index("gy")
    few = [
        pltpu.make_async_copy(src, dst, sem.at[4 + i])
        for i, (src, dst) in enumerate(
            ((x_top, x_both.at[0]), (x_rest, x_both.at[1]), (y_top.at[gy], y_both.at[0]), (y_rest.at[gy], y_both.at[1]))
        )
    ]
    copies = [pltpu.make_async_copy(field.at[:, q], taken.at[q], sem.at[q]) for q in range(4)]
    for copy in few + copies:
        copy.start()
    for copy in few:
        copy.wait()
    groups, rows = taken.shape[1:3]
    halves_of = []
    for q in range(4):
        copies[q].wait()
        part = dot3(parts(taken[q].reshape(groups * rows, NX)), (x_both[0, q % 2], x_both[1, q % 2]))
        if q % 2:
            halves_of[-1] = halves_of[-1] + part
        else:
            halves_of.append(part)
    total = jnp.concatenate(halves_of, axis=1)
    for g in range(groups):
        both = dot3((y_both[0], y_both[1]), parts(total[g * rows : (g + 1) * rows]))
        crossed, is_real = swap_parts(both[MY:])
        modes = both[:MY] + jnp.where(is_real, crossed, -crossed)
        out[pl.ds(2 * g * MY, MY), :] = modes[:, : 4 * MX]
        out[pl.ds((2 * g + 1) * MY, MY), :] = modes[:, 4 * MX :]


def filter_kernel(arrived, gains, f_top, f_rest, i_top, i_rest, out):
    real, imag = (gains[r].reshape(-1, 2 * MX) for r in range(2))
    first, second = slice(0, MX), slice(MX, 2 * MX)
    same = jnp.concatenate([real[:, first], real[:, first], real[:, second], real[:, second]], axis=1)
    cross = jnp.concatenate([-imag[:, first], imag[:, first], -imag[:, second], imag[:, second]], axis=1)
    half = f_top.shape[0] // 2
    turned = dot3((f_top[...], f_rest[...]), parts(arrived[...]))
    crossed, is_real = swap_parts(turned[half:])
    modes = turned[:half] + jnp.where(is_real, crossed, -crossed)
    crossed, _ = swap_parts(modes)
    filtered = modes * same + crossed * cross
    half = i_top.shape[0] // 2
    back = dot3((i_top[...], i_rest[...]), parts(filtered))
    crossed, is_real = swap_parts(back[half:])
    out[...] = back[:half] + jnp.where(is_real, -crossed, crossed)


def fetch_tiles(field, taken, sems, wanted):
    pending = {}
    for k, t in enumerate(wanted):
        pending[t] = [
            pltpu.make_async_copy(
                field.at[:, pl.ds(8 * t, 8), pl.ds(128 * h, 128)], taken.at[k, h], sems.at[k, h]
            )
            for h in range(2)
        ]
        for copy in pending[t]:
            copy.start()

    def row(t, r):
        for copy in pending.pop(t, ()):
            copy.wait()
        k = wanted.index(t)
        return jnp.concatenate(
            [taken.at[k, h].reshape(CH * 8, 128)[pl.ds(r, CH, stride=8), :] for h in range(2)], axis=1
        )

    return row


def spread_gains(weights, gains, offsets):
    for k in [9 * a + j for a in offsets for j in range(9)]:
        gains[k] = jnp.broadcast_to(weights[:, k : k + 1], (CH, 128))


def mixing(points):
    down = (
        lax.broadcasted_iota(jnp.int32, (8 * CH, CH), 0) // 8
        == lax.broadcasted_iota(jnp.int32, (8 * CH, CH), 1)
    ).astype(BF)
    across = (
        lax.broadcasted_iota(jnp.int32, (CH, 8 * CH), 1) % CH
        == lax.broadcasted_iota(jnp.int32, (CH, 8 * CH), 0)
    ).astype(BF)
    same = (
        lax.broadcasted_iota(jnp.int32, (8 * CH, 8 * CH), 0) % 8
        == lax.broadcasted_iota(jnp.int32, (8 * CH, 8 * CH), 1) // CH
    )
    return tuple(
        jnp.where(same, dot(dot(down, part).astype(BF), across), 0.0).astype(BF)
        for part in parts(points)
    )


def tap_sums(load, uses, gains, depth, runs):
    def some(i, _):
        chans = pl.ds(pl.multiple_of(i * 8, 8), 8)
        wanted = sorted({a for use in uses for a, _ in use})
        gain = {k: gains[k, chans, :] for a in wanted for k in range(9 * a, 9 * a + 9)}
        for first, to, rows in runs:
            sums = {}
            for r in range(rows + 2):
                for s, use in enumerate(uses):
                    value = load(s, first + r, chans)
                    turned = (pltpu.roll(value, 1, 1), value, pltpu.roll(value, NX - 1, 1))
                    for b in range(3):
                        o = r - b
                        if o < 0 or o >= rows:
                            continue
                        for a, k in use:
                            for e in range(3):
                                for h in range(2):
                                    term = gain[a * 9 + b * 3 + e] * turned[e][:, 128 * h : 128 * h + 128]
                                    place = (o, k, h)
                                    sums[place] = sums[place] + term if place in sums else term
                if r >= 2:
                    for k in sorted({k for use in uses for _, k in use}):
                        for h in range(2):
                            depth[k, to + r - 2, chans, pl.ds(128 * h, 128)] = sums.pop((r - 2, k, h))
        return 0

    lax.fori_loop(0, CH // 8, some, 0)


def mix_tile(mix, depth, k, t):
    tile = depth[k, pl.ds(8 * t, 8)].reshape(8 * CH, NX)
    return dot3(mix, parts(tile)).reshape(CH, 8, NX)


def pack_kernel(tiles, field, packed, edges, taken, rows, ends, sem_in, sem_out):
    last = field.shape[1] // 8 - 1
    before, after = tiles[0] - 1, tiles[-1] + 1
    wanted = [before, *tiles, after] + [t for t in (0, last) if t not in (before, after)]
    row = fetch_tiles(field, taken, sem_in, wanted)
    places = [(before, 7), *[(t, r) for t in tiles for r in range(8)], (after, 0)]
    copies, cuts = [], (0, len(places) // 2, len(places))
    for k in range(2):
        for i in range(cuts[k], cuts[k + 1]):
            rows[i] = row(*places[i])
        some = pl.ds(cuts[k], cuts[k + 1] - cuts[k])
        copies.append(pltpu.make_async_copy(rows.at[some], packed.at[some], sem_out.at[k]))
        copies[-1].start()
    ends[0] = row(last, 7)
    ends[1] = row(0, 0)
    copies.append(pltpu.make_async_copy(ends, edges, sem_out.at[2]))
    copies[-1].start()
    for copy in copies:
        copy.wait()


def own_kernel(segments, weight, point, field, *refs):
    last = field.shape[1] // 8 - 1
    outer = segments[0][0] == 0
    few = [(weight, refs[-9]), (point, refs[-8])]
    if outer:
        few.append((refs[0], refs[-10]))
        refs = refs[1:]
    outs, (taken, halo_rows, weights, points, sent, lined, depth, gains, sem_in, sem_out, sem_few) = (
        refs[:3],
        refs[3:],
    )
    few = [pltpu.make_async_copy(src, dst, sem_few.at[i]) for i, (src, dst) in enumerate(few)]
    wanted = sorted({t for tiles in segments for t in (tiles[0] - 1, *tiles, tiles[-1] + 1) if 0 <= t <= last})
    row = fetch_tiles(field, taken, sem_in, wanted)
    for copy in few:
        copy.start()
    for copy in few:
        copy.wait()
    spread_gains(weights, gains, range(3))
    mix = mixing(points[...])
    runs, at, done = [], 0, 0
    for tiles in segments:
        places = [(tiles[0] - 1, 7), *[(t, r) for t in tiles for r in range(8)], (tiles[-1] + 1, 0)]
        for i, (t, r) in enumerate(places):
            lined[at + i] = halo_rows[0] if t < 0 else halo_rows[1] if t > last else row(t, r)
        runs.append((at, done, 8 * len(tiles)))
        at, done = at + len(places), done + 8 * len(tiles)
    tap_sums(lambda s, r, c: lined[r, c, :], [[(a, a) for a in range(3)]], gains, depth, runs)
    copies = []
    for t in range(done // 8):
        for k, out in enumerate(outs):
            sent[k, t] = mix_tile(mix, depth, k, t)
            copies.append(
                pltpu.make_async_copy(sent.at[k, t], out.at[:, pl.ds(8 * t, 8), :], sem_out.at[k, t])
            )
            copies[-1].start()
    for copy in copies:
        copy.wait()


def middle_kernel(weight, point, low, own, high, out, taken, weights, points, sent, depth, gains, sem_in, sem_out):
    copies = [
        pltpu.make_async_copy(src, dst, sem_in.at[i])
        for i, (src, dst) in enumerate(
            ((weight, weights), (point, points), (low, taken.at[0]), (own, taken.at[1]), (high, taken.at[2]))
        )
    ]
    for copy in copies:
        copy.start()
    for copy in copies[:2]:
        copy.wait()
    spread_gains(weights, gains, range(3))
    mix = mixing(points[...])
    for copy in copies[2:]:
        copy.wait()
    rows = out.shape[1]
    tap_sums(lambda s, r, c: taken[s, r, c, :], [[(a, 0)] for a in range(3)], gains, depth, [(0, 0, rows)])
    copies = []
    for t in range(rows // 8):
        sent[t] = mix_tile(mix, depth, 0, t)
        copies.append(pltpu.make_async_copy(sent.at[t], out.at[:, pl.ds(8 * t, 8), :], sem_out.at[t]))
        copies[-1].start()
    for copy in copies:
        copy.wait()


def gelu(value):
    size = jnp.abs(value) * math.sqrt(0.5)
    below = 1.0 + 0.3275911 * size
    t = pl.reciprocal(below, approx=True)
    t = t * (2.0 - below * t)
    series = 1.061405429 * t - 1.453152027
    for factor in (1.421413741, -0.284496736, 0.254829592):
        series = series * t + factor
    tail = 0.5 * (series * t) * jnp.exp(-(size * size))
    return value * jnp.where(value < 0.0, tail, 1.0 - tail)


def inverse_kernel(upper, modes, bias, x_top, x_rest, y_top, y_rest, own, middle, second, low, high, out, base, columns):
    q = pl.program_id(0)
    groups, _, y_local, _ = out.shape

    @pl.when(q == 0)
    def _():
        gy = lax.axis_index("gy")
        for g in range(groups):
            own_modes = jnp.concatenate([modes[2 * g], modes[2 * g + 1]], axis=1)
            crossed, is_real = swap_parts(own_modes)
            stack = jnp.concatenate([own_modes, jnp.where(is_real, -crossed, crossed)], axis=0)
            pair = parts(dot3((y_top[gy], y_rest[gy]), parts(stack)))
            for h in range(2):
                for k in range(2):
                    columns[h, k, pl.ds(g * y_local, y_local), :] = pair[k][:, 128 * h : 128 * h + 128]

    h, p = q // 2, q % 2
    rows = dot3((columns[h, 0], columns[h, 1]), (x_top[p], x_rest[p]))
    turn = upper + middle.shape[2]
    stop = turn + second.shape[2]
    for g in range(groups):
        plane = rows[g * y_local : (g + 1) * y_local] + bias[4 * g + q]
        base[g, 0, :upper] = plane[:upper] + own[g, 0, :upper]
        out[g, 0, upper:turn] = gelu(plane[upper:turn] + middle[g, 0])
        out[g, 0, turn:stop] = gelu(plane[turn:stop] + (second[g, 0] + (low[g, 0] + high[g, 0])))
        base[g, 0, upper:] = plane[stop:] + own[g, 0, upper:]


def finish_kernel(upper, _, base, low, high, out, held, sent, sem_in, sem_out):
    tiles = base.shape[1] // 8
    gap = out.shape[1] // 8 - tiles
    arrivals = [
        [
            pltpu.make_async_copy(src.at[:, pl.ds(8 * t, 8), :], held.at[i, t], sem_in.at[i, t])
            for i, src in enumerate((base, low, high))
        ]
        for t in range(tiles)
    ]
    for copies in arrivals:
        for copy in copies:
            copy.start()
    done = []
    for t in range(tiles):
        for copy in arrivals[t]:
            copy.wait()
        sent[t] = gelu(held[0, t] + (held[1, t] + held[2, t]))
        to = t if t < upper else t + gap
        done.append(pltpu.make_async_copy(sent.at[t], out.at[:, pl.ds(8 * to, 8), :], sem_out.at[t]))
        done[-1].start()
    for copy in done:
        copy.wait()


def in_hbm(*arrays):
    return [pltpu.with_memory_space_constraint(a, pltpu.HBM) for a in arrays]


def params():
    return pltpu.CompilerParams(vmem_limit_bytes=VMEM_BYTES)


def cost(flops, moved):
    return pl.CostEstimate(flops=flops, bytes_accessed=moved, transcendentals=0)


def whole_block(table):
    return pl.BlockSpec(table.shape, lambda i: (0,) * table.ndim)


def by_four(array):
    return array.reshape(CH // 4, 4, *array.shape[1:])


def forward_call(field, gy, pinned):
    y_local = field.shape[1]
    tables = [*halves(x_table(False)), *halves(y_table(y_local, gy, False))]
    hbm = pl.BlockSpec(memory_space=pltpu.HBM)
    return pl.pallas_call(
        forward_kernel,
        out_shape=(pltpu.HBM if pinned else jax.ShapeDtypeStruct)((CH // 2 * MY, 4 * MX), F32),
        in_specs=[hbm] * 5,
        scratch_shapes=[
            pltpu.VMEM((4, CH // 4, y_local, NX), F32),
            pltpu.VMEM((2, 2, NX, 4 * MX), BF),
            pltpu.VMEM((2, 2 * MY, y_local), BF),
            pltpu.SemaphoreType.DMA((8,)),
        ],
        compiler_params=params(),
        cost_estimate=cost(10**8, 2**18),
        name="forward_modes",
    )(*in_hbm(by_four(field), *tables))


def filter_call(arrived, gains, gz, gy, scale):
    fwd, inv = z_tables(gz, gy, gains.shape[2], scale)
    fwd, inv = halves(fwd), halves(inv)
    return pl.pallas_call(
        filter_kernel,
        out_shape=pltpu.HBM(arrived.shape, F32),
        compiler_params=params(),
        cost_estimate=cost(2 * 10**11, 2**18),
        name="filter_modes",
    )(arrived, *in_hbm(gains, *fwd, *inv))


def inverse_call(modes, bias, own, middle, second, pair, upper, y_local, gy, scale):
    tables = [*halves(x_table(True, scale)), *halves(y_table(y_local, gy, True))]
    some = lambda rows: pl.BlockSpec((CH // 4, 1, rows, NX), lambda i: (0, i, 0, 0))
    planes = [*in_hbm(*map(by_four, (own, middle, second))), *map(by_four, pair)]
    rim = own.shape[1]
    result, base = pl.pallas_call(
        functools.partial(inverse_kernel, upper),
        out_shape=[
            jax.ShapeDtypeStruct((CH // 4, 4, y_local, NX), F32),
            jax.ShapeDtypeStruct((CH // 4, 4, rim, NX), F32),
        ],
        grid=(4,),
        in_specs=[
            whole_block(modes),
            pl.BlockSpec(memory_space=pltpu.SMEM),
            *[whole_block(t) for t in tables],
            *[some(p.shape[2]) for p in planes],
        ],
        out_specs=[some(y_local), some(rim)],
        scratch_shapes=[pltpu.VMEM((2, 2, CH // 4 * y_local, 128), BF)],
        compiler_params=params(),
        cost_estimate=cost(2 * 10**11, 2**18),
        name="inverse_modes",
    )(modes, *in_hbm(bias, *tables), *planes)
    return result.reshape(CH, y_local, NX), base.reshape(CH, rim, NX)


def finish_call(result, base, low, high, upper):
    tiles = base.shape[1] // 8
    anywhere = pl.BlockSpec(memory_space=pl.ANY)
    return pl.pallas_call(
        functools.partial(finish_kernel, upper),
        out_shape=jax.ShapeDtypeStruct(result.shape, F32),
        in_specs=[anywhere] * 4,
        out_specs=anywhere,
        scratch_shapes=[
            pltpu.VMEM((3, tiles, CH, 8, NX), F32),
            pltpu.VMEM((tiles, CH, 8, NX), F32),
            pltpu.SemaphoreType.DMA((3, tiles)),
            pltpu.SemaphoreType.DMA((tiles,)),
        ],
        input_output_aliases={0: 0},
        compiler_params=params(),
        cost_estimate=cost(10**8, 2**18),
        name="finished_rows",
    )(result, base, low, high)


def pack_call(field, tiles):
    count = 8 * len(tiles) + 2
    fetched = len(tiles) + 4
    hbm = pl.BlockSpec(memory_space=pltpu.HBM)
    return pl.pallas_call(
        functools.partial(pack_kernel, tiles),
        out_shape=[pltpu.HBM((count, CH, NX), F32), pltpu.HBM((2, CH, NX), F32)],
        in_specs=[hbm],
        out_specs=[hbm] * 2,
        scratch_shapes=[
            pltpu.VMEM((fetched, 2, CH, 8, 128), F32),
            pltpu.VMEM((count, CH, NX), F32),
            pltpu.VMEM((2, CH, NX), F32),
            pltpu.SemaphoreType.DMA((fetched, 2)),
            pltpu.SemaphoreType.DMA((3,)),
        ],
        compiler_params=params(),
        cost_estimate=cost(10**8, 2**18),
        name="packed_rows",
    )(*in_hbm(field))


def own_call(field, weight, point, segments, halo=()):
    tiles = sum(map(len, segments))
    rows, fetched = 8 * tiles, tiles + 2 * len(segments)
    hbm = pl.BlockSpec(memory_space=pltpu.HBM)
    return pl.pallas_call(
        functools.partial(own_kernel, segments),
        out_shape=[pltpu.HBM((CH, rows, NX), F32)] * 3,
        in_specs=[hbm] * 3 + [pl.BlockSpec(memory_space=pl.ANY)] * len(halo),
        out_specs=[hbm] * 3,
        scratch_shapes=[
            pltpu.VMEM((fetched, 2, CH, 8, 128), F32),
            pltpu.VMEM((2, CH, NX), F32),
            pltpu.VMEM((CH, 27), F32),
            pltpu.VMEM((CH, CH), F32),
            pltpu.VMEM((3, tiles, CH, 8, NX), F32),
            pltpu.VMEM((rows + 2 * len(segments), CH, NX), F32),
            pltpu.VMEM((3, rows, CH, NX), F32),
            pltpu.VMEM((27, CH, 128), F32),
            pltpu.SemaphoreType.DMA((fetched, 2)),
            pltpu.SemaphoreType.DMA((3, tiles)),
            pltpu.SemaphoreType.DMA((3,)),
        ],
        compiler_params=params(),
        cost_estimate=cost(10**8, 2**18),
        name="own_sums",
    )(*in_hbm(weight, point, field), *halo)


def middle_call(weight, point, low, own, high):
    rows = own.shape[0] - 2
    hbm = pl.BlockSpec(memory_space=pltpu.HBM)
    return pl.pallas_call(
        middle_kernel,
        out_shape=pltpu.HBM((CH, rows, NX), F32),
        in_specs=[hbm] * 2 + [pl.BlockSpec(memory_space=pl.ANY)] * 3,
        out_specs=hbm,
        scratch_shapes=[
            pltpu.VMEM((3, rows + 2, CH, NX), F32),
            pltpu.VMEM((CH, 27), F32),
            pltpu.VMEM((CH, CH), F32),
            pltpu.VMEM((rows // 8, CH, 8, NX), F32),
            pltpu.VMEM((1, rows, CH, NX), F32),
            pltpu.VMEM((27, CH, 128), F32),
            pltpu.SemaphoreType.DMA((5,)),
            pltpu.SemaphoreType.DMA((rows // 8,)),
        ],
        compiler_params=params(),
        cost_estimate=cost(10**8, 2**18),
        name="middle_sums",
    )(*in_hbm(weight, point), low, *in_hbm(own), high)


def general_filter(coarse, gains, gz, gy, scale):
    j_own, n_own = gains.shape[2], gains.shape[3]
    both = ("gz", "gy")
    flat = coarse.reshape(CH // 2, MY, 2, 2, MX).transpose(3, 1, 0, 2, 4).reshape(2, MY, CH * MX)
    sent = flat.reshape(2, gy, j_own, gz, n_own).transpose(3, 1, 0, 2, 4).reshape(gz * gy, -1)
    got = lax.all_to_all(sent, both, split_axis=0, concat_axis=0, tiled=True)
    got = got.reshape(gz, gy, 2, j_own, n_own)
    c, s = (jnp.asarray(t, F32) for t in trig(kept(MZ, gz), np.arange(gz), gz))
    mul = functools.partial(jnp.einsum, precision=lax.Precision.HIGHEST)
    whole = got.sum(axis=1) * scale
    real = mul("zjn,qz->qjn", whole[:, 0], c) + mul("zjn,qz->qjn", whole[:, 1], s)
    imag = mul("zjn,qz->qjn", whole[:, 1], c) - mul("zjn,qz->qjn", whole[:, 0], s)
    real, imag = real * gains[0] - imag * gains[1], real * gains[1] + imag * gains[0]
    out = jnp.stack(
        [
            mul("qjn,qz->zjn", real, c) - mul("qjn,qz->zjn", imag, s),
            mul("qjn,qz->zjn", real, s) + mul("qjn,qz->zjn", imag, c),
        ],
        axis=1,
    )
    out = jnp.broadcast_to(out[:, None], (gz, gy, 2, j_own, n_own)).reshape(gz * gy, -1)
    back = lax.all_to_all(out, both, split_axis=0, concat_axis=0, tiled=True)
    back = back.reshape(gz, gy, 2, j_own, n_own).transpose(2, 1, 3, 0, 4)
    back = back.reshape(2, MY, CH // 2, 2, MX)
    return back.transpose(2, 1, 3, 0, 4).reshape(CH // 2, MY, 4 * MX)


def body(field, spectral_filter, depth_weight, point_weight, bias_vector):
    gz, gy = lax.axis_size("gz"), lax.axis_size("gy")
    y_local = field.shape[2]
    field = field.reshape(CH, y_local, NX)
    y_total = gy * y_local
    forward_scale = 1.0 / math.sqrt(float(NX) * y_total * gz)
    inverse_scale = 1.0 / math.sqrt(2.0 * MX * MY * MZ)

    def ring(axis, count, by):
        return [(i, (i + by) % count) for i in range(count)]

    def to_neighbours(down, up):
        return (
            lax.ppermute(down, "gz", ring("gz", gz, 1)),
            lax.ppermute(up, "gz", ring("gz", gz, -1)),
        )

    def after(value, *others):
        return lax.optimization_barrier((value, *others))[0]

    last = y_local // 8 - 1
    cut = 1 + last // 2
    first_tiles, second_tiles = tuple(range(1, cut)), tuple(range(cut, last))
    sums = functools.partial(own_call, weight=depth_weight, point=point_weight)
    packed, edges = pack_call(field, first_tiles)
    first_low, first_high = to_neighbours(packed, packed)
    if gy == 2:
        halo = lax.ppermute(edges, "gy", ring("gy", gy, 1))
    else:
        halo = jnp.stack(
            [
                lax.ppermute(edges[0], "gy", ring("gy", gy, 1)),
                lax.ppermute(edges[1], "gy", ring("gy", gy, -1)),
            ]
        )
    j_own, n_own = spectral_filter.shape[2], spectral_filter.shape[3]
    whole_tiles = j_own == 8 and n_own == 2 * MX
    coarse = forward_call(after(field, packed), gy, whole_tiles)
    down, second, up = sums(after(field, coarse), segments=(second_tiles,))
    if whole_tiles:
        both = ("gz", "gy")
        got = lax.all_to_all(coarse, both, split_axis=0, concat_axis=0, tiled=True)
        pair = to_neighbours(after(down, got), after(up, got))
        gains = after(spectral_filter, first_low, first_high, second)
        mark = filter_call(got, gains, gz, gy, forward_scale)
        back = lax.all_to_all(mark, both, split_axis=0, concat_axis=0, tiled=True)
        back = back.reshape(CH // 2, MY, 4 * MX)
    else:
        pair = to_neighbours(down, up)
        mark = back = general_filter(coarse, spectral_filter, gz, gy, forward_scale)
    mixed = middle_call(depth_weight, point_weight, first_low, after(packed, mark), first_high)
    down, own, up = sums(after(field, mark), segments=((0,), (last,)), halo=(halo,))
    down, up, _, _ = lax.optimization_barrier((down, up, back, mixed))
    outer_pair = to_neighbours(down, up)
    result, base = inverse_call(
        back, bias_vector, own, mixed, second, pair, 8, y_local, gy, inverse_scale
    )
    result = finish_call(result, base, *outer_pair, 1)
    return result.reshape(CH, 1, y_local, NX)


def solution(mesh):
    in_specs = (P(None, "gz", "gy", None), P(None, None, "gy", "gz"), P(), P(), P())
    out_specs = P(None, "gz", "gy", None)
    return jax.shard_map(body, mesh=mesh, in_specs=in_specs, out_specs=out_specs, check_vma=False)
```

```python
import functools
import math

import jax
import jax.numpy as jnp
import ml_dtypes
import numpy as np
from jax import lax
from jax.experimental import pallas as pl
from jax.experimental.pallas import tpu as pltpu
from jax.sharding import PartitionSpec as P

NX = 256
MX = 32
MY = 16
MZ = 16
CH = 32
VMEM_BYTES = 16 * 1024 * 1024
BF = jnp.bfloat16
F32 = jnp.float32


def kept(count, total):
    series = np.arange(count)
    return np.where(series < count // 2, series, total - count + series)


def trig(freqs, places, total):
    angle = 2.0 * np.pi * ((freqs[:, None] * places[None, :]) % total) / total
    return np.cos(angle), np.sin(angle)


def halves(table):
    table = np.asarray(table, np.float64)
    top = table.astype(np.float32).astype(ml_dtypes.bfloat16)
    rest = (table - top.astype(np.float64)).astype(np.float32).astype(ml_dtypes.bfloat16)
    return jnp.asarray(top), jnp.asarray(rest)


def y_table(y_local, gy, inverse):
    out = []
    for g in range(gy):
        places = g * y_local + np.arange(y_local)
        out.append(np.concatenate(trig(kept(MY, y_local * gy), places, y_local * gy), axis=0))
    return np.stack([t.T for t in out] if inverse else out)


def x_table(inverse, scale=1.0):
    c, s = trig(np.arange(MX), np.arange(NX), NX)
    w = np.where(np.arange(MX) == 0, 1.0, 2.0)[:, None] if inverse else 1.0
    out = np.zeros((2, 2, 2, MX, NX))
    for p in range(2):
        out[p, p, 0] = w * c * scale
        out[p, p, 1] = -w * s * scale
    out = out.reshape(2, 4 * MX, NX)
    return out if inverse else out.transpose(0, 2, 1)


def z_tables(gz, gy, rows, scale):
    c, s = trig(kept(MZ, gz), np.arange(gz), gz)
    eye = np.eye(rows)
    one = np.ones(gy)
    both = np.stack([c, s])
    fwd = np.einsum("tqz,g,jk->tqjzgk", both, one, eye) * scale
    inv = np.einsum("tqz,g,jk->tzgjqk", both, one, eye)
    return fwd.reshape(2 * MZ * rows, gz * gy * rows), inv.reshape(2 * gz * gy * rows, MZ * rows)


def parts(value):
    top = value.astype(BF)
    return top, (value - top.astype(F32)).astype(BF)


def dot(a, b):
    return jnp.dot(a, b, preferred_element_type=F32)


def dot3(a, b):
    rows = a[0].shape[0]
    both = dot(jnp.concatenate([a[0], a[1]], axis=0), b[0])
    return both[:rows] + (both[rows:] + dot(a[0], b[1]))


def swap_parts(value):
    lane = lax.broadcasted_iota(jnp.int32, value.shape, 1)
    is_real = (lane // MX) % 2 == 0
    width = value.shape[1]
    return jnp.where(is_real, pltpu.roll(value, width - MX, 1), pltpu.roll(value, MX, 1)), is_real


def forward_kernel(field, x_top, x_rest, y_top, y_rest, out, taken, x_both, y_both, sem):
    gy = lax.axis_index("gy")
    few = [
        pltpu.make_async_copy(src, dst, sem.at[4 + i])
        for i, (src, dst) in enumerate(
            ((x_top, x_both.at[0]), (x_rest, x_both.at[1]), (y_top.at[gy], y_both.at[0]), (y_rest.at[gy], y_both.at[1]))
        )
    ]
    copies = [pltpu.make_async_copy(field.at[:, q], taken.at[q], sem.at[q]) for q in range(4)]
    for copy in few + copies:
        copy.start()
    for copy in few:
        copy.wait()
    groups, rows = taken.shape[1:3]
    halves_of = []
    for q in range(4):
        copies[q].wait()
        part = dot3(parts(taken[q].reshape(groups * rows, NX)), (x_both[0, q % 2], x_both[1, q % 2]))
        if q % 2:
            halves_of[-1] = halves_of[-1] + part
        else:
            halves_of.append(part)
    total = jnp.concatenate(halves_of, axis=1)
    for g in range(groups):
        both = dot3((y_both[0], y_both[1]), parts(total[g * rows : (g + 1) * rows]))
        crossed, is_real = swap_parts(both[MY:])
        modes = both[:MY] + jnp.where(is_real, crossed, -crossed)
        out[pl.ds(2 * g * MY, MY), :] = modes[:, : 4 * MX]
        out[pl.ds((2 * g + 1) * MY, MY), :] = modes[:, 4 * MX :]


def filter_kernel(arrived, gains, f_top, f_rest, i_top, i_rest, out):
    real, imag = (gains[r].reshape(-1, 2 * MX) for r in range(2))
    first, second = slice(0, MX), slice(MX, 2 * MX)
    same = jnp.concatenate([real[:, first], real[:, first], real[:, second], real[:, second]], axis=1)
    cross = jnp.concatenate([-imag[:, first], imag[:, first], -imag[:, second], imag[:, second]], axis=1)
    half = f_top.shape[0] // 2
    turned = dot3((f_top[...], f_rest[...]), parts(arrived[...]))
    crossed, is_real = swap_parts(turned[half:])
    modes = turned[:half] + jnp.where(is_real, crossed, -crossed)
    crossed, _ = swap_parts(modes)
    filtered = modes * same + crossed * cross
    half = i_top.shape[0] // 2
    back = dot3((i_top[...], i_rest[...]), parts(filtered))
    crossed, is_real = swap_parts(back[half:])
    out[...] = back[:half] + jnp.where(is_real, -crossed, crossed)


def fetch_tiles(field, taken, sems, wanted):
    pending = {}
    for k, t in enumerate(wanted):
        pending[t] = [
            pltpu.make_async_copy(
                field.at[:, pl.ds(8 * t, 8), pl.ds(128 * h, 128)], taken.at[k, h], sems.at[k, h]
            )
            for h in range(2)
        ]
        for copy in pending[t]:
            copy.start()

    def row(t, r):
        for copy in pending.pop(t, ()):
            copy.wait()
        k = wanted.index(t)
        return jnp.concatenate(
            [taken.at[k, h].reshape(CH * 8, 128)[pl.ds(r, CH, stride=8), :] for h in range(2)], axis=1
        )

    return row


def spread_gains(weights, gains, offsets):
    for k in [9 * a + j for a in offsets for j in range(9)]:
        gains[k] = jnp.broadcast_to(weights[:, k : k + 1], (CH, 128))


def mixing(points):
    down = (
        lax.broadcasted_iota(jnp.int32, (8 * CH, CH), 0) // 8
        == lax.broadcasted_iota(jnp.int32, (8 * CH, CH), 1)
    ).astype(BF)
    across = (
        lax.broadcasted_iota(jnp.int32, (CH, 8 * CH), 1) % CH
        == lax.broadcasted_iota(jnp.int32, (CH, 8 * CH), 0)
    ).astype(BF)
    same = (
        lax.broadcasted_iota(jnp.int32, (8 * CH, 8 * CH), 0) % 8
        == lax.broadcasted_iota(jnp.int32, (8 * CH, 8 * CH), 1) // CH
    )
    return tuple(
        jnp.where(same, dot(dot(down, part).astype(BF), across), 0.0).astype(BF)
        for part in parts(points)
    )


def tap_sums(load, uses, gains, depth, runs):
    def some(i, _):
        chans = pl.ds(pl.multiple_of(i * 8, 8), 8)
        wanted = sorted({a for use in uses for a, _ in use})
        gain = {k: gains[k, chans, :] for a in wanted for k in range(9 * a, 9 * a + 9)}
        for first, to, rows in runs:
            sums = {}
            for r in range(rows + 2):
                for s, use in enumerate(uses):
                    value = load(s, first + r, chans)
                    turned = (pltpu.roll(value, 1, 1), value, pltpu.roll(value, NX - 1, 1))
                    for b in range(3):
                        o = r - b
                        if o < 0 or o >= rows:
                            continue
                        for a, k in use:
                            for e in range(3):
                                for h in range(2):
                                    term = gain[a * 9 + b * 3 + e] * turned[e][:, 128 * h : 128 * h + 128]
                                    place = (o, k, h)
                                    sums[place] = sums[place] + term if place in sums else term
                if r >= 2:
                    for k in sorted({k for use in uses for _, k in use}):
                        for h in range(2):
                            depth[k, to + r - 2, chans, pl.ds(128 * h, 128)] = sums.pop((r - 2, k, h))
        return 0

    lax.fori_loop(0, CH // 8, some, 0)


def mix_tile(mix, depth, k, t):
    tile = depth[k, pl.ds(8 * t, 8)].reshape(8 * CH, NX)
    return dot3(mix, parts(tile)).reshape(CH, 8, NX)


def pack_kernel(tiles, field, packed, edges, taken, rows, ends, sem_in, sem_out):
    last = field.shape[1] // 8 - 1
    before, after = tiles[0] - 1, tiles[-1] + 1
    wanted = [before, *tiles, after] + [t for t in (0, last) if t not in (before, after)]
    row = fetch_tiles(field, taken, sem_in, wanted)
    places = [(before, 7), *[(t, r) for t in tiles for r in range(8)], (after, 0)]
    copies, cuts = [], (0, len(places) // 2, len(places))
    for k in range(2):
        for i in range(cuts[k], cuts[k + 1]):
            rows[i] = row(*places[i])
        some = pl.ds(cuts[k], cuts[k + 1] - cuts[k])
        copies.append(pltpu.make_async_copy(rows.at[some], packed.at[some], sem_out.at[k]))
        copies[-1].start()
    ends[0] = row(last, 7)
    ends[1] = row(0, 0)
    copies.append(pltpu.make_async_copy(ends, edges, sem_out.at[2]))
    copies[-1].start()
    for copy in copies:
        copy.wait()


def own_kernel(segments, weight, point, field, *refs):
    last = field.shape[1] // 8 - 1
    outer = segments[0][0] == 0
    few = [(weight, refs[-9]), (point, refs[-8])]
    if outer:
        few.append((refs[0], refs[-10]))
        refs = refs[1:]
    outs, (taken, halo_rows, weights, points, sent, lined, depth, gains, sem_in, sem_out, sem_few) = (
        refs[:3],
        refs[3:],
    )
    few = [pltpu.make_async_copy(src, dst, sem_few.at[i]) for i, (src, dst) in enumerate(few)]
    wanted = sorted({t for tiles in segments for t in (tiles[0] - 1, *tiles, tiles[-1] + 1) if 0 <= t <= last})
    row = fetch_tiles(field, taken, sem_in, wanted)
    for copy in few:
        copy.start()
    for copy in few:
        copy.wait()
    spread_gains(weights, gains, range(3))
    mix = mixing(points[...])
    runs, at, done = [], 0, 0
    for tiles in segments:
        places = [(tiles[0] - 1, 7), *[(t, r) for t in tiles for r in range(8)], (tiles[-1] + 1, 0)]
        for i, (t, r) in enumerate(places):
            lined[at + i] = halo_rows[0] if t < 0 else halo_rows[1] if t > last else row(t, r)
        runs.append((at, done, 8 * len(tiles)))
        at, done = at + len(places), done + 8 * len(tiles)
    tap_sums(lambda s, r, c: lined[r, c, :], [[(a, a) for a in range(3)]], gains, depth, runs)
    copies = []
    for t in range(done // 8):
        for k, out in enumerate(outs):
            sent[k, t] = mix_tile(mix, depth, k, t)
            copies.append(
                pltpu.make_async_copy(sent.at[k, t], out.at[:, pl.ds(8 * t, 8), :], sem_out.at[k, t])
            )
            copies[-1].start()
    for copy in copies:
        copy.wait()


def middle_kernel(weight, point, low, own, high, out, taken, weights, points, sent, depth, gains, sem_in, sem_out):
    copies = [
        pltpu.make_async_copy(src, dst, sem_in.at[i])
        for i, (src, dst) in enumerate(
            ((weight, weights), (point, points), (low, taken.at[0]), (own, taken.at[1]), (high, taken.at[2]))
        )
    ]
    for copy in copies:
        copy.start()
    for copy in copies[:2]:
        copy.wait()
    spread_gains(weights, gains, range(3))
    mix = mixing(points[...])
    for copy in copies[2:]:
        copy.wait()
    rows = out.shape[1]
    tap_sums(lambda s, r, c: taken[s, r, c, :], [[(a, 0)] for a in range(3)], gains, depth, [(0, 0, rows)])
    copies = []
    for t in range(rows // 8):
        sent[t] = mix_tile(mix, depth, 0, t)
        copies.append(pltpu.make_async_copy(sent.at[t], out.at[:, pl.ds(8 * t, 8), :], sem_out.at[t]))
        copies[-1].start()
    for copy in copies:
        copy.wait()


def gelu(value):
    size = jnp.abs(value) * math.sqrt(0.5)
    below = 1.0 + 0.3275911 * size
    t = pl.reciprocal(below, approx=True)
    t = t * (2.0 - below * t)
    series = 1.061405429 * t - 1.453152027
    for factor in (1.421413741, -0.284496736, 0.254829592):
        series = series * t + factor
    tail = 0.5 * (series * t) * jnp.exp(-(size * size))
    return value * jnp.where(value < 0.0, tail, 1.0 - tail)


def inverse_kernel(upper, modes, bias, x_top, x_rest, y_top, y_rest, own, middle, second, low, high, out, base, columns):
    q = pl.program_id(0)
    groups, _, y_local, _ = out.shape

    @pl.when(q == 0)
    def _():
        gy = lax.axis_index("gy")
        for g in range(groups):
            own_modes = jnp.concatenate([modes[2 * g], modes[2 * g + 1]], axis=1)
            crossed, is_real = swap_parts(own_modes)
            stack = jnp.concatenate([own_modes, jnp.where(is_real, -crossed, crossed)], axis=0)
            pair = parts(dot3((y_top[gy], y_rest[gy]), parts(stack)))
            for h in range(2):
                for k in range(2):
                    columns[h, k, pl.ds(g * y_local, y_local), :] = pair[k][:, 128 * h : 128 * h + 128]

    h, p = q // 2, q % 2
    rows = dot3((columns[h, 0], columns[h, 1]), (x_top[p], x_rest[p]))
    turn = upper + middle.shape[2]
    stop = turn + second.shape[2]
    for g in range(groups):
        plane = rows[g * y_local : (g + 1) * y_local] + bias[4 * g + q]
        base[g, 0, :upper] = plane[:upper] + own[g, 0, :upper]
        out[g, 0, upper:turn] = gelu(plane[upper:turn] + middle[g, 0])
        out[g, 0, turn:stop] = gelu(plane[turn:stop] + (second[g, 0] + (low[g, 0] + high[g, 0])))
        base[g, 0, upper:] = plane[stop:] + own[g, 0, upper:]


def finish_kernel(upper, _, base, low, high, out, sent, sem):
    tiles = base.shape[1] // 8
    gap = out.shape[1] // 8 - tiles
    copies = []
    for t in range(tiles):
        rows = pl.ds(8 * t, 8)
        sent[t] = gelu(base[:, rows, :] + (low[:, rows, :] + high[:, rows, :]))
        to = t if t < upper else t + gap
        copies.append(pltpu.make_async_copy(sent.at[t], out.at[:, pl.ds(8 * to, 8), :], sem.at[t]))
        copies[-1].start()
    for copy in copies:
        copy.wait()


def in_hbm(*arrays):
    return [pltpu.with_memory_space_constraint(a, pltpu.HBM) for a in arrays]


def params():
    return pltpu.CompilerParams(vmem_limit_bytes=VMEM_BYTES)


def cost(flops, moved):
    return pl.CostEstimate(flops=flops, bytes_accessed=moved, transcendentals=0)


def whole_block(table):
    return pl.BlockSpec(table.shape, lambda i: (0,) * table.ndim)


def by_four(array):
    return array.reshape(CH // 4, 4, *array.shape[1:])


def forward_call(field, gy, pinned):
    y_local = field.shape[1]
    tables = [*halves(x_table(False)), *halves(y_table(y_local, gy, False))]
    hbm = pl.BlockSpec(memory_space=pltpu.HBM)
    return pl.pallas_call(
        forward_kernel,
        out_shape=(pltpu.HBM if pinned else jax.ShapeDtypeStruct)((CH // 2 * MY, 4 * MX), F32),
        in_specs=[hbm] * 5,
        scratch_shapes=[
            pltpu.VMEM((4, CH // 4, y_local, NX), F32),
            pltpu.VMEM((2, 2, NX, 4 * MX), BF),
            pltpu.VMEM((2, 2 * MY, y_local), BF),
            pltpu.SemaphoreType.DMA((8,)),
        ],
        compiler_params=params(),
        cost_estimate=cost(10**8, 2**18),
        name="forward_modes",
    )(*in_hbm(by_four(field), *tables))


def filter_call(arrived, gains, gz, gy, scale):
    fwd, inv = z_tables(gz, gy, gains.shape[2], scale)
    fwd, inv = halves(fwd), halves(inv)
    return pl.pallas_call(
        filter_kernel,
        out_shape=pltpu.HBM(arrived.shape, F32),
        compiler_params=params(),
        cost_estimate=cost(2 * 10**11, 2**18),
        name="filter_modes",
    )(arrived, *in_hbm(gains, *fwd, *inv))


def inverse_call(modes, bias, own, middle, second, pair, upper, y_local, gy, scale):
    tables = [*halves(x_table(True, scale)), *halves(y_table(y_local, gy, True))]
    some = lambda rows: pl.BlockSpec((CH // 4, 1, rows, NX), lambda i: (0, i, 0, 0))
    planes = [*in_hbm(*map(by_four, (own, middle, second))), *map(by_four, pair)]
    rim = own.shape[1]
    result, base = pl.pallas_call(
        functools.partial(inverse_kernel, upper),
        out_shape=[
            jax.ShapeDtypeStruct((CH // 4, 4, y_local, NX), F32),
            jax.ShapeDtypeStruct((CH // 4, 4, rim, NX), F32),
        ],
        grid=(4,),
        in_specs=[
            whole_block(modes),
            pl.BlockSpec(memory_space=pltpu.SMEM),
            *[whole_block(t) for t in tables],
            *[some(p.shape[2]) for p in planes],
        ],
        out_specs=[some(y_local), some(rim)],
        scratch_shapes=[pltpu.VMEM((2, 2, CH // 4 * y_local, 128), BF)],
        compiler_params=params(),
        cost_estimate=cost(10**8, 2**18),
        name="inverse_modes",
    )(modes, *in_hbm(bias, *tables), *planes)
    return result.reshape(CH, y_local, NX), base.reshape(CH, rim, NX)


def finish_call(result, base, low, high, upper):
    tiles = base.shape[1] // 8
    anywhere = pl.BlockSpec(memory_space=pl.ANY)
    vmem = pl.BlockSpec(memory_space=pltpu.VMEM)
    operands = [pltpu.with_memory_space_constraint(a, pltpu.VMEM) for a in (base, low, high)]
    return pl.pallas_call(
        functools.partial(finish_kernel, upper),
        out_shape=jax.ShapeDtypeStruct(result.shape, F32),
        in_specs=[anywhere] + [vmem] * 3,
        out_specs=anywhere,
        scratch_shapes=[
            pltpu.VMEM((tiles, CH, 8, NX), F32),
            pltpu.SemaphoreType.DMA((tiles,)),
        ],
        input_output_aliases={0: 0},
        compiler_params=params(),
        cost_estimate=cost(10**8, 2**18),
        name="finished_rows",
    )(result, *operands)


def pack_call(field, tiles):
    count = 8 * len(tiles) + 2
    fetched = len(tiles) + 4
    hbm = pl.BlockSpec(memory_space=pltpu.HBM)
    return pl.pallas_call(
        functools.partial(pack_kernel, tiles),
        out_shape=[pltpu.HBM((count, CH, NX), F32), pltpu.HBM((2, CH, NX), F32)],
        in_specs=[hbm],
        out_specs=[hbm] * 2,
        scratch_shapes=[
            pltpu.VMEM((fetched, 2, CH, 8, 128), F32),
            pltpu.VMEM((count, CH, NX), F32),
            pltpu.VMEM((2, CH, NX), F32),
            pltpu.SemaphoreType.DMA((fetched, 2)),
            pltpu.SemaphoreType.DMA((3,)),
        ],
        compiler_params=params(),
        cost_estimate=cost(10**8, 2**18),
        name="packed_rows",
    )(*in_hbm(field))


def own_call(field, weight, point, segments, halo=()):
    tiles = sum(map(len, segments))
    rows, fetched = 8 * tiles, tiles + 2 * len(segments)
    hbm = pl.BlockSpec(memory_space=pltpu.HBM)
    return pl.pallas_call(
        functools.partial(own_kernel, segments),
        out_shape=[pltpu.HBM((CH, rows, NX), F32)] * 3,
        in_specs=[hbm] * 3 + [pl.BlockSpec(memory_space=pl.ANY)] * len(halo),
        out_specs=[hbm] * 3,
        scratch_shapes=[
            pltpu.VMEM((fetched, 2, CH, 8, 128), F32),
            pltpu.VMEM((2, CH, NX), F32),
            pltpu.VMEM((CH, 27), F32),
            pltpu.VMEM((CH, CH), F32),
            pltpu.VMEM((3, tiles, CH, 8, NX), F32),
            pltpu.VMEM((rows + 2 * len(segments), CH, NX), F32),
            pltpu.VMEM((3, rows, CH, NX), F32),
            pltpu.VMEM((27, CH, 128), F32),
            pltpu.SemaphoreType.DMA((fetched, 2)),
            pltpu.SemaphoreType.DMA((3, tiles)),
            pltpu.SemaphoreType.DMA((3,)),
        ],
        compiler_params=params(),
        cost_estimate=cost(10**8, 2**18),
        name="own_sums",
    )(*in_hbm(weight, point, field), *halo)


def middle_call(weight, point, low, own, high):
    rows = own.shape[0] - 2
    hbm = pl.BlockSpec(memory_space=pltpu.HBM)
    return pl.pallas_call(
        middle_kernel,
        out_shape=pltpu.HBM((CH, rows, NX), F32),
        in_specs=[hbm] * 2 + [pl.BlockSpec(memory_space=pl.ANY)] * 3,
        out_specs=hbm,
        scratch_shapes=[
            pltpu.VMEM((3, rows + 2, CH, NX), F32),
            pltpu.VMEM((CH, 27), F32),
            pltpu.VMEM((CH, CH), F32),
            pltpu.VMEM((rows // 8, CH, 8, NX), F32),
            pltpu.VMEM((1, rows, CH, NX), F32),
            pltpu.VMEM((27, CH, 128), F32),
            pltpu.SemaphoreType.DMA((5,)),
            pltpu.SemaphoreType.DMA((rows // 8,)),
        ],
        compiler_params=params(),
        cost_estimate=cost(2 * 10**11, 2**18),
        name="middle_sums",
    )(*in_hbm(weight, point), low, *in_hbm(own), high)


def general_filter(coarse, gains, gz, gy, scale):
    j_own, n_own = gains.shape[2], gains.shape[3]
    both = ("gz", "gy")
    flat = coarse.reshape(CH // 2, MY, 2, 2, MX).transpose(3, 1, 0, 2, 4).reshape(2, MY, CH * MX)
    sent = flat.reshape(2, gy, j_own, gz, n_own).transpose(3, 1, 0, 2, 4).reshape(gz * gy, -1)
    got = lax.all_to_all(sent, both, split_axis=0, concat_axis=0, tiled=True)
    got = got.reshape(gz, gy, 2, j_own, n_own)
    c, s = (jnp.asarray(t, F32) for t in trig(kept(MZ, gz), np.arange(gz), gz))
    mul = functools.partial(jnp.einsum, precision=lax.Precision.HIGHEST)
    whole = got.sum(axis=1) * scale
    real = mul("zjn,qz->qjn", whole[:, 0], c) + mul("zjn,qz->qjn", whole[:, 1], s)
    imag = mul("zjn,qz->qjn", whole[:, 1], c) - mul("zjn,qz->qjn", whole[:, 0], s)
    real, imag = real * gains[0] - imag * gains[1], real * gains[1] + imag * gains[0]
    out = jnp.stack(
        [
            mul("qjn,qz->zjn", real, c) - mul("qjn,qz->zjn", imag, s),
            mul("qjn,qz->zjn", real, s) + mul("qjn,qz->zjn", imag, c),
        ],
        axis=1,
    )
    out = jnp.broadcast_to(out[:, None], (gz, gy, 2, j_own, n_own)).reshape(gz * gy, -1)
    back = lax.all_to_all(out, both, split_axis=0, concat_axis=0, tiled=True)
    back = back.reshape(gz, gy, 2, j_own, n_own).transpose(2, 1, 3, 0, 4)
    back = back.reshape(2, MY, CH // 2, 2, MX)
    return back.transpose(2, 1, 3, 0, 4).reshape(CH // 2, MY, 4 * MX)


def body(field, spectral_filter, depth_weight, point_weight, bias_vector):
    gz, gy = lax.axis_size("gz"), lax.axis_size("gy")
    y_local = field.shape[2]
    field = field.reshape(CH, y_local, NX)
    y_total = gy * y_local
    forward_scale = 1.0 / math.sqrt(float(NX) * y_total * gz)
    inverse_scale = 1.0 / math.sqrt(2.0 * MX * MY * MZ)

    def ring(axis, count, by):
        return [(i, (i + by) % count) for i in range(count)]

    def to_neighbours(down, up):
        return (
            lax.ppermute(down, "gz", ring("gz", gz, 1)),
            lax.ppermute(up, "gz", ring("gz", gz, -1)),
        )

    def after(value, *others):
        return lax.optimization_barrier((value, *others))[0]

    last = y_local // 8 - 1
    cut = 1 + last // 2
    first_tiles, second_tiles = tuple(range(1, cut)), tuple(range(cut, last))
    sums = functools.partial(own_call, weight=depth_weight, point=point_weight)
    packed, edges = pack_call(field, first_tiles)
    first_low, first_high = to_neighbours(packed, packed)
    if gy == 2:
        halo = lax.ppermute(edges, "gy", ring("gy", gy, 1))
    else:
        halo = jnp.stack(
            [
                lax.ppermute(edges[0], "gy", ring("gy", gy, 1)),
                lax.ppermute(edges[1], "gy", ring("gy", gy, -1)),
            ]
        )
    j_own, n_own = spectral_filter.shape[2], spectral_filter.shape[3]
    whole_tiles = j_own == 8 and n_own == 2 * MX
    coarse = forward_call(after(field, packed), gy, whole_tiles)
    down, second, up = sums(after(field, coarse), segments=(second_tiles,))
    if whole_tiles:
        both = ("gz", "gy")
        got = lax.all_to_all(coarse, both, split_axis=0, concat_axis=0, tiled=True)
        pair = to_neighbours(after(down, got), after(up, got))
        gains = after(spectral_filter, first_low, first_high, second, halo)
        mark = filter_call(got, gains, gz, gy, forward_scale)
        back = lax.all_to_all(mark, both, split_axis=0, concat_axis=0, tiled=True)
        back = back.reshape(CH // 2, MY, 4 * MX)
    else:
        pair = to_neighbours(down, up)
        mark = back = general_filter(coarse, spectral_filter, gz, gy, forward_scale)
    down, own, up = sums(after(field, mark), segments=((0,), (last,)), halo=(halo,))
    down, up, packed, _ = lax.optimization_barrier((down, up, packed, back))
    outer_pair = to_neighbours(down, up)
    mixed = middle_call(depth_weight, point_weight, first_low, packed, first_high)
    result, base = inverse_call(
        back, bias_vector, own, mixed, second, pair, 8, y_local, gy, inverse_scale
    )
    result = finish_call(result, base, *outer_pair, 1)
    return result.reshape(CH, 1, y_local, NX)


def solution(mesh):
    in_specs = (P(None, "gz", "gy", None), P(None, None, "gy", "gz"), P(), P(), P())
    out_specs = P(None, "gz", "gy", None)
    return jax.shard_map(body, mesh=mesh, in_specs=in_specs, out_specs=out_specs, check_vma=False)
```

```python
import functools
import math

import jax
import jax.numpy as jnp
import ml_dtypes
import numpy as np
from jax import lax
from jax.experimental import pallas as pl
from jax.experimental.pallas import tpu as pltpu
from jax.sharding import PartitionSpec as P

NX = 256
MX = 32
MY = 16
MZ = 16
CH = 32
VMEM_BYTES = 16 * 1024 * 1024
BF = jnp.bfloat16
F32 = jnp.float32


def kept(count, total):
    series = np.arange(count)
    return np.where(series < count // 2, series, total - count + series)


def trig(freqs, places, total):
    angle = 2.0 * np.pi * ((freqs[:, None] * places[None, :]) % total) / total
    return np.cos(angle), np.sin(angle)


def halves(table):
    table = np.asarray(table, np.float64)
    top = table.astype(np.float32).astype(ml_dtypes.bfloat16)
    rest = (table - top.astype(np.float64)).astype(np.float32).astype(ml_dtypes.bfloat16)
    return jnp.asarray(top), jnp.asarray(rest)


def y_table(y_local, gy, inverse):
    out = []
    for g in range(gy):
        places = g * y_local + np.arange(y_local)
        out.append(np.concatenate(trig(kept(MY, y_local * gy), places, y_local * gy), axis=0))
    return np.stack([t.T for t in out] if inverse else out)


def x_table(inverse, scale=1.0):
    c, s = trig(np.arange(MX), np.arange(NX), NX)
    w = np.where(np.arange(MX) == 0, 1.0, 2.0)[:, None] if inverse else 1.0
    out = np.zeros((2, 2, 2, MX, NX))
    for p in range(2):
        out[p, p, 0] = w * c * scale
        out[p, p, 1] = -w * s * scale
    out = out.reshape(2, 4 * MX, NX)
    return out if inverse else out.transpose(0, 2, 1)


def z_tables(gz, gy, rows, scale):
    c, s = trig(kept(MZ, gz), np.arange(gz), gz)
    eye = np.eye(rows)
    one = np.ones(gy)
    both = np.stack([c, s])
    fwd = np.einsum("tqz,g,jk->tqjzgk", both, one, eye) * scale
    inv = np.einsum("tqz,g,jk->tzgjqk", both, one, eye)
    return fwd.reshape(2 * MZ * rows, gz * gy * rows), inv.reshape(2 * gz * gy * rows, MZ * rows)


def parts(value):
    top = value.astype(BF)
    return top, (value - top.astype(F32)).astype(BF)


def dot(a, b):
    return jnp.dot(a, b, preferred_element_type=F32)


def dot3(a, b):
    rows = a[0].shape[0]
    both = dot(jnp.concatenate([a[0], a[1]], axis=0), b[0])
    return both[:rows] + (both[rows:] + dot(a[0], b[1]))


def swap_parts(value):
    lane = lax.broadcasted_iota(jnp.int32, value.shape, 1)
    is_real = (lane // MX) % 2 == 0
    width = value.shape[1]
    return jnp.where(is_real, pltpu.roll(value, width - MX, 1), pltpu.roll(value, MX, 1)), is_real


def forward_kernel(field, x_top, x_rest, y_top, y_rest, out, taken, x_both, y_both, sem):
    gy = lax.axis_index("gy")
    few = [
        pltpu.make_async_copy(src, dst, sem.at[4 + i])
        for i, (src, dst) in enumerate(
            ((x_top, x_both.at[0]), (x_rest, x_both.at[1]), (y_top.at[gy], y_both.at[0]), (y_rest.at[gy], y_both.at[1]))
        )
    ]
    copies = [pltpu.make_async_copy(field.at[:, q], taken.at[q], sem.at[q]) for q in range(4)]
    for copy in few + copies:
        copy.start()
    for copy in few:
        copy.wait()
    groups, rows = taken.shape[1:3]
    halves_of = []
    for q in range(4):
        copies[q].wait()
        part = dot3(parts(taken[q].reshape(groups * rows, NX)), (x_both[0, q % 2], x_both[1, q % 2]))
        if q % 2:
            halves_of[-1] = halves_of[-1] + part
        else:
            halves_of.append(part)
    total = jnp.concatenate(halves_of, axis=1)
    for g in range(groups):
        both = dot3((y_both[0], y_both[1]), parts(total[g * rows : (g + 1) * rows]))
        crossed, is_real = swap_parts(both[MY:])
        modes = both[:MY] + jnp.where(is_real, crossed, -crossed)
        out[pl.ds(2 * g * MY, MY), :] = modes[:, : 4 * MX]
        out[pl.ds((2 * g + 1) * MY, MY), :] = modes[:, 4 * MX :]


def filter_kernel(arrived, gains, f_top, f_rest, i_top, i_rest, out):
    real, imag = (gains[r].reshape(-1, 2 * MX) for r in range(2))
    first, second = slice(0, MX), slice(MX, 2 * MX)
    same = jnp.concatenate([real[:, first], real[:, first], real[:, second], real[:, second]], axis=1)
    cross = jnp.concatenate([-imag[:, first], imag[:, first], -imag[:, second], imag[:, second]], axis=1)
    half = f_top.shape[0] // 2
    turned = dot3((f_top[...], f_rest[...]), parts(arrived[...]))
    crossed, is_real = swap_parts(turned[half:])
    modes = turned[:half] + jnp.where(is_real, crossed, -crossed)
    crossed, _ = swap_parts(modes)
    filtered = modes * same + crossed * cross
    half = i_top.shape[0] // 2
    back = dot3((i_top[...], i_rest[...]), parts(filtered))
    crossed, is_real = swap_parts(back[half:])
    out[...] = back[:half] + jnp.where(is_real, -crossed, crossed)


def fetch_tiles(field, taken, sems, wanted):
    pending = {}
    for k, t in enumerate(wanted):
        pending[t] = [
            pltpu.make_async_copy(
                field.at[:, pl.ds(8 * t, 8), pl.ds(128 * h, 128)], taken.at[k, h], sems.at[k, h]
            )
            for h in range(2)
        ]
        for copy in pending[t]:
            copy.start()

    def row(t, r):
        for copy in pending.pop(t, ()):
            copy.wait()
        k = wanted.index(t)
        return jnp.concatenate(
            [taken.at[k, h].reshape(CH * 8, 128)[pl.ds(r, CH, stride=8), :] for h in range(2)], axis=1
        )

    return row


def spread_gains(weights, gains, offsets):
    for k in [9 * a + j for a in offsets for j in range(9)]:
        gains[k] = jnp.broadcast_to(weights[:, k : k + 1], (CH, 128))


def mixing(points):
    down = (
        lax.broadcasted_iota(jnp.int32, (8 * CH, CH), 0) // 8
        == lax.broadcasted_iota(jnp.int32, (8 * CH, CH), 1)
    ).astype(BF)
    across = (
        lax.broadcasted_iota(jnp.int32, (CH, 8 * CH), 1) % CH
        == lax.broadcasted_iota(jnp.int32, (CH, 8 * CH), 0)
    ).astype(BF)
    same = (
        lax.broadcasted_iota(jnp.int32, (8 * CH, 8 * CH), 0) % 8
        == lax.broadcasted_iota(jnp.int32, (8 * CH, 8 * CH), 1) // CH
    )
    return tuple(
        jnp.where(same, dot(dot(down, part).astype(BF), across), 0.0).astype(BF)
        for part in parts(points)
    )


def tap_sums(load, uses, gains, depth, runs):
    def some(i, _):
        chans = pl.ds(pl.multiple_of(i * 8, 8), 8)
        wanted = sorted({a for use in uses for a, _ in use})
        gain = {k: gains[k, chans, :] for a in wanted for k in range(9 * a, 9 * a + 9)}
        for first, to, rows in runs:
            sums = {}
            for r in range(rows + 2):
                for s, use in enumerate(uses):
                    value = load(s, first + r, chans)
                    turned = (pltpu.roll(value, 1, 1), value, pltpu.roll(value, NX - 1, 1))
                    for b in range(3):
                        o = r - b
                        if o < 0 or o >= rows:
                            continue
                        for a, k in use:
                            for e in range(3):
                                for h in range(2):
                                    term = gain[a * 9 + b * 3 + e] * turned[e][:, 128 * h : 128 * h + 128]
                                    place = (o, k, h)
                                    sums[place] = sums[place] + term if place in sums else term
                if r >= 2:
                    for k in sorted({k for use in uses for _, k in use}):
                        for h in range(2):
                            depth[k, to + r - 2, chans, pl.ds(128 * h, 128)] = sums.pop((r - 2, k, h))
        return 0

    lax.fori_loop(0, CH // 8, some, 0)


def mix_tile(mix, depth, k, t):
    tile = depth[k, pl.ds(8 * t, 8)].reshape(8 * CH, NX)
    return dot3(mix, parts(tile)).reshape(CH, 8, NX)


def pack_kernel(tiles, field, packed, edges, taken, rows, ends, sem_in, sem_out):
    last = field.shape[1] // 8 - 1
    before, after = tiles[0] - 1, tiles[-1] + 1
    wanted = [before, *tiles, after] + [t for t in (0, last) if t not in (before, after)]
    row = fetch_tiles(field, taken, sem_in, wanted)
    places = [(before, 7), *[(t, r) for t in tiles for r in range(8)], (after, 0)]
    copies, cuts = [], (0, len(places) // 2, len(places))
    for k in range(2):
        for i in range(cuts[k], cuts[k + 1]):
            rows[i] = row(*places[i])
        some = pl.ds(cuts[k], cuts[k + 1] - cuts[k])
        copies.append(pltpu.make_async_copy(rows.at[some], packed.at[some], sem_out.at[k]))
        copies[-1].start()
    ends[0] = row(last, 7)
    ends[1] = row(0, 0)
    copies.append(pltpu.make_async_copy(ends, edges, sem_out.at[2]))
    copies[-1].start()
    for copy in copies:
        copy.wait()


def own_kernel(segments, weight, point, field, *refs):
    last = field.shape[1] // 8 - 1
    outer = segments[0][0] == 0
    few = [(weight, refs[-9]), (point, refs[-8])]
    if outer:
        few.append((refs[0], refs[-10]))
        refs = refs[1:]
    outs, (taken, halo_rows, weights, points, sent, lined, depth, gains, sem_in, sem_out, sem_few) = (
        refs[:3],
        refs[3:],
    )
    few = [pltpu.make_async_copy(src, dst, sem_few.at[i]) for i, (src, dst) in enumerate(few)]
    wanted = sorted({t for tiles in segments for t in (tiles[0] - 1, *tiles, tiles[-1] + 1) if 0 <= t <= last})
    row = fetch_tiles(field, taken, sem_in, wanted)
    for copy in few:
        copy.start()
    for copy in few:
        copy.wait()
    spread_gains(weights, gains, range(3))
    mix = mixing(points[...])
    runs, at, done = [], 0, 0
    for tiles in segments:
        places = [(tiles[0] - 1, 7), *[(t, r) for t in tiles for r in range(8)], (tiles[-1] + 1, 0)]
        for i, (t, r) in enumerate(places):
            lined[at + i] = halo_rows[0] if t < 0 else halo_rows[1] if t > last else row(t, r)
        runs.append((at, done, 8 * len(tiles)))
        at, done = at + len(places), done + 8 * len(tiles)
    tap_sums(lambda s, r, c: lined[r, c, :], [[(a, a) for a in range(3)]], gains, depth, runs)
    copies = []
    for t in range(done // 8):
        for k, out in enumerate(outs):
            sent[k, t] = mix_tile(mix, depth, k, t)
            copies.append(
                pltpu.make_async_copy(sent.at[k, t], out.at[:, pl.ds(8 * t, 8), :], sem_out.at[k, t])
            )
            copies[-1].start()
    for copy in copies:
        copy.wait()


def middle_kernel(weight, point, low, own, high, out, taken, weights, points, sent, depth, gains, sem_in, sem_out):
    copies = [
        pltpu.make_async_copy(src, dst, sem_in.at[i])
        for i, (src, dst) in enumerate(
            ((weight, weights), (point, points), (low, taken.at[0]), (own, taken.at[1]), (high, taken.at[2]))
        )
    ]
    for copy in copies:
        copy.start()
    for copy in copies[:2]:
        copy.wait()
    spread_gains(weights, gains, range(3))
    mix = mixing(points[...])
    for copy in copies[2:]:
        copy.wait()
    rows = out.shape[1]
    tap_sums(lambda s, r, c: taken[s, r, c, :], [[(a, 0)] for a in range(3)], gains, depth, [(0, 0, rows)])
    copies = []
    for t in range(rows // 8):
        sent[t] = mix_tile(mix, depth, 0, t)
        copies.append(pltpu.make_async_copy(sent.at[t], out.at[:, pl.ds(8 * t, 8), :], sem_out.at[t]))
        copies[-1].start()
    for copy in copies:
        copy.wait()


def gelu(value):
    size = jnp.abs(value) * math.sqrt(0.5)
    below = 1.0 + 0.3275911 * size
    t = pl.reciprocal(below, approx=True)
    t = t * (2.0 - below * t)
    series = 1.061405429 * t - 1.453152027
    for factor in (1.421413741, -0.284496736, 0.254829592):
        series = series * t + factor
    tail = 0.5 * (series * t) * jnp.exp(-(size * size))
    return value * jnp.where(value < 0.0, tail, 1.0 - tail)


def inverse_kernel(upper, modes, bias, x_top, x_rest, y_top, y_rest, own, middle, second, low, high, out, base, columns):
    q = pl.program_id(0)
    groups, _, y_local, _ = out.shape

    @pl.when(q == 0)
    def _():
        gy = lax.axis_index("gy")
        for g in range(groups):
            own_modes = jnp.concatenate([modes[2 * g], modes[2 * g + 1]], axis=1)
            crossed, is_real = swap_parts(own_modes)
            stack = jnp.concatenate([own_modes, jnp.where(is_real, -crossed, crossed)], axis=0)
            pair = parts(dot3((y_top[gy], y_rest[gy]), parts(stack)))
            for h in range(2):
                for k in range(2):
                    columns[h, k, pl.ds(g * y_local, y_local), :] = pair[k][:, 128 * h : 128 * h + 128]

    h, p = q // 2, q % 2
    rows = dot3((columns[h, 0], columns[h, 1]), (x_top[p], x_rest[p]))
    turn = upper + middle.shape[2]
    stop = turn + second.shape[2]
    for g in range(groups):
        plane = rows[g * y_local : (g + 1) * y_local] + bias[4 * g + q]
        base[g, 0, :upper] = plane[:upper] + own[g, 0, :upper]
        out[g, 0, upper:turn] = gelu(plane[upper:turn] + middle[g, 0])
        out[g, 0, turn:stop] = gelu(plane[turn:stop] + (second[g, 0] + (low[g, 0] + high[g, 0])))
        base[g, 0, upper:] = plane[stop:] + own[g, 0, upper:]


def finish_kernel(upper, _, base, low, high, out, held, sent, sem_in, sem_out):
    tiles = base.shape[1] // 8
    gap = out.shape[1] // 8 - tiles
    arrivals = [
        [
            pltpu.make_async_copy(src.at[:, pl.ds(8 * t, 8), :], held.at[i, t], sem_in.at[i, t])
            for i, src in enumerate((base, low, high))
        ]
        for t in range(tiles)
    ]
    for copies in arrivals:
        for copy in copies:
            copy.start()
    done = []
    for t in range(tiles):
        for copy in arrivals[t]:
            copy.wait()
        sent[t] = gelu(held[0, t] + (held[1, t] + held[2, t]))
        to = t if t < upper else t + gap
        done.append(pltpu.make_async_copy(sent.at[t], out.at[:, pl.ds(8 * to, 8), :], sem_out.at[t]))
        done[-1].start()
    for copy in done:
        copy.wait()


def in_hbm(*arrays):
    return [pltpu.with_memory_space_constraint(a, pltpu.HBM) for a in arrays]


def params():
    return pltpu.CompilerParams(vmem_limit_bytes=VMEM_BYTES)


def cost(flops, moved):
    return pl.CostEstimate(flops=flops, bytes_accessed=moved, transcendentals=0)


def whole_block(table):
    return pl.BlockSpec(table.shape, lambda i: (0,) * table.ndim)


def by_four(array):
    return array.reshape(CH // 4, 4, *array.shape[1:])


def forward_call(field, gy, pinned):
    y_local = field.shape[1]
    tables = [*halves(x_table(False)), *halves(y_table(y_local, gy, False))]
    hbm = pl.BlockSpec(memory_space=pltpu.HBM)
    return pl.pallas_call(
        forward_kernel,
        out_shape=(pltpu.HBM if pinned else jax.ShapeDtypeStruct)((CH // 2 * MY, 4 * MX), F32),
        in_specs=[hbm] * 5,
        scratch_shapes=[
            pltpu.VMEM((4, CH // 4, y_local, NX), F32),
            pltpu.VMEM((2, 2, NX, 4 * MX), BF),
            pltpu.VMEM((2, 2 * MY, y_local), BF),
            pltpu.SemaphoreType.DMA((8,)),
        ],
        compiler_params=params(),
        cost_estimate=cost(10**8, 2**18),
        name="forward_modes",
    )(*in_hbm(by_four(field), *tables))


def filter_call(arrived, gains, gz, gy, scale):
    fwd, inv = z_tables(gz, gy, gains.shape[2], scale)
    fwd, inv = halves(fwd), halves(inv)
    return pl.pallas_call(
        filter_kernel,
        out_shape=pltpu.HBM(arrived.shape, F32),
        compiler_params=params(),
        cost_estimate=cost(2 * 10**11, 2**18),
        name="filter_modes",
    )(arrived, *in_hbm(gains, *fwd, *inv))


def inverse_call(modes, bias, own, middle, second, pair, upper, y_local, gy, scale):
    tables = [*halves(x_table(True, scale)), *halves(y_table(y_local, gy, True))]
    some = lambda rows: pl.BlockSpec((CH // 4, 1, rows, NX), lambda i: (0, i, 0, 0))
    planes = [*in_hbm(*map(by_four, (own, middle, second))), *map(by_four, pair)]
    rim = own.shape[1]
    result, base = pl.pallas_call(
        functools.partial(inverse_kernel, upper),
        out_shape=[
            jax.ShapeDtypeStruct((CH // 4, 4, y_local, NX), F32),
            jax.ShapeDtypeStruct((CH // 4, 4, rim, NX), F32),
        ],
        grid=(4,),
        in_specs=[
            whole_block(modes),
            pl.BlockSpec(memory_space=pltpu.SMEM),
            *[whole_block(t) for t in tables],
            *[some(p.shape[2]) for p in planes],
        ],
        out_specs=[some(y_local), some(rim)],
        scratch_shapes=[pltpu.VMEM((2, 2, CH // 4 * y_local, 128), BF)],
        compiler_params=params(),
        cost_estimate=cost(10**8, 2**18),
        name="inverse_modes",
    )(modes, *in_hbm(bias, *tables), *planes)
    return result.reshape(CH, y_local, NX), base.reshape(CH, rim, NX)


def finish_call(result, base, low, high, upper):
    tiles = base.shape[1] // 8
    anywhere = pl.BlockSpec(memory_space=pl.ANY)
    return pl.pallas_call(
        functools.partial(finish_kernel, upper),
        out_shape=jax.ShapeDtypeStruct(result.shape, F32),
        in_specs=[anywhere] * 4,
        out_specs=anywhere,
        scratch_shapes=[
            pltpu.VMEM((3, tiles, CH, 8, NX), F32),
            pltpu.VMEM((tiles, CH, 8, NX), F32),
            pltpu.SemaphoreType.DMA((3, tiles)),
            pltpu.SemaphoreType.DMA((tiles,)),
        ],
        input_output_aliases={0: 0},
        compiler_params=params(),
        cost_estimate=cost(10**8, 2**18),
        name="finished_rows",
    )(result, base, low, high)


def pack_call(field, tiles):
    count = 8 * len(tiles) + 2
    fetched = len(tiles) + 4
    hbm = pl.BlockSpec(memory_space=pltpu.HBM)
    return pl.pallas_call(
        functools.partial(pack_kernel, tiles),
        out_shape=[pltpu.HBM((count, CH, NX), F32), pltpu.HBM((2, CH, NX), F32)],
        in_specs=[hbm],
        out_specs=[hbm] * 2,
        scratch_shapes=[
            pltpu.VMEM((fetched, 2, CH, 8, 128), F32),
            pltpu.VMEM((count, CH, NX), F32),
            pltpu.VMEM((2, CH, NX), F32),
            pltpu.SemaphoreType.DMA((fetched, 2)),
            pltpu.SemaphoreType.DMA((3,)),
        ],
        compiler_params=params(),
        cost_estimate=cost(10**8, 2**18),
        name="packed_rows",
    )(*in_hbm(field))


def own_call(field, weight, point, segments, halo=()):
    tiles = sum(map(len, segments))
    rows, fetched = 8 * tiles, tiles + 2 * len(segments)
    hbm = pl.BlockSpec(memory_space=pltpu.HBM)
    return pl.pallas_call(
        functools.partial(own_kernel, segments),
        out_shape=[pltpu.HBM((CH, rows, NX), F32)] * 3,
        in_specs=[hbm] * (3 + len(halo)),
        out_specs=[hbm] * 3,
        scratch_shapes=[
            pltpu.VMEM((fetched, 2, CH, 8, 128), F32),
            pltpu.VMEM((2, CH, NX), F32),
            pltpu.VMEM((CH, 27), F32),
            pltpu.VMEM((CH, CH), F32),
            pltpu.VMEM((3, tiles, CH, 8, NX), F32),
            pltpu.VMEM((rows + 2 * len(segments), CH, NX), F32),
            pltpu.VMEM((3, rows, CH, NX), F32),
            pltpu.VMEM((27, CH, 128), F32),
            pltpu.SemaphoreType.DMA((fetched, 2)),
            pltpu.SemaphoreType.DMA((3, tiles)),
            pltpu.SemaphoreType.DMA((3,)),
        ],
        compiler_params=params(),
        cost_estimate=cost(10**8, 2**18),
        name="own_sums",
    )(*in_hbm(weight, point, field, *halo))


def middle_call(weight, point, low, own, high):
    rows = own.shape[0] - 2
    hbm = pl.BlockSpec(memory_space=pltpu.HBM)
    return pl.pallas_call(
        middle_kernel,
        out_shape=pltpu.HBM((CH, rows, NX), F32),
        in_specs=[hbm] * 5,
        out_specs=hbm,
        scratch_shapes=[
            pltpu.VMEM((3, rows + 2, CH, NX), F32),
            pltpu.VMEM((CH, 27), F32),
            pltpu.VMEM((CH, CH), F32),
            pltpu.VMEM((rows // 8, CH, 8, NX), F32),
            pltpu.VMEM((1, rows, CH, NX), F32),
            pltpu.VMEM((27, CH, 128), F32),
            pltpu.SemaphoreType.DMA((5,)),
            pltpu.SemaphoreType.DMA((rows // 8,)),
        ],
        compiler_params=params(),
        cost_estimate=cost(2 * 10**11, 2**18),
        name="middle_sums",
    )(*in_hbm(weight, point, low, own, high))


def general_filter(coarse, gains, gz, gy, scale):
    j_own, n_own = gains.shape[2], gains.shape[3]
    both = ("gz", "gy")
    flat = coarse.reshape(CH // 2, MY, 2, 2, MX).transpose(3, 1, 0, 2, 4).reshape(2, MY, CH * MX)
    sent = flat.reshape(2, gy, j_own, gz, n_own).transpose(3, 1, 0, 2, 4).reshape(gz * gy, -1)
    got = lax.all_to_all(sent, both, split_axis=0, concat_axis=0, tiled=True)
    got = got.reshape(gz, gy, 2, j_own, n_own)
    c, s = (jnp.asarray(t, F32) for t in trig(kept(MZ, gz), np.arange(gz), gz))
    mul = functools.partial(jnp.einsum, precision=lax.Precision.HIGHEST)
    whole = got.sum(axis=1) * scale
    real = mul("zjn,qz->qjn", whole[:, 0], c) + mul("zjn,qz->qjn", whole[:, 1], s)
    imag = mul("zjn,qz->qjn", whole[:, 1], c) - mul("zjn,qz->qjn", whole[:, 0], s)
    real, imag = real * gains[0] - imag * gains[1], real * gains[1] + imag * gains[0]
    out = jnp.stack(
        [
            mul("qjn,qz->zjn", real, c) - mul("qjn,qz->zjn", imag, s),
            mul("qjn,qz->zjn", real, s) + mul("qjn,qz->zjn", imag, c),
        ],
        axis=1,
    )
    out = jnp.broadcast_to(out[:, None], (gz, gy, 2, j_own, n_own)).reshape(gz * gy, -1)
    back = lax.all_to_all(out, both, split_axis=0, concat_axis=0, tiled=True)
    back = back.reshape(gz, gy, 2, j_own, n_own).transpose(2, 1, 3, 0, 4)
    back = back.reshape(2, MY, CH // 2, 2, MX)
    return back.transpose(2, 1, 3, 0, 4).reshape(CH // 2, MY, 4 * MX)


def body(field, spectral_filter, depth_weight, point_weight, bias_vector):
    gz, gy = lax.axis_size("gz"), lax.axis_size("gy")
    y_local = field.shape[2]
    field = field.reshape(CH, y_local, NX)
    y_total = gy * y_local
    forward_scale = 1.0 / math.sqrt(float(NX) * y_total * gz)
    inverse_scale = 1.0 / math.sqrt(2.0 * MX * MY * MZ)

    def ring(axis, count, by):
        return [(i, (i + by) % count) for i in range(count)]

    def to_neighbours(down, up):
        return (
            lax.ppermute(down, "gz", ring("gz", gz, 1)),
            lax.ppermute(up, "gz", ring("gz", gz, -1)),
        )

    def after(value, *others):
        return lax.optimization_barrier((value, *others))[0]

    last = y_local // 8 - 1
    cut = 1 + last // 2
    first_tiles, second_tiles = tuple(range(1, cut)), tuple(range(cut, min(cut + 2, last)))
    outer_tiles = ((0,), tuple(range(second_tiles[-1] + 1, last + 1)))
    sums = functools.partial(own_call, weight=depth_weight, point=point_weight)
    packed, edges = pack_call(field, first_tiles)
    first_low, first_high = to_neighbours(packed, packed)
    if gy == 2:
        halo = lax.ppermute(edges, "gy", ring("gy", gy, 1))
    else:
        halo = jnp.stack(
            [
                lax.ppermute(edges[0], "gy", ring("gy", gy, 1)),
                lax.ppermute(edges[1], "gy", ring("gy", gy, -1)),
            ]
        )
    j_own, n_own = spectral_filter.shape[2], spectral_filter.shape[3]
    whole_tiles = j_own == 8 and n_own == 2 * MX
    coarse = forward_call(after(field, packed), gy, whole_tiles)
    down, second, up = sums(after(field, coarse), segments=(second_tiles,))
    if whole_tiles:
        both = ("gz", "gy")
        got = lax.all_to_all(coarse, both, split_axis=0, concat_axis=0, tiled=True)
        pair = to_neighbours(after(down, got), after(up, got))
        gains = after(spectral_filter, first_low, first_high, second, halo)
        mark = filter_call(got, gains, gz, gy, forward_scale)
        back = lax.all_to_all(mark, both, split_axis=0, concat_axis=0, tiled=True)
        back = back.reshape(CH // 2, MY, 4 * MX)
    else:
        pair = to_neighbours(down, up)
        mark = back = general_filter(coarse, spectral_filter, gz, gy, forward_scale)
    down, own, up = sums(after(field, mark), segments=outer_tiles, halo=(halo,))
    outer_pair = to_neighbours(after(down, back), after(up, back))
    packed, *pair = lax.optimization_barrier((packed, *pair, back))[:-1]
    mixed = middle_call(depth_weight, point_weight, first_low, packed, first_high)
    result, base = inverse_call(
        back, bias_vector, own, mixed, second, pair, 8, y_local, gy, inverse_scale
    )
    result = finish_call(result, base, *outer_pair, 1)
    return result.reshape(CH, 1, y_local, NX)


def solution(mesh):
    in_specs = (P(None, "gz", "gy", None), P(None, None, "gy", "gz"), P(), P(), P())
    out_specs = P(None, "gz", "gy", None)
    return jax.shard_map(body, mesh=mesh, in_specs=in_specs, out_specs=out_specs, check_vma=False)
```

```python
import functools
import math

import jax
import jax.numpy as jnp
import ml_dtypes
import numpy as np
from jax import lax
from jax.experimental import pallas as pl
from jax.experimental.pallas import tpu as pltpu
from jax.sharding import PartitionSpec as P

NX = 256
MX = 32
MY = 16
MZ = 16
CH = 32
VMEM_BYTES = 20 * 1024 * 1024
BF = jnp.bfloat16
F32 = jnp.float32


def kept(count, total):
    series = np.arange(count)
    return np.where(series < count // 2, series, total - count + series)


def trig(freqs, places, total):
    angle = 2.0 * np.pi * ((freqs[:, None] * places[None, :]) % total) / total
    return np.cos(angle), np.sin(angle)


def halves(table):
    table = np.asarray(table, np.float64)
    top = table.astype(np.float32).astype(ml_dtypes.bfloat16)
    rest = (table - top.astype(np.float64)).astype(np.float32).astype(ml_dtypes.bfloat16)
    return jnp.asarray(top), jnp.asarray(rest)


def y_table(y_local, gy, inverse):
    out = []
    for g in range(gy):
        places = g * y_local + np.arange(y_local)
        out.append(np.concatenate(trig(kept(MY, y_local * gy), places, y_local * gy), axis=0))
    return np.stack([t.T for t in out] if inverse else out)


def x_table(inverse, scale=1.0):
    c, s = trig(np.arange(MX), np.arange(NX), NX)
    w = np.where(np.arange(MX) == 0, 1.0, 2.0)[:, None] if inverse else 1.0
    out = np.zeros((2, 2, 2, MX, NX))
    for p in range(2):
        out[p, p, 0] = w * c * scale
        out[p, p, 1] = -w * s * scale
    out = out.reshape(2, 4 * MX, NX)
    return out if inverse else out.transpose(0, 2, 1)


def z_tables(gz, gy, rows, scale):
    c, s = trig(kept(MZ, gz), np.arange(gz), gz)
    eye = np.eye(rows)
    one = np.ones(gy)
    both = np.stack([c, s])
    fwd = np.einsum("tqz,g,jk->tqjzgk", both, one, eye) * scale
    inv = np.einsum("tqz,g,jk->tzgjqk", both, one, eye)
    return fwd.reshape(2 * MZ * rows, gz * gy * rows), inv.reshape(2 * gz * gy * rows, MZ * rows)


def parts(value):
    top = value.astype(BF)
    return top, (value - top.astype(F32)).astype(BF)


def dot(a, b):
    return jnp.dot(a, b, preferred_element_type=F32)


def dot3(a, b):
    rows = a[0].shape[0]
    both = dot(jnp.concatenate([a[0], a[1]], axis=0), b[0])
    return both[:rows] + (both[rows:] + dot(a[0], b[1]))


def swap_parts(value):
    lane = lax.broadcasted_iota(jnp.int32, value.shape, 1)
    is_real = (lane // MX) % 2 == 0
    width = value.shape[1]
    return jnp.where(is_real, pltpu.roll(value, width - MX, 1), pltpu.roll(value, MX, 1)), is_real


def forward_kernel(field, x_top, x_rest, y_top, y_rest, out, taken, x_both, y_both, sem):
    gy = lax.axis_index("gy")
    few = [
        pltpu.make_async_copy(src, dst, sem.at[4 + i])
        for i, (src, dst) in enumerate(
            ((x_top, x_both.at[0]), (x_rest, x_both.at[1]), (y_top.at[gy], y_both.at[0]), (y_rest.at[gy], y_both.at[1]))
        )
    ]
    copies = [pltpu.make_async_copy(field.at[:, q], taken.at[q], sem.at[q]) for q in range(4)]
    for copy in few + copies:
        copy.start()
    for copy in few:
        copy.wait()
    groups, rows = taken.shape[1:3]
    halves_of = []
    for q in range(4):
        copies[q].wait()
        part = dot3(parts(taken[q].reshape(groups * rows, NX)), (x_both[0, q % 2], x_both[1, q % 2]))
        if q % 2:
            halves_of[-1] = halves_of[-1] + part
        else:
            halves_of.append(part)
    total = jnp.concatenate(halves_of, axis=1)
    for g in range(groups):
        both = dot3((y_both[0], y_both[1]), parts(total[g * rows : (g + 1) * rows]))
        crossed, is_real = swap_parts(both[MY:])
        modes = both[:MY] + jnp.where(is_real, crossed, -crossed)
        out[pl.ds(2 * g * MY, MY), :] = modes[:, : 4 * MX]
        out[pl.ds((2 * g + 1) * MY, MY), :] = modes[:, 4 * MX :]


def filter_kernel(arrived, gains, f_top, f_rest, i_top, i_rest, out):
    real, imag = (gains[r].reshape(-1, 2 * MX) for r in range(2))
    first, second = slice(0, MX), slice(MX, 2 * MX)
    same = jnp.concatenate([real[:, first], real[:, first], real[:, second], real[:, second]], axis=1)
    cross = jnp.concatenate([-imag[:, first], imag[:, first], -imag[:, second], imag[:, second]], axis=1)
    half = f_top.shape[0] // 2
    turned = dot3((f_top[...], f_rest[...]), parts(arrived[...]))
    crossed, is_real = swap_parts(turned[half:])
    modes = turned[:half] + jnp.where(is_real, crossed, -crossed)
    crossed, _ = swap_parts(modes)
    filtered = modes * same + crossed * cross
    half = i_top.shape[0] // 2
    back = dot3((i_top[...], i_rest[...]), parts(filtered))
    crossed, is_real = swap_parts(back[half:])
    out[...] = back[:half] + jnp.where(is_real, -crossed, crossed)


def fetch_tiles(field, taken, sems, wanted):
    pending = {}
    for k, t in enumerate(wanted):
        pending[t] = [
            pltpu.make_async_copy(
                field.at[:, pl.ds(8 * t, 8), pl.ds(128 * h, 128)], taken.at[k, h], sems.at[k, h]
            )
            for h in range(2)
        ]
        for copy in pending[t]:
            copy.start()

    def row(t, r):
        for copy in pending.pop(t, ()):
            copy.wait()
        k = wanted.index(t)
        return jnp.concatenate(
            [taken.at[k, h].reshape(CH * 8, 128)[pl.ds(r, CH, stride=8), :] for h in range(2)], axis=1
        )

    return row


def spread_gains(weights, gains, offsets):
    for k in [9 * a + j for a in offsets for j in range(9)]:
        gains[k] = jnp.broadcast_to(weights[:, k : k + 1], (CH, 128))


def mixing(points):
    down = (
        lax.broadcasted_iota(jnp.int32, (8 * CH, CH), 0) // 8
        == lax.broadcasted_iota(jnp.int32, (8 * CH, CH), 1)
    ).astype(BF)
    across = (
        lax.broadcasted_iota(jnp.int32, (CH, 8 * CH), 1) % CH
        == lax.broadcasted_iota(jnp.int32, (CH, 8 * CH), 0)
    ).astype(BF)
    same = (
        lax.broadcasted_iota(jnp.int32, (8 * CH, 8 * CH), 0) % 8
        == lax.broadcasted_iota(jnp.int32, (8 * CH, 8 * CH), 1) // CH
    )
    return tuple(
        jnp.where(same, dot(dot(down, part).astype(BF), across), 0.0).astype(BF)
        for part in parts(points)
    )


def tap_sums(load, uses, gains, depth, runs):
    def some(i, _):
        chans = pl.ds(pl.multiple_of(i * 8, 8), 8)
        wanted = sorted({a for use in uses for a, _ in use})
        gain = {k: gains[k, chans, :] for a in wanted for k in range(9 * a, 9 * a + 9)}
        for first, to, rows in runs:
            sums = {}
            for r in range(rows + 2):
                for s, use in enumerate(uses):
                    value = load(s, first + r, chans)
                    turned = (pltpu.roll(value, 1, 1), value, pltpu.roll(value, NX - 1, 1))
                    for b in range(3):
                        o = r - b
                        if o < 0 or o >= rows:
                            continue
                        for a, k in use:
                            for e in range(3):
                                for h in range(2):
                                    term = gain[a * 9 + b * 3 + e] * turned[e][:, 128 * h : 128 * h + 128]
                                    place = (o, k, h)
                                    sums[place] = sums[place] + term if place in sums else term
                if r >= 2:
                    for k in sorted({k for use in uses for _, k in use}):
                        for h in range(2):
                            depth[k, to + r - 2, chans, pl.ds(128 * h, 128)] = sums.pop((r - 2, k, h))
        return 0

    lax.fori_loop(0, CH // 8, some, 0)


def mix_tile(mix, depth, k, t):
    tile = depth[k, pl.ds(8 * t, 8)].reshape(8 * CH, NX)
    return dot3(mix, parts(tile)).reshape(CH, 8, NX)


def pack_kernel(tiles, field, packed, edges, taken, rows, ends, sem_in, sem_out):
    last = field.shape[1] // 8 - 1
    before, after = tiles[0] - 1, tiles[-1] + 1
    wanted = [before, *tiles, after] + [t for t in (0, last) if t not in (before, after)]
    row = fetch_tiles(field, taken, sem_in, wanted)
    places = [(before, 7), *[(t, r) for t in tiles for r in range(8)], (after, 0)]
    copies, cuts = [], (0, len(places) // 2, len(places))
    for k in range(2):
        for i in range(cuts[k], cuts[k + 1]):
            rows[i] = row(*places[i])
        some = pl.ds(cuts[k], cuts[k + 1] - cuts[k])
        copies.append(pltpu.make_async_copy(rows.at[some], packed.at[some], sem_out.at[k]))
        copies[-1].start()
    ends[0] = row(last, 7)
    ends[1] = row(0, 0)
    copies.append(pltpu.make_async_copy(ends, edges, sem_out.at[2]))
    copies[-1].start()
    for copy in copies:
        copy.wait()


def own_kernel(segments, groups, weight, point, field, halo, *refs):
    last = field.shape[1] // 8 - 1
    count = 3 * len(groups)
    outs, (taken, halo_rows, weights, points, sent, lined, depth, gains, sem_in, sem_out, sem_few) = (
        refs[:count],
        refs[count:],
    )
    few = [
        pltpu.make_async_copy(src, dst, sem_few.at[i])
        for i, (src, dst) in enumerate(((weight, weights), (point, points), (halo, halo_rows)))
    ]
    for copy in few:
        copy.start()
    wanted = sorted({t for tiles in segments for t in (tiles[0] - 1, *tiles, tiles[-1] + 1) if 0 <= t <= last})
    row = fetch_tiles(field, taken, sem_in, wanted)
    for copy in few:
        copy.wait()
    spread_gains(weights, gains, range(3))
    mix = mixing(points[...])
    runs, at, done, order = [], 0, 0, []
    for tiles in segments:
        places = [(tiles[0] - 1, 7), *[(t, r) for t in tiles for r in range(8)], (tiles[-1] + 1, 0)]
        for i, (t, r) in enumerate(places):
            lined[at + i] = halo_rows[0] if t < 0 else halo_rows[1] if t > last else row(t, r)
        runs.append((at, done, 8 * len(tiles)))
        at, done = at + len(places), done + 8 * len(tiles)
        order += tiles
    tap_sums(lambda s, r, c: lined[r, c, :], [[(a, a) for a in range(3)]], gains, depth, runs)
    copies = []
    for g, tiles in enumerate(groups):
        for i, tile in enumerate(tiles):
            t = order.index(tile)
            for k in range(3):
                sent[k, t] = mix_tile(mix, depth, k, t)
                to = outs[3 * g + k].at[:, pl.ds(8 * i, 8), :]
                copies.append(pltpu.make_async_copy(sent.at[k, t], to, sem_out.at[k, t]))
                copies[-1].start()
    for copy in copies:
        copy.wait()


def middle_kernel(weight, point, low, own, high, out, taken, weights, points, sent, depth, gains, sem_in, sem_out):
    copies = [
        pltpu.make_async_copy(src, dst, sem_in.at[i])
        for i, (src, dst) in enumerate(
            ((weight, weights), (point, points), (low, taken.at[0]), (own, taken.at[1]), (high, taken.at[2]))
        )
    ]
    for copy in copies:
        copy.start()
    for copy in copies[:2]:
        copy.wait()
    spread_gains(weights, gains, range(3))
    mix = mixing(points[...])
    for copy in copies[2:]:
        copy.wait()
    rows = out.shape[1]
    tap_sums(lambda s, r, c: taken[s, r, c, :], [[(a, 0)] for a in range(3)], gains, depth, [(0, 0, rows)])
    copies = []
    for t in range(rows // 8):
        sent[t] = mix_tile(mix, depth, 0, t)
        copies.append(pltpu.make_async_copy(sent.at[t], out.at[:, pl.ds(8 * t, 8), :], sem_out.at[t]))
        copies[-1].start()
    for copy in copies:
        copy.wait()


def gelu(value):
    size = jnp.abs(value) * math.sqrt(0.5)
    below = 1.0 + 0.3275911 * size
    t = pl.reciprocal(below, approx=True)
    t = t * (2.0 - below * t)
    series = 1.061405429 * t - 1.453152027
    for factor in (1.421413741, -0.284496736, 0.254829592):
        series = series * t + factor
    tail = 0.5 * (series * t) * jnp.exp(-(size * size))
    return value * jnp.where(value < 0.0, tail, 1.0 - tail)


def inverse_kernel(upper, modes, bias, x_top, x_rest, y_top, y_rest, own, middle, second, low, high, out, base, columns):
    q = pl.program_id(0)
    groups, _, y_local, _ = out.shape

    @pl.when(q == 0)
    def _():
        gy = lax.axis_index("gy")
        for g in range(groups):
            own_modes = jnp.concatenate([modes[2 * g], modes[2 * g + 1]], axis=1)
            crossed, is_real = swap_parts(own_modes)
            stack = jnp.concatenate([own_modes, jnp.where(is_real, -crossed, crossed)], axis=0)
            pair = parts(dot3((y_top[gy], y_rest[gy]), parts(stack)))
            for h in range(2):
                for k in range(2):
                    columns[h, k, pl.ds(g * y_local, y_local), :] = pair[k][:, 128 * h : 128 * h + 128]

    h, p = q // 2, q % 2
    rows = dot3((columns[h, 0], columns[h, 1]), (x_top[p], x_rest[p]))
    turn = upper + middle.shape[2]
    stop = turn + second.shape[2]
    for g in range(groups):
        plane = rows[g * y_local : (g + 1) * y_local] + bias[4 * g + q]
        base[g, 0, :upper] = plane[:upper] + own[g, 0, :upper]
        out[g, 0, upper:turn] = gelu(plane[upper:turn] + middle[g, 0])
        out[g, 0, turn:stop] = gelu(plane[turn:stop] + (second[g, 0] + (low[g, 0] + high[g, 0])))
        base[g, 0, upper:] = plane[stop:] + own[g, 0, upper:]


def finish_kernel(upper, _, base, low, high, out, held, sent, sem_in, sem_out):
    tiles = base.shape[1] // 8
    gap = out.shape[1] // 8 - tiles
    arrivals = [
        [
            pltpu.make_async_copy(src.at[:, pl.ds(8 * t, 8), :], held.at[i, t], sem_in.at[i, t])
            for i, src in enumerate((base, low, high))
        ]
        for t in range(tiles)
    ]
    for copies in arrivals:
        for copy in copies:
            copy.start()
    done = []
    for t in range(tiles):
        for copy in arrivals[t]:
            copy.wait()
        sent[t] = gelu(held[0, t] + (held[1, t] + held[2, t]))
        to = t if t < upper else t + gap
        done.append(pltpu.make_async_copy(sent.at[t], out.at[:, pl.ds(8 * to, 8), :], sem_out.at[t]))
        done[-1].start()
    for copy in done:
        copy.wait()


def in_hbm(*arrays):
    return [pltpu.with_memory_space_constraint(a, pltpu.HBM) for a in arrays]


def params():
    return pltpu.CompilerParams(vmem_limit_bytes=VMEM_BYTES)


def cost(flops, moved):
    return pl.CostEstimate(flops=flops, bytes_accessed=moved, transcendentals=0)


def whole_block(table):
    return pl.BlockSpec(table.shape, lambda i: (0,) * table.ndim)


def by_four(array):
    return array.reshape(CH // 4, 4, *array.shape[1:])


def forward_call(field, gy, pinned):
    y_local = field.shape[1]
    tables = [*halves(x_table(False)), *halves(y_table(y_local, gy, False))]
    hbm = pl.BlockSpec(memory_space=pltpu.HBM)
    return pl.pallas_call(
        forward_kernel,
        out_shape=(pltpu.HBM if pinned else jax.ShapeDtypeStruct)((CH // 2 * MY, 4 * MX), F32),
        in_specs=[hbm] * 5,
        scratch_shapes=[
            pltpu.VMEM((4, CH // 4, y_local, NX), F32),
            pltpu.VMEM((2, 2, NX, 4 * MX), BF),
            pltpu.VMEM((2, 2 * MY, y_local), BF),
            pltpu.SemaphoreType.DMA((8,)),
        ],
        compiler_params=params(),
        cost_estimate=cost(10**8, 2**18),
        name="forward_modes",
    )(*in_hbm(by_four(field), *tables))


def filter_call(arrived, gains, gz, gy, scale):
    fwd, inv = z_tables(gz, gy, gains.shape[2], scale)
    fwd, inv = halves(fwd), halves(inv)
    return pl.pallas_call(
        filter_kernel,
        out_shape=pltpu.HBM(arrived.shape, F32),
        compiler_params=params(),
        cost_estimate=cost(2 * 10**11, 2**18),
        name="filter_modes",
    )(arrived, *in_hbm(gains, *fwd, *inv))


def inverse_call(modes, bias, own, middle, second, pair, upper, y_local, gy, scale):
    tables = [*halves(x_table(True, scale)), *halves(y_table(y_local, gy, True))]
    some = lambda rows: pl.BlockSpec((CH // 4, 1, rows, NX), lambda i: (0, i, 0, 0))
    planes = [*in_hbm(*map(by_four, (own, middle, second))), *map(by_four, pair)]
    rim = own.shape[1]
    result, base = pl.pallas_call(
        functools.partial(inverse_kernel, upper),
        out_shape=[
            jax.ShapeDtypeStruct((CH // 4, 4, y_local, NX), F32),
            jax.ShapeDtypeStruct((CH // 4, 4, rim, NX), F32),
        ],
        grid=(4,),
        in_specs=[
            whole_block(modes),
            pl.BlockSpec(memory_space=pltpu.SMEM),
            *[whole_block(t) for t in tables],
            *[some(p.shape[2]) for p in planes],
        ],
        out_specs=[some(y_local), some(rim)],
        scratch_shapes=[pltpu.VMEM((2, 2, CH // 4 * y_local, 128), BF)],
        compiler_params=params(),
        cost_estimate=cost(10**8, 2**18),
        name="inverse_modes",
    )(modes, *in_hbm(bias, *tables), *planes)
    return result.reshape(CH, y_local, NX), base.reshape(CH, rim, NX)


def finish_call(result, base, low, high, upper):
    tiles = base.shape[1] // 8
    anywhere = pl.BlockSpec(memory_space=pl.ANY)
    return pl.pallas_call(
        functools.partial(finish_kernel, upper),
        out_shape=jax.ShapeDtypeStruct(result.shape, F32),
        in_specs=[anywhere] * 4,
        out_specs=anywhere,
        scratch_shapes=[
            pltpu.VMEM((3, tiles, CH, 8, NX), F32),
            pltpu.VMEM((tiles, CH, 8, NX), F32),
            pltpu.SemaphoreType.DMA((3, tiles)),
            pltpu.SemaphoreType.DMA((tiles,)),
        ],
        input_output_aliases={0: 0},
        compiler_params=params(),
        cost_estimate=cost(10**8, 2**18),
        name="finished_rows",
    )(result, base, low, high)


def pack_call(field, tiles):
    count = 8 * len(tiles) + 2
    fetched = len(tiles) + 4
    hbm = pl.BlockSpec(memory_space=pltpu.HBM)
    return pl.pallas_call(
        functools.partial(pack_kernel, tiles),
        out_shape=[pltpu.HBM((count, CH, NX), F32), pltpu.HBM((2, CH, NX), F32)],
        in_specs=[hbm],
        out_specs=[hbm] * 2,
        scratch_shapes=[
            pltpu.VMEM((fetched, 2, CH, 8, 128), F32),
            pltpu.VMEM((count, CH, NX), F32),
            pltpu.VMEM((2, CH, NX), F32),
            pltpu.SemaphoreType.DMA((fetched, 2)),
            pltpu.SemaphoreType.DMA((3,)),
        ],
        compiler_params=params(),
        cost_estimate=cost(10**8, 2**18),
        name="packed_rows",
    )(*in_hbm(field))


def own_call(field, halo, weight, point, segments, groups):
    tiles = sum(map(len, segments))
    rows, fetched = 8 * tiles, tiles + 2 * len(segments)
    hbm = pl.BlockSpec(memory_space=pltpu.HBM)
    shapes = [pltpu.HBM((CH, 8 * len(group), NX), F32) for group in groups for _ in range(3)]
    return pl.pallas_call(
        functools.partial(own_kernel, segments, groups),
        out_shape=shapes,
        in_specs=[hbm] * 4,
        out_specs=[hbm] * len(shapes),
        scratch_shapes=[
            pltpu.VMEM((fetched, 2, CH, 8, 128), F32),
            pltpu.VMEM((2, CH, NX), F32),
            pltpu.VMEM((CH, 27), F32),
            pltpu.VMEM((CH, CH), F32),
            pltpu.VMEM((3, tiles, CH, 8, NX), F32),
            pltpu.VMEM((rows + 2 * len(segments), CH, NX), F32),
            pltpu.VMEM((3, rows, CH, NX), F32),
            pltpu.VMEM((27, CH, 128), F32),
            pltpu.SemaphoreType.DMA((fetched, 2)),
            pltpu.SemaphoreType.DMA((3, tiles)),
            pltpu.SemaphoreType.DMA((3,)),
        ],
        compiler_params=params(),
        cost_estimate=cost(10**8, 2**18),
        name="own_sums",
    )(*in_hbm(weight, point, field, halo))


def middle_call(weight, point, low, own, high):
    rows = own.shape[0] - 2
    hbm = pl.BlockSpec(memory_space=pltpu.HBM)
    return pl.pallas_call(
        middle_kernel,
        out_shape=pltpu.HBM((CH, rows, NX), F32),
        in_specs=[hbm] * 5,
        out_specs=hbm,
        scratch_shapes=[
            pltpu.VMEM((3, rows + 2, CH, NX), F32),
            pltpu.VMEM((CH, 27), F32),
            pltpu.VMEM((CH, CH), F32),
            pltpu.VMEM((rows // 8, CH, 8, NX), F32),
            pltpu.VMEM((1, rows, CH, NX), F32),
            pltpu.VMEM((27, CH, 128), F32),
            pltpu.SemaphoreType.DMA((5,)),
            pltpu.SemaphoreType.DMA((rows // 8,)),
        ],
        compiler_params=params(),
        cost_estimate=cost(2 * 10**11, 2**18),
        name="middle_sums",
    )(*in_hbm(weight, point, low, own, high))


def general_filter(coarse, gains, gz, gy, scale):
    j_own, n_own = gains.shape[2], gains.shape[3]
    both = ("gz", "gy")
    flat = coarse.reshape(CH // 2, MY, 2, 2, MX).transpose(3, 1, 0, 2, 4).reshape(2, MY, CH * MX)
    sent = flat.reshape(2, gy, j_own, gz, n_own).transpose(3, 1, 0, 2, 4).reshape(gz * gy, -1)
    got = lax.all_to_all(sent, both, split_axis=0, concat_axis=0, tiled=True)
    got = got.reshape(gz, gy, 2, j_own, n_own)
    c, s = (jnp.asarray(t, F32) for t in trig(kept(MZ, gz), np.arange(gz), gz))
    mul = functools.partial(jnp.einsum, precision=lax.Precision.HIGHEST)
    whole = got.sum(axis=1) * scale
    real = mul("zjn,qz->qjn", whole[:, 0], c) + mul("zjn,qz->qjn", whole[:, 1], s)
    imag = mul("zjn,qz->qjn", whole[:, 1], c) - mul("zjn,qz->qjn", whole[:, 0], s)
    real, imag = real * gains[0] - imag * gains[1], real * gains[1] + imag * gains[0]
    out = jnp.stack(
        [
            mul("qjn,qz->zjn", real, c) - mul("qjn,qz->zjn", imag, s),
            mul("qjn,qz->zjn", real, s) + mul("qjn,qz->zjn", imag, c),
        ],
        axis=1,
    )
    out = jnp.broadcast_to(out[:, None], (gz, gy, 2, j_own, n_own)).reshape(gz * gy, -1)
    back = lax.all_to_all(out, both, split_axis=0, concat_axis=0, tiled=True)
    back = back.reshape(gz, gy, 2, j_own, n_own).transpose(2, 1, 3, 0, 4)
    back = back.reshape(2, MY, CH // 2, 2, MX)
    return back.transpose(2, 1, 3, 0, 4).reshape(CH // 2, MY, 4 * MX)


def body(field, spectral_filter, depth_weight, point_weight, bias_vector):
    gz, gy = lax.axis_size("gz"), lax.axis_size("gy")
    y_local = field.shape[2]
    field = field.reshape(CH, y_local, NX)
    y_total = gy * y_local
    forward_scale = 1.0 / math.sqrt(float(NX) * y_total * gz)
    inverse_scale = 1.0 / math.sqrt(2.0 * MX * MY * MZ)

    def ring(axis, count, by):
        return [(i, (i + by) % count) for i in range(count)]

    def to_neighbours(down, up):
        return (
            lax.ppermute(down, "gz", ring("gz", gz, 1)),
            lax.ppermute(up, "gz", ring("gz", gz, -1)),
        )

    def after(value, *others):
        return lax.optimization_barrier((value, *others))[0]

    last = y_local // 8 - 1
    cut = 1 + last // 2
    first_tiles, second_tiles = tuple(range(1, cut)), tuple(range(cut, min(cut + 2, last)))
    third_tiles = (0, *range(second_tiles[-1] + 1, last + 1))
    packed, edges = pack_call(field, first_tiles)
    first_low, first_high = to_neighbours(packed, packed)
    if gy == 2:
        halo = lax.ppermute(edges, "gy", ring("gy", gy, 1))
    else:
        halo = jnp.stack(
            [
                lax.ppermute(edges[0], "gy", ring("gy", gy, 1)),
                lax.ppermute(edges[1], "gy", ring("gy", gy, -1)),
            ]
        )
    j_own, n_own = spectral_filter.shape[2], spectral_filter.shape[3]
    whole_tiles = j_own == 8 and n_own == 2 * MX
    coarse = after(forward_call(after(field, packed), gy, whole_tiles), halo)
    segments, groups = ((0,), tuple(range(cut, last + 1))), (second_tiles, third_tiles)
    down, second, up, outer_down, own, outer_up = own_call(
        after(field, coarse), halo, depth_weight, point_weight, segments, groups
    )
    if whole_tiles:
        both = ("gz", "gy")
        got = lax.all_to_all(coarse, both, split_axis=0, concat_axis=0, tiled=True)
        pair = to_neighbours(after(down, got), after(up, got))
        gains = after(spectral_filter, first_low, first_high, second)
        mark = filter_call(got, gains, gz, gy, forward_scale)
        back = lax.all_to_all(mark, both, split_axis=0, concat_axis=0, tiled=True)
        back = back.reshape(CH // 2, MY, 4 * MX)
    else:
        pair = to_neighbours(down, up)
        mark = back = general_filter(coarse, spectral_filter, gz, gy, forward_scale)
    outer_pair = to_neighbours(after(outer_down, mark), after(outer_up, mark))
    packed, *pair = lax.optimization_barrier((packed, *pair, back))[:-1]
    mixed = middle_call(depth_weight, point_weight, first_low, packed, first_high)
    result, base = inverse_call(
        back, bias_vector, own, mixed, second, pair, 8, y_local, gy, inverse_scale
    )
    result = finish_call(result, base, *outer_pair, 1)
    return result.reshape(CH, 1, y_local, NX)


def solution(mesh):
    in_specs = (P(None, "gz", "gy", None), P(None, None, "gy", "gz"), P(), P(), P())
    out_specs = P(None, "gz", "gy", None)
    return jax.shard_map(body, mesh=mesh, in_specs=in_specs, out_specs=out_specs, check_vma=False)
```

```python
import functools
import math

import jax
import jax.numpy as jnp
import ml_dtypes
import numpy as np
from jax import lax
from jax.experimental import pallas as pl
from jax.experimental.pallas import tpu as pltpu
from jax.sharding import PartitionSpec as P

NX = 256
MX = 32
MY = 16
MZ = 16
CH = 32
VMEM_BYTES = 20 * 1024 * 1024
BF = jnp.bfloat16
F32 = jnp.float32


def kept(count, total):
    series = np.arange(count)
    return np.where(series < count // 2, series, total - count + series)


def trig(freqs, places, total):
    angle = 2.0 * np.pi * ((freqs[:, None] * places[None, :]) % total) / total
    return np.cos(angle), np.sin(angle)


def halves(table):
    table = np.asarray(table, np.float64)
    top = table.astype(np.float32).astype(ml_dtypes.bfloat16)
    rest = (table - top.astype(np.float64)).astype(np.float32).astype(ml_dtypes.bfloat16)
    return jnp.asarray(top), jnp.asarray(rest)


def y_table(y_local, gy, inverse):
    out = []
    for g in range(gy):
        places = g * y_local + np.arange(y_local)
        out.append(np.concatenate(trig(kept(MY, y_local * gy), places, y_local * gy), axis=0))
    return np.stack([t.T for t in out] if inverse else out)


def x_table(inverse, scale=1.0):
    c, s = trig(np.arange(MX), np.arange(NX), NX)
    w = np.where(np.arange(MX) == 0, 1.0, 2.0)[:, None] if inverse else 1.0
    out = np.zeros((2, 2, 2, MX, NX))
    for p in range(2):
        out[p, p, 0] = w * c * scale
        out[p, p, 1] = -w * s * scale
    out = out.reshape(2, 4 * MX, NX)
    return out if inverse else out.transpose(0, 2, 1)


def z_tables(gz, gy, rows, scale):
    c, s = trig(kept(MZ, gz), np.arange(gz), gz)
    eye = np.eye(rows)
    one = np.ones(gy)
    both = np.stack([c, s])
    fwd = np.einsum("tqz,g,jk->tqjzgk", both, one, eye) * scale
    inv = np.einsum("tqz,g,jk->tzgjqk", both, one, eye)
    return fwd.reshape(2 * MZ * rows, gz * gy * rows), inv.reshape(2 * gz * gy * rows, MZ * rows)


def parts(value):
    top = value.astype(BF)
    return top, (value - top.astype(F32)).astype(BF)


def dot(a, b):
    return jnp.dot(a, b, preferred_element_type=F32)


def dot3(a, b):
    rows = a[0].shape[0]
    both = dot(jnp.concatenate([a[0], a[1]], axis=0), b[0])
    return both[:rows] + (both[rows:] + dot(a[0], b[1]))


def swap_parts(value):
    lane = lax.broadcasted_iota(jnp.int32, value.shape, 1)
    is_real = (lane // MX) % 2 == 0
    width = value.shape[1]
    return jnp.where(is_real, pltpu.roll(value, width - MX, 1), pltpu.roll(value, MX, 1)), is_real


def forward_kernel(field, x_top, x_rest, y_top, y_rest, out, taken, x_both, y_both, sem):
    gy = lax.axis_index("gy")
    few = [
        pltpu.make_async_copy(src, dst, sem.at[4 + i])
        for i, (src, dst) in enumerate(
            ((x_top, x_both.at[0]), (x_rest, x_both.at[1]), (y_top.at[gy], y_both.at[0]), (y_rest.at[gy], y_both.at[1]))
        )
    ]
    copies = [pltpu.make_async_copy(field.at[:, q], taken.at[q], sem.at[q]) for q in range(4)]
    for copy in few + copies:
        copy.start()
    for copy in few:
        copy.wait()
    groups, rows = taken.shape[1:3]
    halves_of = []
    for q in range(4):
        copies[q].wait()
        part = dot3(parts(taken[q].reshape(groups * rows, NX)), (x_both[0, q % 2], x_both[1, q % 2]))
        if q % 2:
            halves_of[-1] = halves_of[-1] + part
        else:
            halves_of.append(part)
    total = jnp.concatenate(halves_of, axis=1)
    for g in range(groups):
        both = dot3((y_both[0], y_both[1]), parts(total[g * rows : (g + 1) * rows]))
        crossed, is_real = swap_parts(both[MY:])
        modes = both[:MY] + jnp.where(is_real, crossed, -crossed)
        out[pl.ds(2 * g * MY, MY), :] = modes[:, : 4 * MX]
        out[pl.ds((2 * g + 1) * MY, MY), :] = modes[:, 4 * MX :]


def filter_kernel(arrived, gains, f_top, f_rest, i_top, i_rest, out):
    real, imag = (gains[r].reshape(-1, 2 * MX) for r in range(2))
    first, second = slice(0, MX), slice(MX, 2 * MX)
    same = jnp.concatenate([real[:, first], real[:, first], real[:, second], real[:, second]], axis=1)
    cross = jnp.concatenate([-imag[:, first], imag[:, first], -imag[:, second], imag[:, second]], axis=1)
    half = f_top.shape[0] // 2
    turned = dot3((f_top[...], f_rest[...]), parts(arrived[...]))
    crossed, is_real = swap_parts(turned[half:])
    modes = turned[:half] + jnp.where(is_real, crossed, -crossed)
    crossed, _ = swap_parts(modes)
    filtered = modes * same + crossed * cross
    half = i_top.shape[0] // 2
    back = dot3((i_top[...], i_rest[...]), parts(filtered))
    crossed, is_real = swap_parts(back[half:])
    out[...] = back[:half] + jnp.where(is_real, -crossed, crossed)


def fetch_tiles(field, taken, sems, wanted):
    pending = {}
    for k, t in enumerate(wanted):
        pending[t] = [
            pltpu.make_async_copy(
                field.at[:, pl.ds(8 * t, 8), pl.ds(128 * h, 128)], taken.at[k, h], sems.at[k, h]
            )
            for h in range(2)
        ]
        for copy in pending[t]:
            copy.start()

    def row(t, r):
        for copy in pending.pop(t, ()):
            copy.wait()
        k = wanted.index(t)
        return jnp.concatenate(
            [taken.at[k, h].reshape(CH * 8, 128)[pl.ds(r, CH, stride=8), :] for h in range(2)], axis=1
        )

    return row


def spread_gains(weights, gains, offsets):
    for k in [9 * a + j for a in offsets for j in range(9)]:
        gains[k] = jnp.broadcast_to(weights[:, k : k + 1], (CH, 128))


def mixing(points):
    down = (
        lax.broadcasted_iota(jnp.int32, (8 * CH, CH), 0) // 8
        == lax.broadcasted_iota(jnp.int32, (8 * CH, CH), 1)
    ).astype(BF)
    across = (
        lax.broadcasted_iota(jnp.int32, (CH, 8 * CH), 1) % CH
        == lax.broadcasted_iota(jnp.int32, (CH, 8 * CH), 0)
    ).astype(BF)
    same = (
        lax.broadcasted_iota(jnp.int32, (8 * CH, 8 * CH), 0) % 8
        == lax.broadcasted_iota(jnp.int32, (8 * CH, 8 * CH), 1) // CH
    )
    return tuple(
        jnp.where(same, dot(dot(down, part).astype(BF), across), 0.0).astype(BF)
        for part in parts(points)
    )


def tap_sums(load, uses, gains, depth, runs):
    def some(i, _):
        chans = pl.ds(pl.multiple_of(i * 8, 8), 8)
        wanted = sorted({a for use in uses for a, _ in use})
        gain = {k: gains[k, chans, :] for a in wanted for k in range(9 * a, 9 * a + 9)}
        for first, to, rows in runs:
            sums = {}
            for r in range(rows + 2):
                for s, use in enumerate(uses):
                    value = load(s, first + r, chans)
                    turned = (pltpu.roll(value, 1, 1), value, pltpu.roll(value, NX - 1, 1))
                    for b in range(3):
                        o = r - b
                        if o < 0 or o >= rows:
                            continue
                        for a, k in use:
                            for e in range(3):
                                for h in range(2):
                                    term = gain[a * 9 + b * 3 + e] * turned[e][:, 128 * h : 128 * h + 128]
                                    place = (o, k, h)
                                    sums[place] = sums[place] + term if place in sums else term
                if r >= 2:
                    for k in sorted({k for use in uses for _, k in use}):
                        for h in range(2):
                            depth[k, to + r - 2, chans, pl.ds(128 * h, 128)] = sums.pop((r - 2, k, h))
        return 0

    lax.fori_loop(0, CH // 8, some, 0)


def mix_tile(mix, depth, k, t):
    tile = depth[k, pl.ds(8 * t, 8)].reshape(8 * CH, NX)
    return dot3(mix, parts(tile)).reshape(CH, 8, NX)


def pack_kernel(tiles, field, packed, edges, taken, rows, ends, sem_in, sem_out):
    last = field.shape[1] // 8 - 1
    before, after = tiles[0] - 1, tiles[-1] + 1
    wanted = [before, *tiles, after] + [t for t in (0, last) if t not in (before, after)]
    row = fetch_tiles(field, taken, sem_in, wanted)
    places = [(before, 7), *[(t, r) for t in tiles for r in range(8)], (after, 0)]
    copies, cuts = [], (0, len(places) // 2, len(places))
    for k in range(2):
        for i in range(cuts[k], cuts[k + 1]):
            rows[i] = row(*places[i])
        some = pl.ds(cuts[k], cuts[k + 1] - cuts[k])
        copies.append(pltpu.make_async_copy(rows.at[some], packed.at[some], sem_out.at[k]))
        copies[-1].start()
    ends[0] = row(last, 7)
    ends[1] = row(0, 0)
    copies.append(pltpu.make_async_copy(ends, edges, sem_out.at[2]))
    copies[-1].start()
    for copy in copies:
        copy.wait()


def own_kernel(segments, groups, weight, point, field, halo, *refs):
    last = field.shape[1] // 8 - 1
    count = 3 * len(groups)
    outs, (taken, halo_rows, weights, points, sent, lined, depth, gains, sem_in, sem_out, sem_few) = (
        refs[:count],
        refs[count:],
    )
    few = [
        pltpu.make_async_copy(src, dst, sem_few.at[i])
        for i, (src, dst) in enumerate(((weight, weights), (point, points), (halo, halo_rows)))
    ]
    for copy in few:
        copy.start()
    wanted = sorted({t for tiles in segments for t in (tiles[0] - 1, *tiles, tiles[-1] + 1) if 0 <= t <= last})
    row = fetch_tiles(field, taken, sem_in, wanted)
    for copy in few:
        copy.wait()
    spread_gains(weights, gains, range(3))
    mix = mixing(points[...])
    runs, at, done, order = [], 0, 0, []
    for tiles in segments:
        places = [(tiles[0] - 1, 7), *[(t, r) for t in tiles for r in range(8)], (tiles[-1] + 1, 0)]
        for i, (t, r) in enumerate(places):
            lined[at + i] = halo_rows[0] if t < 0 else halo_rows[1] if t > last else row(t, r)
        runs.append((at, done, 8 * len(tiles)))
        at, done = at + len(places), done + 8 * len(tiles)
        order += tiles
    tap_sums(lambda s, r, c: lined[r, c, :], [[(a, a) for a in range(3)]], gains, depth, runs)
    copies = []
    for g, tiles in enumerate(groups):
        for i, tile in enumerate(tiles):
            t = order.index(tile)
            for k in range(3):
                sent[k, t] = mix_tile(mix, depth, k, t)
                to = outs[3 * g + k].at[:, pl.ds(8 * i, 8), :]
                copies.append(pltpu.make_async_copy(sent.at[k, t], to, sem_out.at[k, t]))
                copies[-1].start()
    for copy in copies:
        copy.wait()


def middle_kernel(weight, point, low, own, high, out, taken, weights, points, sent, depth, gains, sem_in, sem_out):
    copies = [
        pltpu.make_async_copy(src, dst, sem_in.at[i])
        for i, (src, dst) in enumerate(
            ((weight, weights), (point, points), (low, taken.at[0]), (own, taken.at[1]), (high, taken.at[2]))
        )
    ]
    for copy in copies:
        copy.start()
    for copy in copies[:2]:
        copy.wait()
    spread_gains(weights, gains, range(3))
    mix = mixing(points[...])
    for copy in copies[2:]:
        copy.wait()
    rows = out.shape[1]
    tap_sums(lambda s, r, c: taken[s, r, c, :], [[(a, 0)] for a in range(3)], gains, depth, [(0, 0, rows)])
    copies = []
    for t in range(rows // 8):
        sent[t] = mix_tile(mix, depth, 0, t)
        copies.append(pltpu.make_async_copy(sent.at[t], out.at[:, pl.ds(8 * t, 8), :], sem_out.at[t]))
        copies[-1].start()
    for copy in copies:
        copy.wait()


def gelu(value):
    size = jnp.abs(value) * math.sqrt(0.5)
    below = 1.0 + 0.3275911 * size
    t = pl.reciprocal(below, approx=True)
    t = t * (2.0 - below * t)
    series = 1.061405429 * t - 1.453152027
    for factor in (1.421413741, -0.284496736, 0.254829592):
        series = series * t + factor
    tail = 0.5 * (series * t) * jnp.exp(-(size * size))
    return value * jnp.where(value < 0.0, tail, 1.0 - tail)


def inverse_kernel(upper, modes, bias, x_top, x_rest, y_top, y_rest, own, middle, second, low, high, out, base, columns):
    q = pl.program_id(0)
    groups, _, y_local, _ = out.shape

    @pl.when(q == 0)
    def _():
        gy = lax.axis_index("gy")
        for g in range(groups):
            own_modes = jnp.concatenate([modes[2 * g], modes[2 * g + 1]], axis=1)
            crossed, is_real = swap_parts(own_modes)
            stack = jnp.concatenate([own_modes, jnp.where(is_real, -crossed, crossed)], axis=0)
            pair = parts(dot3((y_top[gy], y_rest[gy]), parts(stack)))
            for h in range(2):
                for k in range(2):
                    columns[h, k, pl.ds(g * y_local, y_local), :] = pair[k][:, 128 * h : 128 * h + 128]

    h, p = q // 2, q % 2
    rows = dot3((columns[h, 0], columns[h, 1]), (x_top[p], x_rest[p]))
    turn = upper + middle.shape[2]
    stop = turn + second.shape[2]
    for g in range(groups):
        plane = rows[g * y_local : (g + 1) * y_local] + bias[4 * g + q]
        base[g, 0, :upper] = plane[:upper] + own[g, 0, :upper]
        out[g, 0, upper:turn] = gelu(plane[upper:turn] + middle[g, 0])
        out[g, 0, turn:stop] = gelu(plane[turn:stop] + (second[g, 0] + (low[g, 0] + high[g, 0])))
        base[g, 0, upper:] = plane[stop:] + own[g, 0, upper:]


def finish_kernel(upper, _, base, low, high, out, sent, sem):
    tiles = base.shape[1] // 8
    gap = out.shape[1] // 8 - tiles
    copies = []
    for t in range(tiles):
        rows = pl.ds(8 * t, 8)
        sent[t] = gelu(base[:, rows, :] + (low[:, rows, :] + high[:, rows, :]))
        to = t if t < upper else t + gap
        copies.append(pltpu.make_async_copy(sent.at[t], out.at[:, pl.ds(8 * to, 8), :], sem.at[t]))
        copies[-1].start()
    for copy in copies:
        copy.wait()


def in_hbm(*arrays):
    return [pltpu.with_memory_space_constraint(a, pltpu.HBM) for a in arrays]


def params():
    return pltpu.CompilerParams(vmem_limit_bytes=VMEM_BYTES)


def cost(flops, moved):
    return pl.CostEstimate(flops=flops, bytes_accessed=moved, transcendentals=0)


def whole_block(table):
    return pl.BlockSpec(table.shape, lambda i: (0,) * table.ndim)


def by_four(array):
    return array.reshape(CH // 4, 4, *array.shape[1:])


def forward_call(field, gy, pinned):
    y_local = field.shape[1]
    tables = [*halves(x_table(False)), *halves(y_table(y_local, gy, False))]
    hbm = pl.BlockSpec(memory_space=pltpu.HBM)
    return pl.pallas_call(
        forward_kernel,
        out_shape=(pltpu.HBM if pinned else jax.ShapeDtypeStruct)((CH // 2 * MY, 4 * MX), F32),
        in_specs=[hbm] * 5,
        scratch_shapes=[
            pltpu.VMEM((4, CH // 4, y_local, NX), F32),
            pltpu.VMEM((2, 2, NX, 4 * MX), BF),
            pltpu.VMEM((2, 2 * MY, y_local), BF),
            pltpu.SemaphoreType.DMA((8,)),
        ],
        compiler_params=params(),
        cost_estimate=cost(10**8, 2**18),
        name="forward_modes",
    )(*in_hbm(by_four(field), *tables))


def filter_call(arrived, gains, gz, gy, scale):
    fwd, inv = z_tables(gz, gy, gains.shape[2], scale)
    fwd, inv = halves(fwd), halves(inv)
    return pl.pallas_call(
        filter_kernel,
        out_shape=pltpu.HBM(arrived.shape, F32),
        compiler_params=params(),
        cost_estimate=cost(4 * 10**10, 2**18),
        name="filter_modes",
    )(arrived, *in_hbm(gains, *fwd, *inv))


def inverse_call(modes, bias, own, middle, second, pair, upper, y_local, gy, scale):
    tables = [*halves(x_table(True, scale)), *halves(y_table(y_local, gy, True))]
    some = lambda rows: pl.BlockSpec((CH // 4, 1, rows, NX), lambda i: (0, i, 0, 0))
    planes = [*in_hbm(*map(by_four, (own, middle, second))), *map(by_four, pair)]
    rim = own.shape[1]
    result, base = pl.pallas_call(
        functools.partial(inverse_kernel, upper),
        out_shape=[
            jax.ShapeDtypeStruct((CH // 4, 4, y_local, NX), F32),
            jax.ShapeDtypeStruct((CH // 4, 4, rim, NX), F32),
        ],
        grid=(4,),
        in_specs=[
            whole_block(modes),
            pl.BlockSpec(memory_space=pltpu.SMEM),
            *[whole_block(t) for t in tables],
            *[some(p.shape[2]) for p in planes],
        ],
        out_specs=[some(y_local), some(rim)],
        scratch_shapes=[pltpu.VMEM((2, 2, CH // 4 * y_local, 128), BF)],
        compiler_params=params(),
        cost_estimate=cost(10**8, 2**18),
        name="inverse_modes",
    )(modes, *in_hbm(bias, *tables), *planes)
    return result.reshape(CH, y_local, NX), base.reshape(CH, rim, NX)


def finish_call(result, base, low, high, upper):
    tiles = base.shape[1] // 8
    anywhere = pl.BlockSpec(memory_space=pl.ANY)
    vmem = pl.BlockSpec(memory_space=pltpu.VMEM)
    return pl.pallas_call(
        functools.partial(finish_kernel, upper),
        out_shape=jax.ShapeDtypeStruct(result.shape, F32),
        in_specs=[anywhere] + [vmem] * 3,
        out_specs=anywhere,
        scratch_shapes=[
            pltpu.VMEM((tiles, CH, 8, NX), F32),
            pltpu.SemaphoreType.DMA((tiles,)),
        ],
        input_output_aliases={0: 0},
        compiler_params=params(),
        cost_estimate=cost(10**8, 2**18),
        name="finished_rows",
    )(result, base, low, high)


def pack_call(field, tiles):
    count = 8 * len(tiles) + 2
    fetched = len(tiles) + 4
    hbm = pl.BlockSpec(memory_space=pltpu.HBM)
    return pl.pallas_call(
        functools.partial(pack_kernel, tiles),
        out_shape=[pltpu.HBM((count, CH, NX), F32), pltpu.HBM((2, CH, NX), F32)],
        in_specs=[hbm],
        out_specs=[hbm] * 2,
        scratch_shapes=[
            pltpu.VMEM((fetched, 2, CH, 8, 128), F32),
            pltpu.VMEM((count, CH, NX), F32),
            pltpu.VMEM((2, CH, NX), F32),
            pltpu.SemaphoreType.DMA((fetched, 2)),
            pltpu.SemaphoreType.DMA((3,)),
        ],
        compiler_params=params(),
        cost_estimate=cost(10**8, 2**18),
        name="packed_rows",
    )(*in_hbm(field))


def own_call(field, halo, weight, point, segments, groups):
    tiles = sum(map(len, segments))
    rows, fetched = 8 * tiles, tiles + 2 * len(segments)
    hbm = pl.BlockSpec(memory_space=pltpu.HBM)
    shapes = [pltpu.HBM((CH, 8 * len(group), NX), F32) for group in groups for _ in range(3)]
    return pl.pallas_call(
        functools.partial(own_kernel, segments, groups),
        out_shape=shapes,
        in_specs=[hbm] * 3 + [pl.BlockSpec(memory_space=pl.ANY)],
        out_specs=[hbm] * len(shapes),
        scratch_shapes=[
            pltpu.VMEM((fetched, 2, CH, 8, 128), F32),
            pltpu.VMEM((2, CH, NX), F32),
            pltpu.VMEM((CH, 27), F32),
            pltpu.VMEM((CH, CH), F32),
            pltpu.VMEM((3, tiles, CH, 8, NX), F32),
            pltpu.VMEM((rows + 2 * len(segments), CH, NX), F32),
            pltpu.VMEM((3, rows, CH, NX), F32),
            pltpu.VMEM((27, CH, 128), F32),
            pltpu.SemaphoreType.DMA((fetched, 2)),
            pltpu.SemaphoreType.DMA((3, tiles)),
            pltpu.SemaphoreType.DMA((3,)),
        ],
        compiler_params=params(),
        cost_estimate=cost(10**8, 2**18),
        name="own_sums",
    )(*in_hbm(weight, point, field), halo)


def middle_call(weight, point, low, own, high):
    rows = own.shape[0] - 2
    hbm = pl.BlockSpec(memory_space=pltpu.HBM)
    return pl.pallas_call(
        middle_kernel,
        out_shape=pltpu.HBM((CH, rows, NX), F32),
        in_specs=[hbm] * 2 + [pl.BlockSpec(memory_space=pl.ANY)] * 3,
        out_specs=hbm,
        scratch_shapes=[
            pltpu.VMEM((3, rows + 2, CH, NX), F32),
            pltpu.VMEM((CH, 27), F32),
            pltpu.VMEM((CH, CH), F32),
            pltpu.VMEM((rows // 8, CH, 8, NX), F32),
            pltpu.VMEM((1, rows, CH, NX), F32),
            pltpu.VMEM((27, CH, 128), F32),
            pltpu.SemaphoreType.DMA((5,)),
            pltpu.SemaphoreType.DMA((rows // 8,)),
        ],
        compiler_params=params(),
        cost_estimate=cost(4 * 10**10, 2**18),
        name="middle_sums",
    )(*in_hbm(weight, point), low, *in_hbm(own), high)


def general_filter(coarse, gains, gz, gy, scale):
    j_own, n_own = gains.shape[2], gains.shape[3]
    both = ("gz", "gy")
    flat = coarse.reshape(CH // 2, MY, 2, 2, MX).transpose(3, 1, 0, 2, 4).reshape(2, MY, CH * MX)
    sent = flat.reshape(2, gy, j_own, gz, n_own).transpose(3, 1, 0, 2, 4).reshape(gz * gy, -1)
    got = lax.all_to_all(sent, both, split_axis=0, concat_axis=0, tiled=True)
    got = got.reshape(gz, gy, 2, j_own, n_own)
    c, s = (jnp.asarray(t, F32) for t in trig(kept(MZ, gz), np.arange(gz), gz))
    mul = functools.partial(jnp.einsum, precision=lax.Precision.HIGHEST)
    whole = got.sum(axis=1) * scale
    real = mul("zjn,qz->qjn", whole[:, 0], c) + mul("zjn,qz->qjn", whole[:, 1], s)
    imag = mul("zjn,qz->qjn", whole[:, 1], c) - mul("zjn,qz->qjn", whole[:, 0], s)
    real, imag = real * gains[0] - imag * gains[1], real * gains[1] + imag * gains[0]
    out = jnp.stack(
        [
            mul("qjn,qz->zjn", real, c) - mul("qjn,qz->zjn", imag, s),
            mul("qjn,qz->zjn", real, s) + mul("qjn,qz->zjn", imag, c),
        ],
        axis=1,
    )
    out = jnp.broadcast_to(out[:, None], (gz, gy, 2, j_own, n_own)).reshape(gz * gy, -1)
    back = lax.all_to_all(out, both, split_axis=0, concat_axis=0, tiled=True)
    back = back.reshape(gz, gy, 2, j_own, n_own).transpose(2, 1, 3, 0, 4)
    back = back.reshape(2, MY, CH // 2, 2, MX)
    return back.transpose(2, 1, 3, 0, 4).reshape(CH // 2, MY, 4 * MX)


def body(field, spectral_filter, depth_weight, point_weight, bias_vector):
    gz, gy = lax.axis_size("gz"), lax.axis_size("gy")
    y_local = field.shape[2]
    field = field.reshape(CH, y_local, NX)
    y_total = gy * y_local
    forward_scale = 1.0 / math.sqrt(float(NX) * y_total * gz)
    inverse_scale = 1.0 / math.sqrt(2.0 * MX * MY * MZ)

    def ring(axis, count, by):
        return [(i, (i + by) % count) for i in range(count)]

    def to_neighbours(down, up):
        return (
            lax.ppermute(down, "gz", ring("gz", gz, 1)),
            lax.ppermute(up, "gz", ring("gz", gz, -1)),
        )

    def after(value, *others):
        return lax.optimization_barrier((value, *others))[0]

    last = y_local // 8 - 1
    cut = 1 + last // 2
    first_tiles, second_tiles = tuple(range(1, cut)), tuple(range(cut, min(cut + 2, last)))
    third_tiles = (0, *range(second_tiles[-1] + 1, last + 1))
    packed, edges = pack_call(field, first_tiles)
    first_low, first_high = to_neighbours(packed, packed)
    if gy == 2:
        halo = lax.ppermute(edges, "gy", ring("gy", gy, 1))
    else:
        halo = jnp.stack(
            [
                lax.ppermute(edges[0], "gy", ring("gy", gy, 1)),
                lax.ppermute(edges[1], "gy", ring("gy", gy, -1)),
            ]
        )
    j_own, n_own = spectral_filter.shape[2], spectral_filter.shape[3]
    whole_tiles = j_own == 8 and n_own == 2 * MX
    coarse = after(forward_call(after(field, packed), gy, whole_tiles), halo)
    segments, groups = ((0,), tuple(range(cut, last + 1))), (second_tiles, third_tiles)
    down, second, up, outer_down, own, outer_up = own_call(
        after(field, coarse), halo, depth_weight, point_weight, segments, groups
    )
    if whole_tiles:
        both = ("gz", "gy")
        got = lax.all_to_all(coarse, both, split_axis=0, concat_axis=0, tiled=True)
        pair = to_neighbours(after(down, got), after(up, got))
        gains = after(spectral_filter, first_low, first_high, second)
        mark = filter_call(got, gains, gz, gy, forward_scale)
        back = lax.all_to_all(mark, both, split_axis=0, concat_axis=0, tiled=True)
        back = back.reshape(CH // 2, MY, 4 * MX)
    else:
        pair = to_neighbours(down, up)
        mark = back = general_filter(coarse, spectral_filter, gz, gy, forward_scale)
    outer_pair = to_neighbours(after(outer_down, mark), after(outer_up, mark))
    packed, *pair = lax.optimization_barrier((packed, *pair, back))[:-1]
    mixed = middle_call(depth_weight, point_weight, first_low, packed, first_high)
    result, base = inverse_call(
        back, bias_vector, own, mixed, second, pair, 8, y_local, gy, inverse_scale
    )
    result = finish_call(result, base, *outer_pair, 1)
    return result.reshape(CH, 1, y_local, NX)


def solution(mesh):
    in_specs = (P(None, "gz", "gy", None), P(None, None, "gy", "gz"), P(), P(), P())
    out_specs = P(None, "gz", "gy", None)
    return jax.shard_map(body, mesh=mesh, in_specs=in_specs, out_specs=out_specs, check_vma=False)
```

```python
import functools
import math

import jax
import jax.numpy as jnp
import ml_dtypes
import numpy as np
from jax import lax
from jax.experimental import pallas as pl
from jax.experimental.pallas import tpu as pltpu
from jax.sharding import PartitionSpec as P

NX = 256
MX = 32
MY = 16
MZ = 16
CH = 32
VMEM_BYTES = 20 * 1024 * 1024
BF = jnp.bfloat16
F32 = jnp.float32


def kept(count, total):
    series = np.arange(count)
    return np.where(series < count // 2, series, total - count + series)


def trig(freqs, places, total):
    angle = 2.0 * np.pi * ((freqs[:, None] * places[None, :]) % total) / total
    return np.cos(angle), np.sin(angle)


def halves(table):
    table = np.asarray(table, np.float64)
    top = table.astype(np.float32).astype(ml_dtypes.bfloat16)
    rest = (table - top.astype(np.float64)).astype(np.float32).astype(ml_dtypes.bfloat16)
    return jnp.asarray(top), jnp.asarray(rest)


def y_table(y_local, gy, inverse):
    out = []
    for g in range(gy):
        places = g * y_local + np.arange(y_local)
        out.append(np.concatenate(trig(kept(MY, y_local * gy), places, y_local * gy), axis=0))
    return np.stack([t.T for t in out] if inverse else out)


def x_table(inverse, scale=1.0):
    c, s = trig(np.arange(MX), np.arange(NX), NX)
    w = np.where(np.arange(MX) == 0, 1.0, 2.0)[:, None] if inverse else 1.0
    out = np.zeros((2, 2, 2, MX, NX))
    for p in range(2):
        out[p, p, 0] = w * c * scale
        out[p, p, 1] = -w * s * scale
    out = out.reshape(2, 4 * MX, NX)
    return out if inverse else out.transpose(0, 2, 1)


def z_tables(gz, gy, rows, scale):
    c, s = trig(kept(MZ, gz), np.arange(gz), gz)
    eye = np.eye(rows)
    one = np.ones(gy)
    both = np.stack([c, s])
    fwd = np.einsum("tqz,g,jk->tqjzgk", both, one, eye) * scale
    inv = np.einsum("tqz,g,jk->tzgjqk", both, one, eye)
    return fwd.reshape(2 * MZ * rows, gz * gy * rows), inv.reshape(2 * gz * gy * rows, MZ * rows)


def parts(value):
    top = value.astype(BF)
    return top, (value - top.astype(F32)).astype(BF)


def dot(a, b):
    return jnp.dot(a, b, preferred_element_type=F32)


def dot3(a, b):
    rows = a[0].shape[0]
    both = dot(jnp.concatenate([a[0], a[1]], axis=0), b[0])
    return both[:rows] + (both[rows:] + dot(a[0], b[1]))


def swap_parts(value):
    lane = lax.broadcasted_iota(jnp.int32, value.shape, 1)
    is_real = (lane // MX) % 2 == 0
    width = value.shape[1]
    return jnp.where(is_real, pltpu.roll(value, width - MX, 1), pltpu.roll(value, MX, 1)), is_real


def forward_kernel(field, x_top, x_rest, y_top, y_rest, out, taken, x_both, y_both, sem):
    gy = lax.axis_index("gy")
    few = [
        pltpu.make_async_copy(src, dst, sem.at[4 + i])
        for i, (src, dst) in enumerate(
            ((x_top, x_both.at[0]), (x_rest, x_both.at[1]), (y_top.at[gy], y_both.at[0]), (y_rest.at[gy], y_both.at[1]))
        )
    ]
    copies = [pltpu.make_async_copy(field.at[:, q], taken.at[q], sem.at[q]) for q in range(4)]
    for copy in few + copies:
        copy.start()
    for copy in few:
        copy.wait()
    groups, rows = taken.shape[1:3]
    halves_of = []
    for q in range(4):
        copies[q].wait()
        part = dot3(parts(taken[q].reshape(groups * rows, NX)), (x_both[0, q % 2], x_both[1, q % 2]))
        if q % 2:
            halves_of[-1] = halves_of[-1] + part
        else:
            halves_of.append(part)
    total = jnp.concatenate(halves_of, axis=1)
    for g in range(groups):
        both = dot3((y_both[0], y_both[1]), parts(total[g * rows : (g + 1) * rows]))
        crossed, is_real = swap_parts(both[MY:])
        modes = both[:MY] + jnp.where(is_real, crossed, -crossed)
        out[pl.ds(2 * g * MY, MY), :] = modes[:, : 4 * MX]
        out[pl.ds((2 * g + 1) * MY, MY), :] = modes[:, 4 * MX :]


def filter_kernel(arrived, gains, f_top, f_rest, i_top, i_rest, out):
    real, imag = (gains[r].reshape(-1, 2 * MX) for r in range(2))
    first, second = slice(0, MX), slice(MX, 2 * MX)
    same = jnp.concatenate([real[:, first], real[:, first], real[:, second], real[:, second]], axis=1)
    cross = jnp.concatenate([-imag[:, first], imag[:, first], -imag[:, second], imag[:, second]], axis=1)
    half = f_top.shape[0] // 2
    turned = dot3((f_top[...], f_rest[...]), parts(arrived[...]))
    crossed, is_real = swap_parts(turned[half:])
    modes = turned[:half] + jnp.where(is_real, crossed, -crossed)
    crossed, _ = swap_parts(modes)
    filtered = modes * same + crossed * cross
    half = i_top.shape[0] // 2
    back = dot3((i_top[...], i_rest[...]), parts(filtered))
    crossed, is_real = swap_parts(back[half:])
    out[...] = back[:half] + jnp.where(is_real, -crossed, crossed)


def fetch_tiles(field, taken, sems, wanted):
    pending = {}
    for k, t in enumerate(wanted):
        pending[t] = [
            pltpu.make_async_copy(
                field.at[:, pl.ds(8 * t, 8), pl.ds(128 * h, 128)], taken.at[k, h], sems.at[k, h]
            )
            for h in range(2)
        ]
        for copy in pending[t]:
            copy.start()

    def row(t, r):
        for copy in pending.pop(t, ()):
            copy.wait()
        k = wanted.index(t)
        return jnp.concatenate(
            [taken.at[k, h].reshape(CH * 8, 128)[pl.ds(r, CH, stride=8), :] for h in range(2)], axis=1
        )

    return row


def spread_gains(weights, gains, offsets):
    for k in [9 * a + j for a in offsets for j in range(9)]:
        gains[k] = jnp.broadcast_to(weights[:, k : k + 1], (CH, 128))


def mixing(points):
    down = (
        lax.broadcasted_iota(jnp.int32, (8 * CH, CH), 0) // 8
        == lax.broadcasted_iota(jnp.int32, (8 * CH, CH), 1)
    ).astype(BF)
    across = (
        lax.broadcasted_iota(jnp.int32, (CH, 8 * CH), 1) % CH
        == lax.broadcasted_iota(jnp.int32, (CH, 8 * CH), 0)
    ).astype(BF)
    same = (
        lax.broadcasted_iota(jnp.int32, (8 * CH, 8 * CH), 0) % 8
        == lax.broadcasted_iota(jnp.int32, (8 * CH, 8 * CH), 1) // CH
    )
    return tuple(
        jnp.where(same, dot(dot(down, part).astype(BF), across), 0.0).astype(BF)
        for part in parts(points)
    )


def tap_sums(load, uses, gains, depth, runs):
    def some(i, _):
        chans = pl.ds(pl.multiple_of(i * 8, 8), 8)
        wanted = sorted({a for use in uses for a, _ in use})
        gain = {k: gains[k, chans, :] for a in wanted for k in range(9 * a, 9 * a + 9)}
        for first, to, rows in runs:
            sums = {}
            for r in range(rows + 2):
                for s, use in enumerate(uses):
                    value = load(s, first + r, chans)
                    turned = (pltpu.roll(value, 1, 1), value, pltpu.roll(value, NX - 1, 1))
                    for b in range(3):
                        o = r - b
                        if o < 0 or o >= rows:
                            continue
                        for a, k in use:
                            for e in range(3):
                                for h in range(2):
                                    term = gain[a * 9 + b * 3 + e] * turned[e][:, 128 * h : 128 * h + 128]
                                    place = (o, k, h)
                                    sums[place] = sums[place] + term if place in sums else term
                if r >= 2:
                    for k in sorted({k for use in uses for _, k in use}):
                        for h in range(2):
                            depth[k, to + r - 2, chans, pl.ds(128 * h, 128)] = sums.pop((r - 2, k, h))
        return 0

    lax.fori_loop(0, CH // 8, some, 0)


def mix_tile(mix, depth, k, t):
    tile = depth[k, pl.ds(8 * t, 8)].reshape(8 * CH, NX)
    return dot3(mix, parts(tile)).reshape(CH, 8, NX)


def pack_kernel(tiles, field, packed, edges, taken, rows, ends, sem_in, sem_out):
    last = field.shape[1] // 8 - 1
    before, after = tiles[0] - 1, tiles[-1] + 1
    wanted = [before, *tiles, after] + [t for t in (0, last) if t not in (before, after)]
    row = fetch_tiles(field, taken, sem_in, wanted)
    places = [(before, 7), *[(t, r) for t in tiles for r in range(8)], (after, 0)]
    copies, cuts = [], (0, len(places) // 2, len(places))
    for k in range(2):
        for i in range(cuts[k], cuts[k + 1]):
            rows[i] = row(*places[i])
        some = pl.ds(cuts[k], cuts[k + 1] - cuts[k])
        copies.append(pltpu.make_async_copy(rows.at[some], packed.at[some], sem_out.at[k]))
        copies[-1].start()
    ends[0] = row(last, 7)
    ends[1] = row(0, 0)
    copies.append(pltpu.make_async_copy(ends, edges, sem_out.at[2]))
    copies[-1].start()
    for copy in copies:
        copy.wait()


def own_kernel(segments, groups, weight, point, field, halo, *refs):
    last = field.shape[1] // 8 - 1
    count = 3 * len(groups)
    outs, (taken, halo_rows, weights, points, sent, lined, depth, gains, sem_in, sem_out, sem_few) = (
        refs[:count],
        refs[count:],
    )
    few = [
        pltpu.make_async_copy(src, dst, sem_few.at[i])
        for i, (src, dst) in enumerate(((weight, weights), (point, points), (halo, halo_rows)))
    ]
    for copy in few:
        copy.start()
    wanted = sorted({t for tiles in segments for t in (tiles[0] - 1, *tiles, tiles[-1] + 1) if 0 <= t <= last})
    row = fetch_tiles(field, taken, sem_in, wanted)
    for copy in few:
        copy.wait()
    spread_gains(weights, gains, range(3))
    mix = mixing(points[...])
    runs, at, done, order = [], 0, 0, []
    for tiles in segments:
        places = [(tiles[0] - 1, 7), *[(t, r) for t in tiles for r in range(8)], (tiles[-1] + 1, 0)]
        for i, (t, r) in enumerate(places):
            lined[at + i] = halo_rows[0] if t < 0 else halo_rows[1] if t > last else row(t, r)
        runs.append((at, done, 8 * len(tiles)))
        at, done = at + len(places), done + 8 * len(tiles)
        order += tiles
    tap_sums(lambda s, r, c: lined[r, c, :], [[(a, a) for a in range(3)]], gains, depth, runs)
    copies = []
    for g, tiles in enumerate(groups):
        for i, tile in enumerate(tiles):
            t = order.index(tile)
            for k in range(3):
                sent[k, t] = mix_tile(mix, depth, k, t)
                to = outs[3 * g + k].at[:, pl.ds(8 * i, 8), :]
                copies.append(pltpu.make_async_copy(sent.at[k, t], to, sem_out.at[k, t]))
                copies[-1].start()
    for copy in copies:
        copy.wait()


def middle_kernel(weight, point, low, own, high, out, taken, weights, points, sent, depth, gains, sem_in, sem_out):
    copies = [
        pltpu.make_async_copy(src, dst, sem_in.at[i])
        for i, (src, dst) in enumerate(
            ((weight, weights), (point, points), (low, taken.at[0]), (own, taken.at[1]), (high, taken.at[2]))
        )
    ]
    for copy in copies:
        copy.start()
    for copy in copies[:2]:
        copy.wait()
    spread_gains(weights, gains, range(3))
    mix = mixing(points[...])
    for copy in copies[2:]:
        copy.wait()
    rows = out.shape[1]
    tap_sums(lambda s, r, c: taken[s, r, c, :], [[(a, 0)] for a in range(3)], gains, depth, [(0, 0, rows)])
    copies = []
    for t in range(rows // 8):
        sent[t] = mix_tile(mix, depth, 0, t)
        copies.append(pltpu.make_async_copy(sent.at[t], out.at[:, pl.ds(8 * t, 8), :], sem_out.at[t]))
        copies[-1].start()
    for copy in copies:
        copy.wait()


def gelu(value):
    size = jnp.abs(value) * math.sqrt(0.5)
    below = 1.0 + 0.3275911 * size
    t = pl.reciprocal(below, approx=True)
    t = t * (2.0 - below * t)
    series = 1.061405429 * t - 1.453152027
    for factor in (1.421413741, -0.284496736, 0.254829592):
        series = series * t + factor
    tail = 0.5 * (series * t) * jnp.exp(-(size * size))
    return value * jnp.where(value < 0.0, tail, 1.0 - tail)


def inverse_kernel(upper, modes, bias, x_top, x_rest, y_top, y_rest, own, middle, second, low, high, out, base, columns):
    q = pl.program_id(0)
    groups, _, y_local, _ = out.shape

    @pl.when(q == 0)
    def _():
        gy = lax.axis_index("gy")
        for g in range(groups):
            own_modes = jnp.concatenate([modes[2 * g], modes[2 * g + 1]], axis=1)
            crossed, is_real = swap_parts(own_modes)
            stack = jnp.concatenate([own_modes, jnp.where(is_real, -crossed, crossed)], axis=0)
            pair = parts(dot3((y_top[gy], y_rest[gy]), parts(stack)))
            for h in range(2):
                for k in range(2):
                    columns[h, k, pl.ds(g * y_local, y_local), :] = pair[k][:, 128 * h : 128 * h + 128]

    h, p = q // 2, q % 2
    rows = dot3((columns[h, 0], columns[h, 1]), (x_top[p], x_rest[p]))
    turn = upper + middle.shape[2]
    stop = turn + second.shape[2]
    for g in range(groups):
        plane = rows[g * y_local : (g + 1) * y_local] + bias[4 * g + q]
        base[g, 0, :upper] = plane[:upper] + own[g, 0, :upper]
        out[g, 0, upper:turn] = gelu(plane[upper:turn] + middle[g, 0])
        out[g, 0, turn:stop] = gelu(plane[turn:stop] + (second[g, 0] + (low[g, 0] + high[g, 0])))
        base[g, 0, upper:] = plane[stop:] + own[g, 0, upper:]


def finish_kernel(upper, _, base, low, high, out, sent, sem):
    tiles = base.shape[1] // 8
    gap = out.shape[1] // 8 - tiles
    copies = []
    for t in range(tiles):
        rows = pl.ds(8 * t, 8)
        sent[t] = gelu(base[:, rows, :] + (low[:, rows, :] + high[:, rows, :]))
        to = t if t < upper else t + gap
        copies.append(pltpu.make_async_copy(sent.at[t], out.at[:, pl.ds(8 * to, 8), :], sem.at[t]))
        copies[-1].start()
    for copy in copies:
        copy.wait()


def in_hbm(*arrays):
    return [pltpu.with_memory_space_constraint(a, pltpu.HBM) for a in arrays]


def params():
    return pltpu.CompilerParams(vmem_limit_bytes=VMEM_BYTES)


def cost(flops, moved):
    return pl.CostEstimate(flops=flops, bytes_accessed=moved, transcendentals=0)


def whole_block(table):
    return pl.BlockSpec(table.shape, lambda i: (0,) * table.ndim)


def by_four(array):
    return array.reshape(CH // 4, 4, *array.shape[1:])


def forward_call(field, gy, pinned):
    y_local = field.shape[1]
    tables = [*halves(x_table(False)), *halves(y_table(y_local, gy, False))]
    hbm = pl.BlockSpec(memory_space=pltpu.HBM)
    return pl.pallas_call(
        forward_kernel,
        out_shape=(pltpu.HBM if pinned else jax.ShapeDtypeStruct)((CH // 2 * MY, 4 * MX), F32),
        in_specs=[hbm] * 5,
        scratch_shapes=[
            pltpu.VMEM((4, CH // 4, y_local, NX), F32),
            pltpu.VMEM((2, 2, NX, 4 * MX), BF),
            pltpu.VMEM((2, 2 * MY, y_local), BF),
            pltpu.SemaphoreType.DMA((8,)),
        ],
        compiler_params=params(),
        cost_estimate=cost(10**8, 2**18),
        name="forward_modes",
    )(*in_hbm(by_four(field), *tables))


def filter_call(arrived, gains, gz, gy, scale):
    fwd, inv = z_tables(gz, gy, gains.shape[2], scale)
    fwd, inv = halves(fwd), halves(inv)
    return pl.pallas_call(
        filter_kernel,
        out_shape=pltpu.HBM(arrived.shape, F32),
        compiler_params=params(),
        cost_estimate=cost(4 * 10**10, 2**18),
        name="filter_modes",
    )(arrived, *in_hbm(gains, *fwd, *inv))


def inverse_call(modes, bias, own, middle, second, pair, upper, y_local, gy, scale):
    tables = [*halves(x_table(True, scale)), *halves(y_table(y_local, gy, True))]
    some = lambda rows: pl.BlockSpec((CH // 4, 1, rows, NX), lambda i: (0, i, 0, 0))
    planes = [*in_hbm(*map(by_four, (own, middle, second))), *map(by_four, pair)]
    rim = own.shape[1]
    result, base = pl.pallas_call(
        functools.partial(inverse_kernel, upper),
        out_shape=[
            jax.ShapeDtypeStruct((CH // 4, 4, y_local, NX), F32),
            jax.ShapeDtypeStruct((CH // 4, 4, rim, NX), F32),
        ],
        grid=(4,),
        in_specs=[
            whole_block(modes),
            pl.BlockSpec(memory_space=pltpu.SMEM),
            *[whole_block(t) for t in tables],
            *[some(p.shape[2]) for p in planes],
        ],
        out_specs=[some(y_local), some(rim)],
        scratch_shapes=[pltpu.VMEM((2, 2, CH // 4 * y_local, 128), BF)],
        compiler_params=params(),
        cost_estimate=cost(10**8, 2**18),
        name="inverse_modes",
    )(modes, *in_hbm(bias, *tables), *planes)
    return result.reshape(CH, y_local, NX), base.reshape(CH, rim, NX)


def finish_call(result, base, low, high, upper):
    tiles = base.shape[1] // 8
    anywhere = pl.BlockSpec(memory_space=pl.ANY)
    vmem = pl.BlockSpec(memory_space=pltpu.VMEM)
    return pl.pallas_call(
        functools.partial(finish_kernel, upper),
        out_shape=jax.ShapeDtypeStruct(result.shape, F32),
        in_specs=[anywhere] + [vmem] * 3,
        out_specs=anywhere,
        scratch_shapes=[
            pltpu.VMEM((tiles, CH, 8, NX), F32),
            pltpu.SemaphoreType.DMA((tiles,)),
        ],
        input_output_aliases={0: 0},
        compiler_params=params(),
        cost_estimate=cost(10**8, 2**18),
        name="finished_rows",
    )(result, base, low, high)


def pack_call(field, tiles):
    count = 8 * len(tiles) + 2
    fetched = len(tiles) + 4
    hbm = pl.BlockSpec(memory_space=pltpu.HBM)
    return pl.pallas_call(
        functools.partial(pack_kernel, tiles),
        out_shape=[pltpu.HBM((count, CH, NX), F32), pltpu.HBM((2, CH, NX), F32)],
        in_specs=[hbm],
        out_specs=[hbm] * 2,
        scratch_shapes=[
            pltpu.VMEM((fetched, 2, CH, 8, 128), F32),
            pltpu.VMEM((count, CH, NX), F32),
            pltpu.VMEM((2, CH, NX), F32),
            pltpu.SemaphoreType.DMA((fetched, 2)),
            pltpu.SemaphoreType.DMA((3,)),
        ],
        compiler_params=params(),
        cost_estimate=cost(10**8, 2**18),
        name="packed_rows",
    )(*in_hbm(field))


def own_call(field, halo, weight, point, segments, groups):
    tiles = sum(map(len, segments))
    rows, fetched = 8 * tiles, tiles + 2 * len(segments)
    hbm = pl.BlockSpec(memory_space=pltpu.HBM)
    shapes = [pltpu.HBM((CH, 8 * len(group), NX), F32) for group in groups for _ in range(3)]
    return pl.pallas_call(
        functools.partial(own_kernel, segments, groups),
        out_shape=shapes,
        in_specs=[hbm] * 3 + [pl.BlockSpec(memory_space=pl.ANY)],
        out_specs=[hbm] * len(shapes),
        scratch_shapes=[
            pltpu.VMEM((fetched, 2, CH, 8, 128), F32),
            pltpu.VMEM((2, CH, NX), F32),
            pltpu.VMEM((CH, 27), F32),
            pltpu.VMEM((CH, CH), F32),
            pltpu.VMEM((3, tiles, CH, 8, NX), F32),
            pltpu.VMEM((rows + 2 * len(segments), CH, NX), F32),
            pltpu.VMEM((3, rows, CH, NX), F32),
            pltpu.VMEM((27, CH, 128), F32),
            pltpu.SemaphoreType.DMA((fetched, 2)),
            pltpu.SemaphoreType.DMA((3, tiles)),
            pltpu.SemaphoreType.DMA((3,)),
        ],
        compiler_params=params(),
        cost_estimate=cost(10**8, 2**18),
        name="own_sums",
    )(*in_hbm(weight, point, field), halo)


def middle_call(weight, point, low, own, high):
    rows = own.shape[0] - 2
    hbm = pl.BlockSpec(memory_space=pltpu.HBM)
    return pl.pallas_call(
        middle_kernel,
        out_shape=pltpu.HBM((CH, rows, NX), F32),
        in_specs=[hbm] * 5,
        out_specs=hbm,
        scratch_shapes=[
            pltpu.VMEM((3, rows + 2, CH, NX), F32),
            pltpu.VMEM((CH, 27), F32),
            pltpu.VMEM((CH, CH), F32),
            pltpu.VMEM((rows // 8, CH, 8, NX), F32),
            pltpu.VMEM((1, rows, CH, NX), F32),
            pltpu.VMEM((27, CH, 128), F32),
            pltpu.SemaphoreType.DMA((5,)),
            pltpu.SemaphoreType.DMA((rows // 8,)),
        ],
        compiler_params=params(),
        cost_estimate=cost(4 * 10**10, 2**18),
        name="middle_sums",
    )(*in_hbm(weight, point, low, own, high))


def general_filter(coarse, gains, gz, gy, scale):
    j_own, n_own = gains.shape[2], gains.shape[3]
    both = ("gz", "gy")
    flat = coarse.reshape(CH // 2, MY, 2, 2, MX).transpose(3, 1, 0, 2, 4).reshape(2, MY, CH * MX)
    sent = flat.reshape(2, gy, j_own, gz, n_own).transpose(3, 1, 0, 2, 4).reshape(gz * gy, -1)
    got = lax.all_to_all(sent, both, split_axis=0, concat_axis=0, tiled=True)
    got = got.reshape(gz, gy, 2, j_own, n_own)
    c, s = (jnp.asarray(t, F32) for t in trig(kept(MZ, gz), np.arange(gz), gz))
    mul = functools.partial(jnp.einsum, precision=lax.Precision.HIGHEST)
    whole = got.sum(axis=1) * scale
    real = mul("zjn,qz->qjn", whole[:, 0], c) + mul("zjn,qz->qjn", whole[:, 1], s)
    imag = mul("zjn,qz->qjn", whole[:, 1], c) - mul("zjn,qz->qjn", whole[:, 0], s)
    real, imag = real * gains[0] - imag * gains[1], real * gains[1] + imag * gains[0]
    out = jnp.stack(
        [
            mul("qjn,qz->zjn", real, c) - mul("qjn,qz->zjn", imag, s),
            mul("qjn,qz->zjn", real, s) + mul("qjn,qz->zjn", imag, c),
        ],
        axis=1,
    )
    out = jnp.broadcast_to(out[:, None], (gz, gy, 2, j_own, n_own)).reshape(gz * gy, -1)
    back = lax.all_to_all(out, both, split_axis=0, concat_axis=0, tiled=True)
    back = back.reshape(gz, gy, 2, j_own, n_own).transpose(2, 1, 3, 0, 4)
    back = back.reshape(2, MY, CH // 2, 2, MX)
    return back.transpose(2, 1, 3, 0, 4).reshape(CH // 2, MY, 4 * MX)


def body(field, spectral_filter, depth_weight, point_weight, bias_vector):
    gz, gy = lax.axis_size("gz"), lax.axis_size("gy")
    y_local = field.shape[2]
    field = field.reshape(CH, y_local, NX)
    y_total = gy * y_local
    forward_scale = 1.0 / math.sqrt(float(NX) * y_total * gz)
    inverse_scale = 1.0 / math.sqrt(2.0 * MX * MY * MZ)

    def ring(axis, count, by):
        return [(i, (i + by) % count) for i in range(count)]

    def to_neighbours(down, up):
        return (
            lax.ppermute(down, "gz", ring("gz", gz, 1)),
            lax.ppermute(up, "gz", ring("gz", gz, -1)),
        )

    def after(value, *others):
        return lax.optimization_barrier((value, *others))[0]

    last = y_local // 8 - 1
    cut = 1 + last // 2
    first_tiles, second_tiles = tuple(range(1, cut)), tuple(range(cut, min(cut + 2, last)))
    third_tiles = (0, *range(second_tiles[-1] + 1, last + 1))
    packed, edges = pack_call(field, first_tiles)
    first_low, first_high = to_neighbours(packed, packed)
    if gy == 2:
        halo = lax.ppermute(edges, "gy", ring("gy", gy, 1))
    else:
        halo = jnp.stack(
            [
                lax.ppermute(edges[0], "gy", ring("gy", gy, 1)),
                lax.ppermute(edges[1], "gy", ring("gy", gy, -1)),
            ]
        )
    j_own, n_own = spectral_filter.shape[2], spectral_filter.shape[3]
    whole_tiles = j_own == 8 and n_own == 2 * MX
    coarse = after(forward_call(after(field, packed), gy, whole_tiles), halo)
    segments, groups = ((0,), tuple(range(cut, last + 1))), (second_tiles, third_tiles)
    down, second, up, outer_down, own, outer_up = own_call(
        after(field, coarse), halo, depth_weight, point_weight, segments, groups
    )
    if whole_tiles:
        both = ("gz", "gy")
        got = lax.all_to_all(coarse, both, split_axis=0, concat_axis=0, tiled=True)
        down, up = lax.optimization_barrier((down, up, first_low, first_high))[:2]
        pair = to_neighbours(down, up)
        gains = after(spectral_filter, first_low, first_high, second)
        mark = filter_call(got, gains, gz, gy, forward_scale)
        back = lax.all_to_all(mark, both, split_axis=0, concat_axis=0, tiled=True)
        back = back.reshape(CH // 2, MY, 4 * MX)
    else:
        pair = to_neighbours(down, up)
        mark = back = general_filter(coarse, spectral_filter, gz, gy, forward_scale)
    outer_pair = to_neighbours(after(outer_down, mark), after(outer_up, mark))
    packed, *pair = lax.optimization_barrier((packed, *pair, back))[:-1]
    mixed = middle_call(depth_weight, point_weight, first_low, packed, first_high)
    result, base = inverse_call(
        back, bias_vector, own, mixed, second, pair, 8, y_local, gy, inverse_scale
    )
    result = finish_call(result, base, *outer_pair, 1)
    return result.reshape(CH, 1, y_local, NX)


def solution(mesh):
    in_specs = (P(None, "gz", "gy", None), P(None, None, "gy", "gz"), P(), P(), P())
    out_specs = P(None, "gz", "gy", None)
    return jax.shard_map(body, mesh=mesh, in_specs=in_specs, out_specs=out_specs, check_vma=False)
```

```python
import functools
import math

import jax
import jax.numpy as jnp
import ml_dtypes
import numpy as np
from jax import lax
from jax.experimental import pallas as pl
from jax.experimental.pallas import tpu as pltpu
from jax.sharding import PartitionSpec as P

NX = 256
MX = 32
MY = 16
MZ = 16
CH = 32
VMEM_BYTES = 20 * 1024 * 1024
BF = jnp.bfloat16
F32 = jnp.float32


def kept(count, total):
    series = np.arange(count)
    return np.where(series < count // 2, series, total - count + series)


def trig(freqs, places, total):
    angle = 2.0 * np.pi * ((freqs[:, None] * places[None, :]) % total) / total
    return np.cos(angle), np.sin(angle)


def halves(table):
    table = np.asarray(table, np.float64)
    top = table.astype(np.float32).astype(ml_dtypes.bfloat16)
    rest = (table - top.astype(np.float64)).astype(np.float32).astype(ml_dtypes.bfloat16)
    return jnp.asarray(top), jnp.asarray(rest)


def y_table(y_local, gy, inverse):
    out = []
    for g in range(gy):
        places = g * y_local + np.arange(y_local)
        out.append(np.concatenate(trig(kept(MY, y_local * gy), places, y_local * gy), axis=0))
    return np.stack([t.T for t in out] if inverse else out)


def x_table(inverse, scale=1.0):
    c, s = trig(np.arange(MX), np.arange(NX), NX)
    w = np.where(np.arange(MX) == 0, 1.0, 2.0)[:, None] if inverse else 1.0
    out = np.zeros((2, 2, 2, MX, NX))
    for p in range(2):
        out[p, p, 0] = w * c * scale
        out[p, p, 1] = -w * s * scale
    out = out.reshape(2, 4 * MX, NX)
    return out if inverse else out.transpose(0, 2, 1)


def z_tables(gz, gy, rows, scale):
    c, s = trig(kept(MZ, gz), np.arange(gz), gz)
    eye = np.eye(rows)
    one = np.ones(gy)
    both = np.stack([c, s])
    fwd = np.einsum("tqz,g,jk->tqjzgk", both, one, eye) * scale
    inv = np.einsum("tqz,g,jk->tzgjqk", both, one, eye)
    return fwd.reshape(2 * MZ * rows, gz * gy * rows), inv.reshape(2 * gz * gy * rows, MZ * rows)


def parts(value):
    top = value.astype(BF)
    return top, (value - top.astype(F32)).astype(BF)


def dot(a, b):
    return jnp.dot(a, b, preferred_element_type=F32)


def dot3(a, b):
    rows = a[0].shape[0]
    both = dot(jnp.concatenate([a[0], a[1]], axis=0), b[0])
    return both[:rows] + (both[rows:] + dot(a[0], b[1]))


def swap_parts(value):
    lane = lax.broadcasted_iota(jnp.int32, value.shape, 1)
    is_real = (lane // MX) % 2 == 0
    width = value.shape[1]
    return jnp.where(is_real, pltpu.roll(value, width - MX, 1), pltpu.roll(value, MX, 1)), is_real


def forward_kernel(field, x_top, x_rest, y_top, y_rest, out, taken, x_both, y_both, sem):
    gy = lax.axis_index("gy")
    few = [
        pltpu.make_async_copy(src, dst, sem.at[4 + i])
        for i, (src, dst) in enumerate(
            ((x_top, x_both.at[0]), (x_rest, x_both.at[1]), (y_top.at[gy], y_both.at[0]), (y_rest.at[gy], y_both.at[1]))
        )
    ]
    copies = [pltpu.make_async_copy(field.at[:, q], taken.at[q], sem.at[q]) for q in range(4)]
    for copy in few + copies:
        copy.start()
    for copy in few:
        copy.wait()
    groups, rows = taken.shape[1:3]
    halves_of = []
    for q in range(4):
        copies[q].wait()
        part = dot3(parts(taken[q].reshape(groups * rows, NX)), (x_both[0, q % 2], x_both[1, q % 2]))
        if q % 2:
            halves_of[-1] = halves_of[-1] + part
        else:
            halves_of.append(part)
    total = jnp.concatenate(halves_of, axis=1)
    for g in range(groups):
        both = dot3((y_both[0], y_both[1]), parts(total[g * rows : (g + 1) * rows]))
        crossed, is_real = swap_parts(both[MY:])
        modes = both[:MY] + jnp.where(is_real, crossed, -crossed)
        out[pl.ds(2 * g * MY, MY), :] = modes[:, : 4 * MX]
        out[pl.ds((2 * g + 1) * MY, MY), :] = modes[:, 4 * MX :]


def filter_kernel(arrived, gains, f_top, f_rest, i_top, i_rest, out):
    real, imag = (gains[r].reshape(-1, 2 * MX) for r in range(2))
    first, second = slice(0, MX), slice(MX, 2 * MX)
    same = jnp.concatenate([real[:, first], real[:, first], real[:, second], real[:, second]], axis=1)
    cross = jnp.concatenate([-imag[:, first], imag[:, first], -imag[:, second], imag[:, second]], axis=1)
    half = f_top.shape[0] // 2
    turned = dot3((f_top[...], f_rest[...]), parts(arrived[...]))
    crossed, is_real = swap_parts(turned[half:])
    modes = turned[:half] + jnp.where(is_real, crossed, -crossed)
    crossed, _ = swap_parts(modes)
    filtered = modes * same + crossed * cross
    half = i_top.shape[0] // 2
    back = dot3((i_top[...], i_rest[...]), parts(filtered))
    crossed, is_real = swap_parts(back[half:])
    out[...] = back[:half] + jnp.where(is_real, -crossed, crossed)


def fetch_tiles(field, taken, sems, wanted):
    pending = {}
    for k, t in enumerate(wanted):
        pending[t] = [
            pltpu.make_async_copy(
                field.at[:, pl.ds(8 * t, 8), pl.ds(128 * h, 128)], taken.at[k, h], sems.at[k, h]
            )
            for h in range(2)
        ]
        for copy in pending[t]:
            copy.start()

    def row(t, r):
        for copy in pending.pop(t, ()):
            copy.wait()
        k = wanted.index(t)
        return jnp.concatenate(
            [taken.at[k, h].reshape(CH * 8, 128)[pl.ds(r, CH, stride=8), :] for h in range(2)], axis=1
        )

    return row


def spread_gains(weights, gains, offsets):
    for k in [9 * a + j for a in offsets for j in range(9)]:
        gains[k] = jnp.broadcast_to(weights[:, k : k + 1], (CH, 128))


def mixing(points):
    down = (
        lax.broadcasted_iota(jnp.int32, (8 * CH, CH), 0) // 8
        == lax.broadcasted_iota(jnp.int32, (8 * CH, CH), 1)
    ).astype(BF)
    across = (
        lax.broadcasted_iota(jnp.int32, (CH, 8 * CH), 1) % CH
        == lax.broadcasted_iota(jnp.int32, (CH, 8 * CH), 0)
    ).astype(BF)
    same = (
        lax.broadcasted_iota(jnp.int32, (8 * CH, 8 * CH), 0) % 8
        == lax.broadcasted_iota(jnp.int32, (8 * CH, 8 * CH), 1) // CH
    )
    return tuple(
        jnp.where(same, dot(dot(down, part).astype(BF), across), 0.0).astype(BF)
        for part in parts(points)
    )


def tap_sums(load, uses, gains, depth, runs):
    def some(i, _):
        chans = pl.ds(pl.multiple_of(i * 8, 8), 8)
        wanted = sorted({a for use in uses for a, _ in use})
        gain = {k: gains[k, chans, :] for a in wanted for k in range(9 * a, 9 * a + 9)}
        for first, to, rows in runs:
            sums = {}
            for r in range(rows + 2):
                for s, use in enumerate(uses):
                    value = load(s, first + r, chans)
                    turned = (pltpu.roll(value, 1, 1), value, pltpu.roll(value, NX - 1, 1))
                    for b in range(3):
                        o = r - b
                        if o < 0 or o >= rows:
                            continue
                        for a, k in use:
                            for e in range(3):
                                for h in range(2):
                                    term = gain[a * 9 + b * 3 + e] * turned[e][:, 128 * h : 128 * h + 128]
                                    place = (o, k, h)
                                    sums[place] = sums[place] + term if place in sums else term
                if r >= 2:
                    for k in sorted({k for use in uses for _, k in use}):
                        for h in range(2):
                            depth[k, to + r - 2, chans, pl.ds(128 * h, 128)] = sums.pop((r - 2, k, h))
        return 0

    lax.fori_loop(0, CH // 8, some, 0)


def mix_tile(mix, depth, k, t):
    tile = depth[k, pl.ds(8 * t, 8)].reshape(8 * CH, NX)
    return dot3(mix, parts(tile)).reshape(CH, 8, NX)


def pack_kernel(tiles, field, packed, edges, taken, rows, ends, sem_in, sem_out):
    last = field.shape[1] // 8 - 1
    before, after = tiles[0] - 1, tiles[-1] + 1
    wanted = [before, *tiles, after] + [t for t in (0, last) if t not in (before, after)]
    row = fetch_tiles(field, taken, sem_in, wanted)
    places = [(before, 7), *[(t, r) for t in tiles for r in range(8)], (after, 0)]
    copies, cuts = [], (0, len(places) // 2, len(places))
    for k in range(2):
        for i in range(cuts[k], cuts[k + 1]):
            rows[i] = row(*places[i])
        some = pl.ds(cuts[k], cuts[k + 1] - cuts[k])
        copies.append(pltpu.make_async_copy(rows.at[some], packed.at[some], sem_out.at[k]))
        copies[-1].start()
    ends[0] = row(last, 7)
    ends[1] = row(0, 0)
    copies.append(pltpu.make_async_copy(ends, edges, sem_out.at[2]))
    copies[-1].start()
    for copy in copies:
        copy.wait()


def own_kernel(segments, groups, weight, point, field, halo, *refs):
    last = field.shape[1] // 8 - 1
    count = 3 * len(groups)
    outs, (taken, halo_rows, weights, points, sent, lined, depth, gains, sem_in, sem_out, sem_few) = (
        refs[:count],
        refs[count:],
    )
    few = [
        pltpu.make_async_copy(src, dst, sem_few.at[i])
        for i, (src, dst) in enumerate(((weight, weights), (point, points), (halo, halo_rows)))
    ]
    for copy in few:
        copy.start()
    wanted = sorted({t for tiles in segments for t in (tiles[0] - 1, *tiles, tiles[-1] + 1) if 0 <= t <= last})
    row = fetch_tiles(field, taken, sem_in, wanted)
    for copy in few:
        copy.wait()
    spread_gains(weights, gains, range(3))
    mix = mixing(points[...])
    runs, at, done, order = [], 0, 0, []
    for tiles in segments:
        places = [(tiles[0] - 1, 7), *[(t, r) for t in tiles for r in range(8)], (tiles[-1] + 1, 0)]
        for i, (t, r) in enumerate(places):
            lined[at + i] = halo_rows[0] if t < 0 else halo_rows[1] if t > last else row(t, r)
        runs.append((at, done, 8 * len(tiles)))
        at, done = at + len(places), done + 8 * len(tiles)
        order += tiles
    tap_sums(lambda s, r, c: lined[r, c, :], [[(a, a) for a in range(3)]], gains, depth, runs)
    copies = []
    for g, tiles in enumerate(groups):
        for i, tile in enumerate(tiles):
            t = order.index(tile)
            for k in range(3):
                sent[k, t] = mix_tile(mix, depth, k, t)
                to = outs[3 * g + k].at[:, pl.ds(8 * i, 8), :]
                copies.append(pltpu.make_async_copy(sent.at[k, t], to, sem_out.at[k, t]))
                copies[-1].start()
    for copy in copies:
        copy.wait()


def middle_kernel(weight, point, low, own, high, out, taken, weights, points, sent, depth, gains, sem_in, sem_out):
    copies = [
        pltpu.make_async_copy(src, dst, sem_in.at[i])
        for i, (src, dst) in enumerate(
            ((weight, weights), (point, points), (low, taken.at[0]), (own, taken.at[1]), (high, taken.at[2]))
        )
    ]
    for copy in copies:
        copy.start()
    for copy in copies[:2]:
        copy.wait()
    spread_gains(weights, gains, range(3))
    mix = mixing(points[...])
    for copy in copies[2:]:
        copy.wait()
    rows = out.shape[1]
    tap_sums(lambda s, r, c: taken[s, r, c, :], [[(a, 0)] for a in range(3)], gains, depth, [(0, 0, rows)])
    copies = []
    for t in range(rows // 8):
        sent[t] = mix_tile(mix, depth, 0, t)
        copies.append(pltpu.make_async_copy(sent.at[t], out.at[:, pl.ds(8 * t, 8), :], sem_out.at[t]))
        copies[-1].start()
    for copy in copies:
        copy.wait()


def gelu(value):
    size = jnp.abs(value) * math.sqrt(0.5)
    below = 1.0 + 0.3275911 * size
    t = pl.reciprocal(below, approx=True)
    t = t * (2.0 - below * t)
    series = 1.061405429 * t - 1.453152027
    for factor in (1.421413741, -0.284496736, 0.254829592):
        series = series * t + factor
    tail = 0.5 * (series * t) * jnp.exp(-(size * size))
    return value * jnp.where(value < 0.0, tail, 1.0 - tail)


def inverse_kernel(upper, modes, bias, x_top, x_rest, y_top, y_rest, own, middle, second, low, high, out, base, columns):
    q = pl.program_id(0)
    groups, _, y_local, _ = out.shape

    @pl.when(q == 0)
    def _():
        gy = lax.axis_index("gy")
        for g in range(groups):
            own_modes = jnp.concatenate([modes[2 * g], modes[2 * g + 1]], axis=1)
            crossed, is_real = swap_parts(own_modes)
            stack = jnp.concatenate([own_modes, jnp.where(is_real, -crossed, crossed)], axis=0)
            pair = parts(dot3((y_top[gy], y_rest[gy]), parts(stack)))
            for h in range(2):
                for k in range(2):
                    columns[h, k, pl.ds(g * y_local, y_local), :] = pair[k][:, 128 * h : 128 * h + 128]

    h, p = q // 2, q % 2
    rows = dot3((columns[h, 0], columns[h, 1]), (x_top[p], x_rest[p]))
    turn = upper + middle.shape[2]
    stop = turn + second.shape[2]
    for g in range(groups):
        plane = rows[g * y_local : (g + 1) * y_local] + bias[4 * g + q]
        base[g, 0, :upper] = plane[:upper] + own[g, 0, :upper]
        out[g, 0, upper:turn] = gelu(plane[upper:turn] + middle[g, 0])
        out[g, 0, turn:stop] = gelu(plane[turn:stop] + (second[g, 0] + (low[g, 0] + high[g, 0])))
        base[g, 0, upper:] = plane[stop:] + own[g, 0, upper:]


def finish_kernel(upper, _, base, low, high, out, sent, sem):
    tiles = base.shape[1] // 8
    gap = out.shape[1] // 8 - tiles
    copies = []
    for t in range(tiles):
        rows = pl.ds(8 * t, 8)
        sent[t] = gelu(base[:, rows, :] + (low[:, rows, :] + high[:, rows, :]))
        to = t if t < upper else t + gap
        copies.append(pltpu.make_async_copy(sent.at[t], out.at[:, pl.ds(8 * to, 8), :], sem.at[t]))
        copies[-1].start()
    for copy in copies:
        copy.wait()


def in_hbm(*arrays):
    return [pltpu.with_memory_space_constraint(a, pltpu.HBM) for a in arrays]


def params():
    return pltpu.CompilerParams(vmem_limit_bytes=VMEM_BYTES)


def cost(flops, moved):
    return pl.CostEstimate(flops=flops, bytes_accessed=moved, transcendentals=0)


def whole_block(table):
    return pl.BlockSpec(table.shape, lambda i: (0,) * table.ndim)


def by_four(array):
    return array.reshape(CH // 4, 4, *array.shape[1:])


def forward_call(field, gy, pinned):
    y_local = field.shape[1]
    tables = [*halves(x_table(False)), *halves(y_table(y_local, gy, False))]
    hbm = pl.BlockSpec(memory_space=pltpu.HBM)
    return pl.pallas_call(
        forward_kernel,
        out_shape=(pltpu.HBM if pinned else jax.ShapeDtypeStruct)((CH // 2 * MY, 4 * MX), F32),
        in_specs=[hbm] * 5,
        scratch_shapes=[
            pltpu.VMEM((4, CH // 4, y_local, NX), F32),
            pltpu.VMEM((2, 2, NX, 4 * MX), BF),
            pltpu.VMEM((2, 2 * MY, y_local), BF),
            pltpu.SemaphoreType.DMA((8,)),
        ],
        compiler_params=params(),
        cost_estimate=cost(10**8, 2**18),
        name="forward_modes",
    )(*in_hbm(by_four(field), *tables))


def filter_call(arrived, gains, gz, gy, scale):
    fwd, inv = z_tables(gz, gy, gains.shape[2], scale)
    fwd, inv = halves(fwd), halves(inv)
    return pl.pallas_call(
        filter_kernel,
        out_shape=pltpu.HBM(arrived.shape, F32),
        compiler_params=params(),
        cost_estimate=cost(4 * 10**10, 2**18),
        name="filter_modes",
    )(arrived, *in_hbm(gains, *fwd, *inv))


def inverse_call(modes, bias, own, middle, second, pair, upper, y_local, gy, scale):
    tables = [*halves(x_table(True, scale)), *halves(y_table(y_local, gy, True))]
    some = lambda rows: pl.BlockSpec((CH // 4, 1, rows, NX), lambda i: (0, i, 0, 0))
    planes = [*in_hbm(*map(by_four, (own, middle, second))), *map(by_four, pair)]
    rim = own.shape[1]
    result, base = pl.pallas_call(
        functools.partial(inverse_kernel, upper),
        out_shape=[
            jax.ShapeDtypeStruct((CH // 4, 4, y_local, NX), F32),
            jax.ShapeDtypeStruct((CH // 4, 4, rim, NX), F32),
        ],
        grid=(4,),
        in_specs=[
            whole_block(modes),
            pl.BlockSpec(memory_space=pltpu.SMEM),
            *[whole_block(t) for t in tables],
            *[some(p.shape[2]) for p in planes],
        ],
        out_specs=[some(y_local), some(rim)],
        scratch_shapes=[pltpu.VMEM((2, 2, CH // 4 * y_local, 128), BF)],
        compiler_params=params(),
        cost_estimate=cost(10**8, 2**18),
        name="inverse_modes",
    )(modes, *in_hbm(bias, *tables), *planes)
    return result.reshape(CH, y_local, NX), base.reshape(CH, rim, NX)


def finish_call(result, base, low, high, upper):
    tiles = base.shape[1] // 8
    anywhere = pl.BlockSpec(memory_space=pl.ANY)
    vmem = pl.BlockSpec(memory_space=pltpu.VMEM)
    return pl.pallas_call(
        functools.partial(finish_kernel, upper),
        out_shape=jax.ShapeDtypeStruct(result.shape, F32),
        in_specs=[anywhere] + [vmem] * 3,
        out_specs=anywhere,
        scratch_shapes=[
            pltpu.VMEM((tiles, CH, 8, NX), F32),
            pltpu.SemaphoreType.DMA((tiles,)),
        ],
        input_output_aliases={0: 0},
        compiler_params=params(),
        cost_estimate=cost(10**8, 2**18),
        name="finished_rows",
    )(result, base, low, high)


def pack_call(field, tiles):
    count = 8 * len(tiles) + 2
    fetched = len(tiles) + 4
    hbm = pl.BlockSpec(memory_space=pltpu.HBM)
    return pl.pallas_call(
        functools.partial(pack_kernel, tiles),
        out_shape=[pltpu.HBM((count, CH, NX), F32), pltpu.HBM((2, CH, NX), F32)],
        in_specs=[hbm],
        out_specs=[hbm] * 2,
        scratch_shapes=[
            pltpu.VMEM((fetched, 2, CH, 8, 128), F32),
            pltpu.VMEM((count, CH, NX), F32),
            pltpu.VMEM((2, CH, NX), F32),
            pltpu.SemaphoreType.DMA((fetched, 2)),
            pltpu.SemaphoreType.DMA((3,)),
        ],
        compiler_params=params(),
        cost_estimate=cost(10**8, 2**18),
        name="packed_rows",
    )(*in_hbm(field))


def own_call(field, halo, weight, point, segments, groups):
    tiles = sum(map(len, segments))
    rows, fetched = 8 * tiles, tiles + 2 * len(segments)
    hbm = pl.BlockSpec(memory_space=pltpu.HBM)
    shapes = [pltpu.HBM((CH, 8 * len(group), NX), F32) for group in groups for _ in range(3)]
    return pl.pallas_call(
        functools.partial(own_kernel, segments, groups),
        out_shape=shapes,
        in_specs=[hbm] * 3 + [pl.BlockSpec(memory_space=pl.ANY)],
        out_specs=[hbm] * len(shapes),
        scratch_shapes=[
            pltpu.VMEM((fetched, 2, CH, 8, 128), F32),
            pltpu.VMEM((2, CH, NX), F32),
            pltpu.VMEM((CH, 27), F32),
            pltpu.VMEM((CH, CH), F32),
            pltpu.VMEM((3, tiles, CH, 8, NX), F32),
            pltpu.VMEM((rows + 2 * len(segments), CH, NX), F32),
            pltpu.VMEM((3, rows, CH, NX), F32),
            pltpu.VMEM((27, CH, 128), F32),
            pltpu.SemaphoreType.DMA((fetched, 2)),
            pltpu.SemaphoreType.DMA((3, tiles)),
            pltpu.SemaphoreType.DMA((3,)),
        ],
        compiler_params=params(),
        cost_estimate=cost(10**8, 2**18),
        name="own_sums",
    )(*in_hbm(weight, point, field), halo)


def middle_call(weight, point, low, own, high):
    rows = own.shape[0] - 2
    hbm = pl.BlockSpec(memory_space=pltpu.HBM)
    return pl.pallas_call(
        middle_kernel,
        out_shape=pltpu.HBM((CH, rows, NX), F32),
        in_specs=[hbm] * 5,
        out_specs=hbm,
        scratch_shapes=[
            pltpu.VMEM((3, rows + 2, CH, NX), F32),
            pltpu.VMEM((CH, 27), F32),
            pltpu.VMEM((CH, CH), F32),
            pltpu.VMEM((rows // 8, CH, 8, NX), F32),
            pltpu.VMEM((1, rows, CH, NX), F32),
            pltpu.VMEM((27, CH, 128), F32),
            pltpu.SemaphoreType.DMA((5,)),
            pltpu.SemaphoreType.DMA((rows // 8,)),
        ],
        compiler_params=params(),
        cost_estimate=cost(4 * 10**10, 2**18),
        name="middle_sums",
    )(*in_hbm(weight, point, low, own, high))


def general_filter(coarse, gains, gz, gy, scale):
    j_own, n_own = gains.shape[2], gains.shape[3]
    both = ("gz", "gy")
    flat = coarse.reshape(CH // 2, MY, 2, 2, MX).transpose(3, 1, 0, 2, 4).reshape(2, MY, CH * MX)
    sent = flat.reshape(2, gy, j_own, gz, n_own).transpose(3, 1, 0, 2, 4).reshape(gz * gy, -1)
    got = lax.all_to_all(sent, both, split_axis=0, concat_axis=0, tiled=True)
    got = got.reshape(gz, gy, 2, j_own, n_own)
    c, s = (jnp.asarray(t, F32) for t in trig(kept(MZ, gz), np.arange(gz), gz))
    mul = functools.partial(jnp.einsum, precision=lax.Precision.HIGHEST)
    whole = got.sum(axis=1) * scale
    real = mul("zjn,qz->qjn", whole[:, 0], c) + mul("zjn,qz->qjn", whole[:, 1], s)
    imag = mul("zjn,qz->qjn", whole[:, 1], c) - mul("zjn,qz->qjn", whole[:, 0], s)
    real, imag = real * gains[0] - imag * gains[1], real * gains[1] + imag * gains[0]
    out = jnp.stack(
        [
            mul("qjn,qz->zjn", real, c) - mul("qjn,qz->zjn", imag, s),
            mul("qjn,qz->zjn", real, s) + mul("qjn,qz->zjn", imag, c),
        ],
        axis=1,
    )
    out = jnp.broadcast_to(out[:, None], (gz, gy, 2, j_own, n_own)).reshape(gz * gy, -1)
    back = lax.all_to_all(out, both, split_axis=0, concat_axis=0, tiled=True)
    back = back.reshape(gz, gy, 2, j_own, n_own).transpose(2, 1, 3, 0, 4)
    back = back.reshape(2, MY, CH // 2, 2, MX)
    return back.transpose(2, 1, 3, 0, 4).reshape(CH // 2, MY, 4 * MX)


def body(field, spectral_filter, depth_weight, point_weight, bias_vector):
    gz, gy = lax.axis_size("gz"), lax.axis_size("gy")
    y_local = field.shape[2]
    field = field.reshape(CH, y_local, NX)
    y_total = gy * y_local
    forward_scale = 1.0 / math.sqrt(float(NX) * y_total * gz)
    inverse_scale = 1.0 / math.sqrt(2.0 * MX * MY * MZ)

    def ring(axis, count, by):
        return [(i, (i + by) % count) for i in range(count)]

    def to_neighbours(down, up):
        return (
            lax.ppermute(down, "gz", ring("gz", gz, 1)),
            lax.ppermute(up, "gz", ring("gz", gz, -1)),
        )

    def after(value, *others):
        return lax.optimization_barrier((value, *others))[0]

    last = y_local // 8 - 1
    cut = 1 + last // 2
    first_tiles, second_tiles = tuple(range(1, cut)), tuple(range(cut, min(cut + 2, last)))
    third_tiles = (0, *range(second_tiles[-1] + 1, last + 1))
    packed, edges = pack_call(field, first_tiles)
    first_low, first_high = to_neighbours(packed, packed)
    if gy == 2:
        halo = lax.ppermute(edges, "gy", ring("gy", gy, 1))
    else:
        halo = jnp.stack(
            [
                lax.ppermute(edges[0], "gy", ring("gy", gy, 1)),
                lax.ppermute(edges[1], "gy", ring("gy", gy, -1)),
            ]
        )
    j_own, n_own = spectral_filter.shape[2], spectral_filter.shape[3]
    whole_tiles = j_own == 8 and n_own == 2 * MX
    coarse = after(forward_call(after(field, packed), gy, whole_tiles), halo)
    segments, groups = ((0,), tuple(range(cut, last + 1))), (second_tiles, third_tiles)
    down, second, up, outer_down, own, outer_up = own_call(
        after(field, coarse), halo, depth_weight, point_weight, segments, groups
    )
    if whole_tiles:
        both = ("gz", "gy")
        got = lax.all_to_all(coarse, both, split_axis=0, concat_axis=0, tiled=True)
        pair = to_neighbours(down, up)
        gains = after(spectral_filter, first_low, first_high, second)
        mark = filter_call(got, gains, gz, gy, forward_scale)
        back = lax.all_to_all(mark, both, split_axis=0, concat_axis=0, tiled=True)
        back = back.reshape(CH // 2, MY, 4 * MX)
    else:
        pair = to_neighbours(down, up)
        mark = back = general_filter(coarse, spectral_filter, gz, gy, forward_scale)
    outer_pair = to_neighbours(after(outer_down, mark), after(outer_up, mark))
    packed, *pair = lax.optimization_barrier((packed, *pair))
    mixed = middle_call(depth_weight, point_weight, first_low, packed, first_high)
    result, base = inverse_call(
        back, bias_vector, own, mixed, second, pair, 8, y_local, gy, inverse_scale
    )
    result = finish_call(result, base, *outer_pair, 1)
    return result.reshape(CH, 1, y_local, NX)


def solution(mesh):
    in_specs = (P(None, "gz", "gy", None), P(None, None, "gy", "gz"), P(), P(), P())
    out_specs = P(None, "gz", "gy", None)
    return jax.shard_map(body, mesh=mesh, in_specs=in_specs, out_specs=out_specs, check_vma=False)
```

```python
import functools
import math

import jax
import jax.numpy as jnp
import ml_dtypes
import numpy as np
from jax import lax
from jax.experimental import pallas as pl
from jax.experimental.pallas import tpu as pltpu
from jax.sharding import PartitionSpec as P

NX = 256
MX = 32
MY = 16
MZ = 16
CH = 32
VMEM_BYTES = 20 * 1024 * 1024
BF = jnp.bfloat16
F32 = jnp.float32


def kept(count, total):
    series = np.arange(count)
    return np.where(series < count // 2, series, total - count + series)


def trig(freqs, places, total):
    angle = 2.0 * np.pi * ((freqs[:, None] * places[None, :]) % total) / total
    return np.cos(angle), np.sin(angle)


def halves(table):
    table = np.asarray(table, np.float64)
    top = table.astype(np.float32).astype(ml_dtypes.bfloat16)
    rest = (table - top.astype(np.float64)).astype(np.float32).astype(ml_dtypes.bfloat16)
    return jnp.asarray(top), jnp.asarray(rest)


def y_table(y_local, gy, inverse):
    out = []
    for g in range(gy):
        places = g * y_local + np.arange(y_local)
        out.append(np.concatenate(trig(kept(MY, y_local * gy), places, y_local * gy), axis=0))
    return np.stack([t.T for t in out] if inverse else out)


def x_table(inverse, scale=1.0):
    c, s = trig(np.arange(MX), np.arange(NX), NX)
    w = np.where(np.arange(MX) == 0, 1.0, 2.0)[:, None] if inverse else 1.0
    out = np.zeros((2, 2, 2, MX, NX))
    for p in range(2):
        out[p, p, 0] = w * c * scale
        out[p, p, 1] = -w * s * scale
    out = out.reshape(2, 4 * MX, NX)
    return out if inverse else out.transpose(0, 2, 1)


def z_tables(gz, gy, rows, scale):
    c, s = trig(kept(MZ, gz), np.arange(gz), gz)
    eye = np.eye(rows)
    one = np.ones(gy)
    both = np.stack([c, s])
    fwd = np.einsum("tqz,g,jk->tqjzgk", both, one, eye) * scale
    inv = np.einsum("tqz,g,jk->tzgjqk", both, one, eye)
    return fwd.reshape(2 * MZ * rows, gz * gy * rows), inv.reshape(2 * gz * gy * rows, MZ * rows)


def parts(value):
    top = value.astype(BF)
    return top, (value - top.astype(F32)).astype(BF)


def dot(a, b):
    return jnp.dot(a, b, preferred_element_type=F32)


def dot3(a, b):
    rows = a[0].shape[0]
    both = dot(jnp.concatenate([a[0], a[1]], axis=0), b[0])
    return both[:rows] + (both[rows:] + dot(a[0], b[1]))


def swap_parts(value):
    lane = lax.broadcasted_iota(jnp.int32, value.shape, 1)
    is_real = (lane // MX) % 2 == 0
    width = value.shape[1]
    return jnp.where(is_real, pltpu.roll(value, width - MX, 1), pltpu.roll(value, MX, 1)), is_real


def forward_kernel(field, x_top, x_rest, y_top, y_rest, out, taken, x_both, y_both, sem):
    gy = lax.axis_index("gy")
    few = [
        pltpu.make_async_copy(src, dst, sem.at[4 + i])
        for i, (src, dst) in enumerate(
            ((x_top, x_both.at[0]), (x_rest, x_both.at[1]), (y_top.at[gy], y_both.at[0]), (y_rest.at[gy], y_both.at[1]))
        )
    ]
    copies = [pltpu.make_async_copy(field.at[:, q], taken.at[q], sem.at[q]) for q in range(4)]
    for copy in few + copies:
        copy.start()
    for copy in few:
        copy.wait()
    groups, rows = taken.shape[1:3]
    halves_of = []
    for q in range(4):
        copies[q].wait()
        part = dot3(parts(taken[q].reshape(groups * rows, NX)), (x_both[0, q % 2], x_both[1, q % 2]))
        if q % 2:
            halves_of[-1] = halves_of[-1] + part
        else:
            halves_of.append(part)
    total = jnp.concatenate(halves_of, axis=1)
    for g in range(groups):
        both = dot3((y_both[0], y_both[1]), parts(total[g * rows : (g + 1) * rows]))
        crossed, is_real = swap_parts(both[MY:])
        modes = both[:MY] + jnp.where(is_real, crossed, -crossed)
        out[pl.ds(2 * g * MY, MY), :] = modes[:, : 4 * MX]
        out[pl.ds((2 * g + 1) * MY, MY), :] = modes[:, 4 * MX :]


def filter_kernel(arrived, gains, f_top, f_rest, i_top, i_rest, out):
    real, imag = (gains[r].reshape(-1, 2 * MX) for r in range(2))
    first, second = slice(0, MX), slice(MX, 2 * MX)
    same = jnp.concatenate([real[:, first], real[:, first], real[:, second], real[:, second]], axis=1)
    cross = jnp.concatenate([-imag[:, first], imag[:, first], -imag[:, second], imag[:, second]], axis=1)
    half = f_top.shape[0] // 2
    turned = dot3((f_top[...], f_rest[...]), parts(arrived[...]))
    crossed, is_real = swap_parts(turned[half:])
    modes = turned[:half] + jnp.where(is_real, crossed, -crossed)
    crossed, _ = swap_parts(modes)
    filtered = modes * same + crossed * cross
    half = i_top.shape[0] // 2
    back = dot3((i_top[...], i_rest[...]), parts(filtered))
    crossed, is_real = swap_parts(back[half:])
    out[...] = back[:half] + jnp.where(is_real, -crossed, crossed)


def fetch_tiles(field, taken, sems, wanted):
    pending = {}
    for k, t in enumerate(wanted):
        pending[t] = [
            pltpu.make_async_copy(
                field.at[:, pl.ds(8 * t, 8), pl.ds(128 * h, 128)], taken.at[k, h], sems.at[k, h]
            )
            for h in range(2)
        ]
        for copy in pending[t]:
            copy.start()

    def row(t, r):
        for copy in pending.pop(t, ()):
            copy.wait()
        k = wanted.index(t)
        return jnp.concatenate(
            [taken.at[k, h].reshape(CH * 8, 128)[pl.ds(r, CH, stride=8), :] for h in range(2)], axis=1
        )

    return row


def spread_gains(weights, gains, offsets):
    for k in [9 * a + j for a in offsets for j in range(9)]:
        gains[k] = jnp.broadcast_to(weights[:, k : k + 1], (CH, 128))


def mixing(points):
    down = (
        lax.broadcasted_iota(jnp.int32, (8 * CH, CH), 0) // 8
        == lax.broadcasted_iota(jnp.int32, (8 * CH, CH), 1)
    ).astype(BF)
    across = (
        lax.broadcasted_iota(jnp.int32, (CH, 8 * CH), 1) % CH
        == lax.broadcasted_iota(jnp.int32, (CH, 8 * CH), 0)
    ).astype(BF)
    same = (
        lax.broadcasted_iota(jnp.int32, (8 * CH, 8 * CH), 0) % 8
        == lax.broadcasted_iota(jnp.int32, (8 * CH, 8 * CH), 1) // CH
    )
    return tuple(
        jnp.where(same, dot(dot(down, part).astype(BF), across), 0.0).astype(BF)
        for part in parts(points)
    )


def tap_sums(load, uses, gains, depth, runs):
    def some(i, _):
        chans = pl.ds(pl.multiple_of(i * 8, 8), 8)
        wanted = sorted({a for use in uses for a, _ in use})
        gain = {k: gains[k, chans, :] for a in wanted for k in range(9 * a, 9 * a + 9)}
        for first, to, rows in runs:
            sums = {}
            for r in range(rows + 2):
                for s, use in enumerate(uses):
                    value = load(s, first + r, chans)
                    turned = (pltpu.roll(value, 1, 1), value, pltpu.roll(value, NX - 1, 1))
                    for b in range(3):
                        o = r - b
                        if o < 0 or o >= rows:
                            continue
                        for a, k in use:
                            for e in range(3):
                                for h in range(2):
                                    term = gain[a * 9 + b * 3 + e] * turned[e][:, 128 * h : 128 * h + 128]
                                    place = (o, k, h)
                                    sums[place] = sums[place] + term if place in sums else term
                if r >= 2:
                    for k in sorted({k for use in uses for _, k in use}):
                        for h in range(2):
                            depth[k, to + r - 2, chans, pl.ds(128 * h, 128)] = sums.pop((r - 2, k, h))
        return 0

    lax.fori_loop(0, CH // 8, some, 0)


def mix_tile(mix, depth, k, t):
    tile = depth[k, pl.ds(8 * t, 8)].reshape(8 * CH, NX)
    return dot3(mix, parts(tile)).reshape(CH, 8, NX)


def pack_kernel(tiles, field, packed, edges, taken, rows, ends, sem_in, sem_out):
    last = field.shape[1] // 8 - 1
    before, after = tiles[0] - 1, tiles[-1] + 1
    wanted = [before, *tiles, after] + [t for t in (0, last) if t not in (before, after)]
    row = fetch_tiles(field, taken, sem_in, wanted)
    places = [(before, 7), *[(t, r) for t in tiles for r in range(8)], (after, 0)]
    copies, cuts = [], (0, len(places) // 2, len(places))
    for k in range(2):
        for i in range(cuts[k], cuts[k + 1]):
            rows[i] = row(*places[i])
        some = pl.ds(cuts[k], cuts[k + 1] - cuts[k])
        copies.append(pltpu.make_async_copy(rows.at[some], packed.at[some], sem_out.at[k]))
        copies[-1].start()
    ends[0] = row(last, 7)
    ends[1] = row(0, 0)
    copies.append(pltpu.make_async_copy(ends, edges, sem_out.at[2]))
    copies[-1].start()
    for copy in copies:
        copy.wait()


def own_kernel(segments, groups, weight, point, field, halo, *refs):
    last = field.shape[1] // 8 - 1
    count = 3 * len(groups)
    outs, (taken, halo_rows, weights, points, sent, lined, depth, gains, sem_in, sem_out, sem_few) = (
        refs[:count],
        refs[count:],
    )
    few = [
        pltpu.make_async_copy(src, dst, sem_few.at[i])
        for i, (src, dst) in enumerate(((weight, weights), (point, points), (halo, halo_rows)))
    ]
    for copy in few:
        copy.start()
    wanted = sorted({t for tiles in segments for t in (tiles[0] - 1, *tiles, tiles[-1] + 1) if 0 <= t <= last})
    row = fetch_tiles(field, taken, sem_in, wanted)
    for copy in few:
        copy.wait()
    spread_gains(weights, gains, range(3))
    mix = mixing(points[...])
    runs, at, done, order = [], 0, 0, []
    for tiles in segments:
        places = [(tiles[0] - 1, 7), *[(t, r) for t in tiles for r in range(8)], (tiles[-1] + 1, 0)]
        for i, (t, r) in enumerate(places):
            lined[at + i] = halo_rows[0] if t < 0 else halo_rows[1] if t > last else row(t, r)
        runs.append((at, done, 8 * len(tiles)))
        at, done = at + len(places), done + 8 * len(tiles)
        order += tiles
    tap_sums(lambda s, r, c: lined[r, c, :], [[(a, a) for a in range(3)]], gains, depth, runs)
    copies = []
    for g, tiles in enumerate(groups):
        for i, tile in enumerate(tiles):
            t = order.index(tile)
            for k in range(3):
                sent[k, t] = mix_tile(mix, depth, k, t)
                to = outs[3 * g + k].at[:, pl.ds(8 * i, 8), :]
                copies.append(pltpu.make_async_copy(sent.at[k, t], to, sem_out.at[k, t]))
                copies[-1].start()
    for copy in copies:
        copy.wait()


def middle_kernel(weight, point, low, own, high, out, taken, weights, points, sent, depth, gains, sem_in, sem_out):
    copies = [
        pltpu.make_async_copy(src, dst, sem_in.at[i])
        for i, (src, dst) in enumerate(
            ((weight, weights), (point, points), (low, taken.at[0]), (own, taken.at[1]), (high, taken.at[2]))
        )
    ]
    for copy in copies:
        copy.start()
    for copy in copies[:2]:
        copy.wait()
    spread_gains(weights, gains, range(3))
    mix = mixing(points[...])
    for copy in copies[2:]:
        copy.wait()
    rows = out.shape[1]
    tap_sums(lambda s, r, c: taken[s, r, c, :], [[(a, 0)] for a in range(3)], gains, depth, [(0, 0, rows)])
    copies = []
    for t in range(rows // 8):
        sent[t] = mix_tile(mix, depth, 0, t)
        copies.append(pltpu.make_async_copy(sent.at[t], out.at[:, pl.ds(8 * t, 8), :], sem_out.at[t]))
        copies[-1].start()
    for copy in copies:
        copy.wait()


def gelu(value):
    size = jnp.abs(value) * math.sqrt(0.5)
    below = 1.0 + 0.3275911 * size
    t = pl.reciprocal(below, approx=True)
    t = t * (2.0 - below * t)
    series = 1.061405429 * t - 1.453152027
    for factor in (1.421413741, -0.284496736, 0.254829592):
        series = series * t + factor
    tail = 0.5 * (series * t) * jnp.exp(-(size * size))
    return value * jnp.where(value < 0.0, tail, 1.0 - tail)


def inverse_kernel(upper, modes, bias, x_top, x_rest, y_top, y_rest, own, middle, second, low, high, out, base, columns):
    q = pl.program_id(0)
    groups, _, y_local, _ = out.shape

    @pl.when(q == 0)
    def _():
        gy = lax.axis_index("gy")
        for g in range(groups):
            own_modes = jnp.concatenate([modes[2 * g], modes[2 * g + 1]], axis=1)
            crossed, is_real = swap_parts(own_modes)
            stack = jnp.concatenate([own_modes, jnp.where(is_real, -crossed, crossed)], axis=0)
            pair = parts(dot3((y_top[gy], y_rest[gy]), parts(stack)))
            for h in range(2):
                for k in range(2):
                    columns[h, k, pl.ds(g * y_local, y_local), :] = pair[k][:, 128 * h : 128 * h + 128]

    h, p = q // 2, q % 2
    rows = dot3((columns[h, 0], columns[h, 1]), (x_top[p], x_rest[p]))
    turn = upper + middle.shape[2]
    stop = turn + second.shape[2]
    for g in range(groups):
        plane = rows[g * y_local : (g + 1) * y_local] + bias[4 * g + q]
        base[g, 0, :upper] = plane[:upper] + own[g, 0, :upper]
        out[g, 0, upper:turn] = gelu(plane[upper:turn] + middle[g, 0])
        out[g, 0, turn:stop] = gelu(plane[turn:stop] + (second[g, 0] + (low[g, 0] + high[g, 0])))
        base[g, 0, upper:] = plane[stop:] + own[g, 0, upper:]


def finish_kernel(upper, _, base, low, high, out, sent, sem):
    tiles = base.shape[1] // 8
    gap = out.shape[1] // 8 - tiles
    copies = []
    for t in range(tiles):
        rows = pl.ds(8 * t, 8)
        sent[t] = gelu(base[:, rows, :] + (low[:, rows, :] + high[:, rows, :]))
        to = t if t < upper else t + gap
        copies.append(pltpu.make_async_copy(sent.at[t], out.at[:, pl.ds(8 * to, 8), :], sem.at[t]))
        copies[-1].start()
    for copy in copies:
        copy.wait()


def in_hbm(*arrays):
    return [pltpu.with_memory_space_constraint(a, pltpu.HBM) for a in arrays]


def params():
    return pltpu.CompilerParams(vmem_limit_bytes=VMEM_BYTES)


def cost(flops, moved):
    return pl.CostEstimate(flops=flops, bytes_accessed=moved, transcendentals=0)


def whole_block(table):
    return pl.BlockSpec(table.shape, lambda i: (0,) * table.ndim)


def by_four(array):
    return array.reshape(CH // 4, 4, *array.shape[1:])


def forward_call(field, gy, pinned):
    y_local = field.shape[1]
    tables = [*halves(x_table(False)), *halves(y_table(y_local, gy, False))]
    hbm = pl.BlockSpec(memory_space=pltpu.HBM)
    return pl.pallas_call(
        forward_kernel,
        out_shape=(pltpu.HBM if pinned else jax.ShapeDtypeStruct)((CH // 2 * MY, 4 * MX), F32),
        in_specs=[hbm] * 5,
        scratch_shapes=[
            pltpu.VMEM((4, CH // 4, y_local, NX), F32),
            pltpu.VMEM((2, 2, NX, 4 * MX), BF),
            pltpu.VMEM((2, 2 * MY, y_local), BF),
            pltpu.SemaphoreType.DMA((8,)),
        ],
        compiler_params=params(),
        cost_estimate=cost(10**8, 2**18),
        name="forward_modes",
    )(*in_hbm(by_four(field), *tables))


def filter_call(arrived, gains, gz, gy, scale):
    fwd, inv = z_tables(gz, gy, gains.shape[2], scale)
    fwd, inv = halves(fwd), halves(inv)
    return pl.pallas_call(
        filter_kernel,
        out_shape=pltpu.HBM(arrived.shape, F32),
        compiler_params=params(),
        cost_estimate=cost(4 * 10**10, 2**18),
        name="filter_modes",
    )(arrived, *in_hbm(gains, *fwd, *inv))


def inverse_call(modes, bias, own, middle, second, pair, upper, y_local, gy, scale):
    tables = [*halves(x_table(True, scale)), *halves(y_table(y_local, gy, True))]
    some = lambda rows: pl.BlockSpec((CH // 4, 1, rows, NX), lambda i: (0, i, 0, 0))
    planes = [*in_hbm(*map(by_four, (own, middle, second))), *map(by_four, pair)]
    rim = own.shape[1]
    result, base = pl.pallas_call(
        functools.partial(inverse_kernel, upper),
        out_shape=[
            jax.ShapeDtypeStruct((CH // 4, 4, y_local, NX), F32),
            jax.ShapeDtypeStruct((CH // 4, 4, rim, NX), F32),
        ],
        grid=(4,),
        in_specs=[
            whole_block(modes),
            pl.BlockSpec(memory_space=pltpu.SMEM),
            *[whole_block(t) for t in tables],
            *[some(p.shape[2]) for p in planes],
        ],
        out_specs=[some(y_local), some(rim)],
        scratch_shapes=[pltpu.VMEM((2, 2, CH // 4 * y_local, 128), BF)],
        compiler_params=params(),
        cost_estimate=cost(10**8, 2**18),
        name="inverse_modes",
    )(modes, *in_hbm(bias, *tables), *planes)
    return result.reshape(CH, y_local, NX), base.reshape(CH, rim, NX)


def finish_call(result, base, low, high, upper):
    tiles = base.shape[1] // 8
    anywhere = pl.BlockSpec(memory_space=pl.ANY)
    vmem = pl.BlockSpec(memory_space=pltpu.VMEM)
    return pl.pallas_call(
        functools.partial(finish_kernel, upper),
        out_shape=jax.ShapeDtypeStruct(result.shape, F32),
        in_specs=[anywhere] + [vmem] * 3,
        out_specs=anywhere,
        scratch_shapes=[
            pltpu.VMEM((tiles, CH, 8, NX), F32),
            pltpu.SemaphoreType.DMA((tiles,)),
        ],
        input_output_aliases={0: 0},
        compiler_params=params(),
        cost_estimate=cost(10**8, 2**18),
        name="finished_rows",
    )(result, base, low, high)


def pack_call(field, tiles):
    count = 8 * len(tiles) + 2
    fetched = len(tiles) + 4
    hbm = pl.BlockSpec(memory_space=pltpu.HBM)
    return pl.pallas_call(
        functools.partial(pack_kernel, tiles),
        out_shape=[pltpu.HBM((count, CH, NX), F32), pltpu.HBM((2, CH, NX), F32)],
        in_specs=[hbm],
        out_specs=[hbm] * 2,
        scratch_shapes=[
            pltpu.VMEM((fetched, 2, CH, 8, 128), F32),
            pltpu.VMEM((count, CH, NX), F32),
            pltpu.VMEM((2, CH, NX), F32),
            pltpu.SemaphoreType.DMA((fetched, 2)),
            pltpu.SemaphoreType.DMA((3,)),
        ],
        compiler_params=params(),
        cost_estimate=cost(10**8, 2**18),
        name="packed_rows",
    )(*in_hbm(field))


def own_call(field, halo, weight, point, segments, groups):
    tiles = sum(map(len, segments))
    rows, fetched = 8 * tiles, tiles + 2 * len(segments)
    hbm = pl.BlockSpec(memory_space=pltpu.HBM)
    shapes = [pltpu.HBM((CH, 8 * len(group), NX), F32) for group in groups for _ in range(3)]
    return pl.pallas_call(
        functools.partial(own_kernel, segments, groups),
        out_shape=shapes,
        in_specs=[hbm] * 3 + [pl.BlockSpec(memory_space=pl.ANY)],
        out_specs=[hbm] * len(shapes),
        scratch_shapes=[
            pltpu.VMEM((fetched, 2, CH, 8, 128), F32),
            pltpu.VMEM((2, CH, NX), F32),
            pltpu.VMEM((CH, 27), F32),
            pltpu.VMEM((CH, CH), F32),
            pltpu.VMEM((3, tiles, CH, 8, NX), F32),
            pltpu.VMEM((rows + 2 * len(segments), CH, NX), F32),
            pltpu.VMEM((3, rows, CH, NX), F32),
            pltpu.VMEM((27, CH, 128), F32),
            pltpu.SemaphoreType.DMA((fetched, 2)),
            pltpu.SemaphoreType.DMA((3, tiles)),
            pltpu.SemaphoreType.DMA((3,)),
        ],
        compiler_params=params(),
        cost_estimate=cost(10**8, 2**18),
        name="own_sums",
    )(*in_hbm(weight, point, field), halo)


def middle_call(weight, point, low, own, high):
    rows = own.shape[0] - 2
    hbm = pl.BlockSpec(memory_space=pltpu.HBM)
    return pl.pallas_call(
        middle_kernel,
        out_shape=pltpu.HBM((CH, rows, NX), F32),
        in_specs=[hbm] * 5,
        out_specs=hbm,
        scratch_shapes=[
            pltpu.VMEM((3, rows + 2, CH, NX), F32),
            pltpu.VMEM((CH, 27), F32),
            pltpu.VMEM((CH, CH), F32),
            pltpu.VMEM((rows // 8, CH, 8, NX), F32),
            pltpu.VMEM((1, rows, CH, NX), F32),
            pltpu.VMEM((27, CH, 128), F32),
            pltpu.SemaphoreType.DMA((5,)),
            pltpu.SemaphoreType.DMA((rows // 8,)),
        ],
        compiler_params=params(),
        cost_estimate=cost(4 * 10**10, 2**18),
        name="middle_sums",
    )(*in_hbm(weight, point, low, own, high))


def general_filter(coarse, gains, gz, gy, scale):
    j_own, n_own = gains.shape[2], gains.shape[3]
    both = ("gz", "gy")
    flat = coarse.reshape(CH // 2, MY, 2, 2, MX).transpose(3, 1, 0, 2, 4).reshape(2, MY, CH * MX)
    sent = flat.reshape(2, gy, j_own, gz, n_own).transpose(3, 1, 0, 2, 4).reshape(gz * gy, -1)
    got = lax.all_to_all(sent, both, split_axis=0, concat_axis=0, tiled=True)
    got = got.reshape(gz, gy, 2, j_own, n_own)
    c, s = (jnp.asarray(t, F32) for t in trig(kept(MZ, gz), np.arange(gz), gz))
    mul = functools.partial(jnp.einsum, precision=lax.Precision.HIGHEST)
    whole = got.sum(axis=1) * scale
    real = mul("zjn,qz->qjn", whole[:, 0], c) + mul("zjn,qz->qjn", whole[:, 1], s)
    imag = mul("zjn,qz->qjn", whole[:, 1], c) - mul("zjn,qz->qjn", whole[:, 0], s)
    real, imag = real * gains[0] - imag * gains[1], real * gains[1] + imag * gains[0]
    out = jnp.stack(
        [
            mul("qjn,qz->zjn", real, c) - mul("qjn,qz->zjn", imag, s),
            mul("qjn,qz->zjn", real, s) + mul("qjn,qz->zjn", imag, c),
        ],
        axis=1,
    )
    out = jnp.broadcast_to(out[:, None], (gz, gy, 2, j_own, n_own)).reshape(gz * gy, -1)
    back = lax.all_to_all(out, both, split_axis=0, concat_axis=0, tiled=True)
    back = back.reshape(gz, gy, 2, j_own, n_own).transpose(2, 1, 3, 0, 4)
    back = back.reshape(2, MY, CH // 2, 2, MX)
    return back.transpose(2, 1, 3, 0, 4).reshape(CH // 2, MY, 4 * MX)


def body(field, spectral_filter, depth_weight, point_weight, bias_vector):
    gz, gy = lax.axis_size("gz"), lax.axis_size("gy")
    y_local = field.shape[2]
    field = field.reshape(CH, y_local, NX)
    y_total = gy * y_local
    forward_scale = 1.0 / math.sqrt(float(NX) * y_total * gz)
    inverse_scale = 1.0 / math.sqrt(2.0 * MX * MY * MZ)

    def ring(axis, count, by):
        return [(i, (i + by) % count) for i in range(count)]

    def to_neighbours(down, up):
        return (
            lax.ppermute(down, "gz", ring("gz", gz, 1)),
            lax.ppermute(up, "gz", ring("gz", gz, -1)),
        )

    def after(value, *others):
        return lax.optimization_barrier((value, *others))[0]

    last = y_local // 8 - 1
    cut = 1 + last // 2
    first_tiles, second_tiles = tuple(range(1, cut)), tuple(range(cut, min(cut + 2, last)))
    third_tiles = (0, *range(second_tiles[-1] + 1, last + 1))
    packed, edges = pack_call(field, first_tiles)
    first_low, first_high = to_neighbours(packed, packed)
    if gy == 2:
        halo = lax.ppermute(edges, "gy", ring("gy", gy, 1))
    else:
        halo = jnp.stack(
            [
                lax.ppermute(edges[0], "gy", ring("gy", gy, 1)),
                lax.ppermute(edges[1], "gy", ring("gy", gy, -1)),
            ]
        )
    j_own, n_own = spectral_filter.shape[2], spectral_filter.shape[3]
    whole_tiles = j_own == 8 and n_own == 2 * MX
    coarse = after(forward_call(after(field, packed), gy, whole_tiles), halo)
    segments, groups = ((0,), tuple(range(cut, last + 1))), (second_tiles, third_tiles)
    down, second, up, outer_down, own, outer_up = own_call(
        after(field, coarse), halo, depth_weight, point_weight, segments, groups
    )
    if whole_tiles:
        both = ("gz", "gy")
        got = lax.all_to_all(coarse, both, split_axis=0, concat_axis=0, tiled=True)
        down, up = lax.optimization_barrier((down, up, first_low, first_high))[:2]
        pair = to_neighbours(down, up)
        gains = after(spectral_filter, first_low, first_high, second)
        mark = filter_call(got, gains, gz, gy, forward_scale)
        back = lax.all_to_all(mark, both, split_axis=0, concat_axis=0, tiled=True)
        back = back.reshape(CH // 2, MY, 4 * MX)
    else:
        pair = to_neighbours(down, up)
        mark = back = general_filter(coarse, spectral_filter, gz, gy, forward_scale)
    outer_pair = to_neighbours(after(outer_down, mark), after(outer_up, mark))
    packed, *pair = lax.optimization_barrier((packed, *pair))
    mixed = middle_call(depth_weight, point_weight, first_low, packed, first_high)
    result, base = inverse_call(
        back, bias_vector, own, mixed, second, pair, 8, y_local, gy, inverse_scale
    )
    result = finish_call(result, base, *outer_pair, 1)
    return result.reshape(CH, 1, y_local, NX)


def solution(mesh):
    in_specs = (P(None, "gz", "gy", None), P(None, None, "gy", "gz"), P(), P(), P())
    out_specs = P(None, "gz", "gy", None)
    return jax.shard_map(body, mesh=mesh, in_specs=in_specs, out_specs=out_specs, check_vma=False)
```

```python
import functools
import math

import jax
import jax.numpy as jnp
import ml_dtypes
import numpy as np
from jax import lax
from jax.experimental import pallas as pl
from jax.experimental.pallas import tpu as pltpu
from jax.sharding import PartitionSpec as P

NX = 256
MX = 32
MY = 16
MZ = 16
CH = 32
VMEM_BYTES = 20 * 1024 * 1024
BF = jnp.bfloat16
F32 = jnp.float32


def kept(count, total):
    series = np.arange(count)
    return np.where(series < count // 2, series, total - count + series)


def trig(freqs, places, total):
    angle = 2.0 * np.pi * ((freqs[:, None] * places[None, :]) % total) / total
    return np.cos(angle), np.sin(angle)


def halves(table):
    table = np.asarray(table, np.float64)
    top = table.astype(np.float32).astype(ml_dtypes.bfloat16)
    rest = (table - top.astype(np.float64)).astype(np.float32).astype(ml_dtypes.bfloat16)
    return jnp.asarray(top), jnp.asarray(rest)


def y_table(y_local, gy, inverse):
    out = []
    for g in range(gy):
        places = g * y_local + np.arange(y_local)
        out.append(np.concatenate(trig(kept(MY, y_local * gy), places, y_local * gy), axis=0))
    return np.stack([t.T for t in out] if inverse else out)


def x_table(inverse, scale=1.0):
    c, s = trig(np.arange(MX), np.arange(NX), NX)
    w = np.where(np.arange(MX) == 0, 1.0, 2.0)[:, None] if inverse else 1.0
    out = np.zeros((2, 2, 2, MX, NX))
    for p in range(2):
        out[p, p, 0] = w * c * scale
        out[p, p, 1] = -w * s * scale
    out = out.reshape(2, 4 * MX, NX)
    return out if inverse else out.transpose(0, 2, 1)


def z_tables(gz, gy, rows, scale):
    c, s = trig(kept(MZ, gz), np.arange(gz), gz)
    eye = np.eye(rows)
    one = np.ones(gy)
    both = np.stack([c, s])
    fwd = np.einsum("tqz,g,jk->tqjzgk", both, one, eye) * scale
    inv = np.einsum("tqz,g,jk->tzgjqk", both, one, eye)
    return fwd.reshape(2 * MZ * rows, gz * gy * rows), inv.reshape(2 * gz * gy * rows, MZ * rows)


def parts(value):
    top = value.astype(BF)
    return top, (value - top.astype(F32)).astype(BF)


def dot(a, b):
    return jnp.dot(a, b, preferred_element_type=F32)


def dot3(a, b):
    rows = a[0].shape[0]
    both = dot(jnp.concatenate([a[0], a[1]], axis=0), b[0])
    return both[:rows] + (both[rows:] + dot(a[0], b[1]))


def swap_parts(value):
    lane = lax.broadcasted_iota(jnp.int32, value.shape, 1)
    is_real = (lane // MX) % 2 == 0
    width = value.shape[1]
    return jnp.where(is_real, pltpu.roll(value, width - MX, 1), pltpu.roll(value, MX, 1)), is_real


def forward_kernel(field, x_top, x_rest, y_top, y_rest, out, taken, x_both, y_both, sem):
    gy = lax.axis_index("gy")
    few = [
        pltpu.make_async_copy(src, dst, sem.at[4 + i])
        for i, (src, dst) in enumerate(
            ((x_top, x_both.at[0]), (x_rest, x_both.at[1]), (y_top.at[gy], y_both.at[0]), (y_rest.at[gy], y_both.at[1]))
        )
    ]
    copies = [pltpu.make_async_copy(field.at[:, q], taken.at[q], sem.at[q]) for q in range(4)]
    for copy in few + copies:
        copy.start()
    for copy in few:
        copy.wait()
    groups, rows = taken.shape[1:3]
    halves_of = []
    for q in range(4):
        copies[q].wait()
        part = dot3(parts(taken[q].reshape(groups * rows, NX)), (x_both[0, q % 2], x_both[1, q % 2]))
        if q % 2:
            halves_of[-1] = halves_of[-1] + part
        else:
            halves_of.append(part)
    total = jnp.concatenate(halves_of, axis=1)
    for g in range(groups):
        both = dot3((y_both[0], y_both[1]), parts(total[g * rows : (g + 1) * rows]))
        crossed, is_real = swap_parts(both[MY:])
        modes = both[:MY] + jnp.where(is_real, crossed, -crossed)
        out[pl.ds(2 * g * MY, MY), :] = modes[:, : 4 * MX]
        out[pl.ds((2 * g + 1) * MY, MY), :] = modes[:, 4 * MX :]


def filter_kernel(arrived, gains, f_top, f_rest, i_top, i_rest, out):
    real, imag = (gains[r].reshape(-1, 2 * MX) for r in range(2))
    first, second = slice(0, MX), slice(MX, 2 * MX)
    same = jnp.concatenate([real[:, first], real[:, first], real[:, second], real[:, second]], axis=1)
    cross = jnp.concatenate([-imag[:, first], imag[:, first], -imag[:, second], imag[:, second]], axis=1)
    half = f_top.shape[0] // 2
    turned = dot3((f_top[...], f_rest[...]), parts(arrived[...]))
    crossed, is_real = swap_parts(turned[half:])
    modes = turned[:half] + jnp.where(is_real, crossed, -crossed)
    crossed, _ = swap_parts(modes)
    filtered = modes * same + crossed * cross
    half = i_top.shape[0] // 2
    back = dot3((i_top[...], i_rest[...]), parts(filtered))
    crossed, is_real = swap_parts(back[half:])
    out[...] = back[:half] + jnp.where(is_real, -crossed, crossed)


def fetch_tiles(field, taken, sems, wanted):
    pending = {}
    for k, t in enumerate(wanted):
        pending[t] = [
            pltpu.make_async_copy(
                field.at[:, pl.ds(8 * t, 8), pl.ds(128 * h, 128)], taken.at[k, h], sems.at[k, h]
            )
            for h in range(2)
        ]
        for copy in pending[t]:
            copy.start()

    def row(t, r):
        for copy in pending.pop(t, ()):
            copy.wait()
        k = wanted.index(t)
        return jnp.concatenate(
            [taken.at[k, h].reshape(CH * 8, 128)[pl.ds(r, CH, stride=8), :] for h in range(2)], axis=1
        )

    return row


def spread_gains(weights, gains, offsets):
    for k in [9 * a + j for a in offsets for j in range(9)]:
        gains[k] = jnp.broadcast_to(weights[:, k : k + 1], (CH, 128))


def mixing(points):
    down = (
        lax.broadcasted_iota(jnp.int32, (8 * CH, CH), 0) // 8
        == lax.broadcasted_iota(jnp.int32, (8 * CH, CH), 1)
    ).astype(BF)
    across = (
        lax.broadcasted_iota(jnp.int32, (CH, 8 * CH), 1) % CH
        == lax.broadcasted_iota(jnp.int32, (CH, 8 * CH), 0)
    ).astype(BF)
    same = (
        lax.broadcasted_iota(jnp.int32, (8 * CH, 8 * CH), 0) % 8
        == lax.broadcasted_iota(jnp.int32, (8 * CH, 8 * CH), 1) // CH
    )
    return tuple(
        jnp.where(same, dot(dot(down, part).astype(BF), across), 0.0).astype(BF)
        for part in parts(points)
    )


def tap_sums(load, uses, gains, depth, runs):
    def some(i, _):
        chans = pl.ds(pl.multiple_of(i * 8, 8), 8)
        wanted = sorted({a for use in uses for a, _ in use})
        gain = {k: gains[k, chans, :] for a in wanted for k in range(9 * a, 9 * a + 9)}
        for first, to, rows in runs:
            sums = {}
            for r in range(rows + 2):
                for s, use in enumerate(uses):
                    value = load(s, first + r, chans)
                    turned = (pltpu.roll(value, 1, 1), value, pltpu.roll(value, NX - 1, 1))
                    for b in range(3):
                        o = r - b
                        if o < 0 or o >= rows:
                            continue
                        for a, k in use:
                            for e in range(3):
                                for h in range(2):
                                    term = gain[a * 9 + b * 3 + e] * turned[e][:, 128 * h : 128 * h + 128]
                                    place = (o, k, h)
                                    sums[place] = sums[place] + term if place in sums else term
                if r >= 2:
                    for k in sorted({k for use in uses for _, k in use}):
                        for h in range(2):
                            depth[k, to + r - 2, chans, pl.ds(128 * h, 128)] = sums.pop((r - 2, k, h))
        return 0

    lax.fori_loop(0, CH // 8, some, 0)


def mix_tile(mix, depth, k, t):
    tile = depth[k, pl.ds(8 * t, 8)].reshape(8 * CH, NX)
    return dot3(mix, parts(tile)).reshape(CH, 8, NX)


def pack_kernel(tiles, field, packed, edges, taken, rows, ends, sem_in, sem_out):
    last = field.shape[1] // 8 - 1
    before, after = tiles[0] - 1, tiles[-1] + 1
    wanted = [before, *tiles, after] + [t for t in (0, last) if t not in (before, after)]
    row = fetch_tiles(field, taken, sem_in, wanted)
    places = [(before, 7), *[(t, r) for t in tiles for r in range(8)], (after, 0)]
    copies, cuts = [], (0, len(places) // 2, len(places))
    for k in range(2):
        for i in range(cuts[k], cuts[k + 1]):
            rows[i] = row(*places[i])
        some = pl.ds(cuts[k], cuts[k + 1] - cuts[k])
        copies.append(pltpu.make_async_copy(rows.at[some], packed.at[some], sem_out.at[k]))
        copies[-1].start()
    ends[0] = row(last, 7)
    ends[1] = row(0, 0)
    copies.append(pltpu.make_async_copy(ends, edges, sem_out.at[2]))
    copies[-1].start()
    for copy in copies:
        copy.wait()


def own_kernel(segments, groups, weight, point, field, halo, *refs):
    last = field.shape[1] // 8 - 1
    count = 3 * len(groups)
    outs, (taken, halo_rows, weights, points, sent, lined, depth, gains, sem_in, sem_out, sem_few) = (
        refs[:count],
        refs[count:],
    )
    few = [
        pltpu.make_async_copy(src, dst, sem_few.at[i])
        for i, (src, dst) in enumerate(((weight, weights), (point, points), (halo, halo_rows)))
    ]
    for copy in few:
        copy.start()
    wanted = sorted({t for tiles in segments for t in (tiles[0] - 1, *tiles, tiles[-1] + 1) if 0 <= t <= last})
    row = fetch_tiles(field, taken, sem_in, wanted)
    for copy in few:
        copy.wait()
    spread_gains(weights, gains, range(3))
    mix = mixing(points[...])
    runs, at, done, order = [], 0, 0, []
    for tiles in segments:
        places = [(tiles[0] - 1, 7), *[(t, r) for t in tiles for r in range(8)], (tiles[-1] + 1, 0)]
        for i, (t, r) in enumerate(places):
            lined[at + i] = halo_rows[0] if t < 0 else halo_rows[1] if t > last else row(t, r)
        runs.append((at, done, 8 * len(tiles)))
        at, done = at + len(places), done + 8 * len(tiles)
        order += tiles
    tap_sums(lambda s, r, c: lined[r, c, :], [[(a, a) for a in range(3)]], gains, depth, runs)
    copies = []
    for g, tiles in enumerate(groups):
        for i, tile in enumerate(tiles):
            t = order.index(tile)
            for k in range(3):
                sent[k, t] = mix_tile(mix, depth, k, t)
                to = outs[3 * g + k].at[:, pl.ds(8 * i, 8), :]
                copies.append(pltpu.make_async_copy(sent.at[k, t], to, sem_out.at[k, t]))
                copies[-1].start()
    for copy in copies:
        copy.wait()


def middle_kernel(weight, point, low, own, high, out, taken, weights, points, sent, depth, gains, sem_in, sem_out):
    copies = [
        pltpu.make_async_copy(src, dst, sem_in.at[i])
        for i, (src, dst) in enumerate(
            ((weight, weights), (point, points), (low, taken.at[0]), (own, taken.at[1]), (high, taken.at[2]))
        )
    ]
    for copy in copies:
        copy.start()
    for copy in copies[:2]:
        copy.wait()
    spread_gains(weights, gains, range(3))
    mix = mixing(points[...])
    for copy in copies[2:]:
        copy.wait()
    rows = out.shape[1]
    tap_sums(lambda s, r, c: taken[s, r, c, :], [[(a, 0)] for a in range(3)], gains, depth, [(0, 0, rows)])
    copies = []
    for t in range(rows // 8):
        sent[t] = mix_tile(mix, depth, 0, t)
        copies.append(pltpu.make_async_copy(sent.at[t], out.at[:, pl.ds(8 * t, 8), :], sem_out.at[t]))
        copies[-1].start()
    for copy in copies:
        copy.wait()


def gelu(value):
    size = jnp.abs(value) * math.sqrt(0.5)
    below = 1.0 + 0.3275911 * size
    t = pl.reciprocal(below, approx=True)
    t = t * (2.0 - below * t)
    series = 1.061405429 * t - 1.453152027
    for factor in (1.421413741, -0.284496736, 0.254829592):
        series = series * t + factor
    tail = 0.5 * (series * t) * jnp.exp(-(size * size))
    return value * jnp.where(value < 0.0, tail, 1.0 - tail)


def inverse_kernel(upper, modes, bias, x_top, x_rest, y_top, y_rest, own, middle, second, low, high, out, base, columns):
    q = pl.program_id(0)
    groups, _, y_local, _ = out.shape

    @pl.when(q == 0)
    def _():
        gy = lax.axis_index("gy")
        for g in range(groups):
            own_modes = jnp.concatenate([modes[2 * g], modes[2 * g + 1]], axis=1)
            crossed, is_real = swap_parts(own_modes)
            stack = jnp.concatenate([own_modes, jnp.where(is_real, -crossed, crossed)], axis=0)
            pair = parts(dot3((y_top[gy], y_rest[gy]), parts(stack)))
            for h in range(2):
                for k in range(2):
                    columns[h, k, pl.ds(g * y_local, y_local), :] = pair[k][:, 128 * h : 128 * h + 128]

    h, p = q // 2, q % 2
    rows = dot3((columns[h, 0], columns[h, 1]), (x_top[p], x_rest[p]))
    turn = upper + middle.shape[2]
    stop = turn + second.shape[2]
    for g in range(groups):
        plane = rows[g * y_local : (g + 1) * y_local] + bias[4 * g + q]
        base[g, 0, :upper] = plane[:upper] + own[g, 0, :upper]
        out[g, 0, upper:turn] = gelu(plane[upper:turn] + middle[g, 0])
        out[g, 0, turn:stop] = gelu(plane[turn:stop] + (second[g, 0] + (low[g, 0] + high[g, 0])))
        base[g, 0, upper:] = plane[stop:] + own[g, 0, upper:]


def finish_kernel(upper, _, base, low, high, out, sent, sem):
    tiles = base.shape[1] // 8
    gap = out.shape[1] // 8 - tiles
    copies = []
    for t in range(tiles):
        rows = pl.ds(8 * t, 8)
        sent[t] = gelu(base[:, rows, :] + (low[:, rows, :] + high[:, rows, :]))
        to = t if t < upper else t + gap
        copies.append(pltpu.make_async_copy(sent.at[t], out.at[:, pl.ds(8 * to, 8), :], sem.at[t]))
        copies[-1].start()
    for copy in copies:
        copy.wait()


def in_hbm(*arrays):
    return [pltpu.with_memory_space_constraint(a, pltpu.HBM) for a in arrays]


def params():
    return pltpu.CompilerParams(vmem_limit_bytes=VMEM_BYTES)


def cost(flops, moved):
    return pl.CostEstimate(flops=flops, bytes_accessed=moved, transcendentals=0)


def whole_block(table):
    return pl.BlockSpec(table.shape, lambda i: (0,) * table.ndim)


def by_four(array):
    return array.reshape(CH // 4, 4, *array.shape[1:])


def forward_call(field, gy, pinned):
    y_local = field.shape[1]
    tables = [*halves(x_table(False)), *halves(y_table(y_local, gy, False))]
    hbm = pl.BlockSpec(memory_space=pltpu.HBM)
    return pl.pallas_call(
        forward_kernel,
        out_shape=(pltpu.HBM if pinned else jax.ShapeDtypeStruct)((CH // 2 * MY, 4 * MX), F32),
        in_specs=[hbm] * 5,
        scratch_shapes=[
            pltpu.VMEM((4, CH // 4, y_local, NX), F32),
            pltpu.VMEM((2, 2, NX, 4 * MX), BF),
            pltpu.VMEM((2, 2 * MY, y_local), BF),
            pltpu.SemaphoreType.DMA((8,)),
        ],
        compiler_params=params(),
        cost_estimate=cost(10**8, 2**18),
        name="forward_modes",
    )(*in_hbm(by_four(field), *tables))


def filter_call(arrived, gains, gz, gy, scale):
    fwd, inv = z_tables(gz, gy, gains.shape[2], scale)
    fwd, inv = halves(fwd), halves(inv)
    return pl.pallas_call(
        filter_kernel,
        out_shape=pltpu.HBM(arrived.shape, F32),
        compiler_params=params(),
        cost_estimate=cost(4 * 10**10, 2**18),
        name="filter_modes",
    )(arrived, *in_hbm(gains, *fwd, *inv))


def inverse_call(modes, bias, own, middle, second, pair, upper, y_local, gy, scale):
    tables = [*halves(x_table(True, scale)), *halves(y_table(y_local, gy, True))]
    some = lambda rows: pl.BlockSpec((CH // 4, 1, rows, NX), lambda i: (0, i, 0, 0))
    planes = [*in_hbm(*map(by_four, (own, middle, second))), *map(by_four, pair)]
    rim = own.shape[1]
    result, base = pl.pallas_call(
        functools.partial(inverse_kernel, upper),
        out_shape=[
            jax.ShapeDtypeStruct((CH // 4, 4, y_local, NX), F32),
            jax.ShapeDtypeStruct((CH // 4, 4, rim, NX), F32),
        ],
        grid=(4,),
        in_specs=[
            whole_block(modes),
            pl.BlockSpec(memory_space=pltpu.SMEM),
            *[whole_block(t) for t in tables],
            *[some(p.shape[2]) for p in planes],
        ],
        out_specs=[some(y_local), some(rim)],
        scratch_shapes=[pltpu.VMEM((2, 2, CH // 4 * y_local, 128), BF)],
        compiler_params=params(),
        cost_estimate=cost(10**8, 2**18),
        name="inverse_modes",
    )(modes, *in_hbm(bias, *tables), *planes)
    return result.reshape(CH, y_local, NX), base.reshape(CH, rim, NX)


def finish_call(result, base, low, high, upper):
    tiles = base.shape[1] // 8
    anywhere = pl.BlockSpec(memory_space=pl.ANY)
    vmem = pl.BlockSpec(memory_space=pltpu.VMEM)
    return pl.pallas_call(
        functools.partial(finish_kernel, upper),
        out_shape=jax.ShapeDtypeStruct(result.shape, F32),
        in_specs=[anywhere] + [vmem] * 3,
        out_specs=anywhere,
        scratch_shapes=[
            pltpu.VMEM((tiles, CH, 8, NX), F32),
            pltpu.SemaphoreType.DMA((tiles,)),
        ],
        input_output_aliases={0: 0},
        compiler_params=params(),
        cost_estimate=cost(10**8, 2**18),
        name="finished_rows",
    )(result, base, low, high)


def pack_call(field, tiles):
    count = 8 * len(tiles) + 2
    fetched = len(tiles) + 4
    hbm = pl.BlockSpec(memory_space=pltpu.HBM)
    return pl.pallas_call(
        functools.partial(pack_kernel, tiles),
        out_shape=[pltpu.HBM((count, CH, NX), F32), pltpu.HBM((2, CH, NX), F32)],
        in_specs=[hbm],
        out_specs=[hbm] * 2,
        scratch_shapes=[
            pltpu.VMEM((fetched, 2, CH, 8, 128), F32),
            pltpu.VMEM((count, CH, NX), F32),
            pltpu.VMEM((2, CH, NX), F32),
            pltpu.SemaphoreType.DMA((fetched, 2)),
            pltpu.SemaphoreType.DMA((3,)),
        ],
        compiler_params=params(),
        cost_estimate=cost(10**8, 2**18),
        name="packed_rows",
    )(*in_hbm(field))


def own_call(field, halo, weight, point, segments, groups):
    tiles = sum(map(len, segments))
    rows, fetched = 8 * tiles, tiles + 2 * len(segments)
    hbm = pl.BlockSpec(memory_space=pltpu.HBM)
    shapes = [pltpu.HBM((CH, 8 * len(group), NX), F32) for group in groups for _ in range(3)]
    return pl.pallas_call(
        functools.partial(own_kernel, segments, groups),
        out_shape=shapes,
        in_specs=[hbm] * 3 + [pl.BlockSpec(memory_space=pl.ANY)],
        out_specs=[hbm] * len(shapes),
        scratch_shapes=[
            pltpu.VMEM((fetched, 2, CH, 8, 128), F32),
            pltpu.VMEM((2, CH, NX), F32),
            pltpu.VMEM((CH, 27), F32),
            pltpu.VMEM((CH, CH), F32),
            pltpu.VMEM((3, tiles, CH, 8, NX), F32),
            pltpu.VMEM((rows + 2 * len(segments), CH, NX), F32),
            pltpu.VMEM((3, rows, CH, NX), F32),
            pltpu.VMEM((27, CH, 128), F32),
            pltpu.SemaphoreType.DMA((fetched, 2)),
            pltpu.SemaphoreType.DMA((3, tiles)),
            pltpu.SemaphoreType.DMA((3,)),
        ],
        compiler_params=params(),
        cost_estimate=cost(10**8, 2**18),
        name="own_sums",
    )(*in_hbm(weight, point, field), halo)


def middle_call(weight, point, low, own, high):
    rows = own.shape[0] - 2
    hbm = pl.BlockSpec(memory_space=pltpu.HBM)
    return pl.pallas_call(
        middle_kernel,
        out_shape=pltpu.HBM((CH, rows, NX), F32),
        in_specs=[hbm] * 5,
        out_specs=hbm,
        scratch_shapes=[
            pltpu.VMEM((3, rows + 2, CH, NX), F32),
            pltpu.VMEM((CH, 27), F32),
            pltpu.VMEM((CH, CH), F32),
            pltpu.VMEM((rows // 8, CH, 8, NX), F32),
            pltpu.VMEM((1, rows, CH, NX), F32),
            pltpu.VMEM((27, CH, 128), F32),
            pltpu.SemaphoreType.DMA((5,)),
            pltpu.SemaphoreType.DMA((rows // 8,)),
        ],
        compiler_params=params(),
        cost_estimate=cost(4 * 10**10, 2**18),
        name="middle_sums",
    )(*in_hbm(weight, point, low, own, high))


def general_filter(coarse, gains, gz, gy, scale):
    j_own, n_own = gains.shape[2], gains.shape[3]
    both = ("gz", "gy")
    flat = coarse.reshape(CH // 2, MY, 2, 2, MX).transpose(3, 1, 0, 2, 4).reshape(2, MY, CH * MX)
    sent = flat.reshape(2, gy, j_own, gz, n_own).transpose(3, 1, 0, 2, 4).reshape(gz * gy, -1)
    got = lax.all_to_all(sent, both, split_axis=0, concat_axis=0, tiled=True)
    got = got.reshape(gz, gy, 2, j_own, n_own)
    c, s = (jnp.asarray(t, F32) for t in trig(kept(MZ, gz), np.arange(gz), gz))
    mul = functools.partial(jnp.einsum, precision=lax.Precision.HIGHEST)
    whole = got.sum(axis=1) * scale
    real = mul("zjn,qz->qjn", whole[:, 0], c) + mul("zjn,qz->qjn", whole[:, 1], s)
    imag = mul("zjn,qz->qjn", whole[:, 1], c) - mul("zjn,qz->qjn", whole[:, 0], s)
    real, imag = real * gains[0] - imag * gains[1], real * gains[1] + imag * gains[0]
    out = jnp.stack(
        [
            mul("qjn,qz->zjn", real, c) - mul("qjn,qz->zjn", imag, s),
            mul("qjn,qz->zjn", real, s) + mul("qjn,qz->zjn", imag, c),
        ],
        axis=1,
    )
    out = jnp.broadcast_to(out[:, None], (gz, gy, 2, j_own, n_own)).reshape(gz * gy, -1)
    back = lax.all_to_all(out, both, split_axis=0, concat_axis=0, tiled=True)
    back = back.reshape(gz, gy, 2, j_own, n_own).transpose(2, 1, 3, 0, 4)
    back = back.reshape(2, MY, CH // 2, 2, MX)
    return back.transpose(2, 1, 3, 0, 4).reshape(CH // 2, MY, 4 * MX)


def body(field, spectral_filter, depth_weight, point_weight, bias_vector):
    gz, gy = lax.axis_size("gz"), lax.axis_size("gy")
    y_local = field.shape[2]
    field = field.reshape(CH, y_local, NX)
    y_total = gy * y_local
    forward_scale = 1.0 / math.sqrt(float(NX) * y_total * gz)
    inverse_scale = 1.0 / math.sqrt(2.0 * MX * MY * MZ)

    def ring(axis, count, by):
        return [(i, (i + by) % count) for i in range(count)]

    def to_neighbours(down, up):
        return (
            lax.ppermute(down, "gz", ring("gz", gz, 1)),
            lax.ppermute(up, "gz", ring("gz", gz, -1)),
        )

    def after(value, *others):
        return lax.optimization_barrier((value, *others))[0]

    last = y_local // 8 - 1
    cut = 1 + last // 2
    first_tiles, second_tiles = tuple(range(1, cut)), tuple(range(cut, min(cut + 2, last)))
    third_tiles = (0, *range(second_tiles[-1] + 1, last + 1))
    packed, edges = pack_call(field, first_tiles)
    first_low, first_high = to_neighbours(packed, packed)
    if gy == 2:
        halo = lax.ppermute(edges, "gy", ring("gy", gy, 1))
    else:
        halo = jnp.stack(
            [
                lax.ppermute(edges[0], "gy", ring("gy", gy, 1)),
                lax.ppermute(edges[1], "gy", ring("gy", gy, -1)),
            ]
        )
    j_own, n_own = spectral_filter.shape[2], spectral_filter.shape[3]
    whole_tiles = j_own == 8 and n_own == 2 * MX
    coarse = after(forward_call(after(field, packed), gy, whole_tiles), halo)
    segments, groups = ((0,), tuple(range(cut, last + 1))), (second_tiles, third_tiles)
    down, second, up, outer_down, own, outer_up = own_call(
        after(field, coarse), halo, depth_weight, point_weight, segments, groups
    )
    if whole_tiles:
        both = ("gz", "gy")
        got = lax.all_to_all(coarse, both, split_axis=0, concat_axis=0, tiled=True)
        down, up = lax.optimization_barrier((down, up, first_low))[:2]
        pair = to_neighbours(down, up)
        gains = after(spectral_filter, first_low, first_high, second)
        mark = filter_call(got, gains, gz, gy, forward_scale)
        back = lax.all_to_all(mark, both, split_axis=0, concat_axis=0, tiled=True)
        back = back.reshape(CH // 2, MY, 4 * MX)
    else:
        pair = to_neighbours(down, up)
        mark = back = general_filter(coarse, spectral_filter, gz, gy, forward_scale)
    outer_pair = to_neighbours(after(outer_down, mark), after(outer_up, mark))
    packed, *pair = lax.optimization_barrier((packed, *pair))
    mixed = middle_call(depth_weight, point_weight, first_low, packed, first_high)
    result, base = inverse_call(
        back, bias_vector, own, mixed, second, pair, 8, y_local, gy, inverse_scale
    )
    result = finish_call(result, base, *outer_pair, 1)
    return result.reshape(CH, 1, y_local, NX)


def solution(mesh):
    in_specs = (P(None, "gz", "gy", None), P(None, None, "gy", "gz"), P(), P(), P())
    out_specs = P(None, "gz", "gy", None)
    return jax.shard_map(body, mesh=mesh, in_specs=in_specs, out_specs=out_specs, check_vma=False)
```

```python
import functools
import math

import jax
import jax.numpy as jnp
import ml_dtypes
import numpy as np
from jax import lax
from jax.experimental import pallas as pl
from jax.experimental.pallas import tpu as pltpu
from jax.sharding import PartitionSpec as P

NX = 256
MX = 32
MY = 16
MZ = 16
CH = 32
VMEM_BYTES = 20 * 1024 * 1024
ALL_VMEM_BYTES = 63 * 1024 * 1024
BF = jnp.bfloat16
F32 = jnp.float32


def kept(count, total):
    series = np.arange(count)
    return np.where(series < count // 2, series, total - count + series)


def trig(freqs, places, total):
    angle = 2.0 * np.pi * ((freqs[:, None] * places[None, :]) % total) / total
    return np.cos(angle), np.sin(angle)


def halves(table):
    table = np.asarray(table, np.float64)
    top = table.astype(np.float32).astype(ml_dtypes.bfloat16)
    rest = (table - top.astype(np.float64)).astype(np.float32).astype(ml_dtypes.bfloat16)
    return jnp.asarray(top), jnp.asarray(rest)


def y_table(y_local, gy, inverse):
    out = []
    for g in range(gy):
        places = g * y_local + np.arange(y_local)
        out.append(np.concatenate(trig(kept(MY, y_local * gy), places, y_local * gy), axis=0))
    return np.stack([t.T for t in out] if inverse else out)


def x_table(inverse, scale=1.0):
    c, s = trig(np.arange(MX), np.arange(NX), NX)
    w = np.where(np.arange(MX) == 0, 1.0, 2.0)[:, None] if inverse else 1.0
    out = np.zeros((2, 2, 2, MX, NX))
    for p in range(2):
        out[p, p, 0] = w * c * scale
        out[p, p, 1] = -w * s * scale
    out = out.reshape(2, 4 * MX, NX)
    return out if inverse else out.transpose(0, 2, 1)


def z_tables(gz, gy, rows, scale):
    c, s = trig(kept(MZ, gz), np.arange(gz), gz)
    eye = np.eye(rows)
    one = np.ones(gy)
    both = np.stack([c, s])
    fwd = np.einsum("tqz,g,jk->tqjzgk", both, one, eye) * scale
    inv = np.einsum("tqz,g,jk->tzgjqk", both, one, eye)
    return fwd.reshape(2 * MZ * rows, gz * gy * rows), inv.reshape(2 * gz * gy * rows, MZ * rows)


def parts(value):
    top = value.astype(BF)
    return top, (value - top.astype(F32)).astype(BF)


def dot(a, b):
    return jnp.dot(a, b, preferred_element_type=F32)


def dot3(a, b):
    rows = a[0].shape[0]
    both = dot(jnp.concatenate([a[0], a[1]], axis=0), b[0])
    return both[:rows] + (both[rows:] + dot(a[0], b[1]))


def swap_parts(value):
    lane = lax.broadcasted_iota(jnp.int32, value.shape, 1)
    is_real = (lane // MX) % 2 == 0
    width = value.shape[1]
    return jnp.where(is_real, pltpu.roll(value, width - MX, 1), pltpu.roll(value, MX, 1)), is_real


def forward_kernel(field, x_top, x_rest, y_top, y_rest, out, taken, x_both, y_both, sem):
    gy = lax.axis_index("gy")
    few = [
        pltpu.make_async_copy(src, dst, sem.at[4 + i])
        for i, (src, dst) in enumerate(
            ((x_top, x_both.at[0]), (x_rest, x_both.at[1]), (y_top.at[gy], y_both.at[0]), (y_rest.at[gy], y_both.at[1]))
        )
    ]
    copies = [pltpu.make_async_copy(field.at[:, q], taken.at[q], sem.at[q]) for q in range(4)]
    for copy in few + copies:
        copy.start()
    for copy in few:
        copy.wait()
    groups, rows = taken.shape[1:3]
    halves_of = []
    for q in range(4):
        copies[q].wait()
        part = dot3(parts(taken[q].reshape(groups * rows, NX)), (x_both[0, q % 2], x_both[1, q % 2]))
        if q % 2:
            halves_of[-1] = halves_of[-1] + part
        else:
            halves_of.append(part)
    total = jnp.concatenate(halves_of, axis=1)
    for g in range(groups):
        both = dot3((y_both[0], y_both[1]), parts(total[g * rows : (g + 1) * rows]))
        crossed, is_real = swap_parts(both[MY:])
        modes = both[:MY] + jnp.where(is_real, crossed, -crossed)
        out[pl.ds(2 * g * MY, MY), :] = modes[:, : 4 * MX]
        out[pl.ds((2 * g + 1) * MY, MY), :] = modes[:, 4 * MX :]


def filter_kernel(arrived, gains, f_top, f_rest, i_top, i_rest, out):
    real, imag = (gains[r].reshape(-1, 2 * MX) for r in range(2))
    first, second = slice(0, MX), slice(MX, 2 * MX)
    same = jnp.concatenate([real[:, first], real[:, first], real[:, second], real[:, second]], axis=1)
    cross = jnp.concatenate([-imag[:, first], imag[:, first], -imag[:, second], imag[:, second]], axis=1)
    half = f_top.shape[0] // 2
    turned = dot3((f_top[...], f_rest[...]), parts(arrived[...]))
    crossed, is_real = swap_parts(turned[half:])
    modes = turned[:half] + jnp.where(is_real, crossed, -crossed)
    crossed, _ = swap_parts(modes)
    filtered = modes * same + crossed * cross
    half = i_top.shape[0] // 2
    back = dot3((i_top[...], i_rest[...]), parts(filtered))
    crossed, is_real = swap_parts(back[half:])
    out[...] = back[:half] + jnp.where(is_real, -crossed, crossed)


def fetch_tiles(field, taken, sems, wanted):
    pending = {}
    for k, t in enumerate(wanted):
        pending[t] = [
            pltpu.make_async_copy(
                field.at[:, pl.ds(8 * t, 8), pl.ds(128 * h, 128)], taken.at[k, h], sems.at[k, h]
            )
            for h in range(2)
        ]
        for copy in pending[t]:
            copy.start()

    def row(t, r):
        for copy in pending.pop(t, ()):
            copy.wait()
        k = wanted.index(t)
        return jnp.concatenate(
            [taken.at[k, h].reshape(CH * 8, 128)[pl.ds(r, CH, stride=8), :] for h in range(2)], axis=1
        )

    return row


def spread_gains(weights, gains, offsets):
    for k in [9 * a + j for a in offsets for j in range(9)]:
        gains[k] = jnp.broadcast_to(weights[:, k : k + 1], (CH, 128))


def mixing(points):
    down = (
        lax.broadcasted_iota(jnp.int32, (8 * CH, CH), 0) // 8
        == lax.broadcasted_iota(jnp.int32, (8 * CH, CH), 1)
    ).astype(BF)
    across = (
        lax.broadcasted_iota(jnp.int32, (CH, 8 * CH), 1) % CH
        == lax.broadcasted_iota(jnp.int32, (CH, 8 * CH), 0)
    ).astype(BF)
    same = (
        lax.broadcasted_iota(jnp.int32, (8 * CH, 8 * CH), 0) % 8
        == lax.broadcasted_iota(jnp.int32, (8 * CH, 8 * CH), 1) // CH
    )
    return tuple(
        jnp.where(same, dot(dot(down, part).astype(BF), across), 0.0).astype(BF)
        for part in parts(points)
    )


def tap_sums(load, uses, gains, depth, runs):
    def some(i, _):
        chans = pl.ds(pl.multiple_of(i * 8, 8), 8)
        wanted = sorted({a for use in uses for a, _ in use})
        gain = {k: gains[k, chans, :] for a in wanted for k in range(9 * a, 9 * a + 9)}
        for first, to, rows in runs:
            sums = {}
            for r in range(rows + 2):
                for s, use in enumerate(uses):
                    value = load(s, first + r, chans)
                    turned = (pltpu.roll(value, 1, 1), value, pltpu.roll(value, NX - 1, 1))
                    for b in range(3):
                        o = r - b
                        if o < 0 or o >= rows:
                            continue
                        for a, k in use:
                            for e in range(3):
                                for h in range(2):
                                    term = gain[a * 9 + b * 3 + e] * turned[e][:, 128 * h : 128 * h + 128]
                                    place = (o, k, h)
                                    sums[place] = sums[place] + term if place in sums else term
                if r >= 2:
                    for k in sorted({k for use in uses for _, k in use}):
                        for h in range(2):
                            depth[k, to + r - 2, chans, pl.ds(128 * h, 128)] = sums.pop((r - 2, k, h))
        return 0

    lax.fori_loop(0, CH // 8, some, 0)


def mix_tile(mix, depth, k, t):
    tile = depth[k, pl.ds(8 * t, 8)].reshape(8 * CH, NX)
    return dot3(mix, parts(tile)).reshape(CH, 8, NX)


def pack_kernel(tiles, field, packed, edges, taken, rows, ends, sem_in, sem_out):
    last = field.shape[1] // 8 - 1
    before, after = tiles[0] - 1, tiles[-1] + 1
    wanted = [before, *tiles, after] + [t for t in (0, last) if t not in (before, after)]
    row = fetch_tiles(field, taken, sem_in, wanted)
    places = [(before, 7), *[(t, r) for t in tiles for r in range(8)], (after, 0)]
    copies, cuts = [], (0, len(places) // 2, len(places))
    for k in range(2):
        for i in range(cuts[k], cuts[k + 1]):
            rows[i] = row(*places[i])
        some = pl.ds(cuts[k], cuts[k + 1] - cuts[k])
        copies.append(pltpu.make_async_copy(rows.at[some], packed.at[some], sem_out.at[k]))
        copies[-1].start()
    ends[0] = row(last, 7)
    ends[1] = row(0, 0)
    copies.append(pltpu.make_async_copy(ends, edges, sem_out.at[2]))
    copies[-1].start()
    for copy in copies:
        copy.wait()


def own_kernel(segments, groups, weight, point, field, halo, *refs):
    last = field.shape[1] // 8 - 1
    count = 3 * len(groups)
    outs, (taken, halo_rows, weights, points, sent, lined, depth, gains, sem_in, sem_out, sem_few) = (
        refs[:count],
        refs[count:],
    )
    few = [
        pltpu.make_async_copy(src, dst, sem_few.at[i])
        for i, (src, dst) in enumerate(((weight, weights), (point, points), (halo, halo_rows)))
    ]
    for copy in few:
        copy.start()
    wanted = sorted({t for tiles in segments for t in (tiles[0] - 1, *tiles, tiles[-1] + 1) if 0 <= t <= last})
    row = fetch_tiles(field, taken, sem_in, wanted)
    for copy in few:
        copy.wait()
    spread_gains(weights, gains, range(3))
    mix = mixing(points[...])
    runs, at, done, order = [], 0, 0, []
    for tiles in segments:
        places = [(tiles[0] - 1, 7), *[(t, r) for t in tiles for r in range(8)], (tiles[-1] + 1, 0)]
        for i, (t, r) in enumerate(places):
            lined[at + i] = halo_rows[0] if t < 0 else halo_rows[1] if t > last else row(t, r)
        runs.append((at, done, 8 * len(tiles)))
        at, done = at + len(places), done + 8 * len(tiles)
        order += tiles
    tap_sums(lambda s, r, c: lined[r, c, :], [[(a, a) for a in range(3)]], gains, depth, runs)
    copies = []
    for g, tiles in enumerate(groups):
        for i, tile in enumerate(tiles):
            t = order.index(tile)
            for k in range(3):
                sent[k, t] = mix_tile(mix, depth, k, t)
                to = outs[3 * g + k].at[:, pl.ds(8 * i, 8), :]
                copies.append(pltpu.make_async_copy(sent.at[k, t], to, sem_out.at[k, t]))
                copies[-1].start()
    for copy in copies:
        copy.wait()


def middle_kernel(weight, point, low, own, high, out, taken, weights, points, sent, depth, gains, sem_in, sem_out):
    copies = [
        pltpu.make_async_copy(src, dst, sem_in.at[i])
        for i, (src, dst) in enumerate(
            ((weight, weights), (point, points), (low, taken.at[0]), (own, taken.at[1]), (high, taken.at[2]))
        )
    ]
    for copy in copies:
        copy.start()
    for copy in copies[:2]:
        copy.wait()
    spread_gains(weights, gains, range(3))
    mix = mixing(points[...])
    for copy in copies[2:]:
        copy.wait()
    rows = out.shape[1]
    tap_sums(lambda s, r, c: taken[s, r, c, :], [[(a, 0)] for a in range(3)], gains, depth, [(0, 0, rows)])
    copies = []
    for t in range(rows // 8):
        sent[t] = mix_tile(mix, depth, 0, t)
        copies.append(pltpu.make_async_copy(sent.at[t], out.at[:, pl.ds(8 * t, 8), :], sem_out.at[t]))
        copies[-1].start()
    for copy in copies:
        copy.wait()


def gelu(value):
    size = jnp.abs(value) * math.sqrt(0.5)
    below = 1.0 + 0.3275911 * size
    t = pl.reciprocal(below, approx=True)
    t = t * (2.0 - below * t)
    series = 1.061405429 * t - 1.453152027
    for factor in (1.421413741, -0.284496736, 0.254829592):
        series = series * t + factor
    tail = 0.5 * (series * t) * jnp.exp(-(size * size))
    return value * jnp.where(value < 0.0, tail, 1.0 - tail)


def inverse_kernel(upper, modes, bias, x_top, x_rest, y_top, y_rest, own, middle, second, low, high, out, base, columns):
    q = pl.program_id(0)
    groups, _, y_local, _ = out.shape

    @pl.when(q == 0)
    def _():
        gy = lax.axis_index("gy")
        for g in range(groups):
            own_modes = jnp.concatenate([modes[2 * g], modes[2 * g + 1]], axis=1)
            crossed, is_real = swap_parts(own_modes)
            stack = jnp.concatenate([own_modes, jnp.where(is_real, -crossed, crossed)], axis=0)
            pair = parts(dot3((y_top[gy], y_rest[gy]), parts(stack)))
            for h in range(2):
                for k in range(2):
                    columns[h, k, pl.ds(g * y_local, y_local), :] = pair[k][:, 128 * h : 128 * h + 128]

    h, p = q // 2, q % 2
    rows = dot3((columns[h, 0], columns[h, 1]), (x_top[p], x_rest[p]))
    turn = upper + middle.shape[2]
    stop = turn + second.shape[2]
    for g in range(groups):
        plane = rows[g * y_local : (g + 1) * y_local] + bias[4 * g + q]
        base[g, 0, :upper] = plane[:upper] + own[g, 0, :upper]
        out[g, 0, upper:turn] = gelu(plane[upper:turn] + middle[g, 0])
        out[g, 0, turn:stop] = gelu(plane[turn:stop] + (second[g, 0] + (low[g, 0] + high[g, 0])))
        base[g, 0, upper:] = plane[stop:] + own[g, 0, upper:]


def finish_kernel(upper, _, base, low, high, out, sent, sem):
    tiles = base.shape[1] // 8
    gap = out.shape[1] // 8 - tiles
    copies = []
    for t in range(tiles):
        rows = pl.ds(8 * t, 8)
        sent[t] = gelu(base[:, rows, :] + (low[:, rows, :] + high[:, rows, :]))
        to = t if t < upper else t + gap
        copies.append(pltpu.make_async_copy(sent.at[t], out.at[:, pl.ds(8 * to, 8), :], sem.at[t]))
        copies[-1].start()
    for copy in copies:
        copy.wait()


def in_hbm(*arrays):
    return [pltpu.with_memory_space_constraint(a, pltpu.HBM) for a in arrays]


def params(limit=VMEM_BYTES):
    return pltpu.CompilerParams(vmem_limit_bytes=limit)


def cost(flops, moved):
    return pl.CostEstimate(flops=flops, bytes_accessed=moved, transcendentals=0)


def whole_block(table):
    return pl.BlockSpec(table.shape, lambda i: (0,) * table.ndim)


def by_four(array):
    return array.reshape(CH // 4, 4, *array.shape[1:])


def forward_call(field, gy, pinned):
    y_local = field.shape[1]
    tables = [*halves(x_table(False)), *halves(y_table(y_local, gy, False))]
    hbm = pl.BlockSpec(memory_space=pltpu.HBM)
    return pl.pallas_call(
        forward_kernel,
        out_shape=(pltpu.HBM if pinned else jax.ShapeDtypeStruct)((CH // 2 * MY, 4 * MX), F32),
        in_specs=[hbm] * 5,
        scratch_shapes=[
            pltpu.VMEM((4, CH // 4, y_local, NX), F32),
            pltpu.VMEM((2, 2, NX, 4 * MX), BF),
            pltpu.VMEM((2, 2 * MY, y_local), BF),
            pltpu.SemaphoreType.DMA((8,)),
        ],
        compiler_params=params(ALL_VMEM_BYTES),
        cost_estimate=cost(10**8, 2**18),
        name="forward_modes",
    )(*in_hbm(by_four(field), *tables))


def filter_call(arrived, gains, gz, gy, scale):
    fwd, inv = z_tables(gz, gy, gains.shape[2], scale)
    fwd, inv = halves(fwd), halves(inv)
    return pl.pallas_call(
        filter_kernel,
        out_shape=pltpu.HBM(arrived.shape, F32),
        compiler_params=params(),
        cost_estimate=cost(4 * 10**10, 2**18),
        name="filter_modes",
    )(arrived, *in_hbm(gains, *fwd, *inv))


def inverse_call(modes, bias, own, middle, second, pair, upper, y_local, gy, scale):
    tables = [*halves(x_table(True, scale)), *halves(y_table(y_local, gy, True))]
    some = lambda rows: pl.BlockSpec((CH // 4, 1, rows, NX), lambda i: (0, i, 0, 0))
    planes = [*in_hbm(*map(by_four, (own, middle, second))), *map(by_four, pair)]
    rim = own.shape[1]
    result, base = pl.pallas_call(
        functools.partial(inverse_kernel, upper),
        out_shape=[
            jax.ShapeDtypeStruct((CH // 4, 4, y_local, NX), F32),
            jax.ShapeDtypeStruct((CH // 4, 4, rim, NX), F32),
        ],
        grid=(4,),
        in_specs=[
            whole_block(modes),
            pl.BlockSpec(memory_space=pltpu.SMEM),
            *[whole_block(t) for t in tables],
            *[some(p.shape[2]) for p in planes],
        ],
        out_specs=[some(y_local), some(rim)],
        scratch_shapes=[pltpu.VMEM((2, 2, CH // 4 * y_local, 128), BF)],
        compiler_params=params(),
        cost_estimate=cost(10**8, 2**18),
        name="inverse_modes",
    )(modes, *in_hbm(bias, *tables), *planes)
    return result.reshape(CH, y_local, NX), base.reshape(CH, rim, NX)


def finish_call(result, base, low, high, upper):
    tiles = base.shape[1] // 8
    anywhere = pl.BlockSpec(memory_space=pl.ANY)
    vmem = pl.BlockSpec(memory_space=pltpu.VMEM)
    return pl.pallas_call(
        functools.partial(finish_kernel, upper),
        out_shape=jax.ShapeDtypeStruct(result.shape, F32),
        in_specs=[anywhere] + [vmem] * 3,
        out_specs=anywhere,
        scratch_shapes=[
            pltpu.VMEM((tiles, CH, 8, NX), F32),
            pltpu.SemaphoreType.DMA((tiles,)),
        ],
        input_output_aliases={0: 0},
        compiler_params=params(),
        cost_estimate=cost(10**8, 2**18),
        name="finished_rows",
    )(result, base, low, high)


def pack_call(field, tiles):
    count = 8 * len(tiles) + 2
    fetched = len(tiles) + 4
    hbm = pl.BlockSpec(memory_space=pltpu.HBM)
    return pl.pallas_call(
        functools.partial(pack_kernel, tiles),
        out_shape=[pltpu.HBM((count, CH, NX), F32), pltpu.HBM((2, CH, NX), F32)],
        in_specs=[hbm],
        out_specs=[hbm] * 2,
        scratch_shapes=[
            pltpu.VMEM((fetched, 2, CH, 8, 128), F32),
            pltpu.VMEM((count, CH, NX), F32),
            pltpu.VMEM((2, CH, NX), F32),
            pltpu.SemaphoreType.DMA((fetched, 2)),
            pltpu.SemaphoreType.DMA((3,)),
        ],
        compiler_params=params(),
        cost_estimate=cost(10**8, 2**18),
        name="packed_rows",
    )(*in_hbm(field))


def own_call(field, halo, weight, point, segments, groups):
    tiles = sum(map(len, segments))
    rows, fetched = 8 * tiles, tiles + 2 * len(segments)
    hbm = pl.BlockSpec(memory_space=pltpu.HBM)
    shapes = [pltpu.HBM((CH, 8 * len(group), NX), F32) for group in groups for _ in range(3)]
    return pl.pallas_call(
        functools.partial(own_kernel, segments, groups),
        out_shape=shapes,
        in_specs=[hbm] * 3 + [pl.BlockSpec(memory_space=pl.ANY)],
        out_specs=[hbm] * len(shapes),
        scratch_shapes=[
            pltpu.VMEM((fetched, 2, CH, 8, 128), F32),
            pltpu.VMEM((2, CH, NX), F32),
            pltpu.VMEM((CH, 27), F32),
            pltpu.VMEM((CH, CH), F32),
            pltpu.VMEM((3, tiles, CH, 8, NX), F32),
            pltpu.VMEM((rows + 2 * len(segments), CH, NX), F32),
            pltpu.VMEM((3, rows, CH, NX), F32),
            pltpu.VMEM((27, CH, 128), F32),
            pltpu.SemaphoreType.DMA((fetched, 2)),
            pltpu.SemaphoreType.DMA((3, tiles)),
            pltpu.SemaphoreType.DMA((3,)),
        ],
        compiler_params=params(),
        cost_estimate=cost(10**8, 2**18),
        name="own_sums",
    )(*in_hbm(weight, point, field), halo)


def middle_call(weight, point, low, own, high):
    rows = own.shape[0] - 2
    hbm = pl.BlockSpec(memory_space=pltpu.HBM)
    return pl.pallas_call(
        middle_kernel,
        out_shape=pltpu.HBM((CH, rows, NX), F32),
        in_specs=[hbm] * 5,
        out_specs=hbm,
        scratch_shapes=[
            pltpu.VMEM((3, rows + 2, CH, NX), F32),
            pltpu.VMEM((CH, 27), F32),
            pltpu.VMEM((CH, CH), F32),
            pltpu.VMEM((rows // 8, CH, 8, NX), F32),
            pltpu.VMEM((1, rows, CH, NX), F32),
            pltpu.VMEM((27, CH, 128), F32),
            pltpu.SemaphoreType.DMA((5,)),
            pltpu.SemaphoreType.DMA((rows // 8,)),
        ],
        compiler_params=params(),
        cost_estimate=cost(4 * 10**10, 2**18),
        name="middle_sums",
    )(*in_hbm(weight, point, low, own, high))


def general_filter(coarse, gains, gz, gy, scale):
    j_own, n_own = gains.shape[2], gains.shape[3]
    both = ("gz", "gy")
    flat = coarse.reshape(CH // 2, MY, 2, 2, MX).transpose(3, 1, 0, 2, 4).reshape(2, MY, CH * MX)
    sent = flat.reshape(2, gy, j_own, gz, n_own).transpose(3, 1, 0, 2, 4).reshape(gz * gy, -1)
    got = lax.all_to_all(sent, both, split_axis=0, concat_axis=0, tiled=True)
    got = got.reshape(gz, gy, 2, j_own, n_own)
    c, s = (jnp.asarray(t, F32) for t in trig(kept(MZ, gz), np.arange(gz), gz))
    mul = functools.partial(jnp.einsum, precision=lax.Precision.HIGHEST)
    whole = got.sum(axis=1) * scale
    real = mul("zjn,qz->qjn", whole[:, 0], c) + mul("zjn,qz->qjn", whole[:, 1], s)
    imag = mul("zjn,qz->qjn", whole[:, 1], c) - mul("zjn,qz->qjn", whole[:, 0], s)
    real, imag = real * gains[0] - imag * gains[1], real * gains[1] + imag * gains[0]
    out = jnp.stack(
        [
            mul("qjn,qz->zjn", real, c) - mul("qjn,qz->zjn", imag, s),
            mul("qjn,qz->zjn", real, s) + mul("qjn,qz->zjn", imag, c),
        ],
        axis=1,
    )
    out = jnp.broadcast_to(out[:, None], (gz, gy, 2, j_own, n_own)).reshape(gz * gy, -1)
    back = lax.all_to_all(out, both, split_axis=0, concat_axis=0, tiled=True)
    back = back.reshape(gz, gy, 2, j_own, n_own).transpose(2, 1, 3, 0, 4)
    back = back.reshape(2, MY, CH // 2, 2, MX)
    return back.transpose(2, 1, 3, 0, 4).reshape(CH // 2, MY, 4 * MX)


def body(field, spectral_filter, depth_weight, point_weight, bias_vector):
    gz, gy = lax.axis_size("gz"), lax.axis_size("gy")
    y_local = field.shape[2]
    field = field.reshape(CH, y_local, NX)
    y_total = gy * y_local
    forward_scale = 1.0 / math.sqrt(float(NX) * y_total * gz)
    inverse_scale = 1.0 / math.sqrt(2.0 * MX * MY * MZ)

    def ring(axis, count, by):
        return [(i, (i + by) % count) for i in range(count)]

    def to_neighbours(down, up):
        return (
            lax.ppermute(down, "gz", ring("gz", gz, 1)),
            lax.ppermute(up, "gz", ring("gz", gz, -1)),
        )

    def after(value, *others):
        return lax.optimization_barrier((value, *others))[0]

    last = y_local // 8 - 1
    cut = 1 + last // 2
    first_tiles, second_tiles = tuple(range(1, cut)), tuple(range(cut, min(cut + 2, last)))
    third_tiles = (0, *range(second_tiles[-1] + 1, last + 1))
    packed, edges = pack_call(field, first_tiles)
    first_low, first_high = to_neighbours(packed, packed)
    if gy == 2:
        halo = lax.ppermute(edges, "gy", ring("gy", gy, 1))
    else:
        halo = jnp.stack(
            [
                lax.ppermute(edges[0], "gy", ring("gy", gy, 1)),
                lax.ppermute(edges[1], "gy", ring("gy", gy, -1)),
            ]
        )
    j_own, n_own = spectral_filter.shape[2], spectral_filter.shape[3]
    whole_tiles = j_own == 8 and n_own == 2 * MX
    coarse = after(forward_call(after(field, packed), gy, whole_tiles), halo)
    segments, groups = ((0,), tuple(range(cut, last + 1))), (second_tiles, third_tiles)
    down, second, up, outer_down, own, outer_up = own_call(
        after(field, coarse), halo, depth_weight, point_weight, segments, groups
    )
    if whole_tiles:
        both = ("gz", "gy")
        got = lax.all_to_all(coarse, both, split_axis=0, concat_axis=0, tiled=True)
        down, up = lax.optimization_barrier((down, up, first_low))[:2]
        pair = to_neighbours(down, up)
        gains = after(spectral_filter, first_low, first_high, second)
        mark = filter_call(got, gains, gz, gy, forward_scale)
        back = lax.all_to_all(mark, both, split_axis=0, concat_axis=0, tiled=True)
        back = back.reshape(CH // 2, MY, 4 * MX)
    else:
        pair = to_neighbours(down, up)
        mark = back = general_filter(coarse, spectral_filter, gz, gy, forward_scale)
    outer_pair = to_neighbours(after(outer_down, mark), after(outer_up, mark))
    packed, *pair = lax.optimization_barrier((packed, *pair))
    mixed = middle_call(depth_weight, point_weight, first_low, packed, first_high)
    result, base = inverse_call(
        back, bias_vector, own, mixed, second, pair, 8, y_local, gy, inverse_scale
    )
    result = finish_call(result, base, *outer_pair, 1)
    return result.reshape(CH, 1, y_local, NX)


def solution(mesh):
    in_specs = (P(None, "gz", "gy", None), P(None, None, "gy", "gz"), P(), P(), P())
    out_specs = P(None, "gz", "gy", None)
    return jax.shard_map(body, mesh=mesh, in_specs=in_specs, out_specs=out_specs, check_vma=False)
```

```python
import functools
import math

import jax
import jax.numpy as jnp
import ml_dtypes
import numpy as np
from jax import lax
from jax.experimental import pallas as pl
from jax.experimental.pallas import tpu as pltpu
from jax.sharding import PartitionSpec as P

NX = 256
MX = 32
MY = 16
MZ = 16
CH = 32
VMEM_BYTES = 20 * 1024 * 1024
ALL_VMEM_BYTES = 63 * 1024 * 1024
BF = jnp.bfloat16
F32 = jnp.float32


def kept(count, total):
    series = np.arange(count)
    return np.where(series < count // 2, series, total - count + series)


def trig(freqs, places, total):
    angle = 2.0 * np.pi * ((freqs[:, None] * places[None, :]) % total) / total
    return np.cos(angle), np.sin(angle)


def halves(table):
    table = np.asarray(table, np.float64)
    top = table.astype(np.float32).astype(ml_dtypes.bfloat16)
    rest = (table - top.astype(np.float64)).astype(np.float32).astype(ml_dtypes.bfloat16)
    return jnp.asarray(top), jnp.asarray(rest)


def y_table(y_local, gy, inverse):
    out = []
    for g in range(gy):
        places = g * y_local + np.arange(y_local)
        out.append(np.concatenate(trig(kept(MY, y_local * gy), places, y_local * gy), axis=0))
    return np.stack([t.T for t in out] if inverse else out)


def x_table(inverse, scale=1.0):
    c, s = trig(np.arange(MX), np.arange(NX), NX)
    w = np.where(np.arange(MX) == 0, 1.0, 2.0)[:, None] if inverse else 1.0
    out = np.zeros((2, 2, 2, MX, NX))
    for p in range(2):
        out[p, p, 0] = w * c * scale
        out[p, p, 1] = -w * s * scale
    out = out.reshape(2, 4 * MX, NX)
    return out if inverse else out.transpose(0, 2, 1)


def z_tables(gz, rows, scale):
    c, s = trig(kept(MZ, gz), np.arange(gz), gz)
    eye = np.eye(rows)
    both = np.stack([c, s])
    fwd = np.einsum("tqz,jk->tqjzk", both, eye) * scale
    inv = np.einsum("tqz,jk->tzjqk", both, eye)
    return fwd.reshape(2 * MZ * rows, gz * rows), inv.reshape(2 * gz * rows, MZ * rows)


def parts(value):
    top = value.astype(BF)
    return top, (value - top.astype(F32)).astype(BF)


def dot(a, b):
    return jnp.dot(a, b, preferred_element_type=F32)


def dot3(a, b):
    rows = a[0].shape[0]
    both = dot(jnp.concatenate([a[0], a[1]], axis=0), b[0])
    return both[:rows] + (both[rows:] + dot(a[0], b[1]))


def swap_parts(value):
    lane = lax.broadcasted_iota(jnp.int32, value.shape, 1)
    is_real = (lane // MX) % 2 == 0
    width = value.shape[1]
    return jnp.where(is_real, pltpu.roll(value, width - MX, 1), pltpu.roll(value, MX, 1)), is_real


def forward_kernel(halved, field, x_top, x_rest, y_top, y_rest, *refs):
    outs, (taken, x_both, y_both, sem) = refs[:-4], refs[-4:]
    gy = lax.axis_index("gy")
    few = [
        pltpu.make_async_copy(src, dst, sem.at[4 + i])
        for i, (src, dst) in enumerate(
            ((x_top, x_both.at[0]), (x_rest, x_both.at[1]), (y_top.at[gy], y_both.at[0]), (y_rest.at[gy], y_both.at[1]))
        )
    ]
    copies = [pltpu.make_async_copy(field.at[:, q], taken.at[q], sem.at[q]) for q in range(4)]
    for copy in few + copies:
        copy.start()
    for copy in few:
        copy.wait()
    groups, rows = taken.shape[1:3]
    halves_of = []
    for q in range(4):
        copies[q].wait()
        part = dot3(parts(taken[q].reshape(groups * rows, NX)), (x_both[0, q % 2], x_both[1, q % 2]))
        if q % 2:
            halves_of[-1] = halves_of[-1] + part
        else:
            halves_of.append(part)
    total = jnp.concatenate(halves_of, axis=1)
    for g in range(groups):
        both = dot3((y_both[0], y_both[1]), parts(total[g * rows : (g + 1) * rows]))
        crossed, is_real = swap_parts(both[MY:])
        modes = both[:MY] + jnp.where(is_real, crossed, -crossed)
        for h in range(2):
            pair, pairs_modes = 2 * g + h, modes[:, 4 * MX * h : 4 * MX * (h + 1)]
            if halved:
                half = MY // 2
                upper, lower = pairs_modes[:half], pairs_modes[half:]
                outs[0][pl.ds(pair * half, half), :] = jnp.where(gy == 0, upper, lower)
                outs[1][pl.ds(pair * half, half), :] = jnp.where(gy == 0, lower, upper)
            else:
                outs[0][pl.ds(pair * MY, MY), :] = pairs_modes


def filter_kernel(arrived, gains, f_top, f_rest, i_top, i_rest, out):
    real, imag = (gains[r].reshape(-1, 2 * MX) for r in range(2))
    first, second = slice(0, MX), slice(MX, 2 * MX)
    same = jnp.concatenate([real[:, first], real[:, first], real[:, second], real[:, second]], axis=1)
    cross = jnp.concatenate([-imag[:, first], imag[:, first], -imag[:, second], imag[:, second]], axis=1)
    half = f_top.shape[0] // 2
    turned = dot3((f_top[...], f_rest[...]), parts(arrived[...]))
    crossed, is_real = swap_parts(turned[half:])
    modes = turned[:half] + jnp.where(is_real, crossed, -crossed)
    crossed, _ = swap_parts(modes)
    filtered = modes * same + crossed * cross
    half = i_top.shape[0] // 2
    back = dot3((i_top[...], i_rest[...]), parts(filtered))
    crossed, is_real = swap_parts(back[half:])
    out[...] = back[:half] + jnp.where(is_real, -crossed, crossed)


def fetch_tiles(field, taken, sems, wanted):
    pending = {}
    for k, t in enumerate(wanted):
        pending[t] = [
            pltpu.make_async_copy(
                field.at[:, pl.ds(8 * t, 8), pl.ds(128 * h, 128)], taken.at[k, h], sems.at[k, h]
            )
            for h in range(2)
        ]
        for copy in pending[t]:
            copy.start()

    def row(t, r):
        for copy in pending.pop(t, ()):
            copy.wait()
        k = wanted.index(t)
        return jnp.concatenate(
            [taken.at[k, h].reshape(CH * 8, 128)[pl.ds(r, CH, stride=8), :] for h in range(2)], axis=1
        )

    return row


def spread_gains(weights, gains, offsets):
    for k in [9 * a + j for a in offsets for j in range(9)]:
        gains[k] = jnp.broadcast_to(weights[:, k : k + 1], (CH, 128))


def mixing(points):
    down = (
        lax.broadcasted_iota(jnp.int32, (8 * CH, CH), 0) // 8
        == lax.broadcasted_iota(jnp.int32, (8 * CH, CH), 1)
    ).astype(BF)
    across = (
        lax.broadcasted_iota(jnp.int32, (CH, 8 * CH), 1) % CH
        == lax.broadcasted_iota(jnp.int32, (CH, 8 * CH), 0)
    ).astype(BF)
    same = (
        lax.broadcasted_iota(jnp.int32, (8 * CH, 8 * CH), 0) % 8
        == lax.broadcasted_iota(jnp.int32, (8 * CH, 8 * CH), 1) // CH
    )
    return tuple(
        jnp.where(same, dot(dot(down, part).astype(BF), across), 0.0).astype(BF)
        for part in parts(points)
    )


def tap_sums(load, uses, gains, depth, runs):
    def some(i, _):
        chans = pl.ds(pl.multiple_of(i * 8, 8), 8)
        wanted = sorted({a for use in uses for a, _ in use})
        gain = {k: gains[k, chans, :] for a in wanted for k in range(9 * a, 9 * a + 9)}
        for first, to, rows in runs:
            sums = {}
            for r in range(rows + 2):
                for s, use in enumerate(uses):
                    value = load(s, first + r, chans)
                    turned = (pltpu.roll(value, 1, 1), value, pltpu.roll(value, NX - 1, 1))
                    for b in range(3):
                        o = r - b
                        if o < 0 or o >= rows:
                            continue
                        for a, k in use:
                            for e in range(3):
                                for h in range(2):
                                    term = gain[a * 9 + b * 3 + e] * turned[e][:, 128 * h : 128 * h + 128]
                                    place = (o, k, h)
                                    sums[place] = sums[place] + term if place in sums else term
                if r >= 2:
                    for k in sorted({k for use in uses for _, k in use}):
                        for h in range(2):
                            depth[k, to + r - 2, chans, pl.ds(128 * h, 128)] = sums.pop((r - 2, k, h))
        return 0

    lax.fori_loop(0, CH // 8, some, 0)


def mix_tile(mix, depth, k, t):
    tile = depth[k, pl.ds(8 * t, 8)].reshape(8 * CH, NX)
    return dot3(mix, parts(tile)).reshape(CH, 8, NX)


def pack_kernel(tiles, field, packed, edges, taken, rows, ends, sem_in, sem_out):
    last = field.shape[1] // 8 - 1
    before, after = tiles[0] - 1, tiles[-1] + 1
    wanted = [before, *tiles, after] + [t for t in (0, last) if t not in (before, after)]
    row = fetch_tiles(field, taken, sem_in, wanted)
    places = [(before, 7), *[(t, r) for t in tiles for r in range(8)], (after, 0)]
    copies, cuts = [], (0, len(places) // 2, len(places))
    for k in range(2):
        for i in range(cuts[k], cuts[k + 1]):
            rows[i] = row(*places[i])
        some = pl.ds(cuts[k], cuts[k + 1] - cuts[k])
        copies.append(pltpu.make_async_copy(rows.at[some], packed.at[some], sem_out.at[k]))
        copies[-1].start()
    ends[0] = row(last, 7)
    ends[1] = row(0, 0)
    copies.append(pltpu.make_async_copy(ends, edges, sem_out.at[2]))
    copies[-1].start()
    for copy in copies:
        copy.wait()


def own_kernel(segments, groups, weight, point, field, halo, *refs):
    last = field.shape[1] // 8 - 1
    count = 3 * len(groups)
    outs, (taken, halo_rows, weights, points, sent, lined, depth, gains, sem_in, sem_out, sem_few) = (
        refs[:count],
        refs[count:],
    )
    few = [
        pltpu.make_async_copy(src, dst, sem_few.at[i])
        for i, (src, dst) in enumerate(((weight, weights), (point, points), (halo, halo_rows)))
    ]
    for copy in few:
        copy.start()
    wanted = sorted({t for tiles in segments for t in (tiles[0] - 1, *tiles, tiles[-1] + 1) if 0 <= t <= last})
    row = fetch_tiles(field, taken, sem_in, wanted)
    for copy in few:
        copy.wait()
    spread_gains(weights, gains, range(3))
    mix = mixing(points[...])
    runs, at, done, order = [], 0, 0, []
    for tiles in segments:
        places = [(tiles[0] - 1, 7), *[(t, r) for t in tiles for r in range(8)], (tiles[-1] + 1, 0)]
        for i, (t, r) in enumerate(places):
            lined[at + i] = halo_rows[0] if t < 0 else halo_rows[1] if t > last else row(t, r)
        runs.append((at, done, 8 * len(tiles)))
        at, done = at + len(places), done + 8 * len(tiles)
        order += tiles
    tap_sums(lambda s, r, c: lined[r, c, :], [[(a, a) for a in range(3)]], gains, depth, runs)
    copies = []
    for g, tiles in enumerate(groups):
        for i, tile in enumerate(tiles):
            t = order.index(tile)
            for k in range(3):
                sent[k, t] = mix_tile(mix, depth, k, t)
                to = outs[3 * g + k].at[:, pl.ds(8 * i, 8), :]
                copies.append(pltpu.make_async_copy(sent.at[k, t], to, sem_out.at[k, t]))
                copies[-1].start()
    for copy in copies:
        copy.wait()


def middle_kernel(weight, point, low, own, high, out, taken, weights, points, sent, depth, gains, sem_in, sem_out):
    copies = [
        pltpu.make_async_copy(src, dst, sem_in.at[i])
        for i, (src, dst) in enumerate(
            ((weight, weights), (point, points), (low, taken.at[0]), (own, taken.at[1]), (high, taken.at[2]))
        )
    ]
    for copy in copies:
        copy.start()
    for copy in copies[:2]:
        copy.wait()
    spread_gains(weights, gains, range(3))
    mix = mixing(points[...])
    for copy in copies[2:]:
        copy.wait()
    rows = out.shape[1]
    tap_sums(lambda s, r, c: taken[s, r, c, :], [[(a, 0)] for a in range(3)], gains, depth, [(0, 0, rows)])
    copies = []
    for t in range(rows // 8):
        sent[t] = mix_tile(mix, depth, 0, t)
        copies.append(pltpu.make_async_copy(sent.at[t], out.at[:, pl.ds(8 * t, 8), :], sem_out.at[t]))
        copies[-1].start()
    for copy in copies:
        copy.wait()


def gelu(value):
    size = jnp.abs(value) * math.sqrt(0.5)
    below = 1.0 + 0.3275911 * size
    t = pl.reciprocal(below, approx=True)
    t = t * (2.0 - below * t)
    series = 1.061405429 * t - 1.453152027
    for factor in (1.421413741, -0.284496736, 0.254829592):
        series = series * t + factor
    tail = 0.5 * (series * t) * jnp.exp(-(size * size))
    return value * jnp.where(value < 0.0, tail, 1.0 - tail)


def inverse_kernel(upper, halved, first_modes, second_modes, bias, x_top, x_rest, y_top, y_rest, own, middle, second, low, high, out, base, columns):
    q = pl.program_id(0)
    groups, _, y_local, _ = out.shape

    @pl.when(q == 0)
    def _():
        gy = lax.axis_index("gy")
        for g in range(groups):
            pairs = []
            for pair in (2 * g, 2 * g + 1):
                some = pl.ds(pair * (MY // 2), MY // 2)
                one, two = first_modes[some, :], second_modes[some, :]
                if halved:
                    one, two = jnp.where(gy == 0, one, two), jnp.where(gy == 0, two, one)
                pairs.append(jnp.concatenate([one, two], axis=0))
            own_modes = jnp.concatenate(pairs, axis=1)
            crossed, is_real = swap_parts(own_modes)
            stack = jnp.concatenate([own_modes, jnp.where(is_real, -crossed, crossed)], axis=0)
            pair = parts(dot3((y_top[gy], y_rest[gy]), parts(stack)))
            for h in range(2):
                for k in range(2):
                    columns[h, k, pl.ds(g * y_local, y_local), :] = pair[k][:, 128 * h : 128 * h + 128]

    h, p = q // 2, q % 2
    rows = dot3((columns[h, 0], columns[h, 1]), (x_top[p], x_rest[p]))
    turn = upper + middle.shape[2]
    stop = turn + second.shape[2]
    for g in range(groups):
        plane = rows[g * y_local : (g + 1) * y_local] + bias[4 * g + q]
        base[g, 0, :upper] = plane[:upper] + own[g, 0, :upper]
        out[g, 0, upper:turn] = gelu(plane[upper:turn] + middle[g, 0])
        out[g, 0, turn:stop] = gelu(plane[turn:stop] + (second[g, 0] + (low[g, 0] + high[g, 0])))
        base[g, 0, upper:] = plane[stop:] + own[g, 0, upper:]


def finish_kernel(upper, _, base, low, high, out, sent, sem):
    tiles = base.shape[1] // 8
    gap = out.shape[1] // 8 - tiles
    copies = []
    for t in range(tiles):
        rows = pl.ds(8 * t, 8)
        sent[t] = gelu(base[:, rows, :] + (low[:, rows, :] + high[:, rows, :]))
        to = t if t < upper else t + gap
        copies.append(pltpu.make_async_copy(sent.at[t], out.at[:, pl.ds(8 * to, 8), :], sem.at[t]))
        copies[-1].start()
    for copy in copies:
        copy.wait()


def in_hbm(*arrays):
    return [pltpu.with_memory_space_constraint(a, pltpu.HBM) for a in arrays]


def params(limit=VMEM_BYTES):
    return pltpu.CompilerParams(vmem_limit_bytes=limit)


def cost(flops, moved):
    return pl.CostEstimate(flops=flops, bytes_accessed=moved, transcendentals=0)


def whole_block(table):
    return pl.BlockSpec(table.shape, lambda i: (0,) * table.ndim)


def by_four(array):
    return array.reshape(CH // 4, 4, *array.shape[1:])


def forward_call(field, gy, halved):
    y_local = field.shape[1]
    tables = [*halves(x_table(False)), *halves(y_table(y_local, gy, False))]
    parts_out = 2 if halved else 1
    hbm = pl.BlockSpec(memory_space=pltpu.HBM)
    return pl.pallas_call(
        functools.partial(forward_kernel, halved),
        out_shape=[jax.ShapeDtypeStruct((CH // 2 * MY // parts_out, 4 * MX), F32)] * parts_out,
        in_specs=[hbm] * 5,
        scratch_shapes=[
            pltpu.VMEM((4, CH // 4, y_local, NX), F32),
            pltpu.VMEM((2, 2, NX, 4 * MX), BF),
            pltpu.VMEM((2, 2 * MY, y_local), BF),
            pltpu.SemaphoreType.DMA((8,)),
        ],
        compiler_params=params(ALL_VMEM_BYTES),
        cost_estimate=cost(10**8, 2**18),
        name="forward_modes",
    )(*in_hbm(by_four(field), *tables))


def filter_call(arrived, gains, gz, scale):
    fwd, inv = z_tables(gz, gains.shape[2], scale)
    fwd, inv = halves(fwd), halves(inv)
    return pl.pallas_call(
        filter_kernel,
        out_shape=pltpu.HBM(arrived.shape, F32),
        compiler_params=params(),
        cost_estimate=cost(4 * 10**10, 2**18),
        name="filter_modes",
    )(arrived, *in_hbm(gains, *fwd, *inv))


def inverse_call(modes, halved, bias, own, middle, second, pair, upper, y_local, gy, scale):
    tables = [*halves(x_table(True, scale)), *halves(y_table(y_local, gy, True))]
    some = lambda rows: pl.BlockSpec((CH // 4, 1, rows, NX), lambda i: (0, i, 0, 0))
    planes = [*in_hbm(*map(by_four, (own, middle, second))), *map(by_four, pair)]
    rim = own.shape[1]
    result, base = pl.pallas_call(
        functools.partial(inverse_kernel, upper, halved),
        out_shape=[
            jax.ShapeDtypeStruct((CH // 4, 4, y_local, NX), F32),
            jax.ShapeDtypeStruct((CH // 4, 4, rim, NX), F32),
        ],
        grid=(4,),
        in_specs=[
            *[whole_block(m) for m in modes],
            pl.BlockSpec(memory_space=pltpu.SMEM),
            *[whole_block(t) for t in tables],
            *[some(p.shape[2]) for p in planes],
        ],
        out_specs=[some(y_local), some(rim)],
        scratch_shapes=[pltpu.VMEM((2, 2, CH // 4 * y_local, 128), BF)],
        compiler_params=params(),
        cost_estimate=cost(10**8, 2**18),
        name="inverse_modes",
    )(*modes, *in_hbm(bias, *tables), *planes)
    return result.reshape(CH, y_local, NX), base.reshape(CH, rim, NX)


def finish_call(result, base, low, high, upper):
    tiles = base.shape[1] // 8
    anywhere = pl.BlockSpec(memory_space=pl.ANY)
    vmem = pl.BlockSpec(memory_space=pltpu.VMEM)
    return pl.pallas_call(
        functools.partial(finish_kernel, upper),
        out_shape=jax.ShapeDtypeStruct(result.shape, F32),
        in_specs=[anywhere] + [vmem] * 3,
        out_specs=anywhere,
        scratch_shapes=[
            pltpu.VMEM((tiles, CH, 8, NX), F32),
            pltpu.SemaphoreType.DMA((tiles,)),
        ],
        input_output_aliases={0: 0},
        compiler_params=params(),
        cost_estimate=cost(10**8, 2**18),
        name="finished_rows",
    )(result, base, low, high)


def pack_call(field, tiles):
    count = 8 * len(tiles) + 2
    fetched = len(tiles) + 4
    hbm = pl.BlockSpec(memory_space=pltpu.HBM)
    return pl.pallas_call(
        functools.partial(pack_kernel, tiles),
        out_shape=[pltpu.HBM((count, CH, NX), F32), pltpu.HBM((2, CH, NX), F32)],
        in_specs=[hbm],
        out_specs=[hbm] * 2,
        scratch_shapes=[
            pltpu.VMEM((fetched, 2, CH, 8, 128), F32),
            pltpu.VMEM((count, CH, NX), F32),
            pltpu.VMEM((2, CH, NX), F32),
            pltpu.SemaphoreType.DMA((fetched, 2)),
            pltpu.SemaphoreType.DMA((3,)),
        ],
        compiler_params=params(),
        cost_estimate=cost(10**8, 2**18),
        name="packed_rows",
    )(*in_hbm(field))


def own_call(field, halo, weight, point, segments, groups):
    tiles = sum(map(len, segments))
    rows, fetched = 8 * tiles, tiles + 2 * len(segments)
    hbm = pl.BlockSpec(memory_space=pltpu.HBM)
    shapes = [pltpu.HBM((CH, 8 * len(group), NX), F32) for group in groups for _ in range(3)]
    return pl.pallas_call(
        functools.partial(own_kernel, segments, groups),
        out_shape=shapes,
        in_specs=[hbm] * 3 + [pl.BlockSpec(memory_space=pl.ANY)],
        out_specs=[hbm] * len(shapes),
        scratch_shapes=[
            pltpu.VMEM((fetched, 2, CH, 8, 128), F32),
            pltpu.VMEM((2, CH, NX), F32),
            pltpu.VMEM((CH, 27), F32),
            pltpu.VMEM((CH, CH), F32),
            pltpu.VMEM((3, tiles, CH, 8, NX), F32),
            pltpu.VMEM((rows + 2 * len(segments), CH, NX), F32),
            pltpu.VMEM((3, rows, CH, NX), F32),
            pltpu.VMEM((27, CH, 128), F32),
            pltpu.SemaphoreType.DMA((fetched, 2)),
            pltpu.SemaphoreType.DMA((3, tiles)),
            pltpu.SemaphoreType.DMA((3,)),
        ],
        compiler_params=params(),
        cost_estimate=cost(10**8, 2**18),
        name="own_sums",
    )(*in_hbm(weight, point, field), halo)


def middle_call(weight, point, low, own, high):
    rows = own.shape[0] - 2
    hbm = pl.BlockSpec(memory_space=pltpu.HBM)
    return pl.pallas_call(
        middle_kernel,
        out_shape=pltpu.HBM((CH, rows, NX), F32),
        in_specs=[hbm] * 5,
        out_specs=hbm,
        scratch_shapes=[
            pltpu.VMEM((3, rows + 2, CH, NX), F32),
            pltpu.VMEM((CH, 27), F32),
            pltpu.VMEM((CH, CH), F32),
            pltpu.VMEM((rows // 8, CH, 8, NX), F32),
            pltpu.VMEM((1, rows, CH, NX), F32),
            pltpu.VMEM((27, CH, 128), F32),
            pltpu.SemaphoreType.DMA((5,)),
            pltpu.SemaphoreType.DMA((rows // 8,)),
        ],
        compiler_params=params(),
        cost_estimate=cost(4 * 10**10, 2**18),
        name="middle_sums",
    )(*in_hbm(weight, point, low, own, high))


def general_filter(coarse, gains, gz, gy, scale):
    j_own, n_own = gains.shape[2], gains.shape[3]
    both = ("gz", "gy")
    flat = coarse.reshape(CH // 2, MY, 2, 2, MX).transpose(3, 1, 0, 2, 4).reshape(2, MY, CH * MX)
    sent = flat.reshape(2, gy, j_own, gz, n_own).transpose(3, 1, 0, 2, 4).reshape(gz * gy, -1)
    got = lax.all_to_all(sent, both, split_axis=0, concat_axis=0, tiled=True)
    got = got.reshape(gz, gy, 2, j_own, n_own)
    c, s = (jnp.asarray(t, F32) for t in trig(kept(MZ, gz), np.arange(gz), gz))
    mul = functools.partial(jnp.einsum, precision=lax.Precision.HIGHEST)
    whole = got.sum(axis=1) * scale
    real = mul("zjn,qz->qjn", whole[:, 0], c) + mul("zjn,qz->qjn", whole[:, 1], s)
    imag = mul("zjn,qz->qjn", whole[:, 1], c) - mul("zjn,qz->qjn", whole[:, 0], s)
    real, imag = real * gains[0] - imag * gains[1], real * gains[1] + imag * gains[0]
    out = jnp.stack(
        [
            mul("qjn,qz->zjn", real, c) - mul("qjn,qz->zjn", imag, s),
            mul("qjn,qz->zjn", real, s) + mul("qjn,qz->zjn", imag, c),
        ],
        axis=1,
    )
    out = jnp.broadcast_to(out[:, None], (gz, gy, 2, j_own, n_own)).reshape(gz * gy, -1)
    back = lax.all_to_all(out, both, split_axis=0, concat_axis=0, tiled=True)
    back = back.reshape(gz, gy, 2, j_own, n_own).transpose(2, 1, 3, 0, 4)
    back = back.reshape(2, MY, CH // 2, 2, MX)
    return back.transpose(2, 1, 3, 0, 4).reshape(CH // 2, MY, 4 * MX)


def body(field, spectral_filter, depth_weight, point_weight, bias_vector):
    gz, gy = lax.axis_size("gz"), lax.axis_size("gy")
    y_local = field.shape[2]
    field = field.reshape(CH, y_local, NX)
    y_total = gy * y_local
    forward_scale = 1.0 / math.sqrt(float(NX) * y_total * gz)
    inverse_scale = 1.0 / math.sqrt(2.0 * MX * MY * MZ)

    def ring(axis, count, by):
        return [(i, (i + by) % count) for i in range(count)]

    def to_neighbours(down, up):
        return (
            lax.ppermute(down, "gz", ring("gz", gz, 1)),
            lax.ppermute(up, "gz", ring("gz", gz, -1)),
        )

    def after(value, *others):
        return lax.optimization_barrier((value, *others))[0]

    last = y_local // 8 - 1
    cut = 1 + last // 2
    first_tiles, second_tiles = tuple(range(1, cut)), tuple(range(cut, min(cut + 2, last)))
    third_tiles = (0, *range(second_tiles[-1] + 1, last + 1))
    packed, edges = pack_call(field, first_tiles)
    first_low, first_high = to_neighbours(packed, packed)
    if gy == 2:
        halo = lax.ppermute(edges, "gy", ring("gy", gy, 1))
    else:
        halo = jnp.stack(
            [
                lax.ppermute(edges[0], "gy", ring("gy", gy, 1)),
                lax.ppermute(edges[1], "gy", ring("gy", gy, -1)),
            ]
        )
    j_own, n_own = spectral_filter.shape[2], spectral_filter.shape[3]
    whole_tiles = j_own == 8 and n_own == 2 * MX
    coarse, *others = forward_call(after(field, packed), gy, whole_tiles)
    if whole_tiles:
        coarse = coarse + lax.ppermute(others[0], "gy", ring("gy", gy, 1))
    coarse = after(coarse, halo)
    segments, groups = ((0,), tuple(range(cut, last + 1))), (second_tiles, third_tiles)
    down, second, up, outer_down, own, outer_up = own_call(
        after(field, coarse), halo, depth_weight, point_weight, segments, groups
    )
    if whole_tiles:
        got = lax.all_to_all(coarse, "gz", split_axis=0, concat_axis=0, tiled=True)
        down, up = lax.optimization_barrier((down, up, first_low))[:2]
        pair = to_neighbours(down, up)
        gains = after(spectral_filter, first_low, first_high, second)
        mark = filter_call(got, gains, gz, forward_scale)
        back = lax.all_to_all(mark, "gz", split_axis=0, concat_axis=0, tiled=True)
    else:
        pair = to_neighbours(down, up)
        mark = general_filter(coarse, spectral_filter, gz, gy, forward_scale)
        modes = [mark[:, part].reshape(-1, 4 * MX) for part in (slice(0, MY // 2), slice(MY // 2, MY))]
    outer_pair = to_neighbours(after(outer_down, mark), after(outer_up, mark))
    packed, *pair = lax.optimization_barrier((packed, *pair))
    mixed = middle_call(depth_weight, point_weight, first_low, packed, first_high)
    if whole_tiles:
        modes = (back, lax.ppermute(after(back, mixed), "gy", ring("gy", gy, 1)))
    result, base = inverse_call(
        modes, whole_tiles, bias_vector, own, mixed, second, pair, 8, y_local, gy, inverse_scale
    )
    result = finish_call(result, base, *outer_pair, 1)
    return result.reshape(CH, 1, y_local, NX)


def solution(mesh):
    in_specs = (P(None, "gz", "gy", None), P(None, None, "gy", "gz"), P(), P(), P())
    out_specs = P(None, "gz", "gy", None)
    return jax.shard_map(body, mesh=mesh, in_specs=in_specs, out_specs=out_specs, check_vma=False)
```

```python
import functools
import math

import jax
import jax.numpy as jnp
import ml_dtypes
import numpy as np
from jax import lax
from jax.experimental import pallas as pl
from jax.experimental.pallas import tpu as pltpu
from jax.sharding import PartitionSpec as P

NX = 256
MX = 32
MY = 16
MZ = 16
CH = 32
VMEM_BYTES = 20 * 1024 * 1024
ALL_VMEM_BYTES = 63 * 1024 * 1024
BF = jnp.bfloat16
F32 = jnp.float32


def kept(count, total):
    series = np.arange(count)
    return np.where(series < count // 2, series, total - count + series)


def trig(freqs, places, total):
    angle = 2.0 * np.pi * ((freqs[:, None] * places[None, :]) % total) / total
    return np.cos(angle), np.sin(angle)


def halves(table):
    table = np.asarray(table, np.float64)
    top = table.astype(np.float32).astype(ml_dtypes.bfloat16)
    rest = (table - top.astype(np.float64)).astype(np.float32).astype(ml_dtypes.bfloat16)
    return jnp.asarray(top), jnp.asarray(rest)


def y_table(y_local, gy, inverse):
    out = []
    for g in range(gy):
        places = g * y_local + np.arange(y_local)
        out.append(np.concatenate(trig(kept(MY, y_local * gy), places, y_local * gy), axis=0))
    return np.stack([t.T for t in out] if inverse else out)


def x_table(inverse, scale=1.0):
    c, s = trig(np.arange(MX), np.arange(NX), NX)
    w = np.where(np.arange(MX) == 0, 1.0, 2.0)[:, None] if inverse else 1.0
    out = np.zeros((2, 2, 2, MX, NX))
    for p in range(2):
        out[p, p, 0] = w * c * scale
        out[p, p, 1] = -w * s * scale
    out = out.reshape(2, 4 * MX, NX)
    return out if inverse else out.transpose(0, 2, 1)


def z_tables(gz, gy, rows, scale):
    c, s = trig(kept(MZ, gz), np.arange(gz), gz)
    eye = np.eye(rows)
    one = np.ones(gy)
    both = np.stack([c, s])
    fwd = np.einsum("tqz,g,jk->tqjzgk", both, one, eye) * scale
    inv = np.einsum("tqz,g,jk->tzgjqk", both, one, eye)
    return fwd.reshape(2 * MZ * rows, gz * gy * rows), inv.reshape(2 * gz * gy * rows, MZ * rows)


def parts(value):
    top = value.astype(BF)
    return top, (value - top.astype(F32)).astype(BF)


def dot(a, b):
    return jnp.dot(a, b, preferred_element_type=F32)


def dot3(a, b):
    rows = a[0].shape[0]
    both = dot(jnp.concatenate([a[0], a[1]], axis=0), b[0])
    return both[:rows] + (both[rows:] + dot(a[0], b[1]))


def swap_parts(value):
    lane = lax.broadcasted_iota(jnp.int32, value.shape, 1)
    is_real = (lane // MX) % 2 == 0
    width = value.shape[1]
    return jnp.where(is_real, pltpu.roll(value, width - MX, 1), pltpu.roll(value, MX, 1)), is_real


def forward_kernel(field, x_top, x_rest, y_top, y_rest, out, taken, x_both, y_both, sem):
    gy = lax.axis_index("gy")
    few = [
        pltpu.make_async_copy(src, dst, sem.at[4 + i])
        for i, (src, dst) in enumerate(
            ((x_top, x_both.at[0]), (x_rest, x_both.at[1]), (y_top.at[gy], y_both.at[0]), (y_rest.at[gy], y_both.at[1]))
        )
    ]
    copies = [pltpu.make_async_copy(field.at[:, q], taken.at[q], sem.at[q]) for q in range(4)]
    for copy in few + copies:
        copy.start()
    for copy in few:
        copy.wait()
    groups, rows = taken.shape[1:3]
    halves_of = []
    for q in range(4):
        copies[q].wait()
        part = dot3(parts(taken[q].reshape(groups * rows, NX)), (x_both[0, q % 2], x_both[1, q % 2]))
        if q % 2:
            halves_of[-1] = halves_of[-1] + part
        else:
            halves_of.append(part)
    total = jnp.concatenate(halves_of, axis=1)
    for g in range(groups):
        both = dot3((y_both[0], y_both[1]), parts(total[g * rows : (g + 1) * rows]))
        crossed, is_real = swap_parts(both[MY:])
        modes = both[:MY] + jnp.where(is_real, crossed, -crossed)
        out[pl.ds(2 * g * MY, MY), :] = modes[:, : 4 * MX]
        out[pl.ds((2 * g + 1) * MY, MY), :] = modes[:, 4 * MX :]


def filter_kernel(arrived, gains, f_top, f_rest, i_top, i_rest, out):
    real, imag = (gains[r].reshape(-1, 2 * MX) for r in range(2))
    first, second = slice(0, MX), slice(MX, 2 * MX)
    same = jnp.concatenate([real[:, first], real[:, first], real[:, second], real[:, second]], axis=1)
    cross = jnp.concatenate([-imag[:, first], imag[:, first], -imag[:, second], imag[:, second]], axis=1)
    half = f_top.shape[0] // 2
    turned = dot3((f_top[...], f_rest[...]), parts(arrived[...]))
    crossed, is_real = swap_parts(turned[half:])
    modes = turned[:half] + jnp.where(is_real, crossed, -crossed)
    crossed, _ = swap_parts(modes)
    filtered = modes * same + crossed * cross
    half = i_top.shape[0] // 2
    back = dot3((i_top[...], i_rest[...]), parts(filtered))
    crossed, is_real = swap_parts(back[half:])
    out[...] = back[:half] + jnp.where(is_real, -crossed, crossed)


def fetch_tiles(field, taken, sems, wanted):
    pending = {}
    for k, t in enumerate(wanted):
        pending[t] = [
            pltpu.make_async_copy(
                field.at[:, pl.ds(8 * t, 8), pl.ds(128 * h, 128)], taken.at[k, h], sems.at[k, h]
            )
            for h in range(2)
        ]
        for copy in pending[t]:
            copy.start()

    def row(t, r):
        for copy in pending.pop(t, ()):
            copy.wait()
        k = wanted.index(t)
        return jnp.concatenate(
            [taken.at[k, h].reshape(CH * 8, 128)[pl.ds(r, CH, stride=8), :] for h in range(2)], axis=1
        )

    return row


def spread_gains(weights, gains, offsets):
    for k in [9 * a + j for a in offsets for j in range(9)]:
        gains[k] = jnp.broadcast_to(weights[:, k : k + 1], (CH, 128))


def mixing(points):
    down = (
        lax.broadcasted_iota(jnp.int32, (8 * CH, CH), 0) // 8
        == lax.broadcasted_iota(jnp.int32, (8 * CH, CH), 1)
    ).astype(BF)
    across = (
        lax.broadcasted_iota(jnp.int32, (CH, 8 * CH), 1) % CH
        == lax.broadcasted_iota(jnp.int32, (CH, 8 * CH), 0)
    ).astype(BF)
    same = (
        lax.broadcasted_iota(jnp.int32, (8 * CH, 8 * CH), 0) % 8
        == lax.broadcasted_iota(jnp.int32, (8 * CH, 8 * CH), 1) // CH
    )
    return tuple(
        jnp.where(same, dot(dot(down, part).astype(BF), across), 0.0).astype(BF)
        for part in parts(points)
    )


def tap_sums(load, uses, gains, depth, runs):
    def some(i, _):
        chans = pl.ds(pl.multiple_of(i * 8, 8), 8)
        wanted = sorted({a for use in uses for a, _ in use})
        gain = {k: gains[k, chans, :] for a in wanted for k in range(9 * a, 9 * a + 9)}
        for first, to, rows in runs:
            sums = {}
            for r in range(rows + 2):
                for s, use in enumerate(uses):
                    value = load(s, first + r, chans)
                    turned = (pltpu.roll(value, 1, 1), value, pltpu.roll(value, NX - 1, 1))
                    for b in range(3):
                        o = r - b
                        if o < 0 or o >= rows:
                            continue
                        for a, k in use:
                            for e in range(3):
                                for h in range(2):
                                    term = gain[a * 9 + b * 3 + e] * turned[e][:, 128 * h : 128 * h + 128]
                                    place = (o, k, h)
                                    sums[place] = sums[place] + term if place in sums else term
                if r >= 2:
                    for k in sorted({k for use in uses for _, k in use}):
                        for h in range(2):
                            depth[k, to + r - 2, chans, pl.ds(128 * h, 128)] = sums.pop((r - 2, k, h))
        return 0

    lax.fori_loop(0, CH // 8, some, 0)


def mix_tile(mix, depth, k, t):
    tile = depth[k, pl.ds(8 * t, 8)].reshape(8 * CH, NX)
    return dot3(mix, parts(tile)).reshape(CH, 8, NX)


def pack_kernel(tiles, field, packed, edges, taken, sem_in):
    last = field.shape[1] // 8 - 1
    before, after = tiles[0] - 1, tiles[-1] + 1
    wanted = [before, *tiles, after] + [t for t in (0, last) if t not in (before, after)]
    row = fetch_tiles(field, taken, sem_in, wanted)
    for i, place in enumerate([(before, 7), *[(t, r) for t in tiles for r in range(8)], (after, 0)]):
        packed[i] = row(*place)
    edges[0] = row(last, 7)
    edges[1] = row(0, 0)


def own_kernel(segments, groups, weight, point, field, halo, *refs):
    last = field.shape[1] // 8 - 1
    count = 3 * len(groups)
    outs, (taken, halo_rows, weights, points, sent, lined, depth, gains, sem_in, sem_out, sem_few) = (
        refs[:count],
        refs[count:],
    )
    few = [
        pltpu.make_async_copy(src, dst, sem_few.at[i])
        for i, (src, dst) in enumerate(((weight, weights), (point, points), (halo, halo_rows)))
    ]
    for copy in few:
        copy.start()
    wanted = sorted({t for tiles in segments for t in (tiles[0] - 1, *tiles, tiles[-1] + 1) if 0 <= t <= last})
    row = fetch_tiles(field, taken, sem_in, wanted)
    for copy in few:
        copy.wait()
    spread_gains(weights, gains, range(3))
    mix = mixing(points[...])
    runs, at, done, order = [], 0, 0, []
    for tiles in segments:
        places = [(tiles[0] - 1, 7), *[(t, r) for t in tiles for r in range(8)], (tiles[-1] + 1, 0)]
        for i, (t, r) in enumerate(places):
            lined[at + i] = halo_rows[0] if t < 0 else halo_rows[1] if t > last else row(t, r)
        runs.append((at, done, 8 * len(tiles)))
        at, done = at + len(places), done + 8 * len(tiles)
        order += tiles
    tap_sums(lambda s, r, c: lined[r, c, :], [[(a, a) for a in range(3)]], gains, depth, runs)
    copies = []
    for g, tiles in enumerate(groups):
        for i, tile in enumerate(tiles):
            t = order.index(tile)
            for k in range(3):
                sent[k, t] = mix_tile(mix, depth, k, t)
                to = outs[3 * g + k].at[:, pl.ds(8 * i, 8), :]
                copies.append(pltpu.make_async_copy(sent.at[k, t], to, sem_out.at[k, t]))
                copies[-1].start()
    for copy in copies:
        copy.wait()


def middle_kernel(weight, point, low, own, high, out, taken, weights, points, sent, depth, gains, sem_in, sem_out):
    copies = [
        pltpu.make_async_copy(src, dst, sem_in.at[i])
        for i, (src, dst) in enumerate(
            ((weight, weights), (point, points), (low, taken.at[0]), (own, taken.at[1]), (high, taken.at[2]))
        )
    ]
    for copy in copies:
        copy.start()
    for copy in copies[:2]:
        copy.wait()
    spread_gains(weights, gains, range(3))
    mix = mixing(points[...])
    for copy in copies[2:]:
        copy.wait()
    rows = out.shape[1]
    tap_sums(lambda s, r, c: taken[s, r, c, :], [[(a, 0)] for a in range(3)], gains, depth, [(0, 0, rows)])
    copies = []
    for t in range(rows // 8):
        sent[t] = mix_tile(mix, depth, 0, t)
        copies.append(pltpu.make_async_copy(sent.at[t], out.at[:, pl.ds(8 * t, 8), :], sem_out.at[t]))
        copies[-1].start()
    for copy in copies:
        copy.wait()


def gelu(value):
    size = jnp.abs(value) * math.sqrt(0.5)
    below = 1.0 + 0.3275911 * size
    t = pl.reciprocal(below, approx=True)
    t = t * (2.0 - below * t)
    series = 1.061405429 * t - 1.453152027
    for factor in (1.421413741, -0.284496736, 0.254829592):
        series = series * t + factor
    tail = 0.5 * (series * t) * jnp.exp(-(size * size))
    return value * jnp.where(value < 0.0, tail, 1.0 - tail)


def inverse_kernel(upper, modes, bias, x_top, x_rest, y_top, y_rest, own, middle, second, low, high, out, base, columns):
    q = pl.program_id(0)
    groups, _, y_local, _ = out.shape

    @pl.when(q == 0)
    def _():
        gy = lax.axis_index("gy")
        for g in range(groups):
            own_modes = jnp.concatenate([modes[2 * g], modes[2 * g + 1]], axis=1)
            crossed, is_real = swap_parts(own_modes)
            stack = jnp.concatenate([own_modes, jnp.where(is_real, -crossed, crossed)], axis=0)
            pair = parts(dot3((y_top[gy], y_rest[gy]), parts(stack)))
            for h in range(2):
                for k in range(2):
                    columns[h, k, pl.ds(g * y_local, y_local), :] = pair[k][:, 128 * h : 128 * h + 128]

    h, p = q // 2, q % 2
    rows = dot3((columns[h, 0], columns[h, 1]), (x_top[p], x_rest[p]))
    turn = upper + middle.shape[2]
    stop = turn + second.shape[2]
    for g in range(groups):
        plane = rows[g * y_local : (g + 1) * y_local] + bias[4 * g + q]
        base[g, 0, :upper] = plane[:upper] + own[g, 0, :upper]
        out[g, 0, upper:turn] = gelu(plane[upper:turn] + middle[g, 0])
        out[g, 0, turn:stop] = gelu(plane[turn:stop] + (second[g, 0] + (low[g, 0] + high[g, 0])))
        base[g, 0, upper:] = plane[stop:] + own[g, 0, upper:]


def finish_kernel(upper, _, base, low, high, out, sent, sem):
    tiles = base.shape[1] // 8
    gap = out.shape[1] // 8 - tiles
    copies = []
    for t in range(tiles):
        rows = pl.ds(8 * t, 8)
        sent[t] = gelu(base[:, rows, :] + (low[:, rows, :] + high[:, rows, :]))
        to = t if t < upper else t + gap
        copies.append(pltpu.make_async_copy(sent.at[t], out.at[:, pl.ds(8 * to, 8), :], sem.at[t]))
        copies[-1].start()
    for copy in copies:
        copy.wait()


def in_hbm(*arrays):
    return [pltpu.with_memory_space_constraint(a, pltpu.HBM) for a in arrays]


def params(limit=VMEM_BYTES):
    return pltpu.CompilerParams(vmem_limit_bytes=limit)


def cost(flops, moved):
    return pl.CostEstimate(flops=flops, bytes_accessed=moved, transcendentals=0)


def whole_block(table):
    return pl.BlockSpec(table.shape, lambda i: (0,) * table.ndim)


def by_four(array):
    return array.reshape(CH // 4, 4, *array.shape[1:])


def forward_call(field, gy, pinned):
    y_local = field.shape[1]
    tables = [*halves(x_table(False)), *halves(y_table(y_local, gy, False))]
    hbm = pl.BlockSpec(memory_space=pltpu.HBM)
    return pl.pallas_call(
        forward_kernel,
        out_shape=(pltpu.HBM if pinned else jax.ShapeDtypeStruct)((CH // 2 * MY, 4 * MX), F32),
        in_specs=[hbm] * 5,
        scratch_shapes=[
            pltpu.VMEM((4, CH // 4, y_local, NX), F32),
            pltpu.VMEM((2, 2, NX, 4 * MX), BF),
            pltpu.VMEM((2, 2 * MY, y_local), BF),
            pltpu.SemaphoreType.DMA((8,)),
        ],
        compiler_params=params(ALL_VMEM_BYTES),
        cost_estimate=cost(10**8, 2**18),
        name="forward_modes",
    )(*in_hbm(by_four(field), *tables))


def filter_call(arrived, gains, gz, gy, scale):
    fwd, inv = z_tables(gz, gy, gains.shape[2], scale)
    fwd, inv = halves(fwd), halves(inv)
    return pl.pallas_call(
        filter_kernel,
        out_shape=pltpu.HBM(arrived.shape, F32),
        compiler_params=params(),
        cost_estimate=cost(4 * 10**10, 2**18),
        name="filter_modes",
    )(arrived, *in_hbm(gains, *fwd, *inv))


def inverse_call(modes, bias, own, middle, second, pair, upper, y_local, gy, scale):
    tables = [*halves(x_table(True, scale)), *halves(y_table(y_local, gy, True))]
    some = lambda rows: pl.BlockSpec((CH // 4, 1, rows, NX), lambda i: (0, i, 0, 0))
    planes = [*in_hbm(*map(by_four, (own, middle, second))), *map(by_four, pair)]
    rim = own.shape[1]
    result, base = pl.pallas_call(
        functools.partial(inverse_kernel, upper),
        out_shape=[
            jax.ShapeDtypeStruct((CH // 4, 4, y_local, NX), F32),
            jax.ShapeDtypeStruct((CH // 4, 4, rim, NX), F32),
        ],
        grid=(4,),
        in_specs=[
            whole_block(modes),
            pl.BlockSpec(memory_space=pltpu.SMEM),
            *[whole_block(t) for t in tables],
            *[some(p.shape[2]) for p in planes],
        ],
        out_specs=[some(y_local), some(rim)],
        scratch_shapes=[pltpu.VMEM((2, 2, CH // 4 * y_local, 128), BF)],
        compiler_params=params(),
        cost_estimate=cost(10**8, 2**18),
        name="inverse_modes",
    )(modes, *in_hbm(bias, *tables), *planes)
    return result.reshape(CH, y_local, NX), base.reshape(CH, rim, NX)


def finish_call(result, base, low, high, upper):
    tiles = base.shape[1] // 8
    anywhere = pl.BlockSpec(memory_space=pl.ANY)
    vmem = pl.BlockSpec(memory_space=pltpu.VMEM)
    return pl.pallas_call(
        functools.partial(finish_kernel, upper),
        out_shape=jax.ShapeDtypeStruct(result.shape, F32),
        in_specs=[anywhere] + [vmem] * 3,
        out_specs=anywhere,
        scratch_shapes=[
            pltpu.VMEM((tiles, CH, 8, NX), F32),
            pltpu.SemaphoreType.DMA((tiles,)),
        ],
        input_output_aliases={0: 0},
        compiler_params=params(),
        cost_estimate=cost(10**8, 2**18),
        name="finished_rows",
    )(result, base, low, high)


def pack_call(field, tiles):
    count = 8 * len(tiles) + 2
    fetched = len(tiles) + 4
    vmem = pl.BlockSpec(memory_space=pltpu.VMEM)
    return pl.pallas_call(
        functools.partial(pack_kernel, tiles),
        out_shape=[jax.ShapeDtypeStruct((count, CH, NX), F32), jax.ShapeDtypeStruct((2, CH, NX), F32)],
        in_specs=[pl.BlockSpec(memory_space=pltpu.HBM)],
        out_specs=[vmem] * 2,
        scratch_shapes=[
            pltpu.VMEM((fetched, 2, CH, 8, 128), F32),
            pltpu.SemaphoreType.DMA((fetched, 2)),
        ],
        compiler_params=params(),
        cost_estimate=cost(10**8, 2**18),
        name="packed_rows",
    )(*in_hbm(field))


def own_call(field, halo, weight, point, segments, groups):
    tiles = sum(map(len, segments))
    rows, fetched = 8 * tiles, tiles + 2 * len(segments)
    hbm = pl.BlockSpec(memory_space=pltpu.HBM)
    shapes = [pltpu.HBM((CH, 8 * len(group), NX), F32) for group in groups for _ in range(3)]
    return pl.pallas_call(
        functools.partial(own_kernel, segments, groups),
        out_shape=shapes,
        in_specs=[hbm] * 3 + [pl.BlockSpec(memory_space=pl.ANY)],
        out_specs=[hbm] * len(shapes),
        scratch_shapes=[
            pltpu.VMEM((fetched, 2, CH, 8, 128), F32),
            pltpu.VMEM((2, CH, NX), F32),
            pltpu.VMEM((CH, 27), F32),
            pltpu.VMEM((CH, CH), F32),
            pltpu.VMEM((3, tiles, CH, 8, NX), F32),
            pltpu.VMEM((rows + 2 * len(segments), CH, NX), F32),
            pltpu.VMEM((3, rows, CH, NX), F32),
            pltpu.VMEM((27, CH, 128), F32),
            pltpu.SemaphoreType.DMA((fetched, 2)),
            pltpu.SemaphoreType.DMA((3, tiles)),
            pltpu.SemaphoreType.DMA((3,)),
        ],
        compiler_params=params(),
        cost_estimate=cost(10**8, 2**18),
        name="own_sums",
    )(*in_hbm(weight, point, field), halo)


def middle_call(weight, point, low, own, high):
    rows = own.shape[0] - 2
    hbm = pl.BlockSpec(memory_space=pltpu.HBM)
    return pl.pallas_call(
        middle_kernel,
        out_shape=pltpu.HBM((CH, rows, NX), F32),
        in_specs=[hbm] * 3 + [pl.BlockSpec(memory_space=pl.ANY), hbm],
        out_specs=hbm,
        scratch_shapes=[
            pltpu.VMEM((3, rows + 2, CH, NX), F32),
            pltpu.VMEM((CH, 27), F32),
            pltpu.VMEM((CH, CH), F32),
            pltpu.VMEM((rows // 8, CH, 8, NX), F32),
            pltpu.VMEM((1, rows, CH, NX), F32),
            pltpu.VMEM((27, CH, 128), F32),
            pltpu.SemaphoreType.DMA((5,)),
            pltpu.SemaphoreType.DMA((rows // 8,)),
        ],
        compiler_params=params(),
        cost_estimate=cost(4 * 10**10, 2**18),
        name="middle_sums",
    )(*in_hbm(weight, point, low), own, *in_hbm(high))


def general_filter(coarse, gains, gz, gy, scale):
    j_own, n_own = gains.shape[2], gains.shape[3]
    both = ("gz", "gy")
    flat = coarse.reshape(CH // 2, MY, 2, 2, MX).transpose(3, 1, 0, 2, 4).reshape(2, MY, CH * MX)
    sent = flat.reshape(2, gy, j_own, gz, n_own).transpose(3, 1, 0, 2, 4).reshape(gz * gy, -1)
    got = lax.all_to_all(sent, both, split_axis=0, concat_axis=0, tiled=True)
    got = got.reshape(gz, gy, 2, j_own, n_own)
    c, s = (jnp.asarray(t, F32) for t in trig(kept(MZ, gz), np.arange(gz), gz))
    mul = functools.partial(jnp.einsum, precision=lax.Precision.HIGHEST)
    whole = got.sum(axis=1) * scale
    real = mul("zjn,qz->qjn", whole[:, 0], c) + mul("zjn,qz->qjn", whole[:, 1], s)
    imag = mul("zjn,qz->qjn", whole[:, 1], c) - mul("zjn,qz->qjn", whole[:, 0], s)
    real, imag = real * gains[0] - imag * gains[1], real * gains[1] + imag * gains[0]
    out = jnp.stack(
        [
            mul("qjn,qz->zjn", real, c) - mul("qjn,qz->zjn", imag, s),
            mul("qjn,qz->zjn", real, s) + mul("qjn,qz->zjn", imag, c),
        ],
        axis=1,
    )
    out = jnp.broadcast_to(out[:, None], (gz, gy, 2, j_own, n_own)).reshape(gz * gy, -1)
    back = lax.all_to_all(out, both, split_axis=0, concat_axis=0, tiled=True)
    back = back.reshape(gz, gy, 2, j_own, n_own).transpose(2, 1, 3, 0, 4)
    back = back.reshape(2, MY, CH // 2, 2, MX)
    return back.transpose(2, 1, 3, 0, 4).reshape(CH // 2, MY, 4 * MX)


def body(field, spectral_filter, depth_weight, point_weight, bias_vector):
    gz, gy = lax.axis_size("gz"), lax.axis_size("gy")
    y_local = field.shape[2]
    field = field.reshape(CH, y_local, NX)
    y_total = gy * y_local
    forward_scale = 1.0 / math.sqrt(float(NX) * y_total * gz)
    inverse_scale = 1.0 / math.sqrt(2.0 * MX * MY * MZ)

    def ring(axis, count, by):
        return [(i, (i + by) % count) for i in range(count)]

    def to_neighbours(down, up):
        return (
            lax.ppermute(down, "gz", ring("gz", gz, 1)),
            lax.ppermute(up, "gz", ring("gz", gz, -1)),
        )

    def after(value, *others):
        return lax.optimization_barrier((value, *others))[0]

    last = y_local // 8 - 1
    cut = 1 + last // 2
    first_tiles, second_tiles = tuple(range(1, cut)), tuple(range(cut, min(cut + 2, last)))
    third_tiles = (0, *range(second_tiles[-1] + 1, last + 1))
    packed, edges = pack_call(field, first_tiles)
    first_low, first_high = to_neighbours(packed, packed)
    if gy == 2:
        halo = lax.ppermute(edges, "gy", ring("gy", gy, 1))
    else:
        halo = jnp.stack(
            [
                lax.ppermute(edges[0], "gy", ring("gy", gy, 1)),
                lax.ppermute(edges[1], "gy", ring("gy", gy, -1)),
            ]
        )
    j_own, n_own = spectral_filter.shape[2], spectral_filter.shape[3]
    whole_tiles = j_own == 8 and n_own == 2 * MX
    coarse = after(forward_call(after(field, packed), gy, whole_tiles), halo)
    segments, groups = ((0,), tuple(range(cut, last + 1))), (second_tiles, third_tiles)
    down, second, up, outer_down, own, outer_up = own_call(
        after(field, coarse), halo, depth_weight, point_weight, segments, groups
    )
    if whole_tiles:
        both = ("gz", "gy")
        got = lax.all_to_all(coarse, both, split_axis=0, concat_axis=0, tiled=True)
        down, up = lax.optimization_barrier((down, up, first_low))[:2]
        pair = to_neighbours(down, up)
        gains = after(spectral_filter, first_low, first_high, second)
        mark = filter_call(got, gains, gz, gy, forward_scale)
        back = lax.all_to_all(mark, both, split_axis=0, concat_axis=0, tiled=True)
        back = back.reshape(CH // 2, MY, 4 * MX)
    else:
        pair = to_neighbours(down, up)
        mark = back = general_filter(coarse, spectral_filter, gz, gy, forward_scale)
    outer_pair = to_neighbours(after(outer_down, mark), after(outer_up, mark))
    packed, *pair = lax.optimization_barrier((packed, *pair))
    mixed = middle_call(depth_weight, point_weight, first_low, packed, first_high)
    result, base = inverse_call(
        back, bias_vector, own, mixed, second, pair, 8, y_local, gy, inverse_scale
    )
    result = finish_call(result, base, *outer_pair, 1)
    return result.reshape(CH, 1, y_local, NX)


def solution(mesh):
    in_specs = (P(None, "gz", "gy", None), P(None, None, "gy", "gz"), P(), P(), P())
    out_specs = P(None, "gz", "gy", None)
    return jax.shard_map(body, mesh=mesh, in_specs=in_specs, out_specs=out_specs, check_vma=False)
```

```python
import functools
import math

import jax
import jax.numpy as jnp
import ml_dtypes
import numpy as np
from jax import lax
from jax.experimental import pallas as pl
from jax.experimental.pallas import tpu as pltpu
from jax.sharding import PartitionSpec as P

NX = 256
MX = 32
MY = 16
MZ = 16
CH = 32
VMEM_BYTES = 20 * 1024 * 1024
ALL_VMEM_BYTES = 63 * 1024 * 1024
BF = jnp.bfloat16
F32 = jnp.float32


def kept(count, total):
    series = np.arange(count)
    return np.where(series < count // 2, series, total - count + series)


def trig(freqs, places, total):
    angle = 2.0 * np.pi * ((freqs[:, None] * places[None, :]) % total) / total
    return np.cos(angle), np.sin(angle)


def halves(table):
    table = np.asarray(table, np.float64)
    top = table.astype(np.float32).astype(ml_dtypes.bfloat16)
    rest = (table - top.astype(np.float64)).astype(np.float32).astype(ml_dtypes.bfloat16)
    return jnp.asarray(top), jnp.asarray(rest)


def y_table(y_local, gy, inverse):
    out = []
    for g in range(gy):
        places = g * y_local + np.arange(y_local)
        out.append(np.concatenate(trig(kept(MY, y_local * gy), places, y_local * gy), axis=0))
    return np.stack([t.T for t in out] if inverse else out)


def x_table(inverse, scale=1.0):
    c, s = trig(np.arange(MX), np.arange(NX), NX)
    w = np.where(np.arange(MX) == 0, 1.0, 2.0)[:, None] if inverse else 1.0
    out = np.zeros((2, 2, 2, MX, NX))
    for p in range(2):
        out[p, p, 0] = w * c * scale
        out[p, p, 1] = -w * s * scale
    out = out.reshape(2, 4 * MX, NX)
    return out if inverse else out.transpose(0, 2, 1)


def z_tables(gz, gy, rows, scale):
    c, s = trig(kept(MZ, gz), np.arange(gz), gz)
    eye = np.eye(rows)
    both = np.stack([c, s])
    fwd = np.einsum("tqz,g,jk->tqjzgk", both, np.ones(gy), eye) * scale
    inv = np.einsum("tqz,jk->tzjqk", both, eye)
    return fwd.reshape(2 * MZ * rows, gz * gy * rows), inv.reshape(2 * gz * rows, MZ * rows)


def parts(value):
    top = value.astype(BF)
    return top, (value - top.astype(F32)).astype(BF)


def dot(a, b):
    return jnp.dot(a, b, preferred_element_type=F32)


def dot3(a, b):
    rows = a[0].shape[0]
    both = dot(jnp.concatenate([a[0], a[1]], axis=0), b[0])
    return both[:rows] + (both[rows:] + dot(a[0], b[1]))


def swap_parts(value):
    lane = lax.broadcasted_iota(jnp.int32, value.shape, 1)
    is_real = (lane // MX) % 2 == 0
    width = value.shape[1]
    return jnp.where(is_real, pltpu.roll(value, width - MX, 1), pltpu.roll(value, MX, 1)), is_real


def forward_kernel(field, x_top, x_rest, y_top, y_rest, out, taken, x_both, y_both, sem):
    gy = lax.axis_index("gy")
    few = [
        pltpu.make_async_copy(src, dst, sem.at[4 + i])
        for i, (src, dst) in enumerate(
            ((x_top, x_both.at[0]), (x_rest, x_both.at[1]), (y_top.at[gy], y_both.at[0]), (y_rest.at[gy], y_both.at[1]))
        )
    ]
    copies = [pltpu.make_async_copy(field.at[:, q], taken.at[q], sem.at[q]) for q in range(4)]
    for copy in few + copies:
        copy.start()
    for copy in few:
        copy.wait()
    groups, rows = taken.shape[1:3]
    halves_of = []
    for q in range(4):
        copies[q].wait()
        part = dot3(parts(taken[q].reshape(groups * rows, NX)), (x_both[0, q % 2], x_both[1, q % 2]))
        if q % 2:
            halves_of[-1] = halves_of[-1] + part
        else:
            halves_of.append(part)
    total = jnp.concatenate(halves_of, axis=1)
    for g in range(groups):
        both = dot3((y_both[0], y_both[1]), parts(total[g * rows : (g + 1) * rows]))
        crossed, is_real = swap_parts(both[MY:])
        modes = both[:MY] + jnp.where(is_real, crossed, -crossed)
        out[pl.ds(2 * g * MY, MY), :] = modes[:, : 4 * MX]
        out[pl.ds((2 * g + 1) * MY, MY), :] = modes[:, 4 * MX :]


def filter_kernel(arrived, gains, f_top, f_rest, i_top, i_rest, out):
    real, imag = (gains[r].reshape(-1, 2 * MX) for r in range(2))
    first, second = slice(0, MX), slice(MX, 2 * MX)
    same = jnp.concatenate([real[:, first], real[:, first], real[:, second], real[:, second]], axis=1)
    cross = jnp.concatenate([-imag[:, first], imag[:, first], -imag[:, second], imag[:, second]], axis=1)
    half = f_top.shape[0] // 2
    turned = dot3((f_top[...], f_rest[...]), parts(arrived[...]))
    crossed, is_real = swap_parts(turned[half:])
    modes = turned[:half] + jnp.where(is_real, crossed, -crossed)
    crossed, _ = swap_parts(modes)
    filtered = modes * same + crossed * cross
    half = i_top.shape[0] // 2
    back = dot3((i_top[...], i_rest[...]), parts(filtered))
    crossed, is_real = swap_parts(back[half:])
    out[...] = back[:half] + jnp.where(is_real, -crossed, crossed)


def fetch_tiles(field, taken, sems, wanted):
    pending = {}
    for k, t in enumerate(wanted):
        pending[t] = [
            pltpu.make_async_copy(
                field.at[:, pl.ds(8 * t, 8), pl.ds(128 * h, 128)], taken.at[k, h], sems.at[k, h]
            )
            for h in range(2)
        ]
        for copy in pending[t]:
            copy.start()

    def row(t, r):
        for copy in pending.pop(t, ()):
            copy.wait()
        k = wanted.index(t)
        return jnp.concatenate(
            [taken.at[k, h].reshape(CH * 8, 128)[pl.ds(r, CH, stride=8), :] for h in range(2)], axis=1
        )

    return row


def spread_gains(weights, gains, offsets):
    for k in [9 * a + j for a in offsets for j in range(9)]:
        gains[k] = jnp.broadcast_to(weights[:, k : k + 1], (CH, 128))


def mixing(points):
    down = (
        lax.broadcasted_iota(jnp.int32, (8 * CH, CH), 0) // 8
        == lax.broadcasted_iota(jnp.int32, (8 * CH, CH), 1)
    ).astype(BF)
    across = (
        lax.broadcasted_iota(jnp.int32, (CH, 8 * CH), 1) % CH
        == lax.broadcasted_iota(jnp.int32, (CH, 8 * CH), 0)
    ).astype(BF)
    same = (
        lax.broadcasted_iota(jnp.int32, (8 * CH, 8 * CH), 0) % 8
        == lax.broadcasted_iota(jnp.int32, (8 * CH, 8 * CH), 1) // CH
    )
    return tuple(
        jnp.where(same, dot(dot(down, part).astype(BF), across), 0.0).astype(BF)
        for part in parts(points)
    )


def tap_sums(load, uses, gains, depth, runs):
    def some(i, _):
        chans = pl.ds(pl.multiple_of(i * 8, 8), 8)
        wanted = sorted({a for use in uses for a, _ in use})
        gain = {k: gains[k, chans, :] for a in wanted for k in range(9 * a, 9 * a + 9)}
        for first, to, rows in runs:
            sums = {}
            for r in range(rows + 2):
                for s, use in enumerate(uses):
                    value = load(s, first + r, chans)
                    turned = (pltpu.roll(value, 1, 1), value, pltpu.roll(value, NX - 1, 1))
                    for b in range(3):
                        o = r - b
                        if o < 0 or o >= rows:
                            continue
                        for a, k in use:
                            for e in range(3):
                                for h in range(2):
                                    term = gain[a * 9 + b * 3 + e] * turned[e][:, 128 * h : 128 * h + 128]
                                    place = (o, k, h)
                                    sums[place] = sums[place] + term if place in sums else term
                if r >= 2:
                    for k in sorted({k for use in uses for _, k in use}):
                        for h in range(2):
                            depth[k, to + r - 2, chans, pl.ds(128 * h, 128)] = sums.pop((r - 2, k, h))
        return 0

    lax.fori_loop(0, CH // 8, some, 0)


def mix_tile(mix, depth, k, t):
    tile = depth[k, pl.ds(8 * t, 8)].reshape(8 * CH, NX)
    return dot3(mix, parts(tile)).reshape(CH, 8, NX)


def pack_kernel(tiles, field, packed, edges, taken, sem_in):
    last = field.shape[1] // 8 - 1
    before, after = tiles[0] - 1, tiles[-1] + 1
    wanted = [before, *tiles, after] + [t for t in (0, last) if t not in (before, after)]
    row = fetch_tiles(field, taken, sem_in, wanted)
    for i, place in enumerate([(before, 7), *[(t, r) for t in tiles for r in range(8)], (after, 0)]):
        packed[i] = row(*place)
    edges[0] = row(last, 7)
    edges[1] = row(0, 0)


def own_kernel(segments, groups, weight, point, field, halo, *refs):
    last = field.shape[1] // 8 - 1
    count = 3 * len(groups)
    outs, (taken, halo_rows, weights, points, sent, lined, depth, gains, sem_in, sem_out, sem_few) = (
        refs[:count],
        refs[count:],
    )
    few = [
        pltpu.make_async_copy(src, dst, sem_few.at[i])
        for i, (src, dst) in enumerate(((weight, weights), (point, points), (halo, halo_rows)))
    ]
    for copy in few:
        copy.start()
    wanted = sorted({t for tiles in segments for t in (tiles[0] - 1, *tiles, tiles[-1] + 1) if 0 <= t <= last})
    row = fetch_tiles(field, taken, sem_in, wanted)
    for copy in few:
        copy.wait()
    spread_gains(weights, gains, range(3))
    mix = mixing(points[...])
    runs, at, done, order = [], 0, 0, []
    for tiles in segments:
        places = [(tiles[0] - 1, 7), *[(t, r) for t in tiles for r in range(8)], (tiles[-1] + 1, 0)]
        for i, (t, r) in enumerate(places):
            lined[at + i] = halo_rows[0] if t < 0 else halo_rows[1] if t > last else row(t, r)
        runs.append((at, done, 8 * len(tiles)))
        at, done = at + len(places), done + 8 * len(tiles)
        order += tiles
    tap_sums(lambda s, r, c: lined[r, c, :], [[(a, a) for a in range(3)]], gains, depth, runs)
    copies = []
    for g, tiles in enumerate(groups):
        for i, tile in enumerate(tiles):
            t = order.index(tile)
            for k in range(3):
                sent[k, t] = mix_tile(mix, depth, k, t)
                to = outs[3 * g + k].at[:, pl.ds(8 * i, 8), :]
                copies.append(pltpu.make_async_copy(sent.at[k, t], to, sem_out.at[k, t]))
                copies[-1].start()
    for copy in copies:
        copy.wait()


def middle_kernel(weight, point, low, own, high, out, taken, weights, points, sent, depth, gains, sem_in, sem_out):
    copies = [
        pltpu.make_async_copy(src, dst, sem_in.at[i])
        for i, (src, dst) in enumerate(
            ((weight, weights), (point, points), (low, taken.at[0]), (own, taken.at[1]), (high, taken.at[2]))
        )
    ]
    for copy in copies:
        copy.start()
    for copy in copies[:2]:
        copy.wait()
    spread_gains(weights, gains, range(3))
    mix = mixing(points[...])
    for copy in copies[2:]:
        copy.wait()
    rows = out.shape[1]
    tap_sums(lambda s, r, c: taken[s, r, c, :], [[(a, 0)] for a in range(3)], gains, depth, [(0, 0, rows)])
    copies = []
    for t in range(rows // 8):
        sent[t] = mix_tile(mix, depth, 0, t)
        copies.append(pltpu.make_async_copy(sent.at[t], out.at[:, pl.ds(8 * t, 8), :], sem_out.at[t]))
        copies[-1].start()
    for copy in copies:
        copy.wait()


def gelu(value):
    size = jnp.abs(value) * math.sqrt(0.5)
    below = 1.0 + 0.3275911 * size
    t = pl.reciprocal(below, approx=True)
    t = t * (2.0 - below * t)
    series = 1.061405429 * t - 1.453152027
    for factor in (1.421413741, -0.284496736, 0.254829592):
        series = series * t + factor
    tail = 0.5 * (series * t) * jnp.exp(-(size * size))
    return value * jnp.where(value < 0.0, tail, 1.0 - tail)


def inverse_kernel(upper, halved, first_modes, second_modes, bias, x_top, x_rest, y_top, y_rest, own, middle, second, low, high, out, base, columns):
    q = pl.program_id(0)
    groups, _, y_local, _ = out.shape

    @pl.when(q == 0)
    def _():
        gy = lax.axis_index("gy")
        for g in range(groups):
            pairs = []
            for pair in (2 * g, 2 * g + 1):
                some = pl.ds(pair * (MY // 2), MY // 2)
                one, two = first_modes[some, :], second_modes[some, :]
                if halved:
                    one, two = jnp.where(gy == 0, one, two), jnp.where(gy == 0, two, one)
                pairs.append(jnp.concatenate([one, two], axis=0))
            own_modes = jnp.concatenate(pairs, axis=1)
            crossed, is_real = swap_parts(own_modes)
            stack = jnp.concatenate([own_modes, jnp.where(is_real, -crossed, crossed)], axis=0)
            pair = parts(dot3((y_top[gy], y_rest[gy]), parts(stack)))
            for h in range(2):
                for k in range(2):
                    columns[h, k, pl.ds(g * y_local, y_local), :] = pair[k][:, 128 * h : 128 * h + 128]

    h, p = q // 2, q % 2
    rows = dot3((columns[h, 0], columns[h, 1]), (x_top[p], x_rest[p]))
    turn = upper + middle.shape[2]
    stop = turn + second.shape[2]
    for g in range(groups):
        plane = rows[g * y_local : (g + 1) * y_local] + bias[4 * g + q]
        base[g, 0, :upper] = plane[:upper] + own[g, 0, :upper]
        out[g, 0, upper:turn] = gelu(plane[upper:turn] + middle[g, 0])
        out[g, 0, turn:stop] = gelu(plane[turn:stop] + (second[g, 0] + (low[g, 0] + high[g, 0])))
        base[g, 0, upper:] = plane[stop:] + own[g, 0, upper:]


def finish_kernel(upper, _, base, low, high, out, sent, sem):
    tiles = base.shape[1] // 8
    gap = out.shape[1] // 8 - tiles
    copies = []
    for t in range(tiles):
        rows = pl.ds(8 * t, 8)
        sent[t] = gelu(base[:, rows, :] + (low[:, rows, :] + high[:, rows, :]))
        to = t if t < upper else t + gap
        copies.append(pltpu.make_async_copy(sent.at[t], out.at[:, pl.ds(8 * to, 8), :], sem.at[t]))
        copies[-1].start()
    for copy in copies:
        copy.wait()


def in_hbm(*arrays):
    return [pltpu.with_memory_space_constraint(a, pltpu.HBM) for a in arrays]


def params(limit=VMEM_BYTES):
    return pltpu.CompilerParams(vmem_limit_bytes=limit)


def cost(flops, moved):
    return pl.CostEstimate(flops=flops, bytes_accessed=moved, transcendentals=0)


def whole_block(table):
    return pl.BlockSpec(table.shape, lambda i: (0,) * table.ndim)


def by_four(array):
    return array.reshape(CH // 4, 4, *array.shape[1:])


def forward_call(field, gy, pinned):
    y_local = field.shape[1]
    tables = [*halves(x_table(False)), *halves(y_table(y_local, gy, False))]
    hbm = pl.BlockSpec(memory_space=pltpu.HBM)
    return pl.pallas_call(
        forward_kernel,
        out_shape=(pltpu.HBM if pinned else jax.ShapeDtypeStruct)((CH // 2 * MY, 4 * MX), F32),
        in_specs=[hbm] * 5,
        scratch_shapes=[
            pltpu.VMEM((4, CH // 4, y_local, NX), F32),
            pltpu.VMEM((2, 2, NX, 4 * MX), BF),
            pltpu.VMEM((2, 2 * MY, y_local), BF),
            pltpu.SemaphoreType.DMA((8,)),
        ],
        compiler_params=params(ALL_VMEM_BYTES),
        cost_estimate=cost(10**8, 2**18),
        name="forward_modes",
    )(*in_hbm(by_four(field), *tables))


def filter_call(arrived, gains, gz, gy, scale):
    fwd, inv = z_tables(gz, gy, gains.shape[2], scale)
    fwd, inv = halves(fwd), halves(inv)
    return pl.pallas_call(
        filter_kernel,
        out_shape=pltpu.HBM((arrived.shape[0] // gy, arrived.shape[1]), F32),
        compiler_params=params(),
        cost_estimate=cost(4 * 10**10, 2**18),
        name="filter_modes",
    )(arrived, *in_hbm(gains, *fwd, *inv))


def inverse_call(modes, halved, bias, own, middle, second, pair, upper, y_local, gy, scale):
    tables = [*halves(x_table(True, scale)), *halves(y_table(y_local, gy, True))]
    some = lambda rows: pl.BlockSpec((CH // 4, 1, rows, NX), lambda i: (0, i, 0, 0))
    planes = [*in_hbm(*map(by_four, (own, middle, second))), *map(by_four, pair)]
    rim = own.shape[1]
    result, base = pl.pallas_call(
        functools.partial(inverse_kernel, upper, halved),
        out_shape=[
            jax.ShapeDtypeStruct((CH // 4, 4, y_local, NX), F32),
            jax.ShapeDtypeStruct((CH // 4, 4, rim, NX), F32),
        ],
        grid=(4,),
        in_specs=[
            *[whole_block(m) for m in modes],
            pl.BlockSpec(memory_space=pltpu.SMEM),
            *[whole_block(t) for t in tables],
            *[some(p.shape[2]) for p in planes],
        ],
        out_specs=[some(y_local), some(rim)],
        scratch_shapes=[pltpu.VMEM((2, 2, CH // 4 * y_local, 128), BF)],
        compiler_params=params(),
        cost_estimate=cost(10**8, 2**18),
        name="inverse_modes",
    )(*modes, *in_hbm(bias, *tables), *planes)
    return result.reshape(CH, y_local, NX), base.reshape(CH, rim, NX)


def finish_call(result, base, low, high, upper):
    tiles = base.shape[1] // 8
    anywhere = pl.BlockSpec(memory_space=pl.ANY)
    vmem = pl.BlockSpec(memory_space=pltpu.VMEM)
    return pl.pallas_call(
        functools.partial(finish_kernel, upper),
        out_shape=jax.ShapeDtypeStruct(result.shape, F32),
        in_specs=[anywhere] + [vmem] * 3,
        out_specs=anywhere,
        scratch_shapes=[
            pltpu.VMEM((tiles, CH, 8, NX), F32),
            pltpu.SemaphoreType.DMA((tiles,)),
        ],
        input_output_aliases={0: 0},
        compiler_params=params(),
        cost_estimate=cost(10**8, 2**18),
        name="finished_rows",
    )(result, base, low, high)


def pack_call(field, tiles):
    count = 8 * len(tiles) + 2
    fetched = len(tiles) + 4
    vmem = pl.BlockSpec(memory_space=pltpu.VMEM)
    return pl.pallas_call(
        functools.partial(pack_kernel, tiles),
        out_shape=[jax.ShapeDtypeStruct((count, CH, NX), F32), jax.ShapeDtypeStruct((2, CH, NX), F32)],
        in_specs=[pl.BlockSpec(memory_space=pltpu.HBM)],
        out_specs=[vmem] * 2,
        scratch_shapes=[
            pltpu.VMEM((fetched, 2, CH, 8, 128), F32),
            pltpu.SemaphoreType.DMA((fetched, 2)),
        ],
        compiler_params=params(),
        cost_estimate=cost(10**8, 2**18),
        name="packed_rows",
    )(*in_hbm(field))


def own_call(field, halo, weight, point, segments, groups):
    tiles = sum(map(len, segments))
    rows, fetched = 8 * tiles, tiles + 2 * len(segments)
    hbm = pl.BlockSpec(memory_space=pltpu.HBM)
    shapes = [pltpu.HBM((CH, 8 * len(group), NX), F32) for group in groups for _ in range(3)]
    return pl.pallas_call(
        functools.partial(own_kernel, segments, groups),
        out_shape=shapes,
        in_specs=[hbm] * 3 + [pl.BlockSpec(memory_space=pl.ANY)],
        out_specs=[hbm] * len(shapes),
        scratch_shapes=[
            pltpu.VMEM((fetched, 2, CH, 8, 128), F32),
            pltpu.VMEM((2, CH, NX), F32),
            pltpu.VMEM((CH, 27), F32),
            pltpu.VMEM((CH, CH), F32),
            pltpu.VMEM((3, tiles, CH, 8, NX), F32),
            pltpu.VMEM((rows + 2 * len(segments), CH, NX), F32),
            pltpu.VMEM((3, rows, CH, NX), F32),
            pltpu.VMEM((27, CH, 128), F32),
            pltpu.SemaphoreType.DMA((fetched, 2)),
            pltpu.SemaphoreType.DMA((3, tiles)),
            pltpu.SemaphoreType.DMA((3,)),
        ],
        compiler_params=params(),
        cost_estimate=cost(10**8, 2**18),
        name="own_sums",
    )(*in_hbm(weight, point, field), halo)


def middle_call(weight, point, low, own, high):
    rows = own.shape[0] - 2
    hbm = pl.BlockSpec(memory_space=pltpu.HBM)
    return pl.pallas_call(
        middle_kernel,
        out_shape=pltpu.HBM((CH, rows, NX), F32),
        in_specs=[hbm] * 3 + [pl.BlockSpec(memory_space=pl.ANY), hbm],
        out_specs=hbm,
        scratch_shapes=[
            pltpu.VMEM((3, rows + 2, CH, NX), F32),
            pltpu.VMEM((CH, 27), F32),
            pltpu.VMEM((CH, CH), F32),
            pltpu.VMEM((rows // 8, CH, 8, NX), F32),
            pltpu.VMEM((1, rows, CH, NX), F32),
            pltpu.VMEM((27, CH, 128), F32),
            pltpu.SemaphoreType.DMA((5,)),
            pltpu.SemaphoreType.DMA((rows // 8,)),
        ],
        compiler_params=params(),
        cost_estimate=cost(4 * 10**10, 2**18),
        name="middle_sums",
    )(*in_hbm(weight, point, low), own, *in_hbm(high))


def general_filter(coarse, gains, gz, gy, scale):
    j_own, n_own = gains.shape[2], gains.shape[3]
    both = ("gz", "gy")
    flat = coarse.reshape(CH // 2, MY, 2, 2, MX).transpose(3, 1, 0, 2, 4).reshape(2, MY, CH * MX)
    sent = flat.reshape(2, gy, j_own, gz, n_own).transpose(3, 1, 0, 2, 4).reshape(gz * gy, -1)
    got = lax.all_to_all(sent, both, split_axis=0, concat_axis=0, tiled=True)
    got = got.reshape(gz, gy, 2, j_own, n_own)
    c, s = (jnp.asarray(t, F32) for t in trig(kept(MZ, gz), np.arange(gz), gz))
    mul = functools.partial(jnp.einsum, precision=lax.Precision.HIGHEST)
    whole = got.sum(axis=1) * scale
    real = mul("zjn,qz->qjn", whole[:, 0], c) + mul("zjn,qz->qjn", whole[:, 1], s)
    imag = mul("zjn,qz->qjn", whole[:, 1], c) - mul("zjn,qz->qjn", whole[:, 0], s)
    real, imag = real * gains[0] - imag * gains[1], real * gains[1] + imag * gains[0]
    out = jnp.stack(
        [
            mul("qjn,qz->zjn", real, c) - mul("qjn,qz->zjn", imag, s),
            mul("qjn,qz->zjn", real, s) + mul("qjn,qz->zjn", imag, c),
        ],
        axis=1,
    )
    out = jnp.broadcast_to(out[:, None], (gz, gy, 2, j_own, n_own)).reshape(gz * gy, -1)
    back = lax.all_to_all(out, both, split_axis=0, concat_axis=0, tiled=True)
    back = back.reshape(gz, gy, 2, j_own, n_own).transpose(2, 1, 3, 0, 4)
    back = back.reshape(2, MY, CH // 2, 2, MX)
    return back.transpose(2, 1, 3, 0, 4).reshape(CH // 2, MY, 4 * MX)


def body(field, spectral_filter, depth_weight, point_weight, bias_vector):
    gz, gy = lax.axis_size("gz"), lax.axis_size("gy")
    y_local = field.shape[2]
    field = field.reshape(CH, y_local, NX)
    y_total = gy * y_local
    forward_scale = 1.0 / math.sqrt(float(NX) * y_total * gz)
    inverse_scale = 1.0 / math.sqrt(2.0 * MX * MY * MZ)

    def ring(axis, count, by):
        return [(i, (i + by) % count) for i in range(count)]

    def to_neighbours(down, up):
        return (
            lax.ppermute(down, "gz", ring("gz", gz, 1)),
            lax.ppermute(up, "gz", ring("gz", gz, -1)),
        )

    def after(value, *others):
        return lax.optimization_barrier((value, *others))[0]

    last = y_local // 8 - 1
    cut = 1 + last // 2
    first_tiles, second_tiles = tuple(range(1, cut)), tuple(range(cut, min(cut + 2, last)))
    third_tiles = (0, *range(second_tiles[-1] + 1, last + 1))
    packed, edges = pack_call(field, first_tiles)
    first_low, first_high = to_neighbours(packed, packed)
    if gy == 2:
        halo = lax.ppermute(edges, "gy", ring("gy", gy, 1))
    else:
        halo = jnp.stack(
            [
                lax.ppermute(edges[0], "gy", ring("gy", gy, 1)),
                lax.ppermute(edges[1], "gy", ring("gy", gy, -1)),
            ]
        )
    j_own, n_own = spectral_filter.shape[2], spectral_filter.shape[3]
    whole_tiles = j_own == 8 and n_own == 2 * MX
    coarse = after(forward_call(after(field, packed), gy, whole_tiles), halo)
    segments, groups = ((0,), tuple(range(cut, last + 1))), (second_tiles, third_tiles)
    down, second, up, outer_down, own, outer_up = own_call(
        after(field, coarse), halo, depth_weight, point_weight, segments, groups
    )
    if whole_tiles:
        both = ("gz", "gy")
        got = lax.all_to_all(coarse, both, split_axis=0, concat_axis=0, tiled=True)
        down, up = lax.optimization_barrier((down, up, first_low))[:2]
        pair = to_neighbours(down, up)
        gains = after(spectral_filter, first_low, first_high, second)
        mark = filter_call(got, gains, gz, gy, forward_scale)
        back = lax.all_to_all(mark, "gz", split_axis=0, concat_axis=0, tiled=True)
    else:
        pair = to_neighbours(down, up)
        mark = general_filter(coarse, spectral_filter, gz, gy, forward_scale)
        modes = [mark[:, part].reshape(-1, 4 * MX) for part in (slice(0, MY // 2), slice(MY // 2, MY))]
    outer_pair = to_neighbours(after(outer_down, mark), after(outer_up, mark))
    packed, *pair = lax.optimization_barrier((packed, *pair))
    mixed = middle_call(depth_weight, point_weight, first_low, packed, first_high)
    if whole_tiles:
        modes = (back, lax.ppermute(after(back, mixed), "gy", ring("gy", gy, 1)))
    result, base = inverse_call(
        modes, whole_tiles, bias_vector, own, mixed, second, pair, 8, y_local, gy, inverse_scale
    )
    result = finish_call(result, base, *outer_pair, 1)
    return result.reshape(CH, 1, y_local, NX)


def solution(mesh):
    in_specs = (P(None, "gz", "gy", None), P(None, None, "gy", "gz"), P(), P(), P())
    out_specs = P(None, "gz", "gy", None)
    return jax.shard_map(body, mesh=mesh, in_specs=in_specs, out_specs=out_specs, check_vma=False)
```

```python
import functools
import math

import jax
import jax.numpy as jnp
import ml_dtypes
import numpy as np
from jax import lax
from jax.experimental import pallas as pl
from jax.experimental.pallas import tpu as pltpu
from jax.sharding import PartitionSpec as P

NX = 256
MX = 32
MY = 16
MZ = 16
CH = 32
VMEM_BYTES = 20 * 1024 * 1024
ALL_VMEM_BYTES = 64000 * 1024
BF = jnp.bfloat16
F32 = jnp.float32


def kept(count, total):
    series = np.arange(count)
    return np.where(series < count // 2, series, total - count + series)


def trig(freqs, places, total):
    angle = 2.0 * np.pi * ((freqs[:, None] * places[None, :]) % total) / total
    return np.cos(angle), np.sin(angle)


def halves(table):
    table = np.asarray(table, np.float64)
    top = table.astype(np.float32).astype(ml_dtypes.bfloat16)
    rest = (table - top.astype(np.float64)).astype(np.float32).astype(ml_dtypes.bfloat16)
    return jnp.asarray(top), jnp.asarray(rest)


def y_table(y_local, gy, inverse):
    out = []
    for g in range(gy):
        places = g * y_local + np.arange(y_local)
        out.append(np.concatenate(trig(kept(MY, y_local * gy), places, y_local * gy), axis=0))
    return np.stack([t.T for t in out] if inverse else out)


def x_table(inverse, scale=1.0):
    c, s = trig(np.arange(MX), np.arange(NX), NX)
    w = np.where(np.arange(MX) == 0, 1.0, 2.0)[:, None] if inverse else 1.0
    out = np.zeros((2, 2, 2, MX, NX))
    for p in range(2):
        out[p, p, 0] = w * c * scale
        out[p, p, 1] = -w * s * scale
    out = out.reshape(2, 4 * MX, NX)
    return out if inverse else out.transpose(0, 2, 1)


def z_tables(gz, gy, rows, scale):
    c, s = trig(kept(MZ, gz), np.arange(gz), gz)
    eye = np.eye(rows)
    both = np.stack([c, s])
    fwd = np.einsum("tqz,g,jk->tqjzgk", both, np.ones(gy), eye) * scale
    inv = np.einsum("tqz,jk->tzjqk", both, eye)
    return fwd.reshape(2 * MZ * rows, gz * gy * rows), inv.reshape(2 * gz * rows, MZ * rows)


def parts(value):
    top = value.astype(BF)
    return top, (value - top.astype(F32)).astype(BF)


def dot(a, b):
    return jnp.dot(a, b, preferred_element_type=F32)


def dot3(a, b):
    rows = a[0].shape[0]
    both = dot(jnp.concatenate([a[0], a[1]], axis=0), b[0])
    return both[:rows] + (both[rows:] + dot(a[0], b[1]))


def swap_parts(value):
    lane = lax.broadcasted_iota(jnp.int32, value.shape, 1)
    is_real = (lane // MX) % 2 == 0
    width = value.shape[1]
    return jnp.where(is_real, pltpu.roll(value, width - MX, 1), pltpu.roll(value, MX, 1)), is_real


def forward_kernel(field, x_top, x_rest, y_top, y_rest, out, taken, x_both, y_both, sem):
    gy = lax.axis_index("gy")
    few = [
        pltpu.make_async_copy(src, dst, sem.at[4 + i])
        for i, (src, dst) in enumerate(
            ((x_top, x_both.at[0]), (x_rest, x_both.at[1]), (y_top.at[gy], y_both.at[0]), (y_rest.at[gy], y_both.at[1]))
        )
    ]
    copies = [pltpu.make_async_copy(field.at[:, q], taken.at[q], sem.at[q]) for q in range(4)]
    for copy in few + copies:
        copy.start()
    for copy in few:
        copy.wait()
    groups, rows = taken.shape[1:3]
    halves_of = []
    for q in range(4):
        copies[q].wait()
        part = dot3(parts(taken[q].reshape(groups * rows, NX)), (x_both[0, q % 2], x_both[1, q % 2]))
        if q % 2:
            halves_of[-1] = halves_of[-1] + part
        else:
            halves_of.append(part)
    total = jnp.concatenate(halves_of, axis=1)
    for g in range(groups):
        both = dot3((y_both[0], y_both[1]), parts(total[g * rows : (g + 1) * rows]))
        crossed, is_real = swap_parts(both[MY:])
        modes = both[:MY] + jnp.where(is_real, crossed, -crossed)
        out[pl.ds(2 * g * MY, MY), :] = modes[:, : 4 * MX]
        out[pl.ds((2 * g + 1) * MY, MY), :] = modes[:, 4 * MX :]


def filter_kernel(arrived, gains, f_top, f_rest, i_top, i_rest, out):
    real, imag = (gains[r].reshape(-1, 2 * MX) for r in range(2))
    first, second = slice(0, MX), slice(MX, 2 * MX)
    same = jnp.concatenate([real[:, first], real[:, first], real[:, second], real[:, second]], axis=1)
    cross = jnp.concatenate([-imag[:, first], imag[:, first], -imag[:, second], imag[:, second]], axis=1)
    half = f_top.shape[0] // 2
    turned = dot3((f_top[...], f_rest[...]), parts(arrived[...]))
    crossed, is_real = swap_parts(turned[half:])
    modes = turned[:half] + jnp.where(is_real, crossed, -crossed)
    crossed, _ = swap_parts(modes)
    filtered = modes * same + crossed * cross
    half = i_top.shape[0] // 2
    back = dot3((i_top[...], i_rest[...]), parts(filtered))
    crossed, is_real = swap_parts(back[half:])
    out[...] = back[:half] + jnp.where(is_real, -crossed, crossed)


def fetch_tiles(field, taken, sems, wanted):
    pending = {}
    for k, t in enumerate(wanted):
        pending[t] = [
            pltpu.make_async_copy(
                field.at[:, pl.ds(8 * t, 8), pl.ds(128 * h, 128)], taken.at[k, h], sems.at[k, h]
            )
            for h in range(2)
        ]
        for copy in pending[t]:
            copy.start()

    def row(t, r):
        for copy in pending.pop(t, ()):
            copy.wait()
        k = wanted.index(t)
        return jnp.concatenate(
            [taken.at[k, h].reshape(CH * 8, 128)[pl.ds(r, CH, stride=8), :] for h in range(2)], axis=1
        )

    return row


def spread_gains(weights, gains, offsets):
    for k in [9 * a + j for a in offsets for j in range(9)]:
        gains[k] = jnp.broadcast_to(weights[:, k : k + 1], (CH, 128))


def mixing(points):
    down = (
        lax.broadcasted_iota(jnp.int32, (8 * CH, CH), 0) // 8
        == lax.broadcasted_iota(jnp.int32, (8 * CH, CH), 1)
    ).astype(BF)
    across = (
        lax.broadcasted_iota(jnp.int32, (CH, 8 * CH), 1) % CH
        == lax.broadcasted_iota(jnp.int32, (CH, 8 * CH), 0)
    ).astype(BF)
    same = (
        lax.broadcasted_iota(jnp.int32, (8 * CH, 8 * CH), 0) % 8
        == lax.broadcasted_iota(jnp.int32, (8 * CH, 8 * CH), 1) // CH
    )
    return tuple(
        jnp.where(same, dot(dot(down, part).astype(BF), across), 0.0).astype(BF)
        for part in parts(points)
    )


def tap_sums(load, uses, gains, depth, runs):
    def some(i, _):
        chans = pl.ds(pl.multiple_of(i * 8, 8), 8)
        wanted = sorted({a for use in uses for a, _ in use})
        gain = {k: gains[k, chans, :] for a in wanted for k in range(9 * a, 9 * a + 9)}
        for first, to, rows in runs:
            sums = {}
            for r in range(rows + 2):
                for s, use in enumerate(uses):
                    value = load(s, first + r, chans)
                    turned = (pltpu.roll(value, 1, 1), value, pltpu.roll(value, NX - 1, 1))
                    for b in range(3):
                        o = r - b
                        if o < 0 or o >= rows:
                            continue
                        for a, k in use:
                            for e in range(3):
                                for h in range(2):
                                    term = gain[a * 9 + b * 3 + e] * turned[e][:, 128 * h : 128 * h + 128]
                                    place = (o, k, h)
                                    sums[place] = sums[place] + term if place in sums else term
                if r >= 2:
                    for k in sorted({k for use in uses for _, k in use}):
                        for h in range(2):
                            depth[k, to + r - 2, chans, pl.ds(128 * h, 128)] = sums.pop((r - 2, k, h))
        return 0

    lax.fori_loop(0, CH // 8, some, 0)


def mix_tile(mix, depth, k, t):
    tile = depth[k, pl.ds(8 * t, 8)].reshape(8 * CH, NX)
    return dot3(mix, parts(tile)).reshape(CH, 8, NX)


def pack_kernel(tiles, field, packed, edges, taken, sem_in):
    last = field.shape[1] // 8 - 1
    before, after = tiles[0] - 1, tiles[-1] + 1
    wanted = [before, *tiles, after] + [t for t in (0, last) if t not in (before, after)]
    row = fetch_tiles(field, taken, sem_in, wanted)
    for i, place in enumerate([(before, 7), *[(t, r) for t in tiles for r in range(8)], (after, 0)]):
        packed[i] = row(*place)
    edges[0] = row(last, 7)
    edges[1] = row(0, 0)


def own_kernel(segments, groups, weight, point, field, halo, *refs):
    last = field.shape[1] // 8 - 1
    count = 3 * len(groups)
    outs, (taken, halo_rows, weights, points, sent, lined, depth, gains, sem_in, sem_out, sem_few) = (
        refs[:count],
        refs[count:],
    )
    few = [
        pltpu.make_async_copy(src, dst, sem_few.at[i])
        for i, (src, dst) in enumerate(((weight, weights), (point, points), (halo, halo_rows)))
    ]
    for copy in few:
        copy.start()
    wanted = sorted({t for tiles in segments for t in (tiles[0] - 1, *tiles, tiles[-1] + 1) if 0 <= t <= last})
    row = fetch_tiles(field, taken, sem_in, wanted)
    for copy in few:
        copy.wait()
    spread_gains(weights, gains, range(3))
    mix = mixing(points[...])
    runs, at, done, order = [], 0, 0, []
    for tiles in segments:
        places = [(tiles[0] - 1, 7), *[(t, r) for t in tiles for r in range(8)], (tiles[-1] + 1, 0)]
        for i, (t, r) in enumerate(places):
            lined[at + i] = halo_rows[0] if t < 0 else halo_rows[1] if t > last else row(t, r)
        runs.append((at, done, 8 * len(tiles)))
        at, done = at + len(places), done + 8 * len(tiles)
        order += tiles
    tap_sums(lambda s, r, c: lined[r, c, :], [[(a, a) for a in range(3)]], gains, depth, runs)
    copies = []
    for g, tiles in enumerate(groups):
        for i, tile in enumerate(tiles):
            t = order.index(tile)
            for k in range(3):
                sent[k, t] = mix_tile(mix, depth, k, t)
                to = outs[3 * g + k].at[:, pl.ds(8 * i, 8), :]
                copies.append(pltpu.make_async_copy(sent.at[k, t], to, sem_out.at[k, t]))
                copies[-1].start()
    for copy in copies:
        copy.wait()


def middle_kernel(weight, point, low, own, high, out, taken, weights, points, sent, depth, gains, sem_in, sem_out):
    copies = [
        pltpu.make_async_copy(src, dst, sem_in.at[i])
        for i, (src, dst) in enumerate(
            ((weight, weights), (point, points), (low, taken.at[0]), (own, taken.at[1]), (high, taken.at[2]))
        )
    ]
    for copy in copies:
        copy.start()
    for copy in copies[:2]:
        copy.wait()
    spread_gains(weights, gains, range(3))
    mix = mixing(points[...])
    for copy in copies[2:]:
        copy.wait()
    rows = out.shape[1]
    tap_sums(lambda s, r, c: taken[s, r, c, :], [[(a, 0)] for a in range(3)], gains, depth, [(0, 0, rows)])
    copies = []
    for t in range(rows // 8):
        sent[t] = mix_tile(mix, depth, 0, t)
        copies.append(pltpu.make_async_copy(sent.at[t], out.at[:, pl.ds(8 * t, 8), :], sem_out.at[t]))
        copies[-1].start()
    for copy in copies:
        copy.wait()


def gelu(value):
    size = jnp.abs(value) * math.sqrt(0.5)
    below = 1.0 + 0.3275911 * size
    t = pl.reciprocal(below, approx=True)
    t = t * (2.0 - below * t)
    series = 1.061405429 * t - 1.453152027
    for factor in (1.421413741, -0.284496736, 0.254829592):
        series = series * t + factor
    tail = 0.5 * (series * t) * jnp.exp(-(size * size))
    return value * jnp.where(value < 0.0, tail, 1.0 - tail)


def inverse_kernel(upper, halved, first_modes, second_modes, bias, x_top, x_rest, y_top, y_rest, own, middle, second, low, high, out, base, columns):
    q = pl.program_id(0)
    groups, _, y_local, _ = out.shape

    @pl.when(q == 0)
    def _():
        gy = lax.axis_index("gy")
        for g in range(groups):
            pairs = []
            for pair in (2 * g, 2 * g + 1):
                some = pl.ds(pair * (MY // 2), MY // 2)
                one, two = first_modes[some, :], second_modes[some, :]
                if halved:
                    one, two = jnp.where(gy == 0, one, two), jnp.where(gy == 0, two, one)
                pairs.append(jnp.concatenate([one, two], axis=0))
            own_modes = jnp.concatenate(pairs, axis=1)
            crossed, is_real = swap_parts(own_modes)
            stack = jnp.concatenate([own_modes, jnp.where(is_real, -crossed, crossed)], axis=0)
            pair = parts(dot3((y_top[gy], y_rest[gy]), parts(stack)))
            for h in range(2):
                for k in range(2):
                    columns[h, k, pl.ds(g * y_local, y_local), :] = pair[k][:, 128 * h : 128 * h + 128]

    h, p = q // 2, q % 2
    rows = dot3((columns[h, 0], columns[h, 1]), (x_top[p], x_rest[p]))
    turn = upper + middle.shape[2]
    stop = turn + second.shape[2]
    for g in range(groups):
        plane = rows[g * y_local : (g + 1) * y_local] + bias[4 * g + q]
        base[g, 0, :upper] = plane[:upper] + own[g, 0, :upper]
        out[g, 0, upper:turn] = gelu(plane[upper:turn] + middle[g, 0])
        out[g, 0, turn:stop] = gelu(plane[turn:stop] + (second[g, 0] + (low[g, 0] + high[g, 0])))
        base[g, 0, upper:] = plane[stop:] + own[g, 0, upper:]


def finish_kernel(upper, _, base, low, high, out, sent, sem):
    tiles = base.shape[1] // 8
    gap = out.shape[1] // 8 - tiles
    copies = []
    for t in range(tiles):
        rows = pl.ds(8 * t, 8)
        sent[t] = gelu(base[:, rows, :] + (low[:, rows, :] + high[:, rows, :]))
        to = t if t < upper else t + gap
        copies.append(pltpu.make_async_copy(sent.at[t], out.at[:, pl.ds(8 * to, 8), :], sem.at[t]))
        copies[-1].start()
    for copy in copies:
        copy.wait()


def in_hbm(*arrays):
    return [pltpu.with_memory_space_constraint(a, pltpu.HBM) for a in arrays]


def params(limit=VMEM_BYTES):
    return pltpu.CompilerParams(vmem_limit_bytes=limit)


def cost(flops, moved):
    return pl.CostEstimate(flops=flops, bytes_accessed=moved, transcendentals=0)


def whole_block(table):
    return pl.BlockSpec(table.shape, lambda i: (0,) * table.ndim)


def by_four(array):
    return array.reshape(CH // 4, 4, *array.shape[1:])


def forward_call(field, gy, pinned):
    y_local = field.shape[1]
    tables = [*halves(x_table(False)), *halves(y_table(y_local, gy, False))]
    hbm = pl.BlockSpec(memory_space=pltpu.HBM)
    return pl.pallas_call(
        forward_kernel,
        out_shape=(pltpu.HBM if pinned else jax.ShapeDtypeStruct)((CH // 2 * MY, 4 * MX), F32),
        in_specs=[hbm] * 5,
        scratch_shapes=[
            pltpu.VMEM((4, CH // 4, y_local, NX), F32),
            pltpu.VMEM((2, 2, NX, 4 * MX), BF),
            pltpu.VMEM((2, 2 * MY, y_local), BF),
            pltpu.SemaphoreType.DMA((8,)),
        ],
        compiler_params=params(ALL_VMEM_BYTES),
        cost_estimate=cost(10**8, 2**18),
        name="forward_modes",
    )(*in_hbm(by_four(field), *tables))


def filter_call(arrived, gains, gz, gy, scale):
    fwd, inv = z_tables(gz, gy, gains.shape[2], scale)
    fwd, inv = halves(fwd), halves(inv)
    return pl.pallas_call(
        filter_kernel,
        out_shape=pltpu.HBM((arrived.shape[0] // gy, arrived.shape[1]), F32),
        compiler_params=params(),
        cost_estimate=cost(4 * 10**10, 2**18),
        name="filter_modes",
    )(arrived, *in_hbm(gains, *fwd, *inv))


def inverse_call(modes, halved, bias, own, middle, second, pair, upper, y_local, gy, scale):
    tables = [*halves(x_table(True, scale)), *halves(y_table(y_local, gy, True))]
    some = lambda rows: pl.BlockSpec((CH // 4, 1, rows, NX), lambda i: (0, i, 0, 0))
    planes = [*in_hbm(*map(by_four, (own, middle, second))), *map(by_four, pair)]
    rim = own.shape[1]
    result, base = pl.pallas_call(
        functools.partial(inverse_kernel, upper, halved),
        out_shape=[
            jax.ShapeDtypeStruct((CH // 4, 4, y_local, NX), F32),
            jax.ShapeDtypeStruct((CH // 4, 4, rim, NX), F32),
        ],
        grid=(4,),
        in_specs=[
            *[whole_block(m) for m in modes],
            pl.BlockSpec(memory_space=pltpu.SMEM),
            *[whole_block(t) for t in tables],
            *[some(p.shape[2]) for p in planes],
        ],
        out_specs=[some(y_local), some(rim)],
        scratch_shapes=[pltpu.VMEM((2, 2, CH // 4 * y_local, 128), BF)],
        compiler_params=params(),
        cost_estimate=cost(10**8, 2**18),
        name="inverse_modes",
    )(*modes, *in_hbm(bias, *tables), *planes)
    return result.reshape(CH, y_local, NX), base.reshape(CH, rim, NX)


def finish_call(result, base, low, high, upper):
    tiles = base.shape[1] // 8
    anywhere = pl.BlockSpec(memory_space=pl.ANY)
    vmem = pl.BlockSpec(memory_space=pltpu.VMEM)
    return pl.pallas_call(
        functools.partial(finish_kernel, upper),
        out_shape=jax.ShapeDtypeStruct(result.shape, F32),
        in_specs=[anywhere] + [vmem] * 3,
        out_specs=anywhere,
        scratch_shapes=[
            pltpu.VMEM((tiles, CH, 8, NX), F32),
            pltpu.SemaphoreType.DMA((tiles,)),
        ],
        input_output_aliases={0: 0},
        compiler_params=params(),
        cost_estimate=cost(10**8, 2**18),
        name="finished_rows",
    )(result, base, low, high)


def pack_call(field, tiles):
    count = 8 * len(tiles) + 2
    fetched = len(tiles) + 4
    vmem = pl.BlockSpec(memory_space=pltpu.VMEM)
    return pl.pallas_call(
        functools.partial(pack_kernel, tiles),
        out_shape=[jax.ShapeDtypeStruct((count, CH, NX), F32), jax.ShapeDtypeStruct((2, CH, NX), F32)],
        in_specs=[pl.BlockSpec(memory_space=pltpu.HBM)],
        out_specs=[vmem] * 2,
        scratch_shapes=[
            pltpu.VMEM((fetched, 2, CH, 8, 128), F32),
            pltpu.SemaphoreType.DMA((fetched, 2)),
        ],
        compiler_params=params(),
        cost_estimate=cost(10**8, 2**18),
        name="packed_rows",
    )(*in_hbm(field))


def own_call(field, halo, weight, point, segments, groups):
    tiles = sum(map(len, segments))
    rows, fetched = 8 * tiles, tiles + 2 * len(segments)
    hbm = pl.BlockSpec(memory_space=pltpu.HBM)
    shapes = [pltpu.HBM((CH, 8 * len(group), NX), F32) for group in groups for _ in range(3)]
    return pl.pallas_call(
        functools.partial(own_kernel, segments, groups),
        out_shape=shapes,
        in_specs=[hbm] * 3 + [pl.BlockSpec(memory_space=pl.ANY)],
        out_specs=[hbm] * len(shapes),
        scratch_shapes=[
            pltpu.VMEM((fetched, 2, CH, 8, 128), F32),
            pltpu.VMEM((2, CH, NX), F32),
            pltpu.VMEM((CH, 27), F32),
            pltpu.VMEM((CH, CH), F32),
            pltpu.VMEM((3, tiles, CH, 8, NX), F32),
            pltpu.VMEM((rows + 2 * len(segments), CH, NX), F32),
            pltpu.VMEM((3, rows, CH, NX), F32),
            pltpu.VMEM((27, CH, 128), F32),
            pltpu.SemaphoreType.DMA((fetched, 2)),
            pltpu.SemaphoreType.DMA((3, tiles)),
            pltpu.SemaphoreType.DMA((3,)),
        ],
        compiler_params=params(),
        cost_estimate=cost(10**8, 2**18),
        name="own_sums",
    )(*in_hbm(weight, point, field), halo)


def middle_call(weight, point, low, own, high):
    rows = own.shape[0] - 2
    hbm = pl.BlockSpec(memory_space=pltpu.HBM)
    return pl.pallas_call(
        middle_kernel,
        out_shape=pltpu.HBM((CH, rows, NX), F32),
        in_specs=[hbm] * 3 + [pl.BlockSpec(memory_space=pl.ANY), hbm],
        out_specs=hbm,
        scratch_shapes=[
            pltpu.VMEM((3, rows + 2, CH, NX), F32),
            pltpu.VMEM((CH, 27), F32),
            pltpu.VMEM((CH, CH), F32),
            pltpu.VMEM((rows // 8, CH, 8, NX), F32),
            pltpu.VMEM((1, rows, CH, NX), F32),
            pltpu.VMEM((27, CH, 128), F32),
            pltpu.SemaphoreType.DMA((5,)),
            pltpu.SemaphoreType.DMA((rows // 8,)),
        ],
        compiler_params=params(),
        cost_estimate=cost(4 * 10**10, 2**18),
        name="middle_sums",
    )(*in_hbm(weight, point, low), own, *in_hbm(high))


def general_filter(coarse, gains, gz, gy, scale):
    j_own, n_own = gains.shape[2], gains.shape[3]
    both = ("gz", "gy")
    flat = coarse.reshape(CH // 2, MY, 2, 2, MX).transpose(3, 1, 0, 2, 4).reshape(2, MY, CH * MX)
    sent = flat.reshape(2, gy, j_own, gz, n_own).transpose(3, 1, 0, 2, 4).reshape(gz * gy, -1)
    got = lax.all_to_all(sent, both, split_axis=0, concat_axis=0, tiled=True)
    got = got.reshape(gz, gy, 2, j_own, n_own)
    c, s = (jnp.asarray(t, F32) for t in trig(kept(MZ, gz), np.arange(gz), gz))
    mul = functools.partial(jnp.einsum, precision=lax.Precision.HIGHEST)
    whole = got.sum(axis=1) * scale
    real = mul("zjn,qz->qjn", whole[:, 0], c) + mul("zjn,qz->qjn", whole[:, 1], s)
    imag = mul("zjn,qz->qjn", whole[:, 1], c) - mul("zjn,qz->qjn", whole[:, 0], s)
    real, imag = real * gains[0] - imag * gains[1], real * gains[1] + imag * gains[0]
    out = jnp.stack(
        [
            mul("qjn,qz->zjn", real, c) - mul("qjn,qz->zjn", imag, s),
            mul("qjn,qz->zjn", real, s) + mul("qjn,qz->zjn", imag, c),
        ],
        axis=1,
    )
    out = jnp.broadcast_to(out[:, None], (gz, gy, 2, j_own, n_own)).reshape(gz * gy, -1)
    back = lax.all_to_all(out, both, split_axis=0, concat_axis=0, tiled=True)
    back = back.reshape(gz, gy, 2, j_own, n_own).transpose(2, 1, 3, 0, 4)
    back = back.reshape(2, MY, CH // 2, 2, MX)
    return back.transpose(2, 1, 3, 0, 4).reshape(CH // 2, MY, 4 * MX)


def body(field, spectral_filter, depth_weight, point_weight, bias_vector):
    gz, gy = lax.axis_size("gz"), lax.axis_size("gy")
    y_local = field.shape[2]
    field = field.reshape(CH, y_local, NX)
    y_total = gy * y_local
    forward_scale = 1.0 / math.sqrt(float(NX) * y_total * gz)
    inverse_scale = 1.0 / math.sqrt(2.0 * MX * MY * MZ)

    def ring(axis, count, by):
        return [(i, (i + by) % count) for i in range(count)]

    def to_neighbours(down, up):
        return (
            lax.ppermute(down, "gz", ring("gz", gz, 1)),
            lax.ppermute(up, "gz", ring("gz", gz, -1)),
        )

    def after(value, *others):
        return lax.optimization_barrier((value, *others))[0]

    last = y_local // 8 - 1
    cut = 1 + last // 2
    first_tiles, second_tiles = tuple(range(1, cut)), tuple(range(cut, min(cut + 2, last)))
    third_tiles = (0, *range(second_tiles[-1] + 1, last + 1))
    packed, edges = pack_call(field, first_tiles)
    first_low, first_high = to_neighbours(packed, packed)
    if gy == 2:
        halo = lax.ppermute(edges, "gy", ring("gy", gy, 1))
    else:
        halo = jnp.stack(
            [
                lax.ppermute(edges[0], "gy", ring("gy", gy, 1)),
                lax.ppermute(edges[1], "gy", ring("gy", gy, -1)),
            ]
        )
    j_own, n_own = spectral_filter.shape[2], spectral_filter.shape[3]
    whole_tiles = j_own == 8 and n_own == 2 * MX
    coarse = after(forward_call(after(field, packed), gy, whole_tiles), halo)
    segments, groups = ((0,), tuple(range(cut, last + 1))), (second_tiles, third_tiles)
    down, second, up, outer_down, own, outer_up = own_call(
        after(field, coarse), halo, depth_weight, point_weight, segments, groups
    )
    if whole_tiles:
        both = ("gz", "gy")
        got = lax.all_to_all(coarse, both, split_axis=0, concat_axis=0, tiled=True)
        down, up = lax.optimization_barrier((down, up, first_low))[:2]
        pair = to_neighbours(down, up)
        gains = after(spectral_filter, first_low, first_high, second)
        mark = filter_call(got, gains, gz, gy, forward_scale)
        back = lax.all_to_all(mark, "gz", split_axis=0, concat_axis=0, tiled=True)
    else:
        pair = to_neighbours(down, up)
        mark = general_filter(coarse, spectral_filter, gz, gy, forward_scale)
        modes = [mark[:, part].reshape(-1, 4 * MX) for part in (slice(0, MY // 2), slice(MY // 2, MY))]
    outer_pair = to_neighbours(after(outer_down, mark), after(outer_up, mark))
    packed, *pair = lax.optimization_barrier((packed, *pair))
    mixed = middle_call(depth_weight, point_weight, first_low, packed, first_high)
    if whole_tiles:
        modes = (back, lax.ppermute(after(back, mixed), "gy", ring("gy", gy, 1)))
    result, base = inverse_call(
        modes, whole_tiles, bias_vector, own, mixed, second, pair, 8, y_local, gy, inverse_scale
    )
    result = finish_call(result, base, *outer_pair, 1)
    return result.reshape(CH, 1, y_local, NX)


def solution(mesh):
    in_specs = (P(None, "gz", "gy", None), P(None, None, "gy", "gz"), P(), P(), P())
    out_specs = P(None, "gz", "gy", None)
    return jax.shard_map(body, mesh=mesh, in_specs=in_specs, out_specs=out_specs, check_vma=False)
```

```python
import functools
import math

import jax
import jax.numpy as jnp
import ml_dtypes
import numpy as np
from jax import lax
from jax.experimental import pallas as pl
from jax.experimental.pallas import tpu as pltpu
from jax.sharding import PartitionSpec as P

NX = 256
MX = 32
MY = 16
MZ = 16
CH = 32
VMEM_BYTES = 20 * 1024 * 1024
ALL_VMEM_BYTES = 64000 * 1024
BF = jnp.bfloat16
F32 = jnp.float32


def kept(count, total):
    series = np.arange(count)
    return np.where(series < count // 2, series, total - count + series)


def trig(freqs, places, total):
    angle = 2.0 * np.pi * ((freqs[:, None] * places[None, :]) % total) / total
    return np.cos(angle), np.sin(angle)


def halves(table):
    table = np.asarray(table, np.float64)
    top = table.astype(np.float32).astype(ml_dtypes.bfloat16)
    rest = (table - top.astype(np.float64)).astype(np.float32).astype(ml_dtypes.bfloat16)
    return jnp.asarray(top), jnp.asarray(rest)


def y_table(y_local, gy, inverse):
    out = []
    for g in range(gy):
        places = g * y_local + np.arange(y_local)
        out.append(np.concatenate(trig(kept(MY, y_local * gy), places, y_local * gy), axis=0))
    return np.stack([t.T for t in out] if inverse else out)


def x_table(inverse, scale=1.0):
    c, s = trig(np.arange(MX), np.arange(NX), NX)
    w = np.where(np.arange(MX) == 0, 1.0, 2.0)[:, None] if inverse else 1.0
    out = np.zeros((2, 2, 2, MX, NX))
    for p in range(2):
        out[p, p, 0] = w * c * scale
        out[p, p, 1] = -w * s * scale
    out = out.reshape(2, 4 * MX, NX)
    return out if inverse else out.transpose(0, 2, 1)


def z_tables(gz, gy, rows, scale):
    c, s = trig(kept(MZ, gz), np.arange(gz), gz)
    eye = np.eye(rows)
    both = np.stack([c, s])
    fwd = np.einsum("tqz,g,jk->tqjzgk", both, np.ones(gy), eye) * scale
    inv = np.einsum("tqz,jk->tzjqk", both, eye)
    return fwd.reshape(2 * MZ * rows, gz * gy * rows), inv.reshape(2 * gz * rows, MZ * rows)


def parts(value):
    top = value.astype(BF)
    return top, (value - top.astype(F32)).astype(BF)


def dot(a, b):
    return jnp.dot(a, b, preferred_element_type=F32)


def dot3(a, b):
    rows = a[0].shape[0]
    both = dot(jnp.concatenate([a[0], a[1]], axis=0), b[0])
    return both[:rows] + (both[rows:] + dot(a[0], b[1]))


def swap_parts(value):
    lane = lax.broadcasted_iota(jnp.int32, value.shape, 1)
    is_real = (lane // MX) % 2 == 0
    width = value.shape[1]
    return jnp.where(is_real, pltpu.roll(value, width - MX, 1), pltpu.roll(value, MX, 1)), is_real


def forward_kernel(field, x_top, x_rest, y_top, y_rest, out, taken, x_both, y_both, sem):
    gy = lax.axis_index("gy")
    few = [
        pltpu.make_async_copy(src, dst, sem.at[4 + i])
        for i, (src, dst) in enumerate(
            ((x_top, x_both.at[0]), (x_rest, x_both.at[1]), (y_top.at[gy], y_both.at[0]), (y_rest.at[gy], y_both.at[1]))
        )
    ]
    copies = [pltpu.make_async_copy(field.at[:, q], taken.at[q], sem.at[q]) for q in range(4)]
    for copy in few + copies:
        copy.start()
    for copy in few:
        copy.wait()
    groups, rows = taken.shape[1:3]
    halves_of = []
    for q in range(4):
        copies[q].wait()
        part = dot3(parts(taken[q].reshape(groups * rows, NX)), (x_both[0, q % 2], x_both[1, q % 2]))
        if q % 2:
            halves_of[-1] = halves_of[-1] + part
        else:
            halves_of.append(part)
    total = jnp.concatenate(halves_of, axis=1)
    for g in range(groups):
        both = dot3((y_both[0], y_both[1]), parts(total[g * rows : (g + 1) * rows]))
        crossed, is_real = swap_parts(both[MY:])
        modes = both[:MY] + jnp.where(is_real, crossed, -crossed)
        out[pl.ds(2 * g * MY, MY), :] = modes[:, : 4 * MX]
        out[pl.ds((2 * g + 1) * MY, MY), :] = modes[:, 4 * MX :]


def filter_kernel(arrived, gains, f_top, f_rest, i_top, i_rest, out):
    real, imag = (gains[r].reshape(-1, 2 * MX) for r in range(2))
    first, second = slice(0, MX), slice(MX, 2 * MX)
    same = jnp.concatenate([real[:, first], real[:, first], real[:, second], real[:, second]], axis=1)
    cross = jnp.concatenate([-imag[:, first], imag[:, first], -imag[:, second], imag[:, second]], axis=1)
    half = f_top.shape[0] // 2
    turned = dot3((f_top[...], f_rest[...]), parts(arrived[...]))
    crossed, is_real = swap_parts(turned[half:])
    modes = turned[:half] + jnp.where(is_real, crossed, -crossed)
    crossed, _ = swap_parts(modes)
    filtered = modes * same + crossed * cross
    half = i_top.shape[0] // 2
    back = dot3((i_top[...], i_rest[...]), parts(filtered))
    crossed, is_real = swap_parts(back[half:])
    out[...] = back[:half] + jnp.where(is_real, -crossed, crossed)


def fetch_tiles(field, taken, sems, wanted):
    pending = {}
    for k, t in enumerate(wanted):
        pending[t] = [
            pltpu.make_async_copy(
                field.at[:, pl.ds(8 * t, 8), pl.ds(128 * h, 128)], taken.at[k, h], sems.at[k, h]
            )
            for h in range(2)
        ]
        for copy in pending[t]:
            copy.start()

    def row(t, r):
        for copy in pending.pop(t, ()):
            copy.wait()
        k = wanted.index(t)
        return jnp.concatenate(
            [taken.at[k, h].reshape(CH * 8, 128)[pl.ds(r, CH, stride=8), :] for h in range(2)], axis=1
        )

    return row


def spread_gains(weights, gains, offsets):
    for k in [9 * a + j for a in offsets for j in range(9)]:
        gains[k] = jnp.broadcast_to(weights[:, k : k + 1], (CH, 128))


def mixing(points):
    down = (
        lax.broadcasted_iota(jnp.int32, (8 * CH, CH), 0) // 8
        == lax.broadcasted_iota(jnp.int32, (8 * CH, CH), 1)
    ).astype(BF)
    across = (
        lax.broadcasted_iota(jnp.int32, (CH, 8 * CH), 1) % CH
        == lax.broadcasted_iota(jnp.int32, (CH, 8 * CH), 0)
    ).astype(BF)
    same = (
        lax.broadcasted_iota(jnp.int32, (8 * CH, 8 * CH), 0) % 8
        == lax.broadcasted_iota(jnp.int32, (8 * CH, 8 * CH), 1) // CH
    )
    return tuple(
        jnp.where(same, dot(dot(down, part).astype(BF), across), 0.0).astype(BF)
        for part in parts(points)
    )


def tap_sums(load, uses, gains, depth, runs):
    def some(i, _):
        chans = pl.ds(pl.multiple_of(i * 8, 8), 8)
        wanted = sorted({a for use in uses for a, _ in use})
        gain = {k: gains[k, chans, :] for a in wanted for k in range(9 * a, 9 * a + 9)}
        for first, to, rows in runs:
            sums = {}
            for r in range(rows + 2):
                for s, use in enumerate(uses):
                    value = load(s, first + r, chans)
                    turned = (pltpu.roll(value, 1, 1), value, pltpu.roll(value, NX - 1, 1))
                    for b in range(3):
                        o = r - b
                        if o < 0 or o >= rows:
                            continue
                        for a, k in use:
                            for e in range(3):
                                for h in range(2):
                                    term = gain[a * 9 + b * 3 + e] * turned[e][:, 128 * h : 128 * h + 128]
                                    place = (o, k, h)
                                    sums[place] = sums[place] + term if place in sums else term
                if r >= 2:
                    for k in sorted({k for use in uses for _, k in use}):
                        for h in range(2):
                            depth[k, to + r - 2, chans, pl.ds(128 * h, 128)] = sums.pop((r - 2, k, h))
        return 0

    lax.fori_loop(0, CH // 8, some, 0)


def mix_tile(mix, depth, k, t):
    tile = depth[k, pl.ds(8 * t, 8)].reshape(8 * CH, NX)
    return dot3(mix, parts(tile)).reshape(CH, 8, NX)


def pack_kernel(tiles, field, packed, edges, taken, sem_in):
    last = field.shape[1] // 8 - 1
    before, after = tiles[0] - 1, tiles[-1] + 1
    wanted = [before, *tiles, after] + [t for t in (0, last) if t not in (before, after)]
    row = fetch_tiles(field, taken, sem_in, wanted)
    for i, place in enumerate([(before, 7), *[(t, r) for t in tiles for r in range(8)], (after, 0)]):
        packed[i] = row(*place)
    edges[0] = row(last, 7)
    edges[1] = row(0, 0)


def own_kernel(segments, groups, weight, point, field, halo, *refs):
    last = field.shape[1] // 8 - 1
    count = 3 * len(groups)
    outs, (taken, halo_rows, weights, points, sent, lined, depth, gains, sem_in, sem_out, sem_few) = (
        refs[:count],
        refs[count:],
    )
    few = [
        pltpu.make_async_copy(src, dst, sem_few.at[i])
        for i, (src, dst) in enumerate(((weight, weights), (point, points), (halo, halo_rows)))
    ]
    for copy in few:
        copy.start()
    wanted = sorted({t for tiles in segments for t in (tiles[0] - 1, *tiles, tiles[-1] + 1) if 0 <= t <= last})
    row = fetch_tiles(field, taken, sem_in, wanted)
    for copy in few:
        copy.wait()
    spread_gains(weights, gains, range(3))
    mix = mixing(points[...])
    runs, at, done, order = [], 0, 0, []
    for tiles in segments:
        places = [(tiles[0] - 1, 7), *[(t, r) for t in tiles for r in range(8)], (tiles[-1] + 1, 0)]
        for i, (t, r) in enumerate(places):
            lined[at + i] = halo_rows[0] if t < 0 else halo_rows[1] if t > last else row(t, r)
        runs.append((at, done, 8 * len(tiles)))
        at, done = at + len(places), done + 8 * len(tiles)
        order += tiles
    tap_sums(lambda s, r, c: lined[r, c, :], [[(a, a) for a in range(3)]], gains, depth, runs)
    copies = []
    for g, tiles in enumerate(groups):
        for i, tile in enumerate(tiles):
            t = order.index(tile)
            for k in range(3):
                sent[k, t] = mix_tile(mix, depth, k, t)
                to = outs[3 * g + k].at[:, pl.ds(8 * i, 8), :]
                copies.append(pltpu.make_async_copy(sent.at[k, t], to, sem_out.at[k, t]))
                copies[-1].start()
    for copy in copies:
        copy.wait()


def middle_kernel(weight, point, low, own, high, out, taken, weights, points, sent, depth, gains, sem_in, sem_out):
    copies = [
        pltpu.make_async_copy(src, dst, sem_in.at[i])
        for i, (src, dst) in enumerate(
            ((weight, weights), (point, points), (low, taken.at[0]), (own, taken.at[1]), (high, taken.at[2]))
        )
    ]
    for copy in copies:
        copy.start()
    for copy in copies[:2]:
        copy.wait()
    spread_gains(weights, gains, range(3))
    mix = mixing(points[...])
    for copy in copies[2:]:
        copy.wait()
    rows = out.shape[1]
    tap_sums(lambda s, r, c: taken[s, r, c, :], [[(a, 0)] for a in range(3)], gains, depth, [(0, 0, rows)])
    copies = []
    for t in range(rows // 8):
        sent[t] = mix_tile(mix, depth, 0, t)
        copies.append(pltpu.make_async_copy(sent.at[t], out.at[:, pl.ds(8 * t, 8), :], sem_out.at[t]))
        copies[-1].start()
    for copy in copies:
        copy.wait()


ERFC = (
    0.17087277, -0.82215223, 1.48851587, -1.13520398, 0.27886807,
    -0.18628806, 0.09678418, 0.37409196, 1.00002368, -1.26551223 - math.log(2.0),
)


def gelu(value):
    size = jnp.abs(value) * math.sqrt(0.5)
    below = 1.0 + 0.5 * size
    t = pl.reciprocal(below, approx=True)
    t = t * (2.0 - below * t)
    series = ERFC[0] * t + ERFC[1]
    for factor in ERFC[2:]:
        series = series * t + factor
    tail = t * jnp.exp(series - size * size)
    return value * jnp.where(value < 0.0, tail, 1.0 - tail)


def inverse_kernel(upper, halved, first_modes, second_modes, bias, x_top, x_rest, y_top, y_rest, own, middle, second, low, high, out, base, columns):
    q = pl.program_id(0)
    groups, _, y_local, _ = out.shape

    @pl.when(q == 0)
    def _():
        gy = lax.axis_index("gy")
        for g in range(groups):
            pairs = []
            for pair in (2 * g, 2 * g + 1):
                some = pl.ds(pair * (MY // 2), MY // 2)
                one, two = first_modes[some, :], second_modes[some, :]
                if halved:
                    one, two = jnp.where(gy == 0, one, two), jnp.where(gy == 0, two, one)
                pairs.append(jnp.concatenate([one, two], axis=0))
            own_modes = jnp.concatenate(pairs, axis=1)
            crossed, is_real = swap_parts(own_modes)
            stack = jnp.concatenate([own_modes, jnp.where(is_real, -crossed, crossed)], axis=0)
            pair = parts(dot3((y_top[gy], y_rest[gy]), parts(stack)))
            for h in range(2):
                for k in range(2):
                    columns[h, k, pl.ds(g * y_local, y_local), :] = pair[k][:, 128 * h : 128 * h + 128]

    h, p = q // 2, q % 2
    rows = dot3((columns[h, 0], columns[h, 1]), (x_top[p], x_rest[p]))
    turn = upper + middle.shape[2]
    stop = turn + second.shape[2]
    for g in range(groups):
        plane = rows[g * y_local : (g + 1) * y_local] + bias[4 * g + q]
        base[g, 0, :upper] = plane[:upper] + own[g, 0, :upper]
        out[g, 0, upper:turn] = gelu(plane[upper:turn] + middle[g, 0])
        out[g, 0, turn:stop] = gelu(plane[turn:stop] + (second[g, 0] + (low[g, 0] + high[g, 0])))
        base[g, 0, upper:] = plane[stop:] + own[g, 0, upper:]


def finish_kernel(upper, _, base, low, high, out, sent, sem):
    tiles = base.shape[1] // 8
    gap = out.shape[1] // 8 - tiles
    copies = []
    for t in range(tiles):
        rows = pl.ds(8 * t, 8)
        sent[t] = gelu(base[:, rows, :] + (low[:, rows, :] + high[:, rows, :]))
        to = t if t < upper else t + gap
        copies.append(pltpu.make_async_copy(sent.at[t], out.at[:, pl.ds(8 * to, 8), :], sem.at[t]))
        copies[-1].start()
    for copy in copies:
        copy.wait()


def in_hbm(*arrays):
    return [pltpu.with_memory_space_constraint(a, pltpu.HBM) for a in arrays]


def params(limit=VMEM_BYTES):
    return pltpu.CompilerParams(vmem_limit_bytes=limit)


def cost(flops, moved):
    return pl.CostEstimate(flops=flops, bytes_accessed=moved, transcendentals=0)


def whole_block(table):
    return pl.BlockSpec(table.shape, lambda i: (0,) * table.ndim)


def by_four(array):
    return array.reshape(CH // 4, 4, *array.shape[1:])


def forward_call(field, gy, pinned):
    y_local = field.shape[1]
    tables = [*halves(x_table(False)), *halves(y_table(y_local, gy, False))]
    hbm = pl.BlockSpec(memory_space=pltpu.HBM)
    return pl.pallas_call(
        forward_kernel,
        out_shape=(pltpu.HBM if pinned else jax.ShapeDtypeStruct)((CH // 2 * MY, 4 * MX), F32),
        in_specs=[hbm] * 5,
        scratch_shapes=[
            pltpu.VMEM((4, CH // 4, y_local, NX), F32),
            pltpu.VMEM((2, 2, NX, 4 * MX), BF),
            pltpu.VMEM((2, 2 * MY, y_local), BF),
            pltpu.SemaphoreType.DMA((8,)),
        ],
        compiler_params=params(ALL_VMEM_BYTES),
        cost_estimate=cost(10**8, 2**18),
        name="forward_modes",
    )(*in_hbm(by_four(field), *tables))


def filter_call(arrived, gains, gz, gy, scale):
    fwd, inv = z_tables(gz, gy, gains.shape[2], scale)
    fwd, inv = halves(fwd), halves(inv)
    return pl.pallas_call(
        filter_kernel,
        out_shape=pltpu.HBM((arrived.shape[0] // gy, arrived.shape[1]), F32),
        compiler_params=params(),
        cost_estimate=cost(4 * 10**10, 2**18),
        name="filter_modes",
    )(arrived, *in_hbm(gains, *fwd, *inv))


def inverse_call(modes, halved, bias, own, middle, second, pair, upper, y_local, gy, scale):
    tables = [*halves(x_table(True, scale)), *halves(y_table(y_local, gy, True))]
    some = lambda rows: pl.BlockSpec((CH // 4, 1, rows, NX), lambda i: (0, i, 0, 0))
    planes = [*in_hbm(*map(by_four, (own, middle, second))), *map(by_four, pair)]
    rim = own.shape[1]
    result, base = pl.pallas_call(
        functools.partial(inverse_kernel, upper, halved),
        out_shape=[
            jax.ShapeDtypeStruct((CH // 4, 4, y_local, NX), F32),
            jax.ShapeDtypeStruct((CH // 4, 4, rim, NX), F32),
        ],
        grid=(4,),
        in_specs=[
            *[whole_block(m) for m in modes],
            pl.BlockSpec(memory_space=pltpu.SMEM),
            *[whole_block(t) for t in tables],
            *[some(p.shape[2]) for p in planes],
        ],
        out_specs=[some(y_local), some(rim)],
        scratch_shapes=[pltpu.VMEM((2, 2, CH // 4 * y_local, 128), BF)],
        compiler_params=params(),
        cost_estimate=cost(10**8, 2**18),
        name="inverse_modes",
    )(*modes, *in_hbm(bias, *tables), *planes)
    return result.reshape(CH, y_local, NX), base.reshape(CH, rim, NX)


def finish_call(result, base, low, high, upper):
    tiles = base.shape[1] // 8
    anywhere = pl.BlockSpec(memory_space=pl.ANY)
    vmem = pl.BlockSpec(memory_space=pltpu.VMEM)
    return pl.pallas_call(
        functools.partial(finish_kernel, upper),
        out_shape=jax.ShapeDtypeStruct(result.shape, F32),
        in_specs=[anywhere] + [vmem] * 3,
        out_specs=anywhere,
        scratch_shapes=[
            pltpu.VMEM((tiles, CH, 8, NX), F32),
            pltpu.SemaphoreType.DMA((tiles,)),
        ],
        input_output_aliases={0: 0},
        compiler_params=params(),
        cost_estimate=cost(10**8, 2**18),
        name="finished_rows",
    )(result, base, low, high)


def pack_call(field, tiles):
    count = 8 * len(tiles) + 2
    fetched = len(tiles) + 4
    vmem = pl.BlockSpec(memory_space=pltpu.VMEM)
    return pl.pallas_call(
        functools.partial(pack_kernel, tiles),
        out_shape=[jax.ShapeDtypeStruct((count, CH, NX), F32), jax.ShapeDtypeStruct((2, CH, NX), F32)],
        in_specs=[pl.BlockSpec(memory_space=pltpu.HBM)],
        out_specs=[vmem] * 2,
        scratch_shapes=[
            pltpu.VMEM((fetched, 2, CH, 8, 128), F32),
            pltpu.SemaphoreType.DMA((fetched, 2)),
        ],
        compiler_params=params(),
        cost_estimate=cost(10**8, 2**18),
        name="packed_rows",
    )(*in_hbm(field))


def own_call(field, halo, weight, point, segments, groups):
    tiles = sum(map(len, segments))
    rows, fetched = 8 * tiles, tiles + 2 * len(segments)
    hbm = pl.BlockSpec(memory_space=pltpu.HBM)
    shapes = [pltpu.HBM((CH, 8 * len(group), NX), F32) for group in groups for _ in range(3)]
    return pl.pallas_call(
        functools.partial(own_kernel, segments, groups),
        out_shape=shapes,
        in_specs=[hbm] * 3 + [pl.BlockSpec(memory_space=pl.ANY)],
        out_specs=[hbm] * len(shapes),
        scratch_shapes=[
            pltpu.VMEM((fetched, 2, CH, 8, 128), F32),
            pltpu.VMEM((2, CH, NX), F32),
            pltpu.VMEM((CH, 27), F32),
            pltpu.VMEM((CH, CH), F32),
            pltpu.VMEM((3, tiles, CH, 8, NX), F32),
            pltpu.VMEM((rows + 2 * len(segments), CH, NX), F32),
            pltpu.VMEM((3, rows, CH, NX), F32),
            pltpu.VMEM((27, CH, 128), F32),
            pltpu.SemaphoreType.DMA((fetched, 2)),
            pltpu.SemaphoreType.DMA((3, tiles)),
            pltpu.SemaphoreType.DMA((3,)),
        ],
        compiler_params=params(),
        cost_estimate=cost(10**8, 2**18),
        name="own_sums",
    )(*in_hbm(weight, point, field), halo)


def middle_call(weight, point, low, own, high):
    rows = own.shape[0] - 2
    hbm = pl.BlockSpec(memory_space=pltpu.HBM)
    return pl.pallas_call(
        middle_kernel,
        out_shape=pltpu.HBM((CH, rows, NX), F32),
        in_specs=[hbm] * 3 + [pl.BlockSpec(memory_space=pl.ANY), hbm],
        out_specs=hbm,
        scratch_shapes=[
            pltpu.VMEM((3, rows + 2, CH, NX), F32),
            pltpu.VMEM((CH, 27), F32),
            pltpu.VMEM((CH, CH), F32),
            pltpu.VMEM((rows // 8, CH, 8, NX), F32),
            pltpu.VMEM((1, rows, CH, NX), F32),
            pltpu.VMEM((27, CH, 128), F32),
            pltpu.SemaphoreType.DMA((5,)),
            pltpu.SemaphoreType.DMA((rows // 8,)),
        ],
        compiler_params=params(),
        cost_estimate=cost(4 * 10**10, 2**18),
        name="middle_sums",
    )(*in_hbm(weight, point, low), own, *in_hbm(high))


def general_filter(coarse, gains, gz, gy, scale):
    j_own, n_own = gains.shape[2], gains.shape[3]
    both = ("gz", "gy")
    flat = coarse.reshape(CH // 2, MY, 2, 2, MX).transpose(3, 1, 0, 2, 4).reshape(2, MY, CH * MX)
    sent = flat.reshape(2, gy, j_own, gz, n_own).transpose(3, 1, 0, 2, 4).reshape(gz * gy, -1)
    got = lax.all_to_all(sent, both, split_axis=0, concat_axis=0, tiled=True)
    got = got.reshape(gz, gy, 2, j_own, n_own)
    c, s = (jnp.asarray(t, F32) for t in trig(kept(MZ, gz), np.arange(gz), gz))
    mul = functools.partial(jnp.einsum, precision=lax.Precision.HIGHEST)
    whole = got.sum(axis=1) * scale
    real = mul("zjn,qz->qjn", whole[:, 0], c) + mul("zjn,qz->qjn", whole[:, 1], s)
    imag = mul("zjn,qz->qjn", whole[:, 1], c) - mul("zjn,qz->qjn", whole[:, 0], s)
    real, imag = real * gains[0] - imag * gains[1], real * gains[1] + imag * gains[0]
    out = jnp.stack(
        [
            mul("qjn,qz->zjn", real, c) - mul("qjn,qz->zjn", imag, s),
            mul("qjn,qz->zjn", real, s) + mul("qjn,qz->zjn", imag, c),
        ],
        axis=1,
    )
    out = jnp.broadcast_to(out[:, None], (gz, gy, 2, j_own, n_own)).reshape(gz * gy, -1)
    back = lax.all_to_all(out, both, split_axis=0, concat_axis=0, tiled=True)
    back = back.reshape(gz, gy, 2, j_own, n_own).transpose(2, 1, 3, 0, 4)
    back = back.reshape(2, MY, CH // 2, 2, MX)
    return back.transpose(2, 1, 3, 0, 4).reshape(CH // 2, MY, 4 * MX)


def body(field, spectral_filter, depth_weight, point_weight, bias_vector):
    gz, gy = lax.axis_size("gz"), lax.axis_size("gy")
    y_local = field.shape[2]
    field = field.reshape(CH, y_local, NX)
    y_total = gy * y_local
    forward_scale = 1.0 / math.sqrt(float(NX) * y_total * gz)
    inverse_scale = 1.0 / math.sqrt(2.0 * MX * MY * MZ)

    def ring(axis, count, by):
        return [(i, (i + by) % count) for i in range(count)]

    def to_neighbours(down, up):
        return (
            lax.ppermute(down, "gz", ring("gz", gz, 1)),
            lax.ppermute(up, "gz", ring("gz", gz, -1)),
        )

    def after(value, *others):
        return lax.optimization_barrier((value, *others))[0]

    last = y_local // 8 - 1
    cut = 1 + last // 2
    first_tiles, second_tiles = tuple(range(1, cut)), tuple(range(cut, min(cut + 2, last)))
    third_tiles = (0, *range(second_tiles[-1] + 1, last + 1))
    packed, edges = pack_call(field, first_tiles)
    first_low, first_high = to_neighbours(packed, packed)
    if gy == 2:
        halo = lax.ppermute(edges, "gy", ring("gy", gy, 1))
    else:
        halo = jnp.stack(
            [
                lax.ppermute(edges[0], "gy", ring("gy", gy, 1)),
                lax.ppermute(edges[1], "gy", ring("gy", gy, -1)),
            ]
        )
    j_own, n_own = spectral_filter.shape[2], spectral_filter.shape[3]
    whole_tiles = j_own == 8 and n_own == 2 * MX
    coarse = after(forward_call(after(field, packed), gy, whole_tiles), halo)
    segments, groups = ((0,), tuple(range(cut, last + 1))), (second_tiles, third_tiles)
    down, second, up, outer_down, own, outer_up = own_call(
        after(field, coarse), halo, depth_weight, point_weight, segments, groups
    )
    if whole_tiles:
        both = ("gz", "gy")
        got = lax.all_to_all(coarse, both, split_axis=0, concat_axis=0, tiled=True)
        down, up = lax.optimization_barrier((down, up, first_low))[:2]
        pair = to_neighbours(down, up)
        gains = after(spectral_filter, first_low, first_high, second)
        mark = filter_call(got, gains, gz, gy, forward_scale)
        back = lax.all_to_all(mark, "gz", split_axis=0, concat_axis=0, tiled=True)
    else:
        pair = to_neighbours(down, up)
        mark = general_filter(coarse, spectral_filter, gz, gy, forward_scale)
        modes = [mark[:, part].reshape(-1, 4 * MX) for part in (slice(0, MY // 2), slice(MY // 2, MY))]
    outer_pair = to_neighbours(after(outer_down, mark), after(outer_up, mark))
    packed, *pair = lax.optimization_barrier((packed, *pair))
    mixed = middle_call(depth_weight, point_weight, first_low, packed, first_high)
    if whole_tiles:
        modes = (back, lax.ppermute(after(back, mixed), "gy", ring("gy", gy, 1)))
    result, base = inverse_call(
        modes, whole_tiles, bias_vector, own, mixed, second, pair, 8, y_local, gy, inverse_scale
    )
    result = finish_call(result, base, *outer_pair, 1)
    return result.reshape(CH, 1, y_local, NX)


def solution(mesh):
    in_specs = (P(None, "gz", "gy", None), P(None, None, "gy", "gz"), P(), P(), P())
    out_specs = P(None, "gz", "gy", None)
    return jax.shard_map(body, mesh=mesh, in_specs=in_specs, out_specs=out_specs, check_vma=False)
```

```python
import functools
import math

import jax
import jax.numpy as jnp
import ml_dtypes
import numpy as np
from jax import lax
from jax.experimental import pallas as pl
from jax.experimental.pallas import tpu as pltpu
from jax.sharding import PartitionSpec as P

NX = 256
MX = 32
MY = 16
MZ = 16
CH = 32
VMEM_BYTES = 20 * 1024 * 1024
ALL_VMEM_BYTES = 64000 * 1024
BF = jnp.bfloat16
F32 = jnp.float32


def kept(count, total):
    series = np.arange(count)
    return np.where(series < count // 2, series, total - count + series)


def trig(freqs, places, total):
    angle = 2.0 * np.pi * ((freqs[:, None] * places[None, :]) % total) / total
    return np.cos(angle), np.sin(angle)


def halves(table):
    table = np.asarray(table, np.float64)
    top = table.astype(np.float32).astype(ml_dtypes.bfloat16)
    rest = (table - top.astype(np.float64)).astype(np.float32).astype(ml_dtypes.bfloat16)
    return jnp.asarray(top), jnp.asarray(rest)


def y_table(y_local, gy, inverse):
    out = []
    for g in range(gy):
        places = g * y_local + np.arange(y_local)
        out.append(np.concatenate(trig(kept(MY, y_local * gy), places, y_local * gy), axis=0))
    return np.stack([t.T for t in out] if inverse else out)


def x_table(inverse, scale=1.0):
    c, s = trig(np.arange(MX), np.arange(NX), NX)
    w = np.where(np.arange(MX) == 0, 1.0, 2.0)[:, None] if inverse else 1.0
    out = np.zeros((2, 2, 2, MX, NX))
    for p in range(2):
        out[p, p, 0] = w * c * scale
        out[p, p, 1] = -w * s * scale
    out = out.reshape(2, 4 * MX, NX)
    return out if inverse else out.transpose(0, 2, 1)


def z_tables(gz, gy, rows, scale):
    c, s = trig(kept(MZ, gz), np.arange(gz), gz)
    eye = np.eye(rows)
    both = np.stack([c, s])
    fwd = np.einsum("tqz,g,jk->tqjzgk", both, np.ones(gy), eye) * scale
    inv = np.einsum("tqz,jk->tzjqk", both, eye)
    return fwd.reshape(2 * MZ * rows, gz * gy * rows), inv.reshape(2 * gz * rows, MZ * rows)


def parts(value):
    top = value.astype(BF)
    return top, (value - top.astype(F32)).astype(BF)


def dot(a, b):
    return jnp.dot(a, b, preferred_element_type=F32)


def dot3(a, b):
    rows = a[0].shape[0]
    both = dot(jnp.concatenate([a[0], a[1]], axis=0), b[0])
    return both[:rows] + (both[rows:] + dot(a[0], b[1]))


def swap_parts(value):
    lane = lax.broadcasted_iota(jnp.int32, value.shape, 1)
    is_real = (lane // MX) % 2 == 0
    width = value.shape[1]
    return jnp.where(is_real, pltpu.roll(value, width - MX, 1), pltpu.roll(value, MX, 1)), is_real


def forward_kernel(field, x_top, x_rest, y_top, y_rest, out, taken, x_both, y_both, sem):
    gy = lax.axis_index("gy")
    few = [
        pltpu.make_async_copy(src, dst, sem.at[4 + i])
        for i, (src, dst) in enumerate(
            ((x_top, x_both.at[0]), (x_rest, x_both.at[1]), (y_top.at[gy], y_both.at[0]), (y_rest.at[gy], y_both.at[1]))
        )
    ]
    copies = [pltpu.make_async_copy(field.at[:, q], taken.at[q], sem.at[q]) for q in range(4)]
    for copy in few + copies:
        copy.start()
    for copy in few:
        copy.wait()
    groups, rows = taken.shape[1:3]
    halves_of = []
    for q in range(4):
        copies[q].wait()
        part = dot3(parts(taken[q].reshape(groups * rows, NX)), (x_both[0, q % 2], x_both[1, q % 2]))
        if q % 2:
            halves_of[-1] = halves_of[-1] + part
        else:
            halves_of.append(part)
    total = jnp.concatenate(halves_of, axis=1)
    for g in range(groups):
        both = dot3((y_both[0], y_both[1]), parts(total[g * rows : (g + 1) * rows]))
        crossed, is_real = swap_parts(both[MY:])
        modes = both[:MY] + jnp.where(is_real, crossed, -crossed)
        out[pl.ds(2 * g * MY, MY), :] = modes[:, : 4 * MX]
        out[pl.ds((2 * g + 1) * MY, MY), :] = modes[:, 4 * MX :]


def filter_kernel(arrived, gains, f_top, f_rest, i_top, i_rest, out):
    real, imag = (gains[r].reshape(-1, 2 * MX) for r in range(2))
    first, second = slice(0, MX), slice(MX, 2 * MX)
    same = jnp.concatenate([real[:, first], real[:, first], real[:, second], real[:, second]], axis=1)
    cross = jnp.concatenate([-imag[:, first], imag[:, first], -imag[:, second], imag[:, second]], axis=1)
    half = f_top.shape[0] // 2
    turned = dot3((f_top[...], f_rest[...]), parts(arrived[...]))
    crossed, is_real = swap_parts(turned[half:])
    modes = turned[:half] + jnp.where(is_real, crossed, -crossed)
    crossed, _ = swap_parts(modes)
    filtered = modes * same + crossed * cross
    half = i_top.shape[0] // 2
    back = dot3((i_top[...], i_rest[...]), parts(filtered))
    crossed, is_real = swap_parts(back[half:])
    out[...] = back[:half] + jnp.where(is_real, -crossed, crossed)


def fetch_tiles(field, taken, sems, wanted):
    pending = {}
    for k, t in enumerate(wanted):
        pending[t] = [
            pltpu.make_async_copy(
                field.at[:, pl.ds(8 * t, 8), pl.ds(128 * h, 128)], taken.at[k, h], sems.at[k, h]
            )
            for h in range(2)
        ]
        for copy in pending[t]:
            copy.start()

    def row(t, r):
        for copy in pending.pop(t, ()):
            copy.wait()
        k = wanted.index(t)
        return jnp.concatenate(
            [taken.at[k, h].reshape(CH * 8, 128)[pl.ds(r, CH, stride=8), :] for h in range(2)], axis=1
        )

    return row


def spread_gains(weights, gains, offsets):
    for k in [9 * a + j for a in offsets for j in range(9)]:
        gains[k] = jnp.broadcast_to(weights[:, k : k + 1], (CH, 128))


def mixing(points):
    down = (
        lax.broadcasted_iota(jnp.int32, (8 * CH, CH), 0) // 8
        == lax.broadcasted_iota(jnp.int32, (8 * CH, CH), 1)
    ).astype(BF)
    across = (
        lax.broadcasted_iota(jnp.int32, (CH, 8 * CH), 1) % CH
        == lax.broadcasted_iota(jnp.int32, (CH, 8 * CH), 0)
    ).astype(BF)
    same = (
        lax.broadcasted_iota(jnp.int32, (8 * CH, 8 * CH), 0) % 8
        == lax.broadcasted_iota(jnp.int32, (8 * CH, 8 * CH), 1) // CH
    )
    return tuple(
        jnp.where(same, dot(dot(down, part).astype(BF), across), 0.0).astype(BF)
        for part in parts(points)
    )


def tap_sums(load, uses, gains, depth, runs):
    def some(i, _):
        chans = pl.ds(pl.multiple_of(i * 8, 8), 8)
        wanted = sorted({a for use in uses for a, _ in use})
        gain = {k: gains[k, chans, :] for a in wanted for k in range(9 * a, 9 * a + 9)}
        for first, to, rows in runs:
            sums = {}
            for r in range(rows + 2):
                for s, use in enumerate(uses):
                    value = load(s, first + r, chans)
                    turned = (pltpu.roll(value, 1, 1), value, pltpu.roll(value, NX - 1, 1))
                    for b in range(3):
                        o = r - b
                        if o < 0 or o >= rows:
                            continue
                        for a, k in use:
                            for e in range(3):
                                for h in range(2):
                                    term = gain[a * 9 + b * 3 + e] * turned[e][:, 128 * h : 128 * h + 128]
                                    place = (o, k, h)
                                    sums[place] = sums[place] + term if place in sums else term
                if r >= 2:
                    for k in sorted({k for use in uses for _, k in use}):
                        for h in range(2):
                            depth[k, to + r - 2, chans, pl.ds(128 * h, 128)] = sums.pop((r - 2, k, h))
        return 0

    lax.fori_loop(0, CH // 8, some, 0)


def mix_tile(mix, depth, k, t):
    tile = depth[k, pl.ds(8 * t, 8)].reshape(8 * CH, NX)
    return dot3(mix, parts(tile)).reshape(CH, 8, NX)


def pack_kernel(tiles, field, packed, edges, taken, sem_in):
    last = field.shape[1] // 8 - 1
    before, after = tiles[0] - 1, tiles[-1] + 1
    wanted = [before, *tiles, after] + [t for t in (0, last) if t not in (before, after)]
    row = fetch_tiles(field, taken, sem_in, wanted)
    for i, place in enumerate([(before, 7), *[(t, r) for t in tiles for r in range(8)], (after, 0)]):
        packed[i] = row(*place)
    edges[0] = row(last, 7)
    edges[1] = row(0, 0)


def own_kernel(segments, groups, weight, point, field, halo, *refs):
    last = field.shape[1] // 8 - 1
    count = 3 * len(groups)
    outs, (taken, halo_rows, weights, points, sent, lined, depth, gains, sem_in, sem_out, sem_few) = (
        refs[:count],
        refs[count:],
    )
    few = [
        pltpu.make_async_copy(src, dst, sem_few.at[i])
        for i, (src, dst) in enumerate(((weight, weights), (point, points), (halo, halo_rows)))
    ]
    for copy in few:
        copy.start()
    wanted = sorted({t for tiles in segments for t in (tiles[0] - 1, *tiles, tiles[-1] + 1) if 0 <= t <= last})
    row = fetch_tiles(field, taken, sem_in, wanted)
    for copy in few:
        copy.wait()
    spread_gains(weights, gains, range(3))
    mix = mixing(points[...])
    runs, at, done, order = [], 0, 0, []
    for tiles in segments:
        places = [(tiles[0] - 1, 7), *[(t, r) for t in tiles for r in range(8)], (tiles[-1] + 1, 0)]
        for i, (t, r) in enumerate(places):
            lined[at + i] = halo_rows[0] if t < 0 else halo_rows[1] if t > last else row(t, r)
        runs.append((at, done, 8 * len(tiles)))
        at, done = at + len(places), done + 8 * len(tiles)
        order += tiles
    tap_sums(lambda s, r, c: lined[r, c, :], [[(a, a) for a in range(3)]], gains, depth, runs)
    copies = []
    for g, tiles in enumerate(groups):
        for i, tile in enumerate(tiles):
            t = order.index(tile)
            for k in range(3):
                sent[k, t] = mix_tile(mix, depth, k, t)
                to = outs[3 * g + k].at[:, pl.ds(8 * i, 8), :]
                copies.append(pltpu.make_async_copy(sent.at[k, t], to, sem_out.at[k, t]))
                copies[-1].start()
    for copy in copies:
        copy.wait()


def middle_kernel(weight, point, low, own, high, out, taken, weights, points, sent, depth, gains, sem_in, sem_out):
    copies = [
        pltpu.make_async_copy(src, dst, sem_in.at[i])
        for i, (src, dst) in enumerate(
            ((weight, weights), (point, points), (low, taken.at[0]), (own, taken.at[1]), (high, taken.at[2]))
        )
    ]
    for copy in copies:
        copy.start()
    for copy in copies[:2]:
        copy.wait()
    spread_gains(weights, gains, range(3))
    mix = mixing(points[...])
    for copy in copies[2:]:
        copy.wait()
    rows = out.shape[1]
    tap_sums(lambda s, r, c: taken[s, r, c, :], [[(a, 0)] for a in range(3)], gains, depth, [(0, 0, rows)])
    copies = []
    for t in range(rows // 8):
        sent[t] = mix_tile(mix, depth, 0, t)
        copies.append(pltpu.make_async_copy(sent.at[t], out.at[:, pl.ds(8 * t, 8), :], sem_out.at[t]))
        copies[-1].start()
    for copy in copies:
        copy.wait()


ERFC = (
    0.17087277, -0.82215223, 1.48851587, -1.13520398, 0.27886807,
    -0.18628806, 0.09678418, 0.37409196, 1.00002368, -1.26551223 - math.log(2.0),
)


def gelu(value):
    size = jnp.abs(value) * math.sqrt(0.5)
    below = 1.0 + 0.5 * size
    t = pl.reciprocal(below, approx=True)
    t = t * (2.0 - below * t)
    series = ERFC[0] * t + ERFC[1]
    for factor in ERFC[2:]:
        series = series * t + factor
    tail = t * jnp.exp(series - size * size)
    return value * jnp.where(value < 0.0, tail, 1.0 - tail)


def inverse_kernel(upper, halved, first_modes, second_modes, bias, x_top, x_rest, y_top, y_rest, own, middle, second, low, high, out, base, columns):
    q = pl.program_id(0)
    groups, _, y_local, _ = out.shape

    @pl.when(q == 0)
    def _():
        gy = lax.axis_index("gy")
        for g in range(groups):
            pairs = []
            for pair in (2 * g, 2 * g + 1):
                some = pl.ds(pair * (MY // 2), MY // 2)
                one, two = first_modes[some, :], second_modes[some, :]
                if halved:
                    one, two = jnp.where(gy == 0, one, two), jnp.where(gy == 0, two, one)
                pairs.append(jnp.concatenate([one, two], axis=0))
            own_modes = jnp.concatenate(pairs, axis=1)
            crossed, is_real = swap_parts(own_modes)
            stack = jnp.concatenate([own_modes, jnp.where(is_real, -crossed, crossed)], axis=0)
            pair = parts(dot3((y_top[gy], y_rest[gy]), parts(stack)))
            for h in range(2):
                for k in range(2):
                    columns[h, k, pl.ds(g * y_local, y_local), :] = pair[k][:, 128 * h : 128 * h + 128]

    h, p = q // 2, q % 2
    rows = dot3((columns[h, 0], columns[h, 1]), (x_top[p], x_rest[p]))
    turn = upper + middle.shape[2]
    stop = turn + second.shape[2]
    for g in range(groups):
        plane = rows[g * y_local : (g + 1) * y_local] + bias[4 * g + q]
        base[g, 0, :upper] = plane[:upper] + own[g, 0, :upper]
        out[g, 0, upper:turn] = gelu(plane[upper:turn] + middle[g, 0])
        out[g, 0, turn:stop] = gelu(plane[turn:stop] + (second[g, 0] + (low[g, 0] + high[g, 0])))
        base[g, 0, upper:] = plane[stop:] + own[g, 0, upper:]


def finish_kernel(upper, _, base, low, high, out, sent, sem):
    tiles = base.shape[1] // 8
    gap = out.shape[1] // 8 - tiles
    copies = []
    for t in range(tiles):
        rows = pl.ds(8 * t, 8)
        sent[t] = gelu(base[:, rows, :] + (low[:, rows, :] + high[:, rows, :]))
        to = t if t < upper else t + gap
        copies.append(pltpu.make_async_copy(sent.at[t], out.at[:, pl.ds(8 * to, 8), :], sem.at[t]))
        copies[-1].start()
    for copy in copies:
        copy.wait()


def in_hbm(*arrays):
    return [pltpu.with_memory_space_constraint(a, pltpu.HBM) for a in arrays]


def params(limit=VMEM_BYTES):
    return pltpu.CompilerParams(vmem_limit_bytes=limit)


def cost(flops, moved):
    return pl.CostEstimate(flops=flops, bytes_accessed=moved, transcendentals=0)


def whole_block(table):
    return pl.BlockSpec(table.shape, lambda i: (0,) * table.ndim)


def by_four(array):
    return array.reshape(CH // 4, 4, *array.shape[1:])


def forward_call(field, gy, pinned):
    y_local = field.shape[1]
    tables = [*halves(x_table(False)), *halves(y_table(y_local, gy, False))]
    hbm = pl.BlockSpec(memory_space=pltpu.HBM)
    return pl.pallas_call(
        forward_kernel,
        out_shape=(pltpu.HBM if pinned else jax.ShapeDtypeStruct)((CH // 2 * MY, 4 * MX), F32),
        in_specs=[hbm] * 5,
        scratch_shapes=[
            pltpu.VMEM((4, CH // 4, y_local, NX), F32),
            pltpu.VMEM((2, 2, NX, 4 * MX), BF),
            pltpu.VMEM((2, 2 * MY, y_local), BF),
            pltpu.SemaphoreType.DMA((8,)),
        ],
        compiler_params=params(ALL_VMEM_BYTES),
        cost_estimate=cost(10**8, 2**18),
        name="forward_modes",
    )(*in_hbm(by_four(field), *tables))


def filter_call(arrived, gains, gz, gy, scale):
    fwd, inv = z_tables(gz, gy, gains.shape[2], scale)
    fwd, inv = halves(fwd), halves(inv)
    return pl.pallas_call(
        filter_kernel,
        out_shape=pltpu.HBM((arrived.shape[0] // gy, arrived.shape[1]), F32),
        compiler_params=params(),
        cost_estimate=cost(4 * 10**10, 2**18),
        name="filter_modes",
    )(arrived, *in_hbm(gains, *fwd, *inv))


def inverse_call(modes, halved, bias, own, middle, second, pair, upper, y_local, gy, scale):
    tables = [*halves(x_table(True, scale)), *halves(y_table(y_local, gy, True))]
    some = lambda rows: pl.BlockSpec((CH // 4, 1, rows, NX), lambda i: (0, i, 0, 0))
    planes = [*in_hbm(*map(by_four, (own, middle, second))), *map(by_four, pair)]
    rim = own.shape[1]
    result, base = pl.pallas_call(
        functools.partial(inverse_kernel, upper, halved),
        out_shape=[
            jax.ShapeDtypeStruct((CH // 4, 4, y_local, NX), F32),
            jax.ShapeDtypeStruct((CH // 4, 4, rim, NX), F32),
        ],
        grid=(4,),
        in_specs=[
            *[whole_block(m) for m in modes],
            pl.BlockSpec(memory_space=pltpu.SMEM),
            *[whole_block(t) for t in tables],
            *[some(p.shape[2]) for p in planes],
        ],
        out_specs=[some(y_local), some(rim)],
        scratch_shapes=[pltpu.VMEM((2, 2, CH // 4 * y_local, 128), BF)],
        compiler_params=params(),
        cost_estimate=cost(10**8, 2**18),
        name="inverse_modes",
    )(*modes, *in_hbm(bias, *tables), *planes)
    return result.reshape(CH, y_local, NX), base.reshape(CH, rim, NX)


def finish_call(result, base, low, high, upper):
    tiles = base.shape[1] // 8
    anywhere = pl.BlockSpec(memory_space=pl.ANY)
    vmem = pl.BlockSpec(memory_space=pltpu.VMEM)
    return pl.pallas_call(
        functools.partial(finish_kernel, upper),
        out_shape=jax.ShapeDtypeStruct(result.shape, F32),
        in_specs=[anywhere] + [vmem] * 3,
        out_specs=anywhere,
        scratch_shapes=[
            pltpu.VMEM((tiles, CH, 8, NX), F32),
            pltpu.SemaphoreType.DMA((tiles,)),
        ],
        input_output_aliases={0: 0},
        compiler_params=params(),
        cost_estimate=cost(10**8, 2**18),
        name="finished_rows",
    )(result, base, low, high)


def pack_call(field, tiles):
    count = 8 * len(tiles) + 2
    fetched = len(tiles) + 4
    vmem = pl.BlockSpec(memory_space=pltpu.VMEM)
    return pl.pallas_call(
        functools.partial(pack_kernel, tiles),
        out_shape=[jax.ShapeDtypeStruct((count, CH, NX), F32), jax.ShapeDtypeStruct((2, CH, NX), F32)],
        in_specs=[pl.BlockSpec(memory_space=pltpu.HBM)],
        out_specs=[vmem] * 2,
        scratch_shapes=[
            pltpu.VMEM((fetched, 2, CH, 8, 128), F32),
            pltpu.SemaphoreType.DMA((fetched, 2)),
        ],
        compiler_params=params(),
        cost_estimate=cost(10**8, 2**18),
        name="packed_rows",
    )(*in_hbm(field))


def own_call(field, halo, weight, point, segments, groups):
    tiles = sum(map(len, segments))
    rows, fetched = 8 * tiles, tiles + 2 * len(segments)
    hbm = pl.BlockSpec(memory_space=pltpu.HBM)
    shapes = [pltpu.HBM((CH, 8 * len(group), NX), F32) for group in groups for _ in range(3)]
    return pl.pallas_call(
        functools.partial(own_kernel, segments, groups),
        out_shape=shapes,
        in_specs=[hbm] * 3 + [pl.BlockSpec(memory_space=pl.ANY)],
        out_specs=[hbm] * len(shapes),
        scratch_shapes=[
            pltpu.VMEM((fetched, 2, CH, 8, 128), F32),
            pltpu.VMEM((2, CH, NX), F32),
            pltpu.VMEM((CH, 27), F32),
            pltpu.VMEM((CH, CH), F32),
            pltpu.VMEM((3, tiles, CH, 8, NX), F32),
            pltpu.VMEM((rows + 2 * len(segments), CH, NX), F32),
            pltpu.VMEM((3, rows, CH, NX), F32),
            pltpu.VMEM((27, CH, 128), F32),
            pltpu.SemaphoreType.DMA((fetched, 2)),
            pltpu.SemaphoreType.DMA((3, tiles)),
            pltpu.SemaphoreType.DMA((3,)),
        ],
        compiler_params=params(),
        cost_estimate=cost(10**8, 2**18),
        name="own_sums",
    )(*in_hbm(weight, point, field), halo)


def middle_call(weight, point, low, own, high):
    rows = own.shape[0] - 2
    hbm = pl.BlockSpec(memory_space=pltpu.HBM)
    return pl.pallas_call(
        middle_kernel,
        out_shape=pltpu.HBM((CH, rows, NX), F32),
        in_specs=[hbm] * 3 + [pl.BlockSpec(memory_space=pl.ANY), hbm],
        out_specs=hbm,
        scratch_shapes=[
            pltpu.VMEM((3, rows + 2, CH, NX), F32),
            pltpu.VMEM((CH, 27), F32),
            pltpu.VMEM((CH, CH), F32),
            pltpu.VMEM((rows // 8, CH, 8, NX), F32),
            pltpu.VMEM((1, rows, CH, NX), F32),
            pltpu.VMEM((27, CH, 128), F32),
            pltpu.SemaphoreType.DMA((5,)),
            pltpu.SemaphoreType.DMA((rows // 8,)),
        ],
        compiler_params=params(),
        cost_estimate=cost(4 * 10**10, 2**18),
        name="middle_sums",
    )(*in_hbm(weight, point, low), own, *in_hbm(high))


def general_filter(coarse, gains, gz, gy, scale):
    j_own, n_own = gains.shape[2], gains.shape[3]
    both = ("gz", "gy")
    flat = coarse.reshape(CH // 2, MY, 2, 2, MX).transpose(3, 1, 0, 2, 4).reshape(2, MY, CH * MX)
    sent = flat.reshape(2, gy, j_own, gz, n_own).transpose(3, 1, 0, 2, 4).reshape(gz * gy, -1)
    got = lax.all_to_all(sent, both, split_axis=0, concat_axis=0, tiled=True)
    got = got.reshape(gz, gy, 2, j_own, n_own)
    c, s = (jnp.asarray(t, F32) for t in trig(kept(MZ, gz), np.arange(gz), gz))
    mul = functools.partial(jnp.einsum, precision=lax.Precision.HIGHEST)
    whole = got.sum(axis=1) * scale
    real = mul("zjn,qz->qjn", whole[:, 0], c) + mul("zjn,qz->qjn", whole[:, 1], s)
    imag = mul("zjn,qz->qjn", whole[:, 1], c) - mul("zjn,qz->qjn", whole[:, 0], s)
    real, imag = real * gains[0] - imag * gains[1], real * gains[1] + imag * gains[0]
    out = jnp.stack(
        [
            mul("qjn,qz->zjn", real, c) - mul("qjn,qz->zjn", imag, s),
            mul("qjn,qz->zjn", real, s) + mul("qjn,qz->zjn", imag, c),
        ],
        axis=1,
    )
    out = jnp.broadcast_to(out[:, None], (gz, gy, 2, j_own, n_own)).reshape(gz * gy, -1)
    back = lax.all_to_all(out, both, split_axis=0, concat_axis=0, tiled=True)
    back = back.reshape(gz, gy, 2, j_own, n_own).transpose(2, 1, 3, 0, 4)
    back = back.reshape(2, MY, CH // 2, 2, MX)
    return back.transpose(2, 1, 3, 0, 4).reshape(CH // 2, MY, 4 * MX)


def body(field, spectral_filter, depth_weight, point_weight, bias_vector):
    gz, gy = lax.axis_size("gz"), lax.axis_size("gy")
    y_local = field.shape[2]
    field = field.reshape(CH, y_local, NX)
    y_total = gy * y_local
    forward_scale = 1.0 / math.sqrt(float(NX) * y_total * gz)
    inverse_scale = 1.0 / math.sqrt(2.0 * MX * MY * MZ)

    def ring(axis, count, by):
        return [(i, (i + by) % count) for i in range(count)]

    def to_neighbours(down, up):
        return (
            lax.ppermute(down, "gz", ring("gz", gz, 1)),
            lax.ppermute(up, "gz", ring("gz", gz, -1)),
        )

    def after(value, *others):
        return lax.optimization_barrier((value, *others))[0]

    last = y_local // 8 - 1
    cut = 1 + last // 2
    first_tiles, second_tiles = tuple(range(1, cut)), tuple(range(cut, min(cut + 2, last)))
    third_tiles = (0, *range(second_tiles[-1] + 1, last + 1))
    packed, edges = pack_call(field, first_tiles)
    first_low, first_high = to_neighbours(packed, packed)
    if gy == 2:
        halo = lax.ppermute(edges, "gy", ring("gy", gy, 1))
    else:
        halo = jnp.stack(
            [
                lax.ppermute(edges[0], "gy", ring("gy", gy, 1)),
                lax.ppermute(edges[1], "gy", ring("gy", gy, -1)),
            ]
        )
    j_own, n_own = spectral_filter.shape[2], spectral_filter.shape[3]
    whole_tiles = j_own == 8 and n_own == 2 * MX
    coarse = after(forward_call(after(field, packed), gy, whole_tiles), halo)
    segments, groups = ((0,), tuple(range(cut, last + 1))), (second_tiles, third_tiles)
    down, second, up, outer_down, own, outer_up = own_call(
        after(field, coarse), halo, depth_weight, point_weight, segments, groups
    )
    if whole_tiles:
        both = ("gz", "gy")
        got = lax.all_to_all(coarse, both, split_axis=0, concat_axis=0, tiled=True)
        pair = to_neighbours(after(down, first_low), after(up, first_high))
        gains = after(spectral_filter, first_low, first_high, second)
        mark = filter_call(got, gains, gz, gy, forward_scale)
        back = lax.all_to_all(mark, "gz", split_axis=0, concat_axis=0, tiled=True)
    else:
        pair = to_neighbours(down, up)
        mark = general_filter(coarse, spectral_filter, gz, gy, forward_scale)
        modes = [mark[:, part].reshape(-1, 4 * MX) for part in (slice(0, MY // 2), slice(MY // 2, MY))]
    outer_pair = to_neighbours(after(outer_down, mark), after(outer_up, mark))
    packed, *pair = lax.optimization_barrier((packed, *pair))
    mixed = middle_call(depth_weight, point_weight, first_low, packed, first_high)
    if whole_tiles:
        modes = (back, lax.ppermute(after(back, mixed), "gy", ring("gy", gy, 1)))
    result, base = inverse_call(
        modes, whole_tiles, bias_vector, own, mixed, second, pair, 8, y_local, gy, inverse_scale
    )
    result = finish_call(result, base, *outer_pair, 1)
    return result.reshape(CH, 1, y_local, NX)


def solution(mesh):
    in_specs = (P(None, "gz", "gy", None), P(None, None, "gy", "gz"), P(), P(), P())
    out_specs = P(None, "gz", "gy", None)
    return jax.shard_map(body, mesh=mesh, in_specs=in_specs, out_specs=out_specs, check_vma=False)
```

```python
import functools
import math

import jax
import jax.numpy as jnp
import ml_dtypes
import numpy as np
from jax import lax
from jax.experimental import pallas as pl
from jax.experimental.pallas import tpu as pltpu
from jax.sharding import PartitionSpec as P

NX = 256
MX = 32
MY = 16
MZ = 16
CH = 32
VMEM_BYTES = 20 * 1024 * 1024
ALL_VMEM_BYTES = 64000 * 1024
BF = jnp.bfloat16
F32 = jnp.float32


def kept(count, total):
    series = np.arange(count)
    return np.where(series < count // 2, series, total - count + series)


def trig(freqs, places, total):
    angle = 2.0 * np.pi * ((freqs[:, None] * places[None, :]) % total) / total
    return np.cos(angle), np.sin(angle)


def halves(table):
    table = np.asarray(table, np.float64)
    top = table.astype(np.float32).astype(ml_dtypes.bfloat16)
    rest = (table - top.astype(np.float64)).astype(np.float32).astype(ml_dtypes.bfloat16)
    return jnp.asarray(top), jnp.asarray(rest)


def y_table(y_local, gy, inverse):
    out = []
    for g in range(gy):
        places = g * y_local + np.arange(y_local)
        out.append(np.concatenate(trig(kept(MY, y_local * gy), places, y_local * gy), axis=0))
    return np.stack([t.T for t in out] if inverse else out)


def x_table(inverse, scale=1.0):
    c, s = trig(np.arange(MX), np.arange(NX), NX)
    w = np.where(np.arange(MX) == 0, 1.0, 2.0)[:, None] if inverse else 1.0
    out = np.zeros((2, 2, 2, MX, NX))
    for p in range(2):
        out[p, p, 0] = w * c * scale
        out[p, p, 1] = -w * s * scale
    out = out.reshape(2, 4 * MX, NX)
    return out if inverse else out.transpose(0, 2, 1)


def z_tables(gz, gy, rows, scale):
    c, s = trig(kept(MZ, gz), np.arange(gz), gz)
    eye = np.eye(rows)
    both = np.stack([c, s])
    fwd = np.einsum("tqz,g,jk->tqjzgk", both, np.ones(gy), eye) * scale
    inv = np.einsum("tqz,jk->tzjqk", both, eye)
    return fwd.reshape(2 * MZ * rows, gz * gy * rows), inv.reshape(2 * gz * rows, MZ * rows)


def parts(value):
    top = value.astype(BF)
    return top, (value - top.astype(F32)).astype(BF)


def dot(a, b):
    return jnp.dot(a, b, preferred_element_type=F32)


def dot3(a, b):
    rows = a[0].shape[0]
    both = dot(jnp.concatenate([a[0], a[1]], axis=0), b[0])
    return both[:rows] + (both[rows:] + dot(a[0], b[1]))


def swap_parts(value):
    lane = lax.broadcasted_iota(jnp.int32, value.shape, 1)
    is_real = (lane // MX) % 2 == 0
    width = value.shape[1]
    return jnp.where(is_real, pltpu.roll(value, width - MX, 1), pltpu.roll(value, MX, 1)), is_real


def forward_kernel(field, x_top, x_rest, y_top, y_rest, out, taken, x_both, y_both, sem):
    gy = lax.axis_index("gy")
    few = [
        pltpu.make_async_copy(src, dst, sem.at[4 + i])
        for i, (src, dst) in enumerate(
            ((x_top, x_both.at[0]), (x_rest, x_both.at[1]), (y_top.at[gy], y_both.at[0]), (y_rest.at[gy], y_both.at[1]))
        )
    ]
    copies = [pltpu.make_async_copy(field.at[:, q], taken.at[q], sem.at[q]) for q in range(4)]
    for copy in few + copies:
        copy.start()
    for copy in few:
        copy.wait()
    groups, rows = taken.shape[1:3]
    halves_of = []
    for q in range(4):
        copies[q].wait()
        part = dot3(parts(taken[q].reshape(groups * rows, NX)), (x_both[0, q % 2], x_both[1, q % 2]))
        if q % 2:
            halves_of[-1] = halves_of[-1] + part
        else:
            halves_of.append(part)
    total = jnp.concatenate(halves_of, axis=1)
    for g in range(groups):
        both = dot3((y_both[0], y_both[1]), parts(total[g * rows : (g + 1) * rows]))
        crossed, is_real = swap_parts(both[MY:])
        modes = both[:MY] + jnp.where(is_real, crossed, -crossed)
        out[pl.ds(2 * g * MY, MY), :] = modes[:, : 4 * MX]
        out[pl.ds((2 * g + 1) * MY, MY), :] = modes[:, 4 * MX :]


def filter_kernel(arrived, gains, f_top, f_rest, i_top, i_rest, out):
    real, imag = (gains[r].reshape(-1, 2 * MX) for r in range(2))
    first, second = slice(0, MX), slice(MX, 2 * MX)
    same = jnp.concatenate([real[:, first], real[:, first], real[:, second], real[:, second]], axis=1)
    cross = jnp.concatenate([-imag[:, first], imag[:, first], -imag[:, second], imag[:, second]], axis=1)
    half = f_top.shape[0] // 2
    turned = dot3((f_top[...], f_rest[...]), parts(arrived[...]))
    crossed, is_real = swap_parts(turned[half:])
    modes = turned[:half] + jnp.where(is_real, crossed, -crossed)
    crossed, _ = swap_parts(modes)
    filtered = modes * same + crossed * cross
    half = i_top.shape[0] // 2
    back = dot3((i_top[...], i_rest[...]), parts(filtered))
    crossed, is_real = swap_parts(back[half:])
    out[...] = back[:half] + jnp.where(is_real, -crossed, crossed)


def fetch_tiles(field, taken, sems, wanted):
    pending = {}
    for k, t in enumerate(wanted):
        pending[t] = [
            pltpu.make_async_copy(
                field.at[:, pl.ds(8 * t, 8), pl.ds(128 * h, 128)], taken.at[k, h], sems.at[k, h]
            )
            for h in range(2)
        ]
        for copy in pending[t]:
            copy.start()

    def row(t, r):
        for copy in pending.pop(t, ()):
            copy.wait()
        k = wanted.index(t)
        return jnp.concatenate(
            [taken.at[k, h].reshape(CH * 8, 128)[pl.ds(r, CH, stride=8), :] for h in range(2)], axis=1
        )

    return row


def odd_plane():
    return lax.rem(lax.axis_index("gz"), 2) == 1


def spread_gains(weights, gains, swapped):
    for k in range(27):
        column = weights[:, k : k + 1]
        mirror = 18 - 18 * (k // 18) + k % 9
        if k // 9 != 1:
            column = jnp.where(swapped, weights[:, mirror : mirror + 1], column)
        gains[k] = jnp.broadcast_to(column, (CH, 128))


def mixing(points):
    down = (
        lax.broadcasted_iota(jnp.int32, (8 * CH, CH), 0) // 8
        == lax.broadcasted_iota(jnp.int32, (8 * CH, CH), 1)
    ).astype(BF)
    across = (
        lax.broadcasted_iota(jnp.int32, (CH, 8 * CH), 1) % CH
        == lax.broadcasted_iota(jnp.int32, (CH, 8 * CH), 0)
    ).astype(BF)
    same = (
        lax.broadcasted_iota(jnp.int32, (8 * CH, 8 * CH), 0) % 8
        == lax.broadcasted_iota(jnp.int32, (8 * CH, 8 * CH), 1) // CH
    )
    return tuple(
        jnp.where(same, dot(dot(down, part).astype(BF), across), 0.0).astype(BF)
        for part in parts(points)
    )


def tap_sums(load, uses, gains, depth, runs):
    def some(i, _):
        chans = pl.ds(pl.multiple_of(i * 8, 8), 8)
        wanted = sorted({a for use in uses for a, _ in use})
        gain = {k: gains[k, chans, :] for a in wanted for k in range(9 * a, 9 * a + 9)}
        for first, to, rows in runs:
            sums = {}
            for r in range(rows + 2):
                for s, use in enumerate(uses):
                    value = load(s, first + r, chans)
                    turned = (pltpu.roll(value, 1, 1), value, pltpu.roll(value, NX - 1, 1))
                    for b in range(3):
                        o = r - b
                        if o < 0 or o >= rows:
                            continue
                        for a, k in use:
                            for e in range(3):
                                for h in range(2):
                                    term = gain[a * 9 + b * 3 + e] * turned[e][:, 128 * h : 128 * h + 128]
                                    place = (o, k, h)
                                    sums[place] = sums[place] + term if place in sums else term
                if r >= 2:
                    for k in sorted({k for use in uses for _, k in use}):
                        for h in range(2):
                            depth[k, to + r - 2, chans, pl.ds(128 * h, 128)] = sums.pop((r - 2, k, h))
        return 0

    lax.fori_loop(0, CH // 8, some, 0)


def mix_tile(mix, depth, k, t):
    tile = depth[k, pl.ds(8 * t, 8)].reshape(8 * CH, NX)
    return dot3(mix, parts(tile)).reshape(CH, 8, NX)


def pack_kernel(tiles, field, packed, edges, taken, sem_in):
    last = field.shape[1] // 8 - 1
    before, after = tiles[0] - 1, tiles[-1] + 1
    wanted = [before, *tiles, after] + [t for t in (0, last) if t not in (before, after)]
    row = fetch_tiles(field, taken, sem_in, wanted)
    for i, place in enumerate([(before, 7), *[(t, r) for t in tiles for r in range(8)], (after, 0)]):
        packed[i] = row(*place)
    edges[0] = row(last, 7)
    edges[1] = row(0, 0)


def own_kernel(segments, groups, weight, point, field, halo, *refs):
    last = field.shape[1] // 8 - 1
    count = 3 * len(groups)
    outs, (taken, halo_rows, weights, points, sent, lined, depth, gains, sem_in, sem_out, sem_few) = (
        refs[:count],
        refs[count:],
    )
    few = [
        pltpu.make_async_copy(src, dst, sem_few.at[i])
        for i, (src, dst) in enumerate(((weight, weights), (point, points), (halo, halo_rows)))
    ]
    for copy in few:
        copy.start()
    wanted = sorted({t for tiles in segments for t in (tiles[0] - 1, *tiles, tiles[-1] + 1) if 0 <= t <= last})
    row = fetch_tiles(field, taken, sem_in, wanted)
    for copy in few:
        copy.wait()
    spread_gains(weights, gains, jnp.logical_not(odd_plane()))
    mix = mixing(points[...])
    runs, at, done, order = [], 0, 0, []
    for tiles in segments:
        places = [(tiles[0] - 1, 7), *[(t, r) for t in tiles for r in range(8)], (tiles[-1] + 1, 0)]
        for i, (t, r) in enumerate(places):
            lined[at + i] = halo_rows[0] if t < 0 else halo_rows[1] if t > last else row(t, r)
        runs.append((at, done, 8 * len(tiles)))
        at, done = at + len(places), done + 8 * len(tiles)
        order += tiles
    tap_sums(lambda s, r, c: lined[r, c, :], [[(a, a) for a in range(3)]], gains, depth, runs)
    copies = []
    for g, tiles in enumerate(groups):
        for i, tile in enumerate(tiles):
            t = order.index(tile)
            for k in range(3):
                sent[k, t] = mix_tile(mix, depth, k, t)
                to = outs[3 * g + k].at[:, pl.ds(8 * i, 8), :]
                copies.append(pltpu.make_async_copy(sent.at[k, t], to, sem_out.at[k, t]))
                copies[-1].start()
    for copy in copies:
        copy.wait()


def middle_kernel(weight, point, low, own, high, out, taken, weights, points, sent, depth, gains, sem_in, sem_out):
    copies = [
        pltpu.make_async_copy(src, dst, sem_in.at[i])
        for i, (src, dst) in enumerate(
            ((weight, weights), (point, points), (low, taken.at[0]), (own, taken.at[1]), (high, taken.at[2]))
        )
    ]
    for copy in copies:
        copy.start()
    for copy in copies[:2]:
        copy.wait()
    spread_gains(weights, gains, odd_plane())
    mix = mixing(points[...])
    for copy in copies[2:]:
        copy.wait()
    rows = out.shape[1]
    tap_sums(lambda s, r, c: taken[s, r, c, :], [[(a, 0)] for a in range(3)], gains, depth, [(0, 0, rows)])
    copies = []
    for t in range(rows // 8):
        sent[t] = mix_tile(mix, depth, 0, t)
        copies.append(pltpu.make_async_copy(sent.at[t], out.at[:, pl.ds(8 * t, 8), :], sem_out.at[t]))
        copies[-1].start()
    for copy in copies:
        copy.wait()


ERFC = (
    0.17087277, -0.82215223, 1.48851587, -1.13520398, 0.27886807,
    -0.18628806, 0.09678418, 0.37409196, 1.00002368, -1.26551223 - math.log(2.0),
)


def gelu(value):
    size = jnp.abs(value) * math.sqrt(0.5)
    below = 1.0 + 0.5 * size
    t = pl.reciprocal(below, approx=True)
    t = t * (2.0 - below * t)
    series = ERFC[0] * t + ERFC[1]
    for factor in ERFC[2:]:
        series = series * t + factor
    tail = t * jnp.exp(series - size * size)
    return value * jnp.where(value < 0.0, tail, 1.0 - tail)


def inverse_kernel(upper, halved, first_modes, second_modes, bias, x_top, x_rest, y_top, y_rest, own, middle, second, low, high, out, base, columns):
    q = pl.program_id(0)
    groups, _, y_local, _ = out.shape

    @pl.when(q == 0)
    def _():
        gy = lax.axis_index("gy")
        for g in range(groups):
            pairs = []
            for pair in (2 * g, 2 * g + 1):
                some = pl.ds(pair * (MY // 2), MY // 2)
                one, two = first_modes[some, :], second_modes[some, :]
                if halved:
                    one, two = jnp.where(gy == 0, one, two), jnp.where(gy == 0, two, one)
                pairs.append(jnp.concatenate([one, two], axis=0))
            own_modes = jnp.concatenate(pairs, axis=1)
            crossed, is_real = swap_parts(own_modes)
            stack = jnp.concatenate([own_modes, jnp.where(is_real, -crossed, crossed)], axis=0)
            pair = parts(dot3((y_top[gy], y_rest[gy]), parts(stack)))
            for h in range(2):
                for k in range(2):
                    columns[h, k, pl.ds(g * y_local, y_local), :] = pair[k][:, 128 * h : 128 * h + 128]

    h, p = q // 2, q % 2
    rows = dot3((columns[h, 0], columns[h, 1]), (x_top[p], x_rest[p]))
    turn = upper + middle.shape[2]
    stop = turn + second.shape[2]
    for g in range(groups):
        plane = rows[g * y_local : (g + 1) * y_local] + bias[4 * g + q]
        base[g, 0, :upper] = plane[:upper] + own[g, 0, :upper]
        out[g, 0, upper:turn] = gelu(plane[upper:turn] + middle[g, 0])
        out[g, 0, turn:stop] = gelu(plane[turn:stop] + (second[g, 0] + (low[g, 0] + high[g, 0])))
        base[g, 0, upper:] = plane[stop:] + own[g, 0, upper:]


def finish_kernel(upper, _, base, low, high, out, sent, sem):
    tiles = base.shape[1] // 8
    gap = out.shape[1] // 8 - tiles
    copies = []
    for t in range(tiles):
        rows = pl.ds(8 * t, 8)
        sent[t] = gelu(base[:, rows, :] + (low[:, rows, :] + high[:, rows, :]))
        to = t if t < upper else t + gap
        copies.append(pltpu.make_async_copy(sent.at[t], out.at[:, pl.ds(8 * to, 8), :], sem.at[t]))
        copies[-1].start()
    for copy in copies:
        copy.wait()


def in_hbm(*arrays):
    return [pltpu.with_memory_space_constraint(a, pltpu.HBM) for a in arrays]


def params(limit=VMEM_BYTES):
    return pltpu.CompilerParams(vmem_limit_bytes=limit)


def cost(flops, moved):
    return pl.CostEstimate(flops=flops, bytes_accessed=moved, transcendentals=0)


def whole_block(table):
    return pl.BlockSpec(table.shape, lambda i: (0,) * table.ndim)


def by_four(array):
    return array.reshape(CH // 4, 4, *array.shape[1:])


def forward_call(field, gy, pinned):
    y_local = field.shape[1]
    tables = [*halves(x_table(False)), *halves(y_table(y_local, gy, False))]
    hbm = pl.BlockSpec(memory_space=pltpu.HBM)
    return pl.pallas_call(
        forward_kernel,
        out_shape=(pltpu.HBM if pinned else jax.ShapeDtypeStruct)((CH // 2 * MY, 4 * MX), F32),
        in_specs=[hbm] * 5,
        scratch_shapes=[
            pltpu.VMEM((4, CH // 4, y_local, NX), F32),
            pltpu.VMEM((2, 2, NX, 4 * MX), BF),
            pltpu.VMEM((2, 2 * MY, y_local), BF),
            pltpu.SemaphoreType.DMA((8,)),
        ],
        compiler_params=params(ALL_VMEM_BYTES),
        cost_estimate=cost(10**8, 2**18),
        name="forward_modes",
    )(*in_hbm(by_four(field), *tables))


def filter_call(arrived, gains, gz, gy, scale):
    fwd, inv = z_tables(gz, gy, gains.shape[2], scale)
    fwd, inv = halves(fwd), halves(inv)
    return pl.pallas_call(
        filter_kernel,
        out_shape=pltpu.HBM((arrived.shape[0] // gy, arrived.shape[1]), F32),
        compiler_params=params(),
        cost_estimate=cost(4 * 10**10, 2**18),
        name="filter_modes",
    )(arrived, *in_hbm(gains, *fwd, *inv))


def inverse_call(modes, halved, bias, own, middle, second, pair, upper, y_local, gy, scale):
    tables = [*halves(x_table(True, scale)), *halves(y_table(y_local, gy, True))]
    some = lambda rows: pl.BlockSpec((CH // 4, 1, rows, NX), lambda i: (0, i, 0, 0))
    planes = [*in_hbm(*map(by_four, (own, middle, second))), *map(by_four, pair)]
    rim = own.shape[1]
    result, base = pl.pallas_call(
        functools.partial(inverse_kernel, upper, halved),
        out_shape=[
            jax.ShapeDtypeStruct((CH // 4, 4, y_local, NX), F32),
            jax.ShapeDtypeStruct((CH // 4, 4, rim, NX), F32),
        ],
        grid=(4,),
        in_specs=[
            *[whole_block(m) for m in modes],
            pl.BlockSpec(memory_space=pltpu.SMEM),
            *[whole_block(t) for t in tables],
            *[some(p.shape[2]) for p in planes],
        ],
        out_specs=[some(y_local), some(rim)],
        scratch_shapes=[pltpu.VMEM((2, 2, CH // 4 * y_local, 128), BF)],
        compiler_params=params(),
        cost_estimate=cost(10**8, 2**18),
        name="inverse_modes",
    )(*modes, *in_hbm(bias, *tables), *planes)
    return result.reshape(CH, y_local, NX), base.reshape(CH, rim, NX)


def finish_call(result, base, low, high, upper):
    tiles = base.shape[1] // 8
    anywhere = pl.BlockSpec(memory_space=pl.ANY)
    vmem = pl.BlockSpec(memory_space=pltpu.VMEM)
    return pl.pallas_call(
        functools.partial(finish_kernel, upper),
        out_shape=jax.ShapeDtypeStruct(result.shape, F32),
        in_specs=[anywhere] + [vmem] * 3,
        out_specs=anywhere,
        scratch_shapes=[
            pltpu.VMEM((tiles, CH, 8, NX), F32),
            pltpu.SemaphoreType.DMA((tiles,)),
        ],
        input_output_aliases={0: 0},
        compiler_params=params(),
        cost_estimate=cost(10**8, 2**18),
        name="finished_rows",
    )(result, base, low, high)


def pack_call(field, tiles):
    count = 8 * len(tiles) + 2
    fetched = len(tiles) + 4
    vmem = pl.BlockSpec(memory_space=pltpu.VMEM)
    return pl.pallas_call(
        functools.partial(pack_kernel, tiles),
        out_shape=[jax.ShapeDtypeStruct((count, CH, NX), F32), jax.ShapeDtypeStruct((2, CH, NX), F32)],
        in_specs=[pl.BlockSpec(memory_space=pltpu.HBM)],
        out_specs=[vmem] * 2,
        scratch_shapes=[
            pltpu.VMEM((fetched, 2, CH, 8, 128), F32),
            pltpu.SemaphoreType.DMA((fetched, 2)),
        ],
        compiler_params=params(),
        cost_estimate=cost(10**8, 2**18),
        name="packed_rows",
    )(*in_hbm(field))


def own_call(field, halo, weight, point, segments, groups):
    tiles = sum(map(len, segments))
    rows, fetched = 8 * tiles, tiles + 2 * len(segments)
    hbm = pl.BlockSpec(memory_space=pltpu.HBM)
    shapes = [pltpu.HBM((CH, 8 * len(group), NX), F32) for group in groups for _ in range(3)]
    return pl.pallas_call(
        functools.partial(own_kernel, segments, groups),
        out_shape=shapes,
        in_specs=[hbm] * 3 + [pl.BlockSpec(memory_space=pl.ANY)],
        out_specs=[hbm] * len(shapes),
        scratch_shapes=[
            pltpu.VMEM((fetched, 2, CH, 8, 128), F32),
            pltpu.VMEM((2, CH, NX), F32),
            pltpu.VMEM((CH, 27), F32),
            pltpu.VMEM((CH, CH), F32),
            pltpu.VMEM((3, tiles, CH, 8, NX), F32),
            pltpu.VMEM((rows + 2 * len(segments), CH, NX), F32),
            pltpu.VMEM((3, rows, CH, NX), F32),
            pltpu.VMEM((27, CH, 128), F32),
            pltpu.SemaphoreType.DMA((fetched, 2)),
            pltpu.SemaphoreType.DMA((3, tiles)),
            pltpu.SemaphoreType.DMA((3,)),
        ],
        compiler_params=params(),
        cost_estimate=cost(10**8, 2**18),
        name="own_sums",
    )(*in_hbm(weight, point, field), halo)


def middle_call(weight, point, low, own, high):
    rows = own.shape[0] - 2
    hbm = pl.BlockSpec(memory_space=pltpu.HBM)
    return pl.pallas_call(
        middle_kernel,
        out_shape=pltpu.HBM((CH, rows, NX), F32),
        in_specs=[hbm] * 3 + [pl.BlockSpec(memory_space=pl.ANY), hbm],
        out_specs=hbm,
        scratch_shapes=[
            pltpu.VMEM((3, rows + 2, CH, NX), F32),
            pltpu.VMEM((CH, 27), F32),
            pltpu.VMEM((CH, CH), F32),
            pltpu.VMEM((rows // 8, CH, 8, NX), F32),
            pltpu.VMEM((1, rows, CH, NX), F32),
            pltpu.VMEM((27, CH, 128), F32),
            pltpu.SemaphoreType.DMA((5,)),
            pltpu.SemaphoreType.DMA((rows // 8,)),
        ],
        compiler_params=params(),
        cost_estimate=cost(4 * 10**10, 2**18),
        name="middle_sums",
    )(*in_hbm(weight, point, low), own, *in_hbm(high))


def general_filter(coarse, gains, gz, gy, scale):
    j_own, n_own = gains.shape[2], gains.shape[3]
    both = ("gz", "gy")
    flat = coarse.reshape(CH // 2, MY, 2, 2, MX).transpose(3, 1, 0, 2, 4).reshape(2, MY, CH * MX)
    sent = flat.reshape(2, gy, j_own, gz, n_own).transpose(3, 1, 0, 2, 4).reshape(gz * gy, -1)
    got = lax.all_to_all(sent, both, split_axis=0, concat_axis=0, tiled=True)
    got = got.reshape(gz, gy, 2, j_own, n_own)
    c, s = (jnp.asarray(t, F32) for t in trig(kept(MZ, gz), np.arange(gz), gz))
    mul = functools.partial(jnp.einsum, precision=lax.Precision.HIGHEST)
    whole = got.sum(axis=1) * scale
    real = mul("zjn,qz->qjn", whole[:, 0], c) + mul("zjn,qz->qjn", whole[:, 1], s)
    imag = mul("zjn,qz->qjn", whole[:, 1], c) - mul("zjn,qz->qjn", whole[:, 0], s)
    real, imag = real * gains[0] - imag * gains[1], real * gains[1] + imag * gains[0]
    out = jnp.stack(
        [
            mul("qjn,qz->zjn", real, c) - mul("qjn,qz->zjn", imag, s),
            mul("qjn,qz->zjn", real, s) + mul("qjn,qz->zjn", imag, c),
        ],
        axis=1,
    )
    out = jnp.broadcast_to(out[:, None], (gz, gy, 2, j_own, n_own)).reshape(gz * gy, -1)
    back = lax.all_to_all(out, both, split_axis=0, concat_axis=0, tiled=True)
    back = back.reshape(gz, gy, 2, j_own, n_own).transpose(2, 1, 3, 0, 4)
    back = back.reshape(2, MY, CH // 2, 2, MX)
    return back.transpose(2, 1, 3, 0, 4).reshape(CH // 2, MY, 4 * MX)


def body(field, spectral_filter, depth_weight, point_weight, bias_vector):
    gz, gy = lax.axis_size("gz"), lax.axis_size("gy")
    y_local = field.shape[2]
    field = field.reshape(CH, y_local, NX)
    y_total = gy * y_local
    forward_scale = 1.0 / math.sqrt(float(NX) * y_total * gz)
    inverse_scale = 1.0 / math.sqrt(2.0 * MX * MY * MZ)

    def ring(axis, count, by):
        return [(i, (i + by) % count) for i in range(count)]

    def to_neighbours(across, within):
        odd_on = [(i, (i + 1 if i % 2 else i - 1) % gz) for i in range(gz)]
        even_on = [(i, (i - 1 if i % 2 else i + 1) % gz) for i in range(gz)]
        return lax.ppermute(across, "gz", odd_on), lax.ppermute(within, "gz", even_on)

    def after(value, *others):
        return lax.optimization_barrier((value, *others))[0]

    last = y_local // 8 - 1
    cut = 1 + last // 2
    first_tiles, second_tiles = tuple(range(1, cut)), tuple(range(cut, min(cut + 2, last)))
    third_tiles = (0, *range(second_tiles[-1] + 1, last + 1))
    packed, edges = pack_call(field, first_tiles)
    first_low, first_high = to_neighbours(packed, packed)
    if gy == 2:
        halo = lax.ppermute(edges, "gy", ring("gy", gy, 1))
    else:
        halo = jnp.stack(
            [
                lax.ppermute(edges[0], "gy", ring("gy", gy, 1)),
                lax.ppermute(edges[1], "gy", ring("gy", gy, -1)),
            ]
        )
    j_own, n_own = spectral_filter.shape[2], spectral_filter.shape[3]
    whole_tiles = j_own == 8 and n_own == 2 * MX
    coarse = after(forward_call(after(field, packed), gy, whole_tiles), halo)
    segments, groups = ((0,), tuple(range(cut, last + 1))), (second_tiles, third_tiles)
    down, second, up, outer_down, own, outer_up = own_call(
        after(field, coarse), halo, depth_weight, point_weight, segments, groups
    )
    if whole_tiles:
        both = ("gz", "gy")
        got = lax.all_to_all(coarse, both, split_axis=0, concat_axis=0, tiled=True)
        down, up = lax.optimization_barrier((down, up, first_low))[:2]
        pair = to_neighbours(down, up)
        gains = after(spectral_filter, first_low, first_high, second)
        mark = filter_call(got, gains, gz, gy, forward_scale)
        back = lax.all_to_all(mark, "gz", split_axis=0, concat_axis=0, tiled=True)
    else:
        pair = to_neighbours(down, up)
        mark = general_filter(coarse, spectral_filter, gz, gy, forward_scale)
        modes = [mark[:, part].reshape(-1, 4 * MX) for part in (slice(0, MY // 2), slice(MY // 2, MY))]
    outer_pair = to_neighbours(after(outer_down, mark), after(outer_up, mark))
    packed, *pair = lax.optimization_barrier((packed, *pair))
    mixed = middle_call(depth_weight, point_weight, first_low, packed, first_high)
    if whole_tiles:
        modes = (back, lax.ppermute(after(back, mixed), "gy", ring("gy", gy, 1)))
    result, base = inverse_call(
        modes, whole_tiles, bias_vector, own, mixed, second, pair, 8, y_local, gy, inverse_scale
    )
    result = finish_call(result, base, *outer_pair, 1)
    return result.reshape(CH, 1, y_local, NX)


def solution(mesh):
    in_specs = (P(None, "gz", "gy", None), P(None, None, "gy", "gz"), P(), P(), P())
    out_specs = P(None, "gz", "gy", None)
    return jax.shard_map(body, mesh=mesh, in_specs=in_specs, out_specs=out_specs, check_vma=False)
```

```python
import functools
import math

import jax
import jax.numpy as jnp
import ml_dtypes
import numpy as np
from jax import lax
from jax.experimental import pallas as pl
from jax.experimental.pallas import tpu as pltpu
from jax.sharding import PartitionSpec as P

NX = 256
MX = 32
MY = 16
MZ = 16
CH = 32
VMEM_BYTES = 20 * 1024 * 1024
ALL_VMEM_BYTES = 64000 * 1024
BF = jnp.bfloat16
F32 = jnp.float32


def kept(count, total):
    series = np.arange(count)
    return np.where(series < count // 2, series, total - count + series)


def trig(freqs, places, total):
    angle = 2.0 * np.pi * ((freqs[:, None] * places[None, :]) % total) / total
    return np.cos(angle), np.sin(angle)


def halves(table):
    table = np.asarray(table, np.float64)
    top = table.astype(np.float32).astype(ml_dtypes.bfloat16)
    rest = (table - top.astype(np.float64)).astype(np.float32).astype(ml_dtypes.bfloat16)
    return jnp.asarray(top), jnp.asarray(rest)


def y_table(y_local, gy, inverse):
    out = []
    for g in range(gy):
        places = g * y_local + np.arange(y_local)
        out.append(np.concatenate(trig(kept(MY, y_local * gy), places, y_local * gy), axis=0))
    return np.stack([t.T for t in out] if inverse else out)


def x_table(inverse, scale=1.0):
    c, s = trig(np.arange(MX), np.arange(NX), NX)
    w = np.where(np.arange(MX) == 0, 1.0, 2.0)[:, None] if inverse else 1.0
    out = np.zeros((2, 2, 2, MX, NX))
    for p in range(2):
        out[p, p, 0] = w * c * scale
        out[p, p, 1] = -w * s * scale
    out = out.reshape(2, 4 * MX, NX)
    return out if inverse else out.transpose(0, 2, 1)


def z_tables(gz, gy, rows, scale):
    c, s = trig(kept(MZ, gz), np.arange(gz), gz)
    eye = np.eye(rows)
    both = np.stack([c, s])
    fwd = np.einsum("tqz,g,jk->tqjzgk", both, np.ones(gy), eye) * scale
    inv = np.einsum("tqz,jk->tzjqk", both, eye)
    return fwd.reshape(2 * MZ * rows, gz * gy * rows), inv.reshape(2 * gz * rows, MZ * rows)


def parts(value):
    top = value.astype(BF)
    return top, (value - top.astype(F32)).astype(BF)


def dot(a, b):
    return jnp.dot(a, b, preferred_element_type=F32)


def dot3(a, b):
    rows = a[0].shape[0]
    both = dot(jnp.concatenate([a[0], a[1]], axis=0), b[0])
    return both[:rows] + (both[rows:] + dot(a[0], b[1]))


def swap_parts(value):
    lane = lax.broadcasted_iota(jnp.int32, value.shape, 1)
    is_real = (lane // MX) % 2 == 0
    width = value.shape[1]
    return jnp.where(is_real, pltpu.roll(value, width - MX, 1), pltpu.roll(value, MX, 1)), is_real


def forward_kernel(field, x_top, x_rest, y_top, y_rest, out, taken, x_both, y_both, sem):
    gy = lax.axis_index("gy")
    few = [
        pltpu.make_async_copy(src, dst, sem.at[4 + i])
        for i, (src, dst) in enumerate(
            ((x_top, x_both.at[0]), (x_rest, x_both.at[1]), (y_top.at[gy], y_both.at[0]), (y_rest.at[gy], y_both.at[1]))
        )
    ]
    copies = [pltpu.make_async_copy(field.at[:, q], taken.at[q], sem.at[q]) for q in range(4)]
    for copy in few + copies:
        copy.start()
    for copy in few:
        copy.wait()
    groups, rows = taken.shape[1:3]
    halves_of = []
    for q in range(4):
        copies[q].wait()
        part = dot3(parts(taken[q].reshape(groups * rows, NX)), (x_both[0, q % 2], x_both[1, q % 2]))
        if q % 2:
            halves_of[-1] = halves_of[-1] + part
        else:
            halves_of.append(part)
    total = jnp.concatenate(halves_of, axis=1)
    for g in range(groups):
        both = dot3((y_both[0], y_both[1]), parts(total[g * rows : (g + 1) * rows]))
        crossed, is_real = swap_parts(both[MY:])
        modes = both[:MY] + jnp.where(is_real, crossed, -crossed)
        out[pl.ds(2 * g * MY, MY), :] = modes[:, : 4 * MX]
        out[pl.ds((2 * g + 1) * MY, MY), :] = modes[:, 4 * MX :]


def filter_kernel(arrived, gains, f_top, f_rest, i_top, i_rest, out):
    real, imag = (gains[r].reshape(-1, 2 * MX) for r in range(2))
    first, second = slice(0, MX), slice(MX, 2 * MX)
    same = jnp.concatenate([real[:, first], real[:, first], real[:, second], real[:, second]], axis=1)
    cross = jnp.concatenate([-imag[:, first], imag[:, first], -imag[:, second], imag[:, second]], axis=1)
    half = f_top.shape[0] // 2
    turned = dot3((f_top[...], f_rest[...]), parts(arrived[...]))
    crossed, is_real = swap_parts(turned[half:])
    modes = turned[:half] + jnp.where(is_real, crossed, -crossed)
    crossed, _ = swap_parts(modes)
    filtered = modes * same + crossed * cross
    half = i_top.shape[0] // 2
    back = dot3((i_top[...], i_rest[...]), parts(filtered))
    crossed, is_real = swap_parts(back[half:])
    out[...] = back[:half] + jnp.where(is_real, -crossed, crossed)


def fetch_tiles(field, taken, sems, wanted):
    pending = {}
    for k, t in enumerate(wanted):
        pending[t] = [
            pltpu.make_async_copy(
                field.at[:, pl.ds(8 * t, 8), pl.ds(128 * h, 128)], taken.at[k, h], sems.at[k, h]
            )
            for h in range(2)
        ]
        for copy in pending[t]:
            copy.start()

    def row(t, r):
        for copy in pending.pop(t, ()):
            copy.wait()
        k = wanted.index(t)
        return jnp.concatenate(
            [taken.at[k, h].reshape(CH * 8, 128)[pl.ds(r, CH, stride=8), :] for h in range(2)], axis=1
        )

    return row


def odd_plane():
    return lax.rem(lax.axis_index("gz"), 2) == 1


def spread_gains(weights, gains, swapped):
    for k in range(27):
        column = weights[:, k : k + 1]
        mirror = 18 - 18 * (k // 18) + k % 9
        if k // 9 != 1:
            column = jnp.where(swapped, weights[:, mirror : mirror + 1], column)
        gains[k] = jnp.broadcast_to(column, (CH, 128))


def mixing(points):
    down = (
        lax.broadcasted_iota(jnp.int32, (8 * CH, CH), 0) // 8
        == lax.broadcasted_iota(jnp.int32, (8 * CH, CH), 1)
    ).astype(BF)
    across = (
        lax.broadcasted_iota(jnp.int32, (CH, 8 * CH), 1) % CH
        == lax.broadcasted_iota(jnp.int32, (CH, 8 * CH), 0)
    ).astype(BF)
    same = (
        lax.broadcasted_iota(jnp.int32, (8 * CH, 8 * CH), 0) % 8
        == lax.broadcasted_iota(jnp.int32, (8 * CH, 8 * CH), 1) // CH
    )
    return tuple(
        jnp.where(same, dot(dot(down, part).astype(BF), across), 0.0).astype(BF)
        for part in parts(points)
    )


def tap_sums(load, uses, gains, depth, runs):
    def some(i, _):
        chans = pl.ds(pl.multiple_of(i * 8, 8), 8)
        wanted = sorted({a for use in uses for a, _ in use})
        gain = {k: gains[k, chans, :] for a in wanted for k in range(9 * a, 9 * a + 9)}
        for first, to, rows in runs:
            sums = {}
            for r in range(rows + 2):
                for s, use in enumerate(uses):
                    value = load(s, first + r, chans)
                    turned = (pltpu.roll(value, 1, 1), value, pltpu.roll(value, NX - 1, 1))
                    for b in range(3):
                        o = r - b
                        if o < 0 or o >= rows:
                            continue
                        for a, k in use:
                            for e in range(3):
                                for h in range(2):
                                    term = gain[a * 9 + b * 3 + e] * turned[e][:, 128 * h : 128 * h + 128]
                                    place = (o, k, h)
                                    sums[place] = sums[place] + term if place in sums else term
                if r >= 2:
                    for k in sorted({k for use in uses for _, k in use}):
                        for h in range(2):
                            depth[k, to + r - 2, chans, pl.ds(128 * h, 128)] = sums.pop((r - 2, k, h))
        return 0

    lax.fori_loop(0, CH // 8, some, 0)


def mix_tile(mix, depth, k, t):
    tile = depth[k, pl.ds(8 * t, 8)].reshape(8 * CH, NX)
    return dot3(mix, parts(tile)).reshape(CH, 8, NX)


def pack_kernel(tiles, field, packed, edges, taken, sem_in):
    last = field.shape[1] // 8 - 1
    before, after = tiles[0] - 1, tiles[-1] + 1
    wanted = [before, *tiles, after] + [t for t in (0, last) if t not in (before, after)]
    row = fetch_tiles(field, taken, sem_in, wanted)
    for i, place in enumerate([(before, 7), *[(t, r) for t in tiles for r in range(8)], (after, 0)]):
        packed[i] = row(*place)
    edges[0] = row(last, 7)
    edges[1] = row(0, 0)


def own_kernel(segments, groups, weight, point, field, halo, *refs):
    last = field.shape[1] // 8 - 1
    count = 3 * len(groups)
    outs, (taken, halo_rows, weights, points, sent, lined, depth, gains, sem_in, sem_out, sem_few) = (
        refs[:count],
        refs[count:],
    )
    few = [
        pltpu.make_async_copy(src, dst, sem_few.at[i])
        for i, (src, dst) in enumerate(((weight, weights), (point, points), (halo, halo_rows)))
    ]
    for copy in few:
        copy.start()
    wanted = sorted({t for tiles in segments for t in (tiles[0] - 1, *tiles, tiles[-1] + 1) if 0 <= t <= last})
    row = fetch_tiles(field, taken, sem_in, wanted)
    for copy in few:
        copy.wait()
    spread_gains(weights, gains, jnp.logical_not(odd_plane()))
    mix = mixing(points[...])
    runs, at, done, order = [], 0, 0, []
    for tiles in segments:
        places = [(tiles[0] - 1, 7), *[(t, r) for t in tiles for r in range(8)], (tiles[-1] + 1, 0)]
        for i, (t, r) in enumerate(places):
            lined[at + i] = halo_rows[0] if t < 0 else halo_rows[1] if t > last else row(t, r)
        runs.append((at, done, 8 * len(tiles)))
        at, done = at + len(places), done + 8 * len(tiles)
        order += tiles
    tap_sums(lambda s, r, c: lined[r, c, :], [[(a, a) for a in range(3)]], gains, depth, runs)
    copies = []
    for g, tiles in enumerate(groups):
        for i, tile in enumerate(tiles):
            t = order.index(tile)
            for k in range(3):
                sent[k, t] = mix_tile(mix, depth, k, t)
                to = outs[3 * g + k].at[:, pl.ds(8 * i, 8), :]
                copies.append(pltpu.make_async_copy(sent.at[k, t], to, sem_out.at[k, t]))
                copies[-1].start()
    for copy in copies:
        copy.wait()


def middle_kernel(weight, point, low, own, high, out, taken, weights, points, sent, depth, gains, sem_in, sem_out):
    copies = [
        pltpu.make_async_copy(src, dst, sem_in.at[i])
        for i, (src, dst) in enumerate(
            ((weight, weights), (point, points), (low, taken.at[0]), (own, taken.at[1]), (high, taken.at[2]))
        )
    ]
    for copy in copies:
        copy.start()
    for copy in copies[:2]:
        copy.wait()
    spread_gains(weights, gains, odd_plane())
    mix = mixing(points[...])
    for copy in copies[2:]:
        copy.wait()
    rows = out.shape[1]
    tap_sums(lambda s, r, c: taken[s, r, c, :], [[(a, 0)] for a in range(3)], gains, depth, [(0, 0, rows)])
    copies = []
    for t in range(rows // 8):
        sent[t] = mix_tile(mix, depth, 0, t)
        copies.append(pltpu.make_async_copy(sent.at[t], out.at[:, pl.ds(8 * t, 8), :], sem_out.at[t]))
        copies[-1].start()
    for copy in copies:
        copy.wait()


ERFC = (
    0.17087277, -0.82215223, 1.48851587, -1.13520398, 0.27886807,
    -0.18628806, 0.09678418, 0.37409196, 1.00002368, -1.26551223 - math.log(2.0),
)


def gelu(value):
    size = jnp.abs(value) * math.sqrt(0.5)
    below = 1.0 + 0.5 * size
    t = pl.reciprocal(below, approx=True)
    t = t * (2.0 - below * t)
    series = ERFC[0] * t + ERFC[1]
    for factor in ERFC[2:]:
        series = series * t + factor
    tail = t * jnp.exp(series - size * size)
    return value * jnp.where(value < 0.0, tail, 1.0 - tail)


def inverse_kernel(upper, halved, first_modes, second_modes, bias, x_top, x_rest, y_top, y_rest, own, middle, second, low, high, out, base, columns):
    q = pl.program_id(0)
    groups, _, y_local, _ = out.shape

    @pl.when(q == 0)
    def _():
        gy = lax.axis_index("gy")
        for g in range(groups):
            pairs = []
            for pair in (2 * g, 2 * g + 1):
                some = pl.ds(pair * (MY // 2), MY // 2)
                one, two = first_modes[some, :], second_modes[some, :]
                if halved:
                    one, two = jnp.where(gy == 0, one, two), jnp.where(gy == 0, two, one)
                pairs.append(jnp.concatenate([one, two], axis=0))
            own_modes = jnp.concatenate(pairs, axis=1)
            crossed, is_real = swap_parts(own_modes)
            stack = jnp.concatenate([own_modes, jnp.where(is_real, -crossed, crossed)], axis=0)
            pair = parts(dot3((y_top[gy], y_rest[gy]), parts(stack)))
            for h in range(2):
                for k in range(2):
                    columns[h, k, pl.ds(g * y_local, y_local), :] = pair[k][:, 128 * h : 128 * h + 128]

    h, p = q // 2, q % 2
    rows = dot3((columns[h, 0], columns[h, 1]), (x_top[p], x_rest[p]))
    turn = upper + middle.shape[2]
    stop = turn + second.shape[2]
    for g in range(groups):
        plane = rows[g * y_local : (g + 1) * y_local] + bias[4 * g + q]
        base[g, 0, :upper] = plane[:upper] + own[g, 0, :upper]
        out[g, 0, upper:turn] = gelu(plane[upper:turn] + middle[g, 0])
        out[g, 0, turn:stop] = gelu(plane[turn:stop] + (second[g, 0] + (low[g, 0] + high[g, 0])))
        base[g, 0, upper:] = plane[stop:] + own[g, 0, upper:]


def finish_kernel(upper, _, base, low, high, out, sent, sem):
    tiles = base.shape[1] // 8
    gap = out.shape[1] // 8 - tiles
    copies = []
    for t in range(tiles):
        rows = pl.ds(8 * t, 8)
        sent[t] = gelu(base[:, rows, :] + (low[:, rows, :] + high[:, rows, :]))
        to = t if t < upper else t + gap
        copies.append(pltpu.make_async_copy(sent.at[t], out.at[:, pl.ds(8 * to, 8), :], sem.at[t]))
        copies[-1].start()
    for copy in copies:
        copy.wait()


def in_hbm(*arrays):
    return [pltpu.with_memory_space_constraint(a, pltpu.HBM) for a in arrays]


def params(limit=VMEM_BYTES):
    return pltpu.CompilerParams(vmem_limit_bytes=limit)


def cost(flops, moved):
    return pl.CostEstimate(flops=flops, bytes_accessed=moved, transcendentals=0)


def whole_block(table):
    return pl.BlockSpec(table.shape, lambda i: (0,) * table.ndim)


def by_four(array):
    return array.reshape(CH // 4, 4, *array.shape[1:])


def forward_call(field, gy, pinned):
    y_local = field.shape[1]
    tables = [*halves(x_table(False)), *halves(y_table(y_local, gy, False))]
    hbm = pl.BlockSpec(memory_space=pltpu.HBM)
    return pl.pallas_call(
        forward_kernel,
        out_shape=(pltpu.HBM if pinned else jax.ShapeDtypeStruct)((CH // 2 * MY, 4 * MX), F32),
        in_specs=[hbm] * 5,
        scratch_shapes=[
            pltpu.VMEM((4, CH // 4, y_local, NX), F32),
            pltpu.VMEM((2, 2, NX, 4 * MX), BF),
            pltpu.VMEM((2, 2 * MY, y_local), BF),
            pltpu.SemaphoreType.DMA((8,)),
        ],
        compiler_params=params(ALL_VMEM_BYTES),
        cost_estimate=cost(10**8, 2**18),
        name="forward_modes",
    )(*in_hbm(by_four(field), *tables))


def filter_call(arrived, gains, gz, gy, scale):
    fwd, inv = z_tables(gz, gy, gains.shape[2], scale)
    fwd, inv = halves(fwd), halves(inv)
    return pl.pallas_call(
        filter_kernel,
        out_shape=pltpu.HBM((arrived.shape[0] // gy, arrived.shape[1]), F32),
        compiler_params=params(),
        cost_estimate=cost(4 * 10**10, 2**18),
        name="filter_modes",
    )(arrived, *in_hbm(gains, *fwd, *inv))


def inverse_call(modes, halved, bias, own, middle, second, pair, upper, y_local, gy, scale):
    tables = [*halves(x_table(True, scale)), *halves(y_table(y_local, gy, True))]
    some = lambda rows: pl.BlockSpec((CH // 4, 1, rows, NX), lambda i: (0, i, 0, 0))
    planes = [*in_hbm(*map(by_four, (own, middle, second))), *map(by_four, pair)]
    rim = own.shape[1]
    result, base = pl.pallas_call(
        functools.partial(inverse_kernel, upper, halved),
        out_shape=[
            jax.ShapeDtypeStruct((CH // 4, 4, y_local, NX), F32),
            jax.ShapeDtypeStruct((CH // 4, 4, rim, NX), F32),
        ],
        grid=(4,),
        in_specs=[
            *[whole_block(m) for m in modes],
            pl.BlockSpec(memory_space=pltpu.SMEM),
            *[whole_block(t) for t in tables],
            *[some(p.shape[2]) for p in planes],
        ],
        out_specs=[some(y_local), some(rim)],
        scratch_shapes=[pltpu.VMEM((2, 2, CH // 4 * y_local, 128), BF)],
        compiler_params=params(),
        cost_estimate=cost(10**8, 2**18),
        name="inverse_modes",
    )(*modes, *in_hbm(bias, *tables), *planes)
    return result.reshape(CH, y_local, NX), base.reshape(CH, rim, NX)


def finish_call(result, base, low, high, upper):
    tiles = base.shape[1] // 8
    anywhere = pl.BlockSpec(memory_space=pl.ANY)
    vmem = pl.BlockSpec(memory_space=pltpu.VMEM)
    return pl.pallas_call(
        functools.partial(finish_kernel, upper),
        out_shape=jax.ShapeDtypeStruct(result.shape, F32),
        in_specs=[anywhere] + [vmem] * 3,
        out_specs=anywhere,
        scratch_shapes=[
            pltpu.VMEM((tiles, CH, 8, NX), F32),
            pltpu.SemaphoreType.DMA((tiles,)),
        ],
        input_output_aliases={0: 0},
        compiler_params=params(),
        cost_estimate=cost(10**8, 2**18),
        name="finished_rows",
    )(result, base, low, high)


def pack_call(field, tiles):
    count = 8 * len(tiles) + 2
    fetched = len(tiles) + 4
    vmem = pl.BlockSpec(memory_space=pltpu.VMEM)
    return pl.pallas_call(
        functools.partial(pack_kernel, tiles),
        out_shape=[jax.ShapeDtypeStruct((count, CH, NX), F32), jax.ShapeDtypeStruct((2, CH, NX), F32)],
        in_specs=[pl.BlockSpec(memory_space=pltpu.HBM)],
        out_specs=[vmem] * 2,
        scratch_shapes=[
            pltpu.VMEM((fetched, 2, CH, 8, 128), F32),
            pltpu.SemaphoreType.DMA((fetched, 2)),
        ],
        compiler_params=params(),
        cost_estimate=cost(10**8, 2**18),
        name="packed_rows",
    )(*in_hbm(field))


def own_call(field, halo, weight, point, segments, groups):
    tiles = sum(map(len, segments))
    rows, fetched = 8 * tiles, tiles + 2 * len(segments)
    hbm = pl.BlockSpec(memory_space=pltpu.HBM)
    shapes = [pltpu.HBM((CH, 8 * len(group), NX), F32) for group in groups for _ in range(3)]
    return pl.pallas_call(
        functools.partial(own_kernel, segments, groups),
        out_shape=shapes,
        in_specs=[hbm] * 3 + [pl.BlockSpec(memory_space=pl.ANY)],
        out_specs=[hbm] * len(shapes),
        scratch_shapes=[
            pltpu.VMEM((fetched, 2, CH, 8, 128), F32),
            pltpu.VMEM((2, CH, NX), F32),
            pltpu.VMEM((CH, 27), F32),
            pltpu.VMEM((CH, CH), F32),
            pltpu.VMEM((3, tiles, CH, 8, NX), F32),
            pltpu.VMEM((rows + 2 * len(segments), CH, NX), F32),
            pltpu.VMEM((3, rows, CH, NX), F32),
            pltpu.VMEM((27, CH, 128), F32),
            pltpu.SemaphoreType.DMA((fetched, 2)),
            pltpu.SemaphoreType.DMA((3, tiles)),
            pltpu.SemaphoreType.DMA((3,)),
        ],
        compiler_params=params(),
        cost_estimate=cost(10**8, 2**18),
        name="own_sums",
    )(*in_hbm(weight, point, field), halo)


def middle_call(weight, point, low, own, high):
    rows = own.shape[0] - 2
    hbm = pl.BlockSpec(memory_space=pltpu.HBM)
    return pl.pallas_call(
        middle_kernel,
        out_shape=pltpu.HBM((CH, rows, NX), F32),
        in_specs=[hbm] * 3 + [pl.BlockSpec(memory_space=pl.ANY), hbm],
        out_specs=hbm,
        scratch_shapes=[
            pltpu.VMEM((3, rows + 2, CH, NX), F32),
            pltpu.VMEM((CH, 27), F32),
            pltpu.VMEM((CH, CH), F32),
            pltpu.VMEM((rows // 8, CH, 8, NX), F32),
            pltpu.VMEM((1, rows, CH, NX), F32),
            pltpu.VMEM((27, CH, 128), F32),
            pltpu.SemaphoreType.DMA((5,)),
            pltpu.SemaphoreType.DMA((rows // 8,)),
        ],
        compiler_params=params(),
        cost_estimate=cost(4 * 10**10, 2**18),
        name="middle_sums",
    )(*in_hbm(weight, point, low), own, *in_hbm(high))


def general_filter(coarse, gains, gz, gy, scale):
    j_own, n_own = gains.shape[2], gains.shape[3]
    both = ("gz", "gy")
    flat = coarse.reshape(CH // 2, MY, 2, 2, MX).transpose(3, 1, 0, 2, 4).reshape(2, MY, CH * MX)
    sent = flat.reshape(2, gy, j_own, gz, n_own).transpose(3, 1, 0, 2, 4).reshape(gz * gy, -1)
    got = lax.all_to_all(sent, both, split_axis=0, concat_axis=0, tiled=True)
    got = got.reshape(gz, gy, 2, j_own, n_own)
    c, s = (jnp.asarray(t, F32) for t in trig(kept(MZ, gz), np.arange(gz), gz))
    mul = functools.partial(jnp.einsum, precision=lax.Precision.HIGHEST)
    whole = got.sum(axis=1) * scale
    real = mul("zjn,qz->qjn", whole[:, 0], c) + mul("zjn,qz->qjn", whole[:, 1], s)
    imag = mul("zjn,qz->qjn", whole[:, 1], c) - mul("zjn,qz->qjn", whole[:, 0], s)
    real, imag = real * gains[0] - imag * gains[1], real * gains[1] + imag * gains[0]
    out = jnp.stack(
        [
            mul("qjn,qz->zjn", real, c) - mul("qjn,qz->zjn", imag, s),
            mul("qjn,qz->zjn", real, s) + mul("qjn,qz->zjn", imag, c),
        ],
        axis=1,
    )
    out = jnp.broadcast_to(out[:, None], (gz, gy, 2, j_own, n_own)).reshape(gz * gy, -1)
    back = lax.all_to_all(out, both, split_axis=0, concat_axis=0, tiled=True)
    back = back.reshape(gz, gy, 2, j_own, n_own).transpose(2, 1, 3, 0, 4)
    back = back.reshape(2, MY, CH // 2, 2, MX)
    return back.transpose(2, 1, 3, 0, 4).reshape(CH // 2, MY, 4 * MX)


def body(field, spectral_filter, depth_weight, point_weight, bias_vector):
    gz, gy = lax.axis_size("gz"), lax.axis_size("gy")
    y_local = field.shape[2]
    field = field.reshape(CH, y_local, NX)
    y_total = gy * y_local
    forward_scale = 1.0 / math.sqrt(float(NX) * y_total * gz)
    inverse_scale = 1.0 / math.sqrt(2.0 * MX * MY * MZ)

    def ring(axis, count, by):
        return [(i, (i + by) % count) for i in range(count)]

    def to_neighbours(across, within):
        odd_on = [(i, (i + 1 if i % 2 else i - 1) % gz) for i in range(gz)]
        even_on = [(i, (i - 1 if i % 2 else i + 1) % gz) for i in range(gz)]
        return lax.ppermute(across, "gz", odd_on), lax.ppermute(within, "gz", even_on)

    def after(value, *others):
        return lax.optimization_barrier((value, *others))[0]

    last = y_local // 8 - 1
    cut = 1 + last // 2
    first_tiles, second_tiles = tuple(range(1, cut)), tuple(range(cut, min(cut + 2, last)))
    third_tiles = (0, *range(second_tiles[-1] + 1, last + 1))
    packed, edges = pack_call(field, first_tiles)
    first_low, first_high = to_neighbours(packed, packed)
    if gy == 2:
        halo = lax.ppermute(edges, "gy", ring("gy", gy, 1))
    else:
        halo = jnp.stack(
            [
                lax.ppermute(edges[0], "gy", ring("gy", gy, 1)),
                lax.ppermute(edges[1], "gy", ring("gy", gy, -1)),
            ]
        )
    j_own, n_own = spectral_filter.shape[2], spectral_filter.shape[3]
    whole_tiles = j_own == 8 and n_own == 2 * MX
    coarse = after(forward_call(after(field, packed), gy, whole_tiles), halo)
    segments, groups = ((0,), tuple(range(cut, last + 1))), (second_tiles, third_tiles)
    down, second, up, outer_down, own, outer_up = own_call(
        after(field, coarse), halo, depth_weight, point_weight, segments, groups
    )
    if whole_tiles:
        both = ("gz", "gy")
        got = lax.all_to_all(coarse, both, split_axis=0, concat_axis=0, tiled=True)
        down, up = lax.optimization_barrier((down, up, first_high))[:2]
        pair = to_neighbours(down, up)
        gains = after(spectral_filter, first_low, first_high, second)
        mark = filter_call(got, gains, gz, gy, forward_scale)
        back = lax.all_to_all(mark, "gz", split_axis=0, concat_axis=0, tiled=True)
    else:
        pair = to_neighbours(down, up)
        mark = general_filter(coarse, spectral_filter, gz, gy, forward_scale)
        modes = [mark[:, part].reshape(-1, 4 * MX) for part in (slice(0, MY // 2), slice(MY // 2, MY))]
    outer_pair = to_neighbours(after(outer_down, mark), after(outer_up, mark))
    packed, *pair = lax.optimization_barrier((packed, *pair))
    mixed = middle_call(depth_weight, point_weight, first_low, packed, first_high)
    if whole_tiles:
        modes = (back, lax.ppermute(after(back, mixed), "gy", ring("gy", gy, 1)))
    result, base = inverse_call(
        modes, whole_tiles, bias_vector, own, mixed, second, pair, 8, y_local, gy, inverse_scale
    )
    result = finish_call(result, base, *outer_pair, 1)
    return result.reshape(CH, 1, y_local, NX)


def solution(mesh):
    in_specs = (P(None, "gz", "gy", None), P(None, None, "gy", "gz"), P(), P(), P())
    out_specs = P(None, "gz", "gy", None)
    return jax.shard_map(body, mesh=mesh, in_specs=in_specs, out_specs=out_specs, check_vma=False)
```

```python
import functools
import math

import jax
import jax.numpy as jnp
import ml_dtypes
import numpy as np
from jax import lax
from jax.experimental import pallas as pl
from jax.experimental.pallas import tpu as pltpu
from jax.sharding import PartitionSpec as P

NX = 256
MX = 32
MY = 16
MZ = 16
CH = 32
VMEM_BYTES = 20 * 1024 * 1024
ALL_VMEM_BYTES = 64000 * 1024
BF = jnp.bfloat16
F32 = jnp.float32


def kept(count, total):
    series = np.arange(count)
    return np.where(series < count // 2, series, total - count + series)


def trig(freqs, places, total):
    angle = 2.0 * np.pi * ((freqs[:, None] * places[None, :]) % total) / total
    return np.cos(angle), np.sin(angle)


def halves(table):
    table = np.asarray(table, np.float64)
    top = table.astype(np.float32).astype(ml_dtypes.bfloat16)
    rest = (table - top.astype(np.float64)).astype(np.float32).astype(ml_dtypes.bfloat16)
    return jnp.asarray(top), jnp.asarray(rest)


def y_table(y_local, gy, inverse):
    out = []
    for g in range(gy):
        places = g * y_local + np.arange(y_local)
        out.append(np.concatenate(trig(kept(MY, y_local * gy), places, y_local * gy), axis=0))
    return np.stack([t.T for t in out] if inverse else out)


def x_table(inverse, scale=1.0):
    c, s = trig(np.arange(MX), np.arange(NX), NX)
    w = np.where(np.arange(MX) == 0, 1.0, 2.0)[:, None] if inverse else 1.0
    out = np.zeros((2, 2, 2, MX, NX))
    for p in range(2):
        out[p, p, 0] = w * c * scale
        out[p, p, 1] = -w * s * scale
    out = out.reshape(2, 4 * MX, NX)
    return out if inverse else out.transpose(0, 2, 1)


def z_tables(gz, gy, rows, scale):
    c, s = trig(kept(MZ, gz), np.arange(gz), gz)
    eye = np.eye(rows)
    both = np.stack([c, s])
    fwd = np.einsum("tqz,g,jk->tqjzgk", both, np.ones(gy), eye) * scale
    inv = np.einsum("tqz,jk->tzjqk", both, eye)
    return fwd.reshape(2 * MZ * rows, gz * gy * rows), inv.reshape(2 * gz * rows, MZ * rows)


def parts(value):
    top = value.astype(BF)
    return top, (value - top.astype(F32)).astype(BF)


def dot(a, b):
    return jnp.dot(a, b, preferred_element_type=F32)


def dot3(a, b):
    rows = a[0].shape[0]
    both = dot(jnp.concatenate([a[0], a[1]], axis=0), b[0])
    return both[:rows] + (both[rows:] + dot(a[0], b[1]))


def swap_parts(value):
    lane = lax.broadcasted_iota(jnp.int32, value.shape, 1)
    is_real = (lane // MX) % 2 == 0
    width = value.shape[1]
    return jnp.where(is_real, pltpu.roll(value, width - MX, 1), pltpu.roll(value, MX, 1)), is_real


def forward_kernel(field, x_top, x_rest, y_top, y_rest, out, taken, x_both, y_both, sem):
    gy = lax.axis_index("gy")
    few = [
        pltpu.make_async_copy(src, dst, sem.at[4 + i])
        for i, (src, dst) in enumerate(
            ((x_top, x_both.at[0]), (x_rest, x_both.at[1]), (y_top.at[gy], y_both.at[0]), (y_rest.at[gy], y_both.at[1]))
        )
    ]
    copies = [pltpu.make_async_copy(field.at[:, q], taken.at[q], sem.at[q]) for q in range(4)]
    for copy in few + copies:
        copy.start()
    for copy in few:
        copy.wait()
    groups, rows = taken.shape[1:3]
    halves_of = []
    for q in range(4):
        copies[q].wait()
        part = dot3(parts(taken[q].reshape(groups * rows, NX)), (x_both[0, q % 2], x_both[1, q % 2]))
        if q % 2:
            halves_of[-1] = halves_of[-1] + part
        else:
            halves_of.append(part)
    total = jnp.concatenate(halves_of, axis=1)
    for g in range(groups):
        both = dot3((y_both[0], y_both[1]), parts(total[g * rows : (g + 1) * rows]))
        crossed, is_real = swap_parts(both[MY:])
        modes = both[:MY] + jnp.where(is_real, crossed, -crossed)
        out[pl.ds(2 * g * MY, MY), :] = modes[:, : 4 * MX]
        out[pl.ds((2 * g + 1) * MY, MY), :] = modes[:, 4 * MX :]


def filter_kernel(arrived, gains, f_top, f_rest, i_top, i_rest, out):
    real, imag = (gains[r].reshape(-1, 2 * MX) for r in range(2))
    first, second = slice(0, MX), slice(MX, 2 * MX)
    same = jnp.concatenate([real[:, first], real[:, first], real[:, second], real[:, second]], axis=1)
    cross = jnp.concatenate([-imag[:, first], imag[:, first], -imag[:, second], imag[:, second]], axis=1)
    half = f_top.shape[0] // 2
    turned = dot3((f_top[...], f_rest[...]), parts(arrived[...]))
    crossed, is_real = swap_parts(turned[half:])
    modes = turned[:half] + jnp.where(is_real, crossed, -crossed)
    crossed, _ = swap_parts(modes)
    filtered = modes * same + crossed * cross
    half = i_top.shape[0] // 2
    back = dot3((i_top[...], i_rest[...]), parts(filtered))
    crossed, is_real = swap_parts(back[half:])
    out[...] = back[:half] + jnp.where(is_real, -crossed, crossed)


def fetch_tiles(field, taken, sems, wanted):
    pending = {}
    for k, t in enumerate(wanted):
        pending[t] = [
            pltpu.make_async_copy(
                field.at[:, pl.ds(8 * t, 8), pl.ds(128 * h, 128)], taken.at[k, h], sems.at[k, h]
            )
            for h in range(2)
        ]
        for copy in pending[t]:
            copy.start()

    def row(t, r):
        for copy in pending.pop(t, ()):
            copy.wait()
        k = wanted.index(t)
        return jnp.concatenate(
            [taken.at[k, h].reshape(CH * 8, 128)[pl.ds(r, CH, stride=8), :] for h in range(2)], axis=1
        )

    return row


def odd_plane():
    return lax.rem(lax.axis_index("gz"), 2) == 1


def spread_gains(weights, gains, swapped):
    for k in range(27):
        column = weights[:, k : k + 1]
        mirror = 18 - 18 * (k // 18) + k % 9
        if k // 9 != 1:
            column = jnp.where(swapped, weights[:, mirror : mirror + 1], column)
        gains[k] = jnp.broadcast_to(column, (CH, 128))


def mixing(points):
    down = (
        lax.broadcasted_iota(jnp.int32, (8 * CH, CH), 0) // 8
        == lax.broadcasted_iota(jnp.int32, (8 * CH, CH), 1)
    ).astype(BF)
    across = (
        lax.broadcasted_iota(jnp.int32, (CH, 8 * CH), 1) % CH
        == lax.broadcasted_iota(jnp.int32, (CH, 8 * CH), 0)
    ).astype(BF)
    same = (
        lax.broadcasted_iota(jnp.int32, (8 * CH, 8 * CH), 0) % 8
        == lax.broadcasted_iota(jnp.int32, (8 * CH, 8 * CH), 1) // CH
    )
    return tuple(
        jnp.where(same, dot(dot(down, part).astype(BF), across), 0.0).astype(BF)
        for part in parts(points)
    )


def tap_sums(load, uses, gains, depth, runs):
    def some(i, _):
        chans = pl.ds(pl.multiple_of(i * 8, 8), 8)
        wanted = sorted({a for use in uses for a, _ in use})
        gain = {k: gains[k, chans, :] for a in wanted for k in range(9 * a, 9 * a + 9)}
        for first, to, rows in runs:
            sums = {}
            for r in range(rows + 2):
                for s, use in enumerate(uses):
                    value = load(s, first + r, chans)
                    turned = (pltpu.roll(value, 1, 1), value, pltpu.roll(value, NX - 1, 1))
                    for b in range(3):
                        o = r - b
                        if o < 0 or o >= rows:
                            continue
                        for a, k in use:
                            for e in range(3):
                                for h in range(2):
                                    term = gain[a * 9 + b * 3 + e] * turned[e][:, 128 * h : 128 * h + 128]
                                    place = (o, k, h)
                                    sums[place] = sums[place] + term if place in sums else term
                if r >= 2:
                    for k in sorted({k for use in uses for _, k in use}):
                        for h in range(2):
                            depth[k, to + r - 2, chans, pl.ds(128 * h, 128)] = sums.pop((r - 2, k, h))
        return 0

    lax.fori_loop(0, CH // 8, some, 0)


def mix_tile(mix, depth, k, t):
    tile = depth[k, pl.ds(8 * t, 8)].reshape(8 * CH, NX)
    return dot3(mix, parts(tile)).reshape(CH, 8, NX)


def pack_kernel(tiles, field, packed, edges, taken, sem_in):
    last = field.shape[1] // 8 - 1
    before, after = tiles[0] - 1, tiles[-1] + 1
    wanted = [before, *tiles, after] + [t for t in (0, last) if t not in (before, after)]
    row = fetch_tiles(field, taken, sem_in, wanted)
    for i, place in enumerate([(before, 7), *[(t, r) for t in tiles for r in range(8)], (after, 0)]):
        packed[i] = row(*place)
    edges[0] = row(last, 7)
    edges[1] = row(0, 0)


def own_kernel(segments, groups, weight, point, field, halo, *refs):
    last = field.shape[1] // 8 - 1
    count = 3 * len(groups)
    outs, (taken, halo_rows, weights, points, sent, lined, depth, gains, sem_in, sem_out, sem_few) = (
        refs[:count],
        refs[count:],
    )
    few = [
        pltpu.make_async_copy(src, dst, sem_few.at[i])
        for i, (src, dst) in enumerate(((weight, weights), (point, points), (halo, halo_rows)))
    ]
    for copy in few:
        copy.start()
    wanted = sorted({t for tiles in segments for t in (tiles[0] - 1, *tiles, tiles[-1] + 1) if 0 <= t <= last})
    row = fetch_tiles(field, taken, sem_in, wanted)
    for copy in few:
        copy.wait()
    spread_gains(weights, gains, jnp.logical_not(odd_plane()))
    mix = mixing(points[...])
    runs, at, done, order = [], 0, 0, []
    for tiles in segments:
        places = [(tiles[0] - 1, 7), *[(t, r) for t in tiles for r in range(8)], (tiles[-1] + 1, 0)]
        for i, (t, r) in enumerate(places):
            lined[at + i] = halo_rows[0] if t < 0 else halo_rows[1] if t > last else row(t, r)
        runs.append((at, done, 8 * len(tiles)))
        at, done = at + len(places), done + 8 * len(tiles)
        order += tiles
    tap_sums(lambda s, r, c: lined[r, c, :], [[(a, a) for a in range(3)]], gains, depth, runs)
    copies = []
    for g, tiles in enumerate(groups):
        for i, tile in enumerate(tiles):
            t = order.index(tile)
            for k in range(3):
                sent[k, t] = mix_tile(mix, depth, k, t)
                to = outs[3 * g + k].at[:, pl.ds(8 * i, 8), :]
                copies.append(pltpu.make_async_copy(sent.at[k, t], to, sem_out.at[k, t]))
                copies[-1].start()
    for copy in copies:
        copy.wait()


def middle_kernel(weight, point, low, own, high, out, taken, weights, points, sent, depth, gains, sem_in, sem_out):
    copies = [
        pltpu.make_async_copy(src, dst, sem_in.at[i])
        for i, (src, dst) in enumerate(
            ((weight, weights), (point, points), (low, taken.at[0]), (own, taken.at[1]), (high, taken.at[2]))
        )
    ]
    for copy in copies:
        copy.start()
    for copy in copies[:2]:
        copy.wait()
    spread_gains(weights, gains, odd_plane())
    mix = mixing(points[...])
    for copy in copies[2:]:
        copy.wait()
    rows = out.shape[1]
    tap_sums(lambda s, r, c: taken[s, r, c, :], [[(a, 0)] for a in range(3)], gains, depth, [(0, 0, rows)])
    copies = []
    for t in range(rows // 8):
        sent[t] = mix_tile(mix, depth, 0, t)
        copies.append(pltpu.make_async_copy(sent.at[t], out.at[:, pl.ds(8 * t, 8), :], sem_out.at[t]))
        copies[-1].start()
    for copy in copies:
        copy.wait()


ERFC = (
    0.17087277, -0.82215223, 1.48851587, -1.13520398, 0.27886807,
    -0.18628806, 0.09678418, 0.37409196, 1.00002368, -1.26551223 - math.log(2.0),
)


def gelu(value):
    size = jnp.abs(value) * math.sqrt(0.5)
    below = 1.0 + 0.5 * size
    t = pl.reciprocal(below, approx=True)
    t = t * (2.0 - below * t)
    series = ERFC[0] * t + ERFC[1]
    for factor in ERFC[2:]:
        series = series * t + factor
    tail = t * jnp.exp(series - size * size)
    return value * jnp.where(value < 0.0, tail, 1.0 - tail)


def inverse_kernel(upper, halved, first_modes, second_modes, bias, x_top, x_rest, y_top, y_rest, own, near, middle, second, low, high, out, base, columns):
    q = pl.program_id(0)
    groups, _, y_local, _ = out.shape

    @pl.when(q == 0)
    def _():
        gy = lax.axis_index("gy")
        for g in range(groups):
            pairs = []
            for pair in (2 * g, 2 * g + 1):
                some = pl.ds(pair * (MY // 2), MY // 2)
                one, two = first_modes[some, :], second_modes[some, :]
                if halved:
                    one, two = jnp.where(gy == 0, one, two), jnp.where(gy == 0, two, one)
                pairs.append(jnp.concatenate([one, two], axis=0))
            own_modes = jnp.concatenate(pairs, axis=1)
            crossed, is_real = swap_parts(own_modes)
            stack = jnp.concatenate([own_modes, jnp.where(is_real, -crossed, crossed)], axis=0)
            pair = parts(dot3((y_top[gy], y_rest[gy]), parts(stack)))
            for h in range(2):
                for k in range(2):
                    columns[h, k, pl.ds(g * y_local, y_local), :] = pair[k][:, 128 * h : 128 * h + 128]

    h, p = q // 2, q % 2
    rows = dot3((columns[h, 0], columns[h, 1]), (x_top[p], x_rest[p]))
    turn = upper + middle.shape[2]
    stop = turn + second.shape[2]
    for g in range(groups):
        plane = rows[g * y_local : (g + 1) * y_local] + bias[4 * g + q]
        rim = own[g, 0] + near[g, 0]
        base[g, 0, :upper] = plane[:upper] + rim[:upper]
        out[g, 0, upper:turn] = gelu(plane[upper:turn] + middle[g, 0])
        out[g, 0, turn:stop] = gelu(plane[turn:stop] + (second[g, 0] + (low[g, 0] + high[g, 0])))
        base[g, 0, upper:] = plane[stop:] + rim[upper:]


def finish_kernel(upper, _, base, across, out, sent, sem):
    tiles = base.shape[1] // 8
    gap = out.shape[1] // 8 - tiles
    copies = []
    for t in range(tiles):
        rows = pl.ds(8 * t, 8)
        sent[t] = gelu(base[:, rows, :] + across[:, rows, :])
        to = t if t < upper else t + gap
        copies.append(pltpu.make_async_copy(sent.at[t], out.at[:, pl.ds(8 * to, 8), :], sem.at[t]))
        copies[-1].start()
    for copy in copies:
        copy.wait()


def in_hbm(*arrays):
    return [pltpu.with_memory_space_constraint(a, pltpu.HBM) for a in arrays]


def params(limit=VMEM_BYTES):
    return pltpu.CompilerParams(vmem_limit_bytes=limit)


def cost(flops, moved):
    return pl.CostEstimate(flops=flops, bytes_accessed=moved, transcendentals=0)


def whole_block(table):
    return pl.BlockSpec(table.shape, lambda i: (0,) * table.ndim)


def by_four(array):
    return array.reshape(CH // 4, 4, *array.shape[1:])


def forward_call(field, gy, pinned):
    y_local = field.shape[1]
    tables = [*halves(x_table(False)), *halves(y_table(y_local, gy, False))]
    hbm = pl.BlockSpec(memory_space=pltpu.HBM)
    return pl.pallas_call(
        forward_kernel,
        out_shape=(pltpu.HBM if pinned else jax.ShapeDtypeStruct)((CH // 2 * MY, 4 * MX), F32),
        in_specs=[hbm] * 5,
        scratch_shapes=[
            pltpu.VMEM((4, CH // 4, y_local, NX), F32),
            pltpu.VMEM((2, 2, NX, 4 * MX), BF),
            pltpu.VMEM((2, 2 * MY, y_local), BF),
            pltpu.SemaphoreType.DMA((8,)),
        ],
        compiler_params=params(ALL_VMEM_BYTES),
        cost_estimate=cost(10**8, 2**18),
        name="forward_modes",
    )(*in_hbm(by_four(field), *tables))


def filter_call(arrived, gains, gz, gy, scale):
    fwd, inv = z_tables(gz, gy, gains.shape[2], scale)
    fwd, inv = halves(fwd), halves(inv)
    return pl.pallas_call(
        filter_kernel,
        out_shape=pltpu.HBM((arrived.shape[0] // gy, arrived.shape[1]), F32),
        compiler_params=params(),
        cost_estimate=cost(4 * 10**10, 2**18),
        name="filter_modes",
    )(arrived, *in_hbm(gains, *fwd, *inv))


def inverse_call(modes, halved, bias, own, near, middle, second, pair, upper, y_local, gy, scale):
    tables = [*halves(x_table(True, scale)), *halves(y_table(y_local, gy, True))]
    some = lambda rows: pl.BlockSpec((CH // 4, 1, rows, NX), lambda i: (0, i, 0, 0))
    planes = [*in_hbm(by_four(own)), by_four(near), *in_hbm(*map(by_four, (middle, second))), *map(by_four, pair)]
    rim = own.shape[1]
    result, base = pl.pallas_call(
        functools.partial(inverse_kernel, upper, halved),
        out_shape=[
            jax.ShapeDtypeStruct((CH // 4, 4, y_local, NX), F32),
            jax.ShapeDtypeStruct((CH // 4, 4, rim, NX), F32),
        ],
        grid=(4,),
        in_specs=[
            *[whole_block(m) for m in modes],
            pl.BlockSpec(memory_space=pltpu.SMEM),
            *[whole_block(t) for t in tables],
            *[some(p.shape[2]) for p in planes],
        ],
        out_specs=[some(y_local), some(rim)],
        scratch_shapes=[pltpu.VMEM((2, 2, CH // 4 * y_local, 128), BF)],
        compiler_params=params(),
        cost_estimate=cost(10**8, 2**18),
        name="inverse_modes",
    )(*modes, *in_hbm(bias, *tables), *planes)
    return result.reshape(CH, y_local, NX), base.reshape(CH, rim, NX)


def finish_call(result, base, across, upper):
    tiles = base.shape[1] // 8
    anywhere = pl.BlockSpec(memory_space=pl.ANY)
    vmem = pl.BlockSpec(memory_space=pltpu.VMEM)
    return pl.pallas_call(
        functools.partial(finish_kernel, upper),
        out_shape=jax.ShapeDtypeStruct(result.shape, F32),
        in_specs=[anywhere] + [vmem] * 2,
        out_specs=anywhere,
        scratch_shapes=[
            pltpu.VMEM((tiles, CH, 8, NX), F32),
            pltpu.SemaphoreType.DMA((tiles,)),
        ],
        input_output_aliases={0: 0},
        compiler_params=params(),
        cost_estimate=cost(10**8, 2**18),
        name="finished_rows",
    )(result, base, across)


def pack_call(field, tiles):
    count = 8 * len(tiles) + 2
    fetched = len(tiles) + 4
    vmem = pl.BlockSpec(memory_space=pltpu.VMEM)
    return pl.pallas_call(
        functools.partial(pack_kernel, tiles),
        out_shape=[jax.ShapeDtypeStruct((count, CH, NX), F32), jax.ShapeDtypeStruct((2, CH, NX), F32)],
        in_specs=[pl.BlockSpec(memory_space=pltpu.HBM)],
        out_specs=[vmem] * 2,
        scratch_shapes=[
            pltpu.VMEM((fetched, 2, CH, 8, 128), F32),
            pltpu.SemaphoreType.DMA((fetched, 2)),
        ],
        compiler_params=params(),
        cost_estimate=cost(10**8, 2**18),
        name="packed_rows",
    )(*in_hbm(field))


def own_call(field, halo, weight, point, segments, groups):
    tiles = sum(map(len, segments))
    rows, fetched = 8 * tiles, tiles + 2 * len(segments)
    hbm = pl.BlockSpec(memory_space=pltpu.HBM)
    shapes = [pltpu.HBM((CH, 8 * len(group), NX), F32) for group in groups for _ in range(3)]
    return pl.pallas_call(
        functools.partial(own_kernel, segments, groups),
        out_shape=shapes,
        in_specs=[hbm] * 3 + [pl.BlockSpec(memory_space=pl.ANY)],
        out_specs=[hbm] * len(shapes),
        scratch_shapes=[
            pltpu.VMEM((fetched, 2, CH, 8, 128), F32),
            pltpu.VMEM((2, CH, NX), F32),
            pltpu.VMEM((CH, 27), F32),
            pltpu.VMEM((CH, CH), F32),
            pltpu.VMEM((3, tiles, CH, 8, NX), F32),
            pltpu.VMEM((rows + 2 * len(segments), CH, NX), F32),
            pltpu.VMEM((3, rows, CH, NX), F32),
            pltpu.VMEM((27, CH, 128), F32),
            pltpu.SemaphoreType.DMA((fetched, 2)),
            pltpu.SemaphoreType.DMA((3, tiles)),
            pltpu.SemaphoreType.DMA((3,)),
        ],
        compiler_params=params(),
        cost_estimate=cost(10**8, 2**18),
        name="own_sums",
    )(*in_hbm(weight, point, field), halo)


def middle_call(weight, point, low, own, high):
    rows = own.shape[0] - 2
    hbm = pl.BlockSpec(memory_space=pltpu.HBM)
    return pl.pallas_call(
        middle_kernel,
        out_shape=pltpu.HBM((CH, rows, NX), F32),
        in_specs=[hbm] * 3 + [pl.BlockSpec(memory_space=pl.ANY), hbm],
        out_specs=hbm,
        scratch_shapes=[
            pltpu.VMEM((3, rows + 2, CH, NX), F32),
            pltpu.VMEM((CH, 27), F32),
            pltpu.VMEM((CH, CH), F32),
            pltpu.VMEM((rows // 8, CH, 8, NX), F32),
            pltpu.VMEM((1, rows, CH, NX), F32),
            pltpu.VMEM((27, CH, 128), F32),
            pltpu.SemaphoreType.DMA((5,)),
            pltpu.SemaphoreType.DMA((rows // 8,)),
        ],
        compiler_params=params(),
        cost_estimate=cost(4 * 10**10, 2**18),
        name="middle_sums",
    )(*in_hbm(weight, point, low), own, *in_hbm(high))


def general_filter(coarse, gains, gz, gy, scale):
    j_own, n_own = gains.shape[2], gains.shape[3]
    both = ("gz", "gy")
    flat = coarse.reshape(CH // 2, MY, 2, 2, MX).transpose(3, 1, 0, 2, 4).reshape(2, MY, CH * MX)
    sent = flat.reshape(2, gy, j_own, gz, n_own).transpose(3, 1, 0, 2, 4).reshape(gz * gy, -1)
    got = lax.all_to_all(sent, both, split_axis=0, concat_axis=0, tiled=True)
    got = got.reshape(gz, gy, 2, j_own, n_own)
    c, s = (jnp.asarray(t, F32) for t in trig(kept(MZ, gz), np.arange(gz), gz))
    mul = functools.partial(jnp.einsum, precision=lax.Precision.HIGHEST)
    whole = got.sum(axis=1) * scale
    real = mul("zjn,qz->qjn", whole[:, 0], c) + mul("zjn,qz->qjn", whole[:, 1], s)
    imag = mul("zjn,qz->qjn", whole[:, 1], c) - mul("zjn,qz->qjn", whole[:, 0], s)
    real, imag = real * gains[0] - imag * gains[1], real * gains[1] + imag * gains[0]
    out = jnp.stack(
        [
            mul("qjn,qz->zjn", real, c) - mul("qjn,qz->zjn", imag, s),
            mul("qjn,qz->zjn", real, s) + mul("qjn,qz->zjn", imag, c),
        ],
        axis=1,
    )
    out = jnp.broadcast_to(out[:, None], (gz, gy, 2, j_own, n_own)).reshape(gz * gy, -1)
    back = lax.all_to_all(out, both, split_axis=0, concat_axis=0, tiled=True)
    back = back.reshape(gz, gy, 2, j_own, n_own).transpose(2, 1, 3, 0, 4)
    back = back.reshape(2, MY, CH // 2, 2, MX)
    return back.transpose(2, 1, 3, 0, 4).reshape(CH // 2, MY, 4 * MX)


def body(field, spectral_filter, depth_weight, point_weight, bias_vector):
    gz, gy = lax.axis_size("gz"), lax.axis_size("gy")
    y_local = field.shape[2]
    field = field.reshape(CH, y_local, NX)
    y_total = gy * y_local
    forward_scale = 1.0 / math.sqrt(float(NX) * y_total * gz)
    inverse_scale = 1.0 / math.sqrt(2.0 * MX * MY * MZ)

    def ring(axis, count, by):
        return [(i, (i + by) % count) for i in range(count)]

    def to_neighbours(across, within):
        odd_on = [(i, (i + 1 if i % 2 else i - 1) % gz) for i in range(gz)]
        even_on = [(i, (i - 1 if i % 2 else i + 1) % gz) for i in range(gz)]
        return lax.ppermute(across, "gz", odd_on), lax.ppermute(within, "gz", even_on)

    def after(value, *others):
        return lax.optimization_barrier((value, *others))[0]

    last = y_local // 8 - 1
    cut = 1 + last // 2
    first_tiles, second_tiles = tuple(range(1, cut)), tuple(range(cut, min(cut + 2, last)))
    third_tiles = (0, *range(second_tiles[-1] + 1, last + 1))
    packed, edges = pack_call(field, first_tiles)
    first_low, first_high = to_neighbours(packed, packed)
    if gy == 2:
        halo = lax.ppermute(edges, "gy", ring("gy", gy, 1))
    else:
        halo = jnp.stack(
            [
                lax.ppermute(edges[0], "gy", ring("gy", gy, 1)),
                lax.ppermute(edges[1], "gy", ring("gy", gy, -1)),
            ]
        )
    j_own, n_own = spectral_filter.shape[2], spectral_filter.shape[3]
    whole_tiles = j_own == 8 and n_own == 2 * MX
    coarse = after(forward_call(after(field, packed), gy, whole_tiles), halo)
    segments, groups = ((0,), tuple(range(cut, last + 1))), (second_tiles, third_tiles)
    down, second, up, outer_down, own, outer_up = own_call(
        after(field, coarse), halo, depth_weight, point_weight, segments, groups
    )
    if whole_tiles:
        both = ("gz", "gy")
        got = lax.all_to_all(coarse, both, split_axis=0, concat_axis=0, tiled=True)
        down, up = lax.optimization_barrier((down, up, first_low))[:2]
        pair = to_neighbours(down, up)
        gains = after(spectral_filter, first_low, first_high, second)
        mark = filter_call(got, gains, gz, gy, forward_scale)
        back = lax.all_to_all(mark, "gz", split_axis=0, concat_axis=0, tiled=True)
    else:
        pair = to_neighbours(down, up)
        mark = general_filter(coarse, spectral_filter, gz, gy, forward_scale)
        modes = [mark[:, part].reshape(-1, 4 * MX) for part in (slice(0, MY // 2), slice(MY // 2, MY))]
    outer_pair = to_neighbours(after(outer_down, mark), after(outer_up, mark))
    packed, *pair = lax.optimization_barrier((packed, *pair))
    mixed = middle_call(depth_weight, point_weight, first_low, packed, first_high)
    if whole_tiles:
        modes = (back, lax.ppermute(after(back, mixed), "gy", ring("gy", gy, 1)))
    result, base = inverse_call(
        modes, whole_tiles, bias_vector, own, outer_pair[1], mixed, second, pair, 8, y_local, gy, inverse_scale
    )
    result = finish_call(result, base, outer_pair[0], 1)
    return result.reshape(CH, 1, y_local, NX)


def solution(mesh):
    in_specs = (P(None, "gz", "gy", None), P(None, None, "gy", "gz"), P(), P(), P())
    out_specs = P(None, "gz", "gy", None)
    return jax.shard_map(body, mesh=mesh, in_specs=in_specs, out_specs=out_specs, check_vma=False)
```

```python
import functools
import math

import jax
import jax.numpy as jnp
import ml_dtypes
import numpy as np
from jax import lax
from jax.experimental import pallas as pl
from jax.experimental.pallas import tpu as pltpu
from jax.sharding import PartitionSpec as P

NX = 256
MX = 32
MY = 16
MZ = 16
CH = 32
VMEM_BYTES = 20 * 1024 * 1024
ALL_VMEM_BYTES = 64000 * 1024
BF = jnp.bfloat16
F32 = jnp.float32


def kept(count, total):
    series = np.arange(count)
    return np.where(series < count // 2, series, total - count + series)


def trig(freqs, places, total):
    angle = 2.0 * np.pi * ((freqs[:, None] * places[None, :]) % total) / total
    return np.cos(angle), np.sin(angle)


def halves(table):
    table = np.asarray(table, np.float64)
    top = table.astype(np.float32).astype(ml_dtypes.bfloat16)
    rest = (table - top.astype(np.float64)).astype(np.float32).astype(ml_dtypes.bfloat16)
    return jnp.asarray(top), jnp.asarray(rest)


def y_table(y_local, gy, inverse):
    out = []
    for g in range(gy):
        places = g * y_local + np.arange(y_local)
        out.append(np.concatenate(trig(kept(MY, y_local * gy), places, y_local * gy), axis=0))
    return np.stack([t.T for t in out] if inverse else out)


def x_table(inverse, scale=1.0):
    c, s = trig(np.arange(MX), np.arange(NX), NX)
    w = np.where(np.arange(MX) == 0, 1.0, 2.0)[:, None] if inverse else 1.0
    out = np.zeros((2, 2, 2, MX, NX))
    for p in range(2):
        out[p, p, 0] = w * c * scale
        out[p, p, 1] = -w * s * scale
    out = out.reshape(2, 4 * MX, NX)
    return out if inverse else out.transpose(0, 2, 1)


def z_tables(gz, gy, rows, scale):
    c, s = trig(kept(MZ, gz), np.arange(gz), gz)
    eye = np.eye(rows)
    both = np.stack([c, s])
    fwd = np.einsum("tqz,g,jk->tqjzgk", both, np.ones(gy), eye) * scale
    inv = np.einsum("tqz,jk->tzjqk", both, eye)
    return fwd.reshape(2 * MZ * rows, gz * gy * rows), inv.reshape(2 * gz * rows, MZ * rows)


def parts(value):
    top = value.astype(BF)
    return top, (value - top.astype(F32)).astype(BF)


def dot(a, b):
    return jnp.dot(a, b, preferred_element_type=F32)


def dot3(a, b):
    rows = a[0].shape[0]
    both = dot(jnp.concatenate([a[0], a[1]], axis=0), b[0])
    return both[:rows] + (both[rows:] + dot(a[0], b[1]))


def swap_parts(value):
    lane = lax.broadcasted_iota(jnp.int32, value.shape, 1)
    is_real = (lane // MX) % 2 == 0
    width = value.shape[1]
    return jnp.where(is_real, pltpu.roll(value, width - MX, 1), pltpu.roll(value, MX, 1)), is_real


def forward_kernel(field, x_top, x_rest, y_top, y_rest, out, taken, x_both, y_both, sem):
    gy = lax.axis_index("gy")
    few = [
        pltpu.make_async_copy(src, dst, sem.at[4 + i])
        for i, (src, dst) in enumerate(
            ((x_top, x_both.at[0]), (x_rest, x_both.at[1]), (y_top.at[gy], y_both.at[0]), (y_rest.at[gy], y_both.at[1]))
        )
    ]
    copies = [pltpu.make_async_copy(field.at[:, q], taken.at[q], sem.at[q]) for q in range(4)]
    for copy in few + copies:
        copy.start()
    for copy in few:
        copy.wait()
    groups, rows = taken.shape[1:3]
    halves_of = []
    for q in range(4):
        copies[q].wait()
        part = dot3(parts(taken[q].reshape(groups * rows, NX)), (x_both[0, q % 2], x_both[1, q % 2]))
        if q % 2:
            halves_of[-1] = halves_of[-1] + part
        else:
            halves_of.append(part)
    total = jnp.concatenate(halves_of, axis=1)
    for g in range(groups):
        both = dot3((y_both[0], y_both[1]), parts(total[g * rows : (g + 1) * rows]))
        crossed, is_real = swap_parts(both[MY:])
        modes = both[:MY] + jnp.where(is_real, crossed, -crossed)
        out[pl.ds(2 * g * MY, MY), :] = modes[:, : 4 * MX]
        out[pl.ds((2 * g + 1) * MY, MY), :] = modes[:, 4 * MX :]


def filter_kernel(arrived, gains, f_top, f_rest, i_top, i_rest, out):
    real, imag = (gains[r].reshape(-1, 2 * MX) for r in range(2))
    first, second = slice(0, MX), slice(MX, 2 * MX)
    same = jnp.concatenate([real[:, first], real[:, first], real[:, second], real[:, second]], axis=1)
    cross = jnp.concatenate([-imag[:, first], imag[:, first], -imag[:, second], imag[:, second]], axis=1)
    half = f_top.shape[0] // 2
    turned = dot3((f_top[...], f_rest[...]), parts(arrived[...]))
    crossed, is_real = swap_parts(turned[half:])
    modes = turned[:half] + jnp.where(is_real, crossed, -crossed)
    crossed, _ = swap_parts(modes)
    filtered = modes * same + crossed * cross
    half = i_top.shape[0] // 2
    back = dot3((i_top[...], i_rest[...]), parts(filtered))
    crossed, is_real = swap_parts(back[half:])
    out[...] = back[:half] + jnp.where(is_real, -crossed, crossed)


def fetch_tiles(field, taken, sems, wanted):
    pending = {}
    for k, t in enumerate(wanted):
        pending[t] = [
            pltpu.make_async_copy(
                field.at[:, pl.ds(8 * t, 8), pl.ds(128 * h, 128)], taken.at[k, h], sems.at[k, h]
            )
            for h in range(2)
        ]
        for copy in pending[t]:
            copy.start()

    def row(t, r):
        for copy in pending.pop(t, ()):
            copy.wait()
        k = wanted.index(t)
        return jnp.concatenate(
            [taken.at[k, h].reshape(CH * 8, 128)[pl.ds(r, CH, stride=8), :] for h in range(2)], axis=1
        )

    return row


def odd_plane():
    return lax.rem(lax.axis_index("gz"), 2) == 1


def spread_gains(weights, gains, swapped):
    for k in range(27):
        column = weights[:, k : k + 1]
        mirror = 18 - 18 * (k // 18) + k % 9
        if k // 9 != 1:
            column = jnp.where(swapped, weights[:, mirror : mirror + 1], column)
        gains[k] = jnp.broadcast_to(column, (CH, 128))


def mixing(points):
    down = (
        lax.broadcasted_iota(jnp.int32, (8 * CH, CH), 0) // 8
        == lax.broadcasted_iota(jnp.int32, (8 * CH, CH), 1)
    ).astype(BF)
    across = (
        lax.broadcasted_iota(jnp.int32, (CH, 8 * CH), 1) % CH
        == lax.broadcasted_iota(jnp.int32, (CH, 8 * CH), 0)
    ).astype(BF)
    same = (
        lax.broadcasted_iota(jnp.int32, (8 * CH, 8 * CH), 0) % 8
        == lax.broadcasted_iota(jnp.int32, (8 * CH, 8 * CH), 1) // CH
    )
    return tuple(
        jnp.where(same, dot(dot(down, part).astype(BF), across), 0.0).astype(BF)
        for part in parts(points)
    )


def tap_sums(load, uses, gains, depth, runs):
    def some(i, _):
        chans = pl.ds(pl.multiple_of(i * 8, 8), 8)
        wanted = sorted({a for use in uses for a, _ in use})
        gain = {k: gains[k, chans, :] for a in wanted for k in range(9 * a, 9 * a + 9)}
        for first, to, rows in runs:
            sums = {}
            for r in range(rows + 2):
                for s, use in enumerate(uses):
                    value = load(s, first + r, chans)
                    turned = (pltpu.roll(value, 1, 1), value, pltpu.roll(value, NX - 1, 1))
                    for b in range(3):
                        o = r - b
                        if o < 0 or o >= rows:
                            continue
                        for a, k in use:
                            for e in range(3):
                                for h in range(2):
                                    term = gain[a * 9 + b * 3 + e] * turned[e][:, 128 * h : 128 * h + 128]
                                    place = (o, k, h)
                                    sums[place] = sums[place] + term if place in sums else term
                if r >= 2:
                    for k in sorted({k for use in uses for _, k in use}):
                        for h in range(2):
                            depth[k, to + r - 2, chans, pl.ds(128 * h, 128)] = sums.pop((r - 2, k, h))
        return 0

    lax.fori_loop(0, CH // 8, some, 0)


def mix_tile(mix, depth, k, t):
    tile = depth[k, pl.ds(8 * t, 8)].reshape(8 * CH, NX)
    return dot3(mix, parts(tile)).reshape(CH, 8, NX)


def pack_kernel(tiles, field, packed, edges, taken, sem_in):
    last = field.shape[1] // 8 - 1
    before, after = tiles[0] - 1, tiles[-1] + 1
    wanted = [before, *tiles, after] + [t for t in (0, last) if t not in (before, after)]
    row = fetch_tiles(field, taken, sem_in, wanted)
    for i, place in enumerate([(before, 7), *[(t, r) for t in tiles for r in range(8)], (after, 0)]):
        packed[i] = row(*place)
    edges[0] = row(last, 7)
    edges[1] = row(0, 0)


def own_kernel(segments, groups, weight, point, field, halo, *refs):
    last = field.shape[1] // 8 - 1
    count = 3 * len(groups)
    outs, (taken, halo_rows, weights, points, sent, lined, depth, gains, sem_in, sem_out, sem_few) = (
        refs[:count],
        refs[count:],
    )
    few = [
        pltpu.make_async_copy(src, dst, sem_few.at[i])
        for i, (src, dst) in enumerate(((weight, weights), (point, points), (halo, halo_rows)))
    ]
    for copy in few:
        copy.start()
    wanted = sorted({t for tiles in segments for t in (tiles[0] - 1, *tiles, tiles[-1] + 1) if 0 <= t <= last})
    row = fetch_tiles(field, taken, sem_in, wanted)
    for copy in few:
        copy.wait()
    spread_gains(weights, gains, jnp.logical_not(odd_plane()))
    mix = mixing(points[...])
    runs, at, done, order = [], 0, 0, []
    for tiles in segments:
        places = [(tiles[0] - 1, 7), *[(t, r) for t in tiles for r in range(8)], (tiles[-1] + 1, 0)]
        for i, (t, r) in enumerate(places):
            lined[at + i] = halo_rows[0] if t < 0 else halo_rows[1] if t > last else row(t, r)
        runs.append((at, done, 8 * len(tiles)))
        at, done = at + len(places), done + 8 * len(tiles)
        order += tiles
    tap_sums(lambda s, r, c: lined[r, c, :], [[(a, a) for a in range(3)]], gains, depth, runs)
    copies = []
    for g, tiles in enumerate(groups):
        for i, tile in enumerate(tiles):
            t = order.index(tile)
            for k in range(3):
                sent[k, t] = mix_tile(mix, depth, k, t)
                to = outs[3 * g + k].at[:, pl.ds(8 * i, 8), :]
                copies.append(pltpu.make_async_copy(sent.at[k, t], to, sem_out.at[k, t]))
                copies[-1].start()
    for copy in copies:
        copy.wait()


def middle_kernel(weight, point, low, own, high, out, taken, weights, points, sent, depth, gains, sem_in, sem_out):
    copies = [
        pltpu.make_async_copy(src, dst, sem_in.at[i])
        for i, (src, dst) in enumerate(
            ((weight, weights), (point, points), (low, taken.at[0]), (own, taken.at[1]), (high, taken.at[2]))
        )
    ]
    for copy in copies:
        copy.start()
    for copy in copies[:2]:
        copy.wait()
    spread_gains(weights, gains, odd_plane())
    mix = mixing(points[...])
    for copy in copies[2:]:
        copy.wait()
    rows = out.shape[1]
    tap_sums(lambda s, r, c: taken[s, r, c, :], [[(a, 0)] for a in range(3)], gains, depth, [(0, 0, rows)])
    copies = []
    for t in range(rows // 8):
        sent[t] = mix_tile(mix, depth, 0, t)
        copies.append(pltpu.make_async_copy(sent.at[t], out.at[:, pl.ds(8 * t, 8), :], sem_out.at[t]))
        copies[-1].start()
    for copy in copies:
        copy.wait()


ERFC = (
    0.17087277, -0.82215223, 1.48851587, -1.13520398, 0.27886807,
    -0.18628806, 0.09678418, 0.37409196, 1.00002368, -1.26551223 - math.log(2.0),
)


def gelu(value):
    size = jnp.abs(value) * math.sqrt(0.5)
    below = 1.0 + 0.5 * size
    t = pl.reciprocal(below, approx=True)
    t = t * (2.0 - below * t)
    series = ERFC[0] * t + ERFC[1]
    for factor in ERFC[2:]:
        series = series * t + factor
    tail = t * jnp.exp(series - size * size)
    return value * jnp.where(value < 0.0, tail, 1.0 - tail)


def inverse_kernel(upper, halved, first_modes, second_modes, bias, x_top, x_rest, y_top, y_rest, own, near, middle, second, low, high, out, base, columns):
    q = pl.program_id(0)
    groups, _, y_local, _ = out.shape

    @pl.when(q == 0)
    def _():
        gy = lax.axis_index("gy")
        for g in range(groups):
            pairs = []
            for pair in (2 * g, 2 * g + 1):
                some = pl.ds(pair * (MY // 2), MY // 2)
                one, two = first_modes[some, :], second_modes[some, :]
                if halved:
                    one, two = jnp.where(gy == 0, one, two), jnp.where(gy == 0, two, one)
                pairs.append(jnp.concatenate([one, two], axis=0))
            own_modes = jnp.concatenate(pairs, axis=1)
            crossed, is_real = swap_parts(own_modes)
            stack = jnp.concatenate([own_modes, jnp.where(is_real, -crossed, crossed)], axis=0)
            pair = parts(dot3((y_top[gy], y_rest[gy]), parts(stack)))
            for h in range(2):
                for k in range(2):
                    columns[h, k, pl.ds(g * y_local, y_local), :] = pair[k][:, 128 * h : 128 * h + 128]

    h, p = q // 2, q % 2
    rows = dot3((columns[h, 0], columns[h, 1]), (x_top[p], x_rest[p]))
    turn = upper + middle.shape[2]
    stop = turn + second.shape[2]
    for g in range(groups):
        plane = rows[g * y_local : (g + 1) * y_local] + bias[4 * g + q]
        rim = own[g, 0] + near[g, 0]
        base[g, 0, :upper] = plane[:upper] + rim[:upper]
        out[g, 0, upper:turn] = gelu(plane[upper:turn] + middle[g, 0])
        out[g, 0, turn:stop] = gelu(plane[turn:stop] + (second[g, 0] + (low[g, 0] + high[g, 0])))
        base[g, 0, upper:] = plane[stop:] + rim[upper:]


def finish_kernel(upper, _, base, across, out, sent, sem):
    tiles = base.shape[1] // 8
    gap = out.shape[1] // 8 - tiles
    copies = []
    for t in range(tiles):
        rows = pl.ds(8 * t, 8)
        to = t if t < upper else t + gap
        for h in range(2):
            half = pl.ds(h * (CH // 2), CH // 2)
            sent[t, half] = gelu(base[half, rows, :] + across[half, rows, :])
            copies.append(
                pltpu.make_async_copy(sent.at[t, half], out.at[half, pl.ds(8 * to, 8), :], sem.at[t, h])
            )
            copies[-1].start()
    for copy in copies:
        copy.wait()


def in_hbm(*arrays):
    return [pltpu.with_memory_space_constraint(a, pltpu.HBM) for a in arrays]


def params(limit=VMEM_BYTES):
    return pltpu.CompilerParams(vmem_limit_bytes=limit)


def cost(flops, moved):
    return pl.CostEstimate(flops=flops, bytes_accessed=moved, transcendentals=0)


def whole_block(table):
    return pl.BlockSpec(table.shape, lambda i: (0,) * table.ndim)


def by_four(array):
    return array.reshape(CH // 4, 4, *array.shape[1:])


def forward_call(field, gy, pinned):
    y_local = field.shape[1]
    tables = [*halves(x_table(False)), *halves(y_table(y_local, gy, False))]
    hbm = pl.BlockSpec(memory_space=pltpu.HBM)
    return pl.pallas_call(
        forward_kernel,
        out_shape=(pltpu.HBM if pinned else jax.ShapeDtypeStruct)((CH // 2 * MY, 4 * MX), F32),
        in_specs=[hbm] * 5,
        scratch_shapes=[
            pltpu.VMEM((4, CH // 4, y_local, NX), F32),
            pltpu.VMEM((2, 2, NX, 4 * MX), BF),
            pltpu.VMEM((2, 2 * MY, y_local), BF),
            pltpu.SemaphoreType.DMA((8,)),
        ],
        compiler_params=params(ALL_VMEM_BYTES),
        cost_estimate=cost(10**8, 2**18),
        name="forward_modes",
    )(*in_hbm(by_four(field), *tables))


def filter_call(arrived, gains, gz, gy, scale):
    fwd, inv = z_tables(gz, gy, gains.shape[2], scale)
    fwd, inv = halves(fwd), halves(inv)
    return pl.pallas_call(
        filter_kernel,
        out_shape=pltpu.HBM((arrived.shape[0] // gy, arrived.shape[1]), F32),
        compiler_params=params(),
        cost_estimate=cost(4 * 10**10, 2**18),
        name="filter_modes",
    )(arrived, *in_hbm(gains, *fwd, *inv))


def inverse_call(modes, halved, bias, own, near, middle, second, pair, upper, y_local, gy, scale):
    tables = [*halves(x_table(True, scale)), *halves(y_table(y_local, gy, True))]
    some = lambda rows: pl.BlockSpec((CH // 4, 1, rows, NX), lambda i: (0, i, 0, 0))
    planes = [*in_hbm(by_four(own)), by_four(near), *in_hbm(*map(by_four, (middle, second))), *map(by_four, pair)]
    rim = own.shape[1]
    result, base = pl.pallas_call(
        functools.partial(inverse_kernel, upper, halved),
        out_shape=[
            jax.ShapeDtypeStruct((CH // 4, 4, y_local, NX), F32),
            jax.ShapeDtypeStruct((CH // 4, 4, rim, NX), F32),
        ],
        grid=(4,),
        in_specs=[
            *[whole_block(m) for m in modes],
            pl.BlockSpec(memory_space=pltpu.SMEM),
            *[whole_block(t) for t in tables],
            *[some(p.shape[2]) for p in planes],
        ],
        out_specs=[some(y_local), some(rim)],
        scratch_shapes=[pltpu.VMEM((2, 2, CH // 4 * y_local, 128), BF)],
        compiler_params=params(),
        cost_estimate=cost(10**8, 2**18),
        name="inverse_modes",
    )(*modes, *in_hbm(bias, *tables), *planes)
    return result.reshape(CH, y_local, NX), base.reshape(CH, rim, NX)


def finish_call(result, base, across, upper):
    tiles = base.shape[1] // 8
    anywhere = pl.BlockSpec(memory_space=pl.ANY)
    vmem = pl.BlockSpec(memory_space=pltpu.VMEM)
    return pl.pallas_call(
        functools.partial(finish_kernel, upper),
        out_shape=jax.ShapeDtypeStruct(result.shape, F32),
        in_specs=[anywhere] + [vmem] * 2,
        out_specs=anywhere,
        scratch_shapes=[
            pltpu.VMEM((tiles, CH, 8, NX), F32),
            pltpu.SemaphoreType.DMA((tiles, 2)),
        ],
        input_output_aliases={0: 0},
        compiler_params=params(),
        cost_estimate=cost(10**8, 2**18),
        name="finished_rows",
    )(result, base, across)


def pack_call(field, tiles):
    count = 8 * len(tiles) + 2
    fetched = len(tiles) + 4
    vmem = pl.BlockSpec(memory_space=pltpu.VMEM)
    return pl.pallas_call(
        functools.partial(pack_kernel, tiles),
        out_shape=[jax.ShapeDtypeStruct((count, CH, NX), F32), jax.ShapeDtypeStruct((2, CH, NX), F32)],
        in_specs=[pl.BlockSpec(memory_space=pltpu.HBM)],
        out_specs=[vmem] * 2,
        scratch_shapes=[
            pltpu.VMEM((fetched, 2, CH, 8, 128), F32),
            pltpu.SemaphoreType.DMA((fetched, 2)),
        ],
        compiler_params=params(),
        cost_estimate=cost(10**8, 2**18),
        name="packed_rows",
    )(*in_hbm(field))


def own_call(field, halo, weight, point, segments, groups):
    tiles = sum(map(len, segments))
    rows, fetched = 8 * tiles, tiles + 2 * len(segments)
    hbm = pl.BlockSpec(memory_space=pltpu.HBM)
    shapes = [pltpu.HBM((CH, 8 * len(group), NX), F32) for group in groups for _ in range(3)]
    return pl.pallas_call(
        functools.partial(own_kernel, segments, groups),
        out_shape=shapes,
        in_specs=[hbm] * 3 + [pl.BlockSpec(memory_space=pl.ANY)],
        out_specs=[hbm] * len(shapes),
        scratch_shapes=[
            pltpu.VMEM((fetched, 2, CH, 8, 128), F32),
            pltpu.VMEM((2, CH, NX), F32),
            pltpu.VMEM((CH, 27), F32),
            pltpu.VMEM((CH, CH), F32),
            pltpu.VMEM((3, tiles, CH, 8, NX), F32),
            pltpu.VMEM((rows + 2 * len(segments), CH, NX), F32),
            pltpu.VMEM((3, rows, CH, NX), F32),
            pltpu.VMEM((27, CH, 128), F32),
            pltpu.SemaphoreType.DMA((fetched, 2)),
            pltpu.SemaphoreType.DMA((3, tiles)),
            pltpu.SemaphoreType.DMA((3,)),
        ],
        compiler_params=params(),
        cost_estimate=cost(10**8, 2**18),
        name="own_sums",
    )(*in_hbm(weight, point, field), halo)


def middle_call(weight, point, low, own, high):
    rows = own.shape[0] - 2
    hbm = pl.BlockSpec(memory_space=pltpu.HBM)
    return pl.pallas_call(
        middle_kernel,
        out_shape=pltpu.HBM((CH, rows, NX), F32),
        in_specs=[hbm] * 3 + [pl.BlockSpec(memory_space=pl.ANY), hbm],
        out_specs=hbm,
        scratch_shapes=[
            pltpu.VMEM((3, rows + 2, CH, NX), F32),
            pltpu.VMEM((CH, 27), F32),
            pltpu.VMEM((CH, CH), F32),
            pltpu.VMEM((rows // 8, CH, 8, NX), F32),
            pltpu.VMEM((1, rows, CH, NX), F32),
            pltpu.VMEM((27, CH, 128), F32),
            pltpu.SemaphoreType.DMA((5,)),
            pltpu.SemaphoreType.DMA((rows // 8,)),
        ],
        compiler_params=params(),
        cost_estimate=cost(4 * 10**10, 2**18),
        name="middle_sums",
    )(*in_hbm(weight, point, low), own, *in_hbm(high))


def general_filter(coarse, gains, gz, gy, scale):
    j_own, n_own = gains.shape[2], gains.shape[3]
    both = ("gz", "gy")
    flat = coarse.reshape(CH // 2, MY, 2, 2, MX).transpose(3, 1, 0, 2, 4).reshape(2, MY, CH * MX)
    sent = flat.reshape(2, gy, j_own, gz, n_own).transpose(3, 1, 0, 2, 4).reshape(gz * gy, -1)
    got = lax.all_to_all(sent, both, split_axis=0, concat_axis=0, tiled=True)
    got = got.reshape(gz, gy, 2, j_own, n_own)
    c, s = (jnp.asarray(t, F32) for t in trig(kept(MZ, gz), np.arange(gz), gz))
    mul = functools.partial(jnp.einsum, precision=lax.Precision.HIGHEST)
    whole = got.sum(axis=1) * scale
    real = mul("zjn,qz->qjn", whole[:, 0], c) + mul("zjn,qz->qjn", whole[:, 1], s)
    imag = mul("zjn,qz->qjn", whole[:, 1], c) - mul("zjn,qz->qjn", whole[:, 0], s)
    real, imag = real * gains[0] - imag * gains[1], real * gains[1] + imag * gains[0]
    out = jnp.stack(
        [
            mul("qjn,qz->zjn", real, c) - mul("qjn,qz->zjn", imag, s),
            mul("qjn,qz->zjn", real, s) + mul("qjn,qz->zjn", imag, c),
        ],
        axis=1,
    )
    out = jnp.broadcast_to(out[:, None], (gz, gy, 2, j_own, n_own)).reshape(gz * gy, -1)
    back = lax.all_to_all(out, both, split_axis=0, concat_axis=0, tiled=True)
    back = back.reshape(gz, gy, 2, j_own, n_own).transpose(2, 1, 3, 0, 4)
    back = back.reshape(2, MY, CH // 2, 2, MX)
    return back.transpose(2, 1, 3, 0, 4).reshape(CH // 2, MY, 4 * MX)


def body(field, spectral_filter, depth_weight, point_weight, bias_vector):
    gz, gy = lax.axis_size("gz"), lax.axis_size("gy")
    y_local = field.shape[2]
    field = field.reshape(CH, y_local, NX)
    y_total = gy * y_local
    forward_scale = 1.0 / math.sqrt(float(NX) * y_total * gz)
    inverse_scale = 1.0 / math.sqrt(2.0 * MX * MY * MZ)

    def ring(axis, count, by):
        return [(i, (i + by) % count) for i in range(count)]

    def to_neighbours(across, within):
        odd_on = [(i, (i + 1 if i % 2 else i - 1) % gz) for i in range(gz)]
        even_on = [(i, (i - 1 if i % 2 else i + 1) % gz) for i in range(gz)]
        return lax.ppermute(across, "gz", odd_on), lax.ppermute(within, "gz", even_on)

    def after(value, *others):
        return lax.optimization_barrier((value, *others))[0]

    last = y_local // 8 - 1
    cut = 1 + last // 2
    first_tiles, second_tiles = tuple(range(1, cut)), tuple(range(cut, min(cut + 2, last)))
    third_tiles = (0, *range(second_tiles[-1] + 1, last + 1))
    packed, edges = pack_call(field, first_tiles)
    first_low, first_high = to_neighbours(packed, packed)
    if gy == 2:
        halo = lax.ppermute(edges, "gy", ring("gy", gy, 1))
    else:
        halo = jnp.stack(
            [
                lax.ppermute(edges[0], "gy", ring("gy", gy, 1)),
                lax.ppermute(edges[1], "gy", ring("gy", gy, -1)),
            ]
        )
    j_own, n_own = spectral_filter.shape[2], spectral_filter.shape[3]
    whole_tiles = j_own == 8 and n_own == 2 * MX
    coarse = after(forward_call(after(field, packed), gy, whole_tiles), halo)
    segments, groups = ((0,), tuple(range(cut, last + 1))), (second_tiles, third_tiles)
    down, second, up, outer_down, own, outer_up = own_call(
        after(field, coarse), halo, depth_weight, point_weight, segments, groups
    )
    if whole_tiles:
        both = ("gz", "gy")
        got = lax.all_to_all(coarse, both, split_axis=0, concat_axis=0, tiled=True)
        down, up = lax.optimization_barrier((down, up, first_low))[:2]
        pair = to_neighbours(down, up)
        gains = after(spectral_filter, first_low, first_high, second)
        mark = filter_call(got, gains, gz, gy, forward_scale)
        back = lax.all_to_all(mark, "gz", split_axis=0, concat_axis=0, tiled=True)
    else:
        pair = to_neighbours(down, up)
        mark = general_filter(coarse, spectral_filter, gz, gy, forward_scale)
        modes = [mark[:, part].reshape(-1, 4 * MX) for part in (slice(0, MY // 2), slice(MY // 2, MY))]
    outer_pair = to_neighbours(after(outer_down, mark), after(outer_up, mark))
    packed, *pair = lax.optimization_barrier((packed, *pair))
    mixed = middle_call(depth_weight, point_weight, first_low, packed, first_high)
    if whole_tiles:
        modes = (back, lax.ppermute(after(back, mixed), "gy", ring("gy", gy, 1)))
    result, base = inverse_call(
        modes, whole_tiles, bias_vector, own, outer_pair[1], mixed, second, pair, 8, y_local, gy, inverse_scale
    )
    result = finish_call(result, base, outer_pair[0], 1)
    return result.reshape(CH, 1, y_local, NX)


def solution(mesh):
    in_specs = (P(None, "gz", "gy", None), P(None, None, "gy", "gz"), P(), P(), P())
    out_specs = P(None, "gz", "gy", None)
    return jax.shard_map(body, mesh=mesh, in_specs=in_specs, out_specs=out_specs, check_vma=False)
```
